32 devices in a mesh: dp: 8 (over z, y), fsdp: 4 (over x, core).
Axes of the slice: x: 2, y: 2, z: 4, core: 2. Of those that a mesh axis runs over, the one named last changes fastest.
Arguments:
- tokens: bfloat16 [32, 32, 64, 768], P(('dp', 'fsdp')), may hold values from -6 to 6
- grad_out: bfloat16 [32, 32, 64, 768], P(('dp', 'fsdp')), may hold values from -6 to 6
- region_rows: int32 [32], P(('dp', 'fsdp')), may hold values from 0 to 32, as said below
- region_cols: int32 [32], P(('dp', 'fsdp')), may hold values from 0 to 64, as said below
- ln1_gain: bfloat16 [768], P(('dp', 'fsdp')), may hold values from 0.5 to 1.5
- ln1_bias: bfloat16 [768], P(('dp', 'fsdp')), may hold values from -4 to 4
- spec_w1: bfloat16 [1536, 96], P(('dp', 'fsdp')), may hold values from -0.4375 to 0.4375
- spec_b1: bfloat16 [1536], P(('dp', 'fsdp')), may hold values from -1.5 to 1.5
- spec_w2: bfloat16 [1536, 96], P(('dp', 'fsdp')), may hold values from -0.4375 to 0.4375
- spec_b2: bfloat16 [1536], P(('dp', 'fsdp')), may hold values from -0.3125 to 0.3125
- ln2_gain: bfloat16 [768], P(('dp', 'fsdp')), may hold values from 0.5 to 1.5
- ln2_bias: bfloat16 [768], P(('dp', 'fsdp')), may hold values from -4 to 4
- w_up: bfloat16 [768, 3072], P(('dp', 'fsdp')), may hold values from -0.21875 to 0.21875
- up_bias: bfloat16 [3072], P(('dp', 'fsdp')), may hold values from -4 to 4
- w_down: bfloat16 [3072, 768], P(('dp', 'fsdp')), may hold values from -0.109375 to 0.109375
- down_bias: bfloat16 [768], P(('dp', 'fsdp')), may hold values from -4 to 4
Outputs:
- mixed: bfloat16 [32, 32, 64, 768], P(('dp', 'fsdp'))
- grad_tokens: float32 [32, 32, 64, 768], P(('dp', 'fsdp'))
- grad_ln1_gain: float32 [768], P(('dp', 'fsdp'))
- grad_ln1_bias: float32 [768], P(('dp', 'fsdp'))
- grad_spec_w1: float32 [1536, 96], P(('dp', 'fsdp'))
- grad_spec_b1: float32 [1536], P(('dp', 'fsdp'))
- grad_spec_w2: float32 [1536, 96], P(('dp', 'fsdp'))
- grad_spec_b2: float32 [1536], P(('dp', 'fsdp'))
- grad_ln2_gain: float32 [768], P(('dp', 'fsdp'))
- grad_ln2_bias: float32 [768], P(('dp', 'fsdp'))
- grad_w_up: float32 [768, 3072], P(('dp', 'fsdp'))
- grad_up_bias: float32 [3072], P(('dp', 'fsdp'))
- grad_w_down: float32 [3072, 768], P(('dp', 'fsdp'))
- grad_down_bias: float32 [768], P(('dp', 'fsdp'))
The draws below stay inside these ranges and needn't reach their ends.
Inputs may be any that keep to these rules, and one draw needn't show every extreme that they name: `region_rows`: each device holds exactly one bucket, and every bucket carries a region. A live region has 16 to 32 rows and 32 to 64 columns; an empty bucket has 0 of both. Some live region fills all 32 rows. `region_cols`: empty exactly where region_rows is 0; some live region fills all 64 columns.
All inputs are finite; a program needn't handle non-finite values.
Results may differ from the reference program's by a relative error of at most 0.0065.
The reference program's roundings to bfloat16 on the way count: a program that leaves them out, or rounds other values in their place, can miss the bound.
Values may be sent and summed in bfloat16 or wider, within the bound.
No kernel may reach another device: no remote copies, remote signals or barrier semaphores. Data moves between devices by JAX's collectives and lax.ppermute only.
A program may use at most 256 MiB of HBM per device.

```python
import jax
import jax.numpy as jnp
from jax import lax

D = 768
FF = 3072
BLOCKS = 8
BLK = 96
BH = 32
BW = 64
SLOTS = 1
REGIONS = 32


def slot_used(key):
    device_count = REGIONS // SLOTS
    counts = jax.random.randint(jax.random.fold_in(key, 5), (device_count,), 1, SLOTS + 1)
    counts = counts.at[0].set(SLOTS)
    places = jnp.arange(REGIONS, dtype=jnp.int32)
    return places % SLOTS < counts[places // SLOTS]


def draw_region_rows(key, part):
    used = slot_used(key)
    key = jax.random.fold_in(key, 11)
    values = jax.random.randint(key, (REGIONS,), BH // 2, BH + 1)
    values = values.at[0].set(BH)
    return jnp.where(used, values, 0).astype(jnp.int32)


def draw_region_cols(key, part):
    used = slot_used(key)
    key = jax.random.fold_in(key, 23)
    values = jax.random.randint(key, (REGIONS,), BW // 2, BW + 1)
    values = values.at[0].set(BW)
    return jnp.where(used, values, 0).astype(jnp.int32)


def block_scale(key, extent, cuts, low, largest):
    loudness = 1.0
    for position, shards_of in cuts:
        heights = jax.random.uniform(jax.random.fold_in(jax.random.fold_in(key, 6), position), (shards_of,), jnp.float32, low / len(cuts), largest / len(cuts))
        loudness = loudness * jnp.repeat(jnp.exp(heights), extent[position] // shards_of).reshape((-1,) + (1,) * (len(extent) - 1 - position))
    return loudness


def normal_values(key, extent, scale, most, cuts=(), held_as=jnp.bfloat16):
    drawn = scale * jax.random.normal(key, extent, jnp.float32)
    if cuts:
        drawn = drawn * block_scale(key, extent, cuts, -0.22, 0.18)
    return jnp.clip(drawn, -most, most).astype(held_as)


def setup_inputs(seed: int = 0) -> dict:
    splits = jax.random.split(jax.random.key(seed), 17)
    return {
        "tokens": normal_values(splits[0], (REGIONS, BH, BW, D), 1.0, 6.0, ((0, 32),)),
        "grad_out": normal_values(splits[1], (REGIONS, BH, BW, D), 1.0, 6.0, ((0, 32),)),
        "region_rows": draw_region_rows(jax.random.fold_in(splits[16], 71), 0),
        "region_cols": draw_region_cols(jax.random.fold_in(splits[16], 71), 0),
        "ln1_gain": jnp.clip(1.0 + 0.1 * jax.random.normal(splits[4], (D,), jnp.float32), 0.5, 1.5).astype(jnp.bfloat16),
        "ln1_bias": normal_values(splits[5], (D,), 0.3, 4.0, ((0, 32),)),
        "spec_w1": normal_values(splits[6], (2 * D, BLK), (2 * BLK) ** -0.5, 0.4375, ((0, 32),)),
        "spec_b1": normal_values(splits[7], (2 * D,), 0.1, 1.5, ((0, 32),)),
        "spec_w2": normal_values(splits[8], (2 * D, BLK), (2 * BLK) ** -0.5, 0.4375, ((0, 32),)),
        "spec_b2": normal_values(splits[9], (2 * D,), 0.02, 0.3125, ((0, 32),)),
        "ln2_gain": jnp.clip(1.0 + 0.1 * jax.random.normal(splits[10], (D,), jnp.float32), 0.5, 1.5).astype(jnp.bfloat16),
        "ln2_bias": normal_values(splits[11], (D,), 0.3, 4.0, ((0, 32),)),
        "w_up": normal_values(splits[12], (D, FF), D ** -0.5, 0.21875, ((0, 32),)),
        "up_bias": normal_values(splits[13], (FF,), 0.3, 4.0, ((0, 32),)),
        "w_down": normal_values(splits[14], (FF, D), FF ** -0.5, 0.109375, ((0, 32),)),
        "down_bias": normal_values(splits[15], (D,), 0.3, 4.0, ((0, 32),)),
    }


norm_eps = 1e-05
shrink_level = 0.01

@jax.custom_vjp
def low(v):
    return lax.optimization_barrier(v.astype(jnp.bfloat16)).astype(jnp.float32)

@jax.custom_vjp
def low_back(v):
    return v

def low_keep(v):
    return (low(v), None)

def low_pass(kept, grad):
    return (grad,)

def back_keep(v):
    return (v, None)

def back_low(kept, grad):
    return (low(grad),)
low.defvjp(low_keep, low_pass)
low_back.defvjp(back_keep, back_low)

def layer_norm(values, gain, shift):
    centred = values - lax.optimization_barrier(jnp.mean(values, axis=-1, keepdims=True))
    variance = lax.optimization_barrier(jnp.mean(centred * centred, axis=-1, keepdims=True))
    return centred * lax.rsqrt(variance + norm_eps) * gain + shift

def block_product(left, right):
    return jnp.einsum('hkbi,bio->hkbo', left, right, precision=lax.Precision.HIGHEST)

def complex_mix(real_in, imag_in, weight, bias):
    real_out = block_product(real_in, weight[0]) - block_product(imag_in, weight[1]) + bias[0]
    imag_out = block_product(real_in, weight[1]) + block_product(imag_in, weight[0]) + bias[1]
    return (real_out, imag_out)

def live_cells(rows_here, cols_here):
    row_place = lax.broadcasted_iota(jnp.int32, (BH, BW), 0)
    col_place = lax.broadcasted_iota(jnp.int32, (BH, BW), 1)
    inside = (row_place < rows_here) & (col_place < cols_here)
    return jnp.where(inside, 1.0, 0.0).astype(jnp.float32)[:, :, None]

def block_layer(region, live, params):
    gain_one, shift_one, weight_one, bias_one, weight_two, bias_two, gain_two, shift_two, up_weight, up_shift, down_weight, down_shift = params
    feature_count = region.shape[-1]
    block_size = feature_count // BLOCKS
    mode_count = BW // 2 + 1
    normed = layer_norm(region, gain_one, shift_one)
    masked = live * normed
    spectrum = jnp.fft.rfft2(masked, axes=(0, 1), norm='ortho')
    real_low = low(jnp.real(spectrum)).reshape(BH, mode_count, BLOCKS, block_size)
    imag_low = low(jnp.imag(spectrum)).reshape(BH, mode_count, BLOCKS, block_size)
    first = weight_one.reshape(2, BLOCKS, block_size, block_size)
    first_bias = bias_one.reshape(2, BLOCKS, block_size)
    second = weight_two.reshape(2, BLOCKS, block_size, block_size)
    second_bias = bias_two.reshape(2, BLOCKS, block_size)
    pre_real, pre_imag = complex_mix(real_low, imag_low, first, first_bias)
    pre_real = low_back(pre_real)
    pre_imag = low_back(pre_imag)
    hidden_real = low(jax.nn.gelu(pre_real))
    hidden_imag = low(jax.nn.gelu(pre_imag))
    out_real, out_imag = complex_mix(hidden_real, hidden_imag, second, second_bias)
    out_real = low_back(out_real)
    out_imag = low_back(out_imag)
    shrunk_real = out_real - shrink_level * jnp.tanh(out_real / shrink_level)
    shrunk_imag = out_imag - shrink_level * jnp.tanh(out_imag / shrink_level)
    shrunk = lax.complex(shrunk_real, shrunk_imag).reshape(BH, mode_count, feature_count)
    spatial = jnp.fft.irfft2(shrunk, s=(BH, BW), axes=(0, 1), norm='ortho')
    middle = region + live * spatial + masked
    lowered = low(layer_norm(middle, gain_two, shift_two))
    pre_up = low_back(jnp.einsum('hwd,df->hwf', lowered, up_weight, precision=lax.Precision.HIGHEST) + up_shift)
    active = low(jax.nn.gelu(pre_up))
    branch = low_back(jnp.einsum('hwf,fd->hwd', active, down_weight, precision=lax.Precision.HIGHEST) + down_shift)
    return middle + live * branch

def reference(tokens, grad_out, region_rows, region_cols, ln1_gain, ln1_bias, spec_w1, spec_b1, spec_w2, spec_b2, ln2_gain, ln2_bias, w_up, up_bias, w_down, down_bias):
    params = tuple((item.astype(jnp.float32) for item in (ln1_gain, ln1_bias, spec_w1, spec_b1, spec_w2, spec_b2, ln2_gain, ln2_bias, w_up, up_bias, w_down, down_bias)))

    def region_step(totals, items):
        region, cotangent, rows_here, cols_here = items
        live = live_cells(rows_here, cols_here)

        def apply_layer(inputs, weights):
            return block_layer(inputs, live, weights)
        result, pullback = jax.vjp(apply_layer, region.astype(jnp.float32), params)
        grad_region, grad_params = pullback(cotangent.astype(jnp.float32))
        totals = jax.tree.map(lambda first, second: first + second, totals, grad_params)
        return (totals, (result.astype(jnp.bfloat16), grad_region))
    zeros = jax.tree.map(jnp.zeros_like, params)
    totals, (mixed, grad_tokens) = lax.scan(region_step, zeros, (tokens, grad_out, region_rows, region_cols))
    return (mixed, grad_tokens, totals[0], totals[1], totals[2], totals[3], totals[4], totals[5], totals[6], totals[7], totals[8], totals[9], totals[10], totals[11])
```

```python
import functools
import math

import jax
import jax.numpy as jnp
import numpy as np
from jax import lax
from jax.experimental import pallas as pl
from jax.experimental.pallas import tpu as pltpu
from jax.sharding import PartitionSpec as P

BF = jnp.bfloat16
F32 = jnp.float32
BLOCKS = 8
EPS = 1e-05
SHRINK = 0.01
ROWS = 32
COLS = 64
KEPT = COLS // 2
GROUP = 4
STEPS = ROWS // GROUP
CELLS = GROUP * COLS
MODES = (KEPT + 1) * ROWS
HEAD = (GROUP + 1) * ROWS
BODY = GROUP * ROWS
LANES = 128
C1 = math.sqrt(2.0 / math.pi)
C3 = 0.044715
UNITS = 16
VMEM_LIMIT = 60 * 1024 * 1024


def table_parts(values):
    high = values.astype(np.float32).astype(jnp.bfloat16)
    low = (values - high.astype(np.float64)).astype(np.float32).astype(jnp.bfloat16)
    return np.stack([high, low])


def wave_matrices():
    scale = 1.0 / math.sqrt(ROWS * COLS)
    w = np.arange(COLS)
    first = np.zeros((KEPT, 2, GROUP, GROUP, COLS))
    for k in range(KEPT):
        for h in range(GROUP):
            if k == 0:
                first[k, 0, h, h] = scale
                first[k, 1, h, h] = scale * np.where(w % 2 == 0, 1.0, -1.0)
            else:
                first[k, 0, h, h] = scale * np.cos(2 * np.pi * (k * w % COLS) / COLS)
                first[k, 1, h, h] = -scale * np.sin(2 * np.pi * (k * w % COLS) / COLS)
    first = first.reshape(CELLS, CELLS)
    p = np.arange(ROWS)
    turn = 2 * np.pi * (np.outer(p, p) % ROWS) / ROWS
    cos = np.cos(turn).reshape(ROWS, STEPS, GROUP)
    sin = np.sin(turn).reshape(ROWS, STEPS, GROUP)
    body = np.zeros((2, GROUP, ROWS, GROUP, STEPS, 2, GROUP))
    head = np.zeros((2, GROUP + 1, ROWS, GROUP, STEPS, 2, GROUP))
    for k in range(GROUP):
        body[0, k, :, k, :, 0] = cos
        body[0, k, :, k, :, 1] = sin
        body[1, k, :, k, :, 1] = cos
        body[1, k, :, k, :, 0] = -sin
    head[:, 1:GROUP, :, 1:] = body[:, 1:, :, 1:]
    for place, part in ((0, 0), (GROUP, 1)):
        head[0, place, :, 0, :, part] = cos
        head[1, place, :, 0, :, part] = -sin
    weight = np.full((2, GROUP + 1, ROWS, 1), 2.0)
    weight[:, 0] = 1.0
    weight[:, GROUP] = 1.0
    head = head.reshape(2 * HEAD, 2 * BODY)
    body = body.reshape(2 * BODY, 2 * BODY)
    head_weighted = head * weight.reshape(2 * HEAD, 1)
    body_weighted = body * 2.0
    return {
        "first": table_parts(first),
        "first_t": table_parts(first.T),
        "head": table_parts(head),
        "body": table_parts(body),
        "head_t": table_parts(head.T),
        "body_t": table_parts(body.T),
        "head_w": table_parts(head_weighted),
        "body_w": table_parts(body_weighted),
        "head_wt": table_parts(head_weighted.T),
        "body_wt": table_parts(body_weighted.T),
    }


def mm(left, right, dims=(1, 0)):
    return lax.dot_general(
        left, right, (((dims[0],), (dims[1],)), ((), ())), preferred_element_type=F32
    )


def split(values):
    high = values.astype(BF)
    return high, (values - high.astype(F32)).astype(BF)


def turn(table, values):
    high, low = split(values)
    return mm(table[0], high) + mm(table[1], high) + mm(table[0], low)


def normalize(values):
    centred = values - jnp.mean(values, axis=-1, keepdims=True)
    inverse = lax.rsqrt(jnp.mean(centred * centred, axis=-1, keepdims=True) + EPS)
    return centred * inverse, inverse


def norm_back(grad, gain, normal, inverse):
    scaled = grad * gain
    return inverse * (
        scaled
        - jnp.mean(scaled, axis=-1, keepdims=True)
        - normal * jnp.mean(scaled * normal, axis=-1, keepdims=True)
    )


def gelu_parts(value):
    square = value * value
    half = 0.5 + 0.5 * jnp.tanh(value * (C1 + (C1 * C3) * square))
    active = value * half
    slope = half + active * (1.0 - half) * (2.0 * C1 + (6.0 * C1 * C3) * square)
    return active, slope


def gelu(value):
    square = value * value
    return value * (0.5 + 0.5 * jnp.tanh(value * (C1 + (C1 * C3) * square)))


def live_rows(start, count, rows_ref, cols_ref):
    cell = start + lax.broadcasted_iota(jnp.int32, (count, 1), 0)
    inside = (cell // COLS < rows_ref[0]) & (cell % COLS < cols_ref[0])
    return jnp.where(inside, 1.0, 0.0).astype(F32)


def spread(piece, per_device, dtype=F32):
    devices = piece.shape[0]
    total = devices * per_device
    lane = lax.broadcasted_iota(jnp.int32, (LANES, total), 0)
    place = lax.broadcasted_iota(jnp.int32, (LANES, total), 1)
    pick = jnp.where(place % per_device == lane, 1.0, 0.0).astype(BF)
    wide = mm(piece.astype(BF), pick)
    owner = lax.broadcasted_iota(jnp.int32, (devices, total), 0)
    where = lax.broadcasted_iota(jnp.int32, (devices, total), 1) // per_device
    return jnp.sum(jnp.where(owner == where, wide, 0.0), axis=0, keepdims=True)


def mode_chunks(body):
    body(0, HEAD, 0, True)

    @pl.loop(1, KEPT // GROUP)
    def _(j):
        body(pl.multiple_of(BODY * j + ROWS, ROWS), BODY, GROUP * j, False)


def transform_kernel(rows_ref, cols_ref, tokens_ref, first_ref, head_ref, body_ref, out_ref, half_ref):
    feature = tokens_ref.shape[1]

    @pl.loop(0, STEPS)
    def _(g):
        start = pl.multiple_of(g * CELLS, CELLS)
        normal, _ = normalize(tokens_ref[pl.ds(start, CELLS), :].astype(F32))
        live = live_rows(start, CELLS, rows_ref, cols_ref)
        place = pl.multiple_of(g * 2 * GROUP, 2 * GROUP)
        half_ref[:, pl.ds(place, 2 * GROUP), :feature] = turn(first_ref, normal * live).reshape(
            KEPT, 2 * GROUP, feature
        )
        ones = jnp.broadcast_to(live, (CELLS, LANES)).astype(BF)
        half_ref[:, pl.ds(place, 2 * GROUP), feature:] = (
            mm(first_ref[0], ones) + mm(first_ref[1], ones)
        ).reshape(KEPT, 2 * GROUP, LANES)

    def chunk(offset, rows, slot, is_head):
        values = half_ref[pl.ds(slot, GROUP)].reshape(2 * BODY, feature + LANES)
        result = turn(head_ref if is_head else body_ref, values)
        out_ref[0, pl.ds(offset, rows), :] = result[:rows]
        out_ref[1, pl.ds(offset, rows), :] = result[rows:]

    mode_chunks(chunk)


def whole(*arrays):
    return [pl.BlockSpec(memory_space=pltpu.VMEM) for _ in arrays]


def smem():
    return pl.BlockSpec(memory_space=pltpu.SMEM)


def params(**more):
    return pltpu.CompilerParams(vmem_limit_bytes=VMEM_LIMIT, **more)


def cost(flops, moved):
    return pl.CostEstimate(flops=int(flops), bytes_accessed=int(moved), transcendentals=0)


def transform(rows, cols, tokens, tables):
    cells, feature = tokens.shape
    operands = (tokens, tables["first"], tables["head"], tables["body"])
    return pl.pallas_call(
        transform_kernel,
        out_shape=jax.ShapeDtypeStruct((2, MODES, feature + LANES), F32),
        in_specs=[smem(), smem()] + whole(*operands),
        out_specs=pl.BlockSpec(memory_space=pltpu.VMEM),
        scratch_shapes=[pltpu.VMEM((KEPT, 2 * ROWS, feature + LANES), F32)],
        compiler_params=params(),
        cost_estimate=cost(12e9, 11e6),
        name="transform",
    )(rows, cols, *operands)


def build_mix(weights_ref, layer, out_ref, feature):
    block = feature // BLOCKS
    half = feature // 2
    per_group = BLOCKS // 2
    out_ref[...] = jnp.zeros_like(out_ref)
    row = lax.broadcasted_iota(jnp.int32, (LANES, half), 0)
    column = lax.broadcasted_iota(jnp.int32, (LANES, half), 1)
    for group in range(2):
        for b in range(per_group):
            shift = jnp.where((column - b * block == row) & (row < block), 1.0, 0.0).astype(BF)
            top = b * block
            for part in range(2):
                at = (part * BLOCKS + group * per_group + b) * block
                placed = mm(weights_ref[layer, at : at + block, :], shift)
                if part == 0:
                    out_ref[group, top : top + block, :half] = placed.astype(BF)
                    out_ref[group, half + top : half + top + block, half:] = placed.astype(BF)
                else:
                    out_ref[group, top : top + block, half:] = placed.astype(BF)
                    out_ref[group, half + top : half + top + block, :half] = (-placed).astype(BF)


def side(values, group, half):
    return values[:, group * half : (group + 1) * half]


def join(left, right):
    return jnp.concatenate([left, right], axis=1)


def mix_kernel(
    rows_ref, cols_ref, spec_ref, tokens_ref, small_ref, vector_ref, first_t_ref, head_ref, body_ref,
    low_ref, middle_ref, normed_ref, mix1_ref, mix2_ref, wide_ref, up_ref, half_ref,
):
    feature = tokens_ref.shape[1]
    half = feature // 2
    devices = vector_ref.shape[1]
    share = feature // devices
    build_mix(small_ref, 0, mix1_ref, feature)
    build_mix(small_ref, 1, mix2_ref, feature)
    for row, at in enumerate((2, 3, 4, 5, 7)):
        wide_ref[row : row + 1, :] = spread(vector_ref[at], share)
    for row, at in ((5, 0), (7, 1)):
        both = spread(vector_ref[at], 2 * share)
        wide_ref[row : row + 1, :] = both[:, :feature]
        wide_ref[row + 1 : row + 2, :] = both[:, feature:]
    wide_ref[9:, :] = jnp.zeros_like(wide_ref[9:, :])
    up_ref[...] = spread(vector_ref[6], up_ref.shape[1] // devices)
    gain = wide_ref[0:1, :]
    shift = wide_ref[1:2, :]

    def chunk(offset, rows, slot, is_head):
        place = pl.ds(offset, rows)
        for part in range(2):
            flat = spec_ref[part, place, feature:]
            flat = jnp.concatenate([flat] * (feature // LANES), axis=1)
            low_ref[part, place, :] = (spec_ref[part, place, :feature] * gain + flat * shift).astype(BF)
        shrunk = []
        for group in range(2):
            inside = join(side(low_ref[0, place, :], group, half), side(low_ref[1, place, :], group, half))
            bias = join(side(wide_ref[5:6, :], group, half), side(wide_ref[6:7, :], group, half))
            hidden = gelu(mm(inside, mix1_ref[group]) + bias).astype(BF)
            bias = join(side(wide_ref[7:8, :], group, half), side(wide_ref[8:9, :], group, half))
            value = mm(hidden, mix2_ref[group]) + bias
            shrunk.append(value - SHRINK * jnp.tanh(value / SHRINK))
        values = jnp.concatenate(
            [join(shrunk[0][:, :half], shrunk[1][:, :half]), join(shrunk[0][:, half:], shrunk[1][:, half:])], axis=0
        )
        half_ref[pl.ds(slot, GROUP)] = turn(head_ref if is_head else body_ref, values).reshape(
            GROUP, 2 * ROWS, feature
        )

    mode_chunks(chunk)
    gain_two = wide_ref[2:3, :]
    shift_two = wide_ref[3:4, :]

    @pl.loop(0, STEPS)
    def _(g):
        start = pl.multiple_of(g * CELLS, CELLS)
        place = pl.multiple_of(g * 2 * GROUP, 2 * GROUP)
        values = half_ref[:, pl.ds(place, 2 * GROUP), :].reshape(CELLS, feature)
        spatial = turn(first_t_ref, values)
        inputs = tokens_ref[pl.ds(start, CELLS), :].astype(F32)
        live = live_rows(start, CELLS, rows_ref, cols_ref)
        normal, _ = normalize(inputs)
        middle = inputs + live * (spatial + (normal * gain + shift))
        middle_ref[pl.ds(start, CELLS), :] = middle
        normal, _ = normalize(middle)
        normed_ref[pl.ds(start, CELLS), :] = (normal * gain_two + shift_two).astype(BF)


def mix(rows, cols, spec, tokens, small, vectors, tables, hidden):
    cells, feature = tokens.shape
    operands = (spec, tokens, small, vectors, tables["first_t"], tables["head_wt"], tables["body_wt"])
    shapes = (
        jax.ShapeDtypeStruct((2, MODES, feature), BF),
        jax.ShapeDtypeStruct((cells, feature), F32),
        jax.ShapeDtypeStruct((cells, feature), BF),
        jax.ShapeDtypeStruct((2, feature, feature), BF),
        jax.ShapeDtypeStruct((2, feature, feature), BF),
        jax.ShapeDtypeStruct((16, feature), F32),
        jax.ShapeDtypeStruct((1, hidden), F32),
    )
    return pl.pallas_call(
        mix_kernel,
        out_shape=shapes,
        in_specs=[smem(), smem()] + whole(*operands),
        out_specs=whole(*shapes),
        scratch_shapes=[pltpu.VMEM((KEPT, 2 * ROWS, feature), F32)],
        compiler_params=params(),
        cost_estimate=cost(20e9, 30e6),
        name="mix",
    )(rows, cols, *operands)


def any_space():
    return pl.BlockSpec(memory_space=pl.ANY)


def single(shape):
    return pl.BlockSpec(shape, lambda *_: (0,) * len(shape), pipeline_mode=pl.Buffered(1))


def fetch_weights(me_ref, pieces, places, up_ref, down_ref, sems):
    count = pieces[0].shape[0] * 2
    chip = me_ref[0] // 2

    def copies(own, core):
        target = (up_ref, down_ref)[core]
        source = pieces[:2] if own else pieces[2:]
        for mask in range(count):
            at = places[core][mask]
            part = source[at // (count // 2)].at[at % (count // 2)]
            yield pltpu.make_async_copy(part, target.at[chip ^ mask], sems.at[core, mask])

    for core in range(2):
        @pl.when(me_ref[0] % 2 == core)
        def _():
            for copy in copies(True, core):
                copy.start()
            for copy in copies(False, 1 - core):
                copy.start()

    for core in range(2):
        for copy in copies(True, core):
            copy.wait()


def weight_scratch(pieces):
    chips, rows, feature = pieces[0].shape[0] * 2, pieces[0].shape[1], pieces[0].shape[2]
    return [
        pltpu.VMEM((chips, rows, feature), BF),
        pltpu.VMEM((chips, rows, feature), BF),
        pltpu.SemaphoreType.DMA((2, chips)),
    ]


def up_part(up_ref, j, feature):
    share = up_ref.shape[1] * feature // (up_ref.shape[0] * up_ref.shape[1])
    return up_ref[:, j * share : (j + 1) * share, :].reshape(feature, feature)


def down_part(down_ref, j, feature):
    share = down_ref.shape[1]
    each = feature // share
    return down_ref[j * each : (j + 1) * each].reshape(feature, feature)


def up_kernel(places, rows_ref, cols_ref, me_ref, normed_ref, grad_ref, bias_ref, *rest):
    pieces = rest[:4]
    active_ref, pre_ref, live_ref, bias_grad_ref, up_ref, down_ref, sems = rest[4:]
    tile, feature = normed_ref.shape
    step = pl.program_id(0)

    @pl.when(step == 0)
    def _():
        fetch_weights(me_ref, pieces, places, up_ref, down_ref, sems)
        bias_grad_ref[...] = jnp.zeros_like(bias_grad_ref)

    live = live_rows(step * tile, tile, rows_ref, cols_ref)
    branch = (grad_ref[...].astype(F32) * live).astype(BF)
    live_ref[...] = branch
    normed = normed_ref[...]
    for j in range(active_ref.shape[1] // feature):
        place = slice(j * feature, (j + 1) * feature)
        value = mm(normed, up_part(up_ref, j, feature)) + bias_ref[:, place]
        grad = mm(branch, down_part(down_ref, j, feature), (1, 1))
        active, slope = gelu_parts(value)
        active_ref[:, place] = active.astype(BF)
        low = (grad * slope).astype(BF)
        pre_ref[:, place] = low
        bias_grad_ref[:, place] += jnp.sum(low.astype(F32), axis=0, keepdims=True)


def feed_up(rows, cols, me, normed, grad, bias, pieces, places, tile=256):
    cells, feature = normed.shape
    hidden = bias.shape[1]
    block = lambda width: pl.BlockSpec((tile, width), lambda i: (i, 0))
    return pl.pallas_call(
        functools.partial(up_kernel, places),
        grid=(cells // tile,),
        out_shape=(
            jax.ShapeDtypeStruct((cells, hidden), BF),
            jax.ShapeDtypeStruct((cells, hidden), BF),
            jax.ShapeDtypeStruct((cells, feature), BF),
            jax.ShapeDtypeStruct((1, hidden), F32),
        ),
        in_specs=[smem(), smem(), smem(), block(feature), block(feature), single(bias.shape)]
        + [any_space() for _ in pieces],
        out_specs=(block(hidden), block(hidden), block(feature), pl.BlockSpec((1, hidden), lambda i: (0, 0))),
        scratch_shapes=weight_scratch(pieces),
        compiler_params=params(),
        cost_estimate=cost(4 * cells * feature * hidden, 40e6),
        name="feed_up",
    )(rows, cols, me, normed, grad, bias, *pieces)


def weight_grad_kernel(places, me_ref, active_ref, pre_ref, branch_ref, normed_ref, send_ref, keep_ref, stage_ref, sems):
    step = pl.program_id(0)
    steps = pl.num_programs(0) // 2
    feature = branch_ref.shape[1]
    chips, rows, _ = send_ref.shape
    each = feature // rows
    share = feature // chips

    def down_copies(j, target):
        for c in range(each):
            source = stage_ref.at[j, pl.ds(c * rows, rows)]
            yield pltpu.make_async_copy(source, target.at[places[1][j * each + c]], sems.at[j, c])

    def up_copies(j, target):
        for c in range(chips):
            source = stage_ref.at[steps + j, pl.ds(c * share, share)]
            there = target.at[places[0][c], pl.ds(j * share, share)]
            yield pltpu.make_async_copy(source, there, sems.at[steps + j, c])

    @pl.when(step < steps)
    def _():
        stage_ref[step] = mm(active_ref[...], branch_ref[...], (0, 0)).astype(BF)

    @pl.when(step >= steps)
    def _():
        stage_ref[step] = mm(normed_ref[...], pre_ref[...], (0, 0)).astype(BF)

    total = stage_ref.shape[0] // 2
    for j in range(total):
        for core in range(2):
            targets = (send_ref, keep_ref) if core == 0 else (keep_ref, send_ref)

            @pl.when((step == j) & (me_ref[0] % 2 == core))
            def _():
                for copy in down_copies(j, targets[0]):
                    copy.start()

            @pl.when((step == total + j) & (me_ref[0] % 2 == core))
            def _():
                for copy in up_copies(j, targets[1]):
                    copy.start()

    @pl.when(step == 2 * steps - 1)
    def _():
        for j in range(total):
            for copy in down_copies(j, send_ref):
                copy.wait()
            for copy in up_copies(j, send_ref):
                copy.wait()


def weight_grads(me, active, pre, branch, normed, places):
    cells, hidden = active.shape
    feature = branch.shape[1]
    tiles = hidden // feature
    chips = UNITS
    shape = jax.ShapeDtypeStruct((chips, hidden // chips, feature), BF)
    return pl.pallas_call(
        functools.partial(weight_grad_kernel, places),
        grid=(2 * tiles,),
        out_shape=(shape, shape),
        in_specs=[
            smem(),
            pl.BlockSpec((cells, feature), lambda i: (0, jnp.minimum(i, tiles - 1))),
            pl.BlockSpec((cells, feature), lambda i: (0, jnp.maximum(i - tiles, 0))),
            single(branch.shape), single(normed.shape),
        ],
        out_specs=(any_space(), any_space()),
        scratch_shapes=[
            pltpu.VMEM((2 * tiles, feature, feature), BF),
            pltpu.SemaphoreType.DMA((2 * tiles, chips)),
        ],
        compiler_params=params(),
        cost_estimate=cost(4 * cells * feature * hidden, 40e6),
        name="weight_grads",
    )(me, active, pre, branch, normed)


def down_kernel(places, rows_ref, cols_ref, me_ref, active_ref, pre_ref, middle_ref, grad_ref, wide_ref, *rest):
    pieces = rest[:4]
    mixed_ref, grad_middle_ref, sums_ref, up_ref, down_ref, sems = rest[4:]
    tile, feature = middle_ref.shape
    hidden = active_ref.shape[1]
    step = pl.program_id(0)

    @pl.when(step == 0)
    def _():
        fetch_weights(me_ref, pieces, places, up_ref, down_ref, sems)
        sums_ref[...] = jnp.zeros_like(sums_ref)

    live = live_rows(step * tile, tile, rows_ref, cols_ref)
    branch = mm(active_ref[...], down_ref[...].reshape(hidden, feature))
    grad_normed = jnp.zeros((tile, feature), F32)
    for j in range(hidden // feature):
        pre = pre_ref[:, j * feature : (j + 1) * feature]
        grad_normed = grad_normed + mm(pre, up_part(up_ref, j, feature), (1, 1))
    middle = middle_ref[...]
    mixed_ref[...] = (middle + live * (branch + wide_ref[4:5, :])).astype(BF)
    normal, inverse = normalize(middle)
    cotangent = grad_ref[...].astype(F32)
    grad_middle_ref[...] = cotangent + norm_back(grad_normed, wide_ref[2:3, :], normal, inverse)
    sums_ref[0:1, :] += jnp.sum(grad_normed * normal, axis=0, keepdims=True)
    sums_ref[1:2, :] += jnp.sum(grad_normed, axis=0, keepdims=True)
    sums_ref[2:3, :] += jnp.sum((cotangent * live).astype(BF).astype(F32), axis=0, keepdims=True)


def feed_down(rows, cols, me, active, pre, middle, grad, wide, pieces, places, tile=256):
    cells, feature = middle.shape
    hidden = active.shape[1]
    block = lambda width: pl.BlockSpec((tile, width), lambda i: (i, 0))
    return pl.pallas_call(
        functools.partial(down_kernel, places),
        grid=(cells // tile,),
        out_shape=(
            jax.ShapeDtypeStruct((cells, feature), BF),
            jax.ShapeDtypeStruct((cells, feature), F32),
            jax.ShapeDtypeStruct((8, feature), F32),
        ),
        in_specs=[smem(), smem(), smem(), block(hidden), block(hidden), block(feature), block(feature),
                  single(wide.shape)] + [any_space() for _ in pieces],
        out_specs=(block(feature), block(feature), pl.BlockSpec((8, feature), lambda i: (0, 0))),
        scratch_shapes=weight_scratch(pieces),
        compiler_params=params(),
        cost_estimate=cost(4 * cells * feature * hidden, 50e6),
        name="feed_down",
    )(rows, cols, me, active, pre, middle, grad, wide, *pieces)


def mix_back_kernel(
    rows_ref, cols_ref, grad_ref, low_ref, mix1_ref, mix2_ref, wide_ref,
    first_ref, head_ref, body_ref, head_t_ref, body_t_ref,
    half_ref, weight_ref, bias_ref, hidden_ref, two_ref, one_ref,
):
    cells, feature = grad_ref.shape
    half = feature // 2

    @pl.loop(0, STEPS)
    def _(g):
        start = pl.multiple_of(g * CELLS, CELLS)
        place = pl.multiple_of(g * 2 * GROUP, 2 * GROUP)
        live = live_rows(start, CELLS, rows_ref, cols_ref)
        half_ref[:, pl.ds(place, 2 * GROUP), :] = turn(
            first_ref, grad_ref[pl.ds(start, CELLS), :] * live
        ).reshape(KEPT, 2 * GROUP, feature)

    bias_ref[...] = jnp.zeros_like(bias_ref)

    def chunk(offset, rows, slot, is_head):
        place = pl.ds(offset, rows)
        values = half_ref[pl.ds(slot, GROUP)].reshape(2 * BODY, feature)
        grad_shrunk = turn(head_ref if is_head else body_ref, values)
        real = []
        imag = []
        for group in range(2):
            inside = join(side(low_ref[0, place, :], group, half), side(low_ref[1, place, :], group, half))
            bias = join(side(wide_ref[5:6, :], group, half), side(wide_ref[6:7, :], group, half))
            active, slope = gelu_parts(mm(inside, mix1_ref[group]) + bias)
            hidden = active.astype(BF)
            bias = join(side(wide_ref[7:8, :], group, half), side(wide_ref[8:9, :], group, half))
            bend = jnp.tanh((mm(hidden, mix2_ref[group]) + bias) / SHRINK)
            grad = join(side(grad_shrunk[:rows], group, half), side(grad_shrunk[rows:], group, half))
            grad_two = (grad * (bend * bend)).astype(BF)
            grad_one = (mm(grad_two, mix2_ref[group], (1, 1)) * slope).astype(BF)
            grad_spec = mm(grad_one, mix1_ref[group], (1, 1))
            real.append(grad_spec[:, :half])
            imag.append(grad_spec[:, half:])
            lanes = slice(group * half, (group + 1) * half)
            for kept, value in ((hidden_ref, hidden), (two_ref, grad_two), (one_ref, grad_one)):
                kept[0, place, lanes] = value[:, :half]
                kept[1, place, lanes] = value[:, half:]
            for row, value in ((0, grad_one), (2, grad_two)):
                total = jnp.sum(value.astype(F32), axis=0, keepdims=True)
                bias_ref[row : row + 1, lanes] += total[:, :half]
                bias_ref[row + 1 : row + 2, lanes] += total[:, half:]
        values = jnp.concatenate([join(real[0], real[1]), join(imag[0], imag[1])], axis=0)
        half_ref[pl.ds(slot, GROUP)] = turn(head_t_ref if is_head else body_t_ref, values).reshape(
            GROUP, 2 * ROWS, feature
        )

    mode_chunks(chunk)
    block = feature // BLOCKS
    for layer, left, right in ((0, low_ref, one_ref), (1, hidden_ref, two_ref)):
        for pair in range(BLOCKS // 2):
            begin = 2 * pair * block // LANES * LANES
            lanes = slice(begin, begin + 2 * LANES)
            lr, li = left[0, :, lanes], left[1, :, lanes]
            rr, ri = right[0, :, lanes], right[1, :, lanes]
            for part, total in (
                (0, mm(lr, rr, (0, 0)) + mm(li, ri, (0, 0))),
                (1, mm(lr, ri, (0, 0)) - mm(li, rr, (0, 0))),
            ):
                for b in range(2):
                    at = (2 * pair + b) * block - begin
                    piece = total[at : at + block, :]
                    if at:
                        piece = pltpu.roll(piece, 2 * LANES - at, axis=1)
                    top = (part * BLOCKS + 2 * pair + b) * block
                    weight_ref[layer, top : top + block, :] = piece[:, :LANES]


def mix_back(rows, cols, grad, low, mix1, mix2, wide, tables):
    cells, feature = grad.shape
    operands = (grad, low, mix1, mix2, wide, tables["first"], tables["head_w"], tables["body_w"],
                tables["head_t"], tables["body_t"])
    shapes = (
        jax.ShapeDtypeStruct((KEPT, 2 * ROWS, feature), F32),
        jax.ShapeDtypeStruct((2, 2 * feature, LANES), F32),
        jax.ShapeDtypeStruct((8, feature), F32),
    )
    return pl.pallas_call(
        mix_back_kernel,
        out_shape=shapes,
        in_specs=[smem(), smem()] + whole(*operands),
        out_specs=whole(*shapes),
        scratch_shapes=[pltpu.VMEM((2, MODES, feature), BF)] * 3,
        compiler_params=params(),
        cost_estimate=cost(30e9, 20e6),
        name="mix_back",
    )(rows, cols, *operands)


def last_kernel(rows_ref, cols_ref, half_ref, tokens_ref, grad_ref, first_t_ref, wide_ref, out_ref, sums_ref):
    tile, feature = tokens_ref.shape
    step = pl.program_id(0)
    live = live_rows(step * tile, tile, rows_ref, cols_ref)
    grad_middle = grad_ref[...]
    grad_normed = live * (grad_middle + turn(first_t_ref, half_ref[...].reshape(CELLS, feature)))
    normal, inverse = normalize(tokens_ref[...].astype(F32))
    out_ref[...] = grad_middle + norm_back(grad_normed, wide_ref[0:1, :], normal, inverse)

    @pl.when(step == 0)
    def _():
        sums_ref[...] = jnp.zeros_like(sums_ref)

    sums_ref[0:1, :] += jnp.sum(grad_normed * normal, axis=0, keepdims=True)
    sums_ref[1:2, :] += jnp.sum(grad_normed, axis=0, keepdims=True)


def last(rows, cols, half, tokens, grad, wide, tables):
    cells, feature = tokens.shape
    first_t = tables["first_t"]
    block = pl.BlockSpec((CELLS, feature), lambda i: (i, 0))
    return pl.pallas_call(
        last_kernel,
        grid=(STEPS,),
        out_shape=(jax.ShapeDtypeStruct((cells, feature), F32), jax.ShapeDtypeStruct((8, feature), F32)),
        in_specs=[smem(), smem(), pl.BlockSpec((KEPT, 2 * GROUP, feature), lambda i: (0, i, 0)), block, block,
                  single(first_t.shape), single(wide.shape)],
        out_specs=(block, pl.BlockSpec((8, feature), lambda i: (0, 0))),
        compiler_params=params(),
        cost_estimate=cost(3e9, 20e6),
        name="last",
    )(rows, cols, half, tokens, grad, first_t, wide)


AXES = ("dp", "fsdp")


def swap(value, devices, bits):
    return lax.ppermute(value, AXES, [(i, i ^ (1 << bits[i & 1])) for i in range(devices)])


def doubling_orders(count):
    first = list(range(count - 1, 0, -1))
    second = list(first)
    for k in range(0, len(second) - 1, 2):
        second[k], second[k + 1] = second[k + 1], second[k]
    return first, second


def places_of(order):
    return [
        sum(1 << k for k, bit in enumerate(order) if mask >> (bit - 1) & 1) for mask in range(1 << len(order))
    ]


def gather_small(value, me, devices, count):
    order = list(range(3, count)) + [2, 1, 0]
    held = value[None]
    for bit in order:
        other = swap(held, devices, (bit, bit))
        upper = (me >> bit) & 1
        held = jnp.where(upper == 0, jnp.concatenate([held, other]), jnp.concatenate([other, held]))
    held = held.reshape((2,) * count + value.shape)
    places = [count - 1 - order.index(bit) for bit in range(count - 1, -1, -1)]
    return held.transpose(places + [count, count + 1]).reshape((devices,) + value.shape)


def scatter_small(value, me, devices, count, exact):
    order = [0, 1, 2] + list(range(count - 1, 2, -1))
    shape = value.shape[1:]
    rows = shape[0]
    places = [count - 1 - bit for bit in order]
    total = value.reshape((2,) * count + shape).transpose(places + [count, count + 1]).reshape(value.shape)
    for bit in order:
        upper = (me >> bit) & 1
        pair = total.reshape((2, -1) + shape)
        away = lax.dynamic_index_in_dim(pair, 1 - upper, 0, keepdims=False)
        keep = lax.dynamic_index_in_dim(pair, upper, 0, keepdims=False)
        sums = away[:, rows - exact :]
        top = lax.reduce_precision(sums, 8, 7)
        packet = jnp.concatenate([away[:, : rows - exact], top, sums - top], axis=1).astype(BF)
        got = swap(packet, devices, (bit, bit)).astype(F32)
        low = got[:, rows - exact : rows] + got[:, rows:]
        total = keep + jnp.concatenate([got[:, : rows - exact], low], axis=1)
    return total[0]


def gather_large(up, down, me, devices, orders):
    core = me & 1
    parts, share, feature = up.shape
    flat = up.reshape(parts * share, feature)
    other = swap(jnp.where(core == 0, down, flat), devices, (0, 0))
    up_unit = jnp.concatenate([up, other.reshape(up.shape)], axis=1).reshape(2 * parts * share, feature)
    held = jnp.where(core == 0, up_unit, jnp.concatenate([other, down]))[None]
    last_step = len(orders[0]) - 1
    for k in range(last_step):
        held = jnp.concatenate([held, swap(held, devices, (orders[0][k], orders[1][k]))])
    far = swap(held, devices, (orders[0][last_step], orders[1][last_step]))
    return held, far, swap(held, devices, (0, 0)), swap(far, devices, (0, 0))


def scatter_large(send, keep, me, devices, orders):
    core = me & 1
    got = swap(send, devices, (0, 0))
    for k in range(len(orders[0]) - 1, -1, -1):
        upper = (me >> jnp.where(core == 0, orders[0][k], orders[1][k])) & 1
        half = keep.shape[0] // 2

        def part(which):
            cut = lambda v: lax.dynamic_slice_in_dim(v, which * half, half, 0).astype(F32)
            return (cut(keep) + cut(got)).astype(BF)

        send, keep = part(1 - upper), part(upper)
        got = swap(send, devices, (orders[0][k], orders[1][k]))
    return keep[0].astype(F32) + got[0].astype(F32)


def on_device(
    tokens, grad_out, region_rows, region_cols, ln1_gain, ln1_bias, spec_w1, spec_b1, spec_w2, spec_b2,
    ln2_gain, ln2_bias, w_up, up_bias, w_down, down_bias,
):
    devices = lax.axis_size(AXES[0]) * lax.axis_size(AXES[1])
    count = devices.bit_length() - 1
    me = lax.axis_index(AXES).astype(jnp.int32)
    core = me & 1
    me_one = me.reshape(1)
    chips = devices // 2
    feature = tokens.shape[-1]
    block = feature // BLOCKS
    share = ln1_gain.shape[0]
    cells = tokens.shape[1] * tokens.shape[2]
    hidden = w_up.shape[1]
    parts = hidden // feature
    tables = {name: jnp.asarray(value) for name, value in wave_matrices().items()}
    orders = doubling_orders(count)
    places = tuple(places_of(order) for order in orders)
    flat_tokens = tokens.reshape(cells, feature)
    flat_grad = grad_out.reshape(cells, feature)

    padded = lambda v: jnp.pad(v, ((0, 0), (0, LANES - v.shape[1])))
    vectors = (spec_b1, spec_b2, ln1_gain, ln1_bias, ln2_gain, ln2_bias, up_bias, down_bias)
    small = jnp.concatenate([padded(spec_w1), padded(spec_w2)] + [padded(v[None]) for v in vectors])
    small = gather_small(small, me, devices, count)
    weights = small[:, : 4 * share].reshape(devices, 2, 2 * share, LANES).transpose(1, 0, 2, 3)
    weights = weights.reshape(2, 2 * feature, LANES)
    vectors = small[:, 4 * share :].transpose(1, 0, 2).astype(F32)

    fast = chips == UNITS
    own_up = w_up.reshape(share, parts, feature).transpose(1, 0, 2)
    if fast:
        pieces = gather_large(own_up, w_down, me, devices, orders)
    else:
        up = lax.all_gather(w_up, AXES, axis=0, tiled=True)
        up = up.reshape(UNITS, feature // UNITS, parts, feature).transpose(0, 2, 1, 3).reshape(UNITS, -1, feature)
        down = lax.all_gather(w_down, AXES, axis=0, tiled=True).reshape(UNITS, -1, feature)
        pieces = tuple(
            jnp.where(core == 0, first, second)[begin : begin + UNITS // 2]
            for first, second in ((up, down), (down, up))
            for begin in (0, UNITS // 2)
        )
        me_one = core.reshape(1)
        places = (tuple(range(UNITS)),) * 2
    spec = transform(region_rows, region_cols, flat_tokens, tables)
    low, middle, normed, mix1, mix2, wide, up_shift = mix(
        region_rows, region_cols, spec, flat_tokens, weights, vectors, tables, hidden
    )
    active, pre, branch, bias_grad = feed_up(
        region_rows, region_cols, me_one, normed, flat_grad, up_shift, pieces, places
    )
    send, keep = weight_grads(me_one, active, pre, branch, normed, places)
    mixed, grad_middle, sums_two = feed_down(
        region_rows, region_cols, me_one, active, pre, middle, flat_grad, wide, pieces, places
    )
    half, weight_sums, bias_sums = mix_back(
        region_rows, region_cols, grad_middle, low, mix1, mix2, wide, tables
    )
    grad_tokens, sums_one = last(region_rows, region_cols, half, flat_tokens, grad_middle, wide, tables)

    if fast:
        total = scatter_large(send, keep, me, devices, orders)
        up_all = total.reshape(parts, 2 * share, feature)
        lower = up_all[:, :share].reshape(parts * share, feature)
        upper = up_all[:, share:].reshape(parts * share, feature)
        each = parts * share
        other = swap(jnp.where(core == 0, upper, total[:each]), devices, (0, 0))
        grad_w_up = jnp.where(core == 0, lower, other).reshape(parts, share, feature).transpose(1, 0, 2)
        grad_w_down = jnp.where(core == 0, other, total[each:])
    else:
        scatter = lambda v: lax.psum_scatter(v.astype(F32), AXES, scatter_dimension=0, tiled=True)
        up = jnp.where(core == 0, keep, send).reshape(UNITS, parts, feature // UNITS, feature)
        grad_w_up = scatter(up.transpose(0, 2, 1, 3).reshape(feature, hidden))
        grad_w_down = scatter(jnp.where(core == 0, send, keep).reshape(hidden, feature))

    owned = lambda v: jnp.pad(
        v.reshape(v.shape[0], devices, -1).transpose(1, 0, 2), ((0, 0), (0, 0), (0, LANES - v.shape[1] // devices))
    )
    narrow = jnp.concatenate([sums_one[:2], sums_two[:3]])
    biases = bias_sums[:4].reshape(2, 2 * feature)
    blocks = weight_sums.reshape(2, devices, 2 * share, LANES).transpose(1, 0, 2, 3).reshape(devices, 4 * share, LANES)
    packet = jnp.concatenate([blocks, owned(narrow), owned(biases), owned(bias_grad)], axis=1)
    result = scatter_small(packet, me, devices, count, 8)
    row = lambda k, width: result[4 * share + k, :width]
    return (
        mixed.reshape(tokens.shape),
        grad_tokens.reshape(tokens.shape),
        row(0, share),
        row(1, share),
        result[: 2 * share, :block],
        row(5, 2 * share),
        result[2 * share : 4 * share, :block],
        row(6, 2 * share),
        row(2, share),
        row(3, share),
        grad_w_up.reshape(share, hidden),
        row(7, bias_grad.shape[1] // devices),
        grad_w_down,
        row(4, share),
    )


def solution(mesh):
    placed = P(AXES)
    return jax.shard_map(
        on_device, mesh=mesh, in_specs=(placed,) * 16, out_specs=(placed,) * 14, check_vma=False
    )
```

```python
import functools
import math

import jax
import jax.numpy as jnp
import numpy as np
from jax import lax
from jax.experimental import pallas as pl
from jax.experimental.pallas import tpu as pltpu
from jax.sharding import PartitionSpec as P

BF = jnp.bfloat16
F32 = jnp.float32
BLOCKS = 8
EPS = 1e-05
SHRINK = 0.01
ROWS = 32
COLS = 64
KEPT = COLS // 2
GROUP = 4
STEPS = ROWS // GROUP
CELLS = GROUP * COLS
MODES = (KEPT + 1) * ROWS
HEAD = (GROUP + 1) * ROWS
BODY = GROUP * ROWS
LANES = 128
C1 = math.sqrt(2.0 / math.pi)
C3 = 0.044715
UNITS = 16
VMEM_LIMIT = 60 * 1024 * 1024


def table_parts(values):
    high = values.astype(np.float32).astype(jnp.bfloat16)
    low = (values - high.astype(np.float64)).astype(np.float32).astype(jnp.bfloat16)
    return np.stack([high, low])


def wave_matrices():
    scale = 1.0 / math.sqrt(ROWS * COLS)
    w = np.arange(COLS)
    first = np.zeros((KEPT, 2, GROUP, GROUP, COLS))
    for k in range(KEPT):
        for h in range(GROUP):
            if k == 0:
                first[k, 0, h, h] = scale
                first[k, 1, h, h] = scale * np.where(w % 2 == 0, 1.0, -1.0)
            else:
                first[k, 0, h, h] = scale * np.cos(2 * np.pi * (k * w % COLS) / COLS)
                first[k, 1, h, h] = -scale * np.sin(2 * np.pi * (k * w % COLS) / COLS)
    first = first.reshape(CELLS, CELLS)
    p = np.arange(ROWS)
    turn = 2 * np.pi * (np.outer(p, p) % ROWS) / ROWS
    cos = np.cos(turn).reshape(ROWS, STEPS, GROUP)
    sin = np.sin(turn).reshape(ROWS, STEPS, GROUP)
    body = np.zeros((2, GROUP, ROWS, GROUP, STEPS, 2, GROUP))
    head = np.zeros((2, GROUP + 1, ROWS, GROUP, STEPS, 2, GROUP))
    for k in range(GROUP):
        body[0, k, :, k, :, 0] = cos
        body[0, k, :, k, :, 1] = sin
        body[1, k, :, k, :, 1] = cos
        body[1, k, :, k, :, 0] = -sin
    head[:, 1:GROUP, :, 1:] = body[:, 1:, :, 1:]
    for place, part in ((0, 0), (GROUP, 1)):
        head[0, place, :, 0, :, part] = cos
        head[1, place, :, 0, :, part] = -sin
    weight = np.full((2, GROUP + 1, ROWS, 1), 2.0)
    weight[:, 0] = 1.0
    weight[:, GROUP] = 1.0
    head = head.reshape(2 * HEAD, 2 * BODY)
    body = body.reshape(2 * BODY, 2 * BODY)
    head_weighted = head * weight.reshape(2 * HEAD, 1)
    body_weighted = body * 2.0
    return {
        "first": table_parts(first),
        "first_t": table_parts(first.T),
        "head": table_parts(head),
        "body": table_parts(body),
        "head_t": table_parts(head.T),
        "body_t": table_parts(body.T),
        "head_w": table_parts(head_weighted),
        "body_w": table_parts(body_weighted),
        "head_wt": table_parts(head_weighted.T),
        "body_wt": table_parts(body_weighted.T),
    }


def mm(left, right, dims=(1, 0)):
    return lax.dot_general(
        left, right, (((dims[0],), (dims[1],)), ((), ())), preferred_element_type=F32
    )


def split(values):
    high = values.astype(BF)
    return high, (values - high.astype(F32)).astype(BF)


def turn(table, values):
    high, low = split(values)
    return mm(table[0], high) + mm(table[1], high) + mm(table[0], low)


def normalize(values):
    centred = values - jnp.mean(values, axis=-1, keepdims=True)
    inverse = lax.rsqrt(jnp.mean(centred * centred, axis=-1, keepdims=True) + EPS)
    return centred * inverse, inverse


def norm_back(grad, gain, normal, inverse):
    scaled = grad * gain
    return inverse * (
        scaled
        - jnp.mean(scaled, axis=-1, keepdims=True)
        - normal * jnp.mean(scaled * normal, axis=-1, keepdims=True)
    )


def gelu_parts(value):
    square = value * value
    half = 0.5 + 0.5 * jnp.tanh(value * (C1 + (C1 * C3) * square))
    active = value * half
    slope = half + active * (1.0 - half) * (2.0 * C1 + (6.0 * C1 * C3) * square)
    return active, slope


def gelu(value):
    square = value * value
    return value * (0.5 + 0.5 * jnp.tanh(value * (C1 + (C1 * C3) * square)))


def live_rows(start, count, rows_ref, cols_ref):
    cell = start + lax.broadcasted_iota(jnp.int32, (count, 1), 0)
    inside = (cell // COLS < rows_ref[0]) & (cell % COLS < cols_ref[0])
    return jnp.where(inside, 1.0, 0.0).astype(F32)


def spread(piece, per_device, me, bits):
    devices = piece.shape[0]
    total = devices * per_device
    lane = lax.broadcasted_iota(jnp.int32, (LANES, total), 0)
    place = lax.broadcasted_iota(jnp.int32, (LANES, total), 1)
    pick = jnp.where(place % per_device == lane, 1.0, 0.0).astype(BF)
    wide = mm(piece.astype(BF), pick)
    row = lax.broadcasted_iota(jnp.int32, (devices, 1), 0)
    owner = jnp.full((devices, 1), me, jnp.int32)
    for k, bit in enumerate(bits):
        owner = owner ^ (((row >> k) & 1) << bit)
    where = lax.broadcasted_iota(jnp.int32, (devices, total), 1) // per_device
    return jnp.sum(jnp.where(owner == where, wide, 0.0), axis=0, keepdims=True)


def place_of(mask, bits):
    return sum(((mask >> bit) & 1) << k for k, bit in enumerate(bits))


def any_space():
    return pl.BlockSpec(memory_space=pl.ANY)


def single(shape):
    return pl.BlockSpec(shape, lambda *_: (0,) * len(shape), pipeline_mode=pl.Buffered(1))


def smem():
    return pl.BlockSpec(memory_space=pltpu.SMEM)


def params(**more):
    return pltpu.CompilerParams(vmem_limit_bytes=VMEM_LIMIT, **more)


def cost(flops, moved):
    return pl.CostEstimate(flops=int(flops), bytes_accessed=int(moved), transcendentals=0)


def launch(deps, kernel, *, in_specs, **more):
    count = len(in_specs)

    def body(*refs):
        kernel(*refs[:count], *refs[count + len(deps) :])

    call = pl.pallas_call(body, in_specs=list(in_specs) + [any_space() for _ in deps], **more)
    return lambda *operands: call(*operands, *deps)


def to_mixed(real, imag):
    tiles = []
    for at in range(0, real.shape[1], LANES):
        tiles += [real[:, at : at + LANES], imag[:, at : at + LANES]]
    return jnp.concatenate(tiles, axis=1)


def from_mixed(values):
    cut = lambda at: values[:, at : at + LANES]
    real = [cut(at) for at in range(0, values.shape[1], 2 * LANES)]
    imag = [cut(at + LANES) for at in range(0, values.shape[1], 2 * LANES)]
    return jnp.concatenate(real, axis=1), jnp.concatenate(imag, axis=1)


def mix_product(values, matrix_ref, back=False):
    feature = values.shape[1] // 2
    wide = 2 * LANES
    groups = []
    for group in range(2):
        part = values[:, group * feature : (group + 1) * feature]
        count = feature // wide
        for t in range(count):
            begin, end = max(t - 1, 0) * wide, min(t + 2, count) * wide
            here = slice(t * wide, (t + 1) * wide)
            if back:
                groups.append(mm(part[:, begin:end], matrix_ref[group, here, begin:end], (1, 1)))
            else:
                groups.append(mm(part[:, begin:end], matrix_ref[group, begin:end, here]))
    return jnp.concatenate(groups, axis=1)


def first_kernel(rows_ref, cols_ref, tokens_ref, first_ref, half_ref):
    feature = tokens_ref.shape[1]
    normal, _ = normalize(tokens_ref[...].astype(F32))
    live = live_rows(pl.program_id(0) * CELLS, CELLS, rows_ref, cols_ref)
    half_ref[:, :, :feature] = turn(first_ref, normal * live).reshape(KEPT, 2 * GROUP, feature)
    ones = jnp.broadcast_to(live, (CELLS, LANES)).astype(BF)
    half_ref[:, :, feature:] = (mm(first_ref[0], ones) + mm(first_ref[1], ones)).reshape(KEPT, 2 * GROUP, LANES)


def first(rows, cols, tokens, tables, deps=()):
    cells, feature = tokens.shape
    table = tables["first"]
    return launch(
        deps,
        first_kernel,
        grid=(STEPS,),
        out_shape=jax.ShapeDtypeStruct((KEPT, 2 * ROWS, feature + LANES), F32),
        in_specs=[smem(), smem(), pl.BlockSpec((CELLS, feature), lambda i: (i, 0)), single(table.shape)],
        out_specs=pl.BlockSpec((KEPT, 2 * GROUP, feature + LANES), lambda i: (0, i, 0)),
        compiler_params=params(),
        cost_estimate=cost(6e9, 11e6),
        name="first",
    )(rows, cols, tokens, table)


def build_mix(me, bits, weights_ref, layer, out_ref, feature):
    block = feature // BLOCKS
    half = feature // 2
    per_group = BLOCKS // 2
    share = 2 * feature // weights_ref.shape[0]
    each = block // share
    out_ref[...] = jnp.zeros_like(out_ref)
    row = lax.broadcasted_iota(jnp.int32, (LANES, half), 0)
    column = lax.broadcasted_iota(jnp.int32, (LANES, half), 1)
    for b in range(per_group):
        shift = jnp.where((column - b * block == row) & (row < block), 1.0, 0.0).astype(BF)
        low, high = b * block, (b + 1) * block
        for group in range(2):
            for part in range(2):
                at = (part * BLOCKS + group * per_group + b) * each
                pieces = [
                    weights_ref[place_of((at + k) ^ me, bits), layer * share : (layer + 1) * share, :]
                    for k in range(each)
                ]
                placed = mm(jnp.concatenate(pieces, axis=0), shift).astype(BF)
                for t in range(low // LANES, (high - 1) // LANES + 1):
                    begin, end = max(low, t * LANES), min(high, (t + 1) * LANES)
                    for c in range(low // LANES, (high - 1) // LANES + 1):
                        piece = placed[begin - low : end - low, c * LANES : (c + 1) * LANES]
                        for up in range(2):
                            top = 2 * t * LANES + up * LANES + begin - t * LANES
                            left = (2 * c + (up ^ part)) * LANES
                            value = -piece if part == 1 and up == 1 else piece
                            here = (group, slice(top, top + end - begin), slice(left, left + LANES))
                            out_ref[here] = out_ref[here] + value


def mix_step(half_ref, head_ref, body_ref, back_head_ref, back_body_ref, mix1_ref, mix2_ref, wide_ref, long_ref,
             outs, heads, out_ref, is_head):
    feature = out_ref.shape[2]
    rows = HEAD if is_head else BODY
    spec = turn(head_ref if is_head else body_ref, half_ref[...].reshape(2 * BODY, feature + LANES))
    gain = wide_ref[0:1, :]
    shift = wide_ref[1:2, :]

    def scaled(part):
        flat = jnp.concatenate([part[:, feature:]] * (feature // LANES), axis=1)
        return (part[:, :feature] * gain + flat * shift).astype(BF)

    inside = to_mixed(scaled(spec[:rows]), scaled(spec[rows:]))
    active, slope = gelu_parts(mix_product(inside, mix1_ref) + long_ref[0:1, :])
    hidden = active.astype(BF)
    value = mix_product(hidden, mix2_ref) + long_ref[1:2, :]
    bend = jnp.tanh(value / SHRINK)
    for ref, head, kept in zip(outs, heads, (inside, hidden, slope, bend * bend)):
        ref[...] = kept[:BODY]
        if is_head:
            head[...] = kept[BODY:]
    values = jnp.concatenate(from_mixed(value - SHRINK * bend), axis=0)
    out_ref[...] = turn(back_head_ref if is_head else back_body_ref, values).reshape(GROUP, 2 * ROWS, feature)


def mix_first_kernel(
    weight_bits, vector_bits, me_ref, half_ref, weights_ref, vector_ref, head_ref, body_ref, back_head_ref, back_body_ref,
    out_ref, low_ref, hidden_ref, slope_ref, bend_ref, low_head_ref, hidden_head_ref, slope_head_ref, bend_head_ref,
    mix1_ref, mix2_ref, wide_ref, long_ref, up_ref,
):
    feature = out_ref.shape[2]
    devices = vector_ref.shape[1]
    share = feature // devices
    step = pl.program_id(0)
    outs = (low_ref, hidden_ref, slope_ref, bend_ref)
    heads = (low_head_ref, hidden_head_ref, slope_head_ref, bend_head_ref)
    work = functools.partial(
        mix_step, half_ref, head_ref, body_ref, back_head_ref, back_body_ref, mix1_ref, mix2_ref, wide_ref, long_ref,
        outs, heads, out_ref,
    )

    @pl.when(step == 0)
    def _():
        me = me_ref[0]
        build_mix(me, weight_bits, weights_ref, 0, mix1_ref, feature)
        build_mix(me, weight_bits, weights_ref, 1, mix2_ref, feature)
        wide_ref[...] = jnp.zeros_like(wide_ref)
        long_ref[...] = jnp.zeros_like(long_ref)
        for row, at in enumerate((2, 3, 4, 5, 7)):
            wide_ref[row : row + 1, :] = spread(vector_ref[at], share, me, vector_bits)
        for row in range(2):
            both = spread(vector_ref[row], 2 * share, me, vector_bits)
            long_ref[row : row + 1, :] = to_mixed(both[:, :feature], both[:, feature:])
        up_ref[...] = spread(vector_ref[6], up_ref.shape[1] // devices, me, vector_bits)
        work(True)

    @pl.when(step > 0)
    def _():
        work(False)


def mix_second_kernel(
    half_ref, mix1_ref, mix2_ref, wide_ref, long_ref, body_ref, back_body_ref,
    out_ref, low_ref, hidden_ref, slope_ref, bend_ref,
):
    mix_step(
        half_ref, None, body_ref, None, back_body_ref, mix1_ref, mix2_ref, wide_ref, long_ref,
        (low_ref, hidden_ref, slope_ref, bend_ref), (None,) * 4, out_ref, False,
    )


def mode_shapes(rows, feature):
    return [jax.ShapeDtypeStruct((rows, 2 * feature), kind) for kind in (BF, BF, F32, F32)]


def mode_blocks(feature):
    return [pl.BlockSpec((BODY, 2 * feature), lambda i: (i, 0)) for _ in range(4)]


def half_block(width, begin=0):
    return pl.BlockSpec((GROUP, 2 * ROWS, width), lambda i: (i + begin, 0, 0))


def mix_first(me, half, weights, vectors, tables, hidden, steps, weight_bits, vector_bits, deps=()):
    feature = half.shape[2] - LANES
    fixed = (weights, vectors, tables["head"], tables["body"], tables["head_wt"], tables["body_wt"])
    more = (
        jax.ShapeDtypeStruct((2, feature, feature), BF),
        jax.ShapeDtypeStruct((2, feature, feature), BF),
        jax.ShapeDtypeStruct((8, feature), F32),
        jax.ShapeDtypeStruct((8, 2 * feature), F32),
        jax.ShapeDtypeStruct((1, hidden), F32),
    )
    heads = mode_shapes(ROWS, feature)
    return launch(
        deps,
        functools.partial(mix_first_kernel, weight_bits, vector_bits),
        grid=(steps,),
        out_shape=[jax.ShapeDtypeStruct((GROUP * steps, 2 * ROWS, feature), F32)]
        + mode_shapes(BODY * steps, feature) + heads + list(more),
        in_specs=[smem(), half_block(feature + LANES)] + [single(v.shape) for v in fixed],
        out_specs=[half_block(feature)] + mode_blocks(feature) + [single(v.shape) for v in heads]
        + [single(v.shape) for v in more],
        compiler_params=params(),
        cost_estimate=cost(9e9, 20e6),
        name="mix_first",
    )(me, half, *fixed)


def mix_second(half, mix1, mix2, wide, long, tables, begin, steps, deps=()):
    feature = half.shape[2] - LANES
    fixed = (mix1, mix2, wide, long, tables["body"], tables["body_wt"])
    return launch(
        deps,
        mix_second_kernel,
        grid=(steps,),
        out_shape=[jax.ShapeDtypeStruct((GROUP * steps, 2 * ROWS, feature), F32)] + mode_shapes(BODY * steps, feature),
        in_specs=[half_block(feature + LANES, begin)] + [single(v.shape) for v in fixed],
        out_specs=[half_block(feature)] + mode_blocks(feature),
        compiler_params=params(),
        cost_estimate=cost(9e9, 20e6),
        name="mix_second",
    )(half, *fixed)


def space_kernel(rows_ref, cols_ref, half1_ref, half2_ref, tokens_ref, first_t_ref, wide_ref, middle_ref, normed_ref):
    feature = tokens_ref.shape[1]
    flat = lambda ref: ref[...].reshape(-1, feature)
    spatial = turn(first_t_ref, jnp.concatenate([flat(half1_ref), flat(half2_ref)], axis=0))
    inputs = tokens_ref[...].astype(F32)
    live = live_rows(pl.program_id(0) * CELLS, CELLS, rows_ref, cols_ref)
    normal, _ = normalize(inputs)
    middle = inputs + live * (spatial + (normal * wide_ref[0:1, :] + wide_ref[1:2, :]))
    middle_ref[...] = middle
    normal, _ = normalize(middle)
    normed_ref[...] = (normal * wide_ref[2:3, :] + wide_ref[3:4, :]).astype(BF)


def column_block(rows, width):
    return pl.BlockSpec((rows, 2 * GROUP, width), lambda i: (0, i, 0))


def space(rows, cols, half1, half2, tokens, wide, tables, deps=()):
    cells, feature = tokens.shape
    table = tables["first_t"]
    block = pl.BlockSpec((CELLS, feature), lambda i: (i, 0))
    return launch(
        deps,
        space_kernel,
        grid=(STEPS,),
        out_shape=(jax.ShapeDtypeStruct((cells, feature), F32), jax.ShapeDtypeStruct((cells, feature), BF)),
        in_specs=[smem(), smem(), column_block(half1.shape[0], feature), column_block(half2.shape[0], feature),
                  block, single(table.shape), single(wide.shape)],
        out_specs=(block, block),
        compiler_params=params(),
        cost_estimate=cost(6e9, 20e6),
        name="space",
    )(rows, cols, half1, half2, tokens, table, wide)


def fetch_weights(me_ref, pieces, places, up_ref, down_ref, sems):
    count = pieces[0].shape[0] * 2
    chip = me_ref[0] // 2

    def copies(own, core):
        target = (up_ref, down_ref)[core]
        source = pieces[:2] if own else pieces[2:]
        for mask in range(count):
            at = places[core][mask]
            part = source[at // (count // 2)].at[at % (count // 2)]
            yield pltpu.make_async_copy(part, target.at[chip ^ mask], sems.at[core, mask])

    for core in range(2):
        @pl.when(me_ref[0] % 2 == core)
        def _():
            for copy in copies(True, core):
                copy.start()
            for copy in copies(False, 1 - core):
                copy.start()

    for core in range(2):
        for copy in copies(True, core):
            copy.wait()


def weight_scratch(pieces):
    chips, rows, feature = pieces[0].shape[0] * 2, pieces[0].shape[1], pieces[0].shape[2]
    return [
        pltpu.VMEM((chips, rows, feature), BF),
        pltpu.VMEM((chips, rows, feature), BF),
        pltpu.SemaphoreType.DMA((2, chips)),
    ]


def up_part(up_ref, j, feature):
    share = up_ref.shape[1] * feature // (up_ref.shape[0] * up_ref.shape[1])
    return up_ref[:, j * share : (j + 1) * share, :].reshape(feature, feature)


def down_part(down_ref, j, feature):
    share = down_ref.shape[1]
    each = feature // share
    return down_ref[j * each : (j + 1) * each].reshape(feature, feature)


def up_kernel(places, rows_ref, cols_ref, me_ref, normed_ref, grad_ref, bias_ref, *rest):
    pieces = rest[:4]
    active_ref, pre_ref, live_ref, bias_grad_ref, up_ref, down_ref, sems = rest[4:]
    tile, feature = normed_ref.shape
    step = pl.program_id(0)

    @pl.when(step == 0)
    def _():
        fetch_weights(me_ref, pieces, places, up_ref, down_ref, sems)
        bias_grad_ref[...] = jnp.zeros_like(bias_grad_ref)

    live = live_rows(step * tile, tile, rows_ref, cols_ref)
    branch = (grad_ref[...].astype(F32) * live).astype(BF)
    live_ref[...] = branch
    normed = normed_ref[...]
    for j in range(active_ref.shape[1] // feature):
        place = slice(j * feature, (j + 1) * feature)
        value = mm(normed, up_part(up_ref, j, feature)) + bias_ref[:, place]
        grad = mm(branch, down_part(down_ref, j, feature), (1, 1))
        active, slope = gelu_parts(value)
        active_ref[:, place] = active.astype(BF)
        low = (grad * slope).astype(BF)
        pre_ref[:, place] = low
        bias_grad_ref[:, place] += jnp.sum(low.astype(F32), axis=0, keepdims=True)


def feed_up(rows, cols, me, normed, grad, bias, pieces, places, tile=256, deps=()):
    cells, feature = normed.shape
    hidden = bias.shape[1]
    block = lambda width: pl.BlockSpec((tile, width), lambda i: (i, 0))
    return launch(
        deps,
        functools.partial(up_kernel, places),
        grid=(cells // tile,),
        out_shape=(
            jax.ShapeDtypeStruct((cells, hidden), BF),
            jax.ShapeDtypeStruct((cells, hidden), BF),
            jax.ShapeDtypeStruct((cells, feature), BF),
            jax.ShapeDtypeStruct((1, hidden), F32),
        ),
        in_specs=[smem(), smem(), smem(), block(feature), block(feature), single(bias.shape)]
        + [any_space() for _ in pieces],
        out_specs=(block(hidden), block(hidden), block(feature), pl.BlockSpec((1, hidden), lambda i: (0, 0))),
        scratch_shapes=weight_scratch(pieces),
        compiler_params=params(),
        cost_estimate=cost(4 * cells * feature * hidden, 40e6),
        name="feed_up",
    )(rows, cols, me, normed, grad, bias, *pieces)


def weight_grad_kernel(places, me_ref, active_ref, pre_ref, branch_ref, normed_ref, send_ref, keep_ref, stage_ref, sems):
    step = pl.program_id(0)
    steps = pl.num_programs(0) // 2
    feature = branch_ref.shape[1]
    chips, rows, _ = send_ref.shape
    each = feature // rows
    share = feature // chips

    def down_copies(j, target):
        for c in range(each):
            source = stage_ref.at[j, pl.ds(c * rows, rows)]
            yield pltpu.make_async_copy(source, target.at[places[1][j * each + c]], sems.at[j, c])

    def up_copies(j, target):
        for c in range(chips):
            source = stage_ref.at[steps + j, pl.ds(c * share, share)]
            there = target.at[places[0][c], pl.ds(j * share, share)]
            yield pltpu.make_async_copy(source, there, sems.at[steps + j, c])

    @pl.when(step < steps)
    def _():
        stage_ref[step] = mm(active_ref[...], branch_ref[...], (0, 0)).astype(BF)

    @pl.when(step >= steps)
    def _():
        stage_ref[step] = mm(normed_ref[...], pre_ref[...], (0, 0)).astype(BF)

    total = stage_ref.shape[0] // 2
    for j in range(total):
        for core in range(2):
            targets = (send_ref, keep_ref) if core == 0 else (keep_ref, send_ref)

            @pl.when((step == j) & (me_ref[0] % 2 == core))
            def _():
                for copy in down_copies(j, targets[0]):
                    copy.start()

            @pl.when((step == total + j) & (me_ref[0] % 2 == core))
            def _():
                for copy in up_copies(j, targets[1]):
                    copy.start()

    @pl.when(step == 2 * steps - 1)
    def _():
        for j in range(total):
            for copy in down_copies(j, send_ref):
                copy.wait()
            for copy in up_copies(j, send_ref):
                copy.wait()


def weight_grads(me, active, pre, branch, normed, places, deps=()):
    cells, hidden = active.shape
    feature = branch.shape[1]
    tiles = hidden // feature
    chips = UNITS
    shape = jax.ShapeDtypeStruct((chips, hidden // chips, feature), BF)
    return launch(
        deps,
        functools.partial(weight_grad_kernel, places),
        grid=(2 * tiles,),
        out_shape=(shape, shape),
        in_specs=[
            smem(),
            pl.BlockSpec((cells, feature), lambda i: (0, jnp.minimum(i, tiles - 1))),
            pl.BlockSpec((cells, feature), lambda i: (0, jnp.maximum(i - tiles, 0))),
            single(branch.shape), single(normed.shape),
        ],
        out_specs=(any_space(), any_space()),
        scratch_shapes=[
            pltpu.VMEM((2 * tiles, feature, feature), BF),
            pltpu.SemaphoreType.DMA((2 * tiles, chips)),
        ],
        compiler_params=params(),
        cost_estimate=cost(4 * cells * feature * hidden, 40e6),
        name="weight_grads",
    )(me, active, pre, branch, normed)


def down_kernel(places, begin, rows_ref, cols_ref, me_ref, active_ref, pre_ref, middle_ref, grad_ref, wide_ref,
                first_ref, *rest):
    pieces = rest[:4]
    old_sums_ref = rest[4] if begin else None
    mixed_ref, grad_middle_ref, half_ref, sums_ref, up_ref, down_ref, sems = rest[-7:]
    tile, feature = middle_ref.shape
    hidden = active_ref.shape[1]
    step = pl.program_id(0)

    @pl.when(step == 0)
    def _():
        fetch_weights(me_ref, pieces, places, up_ref, down_ref, sems)
        sums_ref[...] = old_sums_ref[...] if begin else jnp.zeros_like(sums_ref)

    live = live_rows((step + begin) * tile, tile, rows_ref, cols_ref)
    branch = mm(active_ref[...], down_ref[...].reshape(hidden, feature))
    grad_normed = jnp.zeros((tile, feature), F32)
    for j in range(hidden // feature):
        pre = pre_ref[:, j * feature : (j + 1) * feature]
        grad_normed = grad_normed + mm(pre, up_part(up_ref, j, feature), (1, 1))
    middle = middle_ref[...]
    mixed_ref[...] = (middle + live * (branch + wide_ref[4:5, :])).astype(BF)
    normal, inverse = normalize(middle)
    cotangent = grad_ref[...].astype(F32)
    grad_middle = cotangent + norm_back(grad_normed, wide_ref[2:3, :], normal, inverse)
    grad_middle_ref[...] = grad_middle
    half_ref[...] = turn(first_ref, grad_middle * live).reshape(half_ref.shape)
    sums_ref[0:1, :] += jnp.sum(grad_normed * normal, axis=0, keepdims=True)
    sums_ref[1:2, :] += jnp.sum(grad_normed, axis=0, keepdims=True)
    sums_ref[2:3, :] += jnp.sum((cotangent * live).astype(BF).astype(F32), axis=0, keepdims=True)


def feed_down(rows, cols, me, active, pre, middle, grad, wide, table, pieces, places, begin, steps, before=(), deps=()):
    cells, feature = middle.shape
    hidden = active.shape[1]
    block = lambda width: pl.BlockSpec((CELLS, width), lambda i: (i + begin, 0))
    operands = (rows, cols, me, active, pre, middle, grad, wide, table, *pieces)
    extra = ()
    aliases = {}
    if begin:
        extra = (before[3],) + tuple(before[:3])
        aliases = {len(operands) + 1 + k: k for k in range(3)}
    return launch(
        deps,
        functools.partial(down_kernel, places, begin),
        grid=(steps,),
        out_shape=(
            jax.ShapeDtypeStruct((cells, feature), BF),
            jax.ShapeDtypeStruct((cells, feature), F32),
            jax.ShapeDtypeStruct((KEPT, 2 * ROWS, feature), F32),
            jax.ShapeDtypeStruct((8, feature), F32),
        ),
        in_specs=[smem(), smem(), smem(), block(hidden), block(hidden), block(feature), block(feature),
                  single(wide.shape), single(table.shape)] + [any_space() for _ in pieces]
        + [single(v.shape) for v in extra[:1]] + [any_space() for _ in extra[1:]],
        out_specs=(block(feature), block(feature),
                   pl.BlockSpec((KEPT, 2 * GROUP, feature), lambda i: (0, i + begin, 0)), single((8, feature))),
        scratch_shapes=weight_scratch(pieces),
        input_output_aliases=aliases,
        compiler_params=params(),
        cost_estimate=cost(4 * CELLS * steps * feature * hidden, 25e6),
        name="feed_down_b" if begin else "feed_down_a",
    )(*operands, *extra)


def back_step(half_ref, head_ref, body_ref, back_head_ref, back_body_ref, mix1_ref, mix2_ref, ins, in_heads,
              outs, out_heads, out_ref, sums_ref, is_head):
    feature = out_ref.shape[2]
    rows = HEAD if is_head else BODY

    def read(k):
        if is_head:
            return jnp.concatenate([ins[k][...], in_heads[k][...]], axis=0)
        return ins[k][...]

    grad = turn(head_ref if is_head else body_ref, half_ref[...].reshape(2 * BODY, feature))
    grad_two = (to_mixed(grad[:rows], grad[rows:]) * read(1)).astype(BF)
    grad_one = (mix_product(grad_two, mix2_ref, True) * read(0)).astype(BF)
    grad_spec = mix_product(grad_one, mix1_ref, True)
    values = jnp.concatenate(from_mixed(grad_spec), axis=0)
    out_ref[...] = turn(back_head_ref if is_head else back_body_ref, values).reshape(GROUP, 2 * ROWS, feature)
    for row, value in enumerate((grad_one, grad_two)):
        outs[row][...] = value[:BODY]
        if is_head:
            out_heads[row][...] = value[BODY:]
        total = jnp.sum(value.astype(F32), axis=0, keepdims=True)
        sums_ref[row : row + 1, :] = total if is_head else sums_ref[row : row + 1, :] + total


def mix_back_kernel(
    half_ref, slope1_ref, slope2_ref, bend1_ref, bend2_ref, slope_head_ref, bend_head_ref, mix1_ref, mix2_ref,
    head_ref, body_ref, back_head_ref, back_body_ref,
    out_ref, one_ref, two_ref, one_head_ref, two_head_ref, sums_ref,
):
    step = pl.program_id(0)
    steps = pl.num_programs(0) // 2
    work = functools.partial(
        back_step, half_ref, head_ref, body_ref, back_head_ref, back_body_ref, mix1_ref, mix2_ref
    )
    more = ((slope_head_ref, bend_head_ref), (one_ref, two_ref), (one_head_ref, two_head_ref), out_ref, sums_ref)

    @pl.when(step == 0)
    def _():
        sums_ref[...] = jnp.zeros_like(sums_ref)
        work((slope1_ref, bend1_ref), *more, True)

    @pl.when((step > 0) & (step < steps))
    def _():
        work((slope1_ref, bend1_ref), *more, False)

    @pl.when(step >= steps)
    def _():
        work((slope2_ref, bend2_ref), *more, False)


def mix_back(half, slopes, bends, slope_head, bend_head, mix1, mix2, tables, deps=()):
    feature = half.shape[2]
    steps = KEPT // GROUP
    fixed = (slope_head, bend_head, mix1, mix2, tables["head_w"], tables["body_w"], tables["head_t"], tables["body_t"])
    near = pl.BlockSpec((BODY, 2 * feature), lambda i: (jnp.minimum(i, steps // 2 - 1), 0))
    far = pl.BlockSpec((BODY, 2 * feature), lambda i: (jnp.maximum(i - steps // 2, 0), 0))
    low = lambda rows: jax.ShapeDtypeStruct((rows, 2 * feature), BF)
    body = pl.BlockSpec((BODY, 2 * feature), lambda i: (i, 0))
    shapes = (
        jax.ShapeDtypeStruct((KEPT, 2 * ROWS, feature), F32), low(BODY * steps), low(BODY * steps),
        low(ROWS), low(ROWS), jax.ShapeDtypeStruct((8, 2 * feature), F32),
    )
    return launch(
        deps,
        mix_back_kernel,
        grid=(steps,),
        out_shape=shapes,
        in_specs=[half_block(feature), near, far, near, far] + [single(v.shape) for v in fixed],
        out_specs=[half_block(feature), body, body] + [single(v.shape) for v in shapes[3:]],
        compiler_params=params(),
        cost_estimate=cost(18e9, 30e6),
        name="mix_back",
    )(half, *slopes, *bends, *fixed)


def block_kernel(left1_ref, left2_ref, left_head_ref, right_ref, right_head_ref, out_ref, natural_ref):
    wide = 2 * LANES
    count = left1_ref.shape[1] // wide
    cut = left1_ref.shape[0]
    for t in range(count):
        for c in range(max(t - 1, 0), min(t + 2, count)):
            left, right = slice(t * wide, (t + 1) * wide), slice(c * wide, (c + 1) * wide)
            total = (
                mm(left1_ref[:, left], right_ref[:cut, right], (0, 0))
                + mm(left2_ref[:, left], right_ref[cut:, right], (0, 0))
                + mm(left_head_ref[:, left], right_head_ref[:, right], (0, 0))
            )
            rows, lanes = slice(t * LANES, (t + 1) * LANES), slice(c * LANES, (c + 1) * LANES)
            natural_ref[0, rows, lanes] = total[:LANES, :LANES] + total[LANES:, LANES:]
            natural_ref[1, rows, lanes] = total[:LANES, LANES:] - total[LANES:, :LANES]
    per_group = BLOCKS // 2
    block = count * LANES // per_group
    for b in range(per_group):
        begin = b * block
        base = begin // LANES * LANES
        reach = min(base + wide, count * LANES) - base
        for part in range(2):
            piece = natural_ref[part, begin : begin + block, base : base + reach]
            if begin > base:
                piece = pltpu.roll(piece, reach - (begin - base), axis=1)
            out_ref[part, b * block : (b + 1) * block, :] = piece[:, :LANES]


def block_grads(left1, left2, left_head, right, right_head, name, deps=()):
    feature = left1.shape[1] // 2
    half = feature // 2
    block = lambda v: pl.BlockSpec((v.shape[0], feature), lambda i: (0, i))
    return launch(
        deps,
        block_kernel,
        grid=(2,),
        out_shape=jax.ShapeDtypeStruct((2, feature, LANES), F32),
        in_specs=[block(v) for v in (left1, left2, left_head, right, right_head)],
        out_specs=pl.BlockSpec((2, half, LANES), lambda i: (0, i, 0)),
        scratch_shapes=[pltpu.VMEM((2, half, half), F32)],
        compiler_params=params(),
        cost_estimate=cost(5e9, 7e6),
        name=name,
    )(left1, left2, left_head, right, right_head)


def last_kernel(rows_ref, cols_ref, half_ref, tokens_ref, grad_ref, first_t_ref, wide_ref, out_ref, sums_ref):
    tile, feature = tokens_ref.shape
    step = pl.program_id(0)
    live = live_rows(step * tile, tile, rows_ref, cols_ref)
    grad_middle = grad_ref[...]
    grad_normed = live * (grad_middle + turn(first_t_ref, half_ref[...].reshape(CELLS, feature)))
    normal, inverse = normalize(tokens_ref[...].astype(F32))
    out_ref[...] = grad_middle + norm_back(grad_normed, wide_ref[0:1, :], normal, inverse)

    @pl.when(step == 0)
    def _():
        sums_ref[...] = jnp.zeros_like(sums_ref)

    sums_ref[0:1, :] += jnp.sum(grad_normed * normal, axis=0, keepdims=True)
    sums_ref[1:2, :] += jnp.sum(grad_normed, axis=0, keepdims=True)


def last(rows, cols, half, tokens, grad, wide, tables, deps=()):
    cells, feature = tokens.shape
    first_t = tables["first_t"]
    block = pl.BlockSpec((CELLS, feature), lambda i: (i, 0))
    return launch(
        deps,
        last_kernel,
        grid=(STEPS,),
        out_shape=(jax.ShapeDtypeStruct((cells, feature), F32), jax.ShapeDtypeStruct((8, feature), F32)),
        in_specs=[smem(), smem(), column_block(KEPT, feature), block, block, single(first_t.shape), single(wide.shape)],
        out_specs=(block, single((8, feature))),
        compiler_params=params(),
        cost_estimate=cost(6e9, 20e6),
        name="last",
    )(rows, cols, half, tokens, grad, first_t, wide)


AXES = ("dp", "fsdp")


def swap(value, devices, bits):
    return lax.ppermute(value, AXES, [(i, i ^ (1 << bits[i & 1])) for i in range(devices)])


def doubling_orders(count):
    first = list(range(count - 1, 0, -1))
    second = list(first)
    for k in range(0, len(second) - 1, 2):
        second[k], second[k + 1] = second[k + 1], second[k]
    return first, second


def places_of(order):
    return [
        sum(1 << k for k, bit in enumerate(order) if mask >> (bit - 1) & 1) for mask in range(1 << len(order))
    ]


def pair_kernel(held_ref, got_ref, out_ref, sems):
    count = held_ref.shape[0]
    copies = [
        pltpu.make_async_copy(source, out_ref.at[pl.ds(k * count, count)], sems.at[k])
        for k, source in enumerate((held_ref, got_ref))
    ]
    for copy in copies:
        copy.start()
    for copy in copies:
        copy.wait()


def pair(held, got, deps=()):
    return launch(
        deps,
        pair_kernel,
        out_shape=jax.ShapeDtypeStruct((2 * held.shape[0],) + held.shape[1:], held.dtype),
        in_specs=[any_space(), any_space()],
        out_specs=any_space(),
        scratch_shapes=[pltpu.SemaphoreType.DMA((2,))],
        compiler_params=params(),
        cost_estimate=cost(0, 4 * held.size * 2),
        name="pair",
    )(held, got)


def gather_small(value, me, devices, count):
    held = value[None]
    for bit in list(range(3, count)) + [2, 1, 0]:
        other = swap(held, devices, (bit, bit))
        upper = (me >> bit) & 1
        axis = 0 if bit > 2 else 1
        join_two = lambda a, b: jnp.stack([a, b], axis=axis).reshape((-1,) + value.shape)
        held = jnp.where(upper == 0, join_two(held, other), join_two(other, held))
    return held


def scatter_small(value, me, devices, count, exact):
    shape = value.shape[1:]
    rows = shape[0]
    total = value
    for bit in [0, 1, 2] + list(range(count - 1, 2, -1)):
        upper = (me >> bit) & 1
        axis = 0 if bit > 2 else 1
        pair = total.reshape(((2, -1) if bit > 2 else (-1, 2)) + shape)
        away = lax.dynamic_index_in_dim(pair, 1 - upper, axis, keepdims=False)
        keep = lax.dynamic_index_in_dim(pair, upper, axis, keepdims=False)
        sums = away[:, rows - exact :]
        top = lax.reduce_precision(sums, 8, 7)
        packet = jnp.concatenate([away[:, : rows - exact], top, sums - top], axis=1).astype(BF)
        got = swap(packet, devices, (bit, bit)).astype(F32)
        low = got[:, rows - exact : rows] + got[:, rows:]
        total = keep + jnp.concatenate([got[:, : rows - exact], low], axis=1)
    return total[0]


def chip_unit(up, down, core, devices):
    parts, share, feature = up.shape
    flat = up.reshape(parts * share, feature)
    other = swap(jnp.where(core == 0, down, flat), devices, (0, 0))
    up_unit = jnp.concatenate([up, other.reshape(up.shape)], axis=1).reshape(2 * parts * share, feature)
    return jnp.where(core == 0, up_unit, jnp.concatenate([other, down]))[None]


def fold_kernel(upper_ref, keep_away_ref, got_away_ref, keep_own_ref, got_own_ref, send_ref, keep_ref):
    send_ref[...] = (keep_away_ref[...].astype(F32) + got_away_ref[...].astype(F32)).astype(BF)
    keep_ref[...] = (keep_own_ref[...].astype(F32) + got_own_ref[...].astype(F32)).astype(BF)


def fold(keep, got, upper, deps=()):
    half = keep.shape[0] // 2
    unit = (1,) + keep.shape[1:]
    count = len(deps)
    away = pl.BlockSpec(unit, lambda i, up: ((1 - up[0]) * half + i, 0, 0))
    own = pl.BlockSpec(unit, lambda i, up: (up[0] * half + i, 0, 0))
    out = pl.BlockSpec(unit, lambda i, up: (i, 0, 0))
    shape = jax.ShapeDtypeStruct((half,) + keep.shape[1:], BF)

    def body(*refs):
        fold_kernel(*refs[:5], *refs[5 + count :])

    return pl.pallas_call(
        body,
        grid_spec=pltpu.PrefetchScalarGridSpec(
            num_scalar_prefetch=1,
            grid=(half,),
            in_specs=[away, away, own, own] + [any_space() for _ in deps],
            out_specs=[out, out],
        ),
        out_shape=(shape, shape),
        compiler_params=params(),
        cost_estimate=cost(0, 6 * half * keep[0].size),
        name="fold",
    )(upper, keep, got, keep, got, *deps)


def on_device(
    tokens, grad_out, region_rows, region_cols, ln1_gain, ln1_bias, spec_w1, spec_b1, spec_w2, spec_b2,
    ln2_gain, ln2_bias, w_up, up_bias, w_down, down_bias,
):
    devices = lax.axis_size(AXES[0]) * lax.axis_size(AXES[1])
    count = devices.bit_length() - 1
    me = lax.axis_index(AXES).astype(jnp.int32)
    core = me & 1
    me_one = me.reshape(1)
    feature = tokens.shape[-1]
    block = feature // BLOCKS
    share = ln1_gain.shape[0]
    cells = tokens.shape[1] * tokens.shape[2]
    hidden = w_up.shape[1]
    parts = hidden // feature
    tables = {name: jnp.asarray(value) for name, value in wave_matrices().items()}
    orders = doubling_orders(count)
    places = tuple(places_of(order) for order in orders)
    flat_tokens = tokens.reshape(cells, feature)
    flat_grad = grad_out.reshape(cells, feature)
    fast = devices // 2 == UNITS
    step = lambda value, k: swap(value, devices, (orders[0][k], orders[1][k]))

    padded = lambda v: jnp.pad(v, ((0, 0), (0, LANES - v.shape[1])))
    vectors = (spec_b1, spec_b2, ln1_gain, ln1_bias, ln2_gain, ln2_bias, up_bias, down_bias)
    small = jnp.concatenate([padded(spec_w1), padded(spec_w2)] + [padded(v[None]) for v in vectors])
    if fast:
        own_up = w_up.reshape(share, parts, feature).transpose(1, 0, 2)
        unit = chip_unit(own_up, w_down, core, devices)
        bits = tuple(range(3, count)) + (2, 1, 0)
        meet = lambda value, k: swap(value, devices, (bits[k], bits[k]))
        small = pair(small[None], meet(small[None], 0))
        half = first(region_rows, region_cols, flat_tokens, tables, deps=(unit, small))
        near = pair(unit, step(unit, 0), deps=(half,))
        small = pair(small, meet(small, 1), deps=(near,))
        for k in range(2, count):
            small = pair(small, meet(small, k))
        near = pair(near, step(near, 1), deps=(small,))
        weights, weight_bits, vector_bits, me_small = small, bits, bits, me_one
    else:
        up = lax.all_gather(w_up, AXES, axis=0, tiled=True)
        up = up.reshape(UNITS, feature // UNITS, parts, feature).transpose(0, 2, 1, 3).reshape(UNITS, -1, feature)
        down = lax.all_gather(w_down, AXES, axis=0, tiled=True).reshape(UNITS, -1, feature)
        pieces = tuple(
            jnp.where(core == 0, one, two)[begin : begin + UNITS // 2]
            for one, two in ((up, down), (down, up))
            for begin in (0, UNITS // 2)
        )
        me_one = core.reshape(1)
        me_small = jnp.zeros_like(me_one)
        places = (tuple(range(UNITS)),) * 2
        small = gather_small(small, me, devices, count)
        weights = small[:, : 4 * share].reshape(devices, 2, 2 * share, LANES).transpose(1, 0, 2, 3)
        weights = weights.reshape(2, 2 * UNITS, -1, LANES).transpose(1, 0, 2, 3).reshape(2 * UNITS, -1, LANES)
        weight_bits, vector_bits = tuple(range(5)), tuple(range(count))
        half = first(region_rows, region_cols, flat_tokens, tables)
    vectors = small[:, 4 * share :].transpose(1, 0, 2).astype(F32)

    steps = KEPT // GROUP
    made = mix_first(
        me_small, half, weights, vectors, tables, hidden, steps // 2, weight_bits, vector_bits,
        deps=(near,) if fast else (),
    )
    half1, modes1, heads, (mix1, mix2, wide, long, up_shift) = made[0], made[1:5], made[5:9], made[9:]
    if fast:
        near = pair(near, step(near, 2), deps=(half1,))
        far = step(near, 3)
        pieces = (near, far, swap(near, devices, (0, 0)), swap(far, devices, (0, 0)))
    made = mix_second(
        half, mix1, mix2, wide, long, tables, steps // 2, steps // 2, deps=(near,) if fast else ()
    )
    half2, modes2 = made[0], made[1:5]
    middle, normed = space(region_rows, region_cols, half1, half2, flat_tokens, wide, tables)
    active, pre, branch, bias_grad = feed_up(
        region_rows, region_cols, me_one, normed, flat_grad, up_shift, pieces, places
    )
    send, keep = weight_grads(me_one, active, pre, branch, normed, places)
    down_args = (me_one, active, pre, middle, flat_grad, wide, tables["first"], pieces, places)
    tiles = cells // CELLS
    made = feed_down(region_rows, region_cols, *down_args, 0, tiles // 2, deps=(send,))
    deps = ()
    if fast:
        ranks = [((me >> jnp.where(core == 0, *bit)) & 1).reshape(1) for bit in zip(*orders)]
        send, keep = fold(keep, swap(send, devices, (0, 0)), ranks[3], deps=(made[3],))
        deps = (send,)
    made = feed_down(region_rows, region_cols, *down_args, tiles // 2, tiles // 2, made, deps=deps)
    mixed, grad_middle, half_back, sums_two = made
    made = mix_back(
        half_back, (modes1[2], modes2[2]), (modes1[3], modes2[3]), heads[2], heads[3], mix1, mix2, tables
    )
    half_back, one, two, one_head, two_head, bias_sums = made
    if fast:
        send, keep = fold(keep, step(send, 3), ranks[2], deps=(bias_sums,))
        deps = (send,)
    grad_two = block_grads(modes1[1], modes2[1], heads[1], two, two_head, "grad_mix2", deps=deps)
    grad_one = block_grads(modes1[0], modes2[0], heads[0], one, one_head, "grad_mix1", deps=deps)
    if fast:
        send, keep = fold(keep, step(send, 2), ranks[1], deps=(grad_one, grad_two))
        deps = (send,)
    grad_tokens, sums_one = last(
        region_rows, region_cols, half_back, flat_tokens, grad_middle, wide, tables, deps=deps
    )

    if fast:
        send, keep = fold(keep, step(send, 1), ranks[0])
        total = keep[0].astype(F32) + step(send, 0)[0].astype(F32)
        up_all = total.reshape(parts, 2 * share, feature)
        lower = up_all[:, :share].reshape(parts * share, feature)
        upper = up_all[:, share:].reshape(parts * share, feature)
        each = parts * share
        other = swap(jnp.where(core == 0, upper, total[:each]), devices, (0, 0))
        grad_w_up = jnp.where(core == 0, lower, other).reshape(parts, share, feature).transpose(1, 0, 2)
        grad_w_down = jnp.where(core == 0, other, total[each:])
    else:
        scatter = lambda v: lax.psum_scatter(v.astype(F32), AXES, scatter_dimension=0, tiled=True)
        up = jnp.where(core == 0, keep, send).reshape(UNITS, parts, feature // UNITS, feature)
        grad_w_up = scatter(up.transpose(0, 2, 1, 3).reshape(feature, hidden))
        grad_w_down = scatter(jnp.where(core == 0, send, keep).reshape(hidden, feature))

    owned = lambda v: jnp.pad(
        v.reshape(v.shape[0], devices, -1).transpose(1, 0, 2), ((0, 0), (0, 0), (0, LANES - v.shape[1] // devices))
    )
    narrow = jnp.concatenate([sums_one[:2], sums_two[:3]])
    biases = bias_sums[:2].reshape(2, feature // LANES, 2, LANES).transpose(0, 2, 1, 3).reshape(2, 2 * feature)
    blocks = [v.reshape(devices, 2 * share, LANES) for v in (grad_one, grad_two)]
    packet = jnp.concatenate(blocks + [owned(narrow), owned(biases), owned(bias_grad)], axis=1)
    result = scatter_small(packet, me, devices, count, 8)
    row = lambda k, width: result[4 * share + k, :width]
    return (
        mixed.reshape(tokens.shape),
        grad_tokens.reshape(tokens.shape),
        row(0, share),
        row(1, share),
        result[: 2 * share, :block],
        row(5, 2 * share),
        result[2 * share : 4 * share, :block],
        row(6, 2 * share),
        row(2, share),
        row(3, share),
        grad_w_up.reshape(share, hidden),
        row(7, bias_grad.shape[1] // devices),
        grad_w_down,
        row(4, share),
    )


def solution(mesh):
    placed = P(AXES)
    return jax.shard_map(
        on_device, mesh=mesh, in_specs=(placed,) * 16, out_specs=(placed,) * 14, check_vma=False
    )
```

```python
import functools
import math

import jax
import jax.numpy as jnp
import numpy as np
from jax import lax
from jax.experimental import pallas as pl
from jax.experimental.pallas import tpu as pltpu
from jax.sharding import PartitionSpec as P

BF = jnp.bfloat16
F32 = jnp.float32
BLOCKS = 8
EPS = 1e-05
SHRINK = 0.01
ROWS = 32
COLS = 64
KEPT = COLS // 2
GROUP = 4
STEPS = ROWS // GROUP
CELLS = GROUP * COLS
MODES = (KEPT + 1) * ROWS
HEAD = (GROUP + 1) * ROWS
BODY = GROUP * ROWS
LANES = 128
C1 = math.sqrt(2.0 / math.pi)
C3 = 0.044715
UNITS = 16
VMEM_LIMIT = 60 * 1024 * 1024


def table_parts(values):
    high = values.astype(np.float32).astype(jnp.bfloat16)
    low = (values - high.astype(np.float64)).astype(np.float32).astype(jnp.bfloat16)
    return np.stack([high, low])


def wave_matrices():
    scale = 1.0 / math.sqrt(ROWS * COLS)
    w = np.arange(COLS)
    first = np.zeros((KEPT, 2, GROUP, GROUP, COLS))
    for k in range(KEPT):
        for h in range(GROUP):
            if k == 0:
                first[k, 0, h, h] = scale
                first[k, 1, h, h] = scale * np.where(w % 2 == 0, 1.0, -1.0)
            else:
                first[k, 0, h, h] = scale * np.cos(2 * np.pi * (k * w % COLS) / COLS)
                first[k, 1, h, h] = -scale * np.sin(2 * np.pi * (k * w % COLS) / COLS)
    first = first.reshape(CELLS, CELLS)
    p = np.arange(ROWS)
    turn = 2 * np.pi * (np.outer(p, p) % ROWS) / ROWS
    cos = np.cos(turn).reshape(ROWS, STEPS, GROUP)
    sin = np.sin(turn).reshape(ROWS, STEPS, GROUP)
    body = np.zeros((2, GROUP, ROWS, GROUP, STEPS, 2, GROUP))
    head = np.zeros((2, GROUP + 1, ROWS, GROUP, STEPS, 2, GROUP))
    for k in range(GROUP):
        body[0, k, :, k, :, 0] = cos
        body[0, k, :, k, :, 1] = sin
        body[1, k, :, k, :, 1] = cos
        body[1, k, :, k, :, 0] = -sin
    head[:, 1:GROUP, :, 1:] = body[:, 1:, :, 1:]
    for place, part in ((0, 0), (GROUP, 1)):
        head[0, place, :, 0, :, part] = cos
        head[1, place, :, 0, :, part] = -sin
    weight = np.full((2, GROUP + 1, ROWS, 1), 2.0)
    weight[:, 0] = 1.0
    weight[:, GROUP] = 1.0
    head = head.reshape(2 * HEAD, 2 * BODY)
    body = body.reshape(2 * BODY, 2 * BODY)
    head_weighted = head * weight.reshape(2 * HEAD, 1)
    body_weighted = body * 2.0
    return {
        "first": table_parts(first),
        "first_t": table_parts(first.T),
        "head": table_parts(head),
        "body": table_parts(body),
        "head_t": table_parts(head.T),
        "body_t": table_parts(body.T),
        "head_w": table_parts(head_weighted),
        "body_w": table_parts(body_weighted),
        "head_wt": table_parts(head_weighted.T),
        "body_wt": table_parts(body_weighted.T),
    }


def mm(left, right, dims=(1, 0)):
    return lax.dot_general(
        left, right, (((dims[0],), (dims[1],)), ((), ())), preferred_element_type=F32
    )


def split(values):
    high = values.astype(BF)
    return high, (values - high.astype(F32)).astype(BF)


def turn(table, values):
    high, low = split(values)
    return mm(table[0], high) + mm(table[1], high) + mm(table[0], low)


def normalize(values):
    centred = values - jnp.mean(values, axis=-1, keepdims=True)
    inverse = lax.rsqrt(jnp.mean(centred * centred, axis=-1, keepdims=True) + EPS)
    return centred * inverse, inverse


def norm_back(grad, gain, normal, inverse):
    scaled = grad * gain
    return inverse * (
        scaled
        - jnp.mean(scaled, axis=-1, keepdims=True)
        - normal * jnp.mean(scaled * normal, axis=-1, keepdims=True)
    )


def gelu_parts(value):
    square = value * value
    half = 0.5 + 0.5 * jnp.tanh(value * (C1 + (C1 * C3) * square))
    active = value * half
    slope = half + active * (1.0 - half) * (2.0 * C1 + (6.0 * C1 * C3) * square)
    return active, slope


def gelu(value):
    square = value * value
    return value * (0.5 + 0.5 * jnp.tanh(value * (C1 + (C1 * C3) * square)))


def live_rows(start, count, rows_ref, cols_ref):
    cell = start + lax.broadcasted_iota(jnp.int32, (count, 1), 0)
    inside = (cell // COLS < rows_ref[0]) & (cell % COLS < cols_ref[0])
    return jnp.where(inside, 1.0, 0.0).astype(F32)


def spread(piece, per_device, me, bits):
    devices = piece.shape[0]
    total = devices * per_device
    lane = lax.broadcasted_iota(jnp.int32, (LANES, total), 0)
    place = lax.broadcasted_iota(jnp.int32, (LANES, total), 1)
    pick = jnp.where(place % per_device == lane, 1.0, 0.0).astype(BF)
    wide = mm(piece.astype(BF), pick)
    row = lax.broadcasted_iota(jnp.int32, (devices, 1), 0)
    owner = jnp.full((devices, 1), me, jnp.int32)
    for k, bit in enumerate(bits):
        owner = owner ^ (((row >> k) & 1) << bit)
    where = lax.broadcasted_iota(jnp.int32, (devices, total), 1) // per_device
    return jnp.sum(jnp.where(owner == where, wide, 0.0), axis=0, keepdims=True)


def place_of(mask, bits):
    return sum(((mask >> bit) & 1) << k for k, bit in enumerate(bits))


def any_space():
    return pl.BlockSpec(memory_space=pl.ANY)


def single(shape):
    return pl.BlockSpec(shape, lambda *_: (0,) * len(shape), pipeline_mode=pl.Buffered(1))


def smem():
    return pl.BlockSpec(memory_space=pltpu.SMEM)


def params(**more):
    return pltpu.CompilerParams(vmem_limit_bytes=VMEM_LIMIT, **more)


def cost(flops, moved):
    return pl.CostEstimate(flops=int(flops), bytes_accessed=int(moved), transcendentals=0)


def launch(deps, kernel, *, in_specs, **more):
    count = len(in_specs)

    def body(*refs):
        kernel(*refs[:count], *refs[count + len(deps) :])

    call = pl.pallas_call(body, in_specs=list(in_specs) + [any_space() for _ in deps], **more)
    return lambda *operands: call(*operands, *deps)


def to_mixed(real, imag):
    tiles = []
    for at in range(0, real.shape[1], LANES):
        tiles += [real[:, at : at + LANES], imag[:, at : at + LANES]]
    return jnp.concatenate(tiles, axis=1)


def from_mixed(values):
    cut = lambda at: values[:, at : at + LANES]
    real = [cut(at) for at in range(0, values.shape[1], 2 * LANES)]
    imag = [cut(at + LANES) for at in range(0, values.shape[1], 2 * LANES)]
    return jnp.concatenate(real, axis=1), jnp.concatenate(imag, axis=1)


def mix_product(values, matrix_ref, back=False):
    feature = values.shape[1] // 2
    wide = 2 * LANES
    groups = []
    for group in range(2):
        part = values[:, group * feature : (group + 1) * feature]
        count = feature // wide
        for t in range(count):
            begin, end = max(t - 1, 0) * wide, min(t + 2, count) * wide
            here = slice(t * wide, (t + 1) * wide)
            if back:
                groups.append(mm(part[:, begin:end], matrix_ref[group, here, begin:end], (1, 1)))
            else:
                groups.append(mm(part[:, begin:end], matrix_ref[group, begin:end, here]))
    return jnp.concatenate(groups, axis=1)


def first_kernel(rows_ref, cols_ref, tokens_ref, first_ref, half_ref):
    feature = tokens_ref.shape[1]
    normal, _ = normalize(tokens_ref[...].astype(F32))
    live = live_rows(pl.program_id(0) * CELLS, CELLS, rows_ref, cols_ref)
    half_ref[:, :, :feature] = turn(first_ref, normal * live).reshape(KEPT, 2 * GROUP, feature)
    ones = jnp.broadcast_to(live, (CELLS, LANES)).astype(BF)
    half_ref[:, :, feature:] = (mm(first_ref[0], ones) + mm(first_ref[1], ones)).reshape(KEPT, 2 * GROUP, LANES)


def first(rows, cols, tokens, tables, deps=()):
    cells, feature = tokens.shape
    table = tables["first"]
    return launch(
        deps,
        first_kernel,
        grid=(STEPS,),
        out_shape=jax.ShapeDtypeStruct((KEPT, 2 * ROWS, feature + LANES), F32),
        in_specs=[smem(), smem(), pl.BlockSpec((CELLS, feature), lambda i: (i, 0)), single(table.shape)],
        out_specs=pl.BlockSpec((KEPT, 2 * GROUP, feature + LANES), lambda i: (0, i, 0)),
        compiler_params=params(),
        cost_estimate=cost(6e9, 11e6),
        name="first",
    )(rows, cols, tokens, table)


def build_mix(me, bits, weights_ref, layer, out_ref, feature):
    block = feature // BLOCKS
    half = feature // 2
    per_group = BLOCKS // 2
    share = 2 * feature // weights_ref.shape[0]
    each = block // share
    out_ref[...] = jnp.zeros_like(out_ref)
    row = lax.broadcasted_iota(jnp.int32, (LANES, half), 0)
    column = lax.broadcasted_iota(jnp.int32, (LANES, half), 1)
    for b in range(per_group):
        shift = jnp.where((column - b * block == row) & (row < block), 1.0, 0.0).astype(BF)
        low, high = b * block, (b + 1) * block
        for group in range(2):
            for part in range(2):
                at = (part * BLOCKS + group * per_group + b) * each
                pieces = [
                    weights_ref[place_of((at + k) ^ me, bits), layer * share : (layer + 1) * share, :]
                    for k in range(each)
                ]
                placed = mm(jnp.concatenate(pieces, axis=0), shift).astype(BF)
                for t in range(low // LANES, (high - 1) // LANES + 1):
                    begin, end = max(low, t * LANES), min(high, (t + 1) * LANES)
                    for c in range(low // LANES, (high - 1) // LANES + 1):
                        piece = placed[begin - low : end - low, c * LANES : (c + 1) * LANES]
                        for up in range(2):
                            top = 2 * t * LANES + up * LANES + begin - t * LANES
                            left = (2 * c + (up ^ part)) * LANES
                            value = -piece if part == 1 and up == 1 else piece
                            here = (group, slice(top, top + end - begin), slice(left, left + LANES))
                            out_ref[here] = out_ref[here] + value


def mix_step(half_ref, head_ref, body_ref, back_head_ref, back_body_ref, mix1_ref, mix2_ref, wide_ref, long_ref,
             outs, heads, out_ref, is_head):
    feature = out_ref.shape[2]
    rows = HEAD if is_head else BODY
    spec = turn(head_ref if is_head else body_ref, half_ref[...].reshape(2 * BODY, feature + LANES))
    gain = wide_ref[0:1, :]
    shift = wide_ref[1:2, :]

    def scaled(part):
        flat = jnp.concatenate([part[:, feature:]] * (feature // LANES), axis=1)
        return (part[:, :feature] * gain + flat * shift).astype(BF)

    inside = to_mixed(scaled(spec[:rows]), scaled(spec[rows:]))
    active, slope = gelu_parts(mix_product(inside, mix1_ref) + long_ref[0:1, :])
    hidden = active.astype(BF)
    value = mix_product(hidden, mix2_ref) + long_ref[1:2, :]
    bend = jnp.tanh(value / SHRINK)
    for ref, head, kept in zip(outs, heads, (inside, hidden, slope, bend * bend)):
        ref[...] = kept[:BODY]
        if is_head:
            head[...] = kept[BODY:]
    values = jnp.concatenate(from_mixed(value - SHRINK * bend), axis=0)
    out_ref[...] = turn(back_head_ref if is_head else back_body_ref, values).reshape(GROUP, 2 * ROWS, feature)


def mix_first_kernel(
    weight_bits, vector_bits, me_ref, half_ref, weights_ref, vector_ref, head_ref, body_ref, back_head_ref, back_body_ref,
    out_ref, low_ref, hidden_ref, slope_ref, bend_ref, low_head_ref, hidden_head_ref, slope_head_ref, bend_head_ref,
    mix1_ref, mix2_ref, wide_ref, long_ref, up_ref,
):
    feature = out_ref.shape[2]
    devices = vector_ref.shape[1]
    share = feature // devices
    step = pl.program_id(0)
    outs = (low_ref, hidden_ref, slope_ref, bend_ref)
    heads = (low_head_ref, hidden_head_ref, slope_head_ref, bend_head_ref)
    work = functools.partial(
        mix_step, half_ref, head_ref, body_ref, back_head_ref, back_body_ref, mix1_ref, mix2_ref, wide_ref, long_ref,
        outs, heads, out_ref,
    )

    @pl.when(step == 0)
    def _():
        me = me_ref[0]
        build_mix(me, weight_bits, weights_ref, 0, mix1_ref, feature)
        build_mix(me, weight_bits, weights_ref, 1, mix2_ref, feature)
        wide_ref[...] = jnp.zeros_like(wide_ref)
        long_ref[...] = jnp.zeros_like(long_ref)
        for row, at in enumerate((2, 3, 4, 5, 7)):
            wide_ref[row : row + 1, :] = spread(vector_ref[at], share, me, vector_bits)
        for row in range(2):
            both = spread(vector_ref[row], 2 * share, me, vector_bits)
            long_ref[row : row + 1, :] = to_mixed(both[:, :feature], both[:, feature:])
        up_ref[...] = spread(vector_ref[6], up_ref.shape[1] // devices, me, vector_bits)
        work(True)

    @pl.when(step > 0)
    def _():
        work(False)


def mix_second_kernel(
    half_ref, mix1_ref, mix2_ref, wide_ref, long_ref, body_ref, back_body_ref,
    out_ref, low_ref, hidden_ref, slope_ref, bend_ref,
):
    mix_step(
        half_ref, None, body_ref, None, back_body_ref, mix1_ref, mix2_ref, wide_ref, long_ref,
        (low_ref, hidden_ref, slope_ref, bend_ref), (None,) * 4, out_ref, False,
    )


def mode_shapes(rows, feature):
    return [jax.ShapeDtypeStruct((rows, 2 * feature), kind) for kind in (BF, BF, F32, F32)]


def mode_blocks(feature):
    return [pl.BlockSpec((BODY, 2 * feature), lambda i: (i, 0)) for _ in range(4)]


def half_block(width, begin=0):
    return pl.BlockSpec((GROUP, 2 * ROWS, width), lambda i: (i + begin, 0, 0))


def mix_first(me, half, weights, vectors, tables, hidden, steps, weight_bits, vector_bits, deps=()):
    feature = half.shape[2] - LANES
    fixed = (weights, vectors, tables["head"], tables["body"], tables["head_wt"], tables["body_wt"])
    more = (
        jax.ShapeDtypeStruct((2, feature, feature), BF),
        jax.ShapeDtypeStruct((2, feature, feature), BF),
        jax.ShapeDtypeStruct((8, feature), F32),
        jax.ShapeDtypeStruct((8, 2 * feature), F32),
        jax.ShapeDtypeStruct((1, hidden), F32),
    )
    heads = mode_shapes(ROWS, feature)
    return launch(
        deps,
        functools.partial(mix_first_kernel, weight_bits, vector_bits),
        grid=(steps,),
        out_shape=[jax.ShapeDtypeStruct((GROUP * steps, 2 * ROWS, feature), F32)]
        + mode_shapes(BODY * steps, feature) + heads + list(more),
        in_specs=[smem(), half_block(feature + LANES)] + [single(v.shape) for v in fixed],
        out_specs=[half_block(feature)] + mode_blocks(feature) + [single(v.shape) for v in heads]
        + [single(v.shape) for v in more],
        compiler_params=params(),
        cost_estimate=cost(9e9, 20e6),
        name="mix_first",
    )(me, half, *fixed)


def mix_second(half, mix1, mix2, wide, long, tables, begin, steps, deps=()):
    feature = half.shape[2] - LANES
    fixed = (mix1, mix2, wide, long, tables["body"], tables["body_wt"])
    return launch(
        deps,
        mix_second_kernel,
        grid=(steps,),
        out_shape=[jax.ShapeDtypeStruct((GROUP * steps, 2 * ROWS, feature), F32)] + mode_shapes(BODY * steps, feature),
        in_specs=[half_block(feature + LANES, begin)] + [single(v.shape) for v in fixed],
        out_specs=[half_block(feature)] + mode_blocks(feature),
        compiler_params=params(),
        cost_estimate=cost(9e9, 20e6),
        name="mix_second",
    )(half, *fixed)


def space_kernel(rows_ref, cols_ref, half1_ref, half2_ref, tokens_ref, first_t_ref, wide_ref, middle_ref, normed_ref):
    feature = tokens_ref.shape[1]
    flat = lambda ref: ref[...].reshape(-1, feature)
    spatial = turn(first_t_ref, jnp.concatenate([flat(half1_ref), flat(half2_ref)], axis=0))
    inputs = tokens_ref[...].astype(F32)
    live = live_rows(pl.program_id(0) * CELLS, CELLS, rows_ref, cols_ref)
    normal, _ = normalize(inputs)
    middle = inputs + live * (spatial + (normal * wide_ref[0:1, :] + wide_ref[1:2, :]))
    middle_ref[...] = middle
    normal, _ = normalize(middle)
    normed_ref[...] = (normal * wide_ref[2:3, :] + wide_ref[3:4, :]).astype(BF)


def column_block(rows, width):
    return pl.BlockSpec((rows, 2 * GROUP, width), lambda i: (0, i, 0))


def space(rows, cols, half1, half2, tokens, wide, tables, deps=()):
    cells, feature = tokens.shape
    table = tables["first_t"]
    block = pl.BlockSpec((CELLS, feature), lambda i: (i, 0))
    return launch(
        deps,
        space_kernel,
        grid=(STEPS,),
        out_shape=(jax.ShapeDtypeStruct((cells, feature), F32), jax.ShapeDtypeStruct((cells, feature), BF)),
        in_specs=[smem(), smem(), column_block(half1.shape[0], feature), column_block(half2.shape[0], feature),
                  block, single(table.shape), single(wide.shape)],
        out_specs=(block, block),
        compiler_params=params(),
        cost_estimate=cost(6e9, 20e6),
        name="space",
    )(rows, cols, half1, half2, tokens, table, wide)


def fetch_weights(me_ref, pieces, places, up_ref, down_ref, sems):
    count = pieces[0].shape[0] * 2
    chip = me_ref[0] // 2

    def copies(own, core):
        target = (up_ref, down_ref)[core]
        source = pieces[:2] if own else pieces[2:]
        for mask in range(count):
            at = places[core][mask]
            part = source[at // (count // 2)].at[at % (count // 2)]
            yield pltpu.make_async_copy(part, target.at[chip ^ mask], sems.at[core, mask])

    for core in range(2):
        @pl.when(me_ref[0] % 2 == core)
        def _():
            for copy in copies(True, core):
                copy.start()
            for copy in copies(False, 1 - core):
                copy.start()

    for core in range(2):
        for copy in copies(True, core):
            copy.wait()


def weight_scratch(pieces):
    chips, rows, feature = pieces[0].shape[0] * 2, pieces[0].shape[1], pieces[0].shape[2]
    return [
        pltpu.VMEM((chips, rows, feature), BF),
        pltpu.VMEM((chips, rows, feature), BF),
        pltpu.SemaphoreType.DMA((2, chips)),
    ]


def up_part(up_ref, j, feature):
    share = up_ref.shape[1] * feature // (up_ref.shape[0] * up_ref.shape[1])
    return up_ref[:, j * share : (j + 1) * share, :].reshape(feature, feature)


def down_part(down_ref, j, feature):
    share = down_ref.shape[1]
    each = feature // share
    return down_ref[j * each : (j + 1) * each].reshape(feature, feature)


def up_kernel(places, rows_ref, cols_ref, me_ref, normed_ref, grad_ref, bias_ref, *rest):
    pieces = rest[:4]
    active_ref, pre_ref, live_ref, bias_grad_ref, up_ref, down_ref, sems = rest[4:]
    tile, feature = normed_ref.shape
    step = pl.program_id(0)

    @pl.when(step == 0)
    def _():
        fetch_weights(me_ref, pieces, places, up_ref, down_ref, sems)
        bias_grad_ref[...] = jnp.zeros_like(bias_grad_ref)

    live = live_rows(step * tile, tile, rows_ref, cols_ref)
    branch = (grad_ref[...].astype(F32) * live).astype(BF)
    live_ref[...] = branch
    normed = normed_ref[...]
    for j in range(active_ref.shape[1] // feature):
        place = slice(j * feature, (j + 1) * feature)
        value = mm(normed, up_part(up_ref, j, feature)) + bias_ref[:, place]
        grad = mm(branch, down_part(down_ref, j, feature), (1, 1))
        active, slope = gelu_parts(value)
        active_ref[:, place] = active.astype(BF)
        low = (grad * slope).astype(BF)
        pre_ref[:, place] = low
        bias_grad_ref[:, place] += jnp.sum(low.astype(F32), axis=0, keepdims=True)


def feed_up(rows, cols, me, normed, grad, bias, pieces, places, tile=256, deps=()):
    cells, feature = normed.shape
    hidden = bias.shape[1]
    block = lambda width: pl.BlockSpec((tile, width), lambda i: (i, 0))
    return launch(
        deps,
        functools.partial(up_kernel, places),
        grid=(cells // tile,),
        out_shape=(
            jax.ShapeDtypeStruct((cells, hidden), BF),
            jax.ShapeDtypeStruct((cells, hidden), BF),
            jax.ShapeDtypeStruct((cells, feature), BF),
            jax.ShapeDtypeStruct((1, hidden), F32),
        ),
        in_specs=[smem(), smem(), smem(), block(feature), block(feature), single(bias.shape)]
        + [any_space() for _ in pieces],
        out_specs=(block(hidden), block(hidden), block(feature), pl.BlockSpec((1, hidden), lambda i: (0, 0))),
        scratch_shapes=weight_scratch(pieces),
        compiler_params=params(),
        cost_estimate=cost(4 * cells * feature * hidden, 40e6),
        name="feed_up",
    )(rows, cols, me, normed, grad, bias, *pieces)


def weight_grad_kernel(places, me_ref, active_ref, pre_ref, branch_ref, normed_ref, send_ref, keep_ref, stage_ref, sems):
    step = pl.program_id(0)
    steps = pl.num_programs(0) // 2
    feature = branch_ref.shape[1]
    chips, rows, _ = send_ref.shape
    each = feature // rows
    share = feature // chips

    def down_copies(j, target):
        for c in range(each):
            source = stage_ref.at[j, pl.ds(c * rows, rows)]
            yield pltpu.make_async_copy(source, target.at[places[1][j * each + c]], sems.at[j, c])

    def up_copies(j, target):
        for c in range(chips):
            source = stage_ref.at[steps + j, pl.ds(c * share, share)]
            there = target.at[places[0][c], pl.ds(j * share, share)]
            yield pltpu.make_async_copy(source, there, sems.at[steps + j, c])

    @pl.when(step < steps)
    def _():
        stage_ref[step] = mm(active_ref[...], branch_ref[...], (0, 0)).astype(BF)

    @pl.when(step >= steps)
    def _():
        stage_ref[step] = mm(normed_ref[...], pre_ref[...], (0, 0)).astype(BF)

    total = stage_ref.shape[0] // 2
    for j in range(total):
        for core in range(2):
            targets = (send_ref, keep_ref) if core == 0 else (keep_ref, send_ref)

            @pl.when((step == j) & (me_ref[0] % 2 == core))
            def _():
                for copy in down_copies(j, targets[0]):
                    copy.start()

            @pl.when((step == total + j) & (me_ref[0] % 2 == core))
            def _():
                for copy in up_copies(j, targets[1]):
                    copy.start()

    @pl.when(step == 2 * steps - 1)
    def _():
        for j in range(total):
            for copy in down_copies(j, send_ref):
                copy.wait()
            for copy in up_copies(j, send_ref):
                copy.wait()


def weight_grads(me, active, pre, branch, normed, places, deps=()):
    cells, hidden = active.shape
    feature = branch.shape[1]
    tiles = hidden // feature
    chips = UNITS
    shape = jax.ShapeDtypeStruct((chips, hidden // chips, feature), BF)
    return launch(
        deps,
        functools.partial(weight_grad_kernel, places),
        grid=(2 * tiles,),
        out_shape=(shape, shape),
        in_specs=[
            smem(),
            pl.BlockSpec((cells, feature), lambda i: (0, jnp.minimum(i, tiles - 1))),
            pl.BlockSpec((cells, feature), lambda i: (0, jnp.maximum(i - tiles, 0))),
            single(branch.shape), single(normed.shape),
        ],
        out_specs=(any_space(), any_space()),
        scratch_shapes=[
            pltpu.VMEM((2 * tiles, feature, feature), BF),
            pltpu.SemaphoreType.DMA((2 * tiles, chips)),
        ],
        compiler_params=params(),
        cost_estimate=cost(4 * cells * feature * hidden, 40e6),
        name="weight_grads",
    )(me, active, pre, branch, normed)


def down_kernel(places, begin, rows_ref, cols_ref, me_ref, active_ref, pre_ref, middle_ref, grad_ref, wide_ref,
                first_ref, *rest):
    pieces = rest[:4]
    old_sums_ref = rest[4] if begin else None
    mixed_ref, grad_middle_ref, half_ref, sums_ref, up_ref, down_ref, sems = rest[-7:]
    tile, feature = middle_ref.shape
    hidden = active_ref.shape[1]
    step = pl.program_id(0)

    @pl.when(step == 0)
    def _():
        fetch_weights(me_ref, pieces, places, up_ref, down_ref, sems)
        sums_ref[...] = old_sums_ref[...] if begin else jnp.zeros_like(sums_ref)

    live = live_rows((step + begin) * tile, tile, rows_ref, cols_ref)
    branch = mm(active_ref[...], down_ref[...].reshape(hidden, feature))
    grad_normed = jnp.zeros((tile, feature), F32)
    for j in range(hidden // feature):
        pre = pre_ref[:, j * feature : (j + 1) * feature]
        grad_normed = grad_normed + mm(pre, up_part(up_ref, j, feature), (1, 1))
    middle = middle_ref[...]
    mixed_ref[...] = (middle + live * (branch + wide_ref[4:5, :])).astype(BF)
    normal, inverse = normalize(middle)
    cotangent = grad_ref[...].astype(F32)
    grad_middle = cotangent + norm_back(grad_normed, wide_ref[2:3, :], normal, inverse)
    grad_middle_ref[...] = grad_middle
    half_ref[...] = turn(first_ref, grad_middle * live).reshape(half_ref.shape)
    sums_ref[0:1, :] += jnp.sum(grad_normed * normal, axis=0, keepdims=True)
    sums_ref[1:2, :] += jnp.sum(grad_normed, axis=0, keepdims=True)
    sums_ref[2:3, :] += jnp.sum((cotangent * live).astype(BF).astype(F32), axis=0, keepdims=True)


def feed_down(rows, cols, me, active, pre, middle, grad, wide, table, pieces, places, begin, steps, before=(), deps=()):
    cells, feature = middle.shape
    hidden = active.shape[1]
    block = lambda width: pl.BlockSpec((CELLS, width), lambda i: (i + begin, 0))
    operands = (rows, cols, me, active, pre, middle, grad, wide, table, *pieces)
    extra = ()
    aliases = {}
    if begin:
        extra = (before[3],) + tuple(before[:3])
        aliases = {len(operands) + 1 + k: k for k in range(3)}
    return launch(
        deps,
        functools.partial(down_kernel, places, begin),
        grid=(steps,),
        out_shape=(
            jax.ShapeDtypeStruct((cells, feature), BF),
            jax.ShapeDtypeStruct((cells, feature), F32),
            jax.ShapeDtypeStruct((KEPT, 2 * ROWS, feature), F32),
            jax.ShapeDtypeStruct((8, feature), F32),
        ),
        in_specs=[smem(), smem(), smem(), block(hidden), block(hidden), block(feature), block(feature),
                  single(wide.shape), single(table.shape)] + [any_space() for _ in pieces]
        + [single(v.shape) for v in extra[:1]] + [any_space() for _ in extra[1:]],
        out_specs=(block(feature), block(feature),
                   pl.BlockSpec((KEPT, 2 * GROUP, feature), lambda i: (0, i + begin, 0)), single((8, feature))),
        scratch_shapes=weight_scratch(pieces),
        input_output_aliases=aliases,
        compiler_params=params(),
        cost_estimate=cost(4 * CELLS * steps * feature * hidden, 25e6),
        name="feed_down_b" if begin else "feed_down_a",
    )(*operands, *extra)


def back_step(half_ref, head_ref, body_ref, back_head_ref, back_body_ref, mix1_ref, mix2_ref, ins, in_heads,
              outs, out_heads, out_ref, sums_ref, is_head):
    feature = out_ref.shape[2]
    rows = HEAD if is_head else BODY

    def read(k):
        if is_head:
            return jnp.concatenate([ins[k][...], in_heads[k][...]], axis=0)
        return ins[k][...]

    grad = turn(head_ref if is_head else body_ref, half_ref[...].reshape(2 * BODY, feature))
    grad_two = (to_mixed(grad[:rows], grad[rows:]) * read(1)).astype(BF)
    grad_one = (mix_product(grad_two, mix2_ref, True) * read(0)).astype(BF)
    grad_spec = mix_product(grad_one, mix1_ref, True)
    values = jnp.concatenate(from_mixed(grad_spec), axis=0)
    out_ref[...] = turn(back_head_ref if is_head else back_body_ref, values).reshape(GROUP, 2 * ROWS, feature)
    for row, value in enumerate((grad_one, grad_two)):
        outs[row][...] = value[:BODY]
        if is_head:
            out_heads[row][...] = value[BODY:]
        total = jnp.sum(value.astype(F32), axis=0, keepdims=True)
        sums_ref[row : row + 1, :] = total if is_head else sums_ref[row : row + 1, :] + total


def mix_back_kernel(
    half_ref, slope1_ref, slope2_ref, bend1_ref, bend2_ref, slope_head_ref, bend_head_ref, mix1_ref, mix2_ref,
    head_ref, body_ref, back_head_ref, back_body_ref,
    out_ref, one_ref, two_ref, one_head_ref, two_head_ref, sums_ref,
):
    step = pl.program_id(0)
    steps = pl.num_programs(0) // 2
    work = functools.partial(
        back_step, half_ref, head_ref, body_ref, back_head_ref, back_body_ref, mix1_ref, mix2_ref
    )
    more = ((slope_head_ref, bend_head_ref), (one_ref, two_ref), (one_head_ref, two_head_ref), out_ref, sums_ref)

    @pl.when(step == 0)
    def _():
        sums_ref[...] = jnp.zeros_like(sums_ref)
        work((slope1_ref, bend1_ref), *more, True)

    @pl.when((step > 0) & (step < steps))
    def _():
        work((slope1_ref, bend1_ref), *more, False)

    @pl.when(step >= steps)
    def _():
        work((slope2_ref, bend2_ref), *more, False)


def mix_back(half, slopes, bends, slope_head, bend_head, mix1, mix2, tables, deps=()):
    feature = half.shape[2]
    steps = KEPT // GROUP
    fixed = (slope_head, bend_head, mix1, mix2, tables["head_w"], tables["body_w"], tables["head_t"], tables["body_t"])
    near = pl.BlockSpec((BODY, 2 * feature), lambda i: (jnp.minimum(i, steps // 2 - 1), 0))
    far = pl.BlockSpec((BODY, 2 * feature), lambda i: (jnp.maximum(i - steps // 2, 0), 0))
    low = lambda rows: jax.ShapeDtypeStruct((rows, 2 * feature), BF)
    body = pl.BlockSpec((BODY, 2 * feature), lambda i: (i, 0))
    shapes = (
        jax.ShapeDtypeStruct((KEPT, 2 * ROWS, feature), F32), low(BODY * steps), low(BODY * steps),
        low(ROWS), low(ROWS), jax.ShapeDtypeStruct((8, 2 * feature), F32),
    )
    return launch(
        deps,
        mix_back_kernel,
        grid=(steps,),
        out_shape=shapes,
        in_specs=[half_block(feature), near, far, near, far] + [single(v.shape) for v in fixed],
        out_specs=[half_block(feature), body, body] + [single(v.shape) for v in shapes[3:]],
        compiler_params=params(),
        cost_estimate=cost(18e9, 30e6),
        name="mix_back",
    )(half, *slopes, *bends, *fixed)


def block_kernel(left1_ref, left2_ref, left_head_ref, right_ref, right_head_ref, out_ref, natural_ref):
    wide = 2 * LANES
    count = left1_ref.shape[1] // wide
    cut = left1_ref.shape[0]
    for t in range(count):
        for c in range(max(t - 1, 0), min(t + 2, count)):
            left, right = slice(t * wide, (t + 1) * wide), slice(c * wide, (c + 1) * wide)
            total = (
                mm(left1_ref[:, left], right_ref[:cut, right], (0, 0))
                + mm(left2_ref[:, left], right_ref[cut:, right], (0, 0))
                + mm(left_head_ref[:, left], right_head_ref[:, right], (0, 0))
            )
            rows, lanes = slice(t * LANES, (t + 1) * LANES), slice(c * LANES, (c + 1) * LANES)
            natural_ref[0, rows, lanes] = total[:LANES, :LANES] + total[LANES:, LANES:]
            natural_ref[1, rows, lanes] = total[:LANES, LANES:] - total[LANES:, :LANES]
    per_group = BLOCKS // 2
    block = count * LANES // per_group
    for b in range(per_group):
        begin = b * block
        base = begin // LANES * LANES
        reach = min(base + wide, count * LANES) - base
        for part in range(2):
            piece = natural_ref[part, begin : begin + block, base : base + reach]
            if begin > base:
                piece = pltpu.roll(piece, reach - (begin - base), axis=1)
            out_ref[part, b * block : (b + 1) * block, :] = piece[:, :LANES]


def block_grads(left1, left2, left_head, right, right_head, name, deps=()):
    feature = left1.shape[1] // 2
    half = feature // 2
    block = lambda v: pl.BlockSpec((v.shape[0], feature), lambda i: (0, i))
    return launch(
        deps,
        block_kernel,
        grid=(2,),
        out_shape=jax.ShapeDtypeStruct((2, feature, LANES), F32),
        in_specs=[block(v) for v in (left1, left2, left_head, right, right_head)],
        out_specs=pl.BlockSpec((2, half, LANES), lambda i: (0, i, 0)),
        scratch_shapes=[pltpu.VMEM((2, half, half), F32)],
        compiler_params=params(),
        cost_estimate=cost(5e9, 7e6),
        name=name,
    )(left1, left2, left_head, right, right_head)


def last_kernel(rows_ref, cols_ref, half_ref, tokens_ref, grad_ref, first_t_ref, wide_ref, out_ref, sums_ref):
    tile, feature = tokens_ref.shape
    step = pl.program_id(0)
    live = live_rows(step * tile, tile, rows_ref, cols_ref)
    grad_middle = grad_ref[...]
    grad_normed = live * (grad_middle + turn(first_t_ref, half_ref[...].reshape(CELLS, feature)))
    normal, inverse = normalize(tokens_ref[...].astype(F32))
    out_ref[...] = grad_middle + norm_back(grad_normed, wide_ref[0:1, :], normal, inverse)

    @pl.when(step == 0)
    def _():
        sums_ref[...] = jnp.zeros_like(sums_ref)

    sums_ref[0:1, :] += jnp.sum(grad_normed * normal, axis=0, keepdims=True)
    sums_ref[1:2, :] += jnp.sum(grad_normed, axis=0, keepdims=True)


def last(rows, cols, half, tokens, grad, wide, tables, deps=()):
    cells, feature = tokens.shape
    first_t = tables["first_t"]
    block = pl.BlockSpec((CELLS, feature), lambda i: (i, 0))
    return launch(
        deps,
        last_kernel,
        grid=(STEPS,),
        out_shape=(jax.ShapeDtypeStruct((cells, feature), F32), jax.ShapeDtypeStruct((8, feature), F32)),
        in_specs=[smem(), smem(), column_block(KEPT, feature), block, block, single(first_t.shape), single(wide.shape)],
        out_specs=(block, single((8, feature))),
        compiler_params=params(),
        cost_estimate=cost(6e9, 20e6),
        name="last",
    )(rows, cols, half, tokens, grad, first_t, wide)


AXES = ("dp", "fsdp")


def swap(value, devices, bits):
    return lax.ppermute(value, AXES, [(i, i ^ (1 << bits[i & 1])) for i in range(devices)])


def doubling_orders(count):
    first = list(range(count - 1, 0, -1))
    second = list(first)
    for k in range(0, len(second) - 1, 2):
        second[k], second[k + 1] = second[k + 1], second[k]
    return first, second


def places_of(order):
    return [
        sum(1 << k for k, bit in enumerate(order) if mask >> (bit - 1) & 1) for mask in range(1 << len(order))
    ]


def pair_kernel(held_ref, got_ref, out_ref):
    count = held_ref.shape[0]
    out_ref[:count] = held_ref[...]
    out_ref[count:] = got_ref[...]


def pair(held, got, deps=()):
    shape = jax.ShapeDtypeStruct((2 * held.shape[0],) + held.shape[1:], held.dtype)
    return launch(
        deps,
        pair_kernel,
        out_shape=shape,
        in_specs=[pl.BlockSpec(memory_space=pltpu.VMEM)] * 2,
        out_specs=pl.BlockSpec(memory_space=pltpu.VMEM),
        compiler_params=params(),
        cost_estimate=cost(0, 4 * held.size * 2),
        name="pair",
    )(held, got)


def hold(value, deps):
    def body(*refs):
        pass

    return pl.pallas_call(
        body,
        out_shape=jax.ShapeDtypeStruct(value.shape, value.dtype),
        in_specs=[any_space() for _ in range(1 + len(deps))],
        out_specs=any_space(),
        input_output_aliases={0: 0},
        compiler_params=params(),
        cost_estimate=cost(0, 0),
        name="hold",
    )(value, *deps)


def gather_small(value, me, devices, count):
    held = value[None]
    for bit in list(range(3, count)) + [2, 1, 0]:
        other = swap(held, devices, (bit, bit))
        upper = (me >> bit) & 1
        axis = 0 if bit > 2 else 1
        join_two = lambda a, b: jnp.stack([a, b], axis=axis).reshape((-1,) + value.shape)
        held = jnp.where(upper == 0, join_two(held, other), join_two(other, held))
    return held


def scatter_small(value, me, devices, count, exact):
    shape = value.shape[1:]
    rows = shape[0]
    total = value
    for bit in [0, 1, 2] + list(range(count - 1, 2, -1)):
        upper = (me >> bit) & 1
        axis = 0 if bit > 2 else 1
        pair = total.reshape(((2, -1) if bit > 2 else (-1, 2)) + shape)
        away = lax.dynamic_index_in_dim(pair, 1 - upper, axis, keepdims=False)
        keep = lax.dynamic_index_in_dim(pair, upper, axis, keepdims=False)
        sums = away[:, rows - exact :]
        top = lax.reduce_precision(sums, 8, 7)
        packet = jnp.concatenate([away[:, : rows - exact], top, sums - top], axis=1).astype(BF)
        got = swap(packet, devices, (bit, bit)).astype(F32)
        low = got[:, rows - exact : rows] + got[:, rows:]
        total = keep + jnp.concatenate([got[:, : rows - exact], low], axis=1)
    return total[0]


def chip_unit(up, down, core, devices):
    parts, share, feature = up.shape
    flat = up.reshape(parts * share, feature)
    other = swap(jnp.where(core == 0, down, flat), devices, (0, 0))
    up_unit = jnp.concatenate([up, other.reshape(up.shape)], axis=1).reshape(2 * parts * share, feature)
    return jnp.where(core == 0, up_unit, jnp.concatenate([other, down]))[None]


def fold_kernel(upper_ref, keep_away_ref, got_away_ref, keep_own_ref, got_own_ref, send_ref, keep_ref):
    send_ref[...] = (keep_away_ref[...].astype(F32) + got_away_ref[...].astype(F32)).astype(BF)
    keep_ref[...] = (keep_own_ref[...].astype(F32) + got_own_ref[...].astype(F32)).astype(BF)


def fold(keep, got, upper, deps=()):
    half = keep.shape[0] // 2
    unit = (1,) + keep.shape[1:]
    count = len(deps)
    away = pl.BlockSpec(unit, lambda i, up: ((1 - up[0]) * half + i, 0, 0))
    own = pl.BlockSpec(unit, lambda i, up: (up[0] * half + i, 0, 0))
    out = pl.BlockSpec(unit, lambda i, up: (i, 0, 0))
    shape = jax.ShapeDtypeStruct((half,) + keep.shape[1:], BF)

    def body(*refs):
        fold_kernel(*refs[:5], *refs[5 + count :])

    return pl.pallas_call(
        body,
        grid_spec=pltpu.PrefetchScalarGridSpec(
            num_scalar_prefetch=1,
            grid=(half,),
            in_specs=[away, away, own, own] + [any_space() for _ in deps],
            out_specs=[out, out],
        ),
        out_shape=(shape, shape),
        compiler_params=params(),
        cost_estimate=cost(0, 6 * half * keep[0].size),
        name="fold",
    )(upper, keep, got, keep, got, *deps)


def on_device(
    tokens, grad_out, region_rows, region_cols, ln1_gain, ln1_bias, spec_w1, spec_b1, spec_w2, spec_b2,
    ln2_gain, ln2_bias, w_up, up_bias, w_down, down_bias,
):
    devices = lax.axis_size(AXES[0]) * lax.axis_size(AXES[1])
    count = devices.bit_length() - 1
    me = lax.axis_index(AXES).astype(jnp.int32)
    core = me & 1
    me_one = me.reshape(1)
    feature = tokens.shape[-1]
    block = feature // BLOCKS
    share = ln1_gain.shape[0]
    cells = tokens.shape[1] * tokens.shape[2]
    hidden = w_up.shape[1]
    parts = hidden // feature
    tables = {name: jnp.asarray(value) for name, value in wave_matrices().items()}
    orders = doubling_orders(count)
    places = tuple(places_of(order) for order in orders)
    flat_tokens = tokens.reshape(cells, feature)
    flat_grad = grad_out.reshape(cells, feature)
    fast = devices // 2 == UNITS
    step = lambda value, k: swap(value, devices, (orders[0][k], orders[1][k]))

    padded = lambda v: jnp.pad(v, ((0, 0), (0, LANES - v.shape[1])))
    vectors = (spec_b1, spec_b2, ln1_gain, ln1_bias, ln2_gain, ln2_bias, up_bias, down_bias)
    small = jnp.concatenate([padded(spec_w1), padded(spec_w2)] + [padded(v[None]) for v in vectors])
    if fast:
        own_up = w_up.reshape(share, parts, feature).transpose(1, 0, 2)
        unit = chip_unit(own_up, w_down, core, devices)
        bits = tuple(range(3, count)) + (2, 1, 0)
        meet = lambda value, k: swap(value, devices, (bits[k], bits[k]))
        small = pair(small[None], meet(small[None], 0))
        half = first(region_rows, region_cols, flat_tokens, tables, deps=(unit, small))
        near = pair(unit, step(unit, 0), deps=(half,))
        small = pair(small, meet(small, 1), deps=(near,))
        for k in range(2, count):
            small = pair(small, meet(small, k))
        near = pair(near, step(near, 1), deps=(small,))
        weights, weight_bits, vector_bits, me_small = small, bits, bits, me_one
    else:
        up = lax.all_gather(w_up, AXES, axis=0, tiled=True)
        up = up.reshape(UNITS, feature // UNITS, parts, feature).transpose(0, 2, 1, 3).reshape(UNITS, -1, feature)
        down = lax.all_gather(w_down, AXES, axis=0, tiled=True).reshape(UNITS, -1, feature)
        pieces = tuple(
            jnp.where(core == 0, one, two)[begin : begin + UNITS // 2]
            for one, two in ((up, down), (down, up))
            for begin in (0, UNITS // 2)
        )
        me_one = core.reshape(1)
        me_small = jnp.zeros_like(me_one)
        places = (tuple(range(UNITS)),) * 2
        small = gather_small(small, me, devices, count)
        weights = small[:, : 4 * share].reshape(devices, 2, 2 * share, LANES).transpose(1, 0, 2, 3)
        weights = weights.reshape(2, 2 * UNITS, -1, LANES).transpose(1, 0, 2, 3).reshape(2 * UNITS, -1, LANES)
        weight_bits, vector_bits = tuple(range(5)), tuple(range(count))
        half = first(region_rows, region_cols, flat_tokens, tables)
    vectors = small[:, 4 * share :].transpose(1, 0, 2).astype(F32)

    steps = KEPT // GROUP
    made = mix_first(
        me_small, half, weights, vectors, tables, hidden, steps // 2, weight_bits, vector_bits,
        deps=(near,) if fast else (),
    )
    half1, modes1, heads, (mix1, mix2, wide, long, up_shift) = made[0], made[1:5], made[5:9], made[9:]
    if fast:
        near = pair(near, step(near, 2), deps=(half1,))
        far = step(near, 3)
    made = mix_second(
        half, mix1, mix2, wide, long, tables, steps // 2, steps // 2, deps=(near,) if fast else ()
    )
    half2, modes2 = made[0], made[1:5]
    middle, normed = space(region_rows, region_cols, half1, half2, flat_tokens, wide, tables)
    if fast:
        far = hold(far, (normed,))
        pieces = (near, far, swap(near, devices, (0, 0)), swap(far, devices, (0, 0)))
    active, pre, branch, bias_grad = feed_up(
        region_rows, region_cols, me_one, normed, flat_grad, up_shift, pieces, places
    )
    send, keep = weight_grads(me_one, active, pre, branch, normed, places)
    down_args = (me_one, active, pre, middle, flat_grad, wide, tables["first"], pieces, places)
    tiles = cells // CELLS
    made = feed_down(region_rows, region_cols, *down_args, 0, tiles // 2, deps=(send,))
    deps = ()
    if fast:
        ranks = [((me >> jnp.where(core == 0, *bit)) & 1).reshape(1) for bit in zip(*orders)]
        send, keep = fold(keep, swap(send, devices, (0, 0)), ranks[3], deps=(made[3],))
        deps = (send,)
    made = feed_down(region_rows, region_cols, *down_args, tiles // 2, tiles // 2, made, deps=deps)
    mixed, grad_middle, half_back, sums_two = made
    made = mix_back(
        half_back, (modes1[2], modes2[2]), (modes1[3], modes2[3]), heads[2], heads[3], mix1, mix2, tables
    )
    half_back, one, two, one_head, two_head, bias_sums = made
    if fast:
        send, keep = fold(keep, step(send, 3), ranks[2], deps=(bias_sums,))
        deps = (send,)
    grad_two = block_grads(modes1[1], modes2[1], heads[1], two, two_head, "grad_mix2", deps=deps)
    grad_one = block_grads(modes1[0], modes2[0], heads[0], one, one_head, "grad_mix1", deps=deps)
    if fast:
        send, keep = fold(keep, step(send, 2), ranks[1], deps=(grad_one, grad_two))
        deps = (send,)
    grad_tokens, sums_one = last(
        region_rows, region_cols, half_back, flat_tokens, grad_middle, wide, tables, deps=deps
    )

    if fast:
        send, keep = fold(keep, step(send, 1), ranks[0])
        total = keep[0].astype(F32) + step(send, 0)[0].astype(F32)
        up_all = total.reshape(parts, 2 * share, feature)
        lower = up_all[:, :share].reshape(parts * share, feature)
        upper = up_all[:, share:].reshape(parts * share, feature)
        each = parts * share
        other = swap(jnp.where(core == 0, upper, total[:each]), devices, (0, 0))
        grad_w_up = jnp.where(core == 0, lower, other).reshape(parts, share, feature).transpose(1, 0, 2)
        grad_w_down = jnp.where(core == 0, other, total[each:])
    else:
        scatter = lambda v: lax.psum_scatter(v.astype(F32), AXES, scatter_dimension=0, tiled=True)
        up = jnp.where(core == 0, keep, send).reshape(UNITS, parts, feature // UNITS, feature)
        grad_w_up = scatter(up.transpose(0, 2, 1, 3).reshape(feature, hidden))
        grad_w_down = scatter(jnp.where(core == 0, send, keep).reshape(hidden, feature))

    owned = lambda v: jnp.pad(
        v.reshape(v.shape[0], devices, -1).transpose(1, 0, 2), ((0, 0), (0, 0), (0, LANES - v.shape[1] // devices))
    )
    narrow = jnp.concatenate([sums_one[:2], sums_two[:3]])
    biases = bias_sums[:2].reshape(2, feature // LANES, 2, LANES).transpose(0, 2, 1, 3).reshape(2, 2 * feature)
    blocks = [v.reshape(devices, 2 * share, LANES) for v in (grad_one, grad_two)]
    packet = jnp.concatenate(blocks + [owned(narrow), owned(biases), owned(bias_grad)], axis=1)
    result = scatter_small(packet, me, devices, count, 8)
    row = lambda k, width: result[4 * share + k, :width]
    return (
        mixed.reshape(tokens.shape),
        grad_tokens.reshape(tokens.shape),
        row(0, share),
        row(1, share),
        result[: 2 * share, :block],
        row(5, 2 * share),
        result[2 * share : 4 * share, :block],
        row(6, 2 * share),
        row(2, share),
        row(3, share),
        grad_w_up.reshape(share, hidden),
        row(7, bias_grad.shape[1] // devices),
        grad_w_down,
        row(4, share),
    )


def solution(mesh):
    placed = P(AXES)
    return jax.shard_map(
        on_device, mesh=mesh, in_specs=(placed,) * 16, out_specs=(placed,) * 14, check_vma=False
    )
```

```python
import functools
import math

import jax
import jax.numpy as jnp
import numpy as np
from jax import lax
from jax.experimental import pallas as pl
from jax.experimental.pallas import tpu as pltpu
from jax.sharding import PartitionSpec as P

BF = jnp.bfloat16
F32 = jnp.float32
BLOCKS = 8
EPS = 1e-05
SHRINK = 0.01
ROWS = 32
COLS = 64
KEPT = COLS // 2
GROUP = 4
STEPS = ROWS // GROUP
CELLS = GROUP * COLS
MODES = (KEPT + 1) * ROWS
HEAD = (GROUP + 1) * ROWS
BODY = GROUP * ROWS
LANES = 128
C1 = math.sqrt(2.0 / math.pi)
C3 = 0.044715
UNITS = 16
VMEM_LIMIT = 60 * 1024 * 1024


def table_parts(values):
    high = values.astype(np.float32).astype(jnp.bfloat16)
    low = (values - high.astype(np.float64)).astype(np.float32).astype(jnp.bfloat16)
    return np.stack([high, low])


def wave_matrices():
    scale = 1.0 / math.sqrt(ROWS * COLS)
    w = np.arange(COLS)
    first = np.zeros((KEPT, 2, GROUP, GROUP, COLS))
    for k in range(KEPT):
        for h in range(GROUP):
            if k == 0:
                first[k, 0, h, h] = scale
                first[k, 1, h, h] = scale * np.where(w % 2 == 0, 1.0, -1.0)
            else:
                first[k, 0, h, h] = scale * np.cos(2 * np.pi * (k * w % COLS) / COLS)
                first[k, 1, h, h] = -scale * np.sin(2 * np.pi * (k * w % COLS) / COLS)
    first = first.reshape(CELLS, CELLS)
    p = np.arange(ROWS)
    turn = 2 * np.pi * (np.outer(p, p) % ROWS) / ROWS
    cos = np.cos(turn).reshape(ROWS, STEPS, GROUP)
    sin = np.sin(turn).reshape(ROWS, STEPS, GROUP)
    body = np.zeros((2, GROUP, ROWS, GROUP, STEPS, 2, GROUP))
    head = np.zeros((2, GROUP + 1, ROWS, GROUP, STEPS, 2, GROUP))
    for k in range(GROUP):
        body[0, k, :, k, :, 0] = cos
        body[0, k, :, k, :, 1] = sin
        body[1, k, :, k, :, 1] = cos
        body[1, k, :, k, :, 0] = -sin
    head[:, 1:GROUP, :, 1:] = body[:, 1:, :, 1:]
    for place, part in ((0, 0), (GROUP, 1)):
        head[0, place, :, 0, :, part] = cos
        head[1, place, :, 0, :, part] = -sin
    weight = np.full((2, GROUP + 1, ROWS, 1), 2.0)
    weight[:, 0] = 1.0
    weight[:, GROUP] = 1.0
    head = head.reshape(2 * HEAD, 2 * BODY)
    body = body.reshape(2 * BODY, 2 * BODY)
    head_weighted = head * weight.reshape(2 * HEAD, 1)
    body_weighted = body * 2.0
    return {
        "first": table_parts(first),
        "first_t": table_parts(first.T),
        "head": table_parts(head),
        "body": table_parts(body),
        "head_t": table_parts(head.T),
        "body_t": table_parts(body.T),
        "head_w": table_parts(head_weighted),
        "body_w": table_parts(body_weighted),
        "head_wt": table_parts(head_weighted.T),
        "body_wt": table_parts(body_weighted.T),
    }


def mm(left, right, dims=(1, 0)):
    return lax.dot_general(
        left, right, (((dims[0],), (dims[1],)), ((), ())), preferred_element_type=F32
    )


def split(values):
    high = values.astype(BF)
    return high, (values - high.astype(F32)).astype(BF)


def turn(table, values):
    high, low = split(values)
    return mm(table[0], high) + mm(table[1], high) + mm(table[0], low)


def normalize(values):
    centred = values - jnp.mean(values, axis=-1, keepdims=True)
    inverse = lax.rsqrt(jnp.mean(centred * centred, axis=-1, keepdims=True) + EPS)
    return centred * inverse, inverse


def norm_back(grad, gain, normal, inverse):
    scaled = grad * gain
    return inverse * (
        scaled
        - jnp.mean(scaled, axis=-1, keepdims=True)
        - normal * jnp.mean(scaled * normal, axis=-1, keepdims=True)
    )


def gelu_parts(value):
    square = value * value
    half = 0.5 + 0.5 * jnp.tanh(value * (C1 + (C1 * C3) * square))
    active = value * half
    slope = half + active * (1.0 - half) * (2.0 * C1 + (6.0 * C1 * C3) * square)
    return active, slope


def gelu(value):
    square = value * value
    return value * (0.5 + 0.5 * jnp.tanh(value * (C1 + (C1 * C3) * square)))


def live_rows(start, count, rows_ref, cols_ref):
    cell = start + lax.broadcasted_iota(jnp.int32, (count, 1), 0)
    inside = (cell // COLS < rows_ref[0]) & (cell % COLS < cols_ref[0])
    return jnp.where(inside, 1.0, 0.0).astype(F32)


def spread(piece, per_device, me, bits):
    devices = piece.shape[0]
    total = devices * per_device
    lane = lax.broadcasted_iota(jnp.int32, (LANES, total), 0)
    place = lax.broadcasted_iota(jnp.int32, (LANES, total), 1)
    pick = jnp.where(place % per_device == lane, 1.0, 0.0).astype(BF)
    wide = mm(piece.astype(BF), pick)
    row = lax.broadcasted_iota(jnp.int32, (devices, 1), 0)
    owner = jnp.full((devices, 1), me, jnp.int32)
    for k, bit in enumerate(bits):
        owner = owner ^ (((row >> k) & 1) << bit)
    where = lax.broadcasted_iota(jnp.int32, (devices, total), 1) // per_device
    return jnp.sum(jnp.where(owner == where, wide, 0.0), axis=0, keepdims=True)


def place_of(mask, bits):
    return sum(((mask >> bit) & 1) << k for k, bit in enumerate(bits))


def any_space():
    return pl.BlockSpec(memory_space=pl.ANY)


def single(shape):
    return pl.BlockSpec(shape, lambda *_: (0,) * len(shape), pipeline_mode=pl.Buffered(1))


def smem():
    return pl.BlockSpec(memory_space=pltpu.SMEM)


def params(**more):
    return pltpu.CompilerParams(vmem_limit_bytes=VMEM_LIMIT, **more)


def cost(flops, moved):
    return pl.CostEstimate(flops=0, bytes_accessed=0, transcendentals=0)


def launch(deps, kernel, *, in_specs, **more):
    count = len(in_specs)

    def body(*refs):
        kernel(*refs[:count], *refs[count + len(deps) :])

    call = pl.pallas_call(body, in_specs=list(in_specs) + [any_space() for _ in deps], **more)
    return lambda *operands: call(*operands, *deps)


def to_mixed(real, imag):
    tiles = []
    for at in range(0, real.shape[1], LANES):
        tiles += [real[:, at : at + LANES], imag[:, at : at + LANES]]
    return jnp.concatenate(tiles, axis=1)


def from_mixed(values):
    cut = lambda at: values[:, at : at + LANES]
    real = [cut(at) for at in range(0, values.shape[1], 2 * LANES)]
    imag = [cut(at + LANES) for at in range(0, values.shape[1], 2 * LANES)]
    return jnp.concatenate(real, axis=1), jnp.concatenate(imag, axis=1)


def mix_product(values, matrix_ref, back=False):
    feature = values.shape[1] // 2
    wide = 2 * LANES
    groups = []
    for group in range(2):
        part = values[:, group * feature : (group + 1) * feature]
        count = feature // wide
        for t in range(count):
            begin, end = max(t - 1, 0) * wide, min(t + 2, count) * wide
            here = slice(t * wide, (t + 1) * wide)
            if back:
                groups.append(mm(part[:, begin:end], matrix_ref[group, here, begin:end], (1, 1)))
            else:
                groups.append(mm(part[:, begin:end], matrix_ref[group, begin:end, here]))
    return jnp.concatenate(groups, axis=1)


def first_kernel(rows_ref, cols_ref, tokens_ref, first_ref, half_ref):
    feature = tokens_ref.shape[1]
    normal, _ = normalize(tokens_ref[...].astype(F32))
    live = live_rows(pl.program_id(0) * CELLS, CELLS, rows_ref, cols_ref)
    half_ref[:, :, :feature] = turn(first_ref, normal * live).reshape(KEPT, 2 * GROUP, feature)
    ones = jnp.broadcast_to(live, (CELLS, LANES)).astype(BF)
    half_ref[:, :, feature:] = (mm(first_ref[0], ones) + mm(first_ref[1], ones)).reshape(KEPT, 2 * GROUP, LANES)


def first(rows, cols, tokens, tables, deps=()):
    cells, feature = tokens.shape
    table = tables["first"]
    return launch(
        deps,
        first_kernel,
        grid=(STEPS,),
        out_shape=jax.ShapeDtypeStruct((KEPT, 2 * ROWS, feature + LANES), F32),
        in_specs=[smem(), smem(), pl.BlockSpec((CELLS, feature), lambda i: (i, 0)), single(table.shape)],
        out_specs=pl.BlockSpec((KEPT, 2 * GROUP, feature + LANES), lambda i: (0, i, 0)),
        compiler_params=params(),
        cost_estimate=cost(6e9, 11e6),
        name="first",
    )(rows, cols, tokens, table)


def build_mix(me, bits, weights_ref, layer, out_ref, feature):
    block = feature // BLOCKS
    half = feature // 2
    per_group = BLOCKS // 2
    share = 2 * feature // weights_ref.shape[0]
    each = block // share
    out_ref[...] = jnp.zeros_like(out_ref)
    row = lax.broadcasted_iota(jnp.int32, (LANES, half), 0)
    column = lax.broadcasted_iota(jnp.int32, (LANES, half), 1)
    for b in range(per_group):
        shift = jnp.where((column - b * block == row) & (row < block), 1.0, 0.0).astype(BF)
        low, high = b * block, (b + 1) * block
        for group in range(2):
            for part in range(2):
                at = (part * BLOCKS + group * per_group + b) * each
                pieces = [
                    weights_ref[place_of((at + k) ^ me, bits), layer * share : (layer + 1) * share, :]
                    for k in range(each)
                ]
                placed = mm(jnp.concatenate(pieces, axis=0), shift).astype(BF)
                for t in range(low // LANES, (high - 1) // LANES + 1):
                    begin, end = max(low, t * LANES), min(high, (t + 1) * LANES)
                    for c in range(low // LANES, (high - 1) // LANES + 1):
                        piece = placed[begin - low : end - low, c * LANES : (c + 1) * LANES]
                        for up in range(2):
                            top = 2 * t * LANES + up * LANES + begin - t * LANES
                            left = (2 * c + (up ^ part)) * LANES
                            value = -piece if part == 1 and up == 1 else piece
                            here = (group, slice(top, top + end - begin), slice(left, left + LANES))
                            out_ref[here] = out_ref[here] + value


def mix_step(half_ref, head_ref, body_ref, back_head_ref, back_body_ref, mix1_ref, mix2_ref, wide_ref, long_ref,
             outs, heads, out_ref, is_head):
    feature = out_ref.shape[2]
    rows = HEAD if is_head else BODY
    spec = turn(head_ref if is_head else body_ref, half_ref[...].reshape(2 * BODY, feature + LANES))
    gain = wide_ref[0:1, :]
    shift = wide_ref[1:2, :]

    def scaled(part):
        flat = jnp.concatenate([part[:, feature:]] * (feature // LANES), axis=1)
        return (part[:, :feature] * gain + flat * shift).astype(BF)

    inside = to_mixed(scaled(spec[:rows]), scaled(spec[rows:]))
    active, slope = gelu_parts(mix_product(inside, mix1_ref) + long_ref[0:1, :])
    hidden = active.astype(BF)
    value = mix_product(hidden, mix2_ref) + long_ref[1:2, :]
    bend = jnp.tanh(value / SHRINK)
    flat = jnp.concatenate([spec[:rows, feature:], spec[rows:, feature:]], axis=1)
    for ref, head, kept in zip(outs, heads, (inside, hidden, slope, bend * bend, flat)):
        ref[...] = kept[:BODY]
        if is_head:
            head[...] = kept[BODY:]
    values = jnp.concatenate(from_mixed(value - SHRINK * bend), axis=0)
    out_ref[...] = turn(back_head_ref if is_head else back_body_ref, values).reshape(GROUP, 2 * ROWS, feature)


def mix_first_kernel(
    weight_bits, vector_bits, me_ref, half_ref, weights_ref, vector_ref, head_ref, body_ref, back_head_ref, back_body_ref,
    out_ref, low_ref, hidden_ref, slope_ref, bend_ref, flat_ref,
    low_head_ref, hidden_head_ref, slope_head_ref, bend_head_ref, flat_head_ref, mix1_ref, mix2_ref, wide_ref, long_ref, up_ref,
):
    feature = out_ref.shape[2]
    devices = vector_ref.shape[1]
    share = feature // devices
    step = pl.program_id(0)
    outs = (low_ref, hidden_ref, slope_ref, bend_ref, flat_ref)
    heads = (low_head_ref, hidden_head_ref, slope_head_ref, bend_head_ref, flat_head_ref)
    work = functools.partial(
        mix_step, half_ref, head_ref, body_ref, back_head_ref, back_body_ref, mix1_ref, mix2_ref, wide_ref, long_ref,
        outs, heads, out_ref,
    )

    @pl.when(step == 0)
    def _():
        me = me_ref[0]
        build_mix(me, weight_bits, weights_ref, 0, mix1_ref, feature)
        build_mix(me, weight_bits, weights_ref, 1, mix2_ref, feature)
        wide_ref[...] = jnp.zeros_like(wide_ref)
        long_ref[...] = jnp.zeros_like(long_ref)
        for row, at in enumerate((2, 3, 4, 5, 7)):
            wide_ref[row : row + 1, :] = spread(vector_ref[at], share, me, vector_bits)
        for row in range(2):
            both = spread(vector_ref[row], 2 * share, me, vector_bits)
            long_ref[row : row + 1, :] = to_mixed(both[:, :feature], both[:, feature:])
        up_ref[...] = spread(vector_ref[6], up_ref.shape[1] // devices, me, vector_bits)
        work(True)

    @pl.when(step > 0)
    def _():
        work(False)


def mix_second_kernel(
    half_ref, mix1_ref, mix2_ref, wide_ref, long_ref, body_ref, back_body_ref,
    out_ref, *outs,
):
    mix_step(
        half_ref, None, body_ref, None, back_body_ref, mix1_ref, mix2_ref, wide_ref, long_ref,
        outs, (None,) * 5, out_ref, False,
    )


def mode_shapes(rows, feature):
    wide = [jax.ShapeDtypeStruct((rows, 2 * feature), kind) for kind in (BF, BF, F32, F32)]
    return wide + [jax.ShapeDtypeStruct((rows, 2 * LANES), F32)]


def mode_blocks(feature):
    return [pl.BlockSpec((BODY, width), lambda i: (i, 0)) for width in (2 * feature,) * 4 + (2 * LANES,)]


def half_block(width, begin=0):
    return pl.BlockSpec((GROUP, 2 * ROWS, width), lambda i: (i + begin, 0, 0))


def mix_first(me, half, weights, vectors, tables, hidden, steps, weight_bits, vector_bits, deps=()):
    feature = half.shape[2] - LANES
    fixed = (weights, vectors, tables["head"], tables["body"], tables["head_wt"], tables["body_wt"])
    more = (
        jax.ShapeDtypeStruct((2, feature, feature), BF),
        jax.ShapeDtypeStruct((2, feature, feature), BF),
        jax.ShapeDtypeStruct((8, feature), F32),
        jax.ShapeDtypeStruct((8, 2 * feature), F32),
        jax.ShapeDtypeStruct((1, hidden), F32),
    )
    heads = mode_shapes(ROWS, feature)
    return launch(
        deps,
        functools.partial(mix_first_kernel, weight_bits, vector_bits),
        grid=(steps,),
        out_shape=[jax.ShapeDtypeStruct((GROUP * steps, 2 * ROWS, feature), F32)]
        + mode_shapes(BODY * steps, feature) + heads + list(more),
        in_specs=[smem(), half_block(feature + LANES)] + [single(v.shape) for v in fixed],
        out_specs=[half_block(feature)] + mode_blocks(feature) + [single(v.shape) for v in heads]
        + [single(v.shape) for v in more],
        compiler_params=params(),
        cost_estimate=cost(9e9, 20e6),
        name="mix_first",
    )(me, half, *fixed)


def mix_second(half, mix1, mix2, wide, long, tables, begin, steps, deps=()):
    feature = half.shape[2] - LANES
    fixed = (mix1, mix2, wide, long, tables["body"], tables["body_wt"])
    return launch(
        deps,
        mix_second_kernel,
        grid=(steps,),
        out_shape=[jax.ShapeDtypeStruct((GROUP * steps, 2 * ROWS, feature), F32)] + mode_shapes(BODY * steps, feature),
        in_specs=[half_block(feature + LANES, begin)] + [single(v.shape) for v in fixed],
        out_specs=[half_block(feature)] + mode_blocks(feature),
        compiler_params=params(),
        cost_estimate=cost(9e9, 20e6),
        name="mix_second",
    )(half, *fixed)


def space_kernel(rows_ref, cols_ref, half1_ref, half2_ref, tokens_ref, first_t_ref, wide_ref, middle_ref, normed_ref):
    feature = tokens_ref.shape[1]
    flat = lambda ref: ref[...].reshape(-1, feature)
    spatial = turn(first_t_ref, jnp.concatenate([flat(half1_ref), flat(half2_ref)], axis=0))
    inputs = tokens_ref[...].astype(F32)
    live = live_rows(pl.program_id(0) * CELLS, CELLS, rows_ref, cols_ref)
    normal, _ = normalize(inputs)
    middle = inputs + live * (spatial + (normal * wide_ref[0:1, :] + wide_ref[1:2, :]))
    middle_ref[...] = middle
    normal, _ = normalize(middle)
    normed_ref[...] = (normal * wide_ref[2:3, :] + wide_ref[3:4, :]).astype(BF)


def column_block(rows, width):
    return pl.BlockSpec((rows, 2 * GROUP, width), lambda i: (0, i, 0))


def space(rows, cols, half1, half2, tokens, wide, tables, deps=()):
    cells, feature = tokens.shape
    table = tables["first_t"]
    block = pl.BlockSpec((CELLS, feature), lambda i: (i, 0))
    return launch(
        deps,
        space_kernel,
        grid=(STEPS,),
        out_shape=(jax.ShapeDtypeStruct((cells, feature), F32), jax.ShapeDtypeStruct((cells, feature), BF)),
        in_specs=[smem(), smem(), column_block(half1.shape[0], feature), column_block(half2.shape[0], feature),
                  block, single(table.shape), single(wide.shape)],
        out_specs=(block, block),
        compiler_params=params(),
        cost_estimate=cost(6e9, 20e6),
        name="space",
    )(rows, cols, half1, half2, tokens, table, wide)


def fetch_weights(me_ref, pieces, places, up_ref, down_ref, sems):
    count = pieces[0].shape[0] * 2
    chip = me_ref[0] // 2

    def copies(own, core):
        target = (up_ref, down_ref)[core]
        source = pieces[:2] if own else pieces[2:]
        for mask in range(count):
            at = places[core][mask]
            part = source[at // (count // 2)].at[at % (count // 2)]
            yield pltpu.make_async_copy(part, target.at[chip ^ mask], sems.at[core, mask])

    for core in range(2):
        @pl.when(me_ref[0] % 2 == core)
        def _():
            for copy in copies(True, core):
                copy.start()
            for copy in copies(False, 1 - core):
                copy.start()

    def arrived(core):
        for copy in copies(True, core):
            copy.wait()

    return arrived


def weight_scratch(pieces):
    chips, rows, feature = pieces[0].shape[0] * 2, pieces[0].shape[1], pieces[0].shape[2]
    return [
        pltpu.VMEM((chips, rows, feature), BF),
        pltpu.VMEM((chips, rows, feature), BF),
        pltpu.SemaphoreType.DMA((2, chips)),
    ]


def up_part(up_ref, j, feature):
    share = up_ref.shape[1] * feature // (up_ref.shape[0] * up_ref.shape[1])
    return up_ref[:, j * share : (j + 1) * share, :].reshape(feature, feature)


def down_part(down_ref, j, feature):
    share = down_ref.shape[1]
    each = feature // share
    return down_ref[j * each : (j + 1) * each].reshape(feature, feature)


def up_kernel(places, rows_ref, cols_ref, me_ref, normed_ref, grad_ref, bias_ref, *rest):
    pieces = rest[:4]
    active_ref, pre_ref, live_ref, bias_grad_ref, up_all_ref, down_all_ref, up_ref, down_ref, sems, out_sems = rest[4:]
    tile, feature = normed_ref.shape
    step = pl.program_id(0)
    copies = [
        pltpu.make_async_copy(source, target, out_sems.at[k])
        for k, (source, target) in enumerate(((up_ref, up_all_ref), (down_ref, down_all_ref)))
    ]

    def work(arrived):
        live = live_rows(step * tile, tile, rows_ref, cols_ref)
        branch = (grad_ref[...].astype(F32) * live).astype(BF)
        live_ref[...] = branch
        normed = normed_ref[...]
        if arrived:
            arrived(0)
            copies[0].start()
        for j in range(active_ref.shape[1] // feature):
            place = slice(j * feature, (j + 1) * feature)
            value = mm(normed, up_part(up_ref, j, feature)) + bias_ref[:, place]
            if arrived and j == 0:
                arrived(1)
                copies[1].start()
            grad = mm(branch, down_part(down_ref, j, feature), (1, 1))
            active, slope = gelu_parts(value)
            active_ref[:, place] = active.astype(BF)
            low = (grad * slope).astype(BF)
            pre_ref[:, place] = low
            bias_grad_ref[:, place] += jnp.sum(low.astype(F32), axis=0, keepdims=True)

    @pl.when(step == 0)
    def _():
        bias_grad_ref[...] = jnp.zeros_like(bias_grad_ref)
        work(fetch_weights(me_ref, pieces, places, up_ref, down_ref, sems))

    @pl.when(step > 0)
    def _():
        work(None)

    @pl.when(step == pl.num_programs(0) - 1)
    def _():
        for copy in copies:
            copy.wait()


def feed_up(rows, cols, me, normed, grad, bias, pieces, places, tile=256, deps=()):
    cells, feature = normed.shape
    hidden = bias.shape[1]
    block = lambda width: pl.BlockSpec((tile, width), lambda i: (i, 0))
    weights = jax.ShapeDtypeStruct((2 * pieces[0].shape[0],) + pieces[0].shape[1:], BF)
    return launch(
        deps,
        functools.partial(up_kernel, places),
        grid=(cells // tile,),
        out_shape=(
            jax.ShapeDtypeStruct((cells, hidden), BF),
            jax.ShapeDtypeStruct((cells, hidden), BF),
            jax.ShapeDtypeStruct((cells, feature), BF),
            jax.ShapeDtypeStruct((1, hidden), F32),
            weights,
            weights,
        ),
        in_specs=[smem(), smem(), smem(), block(feature), block(feature), single(bias.shape)]
        + [any_space() for _ in pieces],
        out_specs=(block(hidden), block(hidden), block(feature), single((1, hidden)), any_space(), any_space()),
        scratch_shapes=weight_scratch(pieces) + [pltpu.SemaphoreType.DMA((2,))],
        compiler_params=params(),
        cost_estimate=cost(0, 0),
        name="feed_up",
    )(rows, cols, me, normed, grad, bias, *pieces)


def weight_grad_kernel(places, me_ref, active_ref, pre_ref, branch_ref, normed_ref, send_ref, keep_ref, stage_ref, sems):
    step = pl.program_id(0)
    steps = pl.num_programs(0) // 2
    feature = branch_ref.shape[1]
    chips, rows, _ = send_ref.shape
    each = feature // rows
    share = feature // chips

    def down_copies(j, target):
        for c in range(each):
            source = stage_ref.at[j, pl.ds(c * rows, rows)]
            yield pltpu.make_async_copy(source, target.at[places[1][j * each + c]], sems.at[j, c])

    def up_copies(j, target):
        for c in range(chips):
            source = stage_ref.at[steps + j, pl.ds(c * share, share)]
            there = target.at[places[0][c], pl.ds(j * share, share)]
            yield pltpu.make_async_copy(source, there, sems.at[steps + j, c])

    @pl.when(step < steps)
    def _():
        stage_ref[step] = mm(active_ref[...], branch_ref[...], (0, 0)).astype(BF)

    @pl.when(step >= steps)
    def _():
        stage_ref[step] = mm(normed_ref[...], pre_ref[...], (0, 0)).astype(BF)

    total = stage_ref.shape[0] // 2
    for j in range(total):
        for core in range(2):
            targets = (send_ref, keep_ref) if core == 0 else (keep_ref, send_ref)

            @pl.when((step == j) & (me_ref[0] % 2 == core))
            def _():
                for copy in down_copies(j, targets[0]):
                    copy.start()

            @pl.when((step == total + j) & (me_ref[0] % 2 == core))
            def _():
                for copy in up_copies(j, targets[1]):
                    copy.start()

    @pl.when(step == 2 * steps - 1)
    def _():
        for j in range(total):
            for copy in down_copies(j, send_ref):
                copy.wait()
            for copy in up_copies(j, send_ref):
                copy.wait()


def weight_grads(me, active, pre, branch, normed, places, deps=()):
    cells, hidden = active.shape
    feature = branch.shape[1]
    tiles = hidden // feature
    chips = UNITS
    shape = jax.ShapeDtypeStruct((chips, hidden // chips, feature), BF)
    return launch(
        deps,
        functools.partial(weight_grad_kernel, places),
        grid=(2 * tiles,),
        out_shape=(shape, shape),
        in_specs=[
            smem(),
            pl.BlockSpec((cells, feature), lambda i: (0, jnp.minimum(i, tiles - 1))),
            pl.BlockSpec((cells, feature), lambda i: (0, jnp.maximum(i - tiles, 0))),
            single(branch.shape), single(normed.shape),
        ],
        out_specs=(any_space(), any_space()),
        scratch_shapes=[
            pltpu.VMEM((2 * tiles, feature, feature), BF),
            pltpu.SemaphoreType.DMA((2 * tiles, chips)),
        ],
        compiler_params=params(),
        cost_estimate=cost(4 * cells * feature * hidden, 40e6),
        name="weight_grads",
    )(me, active, pre, branch, normed)


def down_kernel(begin, rows_ref, cols_ref, active_ref, pre_ref, middle_ref, grad_ref, tokens_ref, wide_ref,
                first_ref, up_all_ref, down_all_ref, *rest):
    old_sums_ref = rest[0] if begin else None
    mixed_ref, grad_middle_ref, half_ref, sums_ref, up_ref, down_ref, sems = rest[-7:]
    tile, feature = middle_ref.shape
    parts = active_ref.shape[1] // feature
    step = pl.program_id(0)
    down_rows = down_ref.shape[0] // parts
    up_rows = up_ref.shape[1] // parts
    down_copy = lambda j: pltpu.make_async_copy(
        down_all_ref.at[pl.ds(j * down_rows, down_rows)], down_ref.at[pl.ds(j * down_rows, down_rows)], sems.at[0, j]
    )
    up_copy = lambda j: pltpu.make_async_copy(
        up_all_ref.at[:, pl.ds(j * up_rows, up_rows)], up_ref.at[:, pl.ds(j * up_rows, up_rows)], sems.at[1, j]
    )

    @pl.when(step == 0)
    def _():
        for j in range(parts):
            down_copy(j).start()
        for j in range(parts):
            up_copy(j).start()
        sums_ref[...] = old_sums_ref[...] if begin else jnp.zeros_like(sums_ref)

    def work(waits):
        live = live_rows((step + begin) * tile, tile, rows_ref, cols_ref)
        branch = jnp.zeros((tile, feature), F32)
        for j in range(parts):
            if waits:
                down_copy(j).wait()
            active = active_ref[:, j * feature : (j + 1) * feature]
            branch = branch + mm(active, down_part(down_ref, j, feature))
        grad_normed = jnp.zeros((tile, feature), F32)
        for j in range(parts):
            if waits:
                up_copy(j).wait()
            pre = pre_ref[:, j * feature : (j + 1) * feature]
            grad_normed = grad_normed + mm(pre, up_part(up_ref, j, feature), (1, 1))
        middle = middle_ref[...]
        mixed_ref[...] = (middle + live * (branch + wide_ref[4:5, :])).astype(BF)
        normal, inverse = normalize(middle)
        cotangent = grad_ref[...].astype(F32)
        grad_middle = cotangent + norm_back(grad_normed, wide_ref[2:3, :], normal, inverse)
        grad_middle_ref[...] = grad_middle
        masked = grad_middle * live
        half_ref[...] = turn(first_ref, masked).reshape(half_ref.shape)
        first_normal, _ = normalize(tokens_ref[...].astype(F32))
        rows = (grad_normed * normal, grad_normed, (cotangent * live).astype(BF).astype(F32), masked * first_normal, masked)
        for row, value in enumerate(rows):
            sums_ref[row : row + 1, :] += jnp.sum(value, axis=0, keepdims=True)

    @pl.when(step == 0)
    def _():
        work(True)

    @pl.when(step > 0)
    def _():
        work(False)


def feed_down(rows, cols, active, pre, middle, grad, tokens, wide, table, up, down, begin, steps, before=(), deps=()):
    cells, feature = middle.shape
    hidden = active.shape[1]
    block = lambda width: pl.BlockSpec((CELLS, width), lambda i: (i + begin, 0))
    operands = (rows, cols, active, pre, middle, grad, tokens, wide, table, up, down)
    extra = ()
    aliases = {}
    if begin:
        extra = (before[3],) + tuple(before[:3])
        aliases = {len(operands) + 1 + k: k for k in range(3)}
    return launch(
        deps,
        functools.partial(down_kernel, begin),
        grid=(steps,),
        out_shape=(
            jax.ShapeDtypeStruct((cells, feature), BF),
            jax.ShapeDtypeStruct((cells, feature), F32),
            jax.ShapeDtypeStruct((KEPT, 2 * ROWS, feature), F32),
            jax.ShapeDtypeStruct((8, feature), F32),
        ),
        in_specs=[smem(), smem(), block(hidden), block(hidden), block(feature), block(feature), block(feature),
                  single(wide.shape), single(table.shape), any_space(), any_space()]
        + [single(v.shape) for v in extra[:1]] + [any_space() for _ in extra[1:]],
        out_specs=(block(feature), block(feature),
                   pl.BlockSpec((KEPT, 2 * GROUP, feature), lambda i: (0, i + begin, 0)), single((8, feature))),
        scratch_shapes=[
            pltpu.VMEM(up.shape, BF), pltpu.VMEM(down.shape, BF), pltpu.SemaphoreType.DMA((2, hidden // feature))
        ],
        input_output_aliases=aliases,
        compiler_params=params(),
        cost_estimate=cost(0, 0),
        name="feed_down_b" if begin else "feed_down_a",
    )(*operands, *extra)


def back_step(half_ref, head_ref, body_ref, back_head_ref, back_body_ref, mix1_ref, mix2_ref, ins, in_heads,
              outs, out_heads, out_ref, sums_ref, is_head):
    feature = out_ref.shape[2]
    rows = HEAD if is_head else BODY

    def read(k):
        if is_head:
            return jnp.concatenate([ins[k][...], in_heads[k][...]], axis=0)
        return ins[k][...]

    grad = turn(head_ref if is_head else body_ref, half_ref[...].reshape(2 * BODY, feature))
    grad_two = (to_mixed(grad[:rows], grad[rows:]) * read(1)).astype(BF)
    grad_one = (mix_product(grad_two, mix2_ref, True) * read(0)).astype(BF)
    grad_spec = mix_product(grad_one, mix1_ref, True)
    values = jnp.concatenate(from_mixed(grad_spec), axis=0)
    out_ref[...] = turn(back_head_ref if is_head else back_body_ref, values).reshape(GROUP, 2 * ROWS, feature)
    for row, value in enumerate((grad_one, grad_two)):
        outs[row][...] = value[:BODY]
        if is_head:
            out_heads[row][...] = value[BODY:]
    flat = jnp.concatenate([read(3)] * (feature // LANES), axis=1)
    for row, value in enumerate((grad_one.astype(F32), grad_two.astype(F32), grad_spec * read(2).astype(F32), grad_spec * flat)):
        total = jnp.sum(value, axis=0, keepdims=True)
        sums_ref[row : row + 1, :] = total if is_head else sums_ref[row : row + 1, :] + total


def mix_back_kernel(
    half_ref, slope1_ref, slope2_ref, bend1_ref, bend2_ref, low1_ref, low2_ref, flat1_ref, flat2_ref,
    slope_head_ref, bend_head_ref, low_head_ref, flat_head_ref, mix1_ref, mix2_ref,
    head_ref, body_ref, back_head_ref, back_body_ref,
    out_ref, one_ref, two_ref, one_head_ref, two_head_ref, sums_ref,
):
    step = pl.program_id(0)
    steps = pl.num_programs(0) // 2
    work = functools.partial(
        back_step, half_ref, head_ref, body_ref, back_head_ref, back_body_ref, mix1_ref, mix2_ref
    )
    heads = (slope_head_ref, bend_head_ref, low_head_ref, flat_head_ref)
    more = (heads, (one_ref, two_ref), (one_head_ref, two_head_ref), out_ref, sums_ref)
    near = (slope1_ref, bend1_ref, low1_ref, flat1_ref)
    far = (slope2_ref, bend2_ref, low2_ref, flat2_ref)

    @pl.when(step == 0)
    def _():
        sums_ref[...] = jnp.zeros_like(sums_ref)
        work(near, *more, True)

    @pl.when((step > 0) & (step < steps))
    def _():
        work(near, *more, False)

    @pl.when(step >= steps)
    def _():
        work(far, *more, False)


def mix_back(half, modes1, modes2, heads, mix1, mix2, tables, deps=()):
    feature = half.shape[2]
    steps = KEPT // GROUP
    fixed = tuple(heads[k] for k in (2, 3, 0, 4)) + (
        mix1, mix2, tables["head_w"], tables["body_w"], tables["head_t"], tables["body_t"]
    )
    moving = []
    specs = []
    for k in (2, 3, 0, 4):
        width = modes1[k].shape[1]
        moving += [modes1[k], modes2[k]]
        specs += [
            pl.BlockSpec((BODY, width), lambda i: (jnp.minimum(i, steps // 2 - 1), 0)),
            pl.BlockSpec((BODY, width), lambda i: (jnp.maximum(i - steps // 2, 0), 0)),
        ]
    low = lambda rows: jax.ShapeDtypeStruct((rows, 2 * feature), BF)
    body = pl.BlockSpec((BODY, 2 * feature), lambda i: (i, 0))
    shapes = (
        jax.ShapeDtypeStruct((KEPT, 2 * ROWS, feature), F32), low(BODY * steps), low(BODY * steps),
        low(ROWS), low(ROWS), jax.ShapeDtypeStruct((8, 2 * feature), F32),
    )
    return launch(
        deps,
        mix_back_kernel,
        grid=(steps,),
        out_shape=shapes,
        in_specs=[half_block(feature)] + specs + [single(v.shape) for v in fixed],
        out_specs=[half_block(feature), body, body] + [single(v.shape) for v in shapes[3:]],
        compiler_params=params(),
        cost_estimate=cost(18e9, 30e6),
        name="mix_back",
    )(half, *moving, *fixed)


def block_kernel(left1_ref, left2_ref, left_head_ref, right_ref, right_head_ref, out_ref, natural_ref):
    wide = 2 * LANES
    count = left1_ref.shape[1] // wide
    cut = left1_ref.shape[0]
    for t in range(count):
        for c in range(max(t - 1, 0), min(t + 2, count)):
            left, right = slice(t * wide, (t + 1) * wide), slice(c * wide, (c + 1) * wide)
            total = (
                mm(left1_ref[:, left], right_ref[:cut, right], (0, 0))
                + mm(left2_ref[:, left], right_ref[cut:, right], (0, 0))
                + mm(left_head_ref[:, left], right_head_ref[:, right], (0, 0))
            )
            rows, lanes = slice(t * LANES, (t + 1) * LANES), slice(c * LANES, (c + 1) * LANES)
            natural_ref[0, rows, lanes] = total[:LANES, :LANES] + total[LANES:, LANES:]
            natural_ref[1, rows, lanes] = total[:LANES, LANES:] - total[LANES:, :LANES]
    per_group = BLOCKS // 2
    block = count * LANES // per_group
    for b in range(per_group):
        begin = b * block
        base = begin // LANES * LANES
        reach = min(base + wide, count * LANES) - base
        for part in range(2):
            piece = natural_ref[part, begin : begin + block, base : base + reach]
            if begin > base:
                piece = pltpu.roll(piece, reach - (begin - base), axis=1)
            out_ref[part, b * block : (b + 1) * block, :] = piece[:, :LANES]


def block_grads(left1, left2, left_head, right, right_head, name, deps=()):
    feature = left1.shape[1] // 2
    half = feature // 2
    block = lambda v: pl.BlockSpec((v.shape[0], feature), lambda i: (0, i))
    return launch(
        deps,
        block_kernel,
        grid=(2,),
        out_shape=jax.ShapeDtypeStruct((2, feature, LANES), F32),
        in_specs=[block(v) for v in (left1, left2, left_head, right, right_head)],
        out_specs=pl.BlockSpec((2, half, LANES), lambda i: (0, i, 0)),
        scratch_shapes=[pltpu.VMEM((2, half, half), F32)],
        compiler_params=params(),
        cost_estimate=cost(5e9, 7e6),
        name=name,
    )(left1, left2, left_head, right, right_head)


def last_kernel(begin, rows_ref, cols_ref, half_ref, tokens_ref, grad_ref, first_t_ref, wide_ref, *rest):
    out_ref = rest[-1]
    tile, feature = tokens_ref.shape
    live = live_rows((pl.program_id(0) + begin) * tile, tile, rows_ref, cols_ref)
    grad_middle = grad_ref[...]
    grad_normed = live * (grad_middle + turn(first_t_ref, half_ref[...].reshape(CELLS, feature)))
    normal, inverse = normalize(tokens_ref[...].astype(F32))
    out_ref[...] = grad_middle + norm_back(grad_normed, wide_ref[0:1, :], normal, inverse)


def last(rows, cols, half, tokens, grad, wide, tables, begin, steps, before=(), deps=()):
    cells, feature = tokens.shape
    first_t = tables["first_t"]
    block = pl.BlockSpec((CELLS, feature), lambda i: (i + begin, 0))
    operands = (rows, cols, half, tokens, grad, first_t, wide)
    return launch(
        deps,
        functools.partial(last_kernel, begin),
        grid=(steps,),
        out_shape=jax.ShapeDtypeStruct((cells, feature), F32),
        in_specs=[smem(), smem(), pl.BlockSpec((KEPT, 2 * GROUP, feature), lambda i: (0, i + begin, 0)), block, block,
                  single(first_t.shape), single(wide.shape)] + [any_space() for _ in before],
        out_specs=block,
        input_output_aliases={len(operands): 0} if before else {},
        compiler_params=params(),
        cost_estimate=cost(6e9, 20e6),
        name="last",
    )(*operands, *before)


def collect(value, per_device, devices):
    total = value.shape[1]
    owner = lax.broadcasted_iota(jnp.int32, (devices, total), 1) // per_device
    row = lax.broadcasted_iota(jnp.int32, (devices, total), 0)
    high, low = split(jnp.where(owner == row, jnp.broadcast_to(value, (devices, total)), 0.0))
    place = lax.broadcasted_iota(jnp.int32, (total, LANES), 0)
    lane = lax.broadcasted_iota(jnp.int32, (total, LANES), 1)
    pick = jnp.where(place % per_device == lane, 1.0, 0.0).astype(BF)
    return mm(high, pick) + mm(low, pick)


def emit(upper_ref, sum_ref, send_ref, keep_ref):
    rows = sum_ref.shape[2] - 8
    half = sum_ref.shape[0]
    away = sum_ref[:, pl.ds(1 - upper_ref[0], 1)].reshape(half, rows + 8, LANES)
    high, low = split(away[:, rows:])
    send_ref[:, :rows] = away[:, :rows].astype(BF)
    send_ref[:, rows:] = jnp.concatenate([high.astype(F32), low.astype(F32)], axis=1).astype(BF)
    keep_ref[...] = sum_ref[:, pl.ds(upper_ref[0], 1)].reshape(half, rows + 8, LANES)


def pack_kernel(upper_ref, one_ref, two_ref, mixed_ref, sums_ref, up_ref, wide_ref, send_ref, keep_ref, sum_ref):
    half, _, rows, _ = sum_ref.shape
    devices = 2 * half
    share = (rows - 8) // 4
    feature = sums_ref.shape[1]
    sum_ref[:, :, : 2 * share] = one_ref[...].reshape(half, 2, 2 * share, LANES)
    sum_ref[:, :, 2 * share : 4 * share] = two_ref[...].reshape(half, 2, 2 * share, LANES)
    first_gain, first_bias = scale_grads(mixed_ref, sums_ref, wide_ref)
    natural = [jnp.concatenate(from_mixed(mixed_ref[k : k + 1, :]), axis=1) for k in range(2)]
    narrow = [first_gain, first_bias] + [sums_ref[k : k + 1, :] for k in range(3)]
    for k, value in enumerate(narrow + natural + [up_ref[...]]):
        placed = collect(value, value.shape[1] // devices, devices)
        for d in range(devices):
            sum_ref[d // 2, d % 2, 4 * share + k : 4 * share + k + 1, :] = placed[d : d + 1, :]
    emit(upper_ref, sum_ref, send_ref, keep_ref)


def scale_grads(mixed_ref, sums_ref, wide_ref):
    real, imag = from_mixed(mixed_ref[2:3, :])
    scaled = real + imag
    real, imag = from_mixed(mixed_ref[3:4, :])
    flat = real + imag
    gain = sums_ref[3:4, :] + (scaled - wide_ref[1:2, :] * flat) / wide_ref[0:1, :]
    return gain, sums_ref[4:5, :] + flat


def small_shapes(half, rows):
    return (
        jax.ShapeDtypeStruct((half, rows + 8, LANES), BF),
        jax.ShapeDtypeStruct((half, rows, LANES), F32),
    )


def pack(upper, one, two, mixed, sums, up, wide, devices):
    rows = 2 * one.shape[0] * one.shape[1] // devices + 8
    shapes = small_shapes(devices // 2, rows)
    operands = (one, two, mixed, sums, up, wide)
    return pl.pallas_call(
        pack_kernel,
        out_shape=shapes,
        in_specs=[smem()] + vmem(len(operands)),
        out_specs=vmem(2),
        scratch_shapes=[pltpu.VMEM((devices // 2, 2, rows, LANES), F32)],
        compiler_params=params(),
        cost_estimate=cost(0, 0),
        name="pack",
    )(upper, *operands)


def merge_small(keep_ref, got_ref):
    rows = keep_ref.shape[1] - 8
    tail = got_ref[:, rows:].astype(F32)
    return (
        keep_ref[:, :rows] + got_ref[:, :rows].astype(F32),
        keep_ref[:, rows:] + tail[:, :8] + tail[:, 8:],
    )


def fold_small_kernel(upper_ref, keep_ref, got_ref, send_ref, out_ref, sum_ref):
    half, _, rows, _ = sum_ref.shape
    top, tail = merge_small(keep_ref, got_ref)
    sum_ref[:, :, : rows - 8] = top.reshape(half, 2, rows - 8, LANES)
    sum_ref[:, :, rows - 8 :] = tail.reshape(half, 2, 8, LANES)
    emit(upper_ref, sum_ref, send_ref, out_ref)


def fold_small(keep, got, upper, deps=()):
    half, rows = keep.shape[0] // 2, keep.shape[1]
    return launch(
        deps,
        fold_small_kernel,
        out_shape=small_shapes(half, rows),
        in_specs=[smem()] + vmem(2),
        out_specs=vmem(2),
        scratch_shapes=[pltpu.VMEM((half, 2, rows, LANES), F32)],
        compiler_params=params(),
        cost_estimate=cost(0, 0),
        name="fold_small",
    )(upper, keep, got)


def vmem(count):
    return [pl.BlockSpec(memory_space=pltpu.VMEM)] * count


def end_small_kernel(keep_ref, got_ref, out_ref):
    top, tail = merge_small(keep_ref, got_ref)
    out_ref[: out_ref.shape[0] - 8, :] = top[0]
    out_ref[out_ref.shape[0] - 8 :, :] = tail[0]


def end_small(keep, got):
    return pl.pallas_call(
        end_small_kernel,
        out_shape=jax.ShapeDtypeStruct(keep.shape[1:], F32),
        in_specs=vmem(2),
        out_specs=vmem(1)[0],
        compiler_params=params(),
        cost_estimate=cost(0, 0),
        name="end_small",
    )(keep, got)


AXES = ("dp", "fsdp")


def swap(value, devices, bits):
    return lax.ppermute(value, AXES, [(i, i ^ (1 << bits[i & 1])) for i in range(devices)])


def doubling_orders(count):
    first = list(range(count - 1, 0, -1))
    second = list(first)
    for k in range(0, len(second) - 1, 2):
        second[k], second[k + 1] = second[k + 1], second[k]
    return first, second


def places_of(order):
    return [
        sum(1 << k for k, bit in enumerate(order) if mask >> (bit - 1) & 1) for mask in range(1 << len(order))
    ]


def pair_kernel(held_ref, got_ref, out_ref):
    count = held_ref.shape[0]
    out_ref[:count] = held_ref[...]
    out_ref[count:] = got_ref[...]


def pair(held, got, deps=()):
    shape = jax.ShapeDtypeStruct((2 * held.shape[0],) + held.shape[1:], held.dtype)
    return launch(
        deps,
        pair_kernel,
        out_shape=shape,
        in_specs=[pl.BlockSpec(memory_space=pltpu.VMEM)] * 2,
        out_specs=pl.BlockSpec(memory_space=pltpu.VMEM),
        compiler_params=params(),
        cost_estimate=cost(0, 4 * held.size * 2),
        name="pair",
    )(held, got)


def hold(value, deps):
    def body(*refs):
        pass

    return pl.pallas_call(
        body,
        out_shape=jax.ShapeDtypeStruct(value.shape, value.dtype),
        in_specs=[any_space() for _ in range(1 + len(deps))],
        out_specs=any_space(),
        input_output_aliases={0: 0},
        compiler_params=params(),
        cost_estimate=cost(0, 0),
        name="hold",
    )(value, *deps)


def gather_small(value, me, devices, count):
    held = value[None]
    for bit in list(range(3, count)) + [2, 1, 0]:
        other = swap(held, devices, (bit, bit))
        upper = (me >> bit) & 1
        axis = 0 if bit > 2 else 1
        join_two = lambda a, b: jnp.stack([a, b], axis=axis).reshape((-1,) + value.shape)
        held = jnp.where(upper == 0, join_two(held, other), join_two(other, held))
    return held


def scatter_small(value, me, devices, count, exact):
    shape = value.shape[1:]
    rows = shape[0]
    total = value
    for bit in [0, 1, 2] + list(range(count - 1, 2, -1)):
        upper = (me >> bit) & 1
        axis = 0 if bit > 2 else 1
        pair = total.reshape(((2, -1) if bit > 2 else (-1, 2)) + shape)
        away = lax.dynamic_index_in_dim(pair, 1 - upper, axis, keepdims=False)
        keep = lax.dynamic_index_in_dim(pair, upper, axis, keepdims=False)
        sums = away[:, rows - exact :]
        top = lax.reduce_precision(sums, 8, 7)
        packet = jnp.concatenate([away[:, : rows - exact], top, sums - top], axis=1).astype(BF)
        got = swap(packet, devices, (bit, bit)).astype(F32)
        low = got[:, rows - exact : rows] + got[:, rows:]
        total = keep + jnp.concatenate([got[:, : rows - exact], low], axis=1)
    return total[0]


def chip_unit(up, down, core, devices):
    parts, share, feature = up.shape
    flat = up.reshape(parts * share, feature)
    other = swap(jnp.where(core == 0, down, flat), devices, (0, 0))
    up_unit = jnp.concatenate([up, other.reshape(up.shape)], axis=1).reshape(2 * parts * share, feature)
    return jnp.where(core == 0, up_unit, jnp.concatenate([other, down]))[None]


def fold_kernel(upper_ref, keep_away_ref, got_away_ref, keep_own_ref, got_own_ref, send_ref, keep_ref):
    send_ref[...] = (keep_away_ref[...].astype(F32) + got_away_ref[...].astype(F32)).astype(BF)
    keep_ref[...] = (keep_own_ref[...].astype(F32) + got_own_ref[...].astype(F32)).astype(BF)


def fold(keep, got, upper, deps=()):
    half = keep.shape[0] // 2
    each = min(2, half)
    unit = (each,) + keep.shape[1:]
    count = len(deps)
    away = pl.BlockSpec(unit, lambda i, up: ((1 - up[0]) * (half // each) + i, 0, 0))
    own = pl.BlockSpec(unit, lambda i, up: (up[0] * (half // each) + i, 0, 0))
    out = pl.BlockSpec(unit, lambda i, up: (i, 0, 0))
    shape = jax.ShapeDtypeStruct((half,) + keep.shape[1:], BF)

    def body(*refs):
        fold_kernel(*refs[:5], *refs[5 + count :])

    return pl.pallas_call(
        body,
        grid_spec=pltpu.PrefetchScalarGridSpec(
            num_scalar_prefetch=1,
            grid=(half // each,),
            in_specs=[away, away, own, own] + [any_space() for _ in deps],
            out_specs=[out, out],
        ),
        out_shape=(shape, shape),
        compiler_params=params(),
        cost_estimate=cost(0, 6 * half * keep[0].size),
        name="fold",
    )(upper, keep, got, keep, got, *deps)


def on_device(
    tokens, grad_out, region_rows, region_cols, ln1_gain, ln1_bias, spec_w1, spec_b1, spec_w2, spec_b2,
    ln2_gain, ln2_bias, w_up, up_bias, w_down, down_bias,
):
    devices = lax.axis_size(AXES[0]) * lax.axis_size(AXES[1])
    count = devices.bit_length() - 1
    me = lax.axis_index(AXES).astype(jnp.int32)
    core = me & 1
    me_one = me.reshape(1)
    feature = tokens.shape[-1]
    block = feature // BLOCKS
    share = ln1_gain.shape[0]
    cells = tokens.shape[1] * tokens.shape[2]
    hidden = w_up.shape[1]
    parts = hidden // feature
    tables = {name: jnp.asarray(value) for name, value in wave_matrices().items()}
    orders = doubling_orders(count)
    places = tuple(places_of(order) for order in orders)
    flat_tokens = tokens.reshape(cells, feature)
    flat_grad = grad_out.reshape(cells, feature)
    fast = devices // 2 == UNITS
    step = lambda value, k: swap(value, devices, (orders[0][k], orders[1][k]))

    padded = lambda v: jnp.pad(v, ((0, 0), (0, LANES - v.shape[1])))
    vectors = (spec_b1, spec_b2, ln1_gain, ln1_bias, ln2_gain, ln2_bias, up_bias, down_bias)
    filled = [jnp.concatenate([v, jnp.zeros((LANES - v.shape[0],), BF)]) for v in vectors]
    small = jnp.concatenate([padded(spec_w1), padded(spec_w2), jnp.concatenate(filled).reshape(-1, LANES)])
    if fast:
        own_up = w_up.reshape(share, parts, feature).transpose(1, 0, 2)
        unit = chip_unit(own_up, w_down, core, devices)
        bits = tuple(range(3, count)) + (2, 1, 0)
        meet = lambda value, bit: swap(value, devices, (bit, bit))
        small = pair(small[None], meet(small[None], bits[0]))
        half = first(region_rows, region_cols, flat_tokens, tables, deps=(unit, small))
        near = pair(unit, step(unit, 0), deps=(half,))
        small = pair(small, meet(small, bits[1]), deps=(near,))
        for k in range(2, count):
            small = pair(small, meet(small, bits[k]))
        near = pair(near, step(near, 1), deps=(small,))
        weights, weight_bits, vector_bits, me_small = small, bits, bits, me_one
    else:
        up = lax.all_gather(w_up, AXES, axis=0, tiled=True)
        up = up.reshape(UNITS, feature // UNITS, parts, feature).transpose(0, 2, 1, 3).reshape(UNITS, -1, feature)
        down = lax.all_gather(w_down, AXES, axis=0, tiled=True).reshape(UNITS, -1, feature)
        pieces = tuple(
            jnp.where(core == 0, one, two)[begin : begin + UNITS // 2]
            for one, two in ((up, down), (down, up))
            for begin in (0, UNITS // 2)
        )
        me_one = core.reshape(1)
        me_small = jnp.zeros_like(me_one)
        places = (tuple(range(UNITS)),) * 2
        small = gather_small(small, me, devices, count)
        weights = small[:, : 4 * share].reshape(devices, 2, 2 * share, LANES).transpose(1, 0, 2, 3)
        weights = weights.reshape(2, 2 * UNITS, -1, LANES).transpose(1, 0, 2, 3).reshape(2 * UNITS, -1, LANES)
        weight_bits, vector_bits = tuple(range(5)), tuple(range(count))
        half = first(region_rows, region_cols, flat_tokens, tables)
    vectors = small[:, 4 * share :].transpose(1, 0, 2).astype(F32)

    steps = KEPT // GROUP
    made = mix_first(
        me_small, half, weights, vectors, tables, hidden, steps // 2, weight_bits, vector_bits,
        deps=(near,) if fast else (),
    )
    half1, modes1, heads, (mix1, mix2, wide, long, up_shift) = made[0], made[1:6], made[6:11], made[11:]
    if fast:
        near = pair(near, step(near, 2), deps=(half1,))
        far = step(near, 3)
    made = mix_second(
        half, mix1, mix2, wide, long, tables, steps // 2, steps // 2, deps=(near,) if fast else ()
    )
    half2, modes2 = made[0], made[1:6]
    middle, normed = space(region_rows, region_cols, half1, half2, flat_tokens, wide, tables)
    if fast:
        far = hold(far, (normed,))
        pieces = (near, far, swap(near, devices, (0, 0)), swap(far, devices, (0, 0)))
    active, pre, branch, bias_grad, up_all, down_all = feed_up(
        region_rows, region_cols, me_one, normed, flat_grad, up_shift, pieces, places
    )
    send, keep = weight_grads(me_one, active, pre, branch, normed, places)
    down_args = (active, pre, middle, flat_grad, flat_tokens, wide, tables["first"], up_all, down_all)
    tiles = cells // CELLS
    cut = 3
    made = feed_down(region_rows, region_cols, *down_args, 0, cut, deps=(send,))
    deps = ()
    if fast:
        ranks = [((me >> jnp.where(core == 0, *bit)) & 1).reshape(1) for bit in zip(*orders)]
        send, keep = fold(keep, swap(send, devices, (0, 0)), ranks[3], deps=(made[3],))
        deps = (send,)
    made = feed_down(region_rows, region_cols, *down_args, cut, tiles - cut, made, deps=deps)
    mixed, grad_middle, half_back, sums_two = made
    half_back, one, two, one_head, two_head, bias_sums = mix_back(
        half_back, modes1, modes2, heads, mix1, mix2, tables
    )
    if fast:
        send, keep = fold(keep, step(send, 3), ranks[2], deps=(bias_sums,))
        deps = (send,)
    grad_two = block_grads(modes1[1], modes2[1], heads[1], two, two_head, "grad_mix2", deps=deps)
    grad_one = block_grads(modes1[0], modes2[0], heads[0], one, one_head, "grad_mix1", deps=deps)
    last_args = (region_rows, region_cols, half_back, flat_tokens, grad_middle, wide, tables)
    if fast:
        uppers = [((me >> bit) & 1).reshape(1) for bit in range(count)]
        away, own = pack(uppers[0], grad_one, grad_two, bias_sums, sums_two, bias_grad, wide, devices)
        send, keep = fold(keep, step(send, 2), ranks[1], deps=(away,))
        grad_tokens = last(*last_args, 0, 2, deps=(send, away))
        send, keep = fold(keep, step(send, 1), ranks[0], deps=(grad_tokens,))
        away, own = fold_small(own, meet(away, 0), uppers[1], deps=(send,))
        grad_tokens = last(*last_args, 2, 2, (grad_tokens,), deps=(away,))
        keep = hold(keep, (grad_tokens,))
        total = keep[0].astype(F32) + step(send, 0)[0].astype(F32)
        up_sum = total.reshape(parts, 2 * share, feature)
        lower = up_sum[:, :share].reshape(parts * share, feature)
        upper = up_sum[:, share:].reshape(parts * share, feature)
        each = parts * share
        other = swap(jnp.where(core == 0, upper, total[:each]), devices, (0, 0))
        grad_w_up = jnp.where(core == 0, lower, other).reshape(parts, share, feature).transpose(1, 0, 2)
        grad_w_down = jnp.where(core == 0, other, total[each:])
        away, own = fold_small(own, meet(away, 1), uppers[2], deps=(grad_tokens,))
        grad_tokens = last(*last_args, 4, 2, (grad_tokens,), deps=(away,))
        away, own = fold_small(own, meet(away, 2), uppers[3], deps=(grad_tokens,))
        grad_tokens = last(*last_args, 6, 2, (grad_tokens,), deps=(away,))
        away, own = fold_small(own, meet(away, 3), uppers[4], deps=(grad_tokens,))
        result = end_small(own, meet(away, 4))
    else:
        scatter = lambda v: lax.psum_scatter(v.astype(F32), AXES, scatter_dimension=0, tiled=True)
        up = jnp.where(core == 0, keep, send).reshape(UNITS, parts, feature // UNITS, feature)
        grad_w_up = scatter(up.transpose(0, 2, 1, 3).reshape(feature, hidden))
        grad_w_down = scatter(jnp.where(core == 0, send, keep).reshape(hidden, feature))
        grad_tokens = last(*last_args, 0, tiles)
        owned = lambda v: jnp.pad(
            v.reshape(v.shape[0], devices, -1).transpose(1, 0, 2), ((0, 0), (0, 0), (0, LANES - v.shape[1] // devices))
        )
        narrow = jnp.concatenate(list(scale_grads(bias_sums, sums_two, wide)) + [sums_two[:3]])
        biases = bias_sums[:2].reshape(2, feature // LANES, 2, LANES).transpose(0, 2, 1, 3).reshape(2, 2 * feature)
        blocks = [v.reshape(devices, 2 * share, LANES) for v in (grad_one, grad_two)]
        packet = jnp.concatenate(blocks + [owned(narrow), owned(biases), owned(bias_grad)], axis=1)
        result = scatter_small(packet, me, devices, count, 8)
    row = lambda k, width: result[4 * share + k, :width]
    return (
        mixed.reshape(tokens.shape),
        grad_tokens.reshape(tokens.shape),
        row(0, share),
        row(1, share),
        result[: 2 * share, :block],
        row(5, 2 * share),
        result[2 * share : 4 * share, :block],
        row(6, 2 * share),
        row(2, share),
        row(3, share),
        grad_w_up.reshape(share, hidden),
        row(7, bias_grad.shape[1] // devices),
        grad_w_down,
        row(4, share),
    )


def solution(mesh):
    placed = P(AXES)
    return jax.shard_map(
        on_device, mesh=mesh, in_specs=(placed,) * 16, out_specs=(placed,) * 14, check_vma=False
    )
```

```python
import functools
import math

import jax
import jax.numpy as jnp
import numpy as np
from jax import lax
from jax.experimental import pallas as pl
from jax.experimental.pallas import tpu as pltpu
from jax.sharding import PartitionSpec as P

BF = jnp.bfloat16
F32 = jnp.float32
BLOCKS = 8
EPS = 1e-05
SHRINK = 0.01
ROWS = 32
COLS = 64
KEPT = COLS // 2
GROUP = 4
STEPS = ROWS // GROUP
CELLS = GROUP * COLS
MODES = (KEPT + 1) * ROWS
HEAD = (GROUP + 1) * ROWS
BODY = GROUP * ROWS
LANES = 128
C1 = math.sqrt(2.0 / math.pi)
C3 = 0.044715
UNITS = 16
VMEM_LIMIT = 60 * 1024 * 1024


def table_parts(values):
    high = values.astype(np.float32).astype(jnp.bfloat16)
    low = (values - high.astype(np.float64)).astype(np.float32).astype(jnp.bfloat16)
    return np.stack([high, low])


def wave_matrices():
    scale = 1.0 / math.sqrt(ROWS * COLS)
    w = np.arange(COLS)
    first = np.zeros((KEPT, 2, GROUP, GROUP, COLS))
    for k in range(KEPT):
        for h in range(GROUP):
            if k == 0:
                first[k, 0, h, h] = scale
                first[k, 1, h, h] = scale * np.where(w % 2 == 0, 1.0, -1.0)
            else:
                first[k, 0, h, h] = scale * np.cos(2 * np.pi * (k * w % COLS) / COLS)
                first[k, 1, h, h] = -scale * np.sin(2 * np.pi * (k * w % COLS) / COLS)
    first = first.reshape(CELLS, CELLS)
    p = np.arange(ROWS)
    turn = 2 * np.pi * (np.outer(p, p) % ROWS) / ROWS
    cos = np.cos(turn).reshape(ROWS, STEPS, GROUP)
    sin = np.sin(turn).reshape(ROWS, STEPS, GROUP)
    body = np.zeros((2, GROUP, ROWS, GROUP, STEPS, 2, GROUP))
    head = np.zeros((2, GROUP + 1, ROWS, GROUP, STEPS, 2, GROUP))
    for k in range(GROUP):
        body[0, k, :, k, :, 0] = cos
        body[0, k, :, k, :, 1] = sin
        body[1, k, :, k, :, 1] = cos
        body[1, k, :, k, :, 0] = -sin
    head[:, 1:GROUP, :, 1:] = body[:, 1:, :, 1:]
    for place, part in ((0, 0), (GROUP, 1)):
        head[0, place, :, 0, :, part] = cos
        head[1, place, :, 0, :, part] = -sin
    weight = np.full((2, GROUP + 1, ROWS, 1), 2.0)
    weight[:, 0] = 1.0
    weight[:, GROUP] = 1.0
    head = head.reshape(2 * HEAD, 2 * BODY)
    body = body.reshape(2 * BODY, 2 * BODY)
    head_weighted = head * weight.reshape(2 * HEAD, 1)
    body_weighted = body * 2.0
    return {
        "first": table_parts(first),
        "first_t": table_parts(first.T),
        "head": table_parts(head),
        "body": table_parts(body),
        "head_t": table_parts(head.T),
        "body_t": table_parts(body.T),
        "head_w": table_parts(head_weighted),
        "body_w": table_parts(body_weighted),
        "head_wt": table_parts(head_weighted.T),
        "body_wt": table_parts(body_weighted.T),
    }


def mm(left, right, dims=(1, 0)):
    return lax.dot_general(
        left, right, (((dims[0],), (dims[1],)), ((), ())), preferred_element_type=F32
    )


def split(values):
    high = values.astype(BF)
    return high, (values - high.astype(F32)).astype(BF)


def turn(table, values):
    high, low = split(values)
    return mm(table[0], high) + mm(table[1], high) + mm(table[0], low)


def normalize(values):
    centred = values - jnp.mean(values, axis=-1, keepdims=True)
    inverse = lax.rsqrt(jnp.mean(centred * centred, axis=-1, keepdims=True) + EPS)
    return centred * inverse, inverse


def norm_back(grad, gain, normal, inverse):
    scaled = grad * gain
    return inverse * (
        scaled
        - jnp.mean(scaled, axis=-1, keepdims=True)
        - normal * jnp.mean(scaled * normal, axis=-1, keepdims=True)
    )


def gelu_parts(value):
    square = value * value
    half = 0.5 + 0.5 * jnp.tanh(value * (C1 + (C1 * C3) * square))
    active = value * half
    slope = half + active * (1.0 - half) * (2.0 * C1 + (6.0 * C1 * C3) * square)
    return active, slope


def gelu(value):
    square = value * value
    return value * (0.5 + 0.5 * jnp.tanh(value * (C1 + (C1 * C3) * square)))


def live_rows(start, count, rows_ref, cols_ref):
    cell = start + lax.broadcasted_iota(jnp.int32, (count, 1), 0)
    inside = (cell // COLS < rows_ref[0]) & (cell % COLS < cols_ref[0])
    return jnp.where(inside, 1.0, 0.0).astype(F32)


def spread(piece, per_device, me, bits):
    devices = piece.shape[0]
    total = devices * per_device
    lane = lax.broadcasted_iota(jnp.int32, (LANES, total), 0)
    place = lax.broadcasted_iota(jnp.int32, (LANES, total), 1)
    pick = jnp.where(place % per_device == lane, 1.0, 0.0).astype(BF)
    wide = mm(piece.astype(BF), pick)
    row = lax.broadcasted_iota(jnp.int32, (devices, 1), 0)
    owner = jnp.full((devices, 1), me, jnp.int32)
    for k, bit in enumerate(bits):
        owner = owner ^ (((row >> k) & 1) << bit)
    where = lax.broadcasted_iota(jnp.int32, (devices, total), 1) // per_device
    return jnp.sum(jnp.where(owner == where, wide, 0.0), axis=0, keepdims=True)


def place_of(mask, bits):
    return sum(((mask >> bit) & 1) << k for k, bit in enumerate(bits))


def any_space():
    return pl.BlockSpec(memory_space=pl.ANY)


def single(shape):
    return pl.BlockSpec(shape, lambda *_: (0,) * len(shape), pipeline_mode=pl.Buffered(1))


def smem():
    return pl.BlockSpec(memory_space=pltpu.SMEM)


def params(**more):
    return pltpu.CompilerParams(vmem_limit_bytes=VMEM_LIMIT, **more)


def cost(flops, moved):
    return pl.CostEstimate(flops=0, bytes_accessed=0, transcendentals=0)


def launch(deps, kernel, *, in_specs, **more):
    count = len(in_specs)

    def body(*refs):
        kernel(*refs[:count], *refs[count + len(deps) :])

    call = pl.pallas_call(body, in_specs=list(in_specs) + [any_space() for _ in deps], **more)
    return lambda *operands: call(*operands, *deps)


def to_mixed(real, imag):
    tiles = []
    for at in range(0, real.shape[1], LANES):
        tiles += [real[:, at : at + LANES], imag[:, at : at + LANES]]
    return jnp.concatenate(tiles, axis=1)


def from_mixed(values):
    cut = lambda at: values[:, at : at + LANES]
    real = [cut(at) for at in range(0, values.shape[1], 2 * LANES)]
    imag = [cut(at + LANES) for at in range(0, values.shape[1], 2 * LANES)]
    return jnp.concatenate(real, axis=1), jnp.concatenate(imag, axis=1)


def mix_product(values, matrix_ref, back=False):
    feature = values.shape[1] // 2
    wide = 2 * LANES
    groups = []
    for group in range(2):
        part = values[:, group * feature : (group + 1) * feature]
        count = feature // wide
        for t in range(count):
            begin, end = max(t - 1, 0) * wide, min(t + 2, count) * wide
            here = slice(t * wide, (t + 1) * wide)
            if back:
                groups.append(mm(part[:, begin:end], matrix_ref[group, here, begin:end], (1, 1)))
            else:
                groups.append(mm(part[:, begin:end], matrix_ref[group, begin:end, here]))
    return jnp.concatenate(groups, axis=1)


def first_kernel(rows_ref, cols_ref, tokens_ref, first_ref, half_ref, normal_ref):
    feature = tokens_ref.shape[1]
    normal, _ = normalize(tokens_ref[...].astype(F32))
    live = live_rows(pl.program_id(0) * CELLS, CELLS, rows_ref, cols_ref)
    normal = normal * live
    normal_ref[...] = normal.astype(BF)
    half_ref[:, :, :feature] = turn(first_ref, normal).reshape(KEPT, 2 * GROUP, feature)
    ones = jnp.broadcast_to(live, (CELLS, LANES)).astype(BF)
    half_ref[:, :, feature:] = (mm(first_ref[0], ones) + mm(first_ref[1], ones)).reshape(KEPT, 2 * GROUP, LANES)


def first(rows, cols, tokens, tables, deps=()):
    cells, feature = tokens.shape
    table = tables["first"]
    return launch(
        deps,
        first_kernel,
        grid=(STEPS,),
        out_shape=(
            jax.ShapeDtypeStruct((KEPT, 2 * ROWS, feature + LANES), F32),
            jax.ShapeDtypeStruct((cells, feature), BF),
        ),
        in_specs=[smem(), smem(), pl.BlockSpec((CELLS, feature), lambda i: (i, 0)), single(table.shape)],
        out_specs=(
            pl.BlockSpec((KEPT, 2 * GROUP, feature + LANES), lambda i: (0, i, 0)),
            pl.BlockSpec((CELLS, feature), lambda i: (i, 0)),
        ),
        compiler_params=params(),
        cost_estimate=cost(6e9, 11e6),
        name="first",
    )(rows, cols, tokens, table)


def build_mix(me, bits, weights_ref, layer, out_ref, feature):
    block = feature // BLOCKS
    half = feature // 2
    per_group = BLOCKS // 2
    share = 2 * feature // weights_ref.shape[0]
    each = block // share
    out_ref[...] = jnp.zeros_like(out_ref)
    row = lax.broadcasted_iota(jnp.int32, (LANES, half), 0)
    column = lax.broadcasted_iota(jnp.int32, (LANES, half), 1)
    for b in range(per_group):
        shift = jnp.where((column - b * block == row) & (row < block), 1.0, 0.0).astype(BF)
        low, high = b * block, (b + 1) * block
        for group in range(2):
            for part in range(2):
                at = (part * BLOCKS + group * per_group + b) * each
                pieces = [
                    weights_ref[place_of((at + k) ^ me, bits), layer * share : (layer + 1) * share, :]
                    for k in range(each)
                ]
                placed = mm(jnp.concatenate(pieces, axis=0), shift).astype(BF)
                for t in range(low // LANES, (high - 1) // LANES + 1):
                    begin, end = max(low, t * LANES), min(high, (t + 1) * LANES)
                    for c in range(low // LANES, (high - 1) // LANES + 1):
                        piece = placed[begin - low : end - low, c * LANES : (c + 1) * LANES]
                        for up in range(2):
                            top = 2 * t * LANES + up * LANES + begin - t * LANES
                            left = (2 * c + (up ^ part)) * LANES
                            value = -piece if part == 1 and up == 1 else piece
                            here = (group, slice(top, top + end - begin), slice(left, left + LANES))
                            out_ref[here] = out_ref[here] + value


def mix_step(half_ref, head_ref, body_ref, back_head_ref, back_body_ref, mix1_ref, mix2_ref, wide_ref, long_ref,
             outs, heads, out_ref, is_head):
    feature = out_ref.shape[2]
    rows = HEAD if is_head else BODY
    spec = turn(head_ref if is_head else body_ref, half_ref[...].reshape(2 * BODY, feature + LANES))
    gain = wide_ref[0:1, :]
    shift = wide_ref[1:2, :]

    def scaled(part):
        flat = jnp.concatenate([part[:, feature:]] * (feature // LANES), axis=1)
        return (part[:, :feature] * gain + flat * shift).astype(BF)

    inside = to_mixed(scaled(spec[:rows]), scaled(spec[rows:]))
    active, slope = gelu_parts(mix_product(inside, mix1_ref) + long_ref[0:1, :])
    hidden = active.astype(BF)
    value = mix_product(hidden, mix2_ref) + long_ref[1:2, :]
    bend = jnp.tanh(value / SHRINK)
    flat = jnp.concatenate([spec[:rows, feature:], spec[rows:, feature:]], axis=1)
    for ref, head, kept in zip(outs, heads, (inside, hidden, slope, bend * bend, flat)):
        ref[...] = kept[:BODY]
        if is_head:
            head[...] = kept[BODY:]
    values = jnp.concatenate(from_mixed(value - SHRINK * bend), axis=0)
    out_ref[...] = turn(back_head_ref if is_head else back_body_ref, values).reshape(GROUP, 2 * ROWS, feature)


def mix_first_kernel(
    weight_bits, vector_bits, me_ref, half_ref, weights_ref, vector_ref, head_ref, body_ref, back_head_ref, back_body_ref,
    out_ref, low_ref, hidden_ref, slope_ref, bend_ref, flat_ref,
    low_head_ref, hidden_head_ref, slope_head_ref, bend_head_ref, flat_head_ref, mix1_ref, mix2_ref, wide_ref, long_ref, up_ref,
):
    feature = out_ref.shape[2]
    devices = vector_ref.shape[1]
    share = feature // devices
    step = pl.program_id(0)
    outs = (low_ref, hidden_ref, slope_ref, bend_ref, flat_ref)
    heads = (low_head_ref, hidden_head_ref, slope_head_ref, bend_head_ref, flat_head_ref)
    work = functools.partial(
        mix_step, half_ref, head_ref, body_ref, back_head_ref, back_body_ref, mix1_ref, mix2_ref, wide_ref, long_ref,
        outs, heads, out_ref,
    )

    @pl.when(step == 0)
    def _():
        me = me_ref[0]
        build_mix(me, weight_bits, weights_ref, 0, mix1_ref, feature)
        build_mix(me, weight_bits, weights_ref, 1, mix2_ref, feature)
        wide_ref[...] = jnp.zeros_like(wide_ref)
        long_ref[...] = jnp.zeros_like(long_ref)
        for row, at in enumerate((2, 3, 4, 5, 7)):
            wide_ref[row : row + 1, :] = spread(vector_ref[at], share, me, vector_bits)
        for row in range(2):
            both = spread(vector_ref[row], 2 * share, me, vector_bits)
            long_ref[row : row + 1, :] = to_mixed(both[:, :feature], both[:, feature:])
        up_ref[...] = spread(vector_ref[6], up_ref.shape[1] // devices, me, vector_bits)
        work(True)

    @pl.when(step > 0)
    def _():
        work(False)


def mix_second_kernel(
    half_ref, mix1_ref, mix2_ref, wide_ref, long_ref, body_ref, back_body_ref,
    out_ref, *outs,
):
    mix_step(
        half_ref, None, body_ref, None, back_body_ref, mix1_ref, mix2_ref, wide_ref, long_ref,
        outs, (None,) * 5, out_ref, False,
    )


def mode_shapes(rows, feature):
    wide = [jax.ShapeDtypeStruct((rows, 2 * feature), kind) for kind in (BF, BF, F32, F32)]
    return wide + [jax.ShapeDtypeStruct((rows, 2 * LANES), F32)]


def mode_blocks(feature):
    return [pl.BlockSpec((BODY, width), lambda i: (i, 0)) for width in (2 * feature,) * 4 + (2 * LANES,)]


def half_block(width, begin=0):
    return pl.BlockSpec((GROUP, 2 * ROWS, width), lambda i: (i + begin, 0, 0))


def mix_first(me, half, weights, vectors, tables, hidden, steps, weight_bits, vector_bits, deps=()):
    feature = half.shape[2] - LANES
    fixed = (weights, vectors, tables["head"], tables["body"], tables["head_wt"], tables["body_wt"])
    more = (
        jax.ShapeDtypeStruct((2, feature, feature), BF),
        jax.ShapeDtypeStruct((2, feature, feature), BF),
        jax.ShapeDtypeStruct((8, feature), F32),
        jax.ShapeDtypeStruct((8, 2 * feature), F32),
        jax.ShapeDtypeStruct((1, hidden), F32),
    )
    heads = mode_shapes(ROWS, feature)
    return launch(
        deps,
        functools.partial(mix_first_kernel, weight_bits, vector_bits),
        grid=(steps,),
        out_shape=[jax.ShapeDtypeStruct((GROUP * steps, 2 * ROWS, feature), F32)]
        + mode_shapes(BODY * steps, feature) + heads + list(more),
        in_specs=[smem(), half_block(feature + LANES)] + [single(v.shape) for v in fixed],
        out_specs=[half_block(feature)] + mode_blocks(feature) + [single(v.shape) for v in heads]
        + [single(v.shape) for v in more],
        compiler_params=params(),
        cost_estimate=cost(9e9, 20e6),
        name="mix_first",
    )(me, half, *fixed)


def mix_second(half, mix1, mix2, wide, long, tables, begin, steps, deps=()):
    feature = half.shape[2] - LANES
    fixed = (mix1, mix2, wide, long, tables["body"], tables["body_wt"])
    return launch(
        deps,
        mix_second_kernel,
        grid=(steps,),
        out_shape=[jax.ShapeDtypeStruct((GROUP * steps, 2 * ROWS, feature), F32)] + mode_shapes(BODY * steps, feature),
        in_specs=[half_block(feature + LANES, begin)] + [single(v.shape) for v in fixed],
        out_specs=[half_block(feature)] + mode_blocks(feature),
        compiler_params=params(),
        cost_estimate=cost(9e9, 20e6),
        name="mix_second",
    )(half, *fixed)


def space_kernel(rows_ref, cols_ref, half1_ref, half2_ref, tokens_ref, first_t_ref, wide_ref, middle_ref, normed_ref):
    feature = tokens_ref.shape[1]
    flat = lambda ref: ref[...].reshape(-1, feature)
    spatial = turn(first_t_ref, jnp.concatenate([flat(half1_ref), flat(half2_ref)], axis=0))
    inputs = tokens_ref[...].astype(F32)
    live = live_rows(pl.program_id(0) * CELLS, CELLS, rows_ref, cols_ref)
    normal, _ = normalize(inputs)
    middle = inputs + live * (spatial + (normal * wide_ref[0:1, :] + wide_ref[1:2, :]))
    middle_ref[...] = middle
    normal, _ = normalize(middle)
    normed_ref[...] = (normal * wide_ref[2:3, :] + wide_ref[3:4, :]).astype(BF)


def column_block(rows, width):
    return pl.BlockSpec((rows, 2 * GROUP, width), lambda i: (0, i, 0))


def space(rows, cols, half1, half2, tokens, wide, tables, deps=()):
    cells, feature = tokens.shape
    table = tables["first_t"]
    block = pl.BlockSpec((CELLS, feature), lambda i: (i, 0))
    return launch(
        deps,
        space_kernel,
        grid=(STEPS,),
        out_shape=(jax.ShapeDtypeStruct((cells, feature), F32), jax.ShapeDtypeStruct((cells, feature), BF)),
        in_specs=[smem(), smem(), column_block(half1.shape[0], feature), column_block(half2.shape[0], feature),
                  block, single(table.shape), single(wide.shape)],
        out_specs=(block, block),
        compiler_params=params(),
        cost_estimate=cost(6e9, 20e6),
        name="space",
    )(rows, cols, half1, half2, tokens, table, wide)


def fetch_weights(me_ref, pieces, places, up_ref, down_ref, sems):
    count = pieces[0].shape[0] * 2
    chip = me_ref[0] // 2

    def copies(own, core):
        target = (up_ref, down_ref)[core]
        source = pieces[:2] if own else pieces[2:]
        for mask in range(count):
            at = places[core][mask]
            part = source[at // (count // 2)].at[at % (count // 2)]
            yield pltpu.make_async_copy(part, target.at[chip ^ mask], sems.at[core, mask])

    for core in range(2):
        @pl.when(me_ref[0] % 2 == core)
        def _():
            for copy in copies(True, core):
                copy.start()
            for copy in copies(False, 1 - core):
                copy.start()

    def arrived(core):
        for copy in copies(True, core):
            copy.wait()

    return arrived


def weight_scratch(pieces):
    chips, rows, feature = pieces[0].shape[0] * 2, pieces[0].shape[1], pieces[0].shape[2]
    return [
        pltpu.VMEM((chips, rows, feature), BF),
        pltpu.VMEM((chips, rows, feature), BF),
        pltpu.SemaphoreType.DMA((2, chips)),
    ]


def up_part(up_ref, j, feature):
    share = up_ref.shape[1] * feature // (up_ref.shape[0] * up_ref.shape[1])
    return up_ref[:, j * share : (j + 1) * share, :].reshape(feature, feature)


def down_part(down_ref, j, feature):
    share = down_ref.shape[1]
    each = feature // share
    return down_ref[j * each : (j + 1) * each].reshape(feature, feature)


def up_kernel(places, rows_ref, cols_ref, me_ref, normed_ref, grad_ref, bias_ref, *rest):
    pieces = rest[:4]
    active_ref, pre_ref, live_ref, bias_grad_ref, up_all_ref, down_all_ref, up_ref, down_ref, sems, out_sems = rest[4:]
    tile, feature = normed_ref.shape
    step = pl.program_id(0)
    copies = [
        pltpu.make_async_copy(source, target, out_sems.at[k])
        for k, (source, target) in enumerate(((up_ref, up_all_ref), (down_ref, down_all_ref)))
    ]

    def work(arrived):
        live = live_rows(step * tile, tile, rows_ref, cols_ref)
        branch = (grad_ref[...].astype(F32) * live).astype(BF)
        live_ref[...] = branch
        normed = normed_ref[...]
        if arrived:
            arrived(0)
            copies[0].start()
        for j in range(active_ref.shape[1] // feature):
            place = slice(j * feature, (j + 1) * feature)
            value = mm(normed, up_part(up_ref, j, feature)) + bias_ref[:, place]
            if arrived and j == 0:
                arrived(1)
                copies[1].start()
            grad = mm(branch, down_part(down_ref, j, feature), (1, 1))
            active, slope = gelu_parts(value)
            active_ref[:, place] = active.astype(BF)
            low = (grad * slope).astype(BF)
            pre_ref[:, place] = low
            bias_grad_ref[:, place] += jnp.sum(low.astype(F32), axis=0, keepdims=True)

    @pl.when(step == 0)
    def _():
        bias_grad_ref[...] = jnp.zeros_like(bias_grad_ref)
        work(fetch_weights(me_ref, pieces, places, up_ref, down_ref, sems))

    @pl.when(step > 0)
    def _():
        work(None)

    @pl.when(step == pl.num_programs(0) - 1)
    def _():
        for copy in copies:
            copy.wait()


def feed_up(rows, cols, me, normed, grad, bias, pieces, places, tile=256, deps=()):
    cells, feature = normed.shape
    hidden = bias.shape[1]
    block = lambda width: pl.BlockSpec((tile, width), lambda i: (i, 0))
    weights = jax.ShapeDtypeStruct((2 * pieces[0].shape[0],) + pieces[0].shape[1:], BF)
    return launch(
        deps,
        functools.partial(up_kernel, places),
        grid=(cells // tile,),
        out_shape=(
            jax.ShapeDtypeStruct((cells, hidden), BF),
            jax.ShapeDtypeStruct((cells, hidden), BF),
            jax.ShapeDtypeStruct((cells, feature), BF),
            jax.ShapeDtypeStruct((1, hidden), F32),
            weights,
            weights,
        ),
        in_specs=[smem(), smem(), smem(), block(feature), block(feature), single(bias.shape)]
        + [any_space() for _ in pieces],
        out_specs=(block(hidden), block(hidden), block(feature), single((1, hidden)), any_space(), any_space()),
        scratch_shapes=weight_scratch(pieces) + [pltpu.SemaphoreType.DMA((2,))],
        compiler_params=params(),
        cost_estimate=cost(0, 0),
        name="feed_up",
    )(rows, cols, me, normed, grad, bias, *pieces)


def weight_grad_kernel(places, me_ref, active_ref, pre_ref, branch_ref, normed_ref, send_ref, keep_ref, stage_ref, sems):
    step = pl.program_id(0)
    steps = pl.num_programs(0) // 2
    feature = branch_ref.shape[1]
    chips, rows, _ = send_ref.shape
    each = feature // rows
    share = feature // chips

    def down_copies(j, target):
        for c in range(each):
            source = stage_ref.at[j, pl.ds(c * rows, rows)]
            yield pltpu.make_async_copy(source, target.at[places[1][j * each + c]], sems.at[j, c])

    def up_copies(j, target):
        for c in range(chips):
            source = stage_ref.at[steps + j, pl.ds(c * share, share)]
            there = target.at[places[0][c], pl.ds(j * share, share)]
            yield pltpu.make_async_copy(source, there, sems.at[steps + j, c])

    @pl.when(step < steps)
    def _():
        stage_ref[step] = mm(active_ref[...], branch_ref[...], (0, 0)).astype(BF)

    @pl.when(step >= steps)
    def _():
        stage_ref[step] = mm(normed_ref[...], pre_ref[...], (0, 0)).astype(BF)

    total = stage_ref.shape[0] // 2
    for j in range(total):
        for core in range(2):
            targets = (send_ref, keep_ref) if core == 0 else (keep_ref, send_ref)

            @pl.when((step == j) & (me_ref[0] % 2 == core))
            def _():
                for copy in down_copies(j, targets[0]):
                    copy.start()

            @pl.when((step == total + j) & (me_ref[0] % 2 == core))
            def _():
                for copy in up_copies(j, targets[1]):
                    copy.start()

    @pl.when(step == 2 * steps - 1)
    def _():
        for j in range(total):
            for copy in down_copies(j, send_ref):
                copy.wait()
            for copy in up_copies(j, send_ref):
                copy.wait()


def weight_grads(me, active, pre, branch, normed, places, deps=()):
    cells, hidden = active.shape
    feature = branch.shape[1]
    tiles = hidden // feature
    chips = UNITS
    shape = jax.ShapeDtypeStruct((chips, hidden // chips, feature), BF)
    return launch(
        deps,
        functools.partial(weight_grad_kernel, places),
        grid=(2 * tiles,),
        out_shape=(shape, shape),
        in_specs=[
            smem(),
            pl.BlockSpec((cells, feature), lambda i: (0, jnp.minimum(i, tiles - 1))),
            pl.BlockSpec((cells, feature), lambda i: (0, jnp.maximum(i - tiles, 0))),
            single(branch.shape), single(normed.shape),
        ],
        out_specs=(any_space(), any_space()),
        scratch_shapes=[
            pltpu.VMEM((2 * tiles, feature, feature), BF),
            pltpu.SemaphoreType.DMA((2 * tiles, chips)),
        ],
        compiler_params=params(),
        cost_estimate=cost(4 * cells * feature * hidden, 40e6),
        name="weight_grads",
    )(me, active, pre, branch, normed)


def down_kernel(rows_ref, cols_ref, active_ref, pre_ref, middle_ref, grad_ref, normal_ref, wide_ref, first_ref,
                up_ref, down_ref, mixed_ref, grad_middle_ref, half_ref, sums_ref):
    tile, feature = middle_ref.shape
    hidden = active_ref.shape[1]
    step = pl.program_id(0)

    @pl.when(step == 0)
    def _():
        sums_ref[...] = jnp.zeros_like(sums_ref)

    live = live_rows(step * tile, tile, rows_ref, cols_ref)
    branch = mm(active_ref[...], down_ref[...].reshape(hidden, feature))
    grad_normed = jnp.zeros((tile, feature), F32)
    for j in range(hidden // feature):
        pre = pre_ref[:, j * feature : (j + 1) * feature]
        grad_normed = grad_normed + mm(pre, up_part(up_ref, j, feature), (1, 1))
    middle = middle_ref[...]
    mixed_ref[...] = (middle + live * (branch + wide_ref[4:5, :])).astype(BF)
    normal, inverse = normalize(middle)
    cotangent = grad_ref[...].astype(F32)
    grad_middle = cotangent + norm_back(grad_normed, wide_ref[2:3, :], normal, inverse)
    grad_middle_ref[...] = grad_middle
    masked = grad_middle * live
    half_ref[...] = turn(first_ref, masked).reshape(half_ref.shape)
    rows = (grad_normed * normal, grad_normed, cotangent * live, masked * normal_ref[...].astype(F32), masked)
    for row, value in enumerate(rows):
        sums_ref[row : row + 1, :] += jnp.sum(value, axis=0, keepdims=True)


def feed_down(rows, cols, active, pre, middle, grad, normal, wide, table, up, down, deps=()):
    cells, feature = middle.shape
    hidden = active.shape[1]
    block = lambda width: pl.BlockSpec((CELLS, width), lambda i: (i, 0))
    operands = (rows, cols, active, pre, middle, grad, normal, wide, table, up, down)
    return launch(
        deps,
        down_kernel,
        grid=(cells // CELLS,),
        out_shape=(
            jax.ShapeDtypeStruct((cells, feature), BF),
            jax.ShapeDtypeStruct((cells, feature), F32),
            jax.ShapeDtypeStruct((KEPT, 2 * ROWS, feature), F32),
            jax.ShapeDtypeStruct((8, feature), F32),
        ),
        in_specs=[smem(), smem(), block(hidden), block(hidden), block(feature), block(feature), block(feature)]
        + [single(v.shape) for v in operands[7:]],
        out_specs=(block(feature), block(feature), column_block(KEPT, feature), single((8, feature))),
        compiler_params=params(),
        cost_estimate=cost(0, 0),
        name="feed_down",
    )(*operands)


def back_step(half_ref, head_ref, body_ref, back_head_ref, back_body_ref, mix1_ref, mix2_ref, ins, in_heads,
              outs, out_heads, out_ref, sums_ref, is_head):
    feature = out_ref.shape[2]
    rows = HEAD if is_head else BODY

    def read(k):
        if is_head:
            return jnp.concatenate([ins[k][...], in_heads[k][...]], axis=0)
        return ins[k][...]

    grad = turn(head_ref if is_head else body_ref, half_ref[...].reshape(2 * BODY, feature))
    grad_two = (to_mixed(grad[:rows], grad[rows:]) * read(1)).astype(BF)
    grad_one = (mix_product(grad_two, mix2_ref, True) * read(0)).astype(BF)
    grad_spec = mix_product(grad_one, mix1_ref, True)
    values = jnp.concatenate(from_mixed(grad_spec), axis=0)
    out_ref[...] = turn(back_head_ref if is_head else back_body_ref, values).reshape(GROUP, 2 * ROWS, feature)
    for row, value in enumerate((grad_one, grad_two)):
        outs[row][...] = value[:BODY]
        if is_head:
            out_heads[row][...] = value[BODY:]
    flat = jnp.concatenate([read(3)] * (feature // LANES), axis=1)
    for row, value in enumerate((grad_one.astype(F32), grad_two.astype(F32), grad_spec * read(2).astype(F32), grad_spec * flat)):
        total = jnp.sum(value, axis=0, keepdims=True)
        sums_ref[row : row + 1, :] = total if is_head else sums_ref[row : row + 1, :] + total


def mix_back_kernel(
    half_ref, slope1_ref, slope2_ref, bend1_ref, bend2_ref, low1_ref, low2_ref, flat1_ref, flat2_ref,
    slope_head_ref, bend_head_ref, low_head_ref, flat_head_ref, mix1_ref, mix2_ref,
    head_ref, body_ref, back_head_ref, back_body_ref,
    out_ref, one_ref, two_ref, one_head_ref, two_head_ref, sums_ref,
):
    step = pl.program_id(0)
    steps = pl.num_programs(0) // 2
    work = functools.partial(
        back_step, half_ref, head_ref, body_ref, back_head_ref, back_body_ref, mix1_ref, mix2_ref
    )
    heads = (slope_head_ref, bend_head_ref, low_head_ref, flat_head_ref)
    more = (heads, (one_ref, two_ref), (one_head_ref, two_head_ref), out_ref, sums_ref)
    near = (slope1_ref, bend1_ref, low1_ref, flat1_ref)
    far = (slope2_ref, bend2_ref, low2_ref, flat2_ref)

    @pl.when(step == 0)
    def _():
        sums_ref[...] = jnp.zeros_like(sums_ref)
        work(near, *more, True)

    @pl.when((step > 0) & (step < steps))
    def _():
        work(near, *more, False)

    @pl.when(step >= steps)
    def _():
        work(far, *more, False)


def mix_back(half, modes1, modes2, heads, mix1, mix2, tables, deps=()):
    feature = half.shape[2]
    steps = KEPT // GROUP
    fixed = tuple(heads[k] for k in (2, 3, 0, 4)) + (
        mix1, mix2, tables["head_w"], tables["body_w"], tables["head_t"], tables["body_t"]
    )
    moving = []
    specs = []
    for k in (2, 3, 0, 4):
        width = modes1[k].shape[1]
        moving += [modes1[k], modes2[k]]
        specs += [
            pl.BlockSpec((BODY, width), lambda i: (jnp.minimum(i, steps // 2 - 1), 0)),
            pl.BlockSpec((BODY, width), lambda i: (jnp.maximum(i - steps // 2, 0), 0)),
        ]
    low = lambda rows: jax.ShapeDtypeStruct((rows, 2 * feature), BF)
    body = pl.BlockSpec((BODY, 2 * feature), lambda i: (i, 0))
    shapes = (
        jax.ShapeDtypeStruct((KEPT, 2 * ROWS, feature), F32), low(BODY * steps), low(BODY * steps),
        low(ROWS), low(ROWS), jax.ShapeDtypeStruct((8, 2 * feature), F32),
    )
    return launch(
        deps,
        mix_back_kernel,
        grid=(steps,),
        out_shape=shapes,
        in_specs=[half_block(feature)] + specs + [single(v.shape) for v in fixed],
        out_specs=[half_block(feature), body, body] + [single(v.shape) for v in shapes[3:]],
        compiler_params=params(),
        cost_estimate=cost(18e9, 30e6),
        name="mix_back",
    )(half, *moving, *fixed)


def block_kernel(left1_ref, left2_ref, left_head_ref, right_ref, right_head_ref, out_ref, natural_ref):
    wide = 2 * LANES
    count = left1_ref.shape[1] // wide
    cut = left1_ref.shape[0]
    for t in range(count):
        for c in range(max(t - 1, 0), min(t + 2, count)):
            left, right = slice(t * wide, (t + 1) * wide), slice(c * wide, (c + 1) * wide)
            total = (
                mm(left1_ref[:, left], right_ref[:cut, right], (0, 0))
                + mm(left2_ref[:, left], right_ref[cut:, right], (0, 0))
                + mm(left_head_ref[:, left], right_head_ref[:, right], (0, 0))
            )
            rows, lanes = slice(t * LANES, (t + 1) * LANES), slice(c * LANES, (c + 1) * LANES)
            natural_ref[0, rows, lanes] = total[:LANES, :LANES] + total[LANES:, LANES:]
            natural_ref[1, rows, lanes] = total[:LANES, LANES:] - total[LANES:, :LANES]
    per_group = BLOCKS // 2
    block = count * LANES // per_group
    for b in range(per_group):
        begin = b * block
        base = begin // LANES * LANES
        reach = min(base + wide, count * LANES) - base
        for part in range(2):
            piece = natural_ref[part, begin : begin + block, base : base + reach]
            if begin > base:
                piece = pltpu.roll(piece, reach - (begin - base), axis=1)
            out_ref[part, b * block : (b + 1) * block, :] = piece[:, :LANES]


def block_grads(left1, left2, left_head, right, right_head, name, deps=()):
    feature = left1.shape[1] // 2
    half = feature // 2
    block = lambda v: pl.BlockSpec((v.shape[0], feature), lambda i: (0, i))
    return launch(
        deps,
        block_kernel,
        grid=(2,),
        out_shape=jax.ShapeDtypeStruct((2, feature, LANES), F32),
        in_specs=[block(v) for v in (left1, left2, left_head, right, right_head)],
        out_specs=pl.BlockSpec((2, half, LANES), lambda i: (0, i, 0)),
        scratch_shapes=[pltpu.VMEM((2, half, half), F32)],
        compiler_params=params(),
        cost_estimate=cost(5e9, 7e6),
        name=name,
    )(left1, left2, left_head, right, right_head)


def last_kernel(begin, rows_ref, cols_ref, half_ref, tokens_ref, grad_ref, first_t_ref, wide_ref, *rest):
    out_ref = rest[-1]
    tile, feature = tokens_ref.shape
    live = live_rows((pl.program_id(0) + begin) * tile, tile, rows_ref, cols_ref)
    grad_middle = grad_ref[...]
    grad_normed = live * (grad_middle + turn(first_t_ref, half_ref[...].reshape(CELLS, feature)))
    normal, inverse = normalize(tokens_ref[...].astype(F32))
    out_ref[...] = grad_middle + norm_back(grad_normed, wide_ref[0:1, :], normal, inverse)


def last(rows, cols, half, tokens, grad, wide, tables, begin, steps, before=(), deps=()):
    cells, feature = tokens.shape
    first_t = tables["first_t"]
    block = pl.BlockSpec((CELLS, feature), lambda i: (i + begin, 0))
    operands = (rows, cols, half, tokens, grad, first_t, wide)
    return launch(
        deps,
        functools.partial(last_kernel, begin),
        grid=(steps,),
        out_shape=jax.ShapeDtypeStruct((cells, feature), F32),
        in_specs=[smem(), smem(), pl.BlockSpec((KEPT, 2 * GROUP, feature), lambda i: (0, i + begin, 0)), block, block,
                  single(first_t.shape), single(wide.shape)] + [any_space() for _ in before],
        out_specs=block,
        input_output_aliases={len(operands): 0} if before else {},
        compiler_params=params(),
        cost_estimate=cost(6e9, 20e6),
        name="last",
    )(*operands, *before)


def collect(value, per_device, devices):
    total = value.shape[1]
    owner = lax.broadcasted_iota(jnp.int32, (devices, total), 1) // per_device
    row = lax.broadcasted_iota(jnp.int32, (devices, total), 0)
    high, low = split(jnp.where(owner == row, jnp.broadcast_to(value, (devices, total)), 0.0))
    place = lax.broadcasted_iota(jnp.int32, (total, LANES), 0)
    lane = lax.broadcasted_iota(jnp.int32, (total, LANES), 1)
    pick = jnp.where(place % per_device == lane, 1.0, 0.0).astype(BF)
    return mm(high, pick) + mm(low, pick)


def emit(upper_ref, sum_ref, send_ref, keep_ref):
    rows = sum_ref.shape[2] - 8
    half = sum_ref.shape[0]
    away = sum_ref[:, pl.ds(1 - upper_ref[0], 1)].reshape(half, rows + 8, LANES)
    high, low = split(away[:, rows:])
    send_ref[:, :rows] = away[:, :rows].astype(BF)
    send_ref[:, rows:] = jnp.concatenate([high.astype(F32), low.astype(F32)], axis=1).astype(BF)
    keep_ref[...] = sum_ref[:, pl.ds(upper_ref[0], 1)].reshape(half, rows + 8, LANES)


def pack_kernel(upper_ref, one_ref, two_ref, mixed_ref, sums_ref, up_ref, wide_ref, send_ref, keep_ref, sum_ref):
    half, _, rows, _ = sum_ref.shape
    devices = 2 * half
    share = (rows - 8) // 4
    feature = sums_ref.shape[1]
    sum_ref[:, :, : 2 * share] = one_ref[...].reshape(half, 2, 2 * share, LANES)
    sum_ref[:, :, 2 * share : 4 * share] = two_ref[...].reshape(half, 2, 2 * share, LANES)
    first_gain, first_bias = scale_grads(mixed_ref, sums_ref, wide_ref)
    natural = [jnp.concatenate(from_mixed(mixed_ref[k : k + 1, :]), axis=1) for k in range(2)]
    narrow = [first_gain, first_bias] + [sums_ref[k : k + 1, :] for k in range(3)]
    for k, value in enumerate(narrow + natural + [up_ref[...]]):
        placed = collect(value, value.shape[1] // devices, devices)
        for d in range(devices):
            sum_ref[d // 2, d % 2, 4 * share + k : 4 * share + k + 1, :] = placed[d : d + 1, :]
    emit(upper_ref, sum_ref, send_ref, keep_ref)


def scale_grads(mixed_ref, sums_ref, wide_ref):
    real, imag = from_mixed(mixed_ref[2:3, :])
    scaled = real + imag
    real, imag = from_mixed(mixed_ref[3:4, :])
    flat = real + imag
    gain = sums_ref[3:4, :] + (scaled - wide_ref[1:2, :] * flat) / wide_ref[0:1, :]
    return gain, sums_ref[4:5, :] + flat


def small_shapes(half, rows):
    return (
        jax.ShapeDtypeStruct((half, rows + 8, LANES), BF),
        jax.ShapeDtypeStruct((half, rows, LANES), F32),
    )


def pack(upper, one, two, mixed, sums, up, wide, devices):
    rows = 2 * one.shape[0] * one.shape[1] // devices + 8
    shapes = small_shapes(devices // 2, rows)
    operands = (one, two, mixed, sums, up, wide)
    return pl.pallas_call(
        pack_kernel,
        out_shape=shapes,
        in_specs=[smem()] + vmem(len(operands)),
        out_specs=vmem(2),
        scratch_shapes=[pltpu.VMEM((devices // 2, 2, rows, LANES), F32)],
        compiler_params=params(),
        cost_estimate=cost(0, 0),
        name="pack",
    )(upper, *operands)


def merge_small(keep_ref, got_ref):
    rows = keep_ref.shape[1] - 8
    tail = got_ref[:, rows:].astype(F32)
    return (
        keep_ref[:, :rows] + got_ref[:, :rows].astype(F32),
        keep_ref[:, rows:] + tail[:, :8] + tail[:, 8:],
    )


def fold_small_kernel(upper_ref, keep_ref, got_ref, send_ref, out_ref, sum_ref):
    half, _, rows, _ = sum_ref.shape
    top, tail = merge_small(keep_ref, got_ref)
    sum_ref[:, :, : rows - 8] = top.reshape(half, 2, rows - 8, LANES)
    sum_ref[:, :, rows - 8 :] = tail.reshape(half, 2, 8, LANES)
    emit(upper_ref, sum_ref, send_ref, out_ref)


def fold_small(keep, got, upper, deps=()):
    half, rows = keep.shape[0] // 2, keep.shape[1]
    return launch(
        deps,
        fold_small_kernel,
        out_shape=small_shapes(half, rows),
        in_specs=[smem()] + vmem(2),
        out_specs=vmem(2),
        scratch_shapes=[pltpu.VMEM((half, 2, rows, LANES), F32)],
        compiler_params=params(),
        cost_estimate=cost(0, 0),
        name="fold_small",
    )(upper, keep, got)


def vmem(count):
    return [pl.BlockSpec(memory_space=pltpu.VMEM)] * count


def end_small_kernel(keep_ref, got_ref, one_ref, two_ref, *rows_refs):
    top, tail = merge_small(keep_ref, got_ref)
    share, block = one_ref.shape
    one_ref[...] = top[0, :share, :block]
    two_ref[...] = top[0, share:, :block]
    for row, ref in enumerate(rows_refs):
        ref[...] = tail[0, row : row + 1, : ref.shape[1]]


def end_small(keep, got, share, block, widths):
    shapes = [jax.ShapeDtypeStruct((share, block), F32)] * 2
    shapes += [jax.ShapeDtypeStruct((1, width), F32) for width in widths]
    return pl.pallas_call(
        end_small_kernel,
        out_shape=shapes,
        in_specs=vmem(2),
        out_specs=vmem(len(shapes)),
        compiler_params=params(),
        cost_estimate=cost(0, 0),
        name="end_small",
    )(keep, got)


def begin_small_kernel(one_ref, two_ref, *rest):
    out_ref, rows_ref = rest[-2:]
    share, block = one_ref.shape
    out_ref[...] = jnp.zeros_like(out_ref)
    rows_ref[...] = jnp.zeros_like(rows_ref)
    out_ref[0, :share, :block] = one_ref[...]
    out_ref[0, share : 2 * share, :block] = two_ref[...]
    for row, ref in enumerate(rest[:-2]):
        rows_ref[row : row + 1, : ref.shape[1]] = ref[...].astype(F32)
    out_ref[0, 2 * share :, :] = rows_ref[...].astype(BF)


def begin_small(one, two, vectors):
    share = one.shape[0]
    operands = (one, two) + tuple(v[None] for v in vectors)
    return pl.pallas_call(
        begin_small_kernel,
        out_shape=jax.ShapeDtypeStruct((1, 2 * share + 16, LANES), BF),
        in_specs=vmem(len(operands)),
        out_specs=vmem(1)[0],
        scratch_shapes=[pltpu.VMEM((16, LANES), F32)],
        compiler_params=params(),
        cost_estimate=cost(0, 0),
        name="begin_small",
    )(*operands)


AXES = ("dp", "fsdp")


def swap(value, devices, bits):
    return lax.ppermute(value, AXES, [(i, i ^ (1 << bits[i & 1])) for i in range(devices)])


def doubling_orders(count):
    first = list(range(count - 1, 0, -1))
    second = list(first)
    for k in range(0, len(second) - 1, 2):
        second[k], second[k + 1] = second[k + 1], second[k]
    return first, second


def places_of(order):
    return [
        sum(1 << k for k, bit in enumerate(order) if mask >> (bit - 1) & 1) for mask in range(1 << len(order))
    ]


def pair_kernel(held_ref, got_ref, out_ref):
    count = held_ref.shape[0]
    out_ref[:count] = held_ref[...]
    out_ref[count:] = got_ref[...]


def pair(held, got, deps=()):
    shape = jax.ShapeDtypeStruct((2 * held.shape[0],) + held.shape[1:], held.dtype)
    return launch(
        deps,
        pair_kernel,
        out_shape=shape,
        in_specs=[pl.BlockSpec(memory_space=pltpu.VMEM)] * 2,
        out_specs=pl.BlockSpec(memory_space=pltpu.VMEM),
        compiler_params=params(),
        cost_estimate=cost(0, 4 * held.size * 2),
        name="pair",
    )(held, got)


def hold(value, deps):
    def body(*refs):
        pass

    return pl.pallas_call(
        body,
        out_shape=jax.ShapeDtypeStruct(value.shape, value.dtype),
        in_specs=[any_space() for _ in range(1 + len(deps))],
        out_specs=any_space(),
        input_output_aliases={0: 0},
        compiler_params=params(),
        cost_estimate=cost(0, 0),
        name="hold",
    )(value, *deps)


def gather_small(value, me, devices, count):
    held = value[None]
    for bit in list(range(3, count)) + [2, 1, 0]:
        other = swap(held, devices, (bit, bit))
        upper = (me >> bit) & 1
        axis = 0 if bit > 2 else 1
        join_two = lambda a, b: jnp.stack([a, b], axis=axis).reshape((-1,) + value.shape)
        held = jnp.where(upper == 0, join_two(held, other), join_two(other, held))
    return held


def scatter_small(value, me, devices, count, exact):
    shape = value.shape[1:]
    rows = shape[0]
    total = value
    for bit in [0, 1, 2] + list(range(count - 1, 2, -1)):
        upper = (me >> bit) & 1
        axis = 0 if bit > 2 else 1
        pair = total.reshape(((2, -1) if bit > 2 else (-1, 2)) + shape)
        away = lax.dynamic_index_in_dim(pair, 1 - upper, axis, keepdims=False)
        keep = lax.dynamic_index_in_dim(pair, upper, axis, keepdims=False)
        sums = away[:, rows - exact :]
        top = lax.reduce_precision(sums, 8, 7)
        packet = jnp.concatenate([away[:, : rows - exact], top, sums - top], axis=1).astype(BF)
        got = swap(packet, devices, (bit, bit)).astype(F32)
        low = got[:, rows - exact : rows] + got[:, rows:]
        total = keep + jnp.concatenate([got[:, : rows - exact], low], axis=1)
    return total[0]


def chip_unit(up, down, core, devices):
    parts, share, feature = up.shape
    flat = up.reshape(parts * share, feature)
    other = swap(jnp.where(core == 0, down, flat), devices, (0, 0))
    up_unit = jnp.concatenate([up, other.reshape(up.shape)], axis=1).reshape(2 * parts * share, feature)
    return jnp.where(core == 0, up_unit, jnp.concatenate([other, down]))[None]


def fold_kernel(upper_ref, keep_away_ref, got_away_ref, keep_own_ref, got_own_ref, send_ref, keep_ref):
    send_ref[...] = (keep_away_ref[...].astype(F32) + got_away_ref[...].astype(F32)).astype(BF)
    keep_ref[...] = (keep_own_ref[...].astype(F32) + got_own_ref[...].astype(F32)).astype(BF)


def fold(keep, got, upper, deps=()):
    half = keep.shape[0] // 2
    each = min(2, half)
    unit = (each,) + keep.shape[1:]
    count = len(deps)
    away = pl.BlockSpec(unit, lambda i, up: ((1 - up[0]) * (half // each) + i, 0, 0))
    own = pl.BlockSpec(unit, lambda i, up: (up[0] * (half // each) + i, 0, 0))
    out = pl.BlockSpec(unit, lambda i, up: (i, 0, 0))
    shape = jax.ShapeDtypeStruct((half,) + keep.shape[1:], BF)

    def body(*refs):
        fold_kernel(*refs[:5], *refs[5 + count :])

    return pl.pallas_call(
        body,
        grid_spec=pltpu.PrefetchScalarGridSpec(
            num_scalar_prefetch=1,
            grid=(half // each,),
            in_specs=[away, away, own, own] + [any_space() for _ in deps],
            out_specs=[out, out],
        ),
        out_shape=(shape, shape),
        compiler_params=params(),
        cost_estimate=cost(0, 6 * half * keep[0].size),
        name="fold",
    )(upper, keep, got, keep, got, *deps)


def on_device(
    tokens, grad_out, region_rows, region_cols, ln1_gain, ln1_bias, spec_w1, spec_b1, spec_w2, spec_b2,
    ln2_gain, ln2_bias, w_up, up_bias, w_down, down_bias,
):
    devices = lax.axis_size(AXES[0]) * lax.axis_size(AXES[1])
    count = devices.bit_length() - 1
    me = lax.axis_index(AXES).astype(jnp.int32)
    core = me & 1
    me_one = me.reshape(1)
    feature = tokens.shape[-1]
    block = feature // BLOCKS
    share = ln1_gain.shape[0]
    cells = tokens.shape[1] * tokens.shape[2]
    hidden = w_up.shape[1]
    parts = hidden // feature
    tables = {name: jnp.asarray(value) for name, value in wave_matrices().items()}
    orders = doubling_orders(count)
    places = tuple(places_of(order) for order in orders)
    flat_tokens = tokens.reshape(cells, feature)
    flat_grad = grad_out.reshape(cells, feature)
    fast = devices // 2 == UNITS
    step = lambda value, k: swap(value, devices, (orders[0][k], orders[1][k]))

    padded = lambda v: jnp.pad(v, ((0, 0), (0, LANES - v.shape[1])))
    vectors = (spec_b1, spec_b2, ln1_gain, ln1_bias, ln2_gain, ln2_bias, up_bias, down_bias)
    if fast:
        own_up = w_up.reshape(share, parts, feature).transpose(1, 0, 2)
        unit = chip_unit(own_up, w_down, core, devices)
        bits = tuple(range(3, count)) + (2, 1, 0)
        meet = lambda value, bit: swap(value, devices, (bit, bit))
        small = begin_small(spec_w1, spec_w2, vectors)
        half, normal = first(region_rows, region_cols, flat_tokens, tables, deps=(unit, small))
        near = pair(unit, step(unit, 0), deps=(half,))
        small = pair(small, meet(small, bits[0]), deps=(near,))
        for k in range(1, count):
            small = pair(small, meet(small, bits[k]))
            if k == 2:
                near = pair(near, step(near, 1), deps=(small,))
        weights, weight_bits, vector_bits, me_small = small, bits, bits, me_one
        vectors = small[:, 4 * share : 4 * share + 8].transpose(1, 0, 2).astype(F32)
    else:
        up = lax.all_gather(w_up, AXES, axis=0, tiled=True)
        up = up.reshape(UNITS, feature // UNITS, parts, feature).transpose(0, 2, 1, 3).reshape(UNITS, -1, feature)
        down = lax.all_gather(w_down, AXES, axis=0, tiled=True).reshape(UNITS, -1, feature)
        pieces = tuple(
            jnp.where(core == 0, one, two)[begin : begin + UNITS // 2]
            for one, two in ((up, down), (down, up))
            for begin in (0, UNITS // 2)
        )
        me_one = core.reshape(1)
        me_small = jnp.zeros_like(me_one)
        places = (tuple(range(UNITS)),) * 2
        small = jnp.concatenate([padded(spec_w1), padded(spec_w2)] + [padded(v[None]) for v in vectors])
        small = gather_small(small, me, devices, count)
        weights = small[:, : 4 * share].reshape(devices, 2, 2 * share, LANES).transpose(1, 0, 2, 3)
        weights = weights.reshape(2, 2 * UNITS, -1, LANES).transpose(1, 0, 2, 3).reshape(2 * UNITS, -1, LANES)
        weight_bits, vector_bits = tuple(range(5)), tuple(range(count))
        half, normal = first(region_rows, region_cols, flat_tokens, tables)
        vectors = small[:, 4 * share :].transpose(1, 0, 2).astype(F32)

    steps = KEPT // GROUP
    made = mix_first(
        me_small, half, weights, vectors, tables, hidden, steps // 2, weight_bits, vector_bits,
        deps=(near,) if fast else (),
    )
    half1, modes1, heads, (mix1, mix2, wide, long, up_shift) = made[0], made[1:6], made[6:11], made[11:]
    if fast:
        near = pair(near, step(near, 2), deps=(half1,))
        far = step(near, 3)
    made = mix_second(
        half, mix1, mix2, wide, long, tables, steps // 2, steps // 2, deps=(near,) if fast else ()
    )
    half2, modes2 = made[0], made[1:6]
    middle, normed = space(region_rows, region_cols, half1, half2, flat_tokens, wide, tables)
    if fast:
        far = hold(far, (normed,))
        pieces = (near, far, swap(near, devices, (0, 0)), swap(far, devices, (0, 0)))
    active, pre, branch, bias_grad, up_all, down_all = feed_up(
        region_rows, region_cols, me_one, normed, flat_grad, up_shift, pieces, places
    )
    send, keep = weight_grads(me_one, active, pre, branch, normed, places)
    tiles = cells // CELLS
    mixed, grad_middle, half_back, sums_two = feed_down(
        region_rows, region_cols, active, pre, middle, flat_grad, normal, wide, tables["first"], up_all, down_all,
        deps=(send,),
    )
    deps = ()
    if fast:
        ranks = [((me >> jnp.where(core == 0, *bit)) & 1).reshape(1) for bit in zip(*orders)]
        send, keep = fold(keep, swap(send, devices, (0, 0)), ranks[3], deps=(sums_two,))
        deps = (send,)
    half_back, one, two, one_head, two_head, bias_sums = mix_back(
        half_back, modes1, modes2, heads, mix1, mix2, tables, deps=deps
    )
    if fast:
        send, keep = fold(keep, step(send, 3), ranks[2], deps=(bias_sums,))
        deps = (send,)
    grad_two = block_grads(modes1[1], modes2[1], heads[1], two, two_head, "grad_mix2", deps=deps)
    grad_one = block_grads(modes1[0], modes2[0], heads[0], one, one_head, "grad_mix1", deps=deps)
    last_args = (region_rows, region_cols, half_back, flat_tokens, grad_middle, wide, tables)
    if fast:
        uppers = [((me >> bit) & 1).reshape(1) for bit in range(count)]
        away, own = pack(uppers[0], grad_one, grad_two, bias_sums, sums_two, bias_grad, wide, devices)
        send, keep = fold(keep, step(send, 2), ranks[1], deps=(away,))
        grad_tokens = last(*last_args, 0, 2, deps=(send, away))
        send, keep = fold(keep, step(send, 1), ranks[0], deps=(grad_tokens,))
        away, own = fold_small(own, meet(away, 0), uppers[1], deps=(send,))
        grad_tokens = last(*last_args, 2, 2, (grad_tokens,), deps=(away,))
        away, own = fold_small(own, meet(away, 1), uppers[2], deps=(grad_tokens,))
        grad_tokens = last(*last_args, 4, 2, (grad_tokens,), deps=(away,))
        keep = hold(keep, (grad_tokens,))
        total = keep[0].astype(F32) + step(send, 0)[0].astype(F32)
        up_sum = total.reshape(parts, 2 * share, feature)
        lower = up_sum[:, :share].reshape(parts * share, feature)
        upper = up_sum[:, share:].reshape(parts * share, feature)
        each = parts * share
        other = swap(jnp.where(core == 0, upper, total[:each]), devices, (0, 0))
        grad_w_up = jnp.where(core == 0, lower, other).reshape(parts, share, feature).transpose(1, 0, 2)
        grad_w_down = jnp.where(core == 0, other, total[each:])
        away, own = fold_small(own, meet(away, 2), uppers[3], deps=(grad_tokens,))
        grad_tokens = last(*last_args, 6, 2, (grad_tokens,), deps=(away,))
        away, own = fold_small(own, meet(away, 3), uppers[4], deps=(grad_tokens,))
        widths = (share,) * 5 + (2 * share,) * 2 + (hidden // devices,)
        blocks = end_small(own, meet(away, 4), 2 * share, block, widths)
        rows = [v.reshape(-1) for v in blocks[2:]]
        blocks = blocks[:2]
    else:
        scatter = lambda v: lax.psum_scatter(v.astype(F32), AXES, scatter_dimension=0, tiled=True)
        up = jnp.where(core == 0, keep, send).reshape(UNITS, parts, feature // UNITS, feature)
        grad_w_up = scatter(up.transpose(0, 2, 1, 3).reshape(feature, hidden))
        grad_w_down = scatter(jnp.where(core == 0, send, keep).reshape(hidden, feature))
        grad_tokens = last(*last_args, 0, tiles)
        owned = lambda v: jnp.pad(
            v.reshape(v.shape[0], devices, -1).transpose(1, 0, 2), ((0, 0), (0, 0), (0, LANES - v.shape[1] // devices))
        )
        narrow = jnp.concatenate(list(scale_grads(bias_sums, sums_two, wide)) + [sums_two[:3]])
        biases = bias_sums[:2].reshape(2, feature // LANES, 2, LANES).transpose(0, 2, 1, 3).reshape(2, 2 * feature)
        blocks = [v.reshape(devices, 2 * share, LANES) for v in (grad_one, grad_two)]
        packet = jnp.concatenate(blocks + [owned(narrow), owned(biases), owned(bias_grad)], axis=1)
        result = scatter_small(packet, me, devices, count, 8)
        widths = (share,) * 5 + (2 * share,) * 2 + (hidden // devices,)
        rows = [result[4 * share + k, :width] for k, width in enumerate(widths)]
        blocks = [result[k * 2 * share : (k + 1) * 2 * share, :block] for k in range(2)]
    return (
        mixed.reshape(tokens.shape),
        grad_tokens.reshape(tokens.shape),
        rows[0],
        rows[1],
        blocks[0],
        rows[5],
        blocks[1],
        rows[6],
        rows[2],
        rows[3],
        grad_w_up.reshape(share, hidden),
        rows[7],
        grad_w_down,
        rows[4],
    )


def solution(mesh):
    placed = P(AXES)
    return jax.shard_map(
        on_device, mesh=mesh, in_specs=(placed,) * 16, out_specs=(placed,) * 14, check_vma=False
    )
```

```python
import functools
import math

import jax
import jax.numpy as jnp
import numpy as np
from jax import lax
from jax.experimental import pallas as pl
from jax.experimental.pallas import tpu as pltpu
from jax.sharding import PartitionSpec as P

BF = jnp.bfloat16
F32 = jnp.float32
BLOCKS = 8
EPS = 1e-05
SHRINK = 0.01
ROWS = 32
COLS = 64
KEPT = COLS // 2
GROUP = 4
STEPS = ROWS // GROUP
CELLS = GROUP * COLS
MODES = (KEPT + 1) * ROWS
HEAD = (GROUP + 1) * ROWS
BODY = GROUP * ROWS
LANES = 128
C1 = math.sqrt(2.0 / math.pi)
C3 = 0.044715
UNITS = 16
VMEM_LIMIT = 60 * 1024 * 1024


def table_parts(values):
    high = values.astype(np.float32).astype(jnp.bfloat16)
    low = (values - high.astype(np.float64)).astype(np.float32).astype(jnp.bfloat16)
    return np.stack([high, low])


def wave_matrices():
    scale = 1.0 / math.sqrt(ROWS * COLS)
    w = np.arange(COLS)
    first = np.zeros((KEPT, 2, GROUP, GROUP, COLS))
    for k in range(KEPT):
        for h in range(GROUP):
            if k == 0:
                first[k, 0, h, h] = scale
                first[k, 1, h, h] = scale * np.where(w % 2 == 0, 1.0, -1.0)
            else:
                first[k, 0, h, h] = scale * np.cos(2 * np.pi * (k * w % COLS) / COLS)
                first[k, 1, h, h] = -scale * np.sin(2 * np.pi * (k * w % COLS) / COLS)
    first = first.reshape(CELLS, CELLS)
    p = np.arange(ROWS)
    turn = 2 * np.pi * (np.outer(p, p) % ROWS) / ROWS
    cos = np.cos(turn).reshape(ROWS, STEPS, GROUP)
    sin = np.sin(turn).reshape(ROWS, STEPS, GROUP)
    body = np.zeros((2, GROUP, ROWS, GROUP, STEPS, 2, GROUP))
    head = np.zeros((2, GROUP + 1, ROWS, GROUP, STEPS, 2, GROUP))
    for k in range(GROUP):
        body[0, k, :, k, :, 0] = cos
        body[0, k, :, k, :, 1] = sin
        body[1, k, :, k, :, 1] = cos
        body[1, k, :, k, :, 0] = -sin
    head[:, 1:GROUP, :, 1:] = body[:, 1:, :, 1:]
    for place, part in ((0, 0), (GROUP, 1)):
        head[0, place, :, 0, :, part] = cos
        head[1, place, :, 0, :, part] = -sin
    weight = np.full((2, GROUP + 1, ROWS, 1), 2.0)
    weight[:, 0] = 1.0
    weight[:, GROUP] = 1.0
    head = head.reshape(2 * HEAD, 2 * BODY)
    body = body.reshape(2 * BODY, 2 * BODY)
    head_weighted = head * weight.reshape(2 * HEAD, 1)
    body_weighted = body * 2.0
    return {
        "first": table_parts(first),
        "first_t": table_parts(first.T),
        "head": table_parts(head),
        "body": table_parts(body),
        "head_t": table_parts(head.T),
        "body_t": table_parts(body.T),
        "head_w": table_parts(head_weighted),
        "body_w": table_parts(body_weighted),
        "head_wt": table_parts(head_weighted.T),
        "body_wt": table_parts(body_weighted.T),
    }


def mm(left, right, dims=(1, 0)):
    return lax.dot_general(
        left, right, (((dims[0],), (dims[1],)), ((), ())), preferred_element_type=F32
    )


def split(values):
    high = values.astype(BF)
    return high, (values - high.astype(F32)).astype(BF)


def turn(table, values):
    high, low = split(values)
    return mm(table[0], high) + mm(table[1], high) + mm(table[0], low)


def normalize(values):
    centred = values - jnp.mean(values, axis=-1, keepdims=True)
    inverse = lax.rsqrt(jnp.mean(centred * centred, axis=-1, keepdims=True) + EPS)
    return centred * inverse, inverse


def norm_back(grad, gain, normal, inverse):
    scaled = grad * gain
    return inverse * (
        scaled
        - jnp.mean(scaled, axis=-1, keepdims=True)
        - normal * jnp.mean(scaled * normal, axis=-1, keepdims=True)
    )


def gelu_parts(value):
    square = value * value
    half = 0.5 + 0.5 * jnp.tanh(value * (C1 + (C1 * C3) * square))
    active = value * half
    slope = half + active * (1.0 - half) * (2.0 * C1 + (6.0 * C1 * C3) * square)
    return active, slope


def gelu(value):
    square = value * value
    return value * (0.5 + 0.5 * jnp.tanh(value * (C1 + (C1 * C3) * square)))


def live_rows(start, count, rows_ref, cols_ref):
    cell = start + lax.broadcasted_iota(jnp.int32, (count, 1), 0)
    inside = (cell // COLS < rows_ref[0]) & (cell % COLS < cols_ref[0])
    return jnp.where(inside, 1.0, 0.0).astype(F32)


def spread(piece, per_device, me, bits):
    devices = piece.shape[0]
    total = devices * per_device
    lane = lax.broadcasted_iota(jnp.int32, (LANES, total), 0)
    place = lax.broadcasted_iota(jnp.int32, (LANES, total), 1)
    pick = jnp.where(place % per_device == lane, 1.0, 0.0).astype(BF)
    wide = mm(piece.astype(BF), pick)
    row = lax.broadcasted_iota(jnp.int32, (devices, 1), 0)
    owner = jnp.full((devices, 1), me, jnp.int32)
    for k, bit in enumerate(bits):
        owner = owner ^ (((row >> k) & 1) << bit)
    where = lax.broadcasted_iota(jnp.int32, (devices, total), 1) // per_device
    return jnp.sum(jnp.where(owner == where, wide, 0.0), axis=0, keepdims=True)


def place_of(mask, bits):
    return sum(((mask >> bit) & 1) << k for k, bit in enumerate(bits))


def any_space():
    return pl.BlockSpec(memory_space=pl.ANY)


def single(shape):
    return pl.BlockSpec(shape, lambda *_: (0,) * len(shape), pipeline_mode=pl.Buffered(1))


def smem():
    return pl.BlockSpec(memory_space=pltpu.SMEM)


def params(**more):
    return pltpu.CompilerParams(vmem_limit_bytes=VMEM_LIMIT, **more)


def cost(flops, moved):
    return pl.CostEstimate(flops=0, bytes_accessed=0, transcendentals=0)


def launch(deps, kernel, *, in_specs, **more):
    count = len(in_specs)

    def body(*refs):
        kernel(*refs[:count], *refs[count + len(deps) :])

    call = pl.pallas_call(body, in_specs=list(in_specs) + [any_space() for _ in deps], **more)
    return lambda *operands: call(*operands, *deps)


def to_mixed(real, imag):
    tiles = []
    for at in range(0, real.shape[1], LANES):
        tiles += [real[:, at : at + LANES], imag[:, at : at + LANES]]
    return jnp.concatenate(tiles, axis=1)


def from_mixed(values):
    cut = lambda at: values[:, at : at + LANES]
    real = [cut(at) for at in range(0, values.shape[1], 2 * LANES)]
    imag = [cut(at + LANES) for at in range(0, values.shape[1], 2 * LANES)]
    return jnp.concatenate(real, axis=1), jnp.concatenate(imag, axis=1)


def mix_product(values, matrix_ref, back=False):
    feature = values.shape[1] // 2
    wide = 2 * LANES
    groups = []
    for group in range(2):
        part = values[:, group * feature : (group + 1) * feature]
        count = feature // wide
        for t in range(count):
            begin, end = max(t - 1, 0) * wide, min(t + 2, count) * wide
            here = slice(t * wide, (t + 1) * wide)
            if back:
                groups.append(mm(part[:, begin:end], matrix_ref[group, here, begin:end], (1, 1)))
            else:
                groups.append(mm(part[:, begin:end], matrix_ref[group, begin:end, here]))
    return jnp.concatenate(groups, axis=1)


def first_kernel(rows_ref, cols_ref, tokens_ref, first_ref, half_ref, normal_ref):
    feature = tokens_ref.shape[1]
    normal, _ = normalize(tokens_ref[...].astype(F32))
    live = live_rows(pl.program_id(0) * CELLS, CELLS, rows_ref, cols_ref)
    normal = normal * live
    normal_ref[...] = normal.astype(BF)
    half_ref[:, :, :feature] = turn(first_ref, normal).reshape(KEPT, 2 * GROUP, feature)
    ones = jnp.broadcast_to(live, (CELLS, LANES)).astype(BF)
    half_ref[:, :, feature:] = (mm(first_ref[0], ones) + mm(first_ref[1], ones)).reshape(KEPT, 2 * GROUP, LANES)


def first(rows, cols, tokens, tables, deps=()):
    cells, feature = tokens.shape
    table = tables["first"]
    return launch(
        deps,
        first_kernel,
        grid=(STEPS,),
        out_shape=(
            jax.ShapeDtypeStruct((KEPT, 2 * ROWS, feature + LANES), F32),
            jax.ShapeDtypeStruct((cells, feature), BF),
        ),
        in_specs=[smem(), smem(), pl.BlockSpec((CELLS, feature), lambda i: (i, 0)), single(table.shape)],
        out_specs=(
            pl.BlockSpec((KEPT, 2 * GROUP, feature + LANES), lambda i: (0, i, 0)),
            pl.BlockSpec((CELLS, feature), lambda i: (i, 0)),
        ),
        compiler_params=params(),
        cost_estimate=cost(6e9, 11e6),
        name="first",
    )(rows, cols, tokens, table)


def build_mix(me, bits, weights_ref, layer, out_ref, feature):
    block = feature // BLOCKS
    half = feature // 2
    per_group = BLOCKS // 2
    share = 2 * feature // weights_ref.shape[0]
    each = block // share
    out_ref[...] = jnp.zeros_like(out_ref)
    row = lax.broadcasted_iota(jnp.int32, (LANES, half), 0)
    column = lax.broadcasted_iota(jnp.int32, (LANES, half), 1)
    for b in range(per_group):
        shift = jnp.where((column - b * block == row) & (row < block), 1.0, 0.0).astype(BF)
        low, high = b * block, (b + 1) * block
        for group in range(2):
            for part in range(2):
                at = (part * BLOCKS + group * per_group + b) * each
                pieces = [
                    weights_ref[place_of((at + k) ^ me, bits), layer * share : (layer + 1) * share, :]
                    for k in range(each)
                ]
                placed = mm(jnp.concatenate(pieces, axis=0), shift).astype(BF)
                for t in range(low // LANES, (high - 1) // LANES + 1):
                    begin, end = max(low, t * LANES), min(high, (t + 1) * LANES)
                    for c in range(low // LANES, (high - 1) // LANES + 1):
                        piece = placed[begin - low : end - low, c * LANES : (c + 1) * LANES]
                        for up in range(2):
                            top = 2 * t * LANES + up * LANES + begin - t * LANES
                            left = (2 * c + (up ^ part)) * LANES
                            value = -piece if part == 1 and up == 1 else piece
                            here = (group, slice(top, top + end - begin), slice(left, left + LANES))
                            out_ref[here] = out_ref[here] + value


def mix_step(half_ref, head_ref, body_ref, back_head_ref, back_body_ref, mix1_ref, mix2_ref, wide_ref, long_ref,
             outs, heads, out_ref, is_head):
    feature = out_ref.shape[2]
    rows = HEAD if is_head else BODY
    spec = turn(head_ref if is_head else body_ref, half_ref[...].reshape(2 * BODY, feature + LANES))
    gain = wide_ref[0:1, :]
    shift = wide_ref[1:2, :]

    def scaled(part):
        flat = jnp.concatenate([part[:, feature:]] * (feature // LANES), axis=1)
        return (part[:, :feature] * gain + flat * shift).astype(BF)

    inside = to_mixed(scaled(spec[:rows]), scaled(spec[rows:]))
    active, slope = gelu_parts(mix_product(inside, mix1_ref) + long_ref[0:1, :])
    hidden = active.astype(BF)
    value = mix_product(hidden, mix2_ref) + long_ref[1:2, :]
    bend = jnp.tanh(value / SHRINK)
    flat = jnp.concatenate([spec[:rows, feature:], spec[rows:, feature:]], axis=1)
    for ref, head, kept in zip(outs, heads, (inside, hidden, slope, bend * bend, flat)):
        ref[...] = kept[:BODY]
        if is_head:
            head[...] = kept[BODY:]
    values = jnp.concatenate(from_mixed(value - SHRINK * bend), axis=0)
    out_ref[...] = turn(back_head_ref if is_head else back_body_ref, values).reshape(GROUP, 2 * ROWS, feature)


def mix_first_kernel(
    weight_bits, vector_bits, me_ref, half_ref, weights_ref, vector_ref, head_ref, body_ref, back_head_ref, back_body_ref,
    out_ref, low_ref, hidden_ref, slope_ref, bend_ref, flat_ref,
    low_head_ref, hidden_head_ref, slope_head_ref, bend_head_ref, flat_head_ref, mix1_ref, mix2_ref, wide_ref, long_ref, up_ref,
):
    feature = out_ref.shape[2]
    devices = vector_ref.shape[1]
    share = feature // devices
    step = pl.program_id(0)
    outs = (low_ref, hidden_ref, slope_ref, bend_ref, flat_ref)
    heads = (low_head_ref, hidden_head_ref, slope_head_ref, bend_head_ref, flat_head_ref)
    work = functools.partial(
        mix_step, half_ref, head_ref, body_ref, back_head_ref, back_body_ref, mix1_ref, mix2_ref, wide_ref, long_ref,
        outs, heads, out_ref,
    )

    @pl.when(step == 0)
    def _():
        me = me_ref[0]
        build_mix(me, weight_bits, weights_ref, 0, mix1_ref, feature)
        build_mix(me, weight_bits, weights_ref, 1, mix2_ref, feature)
        wide_ref[...] = jnp.zeros_like(wide_ref)
        long_ref[...] = jnp.zeros_like(long_ref)
        for row, at in enumerate((2, 3, 4, 5, 7)):
            wide_ref[row : row + 1, :] = spread(vector_ref[at], share, me, vector_bits)
        for row in range(2):
            both = spread(vector_ref[row], 2 * share, me, vector_bits)
            long_ref[row : row + 1, :] = to_mixed(both[:, :feature], both[:, feature:])
        up_ref[...] = spread(vector_ref[6], up_ref.shape[1] // devices, me, vector_bits)
        work(True)

    @pl.when(step > 0)
    def _():
        work(False)


def mix_second_kernel(
    half_ref, mix1_ref, mix2_ref, wide_ref, long_ref, body_ref, back_body_ref,
    out_ref, *outs,
):
    mix_step(
        half_ref, None, body_ref, None, back_body_ref, mix1_ref, mix2_ref, wide_ref, long_ref,
        outs, (None,) * 5, out_ref, False,
    )


def mode_shapes(rows, feature):
    wide = [jax.ShapeDtypeStruct((rows, 2 * feature), kind) for kind in (BF, BF, F32, F32)]
    return wide + [jax.ShapeDtypeStruct((rows, 2 * LANES), F32)]


def mode_blocks(feature):
    return [pl.BlockSpec((BODY, width), lambda i: (i, 0)) for width in (2 * feature,) * 4 + (2 * LANES,)]


def half_block(width, begin=0):
    return pl.BlockSpec((GROUP, 2 * ROWS, width), lambda i: (i + begin, 0, 0))


def mix_first(me, half, weights, vectors, tables, hidden, steps, weight_bits, vector_bits, deps=()):
    feature = half.shape[2] - LANES
    fixed = (weights, vectors, tables["head"], tables["body"], tables["head_wt"], tables["body_wt"])
    more = (
        jax.ShapeDtypeStruct((2, feature, feature), BF),
        jax.ShapeDtypeStruct((2, feature, feature), BF),
        jax.ShapeDtypeStruct((8, feature), F32),
        jax.ShapeDtypeStruct((8, 2 * feature), F32),
        jax.ShapeDtypeStruct((1, hidden), F32),
    )
    heads = mode_shapes(ROWS, feature)
    return launch(
        deps,
        functools.partial(mix_first_kernel, weight_bits, vector_bits),
        grid=(steps,),
        out_shape=[jax.ShapeDtypeStruct((GROUP * steps, 2 * ROWS, feature), F32)]
        + mode_shapes(BODY * steps, feature) + heads + list(more),
        in_specs=[smem(), half_block(feature + LANES)] + [single(v.shape) for v in fixed],
        out_specs=[half_block(feature)] + mode_blocks(feature) + [single(v.shape) for v in heads]
        + [single(v.shape) for v in more],
        compiler_params=params(),
        cost_estimate=cost(9e9, 20e6),
        name="mix_first",
    )(me, half, *fixed)


def mix_second(half, mix1, mix2, wide, long, tables, begin, steps, deps=()):
    feature = half.shape[2] - LANES
    fixed = (mix1, mix2, wide, long, tables["body"], tables["body_wt"])
    return launch(
        deps,
        mix_second_kernel,
        grid=(steps,),
        out_shape=[jax.ShapeDtypeStruct((GROUP * steps, 2 * ROWS, feature), F32)] + mode_shapes(BODY * steps, feature),
        in_specs=[half_block(feature + LANES, begin)] + [single(v.shape) for v in fixed],
        out_specs=[half_block(feature)] + mode_blocks(feature),
        compiler_params=params(),
        cost_estimate=cost(9e9, 20e6),
        name="mix_second",
    )(half, *fixed)


def space_kernel(rows_ref, cols_ref, half1_ref, half2_ref, tokens_ref, first_t_ref, wide_ref, middle_ref, normed_ref):
    feature = tokens_ref.shape[1]
    flat = lambda ref: ref[...].reshape(-1, feature)
    spatial = turn(first_t_ref, jnp.concatenate([flat(half1_ref), flat(half2_ref)], axis=0))
    inputs = tokens_ref[...].astype(F32)
    live = live_rows(pl.program_id(0) * CELLS, CELLS, rows_ref, cols_ref)
    normal, _ = normalize(inputs)
    middle = inputs + live * (spatial + (normal * wide_ref[0:1, :] + wide_ref[1:2, :]))
    middle_ref[...] = middle
    normal, _ = normalize(middle)
    normed_ref[...] = (normal * wide_ref[2:3, :] + wide_ref[3:4, :]).astype(BF)


def column_block(rows, width):
    return pl.BlockSpec((rows, 2 * GROUP, width), lambda i: (0, i, 0))


def space(rows, cols, half1, half2, tokens, wide, tables, deps=()):
    cells, feature = tokens.shape
    table = tables["first_t"]
    block = pl.BlockSpec((CELLS, feature), lambda i: (i, 0))
    return launch(
        deps,
        space_kernel,
        grid=(STEPS,),
        out_shape=(jax.ShapeDtypeStruct((cells, feature), F32), jax.ShapeDtypeStruct((cells, feature), BF)),
        in_specs=[smem(), smem(), column_block(half1.shape[0], feature), column_block(half2.shape[0], feature),
                  block, single(table.shape), single(wide.shape)],
        out_specs=(block, block),
        compiler_params=params(),
        cost_estimate=cost(6e9, 20e6),
        name="space",
    )(rows, cols, half1, half2, tokens, table, wide)


def fetch_weights(me_ref, pieces, places, up_ref, down_ref, sems):
    count = pieces[0].shape[0] * 2
    chip = me_ref[0] // 2

    def copies(own, core):
        target = (up_ref, down_ref)[core]
        source = pieces[:2] if own else pieces[2:]
        for mask in range(count):
            at = places[core][mask]
            part = source[at // (count // 2)].at[at % (count // 2)]
            yield pltpu.make_async_copy(part, target.at[chip ^ mask], sems.at[core, mask])

    for core in range(2):
        @pl.when(me_ref[0] % 2 == core)
        def _():
            for copy in copies(True, core):
                copy.start()
            for copy in copies(False, 1 - core):
                copy.start()

    def arrived(core):
        for copy in copies(True, core):
            copy.wait()

    return arrived


def weight_scratch(pieces):
    chips, rows, feature = pieces[0].shape[0] * 2, pieces[0].shape[1], pieces[0].shape[2]
    return [
        pltpu.VMEM((chips, rows, feature), BF),
        pltpu.VMEM((chips, rows, feature), BF),
        pltpu.SemaphoreType.DMA((2, chips)),
    ]


def up_part(up_ref, j, feature):
    share = up_ref.shape[1] * feature // (up_ref.shape[0] * up_ref.shape[1])
    return up_ref[:, j * share : (j + 1) * share, :].reshape(feature, feature)


def down_part(down_ref, j, feature):
    share = down_ref.shape[1]
    each = feature // share
    return down_ref[j * each : (j + 1) * each].reshape(feature, feature)


def up_kernel(places, rows_ref, cols_ref, me_ref, normed_ref, grad_ref, bias_ref, *rest):
    pieces = rest[:4]
    active_ref, pre_ref, live_ref, bias_grad_ref, up_all_ref, down_all_ref, up_ref, down_ref, sems, out_sems = rest[4:]
    tile, feature = normed_ref.shape
    step = pl.program_id(0)
    copies = [
        pltpu.make_async_copy(source, target, out_sems.at[k])
        for k, (source, target) in enumerate(((up_ref, up_all_ref), (down_ref, down_all_ref)))
    ]

    def work(arrived):
        live = live_rows(step * tile, tile, rows_ref, cols_ref)
        branch = (grad_ref[...].astype(F32) * live).astype(BF)
        live_ref[...] = branch
        normed = normed_ref[...]
        if arrived:
            arrived(0)
            copies[0].start()
        for j in range(active_ref.shape[1] // feature):
            place = slice(j * feature, (j + 1) * feature)
            value = mm(normed, up_part(up_ref, j, feature)) + bias_ref[:, place]
            if arrived and j == 0:
                arrived(1)
                copies[1].start()
            grad = mm(branch, down_part(down_ref, j, feature), (1, 1))
            active, slope = gelu_parts(value)
            active_ref[:, place] = active.astype(BF)
            low = (grad * slope).astype(BF)
            pre_ref[:, place] = low
            bias_grad_ref[:, place] += jnp.sum(low.astype(F32), axis=0, keepdims=True)

    @pl.when(step == 0)
    def _():
        bias_grad_ref[...] = jnp.zeros_like(bias_grad_ref)
        work(fetch_weights(me_ref, pieces, places, up_ref, down_ref, sems))

    @pl.when(step > 0)
    def _():
        work(None)

    @pl.when(step == pl.num_programs(0) - 1)
    def _():
        for copy in copies:
            copy.wait()


def feed_up(rows, cols, me, normed, grad, bias, pieces, places, tile=256, deps=()):
    cells, feature = normed.shape
    hidden = bias.shape[1]
    block = lambda width: pl.BlockSpec((tile, width), lambda i: (i, 0))
    weights = jax.ShapeDtypeStruct((2 * pieces[0].shape[0],) + pieces[0].shape[1:], BF)
    return launch(
        deps,
        functools.partial(up_kernel, places),
        grid=(cells // tile,),
        out_shape=(
            jax.ShapeDtypeStruct((cells, hidden), BF),
            jax.ShapeDtypeStruct((cells, hidden), BF),
            jax.ShapeDtypeStruct((cells, feature), BF),
            jax.ShapeDtypeStruct((1, hidden), F32),
            weights,
            weights,
        ),
        in_specs=[smem(), smem(), smem(), block(feature), block(feature), single(bias.shape)]
        + [any_space() for _ in pieces],
        out_specs=(block(hidden), block(hidden), block(feature), single((1, hidden)), any_space(), any_space()),
        scratch_shapes=weight_scratch(pieces) + [pltpu.SemaphoreType.DMA((2,))],
        compiler_params=params(),
        cost_estimate=cost(0, 0),
        name="feed_up",
    )(rows, cols, me, normed, grad, bias, *pieces)


def weight_grad_kernel(places, me_ref, active_ref, pre_ref, branch_ref, normed_ref, send_ref, keep_ref, stage_ref, sems):
    step = pl.program_id(0)
    steps = pl.num_programs(0) // 2
    feature = branch_ref.shape[1]
    chips, rows, _ = send_ref.shape
    each = feature // rows
    share = feature // chips

    def down_copies(j, target):
        for c in range(each):
            source = stage_ref.at[j, pl.ds(c * rows, rows)]
            yield pltpu.make_async_copy(source, target.at[places[1][j * each + c]], sems.at[j, c])

    def up_copies(j, target):
        for c in range(chips):
            source = stage_ref.at[steps + j, pl.ds(c * share, share)]
            there = target.at[places[0][c], pl.ds(j * share, share)]
            yield pltpu.make_async_copy(source, there, sems.at[steps + j, c])

    @pl.when(step < steps)
    def _():
        stage_ref[step] = mm(active_ref[...], branch_ref[...], (0, 0)).astype(BF)

    @pl.when(step >= steps)
    def _():
        stage_ref[step] = mm(normed_ref[...], pre_ref[...], (0, 0)).astype(BF)

    total = stage_ref.shape[0] // 2
    for j in range(total):
        for core in range(2):
            targets = (send_ref, keep_ref) if core == 0 else (keep_ref, send_ref)

            @pl.when((step == j) & (me_ref[0] % 2 == core))
            def _():
                for copy in down_copies(j, targets[0]):
                    copy.start()

            @pl.when((step == total + j) & (me_ref[0] % 2 == core))
            def _():
                for copy in up_copies(j, targets[1]):
                    copy.start()

    @pl.when(step == 2 * steps - 1)
    def _():
        for j in range(total):
            for copy in down_copies(j, send_ref):
                copy.wait()
            for copy in up_copies(j, send_ref):
                copy.wait()


def weight_grads(me, active, pre, branch, normed, places, deps=()):
    cells, hidden = active.shape
    feature = branch.shape[1]
    tiles = hidden // feature
    chips = UNITS
    shape = jax.ShapeDtypeStruct((chips, hidden // chips, feature), BF)
    return launch(
        deps,
        functools.partial(weight_grad_kernel, places),
        grid=(2 * tiles,),
        out_shape=(shape, shape),
        in_specs=[
            smem(),
            pl.BlockSpec((cells, feature), lambda i: (0, jnp.minimum(i, tiles - 1))),
            pl.BlockSpec((cells, feature), lambda i: (0, jnp.maximum(i - tiles, 0))),
            single(branch.shape), single(normed.shape),
        ],
        out_specs=(any_space(), any_space()),
        scratch_shapes=[
            pltpu.VMEM((2 * tiles, feature, feature), BF),
            pltpu.SemaphoreType.DMA((2 * tiles, chips)),
        ],
        compiler_params=params(),
        cost_estimate=cost(4 * cells * feature * hidden, 40e6),
        name="weight_grads",
    )(me, active, pre, branch, normed)


def down_kernel(rows_ref, cols_ref, active_ref, pre_ref, middle_ref, grad_ref, normal_ref, wide_ref, first_ref,
                up_ref, down_ref, mixed_ref, grad_middle_ref, half_ref, sums_ref):
    tile, feature = middle_ref.shape
    hidden = active_ref.shape[1]
    step = pl.program_id(0)

    @pl.when(step == 0)
    def _():
        sums_ref[...] = jnp.zeros_like(sums_ref)

    live = live_rows(step * tile, tile, rows_ref, cols_ref)
    branch = mm(active_ref[...], down_ref[...].reshape(hidden, feature))
    grad_normed = jnp.zeros((tile, feature), F32)
    for j in range(hidden // feature):
        pre = pre_ref[:, j * feature : (j + 1) * feature]
        grad_normed = grad_normed + mm(pre, up_part(up_ref, j, feature), (1, 1))
    middle = middle_ref[...]
    mixed_ref[...] = (middle + live * (branch + wide_ref[4:5, :])).astype(BF)
    normal, inverse = normalize(middle)
    cotangent = grad_ref[...].astype(F32)
    grad_middle = cotangent + norm_back(grad_normed, wide_ref[2:3, :], normal, inverse)
    grad_middle_ref[...] = grad_middle
    masked = grad_middle * live
    half_ref[...] = turn(first_ref, masked).reshape(half_ref.shape)
    rows = (grad_normed * normal, grad_normed, cotangent * live, masked * normal_ref[...].astype(F32), masked)
    for row, value in enumerate(rows):
        sums_ref[row : row + 1, :] += jnp.sum(value, axis=0, keepdims=True)


def feed_down(rows, cols, active, pre, middle, grad, normal, wide, table, up, down, deps=()):
    cells, feature = middle.shape
    hidden = active.shape[1]
    block = lambda width: pl.BlockSpec((CELLS, width), lambda i: (i, 0))
    operands = (rows, cols, active, pre, middle, grad, normal, wide, table, up, down)
    return launch(
        deps,
        down_kernel,
        grid=(cells // CELLS,),
        out_shape=(
            jax.ShapeDtypeStruct((cells, feature), BF),
            jax.ShapeDtypeStruct((cells, feature), F32),
            jax.ShapeDtypeStruct((KEPT, 2 * ROWS, feature), F32),
            jax.ShapeDtypeStruct((8, feature), F32),
        ),
        in_specs=[smem(), smem(), block(hidden), block(hidden), block(feature), block(feature), block(feature)]
        + [single(v.shape) for v in operands[7:]],
        out_specs=(block(feature), block(feature), column_block(KEPT, feature), single((8, feature))),
        compiler_params=params(),
        cost_estimate=cost(0, 0),
        name="feed_down",
    )(*operands)


def back_step(half_ref, head_ref, body_ref, back_head_ref, back_body_ref, mix1_ref, mix2_ref, ins, in_heads,
              outs, out_heads, out_ref, sums_ref, is_head):
    feature = out_ref.shape[2]
    rows = HEAD if is_head else BODY

    def read(k):
        if is_head:
            return jnp.concatenate([ins[k][...], in_heads[k][...]], axis=0)
        return ins[k][...]

    grad = turn(head_ref if is_head else body_ref, half_ref[...].reshape(2 * BODY, feature))
    grad_two = (to_mixed(grad[:rows], grad[rows:]) * read(1)).astype(BF)
    grad_one = (mix_product(grad_two, mix2_ref, True) * read(0)).astype(BF)
    grad_spec = mix_product(grad_one, mix1_ref, True)
    values = jnp.concatenate(from_mixed(grad_spec), axis=0)
    out_ref[...] = turn(back_head_ref if is_head else back_body_ref, values).reshape(GROUP, 2 * ROWS, feature)
    for row, value in enumerate((grad_one, grad_two)):
        outs[row][...] = value[:BODY]
        if is_head:
            out_heads[row][...] = value[BODY:]
    flat = jnp.concatenate([read(3)] * (feature // LANES), axis=1)
    for row, value in enumerate((grad_one.astype(F32), grad_two.astype(F32), grad_spec * read(2).astype(F32), grad_spec * flat)):
        total = jnp.sum(value, axis=0, keepdims=True)
        sums_ref[row : row + 1, :] = total if is_head else sums_ref[row : row + 1, :] + total


def mix_back_kernel(
    half_ref, slope1_ref, slope2_ref, bend1_ref, bend2_ref, low1_ref, low2_ref, flat1_ref, flat2_ref,
    slope_head_ref, bend_head_ref, low_head_ref, flat_head_ref, mix1_ref, mix2_ref,
    head_ref, body_ref, back_head_ref, back_body_ref,
    out_ref, one_ref, two_ref, one_head_ref, two_head_ref, sums_ref,
):
    step = pl.program_id(0)
    steps = pl.num_programs(0) // 2
    work = functools.partial(
        back_step, half_ref, head_ref, body_ref, back_head_ref, back_body_ref, mix1_ref, mix2_ref
    )
    heads = (slope_head_ref, bend_head_ref, low_head_ref, flat_head_ref)
    more = (heads, (one_ref, two_ref), (one_head_ref, two_head_ref), out_ref, sums_ref)
    near = (slope1_ref, bend1_ref, low1_ref, flat1_ref)
    far = (slope2_ref, bend2_ref, low2_ref, flat2_ref)

    @pl.when(step == 0)
    def _():
        sums_ref[...] = jnp.zeros_like(sums_ref)
        work(near, *more, True)

    @pl.when((step > 0) & (step < steps))
    def _():
        work(near, *more, False)

    @pl.when(step >= steps)
    def _():
        work(far, *more, False)


def mix_back(half, modes1, modes2, heads, mix1, mix2, tables, deps=()):
    feature = half.shape[2]
    steps = KEPT // GROUP
    fixed = tuple(heads[k] for k in (2, 3, 0, 4)) + (
        mix1, mix2, tables["head_w"], tables["body_w"], tables["head_t"], tables["body_t"]
    )
    moving = []
    specs = []
    for k in (2, 3, 0, 4):
        width = modes1[k].shape[1]
        moving += [modes1[k], modes2[k]]
        specs += [
            pl.BlockSpec((BODY, width), lambda i: (jnp.minimum(i, steps // 2 - 1), 0)),
            pl.BlockSpec((BODY, width), lambda i: (jnp.maximum(i - steps // 2, 0), 0)),
        ]
    low = lambda rows: jax.ShapeDtypeStruct((rows, 2 * feature), BF)
    body = pl.BlockSpec((BODY, 2 * feature), lambda i: (i, 0))
    shapes = (
        jax.ShapeDtypeStruct((KEPT, 2 * ROWS, feature), F32), low(BODY * steps), low(BODY * steps),
        low(ROWS), low(ROWS), jax.ShapeDtypeStruct((8, 2 * feature), F32),
    )
    return launch(
        deps,
        mix_back_kernel,
        grid=(steps,),
        out_shape=shapes,
        in_specs=[half_block(feature)] + specs + [single(v.shape) for v in fixed],
        out_specs=[half_block(feature), body, body] + [single(v.shape) for v in shapes[3:]],
        compiler_params=params(),
        cost_estimate=cost(18e9, 30e6),
        name="mix_back",
    )(half, *moving, *fixed)


def block_kernel(left1_ref, left2_ref, left_head_ref, right_ref, right_head_ref, out_ref, natural_ref):
    wide = 2 * LANES
    count = left1_ref.shape[1] // wide
    cut = left1_ref.shape[0]
    for t in range(count):
        for c in range(max(t - 1, 0), min(t + 2, count)):
            left, right = slice(t * wide, (t + 1) * wide), slice(c * wide, (c + 1) * wide)
            total = (
                mm(left1_ref[:, left], right_ref[:cut, right], (0, 0))
                + mm(left2_ref[:, left], right_ref[cut:, right], (0, 0))
                + mm(left_head_ref[:, left], right_head_ref[:, right], (0, 0))
            )
            rows, lanes = slice(t * LANES, (t + 1) * LANES), slice(c * LANES, (c + 1) * LANES)
            natural_ref[0, rows, lanes] = total[:LANES, :LANES] + total[LANES:, LANES:]
            natural_ref[1, rows, lanes] = total[:LANES, LANES:] - total[LANES:, :LANES]
    per_group = BLOCKS // 2
    block = count * LANES // per_group
    for b in range(per_group):
        begin = b * block
        base = begin // LANES * LANES
        reach = min(base + wide, count * LANES) - base
        for part in range(2):
            piece = natural_ref[part, begin : begin + block, base : base + reach]
            if begin > base:
                piece = pltpu.roll(piece, reach - (begin - base), axis=1)
            out_ref[part, b * block : (b + 1) * block, :] = piece[:, :LANES]


def block_grads(left1, left2, left_head, right, right_head, name, deps=()):
    feature = left1.shape[1] // 2
    half = feature // 2
    block = lambda v: pl.BlockSpec((v.shape[0], feature), lambda i: (0, i))
    return launch(
        deps,
        block_kernel,
        grid=(2,),
        out_shape=jax.ShapeDtypeStruct((2, feature, LANES), F32),
        in_specs=[block(v) for v in (left1, left2, left_head, right, right_head)],
        out_specs=pl.BlockSpec((2, half, LANES), lambda i: (0, i, 0)),
        scratch_shapes=[pltpu.VMEM((2, half, half), F32)],
        compiler_params=params(),
        cost_estimate=cost(5e9, 7e6),
        name=name,
    )(left1, left2, left_head, right, right_head)


def last_kernel(begin, rows_ref, cols_ref, half_ref, tokens_ref, grad_ref, first_t_ref, wide_ref, *rest):
    out_ref = rest[-1]
    tile, feature = tokens_ref.shape
    live = live_rows((pl.program_id(0) + begin) * tile, tile, rows_ref, cols_ref)
    grad_middle = grad_ref[...]
    grad_normed = live * (grad_middle + turn(first_t_ref, half_ref[...].reshape(CELLS, feature)))
    normal, inverse = normalize(tokens_ref[...].astype(F32))
    out_ref[...] = grad_middle + norm_back(grad_normed, wide_ref[0:1, :], normal, inverse)


def last(rows, cols, half, tokens, grad, wide, tables, begin, steps, before=(), deps=()):
    cells, feature = tokens.shape
    first_t = tables["first_t"]
    block = pl.BlockSpec((CELLS, feature), lambda i: (i + begin, 0))
    operands = (rows, cols, half, tokens, grad, first_t, wide)
    return launch(
        deps,
        functools.partial(last_kernel, begin),
        grid=(steps,),
        out_shape=jax.ShapeDtypeStruct((cells, feature), F32),
        in_specs=[smem(), smem(), pl.BlockSpec((KEPT, 2 * GROUP, feature), lambda i: (0, i + begin, 0)), block, block,
                  single(first_t.shape), single(wide.shape)] + [any_space() for _ in before],
        out_specs=block,
        input_output_aliases={len(operands): 0} if before else {},
        compiler_params=params(),
        cost_estimate=cost(6e9, 20e6),
        name="last",
    )(*operands, *before)


def collect(value, per_device, devices):
    total = value.shape[1]
    owner = lax.broadcasted_iota(jnp.int32, (devices, total), 1) // per_device
    row = lax.broadcasted_iota(jnp.int32, (devices, total), 0)
    high, low = split(jnp.where(owner == row, jnp.broadcast_to(value, (devices, total)), 0.0))
    place = lax.broadcasted_iota(jnp.int32, (total, LANES), 0)
    lane = lax.broadcasted_iota(jnp.int32, (total, LANES), 1)
    pick = jnp.where(place % per_device == lane, 1.0, 0.0).astype(BF)
    return mm(high, pick) + mm(low, pick)


def emit(upper_ref, sum_ref, send_ref, keep_ref):
    rows = sum_ref.shape[2] - 8
    half = sum_ref.shape[0]
    away = sum_ref[:, pl.ds(1 - upper_ref[0], 1)].reshape(half, rows + 8, LANES)
    high, low = split(away[:, rows:])
    send_ref[:, :rows] = away[:, :rows].astype(BF)
    send_ref[:, rows:] = jnp.concatenate([high.astype(F32), low.astype(F32)], axis=1).astype(BF)
    keep_ref[...] = sum_ref[:, pl.ds(upper_ref[0], 1)].reshape(half, rows + 8, LANES)


def pack_kernel(upper_ref, one_ref, two_ref, mixed_ref, sums_ref, up_ref, wide_ref, send_ref, keep_ref, sum_ref):
    half, _, rows, _ = sum_ref.shape
    devices = 2 * half
    share = (rows - 8) // 4
    feature = sums_ref.shape[1]
    sum_ref[:, :, : 2 * share] = one_ref[...].reshape(half, 2, 2 * share, LANES)
    sum_ref[:, :, 2 * share : 4 * share] = two_ref[...].reshape(half, 2, 2 * share, LANES)
    first_gain, first_bias = scale_grads(mixed_ref, sums_ref, wide_ref)
    natural = [jnp.concatenate(from_mixed(mixed_ref[k : k + 1, :]), axis=1) for k in range(2)]
    narrow = [first_gain, first_bias] + [sums_ref[k : k + 1, :] for k in range(3)]
    for k, value in enumerate(narrow + natural + [up_ref[...]]):
        placed = collect(value, value.shape[1] // devices, devices)
        for d in range(devices):
            sum_ref[d // 2, d % 2, 4 * share + k : 4 * share + k + 1, :] = placed[d : d + 1, :]
    emit(upper_ref, sum_ref, send_ref, keep_ref)


def scale_grads(mixed_ref, sums_ref, wide_ref):
    real, imag = from_mixed(mixed_ref[2:3, :])
    scaled = real + imag
    real, imag = from_mixed(mixed_ref[3:4, :])
    flat = real + imag
    gain = sums_ref[3:4, :] + (scaled - wide_ref[1:2, :] * flat) / wide_ref[0:1, :]
    return gain, sums_ref[4:5, :] + flat


def small_shapes(half, rows):
    return (
        jax.ShapeDtypeStruct((half, rows + 8, LANES), BF),
        jax.ShapeDtypeStruct((half, rows, LANES), F32),
    )


def pack(upper, one, two, mixed, sums, up, wide, devices):
    rows = 2 * one.shape[0] * one.shape[1] // devices + 8
    shapes = small_shapes(devices // 2, rows)
    operands = (one, two, mixed, sums, up, wide)
    return pl.pallas_call(
        pack_kernel,
        out_shape=shapes,
        in_specs=[smem()] + vmem(len(operands)),
        out_specs=vmem(2),
        scratch_shapes=[pltpu.VMEM((devices // 2, 2, rows, LANES), F32)],
        compiler_params=params(),
        cost_estimate=cost(0, 0),
        name="pack",
    )(upper, *operands)


def merge_small(keep_ref, got_ref):
    rows = keep_ref.shape[1] - 8
    tail = got_ref[:, rows:].astype(F32)
    return (
        keep_ref[:, :rows] + got_ref[:, :rows].astype(F32),
        keep_ref[:, rows:] + tail[:, :8] + tail[:, 8:],
    )


def fold_small_kernel(upper_ref, keep_ref, got_ref, send_ref, out_ref, sum_ref):
    half, _, rows, _ = sum_ref.shape
    top, tail = merge_small(keep_ref, got_ref)
    sum_ref[:, :, : rows - 8] = top.reshape(half, 2, rows - 8, LANES)
    sum_ref[:, :, rows - 8 :] = tail.reshape(half, 2, 8, LANES)
    emit(upper_ref, sum_ref, send_ref, out_ref)


def fold_small(keep, got, upper, deps=()):
    half, rows = keep.shape[0] // 2, keep.shape[1]
    return launch(
        deps,
        fold_small_kernel,
        out_shape=small_shapes(half, rows),
        in_specs=[smem()] + vmem(2),
        out_specs=vmem(2),
        scratch_shapes=[pltpu.VMEM((half, 2, rows, LANES), F32)],
        compiler_params=params(),
        cost_estimate=cost(0, 0),
        name="fold_small",
    )(upper, keep, got)


def vmem(count):
    return [pl.BlockSpec(memory_space=pltpu.VMEM)] * count


def end_small_kernel(keep_ref, got_ref, one_ref, two_ref, *rows_refs):
    top, tail = merge_small(keep_ref, got_ref)
    share, block = one_ref.shape
    one_ref[...] = top[0, :share, :block]
    two_ref[...] = top[0, share:, :block]
    for row, ref in enumerate(rows_refs):
        ref[...] = tail[0, row : row + 1, : ref.shape[1]]


def end_small(keep, got, share, block, widths):
    shapes = [jax.ShapeDtypeStruct((share, block), F32)] * 2
    shapes += [jax.ShapeDtypeStruct((1, width), F32) for width in widths]
    return pl.pallas_call(
        end_small_kernel,
        out_shape=shapes,
        in_specs=vmem(2),
        out_specs=vmem(len(shapes)),
        compiler_params=params(),
        cost_estimate=cost(0, 0),
        name="end_small",
    )(keep, got)


def begin_small_kernel(one_ref, two_ref, *rest):
    out_ref, rows_ref = rest[-2:]
    share, block = one_ref.shape
    out_ref[...] = jnp.zeros_like(out_ref)
    rows_ref[...] = jnp.zeros_like(rows_ref)
    out_ref[0, :share, :block] = one_ref[...]
    out_ref[0, share : 2 * share, :block] = two_ref[...]
    for row, ref in enumerate(rest[:-2]):
        rows_ref[row : row + 1, : ref.shape[1]] = ref[...].astype(F32)
    out_ref[0, 2 * share :, :] = rows_ref[...].astype(BF)


def begin_small(one, two, vectors):
    share = one.shape[0]
    operands = (one, two) + tuple(v[None] for v in vectors)
    return pl.pallas_call(
        begin_small_kernel,
        out_shape=jax.ShapeDtypeStruct((1, 2 * share + 16, LANES), BF),
        in_specs=vmem(len(operands)),
        out_specs=vmem(1)[0],
        scratch_shapes=[pltpu.VMEM((16, LANES), F32)],
        compiler_params=params(),
        cost_estimate=cost(0, 0),
        name="begin_small",
    )(*operands)


AXES = ("dp", "fsdp")


def swap(value, devices, bits):
    return lax.ppermute(value, AXES, [(i, i ^ (1 << bits[i & 1])) for i in range(devices)])


def doubling_orders(count):
    first = list(range(count - 1, 0, -1))
    second = list(first)
    for k in range(0, len(second) - 1, 2):
        second[k], second[k + 1] = second[k + 1], second[k]
    return first, second


def places_of(order):
    return [
        sum(1 << k for k, bit in enumerate(order) if mask >> (bit - 1) & 1) for mask in range(1 << len(order))
    ]


def pair_kernel(held_ref, got_ref, out_ref):
    count = held_ref.shape[0]
    out_ref[:count] = held_ref[...]
    out_ref[count:] = got_ref[...]


def pair(held, got, deps=()):
    shape = jax.ShapeDtypeStruct((2 * held.shape[0],) + held.shape[1:], held.dtype)
    return launch(
        deps,
        pair_kernel,
        out_shape=shape,
        in_specs=[pl.BlockSpec(memory_space=pltpu.VMEM)] * 2,
        out_specs=pl.BlockSpec(memory_space=pltpu.VMEM),
        compiler_params=params(),
        cost_estimate=cost(0, 4 * held.size * 2),
        name="pair",
    )(held, got)


def hold(value, deps):
    def body(*refs):
        pass

    return pl.pallas_call(
        body,
        out_shape=jax.ShapeDtypeStruct(value.shape, value.dtype),
        in_specs=[any_space() for _ in range(1 + len(deps))],
        out_specs=any_space(),
        input_output_aliases={0: 0},
        compiler_params=params(),
        cost_estimate=cost(0, 0),
        name="hold",
    )(value, *deps)


def gather_small(value, me, devices, count):
    held = value[None]
    for bit in list(range(3, count)) + [2, 1, 0]:
        other = swap(held, devices, (bit, bit))
        upper = (me >> bit) & 1
        axis = 0 if bit > 2 else 1
        join_two = lambda a, b: jnp.stack([a, b], axis=axis).reshape((-1,) + value.shape)
        held = jnp.where(upper == 0, join_two(held, other), join_two(other, held))
    return held


def scatter_small(value, me, devices, count, exact):
    shape = value.shape[1:]
    rows = shape[0]
    total = value
    for bit in [0, 1, 2] + list(range(count - 1, 2, -1)):
        upper = (me >> bit) & 1
        axis = 0 if bit > 2 else 1
        pair = total.reshape(((2, -1) if bit > 2 else (-1, 2)) + shape)
        away = lax.dynamic_index_in_dim(pair, 1 - upper, axis, keepdims=False)
        keep = lax.dynamic_index_in_dim(pair, upper, axis, keepdims=False)
        sums = away[:, rows - exact :]
        top = lax.reduce_precision(sums, 8, 7)
        packet = jnp.concatenate([away[:, : rows - exact], top, sums - top], axis=1).astype(BF)
        got = swap(packet, devices, (bit, bit)).astype(F32)
        low = got[:, rows - exact : rows] + got[:, rows:]
        total = keep + jnp.concatenate([got[:, : rows - exact], low], axis=1)
    return total[0]


def chip_unit(up, down, core, devices):
    parts, share, feature = up.shape
    flat = up.reshape(parts * share, feature)
    other = swap(jnp.where(core == 0, down, flat), devices, (0, 0))
    up_unit = jnp.concatenate([up, other.reshape(up.shape)], axis=1).reshape(2 * parts * share, feature)
    return jnp.where(core == 0, up_unit, jnp.concatenate([other, down]))[None]


def fold_kernel(upper_ref, keep_away_ref, got_away_ref, keep_own_ref, got_own_ref, send_ref, keep_ref):
    send_ref[...] = (keep_away_ref[...].astype(F32) + got_away_ref[...].astype(F32)).astype(BF)
    keep_ref[...] = (keep_own_ref[...].astype(F32) + got_own_ref[...].astype(F32)).astype(BF)


def fold(keep, got, upper, deps=()):
    half = keep.shape[0] // 2
    each = min(2, half)
    unit = (each,) + keep.shape[1:]
    count = len(deps)
    away = pl.BlockSpec(unit, lambda i, up: ((1 - up[0]) * (half // each) + i, 0, 0))
    own = pl.BlockSpec(unit, lambda i, up: (up[0] * (half // each) + i, 0, 0))
    out = pl.BlockSpec(unit, lambda i, up: (i, 0, 0))
    shape = jax.ShapeDtypeStruct((half,) + keep.shape[1:], BF)

    def body(*refs):
        fold_kernel(*refs[:5], *refs[5 + count :])

    return pl.pallas_call(
        body,
        grid_spec=pltpu.PrefetchScalarGridSpec(
            num_scalar_prefetch=1,
            grid=(half // each,),
            in_specs=[away, away, own, own] + [any_space() for _ in deps],
            out_specs=[out, out],
        ),
        out_shape=(shape, shape),
        compiler_params=params(),
        cost_estimate=cost(0, 6 * half * keep[0].size),
        name="fold",
    )(upper, keep, got, keep, got, *deps)


def on_device(
    tokens, grad_out, region_rows, region_cols, ln1_gain, ln1_bias, spec_w1, spec_b1, spec_w2, spec_b2,
    ln2_gain, ln2_bias, w_up, up_bias, w_down, down_bias,
):
    devices = lax.axis_size(AXES[0]) * lax.axis_size(AXES[1])
    count = devices.bit_length() - 1
    me = lax.axis_index(AXES).astype(jnp.int32)
    core = me & 1
    me_one = me.reshape(1)
    feature = tokens.shape[-1]
    block = feature // BLOCKS
    share = ln1_gain.shape[0]
    cells = tokens.shape[1] * tokens.shape[2]
    hidden = w_up.shape[1]
    parts = hidden // feature
    tables = {name: jnp.asarray(value) for name, value in wave_matrices().items()}
    orders = doubling_orders(count)
    places = tuple(places_of(order) for order in orders)
    flat_tokens = tokens.reshape(cells, feature)
    flat_grad = grad_out.reshape(cells, feature)
    fast = devices // 2 == UNITS
    step = lambda value, k: swap(value, devices, (orders[0][k], orders[1][k]))

    padded = lambda v: jnp.pad(v, ((0, 0), (0, LANES - v.shape[1])))
    vectors = (spec_b1, spec_b2, ln1_gain, ln1_bias, ln2_gain, ln2_bias, up_bias, down_bias)
    if fast:
        own_up = w_up.reshape(share, parts, feature).transpose(1, 0, 2)
        unit = chip_unit(own_up, w_down, core, devices)
        bits = tuple(range(3, count)) + (2, 1, 0)
        meet = lambda value, bit: swap(value, devices, (bit, bit))
        small = begin_small(spec_w1, spec_w2, vectors)
        small = pair(small, meet(small, bits[0]))
        unit = hold(unit, (small,))
        half, normal = first(region_rows, region_cols, flat_tokens, tables, deps=(unit, small))
        small = pair(small, meet(small, bits[1]), deps=(half,))
        near = pair(unit, step(unit, 0), deps=(small,))
        small = pair(small, meet(small, bits[2]), deps=(near,))
        for k in range(3, count):
            small = pair(small, meet(small, bits[k]))
        near = pair(near, step(near, 1), deps=(small,))
        weights, weight_bits, vector_bits, me_small = small, bits, bits, me_one
        vectors = small[:, 4 * share : 4 * share + 8].transpose(1, 0, 2).astype(F32)
    else:
        up = lax.all_gather(w_up, AXES, axis=0, tiled=True)
        up = up.reshape(UNITS, feature // UNITS, parts, feature).transpose(0, 2, 1, 3).reshape(UNITS, -1, feature)
        down = lax.all_gather(w_down, AXES, axis=0, tiled=True).reshape(UNITS, -1, feature)
        pieces = tuple(
            jnp.where(core == 0, one, two)[begin : begin + UNITS // 2]
            for one, two in ((up, down), (down, up))
            for begin in (0, UNITS // 2)
        )
        me_one = core.reshape(1)
        me_small = jnp.zeros_like(me_one)
        places = (tuple(range(UNITS)),) * 2
        small = jnp.concatenate([padded(spec_w1), padded(spec_w2)] + [padded(v[None]) for v in vectors])
        small = gather_small(small, me, devices, count)
        weights = small[:, : 4 * share].reshape(devices, 2, 2 * share, LANES).transpose(1, 0, 2, 3)
        weights = weights.reshape(2, 2 * UNITS, -1, LANES).transpose(1, 0, 2, 3).reshape(2 * UNITS, -1, LANES)
        weight_bits, vector_bits = tuple(range(5)), tuple(range(count))
        half, normal = first(region_rows, region_cols, flat_tokens, tables)
        vectors = small[:, 4 * share :].transpose(1, 0, 2).astype(F32)

    steps = KEPT // GROUP
    made = mix_first(
        me_small, half, weights, vectors, tables, hidden, steps // 2, weight_bits, vector_bits,
        deps=(near,) if fast else (),
    )
    half1, modes1, heads, (mix1, mix2, wide, long, up_shift) = made[0], made[1:6], made[6:11], made[11:]
    if fast:
        near = pair(near, step(near, 2), deps=(half1,))
        far = step(near, 3)
    made = mix_second(
        half, mix1, mix2, wide, long, tables, steps // 2, steps // 2, deps=(near,) if fast else ()
    )
    half2, modes2 = made[0], made[1:6]
    middle, normed = space(region_rows, region_cols, half1, half2, flat_tokens, wide, tables)
    if fast:
        far = hold(far, (normed,))
        pieces = (near, far, swap(near, devices, (0, 0)), swap(far, devices, (0, 0)))
    active, pre, branch, bias_grad, up_all, down_all = feed_up(
        region_rows, region_cols, me_one, normed, flat_grad, up_shift, pieces, places
    )
    send, keep = weight_grads(me_one, active, pre, branch, normed, places)
    tiles = cells // CELLS
    mixed, grad_middle, half_back, sums_two = feed_down(
        region_rows, region_cols, active, pre, middle, flat_grad, normal, wide, tables["first"], up_all, down_all,
        deps=(send,),
    )
    deps = ()
    if fast:
        ranks = [((me >> jnp.where(core == 0, *bit)) & 1).reshape(1) for bit in zip(*orders)]
        send, keep = fold(keep, swap(send, devices, (0, 0)), ranks[3], deps=(sums_two,))
        deps = (send,)
    half_back, one, two, one_head, two_head, bias_sums = mix_back(
        half_back, modes1, modes2, heads, mix1, mix2, tables, deps=deps
    )
    if fast:
        send, keep = fold(keep, step(send, 3), ranks[2], deps=(bias_sums,))
        deps = (send,)
    grad_two = block_grads(modes1[1], modes2[1], heads[1], two, two_head, "grad_mix2", deps=deps)
    grad_one = block_grads(modes1[0], modes2[0], heads[0], one, one_head, "grad_mix1", deps=deps)
    last_args = (region_rows, region_cols, half_back, flat_tokens, grad_middle, wide, tables)
    if fast:
        uppers = [((me >> bit) & 1).reshape(1) for bit in range(count)]
        away, own = pack(uppers[0], grad_one, grad_two, bias_sums, sums_two, bias_grad, wide, devices)
        send, keep = fold(keep, step(send, 2), ranks[1], deps=(away,))
        grad_tokens = last(*last_args, 0, 2, deps=(send, away))
        away, own = fold_small(own, meet(away, 0), uppers[1], deps=(grad_tokens,))
        grad_tokens = last(*last_args, 2, 2, (grad_tokens,), deps=(away,))
        send, keep = fold(keep, step(send, 1), ranks[0], deps=(grad_tokens,))
        away, own = fold_small(own, meet(away, 1), uppers[2], deps=(send,))
        grad_tokens = last(*last_args, 4, 2, (grad_tokens,), deps=(away,))
        keep = hold(keep, (grad_tokens,))
        total = keep[0].astype(F32) + step(send, 0)[0].astype(F32)
        up_sum = total.reshape(parts, 2 * share, feature)
        lower = up_sum[:, :share].reshape(parts * share, feature)
        upper = up_sum[:, share:].reshape(parts * share, feature)
        each = parts * share
        other = swap(jnp.where(core == 0, upper, total[:each]), devices, (0, 0))
        grad_w_up = jnp.where(core == 0, lower, other).reshape(parts, share, feature).transpose(1, 0, 2)
        grad_w_down = jnp.where(core == 0, other, total[each:])
        away, own = fold_small(own, meet(away, 2), uppers[3], deps=(grad_tokens,))
        grad_tokens = last(*last_args, 6, 2, (grad_tokens,), deps=(away,))
        away, own = fold_small(own, meet(away, 3), uppers[4], deps=(grad_tokens,))
        widths = (share,) * 5 + (2 * share,) * 2 + (hidden // devices,)
        blocks = end_small(own, meet(away, 4), 2 * share, block, widths)
        rows = [v.reshape(-1) for v in blocks[2:]]
        blocks = blocks[:2]
    else:
        scatter = lambda v: lax.psum_scatter(v.astype(F32), AXES, scatter_dimension=0, tiled=True)
        up = jnp.where(core == 0, keep, send).reshape(UNITS, parts, feature // UNITS, feature)
        grad_w_up = scatter(up.transpose(0, 2, 1, 3).reshape(feature, hidden))
        grad_w_down = scatter(jnp.where(core == 0, send, keep).reshape(hidden, feature))
        grad_tokens = last(*last_args, 0, tiles)
        owned = lambda v: jnp.pad(
            v.reshape(v.shape[0], devices, -1).transpose(1, 0, 2), ((0, 0), (0, 0), (0, LANES - v.shape[1] // devices))
        )
        narrow = jnp.concatenate(list(scale_grads(bias_sums, sums_two, wide)) + [sums_two[:3]])
        biases = bias_sums[:2].reshape(2, feature // LANES, 2, LANES).transpose(0, 2, 1, 3).reshape(2, 2 * feature)
        blocks = [v.reshape(devices, 2 * share, LANES) for v in (grad_one, grad_two)]
        packet = jnp.concatenate(blocks + [owned(narrow), owned(biases), owned(bias_grad)], axis=1)
        result = scatter_small(packet, me, devices, count, 8)
        widths = (share,) * 5 + (2 * share,) * 2 + (hidden // devices,)
        rows = [result[4 * share + k, :width] for k, width in enumerate(widths)]
        blocks = [result[k * 2 * share : (k + 1) * 2 * share, :block] for k in range(2)]
    return (
        mixed.reshape(tokens.shape),
        grad_tokens.reshape(tokens.shape),
        rows[0],
        rows[1],
        blocks[0],
        rows[5],
        blocks[1],
        rows[6],
        rows[2],
        rows[3],
        grad_w_up.reshape(share, hidden),
        rows[7],
        grad_w_down,
        rows[4],
    )


def solution(mesh):
    placed = P(AXES)
    return jax.shard_map(
        on_device, mesh=mesh, in_specs=(placed,) * 16, out_specs=(placed,) * 14, check_vma=False
    )
```

```python
import functools
import math

import jax
import jax.numpy as jnp
import numpy as np
from jax import lax
from jax.experimental import pallas as pl
from jax.experimental.pallas import tpu as pltpu
from jax.sharding import PartitionSpec as P

BF = jnp.bfloat16
F32 = jnp.float32
BLOCKS = 8
EPS = 1e-05
SHRINK = 0.01
ROWS = 32
COLS = 64
KEPT = COLS // 2
GROUP = 4
STEPS = ROWS // GROUP
CELLS = GROUP * COLS
MODES = (KEPT + 1) * ROWS
HEAD = (GROUP + 1) * ROWS
BODY = GROUP * ROWS
TAKE = 2
TOOK = TAKE * BODY
LANES = 128
C1 = math.sqrt(2.0 / math.pi)
C3 = 0.044715
UNITS = 16
VMEM_LIMIT = 60 * 1024 * 1024


def table_parts(values):
    high = values.astype(np.float32).astype(jnp.bfloat16)
    low = (values - high.astype(np.float64)).astype(np.float32).astype(jnp.bfloat16)
    return np.stack([high, low])


def wave_matrices():
    scale = 1.0 / math.sqrt(ROWS * COLS)
    w = np.arange(COLS)
    first = np.zeros((KEPT, 2, GROUP, GROUP, COLS))
    for k in range(KEPT):
        for h in range(GROUP):
            if k == 0:
                first[k, 0, h, h] = scale
                first[k, 1, h, h] = scale * np.where(w % 2 == 0, 1.0, -1.0)
            else:
                first[k, 0, h, h] = scale * np.cos(2 * np.pi * (k * w % COLS) / COLS)
                first[k, 1, h, h] = -scale * np.sin(2 * np.pi * (k * w % COLS) / COLS)
    first = first.reshape(CELLS, CELLS)
    p = np.arange(ROWS)
    turn = 2 * np.pi * (np.outer(p, p) % ROWS) / ROWS
    cos = np.cos(turn).reshape(ROWS, STEPS, GROUP)
    sin = np.sin(turn).reshape(ROWS, STEPS, GROUP)
    body = np.zeros((2, GROUP, ROWS, GROUP, STEPS, 2, GROUP))
    head = np.zeros((2, GROUP + 1, ROWS, GROUP, STEPS, 2, GROUP))
    for k in range(GROUP):
        body[0, k, :, k, :, 0] = cos
        body[0, k, :, k, :, 1] = sin
        body[1, k, :, k, :, 1] = cos
        body[1, k, :, k, :, 0] = -sin
    head[:, 1:GROUP, :, 1:] = body[:, 1:, :, 1:]
    for place, part in ((0, 0), (GROUP, 1)):
        head[0, place, :, 0, :, part] = cos
        head[1, place, :, 0, :, part] = -sin
    weight = np.full((2, GROUP + 1, ROWS, 1), 2.0)
    weight[:, 0] = 1.0
    weight[:, GROUP] = 1.0
    head = head.reshape(2 * HEAD, 2 * BODY)
    body = body.reshape(2 * BODY, 2 * BODY)
    head_weighted = head * weight.reshape(2 * HEAD, 1)
    body_weighted = body * 2.0
    return {
        "first": table_parts(first),
        "first_t": table_parts(first.T),
        "head": table_parts(head),
        "body": table_parts(body),
        "head_t": table_parts(head.T),
        "body_t": table_parts(body.T),
        "head_w": table_parts(head_weighted),
        "body_w": table_parts(body_weighted),
        "head_wt": table_parts(head_weighted.T),
        "body_wt": table_parts(body_weighted.T),
    }


def mm(left, right, dims=(1, 0)):
    return lax.dot_general(
        left, right, (((dims[0],), (dims[1],)), ((), ())), preferred_element_type=F32
    )


def split(values):
    high = values.astype(BF)
    return high, (values - high.astype(F32)).astype(BF)


def turn(table, values):
    high, low = split(values)
    return mm(table[0], high) + mm(table[1], high) + mm(table[0], low)


def normalize(values):
    centred = values - jnp.mean(values, axis=-1, keepdims=True)
    inverse = lax.rsqrt(jnp.mean(centred * centred, axis=-1, keepdims=True) + EPS)
    return centred * inverse, inverse


def norm_back(grad, gain, normal, inverse):
    scaled = grad * gain
    return inverse * (
        scaled
        - jnp.mean(scaled, axis=-1, keepdims=True)
        - normal * jnp.mean(scaled * normal, axis=-1, keepdims=True)
    )


def gelu_parts(value):
    square = value * value
    half = 0.5 + 0.5 * jnp.tanh(value * (C1 + (C1 * C3) * square))
    active = value * half
    slope = half + active * (1.0 - half) * (2.0 * C1 + (6.0 * C1 * C3) * square)
    return active, slope


def gelu(value):
    square = value * value
    return value * (0.5 + 0.5 * jnp.tanh(value * (C1 + (C1 * C3) * square)))


def live_rows(start, count, rows_ref, cols_ref):
    cell = start + lax.broadcasted_iota(jnp.int32, (count, 1), 0)
    inside = (cell // COLS < rows_ref[0]) & (cell % COLS < cols_ref[0])
    return jnp.where(inside, 1.0, 0.0).astype(F32)


def spread(piece, per_device, me, bits):
    devices = piece.shape[0]
    total = devices * per_device
    lane = lax.broadcasted_iota(jnp.int32, (LANES, total), 0)
    place = lax.broadcasted_iota(jnp.int32, (LANES, total), 1)
    pick = jnp.where(place % per_device == lane, 1.0, 0.0).astype(BF)
    wide = mm(piece.astype(BF), pick)
    row = lax.broadcasted_iota(jnp.int32, (devices, 1), 0)
    owner = jnp.full((devices, 1), me, jnp.int32)
    for k, bit in enumerate(bits):
        owner = owner ^ (((row >> k) & 1) << bit)
    where = lax.broadcasted_iota(jnp.int32, (devices, total), 1) // per_device
    return jnp.sum(jnp.where(owner == where, wide, 0.0), axis=0, keepdims=True)


def place_of(mask, bits):
    return sum(((mask >> bit) & 1) << k for k, bit in enumerate(bits))


def any_space():
    return pl.BlockSpec(memory_space=pl.ANY)


def single(shape):
    return pl.BlockSpec(shape, lambda *_: (0,) * len(shape), pipeline_mode=pl.Buffered(1))


def smem():
    return pl.BlockSpec(memory_space=pltpu.SMEM)


def params(**more):
    return pltpu.CompilerParams(vmem_limit_bytes=VMEM_LIMIT, **more)


def cost(flops, moved):
    return pl.CostEstimate(flops=0, bytes_accessed=0, transcendentals=0)


def launch(deps, kernel, *, in_specs, **more):
    count = len(in_specs)

    def body(*refs):
        kernel(*refs[:count], *refs[count + len(deps) :])

    call = pl.pallas_call(body, in_specs=list(in_specs) + [any_space() for _ in deps], **more)
    return lambda *operands: call(*operands, *deps)


def to_mixed(real, imag):
    tiles = []
    for at in range(0, real.shape[1], LANES):
        tiles += [real[:, at : at + LANES], imag[:, at : at + LANES]]
    return jnp.concatenate(tiles, axis=1)


def from_mixed(values):
    cut = lambda at: values[:, at : at + LANES]
    real = [cut(at) for at in range(0, values.shape[1], 2 * LANES)]
    imag = [cut(at + LANES) for at in range(0, values.shape[1], 2 * LANES)]
    return jnp.concatenate(real, axis=1), jnp.concatenate(imag, axis=1)


def mix_product(values, matrix_ref, back=False):
    feature = values.shape[1] // 2
    wide = 2 * LANES
    groups = []
    for group in range(2):
        part = values[:, group * feature : (group + 1) * feature]
        count = feature // wide
        for t in range(count):
            begin, end = max(t - 1, 0) * wide, min(t + 2, count) * wide
            here = slice(t * wide, (t + 1) * wide)
            if back:
                groups.append(mm(part[:, begin:end], matrix_ref[group, here, begin:end], (1, 1)))
            else:
                groups.append(mm(part[:, begin:end], matrix_ref[group, begin:end, here]))
    return jnp.concatenate(groups, axis=1)


def first_kernel(rows_ref, cols_ref, tokens_ref, first_ref, half_ref, normal_ref):
    feature = tokens_ref.shape[1]
    normal, _ = normalize(tokens_ref[...].astype(F32))
    live = live_rows(pl.program_id(0) * CELLS, CELLS, rows_ref, cols_ref)
    normal = normal * live
    normal_ref[...] = normal.astype(BF)
    half_ref[:, :, :feature] = turn(first_ref, normal).reshape(KEPT, 2 * GROUP, feature)
    ones = jnp.broadcast_to(live, (CELLS, LANES)).astype(BF)
    half_ref[:, :, feature:] = (mm(first_ref[0], ones) + mm(first_ref[1], ones)).reshape(KEPT, 2 * GROUP, LANES)


def first(rows, cols, tokens, tables, deps=()):
    cells, feature = tokens.shape
    table = tables["first"]
    return launch(
        deps,
        first_kernel,
        grid=(STEPS,),
        out_shape=(
            jax.ShapeDtypeStruct((KEPT, 2 * ROWS, feature + LANES), F32),
            jax.ShapeDtypeStruct((cells, feature), BF),
        ),
        in_specs=[smem(), smem(), pl.BlockSpec((CELLS, feature), lambda i: (i, 0)), single(table.shape)],
        out_specs=(
            pl.BlockSpec((KEPT, 2 * GROUP, feature + LANES), lambda i: (0, i, 0)),
            pl.BlockSpec((CELLS, feature), lambda i: (i, 0)),
        ),
        compiler_params=params(),
        cost_estimate=cost(6e9, 11e6),
        name="first",
    )(rows, cols, tokens, table)


def build_mix(me, bits, weights_ref, layer, out_ref, feature):
    block = feature // BLOCKS
    half = feature // 2
    per_group = BLOCKS // 2
    share = 2 * feature // weights_ref.shape[0]
    each = block // share
    out_ref[...] = jnp.zeros_like(out_ref)
    row = lax.broadcasted_iota(jnp.int32, (LANES, half), 0)
    column = lax.broadcasted_iota(jnp.int32, (LANES, half), 1)
    for b in range(per_group):
        shift = jnp.where((column - b * block == row) & (row < block), 1.0, 0.0).astype(BF)
        low, high = b * block, (b + 1) * block
        for group in range(2):
            for part in range(2):
                at = (part * BLOCKS + group * per_group + b) * each
                pieces = [
                    weights_ref[place_of((at + k) ^ me, bits), layer * share : (layer + 1) * share, :]
                    for k in range(each)
                ]
                placed = mm(jnp.concatenate(pieces, axis=0), shift).astype(BF)
                for t in range(low // LANES, (high - 1) // LANES + 1):
                    begin, end = max(low, t * LANES), min(high, (t + 1) * LANES)
                    for c in range(low // LANES, (high - 1) // LANES + 1):
                        piece = placed[begin - low : end - low, c * LANES : (c + 1) * LANES]
                        for up in range(2):
                            top = 2 * t * LANES + up * LANES + begin - t * LANES
                            left = (2 * c + (up ^ part)) * LANES
                            value = -piece if part == 1 and up == 1 else piece
                            here = (group, slice(top, top + end - begin), slice(left, left + LANES))
                            out_ref[here] = out_ref[here] + value


def to_modes(half_ref, head_ref, body_ref, is_head):
    width = half_ref.shape[2]
    real, imag, ends = [], [], ()
    for k in range(TAKE):
        begin = is_head and k == 0
        rows = HEAD if begin else BODY
        spec = turn(head_ref if begin else body_ref, half_ref[k * GROUP : (k + 1) * GROUP].reshape(2 * BODY, width))
        real.append(spec[:BODY])
        imag.append(spec[rows : rows + BODY])
        if begin:
            ends = (spec[BODY:rows], spec[rows + BODY :])
    if is_head:
        real.append(ends[0])
        imag.append(ends[1])
    return jnp.concatenate(real, axis=0), jnp.concatenate(imag, axis=0)


def from_modes(pair_of, head_ref, body_ref, is_head, out_ref):
    for k in range(TAKE):
        begin = is_head and k == 0
        parts = []
        for part in pair_of:
            parts.append(part[k * BODY : (k + 1) * BODY])
            if begin:
                parts.append(part[TOOK:])
        result = turn(head_ref if begin else body_ref, jnp.concatenate(parts, axis=0))
        out_ref[k * GROUP : (k + 1) * GROUP] = result.reshape(GROUP, 2 * ROWS, result.shape[1])


def mix_step(half_ref, head_ref, body_ref, back_head_ref, back_body_ref, mix1_ref, mix2_ref, wide_ref, long_ref,
             outs, heads, out_ref, is_head):
    feature = out_ref.shape[2]
    specs = to_modes(half_ref, head_ref, body_ref, is_head)
    gain = wide_ref[0:1, :]
    shift = wide_ref[1:2, :]

    def scaled(part):
        flat = jnp.concatenate([part[:, feature:]] * (feature // LANES), axis=1)
        return (part[:, :feature] * gain + flat * shift).astype(BF)

    inside = to_mixed(*(scaled(part) for part in specs))
    active, slope = gelu_parts(mix_product(inside, mix1_ref) + long_ref[0:1, :])
    hidden = active.astype(BF)
    value = mix_product(hidden, mix2_ref) + long_ref[1:2, :]
    bend = jnp.tanh(value / SHRINK)
    flat = jnp.concatenate([part[:, feature:] for part in specs], axis=1)
    for ref, head, kept in zip(outs, heads, (inside, hidden, slope, bend * bend, flat)):
        ref[...] = kept[:TOOK]
        if is_head:
            head[...] = kept[TOOK:]
    from_modes(from_mixed(value - SHRINK * bend), back_head_ref, back_body_ref, is_head, out_ref)


def mix_first_kernel(
    weight_bits, vector_bits, me_ref, half_ref, weights_ref, vector_ref, head_ref, body_ref, back_head_ref, back_body_ref,
    out_ref, low_ref, hidden_ref, slope_ref, bend_ref, flat_ref,
    low_head_ref, hidden_head_ref, slope_head_ref, bend_head_ref, flat_head_ref, mix1_ref, mix2_ref, wide_ref, long_ref, up_ref,
):
    feature = out_ref.shape[2]
    devices = vector_ref.shape[1]
    share = feature // devices
    step = pl.program_id(0)
    outs = (low_ref, hidden_ref, slope_ref, bend_ref, flat_ref)
    heads = (low_head_ref, hidden_head_ref, slope_head_ref, bend_head_ref, flat_head_ref)
    work = functools.partial(
        mix_step, half_ref, head_ref, body_ref, back_head_ref, back_body_ref, mix1_ref, mix2_ref, wide_ref, long_ref,
        outs, heads, out_ref,
    )

    @pl.when(step == 0)
    def _():
        me = me_ref[0]
        build_mix(me, weight_bits, weights_ref, 0, mix1_ref, feature)
        build_mix(me, weight_bits, weights_ref, 1, mix2_ref, feature)
        wide_ref[...] = jnp.zeros_like(wide_ref)
        long_ref[...] = jnp.zeros_like(long_ref)
        for row, at in enumerate((2, 3, 4, 5, 7)):
            wide_ref[row : row + 1, :] = spread(vector_ref[at], share, me, vector_bits)
        for row in range(2):
            both = spread(vector_ref[row], 2 * share, me, vector_bits)
            long_ref[row : row + 1, :] = to_mixed(both[:, :feature], both[:, feature:])
        up_ref[...] = spread(vector_ref[6], up_ref.shape[1] // devices, me, vector_bits)
        work(True)

    @pl.when(step > 0)
    def _():
        work(False)


def mix_second_kernel(
    half_ref, mix1_ref, mix2_ref, wide_ref, long_ref, body_ref, back_body_ref,
    out_ref, *outs,
):
    mix_step(
        half_ref, None, body_ref, None, back_body_ref, mix1_ref, mix2_ref, wide_ref, long_ref,
        outs, (None,) * 5, out_ref, False,
    )


def mode_shapes(rows, feature):
    wide = [jax.ShapeDtypeStruct((rows, 2 * feature), kind) for kind in (BF, BF, F32, F32)]
    return wide + [jax.ShapeDtypeStruct((rows, 2 * LANES), F32)]


def mode_blocks(feature):
    return [pl.BlockSpec((TOOK, width), lambda i: (i, 0)) for width in (2 * feature,) * 4 + (2 * LANES,)]


def half_block(width, begin=0):
    return pl.BlockSpec((TAKE * GROUP, 2 * ROWS, width), lambda i: (i + begin, 0, 0))


def mix_first(me, half, weights, vectors, tables, hidden, steps, weight_bits, vector_bits, deps=()):
    feature = half.shape[2] - LANES
    fixed = (weights, vectors, tables["head"], tables["body"], tables["head_wt"], tables["body_wt"])
    more = (
        jax.ShapeDtypeStruct((2, feature, feature), BF),
        jax.ShapeDtypeStruct((2, feature, feature), BF),
        jax.ShapeDtypeStruct((8, feature), F32),
        jax.ShapeDtypeStruct((8, 2 * feature), F32),
        jax.ShapeDtypeStruct((1, hidden), F32),
    )
    heads = mode_shapes(ROWS, feature)
    return launch(
        deps,
        functools.partial(mix_first_kernel, weight_bits, vector_bits),
        grid=(steps,),
        out_shape=[jax.ShapeDtypeStruct((TAKE * GROUP * steps, 2 * ROWS, feature), F32)]
        + mode_shapes(TOOK * steps, feature) + heads + list(more),
        in_specs=[smem(), half_block(feature + LANES)] + [single(v.shape) for v in fixed],
        out_specs=[half_block(feature)] + mode_blocks(feature) + [single(v.shape) for v in heads]
        + [single(v.shape) for v in more],
        compiler_params=params(),
        cost_estimate=cost(9e9, 20e6),
        name="mix_first",
    )(me, half, *fixed)


def mix_second(half, mix1, mix2, wide, long, tables, begin, steps, deps=()):
    feature = half.shape[2] - LANES
    fixed = (mix1, mix2, wide, long, tables["body"], tables["body_wt"])
    return launch(
        deps,
        mix_second_kernel,
        grid=(steps,),
        out_shape=[jax.ShapeDtypeStruct((TAKE * GROUP * steps, 2 * ROWS, feature), F32)] + mode_shapes(TOOK * steps, feature),
        in_specs=[half_block(feature + LANES, begin)] + [single(v.shape) for v in fixed],
        out_specs=[half_block(feature)] + mode_blocks(feature),
        compiler_params=params(),
        cost_estimate=cost(9e9, 20e6),
        name="mix_second",
    )(half, *fixed)


def space_kernel(rows_ref, cols_ref, half1_ref, half2_ref, tokens_ref, first_t_ref, wide_ref, middle_ref, normed_ref):
    feature = tokens_ref.shape[1]
    flat = lambda ref: ref[...].reshape(-1, feature)
    spatial = turn(first_t_ref, jnp.concatenate([flat(half1_ref), flat(half2_ref)], axis=0))
    inputs = tokens_ref[...].astype(F32)
    live = live_rows(pl.program_id(0) * CELLS, CELLS, rows_ref, cols_ref)
    normal, _ = normalize(inputs)
    middle = inputs + live * (spatial + (normal * wide_ref[0:1, :] + wide_ref[1:2, :]))
    middle_ref[...] = middle
    normal, _ = normalize(middle)
    normed_ref[...] = (normal * wide_ref[2:3, :] + wide_ref[3:4, :]).astype(BF)


def column_block(rows, width):
    return pl.BlockSpec((rows, 2 * GROUP, width), lambda i: (0, i, 0))


def space(rows, cols, half1, half2, tokens, wide, tables, deps=()):
    cells, feature = tokens.shape
    table = tables["first_t"]
    block = pl.BlockSpec((CELLS, feature), lambda i: (i, 0))
    return launch(
        deps,
        space_kernel,
        grid=(STEPS,),
        out_shape=(jax.ShapeDtypeStruct((cells, feature), F32), jax.ShapeDtypeStruct((cells, feature), BF)),
        in_specs=[smem(), smem(), column_block(half1.shape[0], feature), column_block(half2.shape[0], feature),
                  block, single(table.shape), single(wide.shape)],
        out_specs=(block, block),
        compiler_params=params(),
        cost_estimate=cost(6e9, 20e6),
        name="space",
    )(rows, cols, half1, half2, tokens, table, wide)


def fetch_weights(me_ref, pieces, places, up_ref, down_ref, sems):
    each = pieces[0].shape[0]
    held = len(pieces) // 2
    count = each * held
    chip = me_ref[0] // 2

    def copies(own, core):
        target = (up_ref, down_ref)[core]
        source = pieces[:held] if own else pieces[held:]
        for mask in range(count):
            at = places[core][mask]
            part = source[at // each].at[at % each]
            yield pltpu.make_async_copy(part, target.at[chip ^ mask], sems.at[core, mask])

    for core in range(2):
        @pl.when(me_ref[0] % 2 == core)
        def _():
            for copy in copies(True, core):
                copy.start()
            for copy in copies(False, 1 - core):
                copy.start()

    def arrived(core):
        for copy in copies(True, core):
            copy.wait()

    return arrived


def weight_scratch(pieces):
    chips, rows, feature = UNITS, pieces[0].shape[1], pieces[0].shape[2]
    return [
        pltpu.VMEM((chips, rows, feature), BF),
        pltpu.VMEM((chips, rows, feature), BF),
        pltpu.SemaphoreType.DMA((2, chips)),
    ]


def up_part(up_ref, j, feature):
    share = up_ref.shape[1] * feature // (up_ref.shape[0] * up_ref.shape[1])
    return up_ref[:, j * share : (j + 1) * share, :].reshape(feature, feature)


def down_part(down_ref, j, feature):
    share = down_ref.shape[1]
    each = feature // share
    return down_ref[j * each : (j + 1) * each].reshape(feature, feature)


def up_kernel(places, rows_ref, cols_ref, me_ref, normed_ref, grad_ref, bias_ref, *rest):
    pieces = rest[:-10]
    active_ref, pre_ref, live_ref, bias_grad_ref, up_all_ref, down_all_ref, up_ref, down_ref, sems, out_sems = rest[-10:]
    tile, feature = normed_ref.shape
    step = pl.program_id(0)
    copies = [
        pltpu.make_async_copy(source, target, out_sems.at[k])
        for k, (source, target) in enumerate(((up_ref, up_all_ref), (down_ref, down_all_ref)))
    ]

    def work(arrived):
        live = live_rows(step * tile, tile, rows_ref, cols_ref)
        branch = (grad_ref[...].astype(F32) * live).astype(BF)
        live_ref[...] = branch
        normed = normed_ref[...]
        if arrived:
            arrived(0)
            copies[0].start()
        for j in range(active_ref.shape[1] // feature):
            place = slice(j * feature, (j + 1) * feature)
            value = mm(normed, up_part(up_ref, j, feature)) + bias_ref[:, place]
            if arrived and j == 0:
                arrived(1)
                copies[1].start()
            grad = mm(branch, down_part(down_ref, j, feature), (1, 1))
            active, slope = gelu_parts(value)
            active_ref[:, place] = active.astype(BF)
            low = (grad * slope).astype(BF)
            pre_ref[:, place] = low
            bias_grad_ref[:, place] += jnp.sum(low.astype(F32), axis=0, keepdims=True)

    @pl.when(step == 0)
    def _():
        bias_grad_ref[...] = jnp.zeros_like(bias_grad_ref)
        work(fetch_weights(me_ref, pieces, places, up_ref, down_ref, sems))

    @pl.when(step > 0)
    def _():
        work(None)

    @pl.when(step == pl.num_programs(0) - 1)
    def _():
        for copy in copies:
            copy.wait()


def feed_up(rows, cols, me, normed, grad, bias, pieces, places, tile=256, deps=()):
    cells, feature = normed.shape
    hidden = bias.shape[1]
    block = lambda width: pl.BlockSpec((tile, width), lambda i: (i, 0))
    weights = jax.ShapeDtypeStruct((UNITS,) + pieces[0].shape[1:], BF)
    return launch(
        deps,
        functools.partial(up_kernel, places),
        grid=(cells // tile,),
        out_shape=(
            jax.ShapeDtypeStruct((cells, hidden), BF),
            jax.ShapeDtypeStruct((cells, hidden), BF),
            jax.ShapeDtypeStruct((cells, feature), BF),
            jax.ShapeDtypeStruct((1, hidden), F32),
            weights,
            weights,
        ),
        in_specs=[smem(), smem(), smem(), block(feature), block(feature), single(bias.shape)]
        + [any_space() for _ in pieces],
        out_specs=(block(hidden), block(hidden), block(feature), single((1, hidden)), any_space(), any_space()),
        scratch_shapes=weight_scratch(pieces) + [pltpu.SemaphoreType.DMA((2,))],
        compiler_params=params(),
        cost_estimate=cost(0, 0),
        name="feed_up",
    )(rows, cols, me, normed, grad, bias, *pieces)


def weight_grad_kernel(places, me_ref, active_ref, pre_ref, branch_ref, normed_ref, send_ref, keep_ref, stage_ref, sems):
    step = pl.program_id(0)
    steps = pl.num_programs(0) // 2
    feature = branch_ref.shape[1]
    chips, rows, _ = send_ref.shape
    each = feature // rows
    share = feature // chips

    def down_copies(j, target):
        for c in range(each):
            source = stage_ref.at[j, pl.ds(c * rows, rows)]
            yield pltpu.make_async_copy(source, target.at[places[1][j * each + c]], sems.at[j, c])

    def up_copies(j, target):
        for c in range(chips):
            source = stage_ref.at[steps + j, pl.ds(c * share, share)]
            there = target.at[places[0][c], pl.ds(j * share, share)]
            yield pltpu.make_async_copy(source, there, sems.at[steps + j, c])

    @pl.when(step < steps)
    def _():
        stage_ref[step] = mm(active_ref[...], branch_ref[...], (0, 0)).astype(BF)

    @pl.when(step >= steps)
    def _():
        stage_ref[step] = mm(normed_ref[...], pre_ref[...], (0, 0)).astype(BF)

    total = stage_ref.shape[0] // 2
    for j in range(total):
        for core in range(2):
            targets = (send_ref, keep_ref) if core == 0 else (keep_ref, send_ref)

            @pl.when((step == j) & (me_ref[0] % 2 == core))
            def _():
                for copy in down_copies(j, targets[0]):
                    copy.start()

            @pl.when((step == total + j) & (me_ref[0] % 2 == core))
            def _():
                for copy in up_copies(j, targets[1]):
                    copy.start()

    @pl.when(step == 2 * steps - 1)
    def _():
        for j in range(total):
            for copy in down_copies(j, send_ref):
                copy.wait()
            for copy in up_copies(j, send_ref):
                copy.wait()


def weight_grads(me, active, pre, branch, normed, places, deps=()):
    cells, hidden = active.shape
    feature = branch.shape[1]
    tiles = hidden // feature
    chips = UNITS
    shape = jax.ShapeDtypeStruct((chips, hidden // chips, feature), BF)
    return launch(
        deps,
        functools.partial(weight_grad_kernel, places),
        grid=(2 * tiles,),
        out_shape=(shape, shape),
        in_specs=[
            smem(),
            pl.BlockSpec((cells, feature), lambda i: (0, jnp.minimum(i, tiles - 1))),
            pl.BlockSpec((cells, feature), lambda i: (0, jnp.maximum(i - tiles, 0))),
            single(branch.shape), single(normed.shape),
        ],
        out_specs=(any_space(), any_space()),
        scratch_shapes=[
            pltpu.VMEM((2 * tiles, feature, feature), BF),
            pltpu.SemaphoreType.DMA((2 * tiles, chips)),
        ],
        compiler_params=params(),
        cost_estimate=cost(4 * cells * feature * hidden, 40e6),
        name="weight_grads",
    )(me, active, pre, branch, normed)


def down_kernel(rows_ref, cols_ref, active_ref, pre_ref, middle_ref, grad_ref, normal_ref, wide_ref, first_ref,
                up_ref, down_ref, mixed_ref, grad_middle_ref, half_ref, sums_ref):
    tile, feature = middle_ref.shape
    hidden = active_ref.shape[1]
    step = pl.program_id(0)

    @pl.when(step == 0)
    def _():
        sums_ref[...] = jnp.zeros_like(sums_ref)

    live = live_rows(step * tile, tile, rows_ref, cols_ref)
    branch = mm(active_ref[...], down_ref[...].reshape(hidden, feature))
    grad_normed = jnp.zeros((tile, feature), F32)
    for j in range(hidden // feature):
        pre = pre_ref[:, j * feature : (j + 1) * feature]
        grad_normed = grad_normed + mm(pre, up_part(up_ref, j, feature), (1, 1))
    middle = middle_ref[...]
    mixed_ref[...] = (middle + live * (branch + wide_ref[4:5, :])).astype(BF)
    normal, inverse = normalize(middle)
    cotangent = grad_ref[...].astype(F32)
    grad_middle = cotangent + norm_back(grad_normed, wide_ref[2:3, :], normal, inverse)
    grad_middle_ref[...] = grad_middle
    masked = grad_middle * live
    half_ref[...] = turn(first_ref, masked).reshape(half_ref.shape)
    rows = (grad_normed * normal, grad_normed, cotangent * live, masked * normal_ref[...].astype(F32), masked)
    for row, value in enumerate(rows):
        sums_ref[row : row + 1, :] += jnp.sum(value, axis=0, keepdims=True)


def feed_down(rows, cols, active, pre, middle, grad, normal, wide, table, up, down, deps=()):
    cells, feature = middle.shape
    hidden = active.shape[1]
    block = lambda width: pl.BlockSpec((CELLS, width), lambda i: (i, 0))
    operands = (rows, cols, active, pre, middle, grad, normal, wide, table, up, down)
    return launch(
        deps,
        down_kernel,
        grid=(cells // CELLS,),
        out_shape=(
            jax.ShapeDtypeStruct((cells, feature), BF),
            jax.ShapeDtypeStruct((cells, feature), F32),
            jax.ShapeDtypeStruct((KEPT, 2 * ROWS, feature), F32),
            jax.ShapeDtypeStruct((8, feature), F32),
        ),
        in_specs=[smem(), smem(), block(hidden), block(hidden), block(feature), block(feature), block(feature)]
        + [single(v.shape) for v in operands[7:]],
        out_specs=(block(feature), block(feature), column_block(KEPT, feature), single((8, feature))),
        compiler_params=params(),
        cost_estimate=cost(0, 0),
        name="feed_down",
    )(*operands)


def back_step(half_ref, head_ref, body_ref, back_head_ref, back_body_ref, mix1_ref, mix2_ref, ins, in_heads,
              outs, out_heads, out_ref, sums_ref, is_head):
    feature = out_ref.shape[2]

    def read(k):
        if is_head:
            return jnp.concatenate([ins[k][...], in_heads[k][...]], axis=0)
        return ins[k][...]

    grads = to_modes(half_ref, head_ref, body_ref, is_head)
    grad_two = (to_mixed(*grads) * read(1)).astype(BF)
    grad_one = (mix_product(grad_two, mix2_ref, True) * read(0)).astype(BF)
    grad_spec = mix_product(grad_one, mix1_ref, True)
    from_modes(from_mixed(grad_spec), back_head_ref, back_body_ref, is_head, out_ref)
    for row, value in enumerate((grad_one, grad_two)):
        outs[row][...] = value[:TOOK]
        if is_head:
            out_heads[row][...] = value[TOOK:]
    flat = jnp.concatenate([read(3)] * (feature // LANES), axis=1)
    for row, value in enumerate((grad_one.astype(F32), grad_two.astype(F32), grad_spec * read(2).astype(F32), grad_spec * flat)):
        total = jnp.sum(value, axis=0, keepdims=True)
        sums_ref[row : row + 1, :] = total if is_head else sums_ref[row : row + 1, :] + total


def mix_back_kernel(
    half_ref, slope1_ref, slope2_ref, bend1_ref, bend2_ref, low1_ref, low2_ref, flat1_ref, flat2_ref,
    slope_head_ref, bend_head_ref, low_head_ref, flat_head_ref, mix1_ref, mix2_ref,
    head_ref, body_ref, back_head_ref, back_body_ref,
    out_ref, one_ref, two_ref, one_head_ref, two_head_ref, sums_ref,
):
    step = pl.program_id(0)
    steps = pl.num_programs(0) // 2
    work = functools.partial(
        back_step, half_ref, head_ref, body_ref, back_head_ref, back_body_ref, mix1_ref, mix2_ref
    )
    heads = (slope_head_ref, bend_head_ref, low_head_ref, flat_head_ref)
    more = (heads, (one_ref, two_ref), (one_head_ref, two_head_ref), out_ref, sums_ref)
    near = (slope1_ref, bend1_ref, low1_ref, flat1_ref)
    far = (slope2_ref, bend2_ref, low2_ref, flat2_ref)

    @pl.when(step == 0)
    def _():
        sums_ref[...] = jnp.zeros_like(sums_ref)
        work(near, *more, True)

    @pl.when((step > 0) & (step < steps))
    def _():
        work(near, *more, False)

    @pl.when(step >= steps)
    def _():
        work(far, *more, False)


def mix_back(half, modes1, modes2, heads, mix1, mix2, tables, deps=()):
    feature = half.shape[2]
    steps = KEPT // GROUP // TAKE
    fixed = tuple(heads[k] for k in (2, 3, 0, 4)) + (
        mix1, mix2, tables["head_w"], tables["body_w"], tables["head_t"], tables["body_t"]
    )
    moving = []
    specs = []
    for k in (2, 3, 0, 4):
        width = modes1[k].shape[1]
        moving += [modes1[k], modes2[k]]
        specs += [
            pl.BlockSpec((TOOK, width), lambda i: (jnp.minimum(i, steps // 2 - 1), 0)),
            pl.BlockSpec((TOOK, width), lambda i: (jnp.maximum(i - steps // 2, 0), 0)),
        ]
    low = lambda rows: jax.ShapeDtypeStruct((rows, 2 * feature), BF)
    body = pl.BlockSpec((TOOK, 2 * feature), lambda i: (i, 0))
    shapes = (
        jax.ShapeDtypeStruct((KEPT, 2 * ROWS, feature), F32), low(TOOK * steps), low(TOOK * steps),
        low(ROWS), low(ROWS), jax.ShapeDtypeStruct((8, 2 * feature), F32),
    )
    return launch(
        deps,
        mix_back_kernel,
        grid=(steps,),
        out_shape=shapes,
        in_specs=[half_block(feature)] + specs + [single(v.shape) for v in fixed],
        out_specs=[half_block(feature), body, body] + [single(v.shape) for v in shapes[3:]],
        compiler_params=params(),
        cost_estimate=cost(18e9, 30e6),
        name="mix_back",
    )(half, *moving, *fixed)


def block_kernel(left1_ref, left2_ref, left_head_ref, right_ref, right_head_ref, out_ref, natural_ref):
    wide = 2 * LANES
    count = left1_ref.shape[1] // wide
    cut = left1_ref.shape[0]
    for t in range(count):
        for c in range(max(t - 1, 0), min(t + 2, count)):
            left, right = slice(t * wide, (t + 1) * wide), slice(c * wide, (c + 1) * wide)
            total = (
                mm(left1_ref[:, left], right_ref[:cut, right], (0, 0))
                + mm(left2_ref[:, left], right_ref[cut:, right], (0, 0))
                + mm(left_head_ref[:, left], right_head_ref[:, right], (0, 0))
            )
            rows, lanes = slice(t * LANES, (t + 1) * LANES), slice(c * LANES, (c + 1) * LANES)
            natural_ref[0, rows, lanes] = total[:LANES, :LANES] + total[LANES:, LANES:]
            natural_ref[1, rows, lanes] = total[:LANES, LANES:] - total[LANES:, :LANES]
    per_group = BLOCKS // 2
    block = count * LANES // per_group
    for b in range(per_group):
        begin = b * block
        base = begin // LANES * LANES
        reach = min(base + wide, count * LANES) - base
        for part in range(2):
            piece = natural_ref[part, begin : begin + block, base : base + reach]
            if begin > base:
                piece = pltpu.roll(piece, reach - (begin - base), axis=1)
            out_ref[part, b * block : (b + 1) * block, :] = piece[:, :LANES]


def block_grads(left1, left2, left_head, right, right_head, name, deps=()):
    feature = left1.shape[1] // 2
    half = feature // 2
    block = lambda v: pl.BlockSpec((v.shape[0], feature), lambda i: (0, i))
    return launch(
        deps,
        block_kernel,
        grid=(2,),
        out_shape=jax.ShapeDtypeStruct((2, feature, LANES), F32),
        in_specs=[block(v) for v in (left1, left2, left_head, right, right_head)],
        out_specs=pl.BlockSpec((2, half, LANES), lambda i: (0, i, 0)),
        scratch_shapes=[pltpu.VMEM((2, half, half), F32)],
        compiler_params=params(),
        cost_estimate=cost(5e9, 7e6),
        name=name,
    )(left1, left2, left_head, right, right_head)


def last_kernel(begin, rows_ref, cols_ref, half_ref, tokens_ref, grad_ref, first_t_ref, wide_ref, *rest):
    out_ref = rest[-1]
    tile, feature = tokens_ref.shape
    live = live_rows((pl.program_id(0) + begin) * tile, tile, rows_ref, cols_ref)
    grad_middle = grad_ref[...]
    grad_normed = live * (grad_middle + turn(first_t_ref, half_ref[...].reshape(CELLS, feature)))
    normal, inverse = normalize(tokens_ref[...].astype(F32))
    out_ref[...] = grad_middle + norm_back(grad_normed, wide_ref[0:1, :], normal, inverse)


def last(rows, cols, half, tokens, grad, wide, tables, begin, steps, before=(), deps=()):
    cells, feature = tokens.shape
    first_t = tables["first_t"]
    block = pl.BlockSpec((CELLS, feature), lambda i: (i + begin, 0))
    operands = (rows, cols, half, tokens, grad, first_t, wide)
    return launch(
        deps,
        functools.partial(last_kernel, begin),
        grid=(steps,),
        out_shape=jax.ShapeDtypeStruct((cells, feature), F32),
        in_specs=[smem(), smem(), pl.BlockSpec((KEPT, 2 * GROUP, feature), lambda i: (0, i + begin, 0)), block, block,
                  single(first_t.shape), single(wide.shape)] + [any_space() for _ in before],
        out_specs=block,
        input_output_aliases={len(operands): 0} if before else {},
        compiler_params=params(),
        cost_estimate=cost(6e9, 20e6),
        name="last",
    )(*operands, *before)


def collect(value, per_device, devices):
    total = value.shape[1]
    owner = lax.broadcasted_iota(jnp.int32, (devices, total), 1) // per_device
    row = lax.broadcasted_iota(jnp.int32, (devices, total), 0)
    high, low = split(jnp.where(owner == row, jnp.broadcast_to(value, (devices, total)), 0.0))
    place = lax.broadcasted_iota(jnp.int32, (total, LANES), 0)
    lane = lax.broadcasted_iota(jnp.int32, (total, LANES), 1)
    pick = jnp.where(place % per_device == lane, 1.0, 0.0).astype(BF)
    return mm(high, pick) + mm(low, pick)


def emit(upper_ref, sum_ref, send_ref, keep_ref):
    rows = sum_ref.shape[2] - 8
    half = sum_ref.shape[0]
    away = sum_ref[:, pl.ds(1 - upper_ref[0], 1)].reshape(half, rows + 8, LANES)
    high, low = split(away[:, rows:])
    send_ref[:, :rows] = away[:, :rows].astype(BF)
    send_ref[:, rows:] = jnp.concatenate([high.astype(F32), low.astype(F32)], axis=1).astype(BF)
    keep_ref[...] = sum_ref[:, pl.ds(upper_ref[0], 1)].reshape(half, rows + 8, LANES)


def pack_kernel(upper_ref, one_ref, two_ref, mixed_ref, sums_ref, up_ref, wide_ref, send_ref, keep_ref, sum_ref):
    half, _, rows, _ = sum_ref.shape
    devices = 2 * half
    share = (rows - 8) // 4
    feature = sums_ref.shape[1]
    sum_ref[:, :, : 2 * share] = one_ref[...].reshape(half, 2, 2 * share, LANES)
    sum_ref[:, :, 2 * share : 4 * share] = two_ref[...].reshape(half, 2, 2 * share, LANES)
    first_gain, first_bias = scale_grads(mixed_ref, sums_ref, wide_ref)
    natural = [jnp.concatenate(from_mixed(mixed_ref[k : k + 1, :]), axis=1) for k in range(2)]
    narrow = [first_gain, first_bias] + [sums_ref[k : k + 1, :] for k in range(3)]
    for k, value in enumerate(narrow + natural + [up_ref[...]]):
        placed = collect(value, value.shape[1] // devices, devices)
        for d in range(devices):
            sum_ref[d // 2, d % 2, 4 * share + k : 4 * share + k + 1, :] = placed[d : d + 1, :]
    emit(upper_ref, sum_ref, send_ref, keep_ref)


def scale_grads(mixed_ref, sums_ref, wide_ref):
    real, imag = from_mixed(mixed_ref[2:3, :])
    scaled = real + imag
    real, imag = from_mixed(mixed_ref[3:4, :])
    flat = real + imag
    gain = sums_ref[3:4, :] + (scaled - wide_ref[1:2, :] * flat) / wide_ref[0:1, :]
    return gain, sums_ref[4:5, :] + flat


def small_shapes(half, rows):
    return (
        jax.ShapeDtypeStruct((half, rows + 8, LANES), BF),
        jax.ShapeDtypeStruct((half, rows, LANES), F32),
    )


def pack(upper, one, two, mixed, sums, up, wide, devices):
    rows = 2 * one.shape[0] * one.shape[1] // devices + 8
    shapes = small_shapes(devices // 2, rows)
    operands = (one, two, mixed, sums, up, wide)
    return pl.pallas_call(
        pack_kernel,
        out_shape=shapes,
        in_specs=[smem()] + vmem(len(operands)),
        out_specs=vmem(2),
        scratch_shapes=[pltpu.VMEM((devices // 2, 2, rows, LANES), F32)],
        compiler_params=params(),
        cost_estimate=cost(0, 0),
        name="pack",
    )(upper, *operands)


def merge_small(keep_ref, got_ref):
    rows = keep_ref.shape[1] - 8
    tail = got_ref[:, rows:].astype(F32)
    return (
        keep_ref[:, :rows] + got_ref[:, :rows].astype(F32),
        keep_ref[:, rows:] + tail[:, :8] + tail[:, 8:],
    )


def fold_small_kernel(upper_ref, keep_ref, got_ref, send_ref, out_ref, sum_ref):
    half, _, rows, _ = sum_ref.shape
    top, tail = merge_small(keep_ref, got_ref)
    sum_ref[:, :, : rows - 8] = top.reshape(half, 2, rows - 8, LANES)
    sum_ref[:, :, rows - 8 :] = tail.reshape(half, 2, 8, LANES)
    emit(upper_ref, sum_ref, send_ref, out_ref)


def fold_small(keep, got, upper, deps=()):
    half, rows = keep.shape[0] // 2, keep.shape[1]
    return launch(
        deps,
        fold_small_kernel,
        out_shape=small_shapes(half, rows),
        in_specs=[smem()] + vmem(2),
        out_specs=vmem(2),
        scratch_shapes=[pltpu.VMEM((half, 2, rows, LANES), F32)],
        compiler_params=params(),
        cost_estimate=cost(0, 0),
        name="fold_small",
    )(upper, keep, got)


def vmem(count):
    return [pl.BlockSpec(memory_space=pltpu.VMEM)] * count


def end_small_kernel(keep_ref, got_ref, one_ref, two_ref, *rows_refs):
    top, tail = merge_small(keep_ref, got_ref)
    share, block = one_ref.shape
    one_ref[...] = top[0, :share, :block]
    two_ref[...] = top[0, share:, :block]
    for row, ref in enumerate(rows_refs):
        ref[...] = tail[0, row : row + 1, : ref.shape[1]]


def end_small(keep, got, share, block, widths):
    shapes = [jax.ShapeDtypeStruct((share, block), F32)] * 2
    shapes += [jax.ShapeDtypeStruct((1, width), F32) for width in widths]
    return pl.pallas_call(
        end_small_kernel,
        out_shape=shapes,
        in_specs=vmem(2),
        out_specs=vmem(len(shapes)),
        compiler_params=params(),
        cost_estimate=cost(0, 0),
        name="end_small",
    )(keep, got)


def begin_small_kernel(one_ref, two_ref, *rest):
    out_ref, rows_ref = rest[-2:]
    share, block = one_ref.shape
    out_ref[...] = jnp.zeros_like(out_ref)
    rows_ref[...] = jnp.zeros_like(rows_ref)
    out_ref[0, :share, :block] = one_ref[...]
    out_ref[0, share : 2 * share, :block] = two_ref[...]
    for row, ref in enumerate(rest[:-2]):
        rows_ref[row : row + 1, : ref.shape[1]] = ref[...].astype(F32)
    out_ref[0, 2 * share :, :] = rows_ref[...].astype(BF)


def begin_small(one, two, vectors):
    share = one.shape[0]
    operands = (one, two) + tuple(v[None] for v in vectors)
    return pl.pallas_call(
        begin_small_kernel,
        out_shape=jax.ShapeDtypeStruct((1, 2 * share + 16, LANES), BF),
        in_specs=vmem(len(operands)),
        out_specs=vmem(1)[0],
        scratch_shapes=[pltpu.VMEM((16, LANES), F32)],
        compiler_params=params(),
        cost_estimate=cost(0, 0),
        name="begin_small",
    )(*operands)


AXES = ("dp", "fsdp")


def swap(value, devices, bits):
    return lax.ppermute(value, AXES, [(i, i ^ (1 << bits[i & 1])) for i in range(devices)])


def doubling_orders(count):
    first = list(range(count - 1, 0, -1))
    second = list(first)
    for k in range(0, len(second) - 1, 2):
        second[k], second[k + 1] = second[k + 1], second[k]
    return first, second


def places_of(order):
    return [
        sum(1 << k for k, bit in enumerate(order) if mask >> (bit - 1) & 1) for mask in range(1 << len(order))
    ]


def pair_kernel(held_ref, got_ref, out_ref):
    count = held_ref.shape[0]
    out_ref[:count] = held_ref[...]
    out_ref[count:] = got_ref[...]


def pair(held, got, deps=()):
    shape = jax.ShapeDtypeStruct((2 * held.shape[0],) + held.shape[1:], held.dtype)
    return launch(
        deps,
        pair_kernel,
        out_shape=shape,
        in_specs=[pl.BlockSpec(memory_space=pltpu.VMEM)] * 2,
        out_specs=pl.BlockSpec(memory_space=pltpu.VMEM),
        compiler_params=params(),
        cost_estimate=cost(0, 4 * held.size * 2),
        name="pair",
    )(held, got)


def hold(value, deps):
    def body(*refs):
        pass

    return pl.pallas_call(
        body,
        out_shape=jax.ShapeDtypeStruct(value.shape, value.dtype),
        in_specs=[any_space() for _ in range(1 + len(deps))],
        out_specs=any_space(),
        input_output_aliases={0: 0},
        compiler_params=params(),
        cost_estimate=cost(0, 0),
        name="hold",
    )(value, *deps)


def gather_small(value, me, devices, count):
    held = value[None]
    for bit in list(range(3, count)) + [2, 1, 0]:
        other = swap(held, devices, (bit, bit))
        upper = (me >> bit) & 1
        axis = 0 if bit > 2 else 1
        join_two = lambda a, b: jnp.stack([a, b], axis=axis).reshape((-1,) + value.shape)
        held = jnp.where(upper == 0, join_two(held, other), join_two(other, held))
    return held


def scatter_small(value, me, devices, count, exact):
    shape = value.shape[1:]
    rows = shape[0]
    total = value
    for bit in [0, 1, 2] + list(range(count - 1, 2, -1)):
        upper = (me >> bit) & 1
        axis = 0 if bit > 2 else 1
        pair = total.reshape(((2, -1) if bit > 2 else (-1, 2)) + shape)
        away = lax.dynamic_index_in_dim(pair, 1 - upper, axis, keepdims=False)
        keep = lax.dynamic_index_in_dim(pair, upper, axis, keepdims=False)
        sums = away[:, rows - exact :]
        top = lax.reduce_precision(sums, 8, 7)
        packet = jnp.concatenate([away[:, : rows - exact], top, sums - top], axis=1).astype(BF)
        got = swap(packet, devices, (bit, bit)).astype(F32)
        low = got[:, rows - exact : rows] + got[:, rows:]
        total = keep + jnp.concatenate([got[:, : rows - exact], low], axis=1)
    return total[0]


def chip_unit(up, down, core, devices):
    parts, share, feature = up.shape
    flat = up.reshape(parts * share, feature)
    other = swap(jnp.where(core == 0, down, flat), devices, (0, 0))
    up_unit = jnp.concatenate([up, other.reshape(up.shape)], axis=1).reshape(2 * parts * share, feature)
    return jnp.where(core == 0, up_unit, jnp.concatenate([other, down]))[None]


def fold_kernel(upper_ref, keep_away_ref, got_away_ref, keep_own_ref, got_own_ref, send_ref, keep_ref):
    send_ref[...] = (keep_away_ref[...].astype(F32) + got_away_ref[...].astype(F32)).astype(BF)
    keep_ref[...] = (keep_own_ref[...].astype(F32) + got_own_ref[...].astype(F32)).astype(BF)


def fold(keep, got, upper, deps=()):
    half = keep.shape[0] // 2
    each = min(2, half)
    unit = (each,) + keep.shape[1:]
    count = len(deps)
    away = pl.BlockSpec(unit, lambda i, up: ((1 - up[0]) * (half // each) + i, 0, 0))
    own = pl.BlockSpec(unit, lambda i, up: (up[0] * (half // each) + i, 0, 0))
    out = pl.BlockSpec(unit, lambda i, up: (i, 0, 0))
    shape = jax.ShapeDtypeStruct((half,) + keep.shape[1:], BF)

    def body(*refs):
        fold_kernel(*refs[:5], *refs[5 + count :])

    return pl.pallas_call(
        body,
        grid_spec=pltpu.PrefetchScalarGridSpec(
            num_scalar_prefetch=1,
            grid=(half // each,),
            in_specs=[away, away, own, own] + [any_space() for _ in deps],
            out_specs=[out, out],
        ),
        out_shape=(shape, shape),
        compiler_params=params(),
        cost_estimate=cost(0, 6 * half * keep[0].size),
        name="fold",
    )(upper, keep, got, keep, got, *deps)


def on_device(
    tokens, grad_out, region_rows, region_cols, ln1_gain, ln1_bias, spec_w1, spec_b1, spec_w2, spec_b2,
    ln2_gain, ln2_bias, w_up, up_bias, w_down, down_bias,
):
    devices = lax.axis_size(AXES[0]) * lax.axis_size(AXES[1])
    count = devices.bit_length() - 1
    me = lax.axis_index(AXES).astype(jnp.int32)
    core = me & 1
    me_one = me.reshape(1)
    feature = tokens.shape[-1]
    block = feature // BLOCKS
    share = ln1_gain.shape[0]
    cells = tokens.shape[1] * tokens.shape[2]
    hidden = w_up.shape[1]
    parts = hidden // feature
    tables = {name: jnp.asarray(value) for name, value in wave_matrices().items()}
    orders = doubling_orders(count)
    places = tuple(places_of(order) for order in orders)
    flat_tokens = tokens.reshape(cells, feature)
    flat_grad = grad_out.reshape(cells, feature)
    fast = devices // 2 == UNITS
    step = lambda value, k: swap(value, devices, (orders[0][k], orders[1][k]))

    padded = lambda v: jnp.pad(v, ((0, 0), (0, LANES - v.shape[1])))
    vectors = (spec_b1, spec_b2, ln1_gain, ln1_bias, ln2_gain, ln2_bias, up_bias, down_bias)
    if fast:
        own_up = w_up.reshape(share, parts, feature).transpose(1, 0, 2)
        unit = chip_unit(own_up, w_down, core, devices)
        bits = tuple(range(3, count)) + (2, 1, 0)
        meet = lambda value, bit: swap(value, devices, (bit, bit))
        small = begin_small(spec_w1, spec_w2, vectors)
        half, normal = first(region_rows, region_cols, flat_tokens, tables, deps=(unit, small))
        small = pair(small, meet(small, bits[0]), deps=(half,))
        small = pair(small, meet(small, bits[1]))
        near = pair(unit, step(unit, 0), deps=(small,))
        small = pair(small, meet(small, bits[2]), deps=(near,))
        for k in range(3, count - 1):
            small = pair(small, meet(small, bits[k]))
        near = pair(near, step(near, 1), deps=(small,))
        small = pair(small, meet(small, bits[count - 1]), deps=(near,))
        beside, across = step(near, 2), step(near, 3)
        weights, weight_bits, vector_bits, me_small = small, bits, bits, me_one
        vectors = small[:, 4 * share : 4 * share + 8].transpose(1, 0, 2).astype(F32)
    else:
        up = lax.all_gather(w_up, AXES, axis=0, tiled=True)
        up = up.reshape(UNITS, feature // UNITS, parts, feature).transpose(0, 2, 1, 3).reshape(UNITS, -1, feature)
        down = lax.all_gather(w_down, AXES, axis=0, tiled=True).reshape(UNITS, -1, feature)
        pieces = tuple(
            jnp.where(core == 0, one, two)[begin : begin + UNITS // 2]
            for one, two in ((up, down), (down, up))
            for begin in (0, UNITS // 2)
        )
        me_one = core.reshape(1)
        me_small = jnp.zeros_like(me_one)
        places = (tuple(range(UNITS)),) * 2
        small = jnp.concatenate([padded(spec_w1), padded(spec_w2)] + [padded(v[None]) for v in vectors])
        small = gather_small(small, me, devices, count)
        weights = small[:, : 4 * share].reshape(devices, 2, 2 * share, LANES).transpose(1, 0, 2, 3)
        weights = weights.reshape(2, 2 * UNITS, -1, LANES).transpose(1, 0, 2, 3).reshape(2 * UNITS, -1, LANES)
        weight_bits, vector_bits = tuple(range(5)), tuple(range(count))
        half, normal = first(region_rows, region_cols, flat_tokens, tables)
        vectors = small[:, 4 * share :].transpose(1, 0, 2).astype(F32)

    steps = KEPT // GROUP // TAKE
    core_swap = lambda value: swap(value, devices, (0, 0))
    made = mix_first(
        me_small, half, weights, vectors, tables, hidden, steps // 2, weight_bits, vector_bits,
        deps=(near,) if fast else (),
    )
    half1, modes1, heads, (mix1, mix2, wide, long, up_shift) = made[0], made[1:6], made[6:11], made[11:]
    deps = ()
    if fast:
        beside = hold(beside, (half1,))
        other_near = core_swap(near)
        deps = (beside, other_near)
    made = mix_second(half, mix1, mix2, wide, long, tables, steps // 2, steps // 2, deps=deps)
    half2, modes2 = made[0], made[1:6]
    if fast:
        far = step(beside, 3)
        across = hold(across, (half2,))
        other_beside = core_swap(beside)
        deps = (across, other_beside)
    middle, normed = space(region_rows, region_cols, half1, half2, flat_tokens, wide, tables, deps=deps)
    if fast:
        far = hold(far, (normed,))
        pieces = (near, beside, across, far, other_near, other_beside, core_swap(across), core_swap(far))
    active, pre, branch, bias_grad, up_all, down_all = feed_up(
        region_rows, region_cols, me_one, normed, flat_grad, up_shift, pieces, places
    )
    send, keep = weight_grads(me_one, active, pre, branch, normed, places)
    tiles = cells // CELLS
    mixed, grad_middle, half_back, sums_two = feed_down(
        region_rows, region_cols, active, pre, middle, flat_grad, normal, wide, tables["first"], up_all, down_all,
        deps=(send,),
    )
    deps = ()
    if fast:
        ranks = [((me >> jnp.where(core == 0, *bit)) & 1).reshape(1) for bit in zip(*orders)]
        send, keep = fold(keep, swap(send, devices, (0, 0)), ranks[3], deps=(sums_two,))
        deps = (send,)
    half_back, one, two, one_head, two_head, bias_sums = mix_back(
        half_back, modes1, modes2, heads, mix1, mix2, tables, deps=deps
    )
    if fast:
        send, keep = fold(keep, step(send, 3), ranks[2], deps=(bias_sums,))
        deps = (send,)
    grad_two = block_grads(modes1[1], modes2[1], heads[1], two, two_head, "grad_mix2", deps=deps)
    grad_one = block_grads(modes1[0], modes2[0], heads[0], one, one_head, "grad_mix1", deps=deps)
    last_args = (region_rows, region_cols, half_back, flat_tokens, grad_middle, wide, tables)
    if fast:
        uppers = [((me >> bit) & 1).reshape(1) for bit in range(count)]
        away, own = pack(uppers[0], grad_one, grad_two, bias_sums, sums_two, bias_grad, wide, devices)
        send, keep = fold(keep, step(send, 2), ranks[1], deps=(away,))
        grad_tokens = last(*last_args, 0, 2, deps=(send, away))
        away, own = fold_small(own, meet(away, 0), uppers[1], deps=(grad_tokens,))
        grad_tokens = last(*last_args, 2, 2, (grad_tokens,), deps=(away,))
        send, keep = fold(keep, step(send, 1), ranks[0], deps=(grad_tokens,))
        away, own = fold_small(own, meet(away, 1), uppers[2], deps=(send,))
        grad_tokens = last(*last_args, 4, 2, (grad_tokens,), deps=(away,))
        keep = hold(keep, (grad_tokens,))
        total = keep[0].astype(F32) + step(send, 0)[0].astype(F32)
        up_sum = total.reshape(parts, 2 * share, feature)
        lower = up_sum[:, :share].reshape(parts * share, feature)
        upper = up_sum[:, share:].reshape(parts * share, feature)
        each = parts * share
        other = swap(jnp.where(core == 0, upper, total[:each]), devices, (0, 0))
        grad_w_up = jnp.where(core == 0, lower, other).reshape(parts, share, feature).transpose(1, 0, 2)
        grad_w_down = jnp.where(core == 0, other, total[each:])
        away, own = fold_small(own, meet(away, 2), uppers[3], deps=(grad_tokens,))
        grad_tokens = last(*last_args, 6, 2, (grad_tokens,), deps=(away,))
        away, own = fold_small(own, meet(away, 3), uppers[4], deps=(grad_tokens,))
        widths = (share,) * 5 + (2 * share,) * 2 + (hidden // devices,)
        blocks = end_small(own, meet(away, 4), 2 * share, block, widths)
        rows = [v.reshape(-1) for v in blocks[2:]]
        blocks = blocks[:2]
    else:
        scatter = lambda v: lax.psum_scatter(v.astype(F32), AXES, scatter_dimension=0, tiled=True)
        up = jnp.where(core == 0, keep, send).reshape(UNITS, parts, feature // UNITS, feature)
        grad_w_up = scatter(up.transpose(0, 2, 1, 3).reshape(feature, hidden))
        grad_w_down = scatter(jnp.where(core == 0, send, keep).reshape(hidden, feature))
        grad_tokens = last(*last_args, 0, tiles)
        owned = lambda v: jnp.pad(
            v.reshape(v.shape[0], devices, -1).transpose(1, 0, 2), ((0, 0), (0, 0), (0, LANES - v.shape[1] // devices))
        )
        narrow = jnp.concatenate(list(scale_grads(bias_sums, sums_two, wide)) + [sums_two[:3]])
        biases = bias_sums[:2].reshape(2, feature // LANES, 2, LANES).transpose(0, 2, 1, 3).reshape(2, 2 * feature)
        blocks = [v.reshape(devices, 2 * share, LANES) for v in (grad_one, grad_two)]
        packet = jnp.concatenate(blocks + [owned(narrow), owned(biases), owned(bias_grad)], axis=1)
        result = scatter_small(packet, me, devices, count, 8)
        widths = (share,) * 5 + (2 * share,) * 2 + (hidden // devices,)
        rows = [result[4 * share + k, :width] for k, width in enumerate(widths)]
        blocks = [result[k * 2 * share : (k + 1) * 2 * share, :block] for k in range(2)]
    return (
        mixed.reshape(tokens.shape),
        grad_tokens.reshape(tokens.shape),
        rows[0],
        rows[1],
        blocks[0],
        rows[5],
        blocks[1],
        rows[6],
        rows[2],
        rows[3],
        grad_w_up.reshape(share, hidden),
        rows[7],
        grad_w_down,
        rows[4],
    )


def solution(mesh):
    placed = P(AXES)
    return jax.shard_map(
        on_device, mesh=mesh, in_specs=(placed,) * 16, out_specs=(placed,) * 14, check_vma=False
    )
```

```python
import functools
import math

import jax
import jax.numpy as jnp
import numpy as np
from jax import lax
from jax.experimental import pallas as pl
from jax.experimental.pallas import tpu as pltpu
from jax.sharding import PartitionSpec as P

BF = jnp.bfloat16
F32 = jnp.float32
BLOCKS = 8
EPS = 1e-05
SHRINK = 0.01
ROWS = 32
COLS = 64
KEPT = COLS // 2
GROUP = 4
STEPS = ROWS // GROUP
CELLS = GROUP * COLS
MODES = (KEPT + 1) * ROWS
HEAD = (GROUP + 1) * ROWS
BODY = GROUP * ROWS
TAKE = 2
TOOK = TAKE * BODY
LANES = 128
C1 = math.sqrt(2.0 / math.pi)
C3 = 0.044715
UNITS = 16
VMEM_LIMIT = 60 * 1024 * 1024


def table_parts(values):
    high = values.astype(np.float32).astype(jnp.bfloat16)
    low = (values - high.astype(np.float64)).astype(np.float32).astype(jnp.bfloat16)
    return np.stack([high, low])


def wave_matrices():
    scale = 1.0 / math.sqrt(ROWS * COLS)
    w = np.arange(COLS)
    first = np.zeros((KEPT, 2, GROUP, GROUP, COLS))
    for k in range(KEPT):
        for h in range(GROUP):
            if k == 0:
                first[k, 0, h, h] = scale
                first[k, 1, h, h] = scale * np.where(w % 2 == 0, 1.0, -1.0)
            else:
                first[k, 0, h, h] = scale * np.cos(2 * np.pi * (k * w % COLS) / COLS)
                first[k, 1, h, h] = -scale * np.sin(2 * np.pi * (k * w % COLS) / COLS)
    first = first.reshape(CELLS, CELLS)
    p = np.arange(ROWS)
    turn = 2 * np.pi * (np.outer(p, p) % ROWS) / ROWS
    cos = np.cos(turn).reshape(ROWS, STEPS, GROUP)
    sin = np.sin(turn).reshape(ROWS, STEPS, GROUP)
    body = np.zeros((2, GROUP, ROWS, GROUP, STEPS, 2, GROUP))
    head = np.zeros((2, GROUP + 1, ROWS, GROUP, STEPS, 2, GROUP))
    for k in range(GROUP):
        body[0, k, :, k, :, 0] = cos
        body[0, k, :, k, :, 1] = sin
        body[1, k, :, k, :, 1] = cos
        body[1, k, :, k, :, 0] = -sin
    head[:, 1:GROUP, :, 1:] = body[:, 1:, :, 1:]
    for place, part in ((0, 0), (GROUP, 1)):
        head[0, place, :, 0, :, part] = cos
        head[1, place, :, 0, :, part] = -sin
    weight = np.full((2, GROUP + 1, ROWS, 1), 2.0)
    weight[:, 0] = 1.0
    weight[:, GROUP] = 1.0
    head = head.reshape(2 * HEAD, 2 * BODY)
    body = body.reshape(2 * BODY, 2 * BODY)
    head_weighted = head * weight.reshape(2 * HEAD, 1)
    body_weighted = body * 2.0
    return {
        "first": table_parts(first),
        "first_t": table_parts(first.T),
        "head": table_parts(head),
        "body": table_parts(body),
        "head_t": table_parts(head.T),
        "body_t": table_parts(body.T),
        "head_w": table_parts(head_weighted),
        "body_w": table_parts(body_weighted),
        "head_wt": table_parts(head_weighted.T),
        "body_wt": table_parts(body_weighted.T),
    }


def mm(left, right, dims=(1, 0)):
    return lax.dot_general(
        left, right, (((dims[0],), (dims[1],)), ((), ())), preferred_element_type=F32
    )


def split(values):
    high = values.astype(BF)
    return high, (values - high.astype(F32)).astype(BF)


def turn(table, values):
    high, low = split(values)
    return mm(table[0], high) + mm(table[1], high) + mm(table[0], low)


def normalize(values):
    centred = values - jnp.mean(values, axis=-1, keepdims=True)
    inverse = lax.rsqrt(jnp.mean(centred * centred, axis=-1, keepdims=True) + EPS)
    return centred * inverse, inverse


def norm_back(grad, gain, normal, inverse):
    scaled = grad * gain
    return inverse * (
        scaled
        - jnp.mean(scaled, axis=-1, keepdims=True)
        - normal * jnp.mean(scaled * normal, axis=-1, keepdims=True)
    )


def gelu_parts(value):
    square = value * value
    half = 0.5 + 0.5 * jnp.tanh(value * (C1 + (C1 * C3) * square))
    active = value * half
    slope = half + active * (1.0 - half) * (2.0 * C1 + (6.0 * C1 * C3) * square)
    return active, slope


def gelu(value):
    square = value * value
    return value * (0.5 + 0.5 * jnp.tanh(value * (C1 + (C1 * C3) * square)))


def live_rows(start, count, rows_ref, cols_ref):
    cell = start + lax.broadcasted_iota(jnp.int32, (count, 1), 0)
    inside = (cell // COLS < rows_ref[0]) & (cell % COLS < cols_ref[0])
    return jnp.where(inside, 1.0, 0.0).astype(F32)


def spread(piece, per_device, me, bits):
    devices = piece.shape[0]
    total = devices * per_device
    lane = lax.broadcasted_iota(jnp.int32, (LANES, total), 0)
    place = lax.broadcasted_iota(jnp.int32, (LANES, total), 1)
    pick = jnp.where(place % per_device == lane, 1.0, 0.0).astype(BF)
    wide = mm(piece.astype(BF), pick)
    row = lax.broadcasted_iota(jnp.int32, (devices, 1), 0)
    owner = jnp.full((devices, 1), me, jnp.int32)
    for k, bit in enumerate(bits):
        owner = owner ^ (((row >> k) & 1) << bit)
    where = lax.broadcasted_iota(jnp.int32, (devices, total), 1) // per_device
    return jnp.sum(jnp.where(owner == where, wide, 0.0), axis=0, keepdims=True)


def place_of(mask, bits):
    return sum(((mask >> bit) & 1) << k for k, bit in enumerate(bits))


def any_space():
    return pl.BlockSpec(memory_space=pl.ANY)


def single(shape):
    return pl.BlockSpec(shape, lambda *_: (0,) * len(shape), pipeline_mode=pl.Buffered(1))


def smem():
    return pl.BlockSpec(memory_space=pltpu.SMEM)


def params(**more):
    return pltpu.CompilerParams(vmem_limit_bytes=VMEM_LIMIT, **more)


def cost(flops, moved):
    return pl.CostEstimate(flops=0, bytes_accessed=0, transcendentals=0)


def launch(deps, kernel, *, in_specs, **more):
    count = len(in_specs)

    def body(*refs):
        kernel(*refs[:count], *refs[count + len(deps) :])

    call = pl.pallas_call(body, in_specs=list(in_specs) + [any_space() for _ in deps], **more)
    return lambda *operands: call(*operands, *deps)


def to_mixed(real, imag):
    tiles = []
    for at in range(0, real.shape[1], LANES):
        tiles += [real[:, at : at + LANES], imag[:, at : at + LANES]]
    return jnp.concatenate(tiles, axis=1)


def from_mixed(values):
    cut = lambda at: values[:, at : at + LANES]
    real = [cut(at) for at in range(0, values.shape[1], 2 * LANES)]
    imag = [cut(at + LANES) for at in range(0, values.shape[1], 2 * LANES)]
    return jnp.concatenate(real, axis=1), jnp.concatenate(imag, axis=1)


def mix_product(values, matrix_ref, back=False):
    feature = values.shape[1] // 2
    wide = 2 * LANES
    groups = []
    for group in range(2):
        part = values[:, group * feature : (group + 1) * feature]
        count = feature // wide
        for t in range(count):
            begin, end = max(t - 1, 0) * wide, min(t + 2, count) * wide
            here = slice(t * wide, (t + 1) * wide)
            if back:
                groups.append(mm(part[:, begin:end], matrix_ref[group, here, begin:end], (1, 1)))
            else:
                groups.append(mm(part[:, begin:end], matrix_ref[group, begin:end, here]))
    return jnp.concatenate(groups, axis=1)


def first_kernel(rows_ref, cols_ref, tokens_ref, first_ref, half_ref, normal_ref):
    feature = tokens_ref.shape[1]
    normal, _ = normalize(tokens_ref[...].astype(F32))
    live = live_rows(pl.program_id(0) * CELLS, CELLS, rows_ref, cols_ref)
    normal = normal * live
    normal_ref[...] = normal.astype(BF)
    half_ref[:, :, :feature] = turn(first_ref, normal).reshape(KEPT, 2 * GROUP, feature)
    ones = jnp.broadcast_to(live, (CELLS, LANES)).astype(BF)
    half_ref[:, :, feature:] = (mm(first_ref[0], ones) + mm(first_ref[1], ones)).reshape(KEPT, 2 * GROUP, LANES)


def first(rows, cols, tokens, tables, deps=()):
    cells, feature = tokens.shape
    table = tables["first"]
    return launch(
        deps,
        first_kernel,
        grid=(STEPS,),
        out_shape=(
            jax.ShapeDtypeStruct((KEPT, 2 * ROWS, feature + LANES), F32),
            jax.ShapeDtypeStruct((cells, feature), BF),
        ),
        in_specs=[smem(), smem(), pl.BlockSpec((CELLS, feature), lambda i: (i, 0)), single(table.shape)],
        out_specs=(
            pl.BlockSpec((KEPT, 2 * GROUP, feature + LANES), lambda i: (0, i, 0)),
            pl.BlockSpec((CELLS, feature), lambda i: (i, 0)),
        ),
        compiler_params=params(),
        cost_estimate=cost(6e9, 11e6),
        name="first",
    )(rows, cols, tokens, table)


def build_mix(me, bits, weights_ref, layer, out_ref, feature):
    block = feature // BLOCKS
    half = feature // 2
    per_group = BLOCKS // 2
    share = 2 * feature // weights_ref.shape[0]
    each = block // share
    out_ref[...] = jnp.zeros_like(out_ref)
    row = lax.broadcasted_iota(jnp.int32, (LANES, half), 0)
    column = lax.broadcasted_iota(jnp.int32, (LANES, half), 1)
    for b in range(per_group):
        shift = jnp.where((column - b * block == row) & (row < block), 1.0, 0.0).astype(BF)
        low, high = b * block, (b + 1) * block
        for group in range(2):
            for part in range(2):
                at = (part * BLOCKS + group * per_group + b) * each
                pieces = [
                    weights_ref[place_of((at + k) ^ me, bits), layer * share : (layer + 1) * share, :]
                    for k in range(each)
                ]
                placed = mm(jnp.concatenate(pieces, axis=0), shift).astype(BF)
                for t in range(low // LANES, (high - 1) // LANES + 1):
                    begin, end = max(low, t * LANES), min(high, (t + 1) * LANES)
                    for c in range(low // LANES, (high - 1) // LANES + 1):
                        piece = placed[begin - low : end - low, c * LANES : (c + 1) * LANES]
                        for up in range(2):
                            top = 2 * t * LANES + up * LANES + begin - t * LANES
                            left = (2 * c + (up ^ part)) * LANES
                            value = -piece if part == 1 and up == 1 else piece
                            here = (group, slice(top, top + end - begin), slice(left, left + LANES))
                            out_ref[here] = out_ref[here] + value


def to_modes(half_ref, head_ref, body_ref, is_head):
    width = half_ref.shape[2]
    real, imag, ends = [], [], ()
    for k in range(TAKE):
        begin = is_head and k == 0
        rows = HEAD if begin else BODY
        spec = turn(head_ref if begin else body_ref, half_ref[k * GROUP : (k + 1) * GROUP].reshape(2 * BODY, width))
        real.append(spec[:BODY])
        imag.append(spec[rows : rows + BODY])
        if begin:
            ends = (spec[BODY:rows], spec[rows + BODY :])
    if is_head:
        real.append(ends[0])
        imag.append(ends[1])
    return jnp.concatenate(real, axis=0), jnp.concatenate(imag, axis=0)


def from_modes(pair_of, head_ref, body_ref, is_head, out_ref):
    for k in range(TAKE):
        begin = is_head and k == 0
        parts = []
        for part in pair_of:
            parts.append(part[k * BODY : (k + 1) * BODY])
            if begin:
                parts.append(part[TOOK:])
        result = turn(head_ref if begin else body_ref, jnp.concatenate(parts, axis=0))
        out_ref[k * GROUP : (k + 1) * GROUP] = result.reshape(GROUP, 2 * ROWS, result.shape[1])


def mix_step(half_ref, head_ref, body_ref, back_head_ref, back_body_ref, mix1_ref, mix2_ref, wide_ref, long_ref,
             outs, heads, out_ref, is_head):
    feature = out_ref.shape[2]
    specs = to_modes(half_ref, head_ref, body_ref, is_head)
    gain = wide_ref[0:1, :]
    shift = wide_ref[1:2, :]

    def scaled(part):
        flat = jnp.concatenate([part[:, feature:]] * (feature // LANES), axis=1)
        return (part[:, :feature] * gain + flat * shift).astype(BF)

    inside = to_mixed(*(scaled(part) for part in specs))
    active, slope = gelu_parts(mix_product(inside, mix1_ref) + long_ref[0:1, :])
    hidden = active.astype(BF)
    value = mix_product(hidden, mix2_ref) + long_ref[1:2, :]
    bend = jnp.tanh(value / SHRINK)
    flat = jnp.concatenate([part[:, feature:] for part in specs], axis=1)
    for ref, head, kept in zip(outs, heads, (inside, hidden, slope, bend * bend, flat)):
        ref[...] = kept[:TOOK]
        if is_head:
            head[...] = kept[TOOK:]
    from_modes(from_mixed(value - SHRINK * bend), back_head_ref, back_body_ref, is_head, out_ref)


def mix_first_kernel(
    weight_bits, vector_bits, me_ref, half_ref, weights_ref, vector_ref, head_ref, body_ref, back_head_ref, back_body_ref,
    out_ref, low_ref, hidden_ref, slope_ref, bend_ref, flat_ref,
    low_head_ref, hidden_head_ref, slope_head_ref, bend_head_ref, flat_head_ref, mix1_ref, mix2_ref, wide_ref, long_ref, up_ref,
):
    feature = out_ref.shape[2]
    devices = vector_ref.shape[1]
    share = feature // devices
    step = pl.program_id(0)
    outs = (low_ref, hidden_ref, slope_ref, bend_ref, flat_ref)
    heads = (low_head_ref, hidden_head_ref, slope_head_ref, bend_head_ref, flat_head_ref)
    work = functools.partial(
        mix_step, half_ref, head_ref, body_ref, back_head_ref, back_body_ref, mix1_ref, mix2_ref, wide_ref, long_ref,
        outs, heads, out_ref,
    )

    @pl.when(step == 0)
    def _():
        me = me_ref[0]
        build_mix(me, weight_bits, weights_ref, 0, mix1_ref, feature)
        build_mix(me, weight_bits, weights_ref, 1, mix2_ref, feature)
        wide_ref[...] = jnp.zeros_like(wide_ref)
        long_ref[...] = jnp.zeros_like(long_ref)
        for row, at in enumerate((2, 3, 4, 5, 7)):
            wide_ref[row : row + 1, :] = spread(vector_ref[at], share, me, vector_bits)
        for row in range(2):
            both = spread(vector_ref[row], 2 * share, me, vector_bits)
            long_ref[row : row + 1, :] = to_mixed(both[:, :feature], both[:, feature:])
        up_ref[...] = spread(vector_ref[6], up_ref.shape[1] // devices, me, vector_bits)
        work(True)

    @pl.when(step > 0)
    def _():
        work(False)


def mix_second_kernel(
    half_ref, mix1_ref, mix2_ref, wide_ref, long_ref, body_ref, back_body_ref,
    out_ref, *outs,
):
    mix_step(
        half_ref, None, body_ref, None, back_body_ref, mix1_ref, mix2_ref, wide_ref, long_ref,
        outs, (None,) * 5, out_ref, False,
    )


def mode_shapes(rows, feature):
    wide = [jax.ShapeDtypeStruct((rows, 2 * feature), kind) for kind in (BF, BF, F32, F32)]
    return wide + [jax.ShapeDtypeStruct((rows, 2 * LANES), F32)]


def mode_blocks(feature):
    return [pl.BlockSpec((TOOK, width), lambda i: (i, 0)) for width in (2 * feature,) * 4 + (2 * LANES,)]


def half_block(width, begin=0):
    return pl.BlockSpec((TAKE * GROUP, 2 * ROWS, width), lambda i: (i + begin, 0, 0))


def mix_first(me, half, weights, vectors, tables, hidden, steps, weight_bits, vector_bits, deps=()):
    feature = half.shape[2] - LANES
    fixed = (weights, vectors, tables["head"], tables["body"], tables["head_wt"], tables["body_wt"])
    more = (
        jax.ShapeDtypeStruct((2, feature, feature), BF),
        jax.ShapeDtypeStruct((2, feature, feature), BF),
        jax.ShapeDtypeStruct((8, feature), F32),
        jax.ShapeDtypeStruct((8, 2 * feature), F32),
        jax.ShapeDtypeStruct((1, hidden), F32),
    )
    heads = mode_shapes(ROWS, feature)
    return launch(
        deps,
        functools.partial(mix_first_kernel, weight_bits, vector_bits),
        grid=(steps,),
        out_shape=[jax.ShapeDtypeStruct((TAKE * GROUP * steps, 2 * ROWS, feature), F32)]
        + mode_shapes(TOOK * steps, feature) + heads + list(more),
        in_specs=[smem(), half_block(feature + LANES)] + [single(v.shape) for v in fixed],
        out_specs=[half_block(feature)] + mode_blocks(feature) + [single(v.shape) for v in heads]
        + [single(v.shape) for v in more],
        compiler_params=params(),
        cost_estimate=cost(9e9, 20e6),
        name="mix_first",
    )(me, half, *fixed)


def mix_second(half, mix1, mix2, wide, long, tables, begin, steps, deps=()):
    feature = half.shape[2] - LANES
    fixed = (mix1, mix2, wide, long, tables["body"], tables["body_wt"])
    return launch(
        deps,
        mix_second_kernel,
        grid=(steps,),
        out_shape=[jax.ShapeDtypeStruct((TAKE * GROUP * steps, 2 * ROWS, feature), F32)] + mode_shapes(TOOK * steps, feature),
        in_specs=[half_block(feature + LANES, begin)] + [single(v.shape) for v in fixed],
        out_specs=[half_block(feature)] + mode_blocks(feature),
        compiler_params=params(),
        cost_estimate=cost(9e9, 20e6),
        name="mix_second",
    )(half, *fixed)


def space_kernel(rows_ref, cols_ref, half1_ref, half2_ref, tokens_ref, first_t_ref, wide_ref, middle_ref, normed_ref):
    feature = tokens_ref.shape[1]
    flat = lambda ref: ref[...].reshape(-1, feature)
    spatial = turn(first_t_ref, jnp.concatenate([flat(half1_ref), flat(half2_ref)], axis=0))
    inputs = tokens_ref[...].astype(F32)
    live = live_rows(pl.program_id(0) * CELLS, CELLS, rows_ref, cols_ref)
    normal, _ = normalize(inputs)
    middle = inputs + live * (spatial + (normal * wide_ref[0:1, :] + wide_ref[1:2, :]))
    middle_ref[...] = middle
    normal, _ = normalize(middle)
    normed_ref[...] = (normal * wide_ref[2:3, :] + wide_ref[3:4, :]).astype(BF)


def column_block(rows, width):
    return pl.BlockSpec((rows, 2 * GROUP, width), lambda i: (0, i, 0))


def space(rows, cols, half1, half2, tokens, wide, tables, deps=()):
    cells, feature = tokens.shape
    table = tables["first_t"]
    block = pl.BlockSpec((CELLS, feature), lambda i: (i, 0))
    return launch(
        deps,
        space_kernel,
        grid=(STEPS,),
        out_shape=(jax.ShapeDtypeStruct((cells, feature), F32), jax.ShapeDtypeStruct((cells, feature), BF)),
        in_specs=[smem(), smem(), column_block(half1.shape[0], feature), column_block(half2.shape[0], feature),
                  block, single(table.shape), single(wide.shape)],
        out_specs=(block, block),
        compiler_params=params(),
        cost_estimate=cost(6e9, 20e6),
        name="space",
    )(rows, cols, half1, half2, tokens, table, wide)


def fetch_weights(me_ref, pieces, places, up_ref, down_ref, sems):
    each = pieces[0].shape[0]
    held = len(pieces) // 2
    count = each * held
    chip = me_ref[0] // 2

    def copies(own, core):
        target = (up_ref, down_ref)[core]
        source = pieces[:held] if own else pieces[held:]
        for mask in range(count):
            at = places[core][mask]
            part = source[at // each].at[at % each]
            yield pltpu.make_async_copy(part, target.at[chip ^ mask], sems.at[core, mask])

    for core in range(2):
        @pl.when(me_ref[0] % 2 == core)
        def _():
            for copy in copies(True, core):
                copy.start()
            for copy in copies(False, 1 - core):
                copy.start()

    def arrived(core):
        for copy in copies(True, core):
            copy.wait()

    return arrived


def weight_scratch(pieces):
    chips, rows, feature = UNITS, pieces[0].shape[1], pieces[0].shape[2]
    return [
        pltpu.VMEM((chips, rows, feature), BF),
        pltpu.VMEM((chips, rows, feature), BF),
        pltpu.SemaphoreType.DMA((2, chips)),
    ]


def up_part(up_ref, j, feature):
    share = up_ref.shape[1] * feature // (up_ref.shape[0] * up_ref.shape[1])
    return up_ref[:, j * share : (j + 1) * share, :].reshape(feature, feature)


def down_part(down_ref, j, feature):
    share = down_ref.shape[1]
    each = feature // share
    return down_ref[j * each : (j + 1) * each].reshape(feature, feature)


def up_kernel(places, rows_ref, cols_ref, me_ref, normed_ref, grad_ref, bias_ref, *rest):
    pieces = rest[:-10]
    active_ref, pre_ref, live_ref, bias_grad_ref, up_all_ref, down_all_ref, up_ref, down_ref, sems, out_sems = rest[-10:]
    tile, feature = normed_ref.shape
    step = pl.program_id(0)
    copies = [
        pltpu.make_async_copy(source, target, out_sems.at[k])
        for k, (source, target) in enumerate(((up_ref, up_all_ref), (down_ref, down_all_ref)))
    ]

    def work(arrived):
        live = live_rows(step * tile, tile, rows_ref, cols_ref)
        branch = (grad_ref[...].astype(F32) * live).astype(BF)
        live_ref[...] = branch
        normed = normed_ref[...]
        if arrived:
            arrived(0)
            copies[0].start()
        for j in range(active_ref.shape[1] // feature):
            place = slice(j * feature, (j + 1) * feature)
            value = mm(normed, up_part(up_ref, j, feature)) + bias_ref[:, place]
            if arrived and j == 0:
                arrived(1)
                copies[1].start()
            grad = mm(branch, down_part(down_ref, j, feature), (1, 1))
            active, slope = gelu_parts(value)
            active_ref[:, place] = active.astype(BF)
            low = (grad * slope).astype(BF)
            pre_ref[:, place] = low
            bias_grad_ref[:, place] += jnp.sum(low.astype(F32), axis=0, keepdims=True)

    @pl.when(step == 0)
    def _():
        bias_grad_ref[...] = jnp.zeros_like(bias_grad_ref)
        work(fetch_weights(me_ref, pieces, places, up_ref, down_ref, sems))

    @pl.when(step > 0)
    def _():
        work(None)

    @pl.when(step == pl.num_programs(0) - 1)
    def _():
        for copy in copies:
            copy.wait()


def feed_up(rows, cols, me, normed, grad, bias, pieces, places, tile=256, deps=()):
    cells, feature = normed.shape
    hidden = bias.shape[1]
    block = lambda width: pl.BlockSpec((tile, width), lambda i: (i, 0))
    weights = jax.ShapeDtypeStruct((UNITS,) + pieces[0].shape[1:], BF)
    return launch(
        deps,
        functools.partial(up_kernel, places),
        grid=(cells // tile,),
        out_shape=(
            jax.ShapeDtypeStruct((cells, hidden), BF),
            jax.ShapeDtypeStruct((cells, hidden), BF),
            jax.ShapeDtypeStruct((cells, feature), BF),
            jax.ShapeDtypeStruct((1, hidden), F32),
            weights,
            weights,
        ),
        in_specs=[smem(), smem(), smem(), block(feature), block(feature), single(bias.shape)]
        + [any_space() for _ in pieces],
        out_specs=(block(hidden), block(hidden), block(feature), single((1, hidden)), any_space(), any_space()),
        scratch_shapes=weight_scratch(pieces) + [pltpu.SemaphoreType.DMA((2,))],
        compiler_params=params(),
        cost_estimate=cost(0, 0),
        name="feed_up",
    )(rows, cols, me, normed, grad, bias, *pieces)


def weight_grad_kernel(places, me_ref, active_ref, pre_ref, branch_ref, normed_ref, send_ref, keep_ref, stage_ref, sems):
    step = pl.program_id(0)
    steps = pl.num_programs(0) // 2
    feature = branch_ref.shape[1]
    chips, rows, _ = send_ref.shape
    each = feature // rows
    share = feature // chips

    def down_copies(j, target):
        for c in range(each):
            source = stage_ref.at[j, pl.ds(c * rows, rows)]
            yield pltpu.make_async_copy(source, target.at[places[1][j * each + c]], sems.at[j, c])

    def up_copies(j, target):
        for c in range(chips):
            source = stage_ref.at[steps + j, pl.ds(c * share, share)]
            there = target.at[places[0][c], pl.ds(j * share, share)]
            yield pltpu.make_async_copy(source, there, sems.at[steps + j, c])

    @pl.when(step < steps)
    def _():
        stage_ref[step] = mm(active_ref[...], branch_ref[...], (0, 0)).astype(BF)

    @pl.when(step >= steps)
    def _():
        stage_ref[step] = mm(normed_ref[...], pre_ref[...], (0, 0)).astype(BF)

    total = stage_ref.shape[0] // 2
    for j in range(total):
        for core in range(2):
            targets = (send_ref, keep_ref) if core == 0 else (keep_ref, send_ref)

            @pl.when((step == j) & (me_ref[0] % 2 == core))
            def _():
                for copy in down_copies(j, targets[0]):
                    copy.start()

            @pl.when((step == total + j) & (me_ref[0] % 2 == core))
            def _():
                for copy in up_copies(j, targets[1]):
                    copy.start()

    @pl.when(step == 2 * steps - 1)
    def _():
        for j in range(total):
            for copy in down_copies(j, send_ref):
                copy.wait()
            for copy in up_copies(j, send_ref):
                copy.wait()


def weight_grads(me, active, pre, branch, normed, places, deps=()):
    cells, hidden = active.shape
    feature = branch.shape[1]
    tiles = hidden // feature
    chips = UNITS
    shape = jax.ShapeDtypeStruct((chips, hidden // chips, feature), BF)
    return launch(
        deps,
        functools.partial(weight_grad_kernel, places),
        grid=(2 * tiles,),
        out_shape=(shape, shape),
        in_specs=[
            smem(),
            pl.BlockSpec((cells, feature), lambda i: (0, jnp.minimum(i, tiles - 1))),
            pl.BlockSpec((cells, feature), lambda i: (0, jnp.maximum(i - tiles, 0))),
            single(branch.shape), single(normed.shape),
        ],
        out_specs=(any_space(), any_space()),
        scratch_shapes=[
            pltpu.VMEM((2 * tiles, feature, feature), BF),
            pltpu.SemaphoreType.DMA((2 * tiles, chips)),
        ],
        compiler_params=params(),
        cost_estimate=cost(4 * cells * feature * hidden, 40e6),
        name="weight_grads",
    )(me, active, pre, branch, normed)


def down_kernel(rows_ref, cols_ref, active_ref, pre_ref, middle_ref, grad_ref, normal_ref, wide_ref, first_ref,
                up_ref, down_ref, mixed_ref, grad_middle_ref, half_ref, sums_ref):
    tile, feature = middle_ref.shape
    hidden = active_ref.shape[1]
    step = pl.program_id(0)

    @pl.when(step == 0)
    def _():
        sums_ref[...] = jnp.zeros_like(sums_ref)

    live = live_rows(step * tile, tile, rows_ref, cols_ref)
    branch = mm(active_ref[...], down_ref[...].reshape(hidden, feature))
    grad_normed = jnp.zeros((tile, feature), F32)
    for j in range(hidden // feature):
        pre = pre_ref[:, j * feature : (j + 1) * feature]
        grad_normed = grad_normed + mm(pre, up_part(up_ref, j, feature), (1, 1))
    middle = middle_ref[...]
    mixed_ref[...] = (middle + live * (branch + wide_ref[4:5, :])).astype(BF)
    normal, inverse = normalize(middle)
    cotangent = grad_ref[...].astype(F32)
    grad_middle = cotangent + norm_back(grad_normed, wide_ref[2:3, :], normal, inverse)
    grad_middle_ref[...] = grad_middle
    masked = grad_middle * live
    half_ref[...] = turn(first_ref, masked).reshape(half_ref.shape)
    rows = (grad_normed * normal, grad_normed, cotangent * live, masked * normal_ref[...].astype(F32), masked)
    for row, value in enumerate(rows):
        sums_ref[row : row + 1, :] += jnp.sum(value, axis=0, keepdims=True)


def feed_down(rows, cols, active, pre, middle, grad, normal, wide, table, up, down, deps=()):
    cells, feature = middle.shape
    hidden = active.shape[1]
    block = lambda width: pl.BlockSpec((CELLS, width), lambda i: (i, 0))
    operands = (rows, cols, active, pre, middle, grad, normal, wide, table, up, down)
    return launch(
        deps,
        down_kernel,
        grid=(cells // CELLS,),
        out_shape=(
            jax.ShapeDtypeStruct((cells, feature), BF),
            jax.ShapeDtypeStruct((cells, feature), F32),
            jax.ShapeDtypeStruct((KEPT, 2 * ROWS, feature), F32),
            jax.ShapeDtypeStruct((8, feature), F32),
        ),
        in_specs=[smem(), smem(), block(hidden), block(hidden), block(feature), block(feature), block(feature)]
        + [single(v.shape) for v in operands[7:]],
        out_specs=(block(feature), block(feature), column_block(KEPT, feature), single((8, feature))),
        compiler_params=params(),
        cost_estimate=cost(0, 0),
        name="feed_down",
    )(*operands)


def back_step(half_ref, head_ref, body_ref, back_head_ref, back_body_ref, mix1_ref, mix2_ref, ins, in_heads,
              outs, out_heads, out_ref, sums_ref, is_head):
    feature = out_ref.shape[2]

    def read(k):
        if is_head:
            return jnp.concatenate([ins[k][...], in_heads[k][...]], axis=0)
        return ins[k][...]

    grads = to_modes(half_ref, head_ref, body_ref, is_head)
    grad_two = (to_mixed(*grads) * read(1)).astype(BF)
    grad_one = (mix_product(grad_two, mix2_ref, True) * read(0)).astype(BF)
    grad_spec = mix_product(grad_one, mix1_ref, True)
    from_modes(from_mixed(grad_spec), back_head_ref, back_body_ref, is_head, out_ref)
    for row, value in enumerate((grad_one, grad_two)):
        outs[row][...] = value[:TOOK]
        if is_head:
            out_heads[row][...] = value[TOOK:]
    flat = jnp.concatenate([read(3)] * (feature // LANES), axis=1)
    for row, value in enumerate((grad_one.astype(F32), grad_two.astype(F32), grad_spec * read(2).astype(F32), grad_spec * flat)):
        total = jnp.sum(value, axis=0, keepdims=True)
        sums_ref[row : row + 1, :] = total if is_head else sums_ref[row : row + 1, :] + total


def mix_back_kernel(
    half_ref, slope1_ref, slope2_ref, bend1_ref, bend2_ref, low1_ref, low2_ref, flat1_ref, flat2_ref,
    slope_head_ref, bend_head_ref, low_head_ref, flat_head_ref, mix1_ref, mix2_ref,
    head_ref, body_ref, back_head_ref, back_body_ref,
    out_ref, one_ref, two_ref, one_head_ref, two_head_ref, sums_ref,
):
    step = pl.program_id(0)
    steps = pl.num_programs(0) // 2
    work = functools.partial(
        back_step, half_ref, head_ref, body_ref, back_head_ref, back_body_ref, mix1_ref, mix2_ref
    )
    heads = (slope_head_ref, bend_head_ref, low_head_ref, flat_head_ref)
    more = (heads, (one_ref, two_ref), (one_head_ref, two_head_ref), out_ref, sums_ref)
    near = (slope1_ref, bend1_ref, low1_ref, flat1_ref)
    far = (slope2_ref, bend2_ref, low2_ref, flat2_ref)

    @pl.when(step == 0)
    def _():
        sums_ref[...] = jnp.zeros_like(sums_ref)
        work(near, *more, True)

    @pl.when((step > 0) & (step < steps))
    def _():
        work(near, *more, False)

    @pl.when(step >= steps)
    def _():
        work(far, *more, False)


def mix_back(half, modes1, modes2, heads, mix1, mix2, tables, deps=()):
    feature = half.shape[2]
    steps = KEPT // GROUP // TAKE
    fixed = tuple(heads[k] for k in (2, 3, 0, 4)) + (
        mix1, mix2, tables["head_w"], tables["body_w"], tables["head_t"], tables["body_t"]
    )
    moving = []
    specs = []
    for k in (2, 3, 0, 4):
        width = modes1[k].shape[1]
        moving += [modes1[k], modes2[k]]
        specs += [
            pl.BlockSpec((TOOK, width), lambda i: (jnp.minimum(i, steps // 2 - 1), 0)),
            pl.BlockSpec((TOOK, width), lambda i: (jnp.maximum(i - steps // 2, 0), 0)),
        ]
    low = lambda rows: jax.ShapeDtypeStruct((rows, 2 * feature), BF)
    body = pl.BlockSpec((TOOK, 2 * feature), lambda i: (i, 0))
    shapes = (
        jax.ShapeDtypeStruct((KEPT, 2 * ROWS, feature), F32), low(TOOK * steps), low(TOOK * steps),
        low(ROWS), low(ROWS), jax.ShapeDtypeStruct((8, 2 * feature), F32),
    )
    return launch(
        deps,
        mix_back_kernel,
        grid=(steps,),
        out_shape=shapes,
        in_specs=[half_block(feature)] + specs + [single(v.shape) for v in fixed],
        out_specs=[half_block(feature), body, body] + [single(v.shape) for v in shapes[3:]],
        compiler_params=params(),
        cost_estimate=cost(18e9, 30e6),
        name="mix_back",
    )(half, *moving, *fixed)


def block_kernel(left1_ref, left2_ref, left_head_ref, right_ref, right_head_ref, out_ref, natural_ref):
    wide = 2 * LANES
    count = left1_ref.shape[1] // wide
    cut = left1_ref.shape[0]
    for t in range(count):
        for c in range(max(t - 1, 0), min(t + 2, count)):
            left, right = slice(t * wide, (t + 1) * wide), slice(c * wide, (c + 1) * wide)
            total = (
                mm(left1_ref[:, left], right_ref[:cut, right], (0, 0))
                + mm(left2_ref[:, left], right_ref[cut:, right], (0, 0))
                + mm(left_head_ref[:, left], right_head_ref[:, right], (0, 0))
            )
            rows, lanes = slice(t * LANES, (t + 1) * LANES), slice(c * LANES, (c + 1) * LANES)
            natural_ref[0, rows, lanes] = total[:LANES, :LANES] + total[LANES:, LANES:]
            natural_ref[1, rows, lanes] = total[:LANES, LANES:] - total[LANES:, :LANES]
    per_group = BLOCKS // 2
    block = count * LANES // per_group
    for b in range(per_group):
        begin = b * block
        base = begin // LANES * LANES
        reach = min(base + wide, count * LANES) - base
        for part in range(2):
            piece = natural_ref[part, begin : begin + block, base : base + reach]
            if begin > base:
                piece = pltpu.roll(piece, reach - (begin - base), axis=1)
            out_ref[part, b * block : (b + 1) * block, :] = piece[:, :LANES]


def block_grads(left1, left2, left_head, right, right_head, name, deps=()):
    feature = left1.shape[1] // 2
    half = feature // 2
    block = lambda v: pl.BlockSpec((v.shape[0], feature), lambda i: (0, i))
    return launch(
        deps,
        block_kernel,
        grid=(2,),
        out_shape=jax.ShapeDtypeStruct((2, feature, LANES), F32),
        in_specs=[block(v) for v in (left1, left2, left_head, right, right_head)],
        out_specs=pl.BlockSpec((2, half, LANES), lambda i: (0, i, 0)),
        scratch_shapes=[pltpu.VMEM((2, half, half), F32)],
        compiler_params=params(),
        cost_estimate=cost(5e9, 7e6),
        name=name,
    )(left1, left2, left_head, right, right_head)


def last_kernel(begin, rows_ref, cols_ref, half_ref, tokens_ref, grad_ref, first_t_ref, wide_ref, *rest):
    out_ref = rest[-1]
    tile, feature = tokens_ref.shape
    live = live_rows((pl.program_id(0) + begin) * tile, tile, rows_ref, cols_ref)
    grad_middle = grad_ref[...]
    grad_normed = live * (grad_middle + turn(first_t_ref, half_ref[...].reshape(CELLS, feature)))
    normal, inverse = normalize(tokens_ref[...].astype(F32))
    out_ref[...] = grad_middle + norm_back(grad_normed, wide_ref[0:1, :], normal, inverse)


def last(rows, cols, half, tokens, grad, wide, tables, begin, steps, before=(), deps=()):
    cells, feature = tokens.shape
    first_t = tables["first_t"]
    block = pl.BlockSpec((CELLS, feature), lambda i: (i + begin, 0))
    operands = (rows, cols, half, tokens, grad, first_t, wide)
    return launch(
        deps,
        functools.partial(last_kernel, begin),
        grid=(steps,),
        out_shape=jax.ShapeDtypeStruct((cells, feature), F32),
        in_specs=[smem(), smem(), pl.BlockSpec((KEPT, 2 * GROUP, feature), lambda i: (0, i + begin, 0)), block, block,
                  single(first_t.shape), single(wide.shape)] + [any_space() for _ in before],
        out_specs=block,
        input_output_aliases={len(operands): 0} if before else {},
        compiler_params=params(),
        cost_estimate=cost(6e9, 20e6),
        name="last",
    )(*operands, *before)


def collect(value, per_device, devices):
    total = value.shape[1]
    owner = lax.broadcasted_iota(jnp.int32, (devices, total), 1) // per_device
    row = lax.broadcasted_iota(jnp.int32, (devices, total), 0)
    high, low = split(jnp.where(owner == row, jnp.broadcast_to(value, (devices, total)), 0.0))
    place = lax.broadcasted_iota(jnp.int32, (total, LANES), 0)
    lane = lax.broadcasted_iota(jnp.int32, (total, LANES), 1)
    pick = jnp.where(place % per_device == lane, 1.0, 0.0).astype(BF)
    return mm(high, pick) + mm(low, pick)


def emit(upper_ref, sum_ref, send_ref, keep_ref):
    rows = sum_ref.shape[2] - 8
    half = sum_ref.shape[0]
    away = sum_ref[:, pl.ds(1 - upper_ref[0], 1)].reshape(half, rows + 8, LANES)
    high, low = split(away[:, rows:])
    send_ref[:, :rows] = away[:, :rows].astype(BF)
    send_ref[:, rows:] = jnp.concatenate([high.astype(F32), low.astype(F32)], axis=1).astype(BF)
    keep_ref[...] = sum_ref[:, pl.ds(upper_ref[0], 1)].reshape(half, rows + 8, LANES)


def pack_kernel(upper_ref, one_ref, two_ref, mixed_ref, sums_ref, up_ref, wide_ref, send_ref, keep_ref, sum_ref):
    half, _, rows, _ = sum_ref.shape
    devices = 2 * half
    share = (rows - 8) // 4
    feature = sums_ref.shape[1]
    sum_ref[:, :, : 2 * share] = one_ref[...].reshape(half, 2, 2 * share, LANES)
    sum_ref[:, :, 2 * share : 4 * share] = two_ref[...].reshape(half, 2, 2 * share, LANES)
    first_gain, first_bias = scale_grads(mixed_ref, sums_ref, wide_ref)
    natural = [jnp.concatenate(from_mixed(mixed_ref[k : k + 1, :]), axis=1) for k in range(2)]
    narrow = [first_gain, first_bias] + [sums_ref[k : k + 1, :] for k in range(3)]
    for k, value in enumerate(narrow + natural + [up_ref[...]]):
        placed = collect(value, value.shape[1] // devices, devices)
        for d in range(devices):
            sum_ref[d // 2, d % 2, 4 * share + k : 4 * share + k + 1, :] = placed[d : d + 1, :]
    emit(upper_ref, sum_ref, send_ref, keep_ref)


def scale_grads(mixed_ref, sums_ref, wide_ref):
    real, imag = from_mixed(mixed_ref[2:3, :])
    scaled = real + imag
    real, imag = from_mixed(mixed_ref[3:4, :])
    flat = real + imag
    gain = sums_ref[3:4, :] + (scaled - wide_ref[1:2, :] * flat) / wide_ref[0:1, :]
    return gain, sums_ref[4:5, :] + flat


def small_shapes(half, rows):
    return (
        jax.ShapeDtypeStruct((half, rows + 8, LANES), BF),
        jax.ShapeDtypeStruct((half, rows, LANES), F32),
    )


def pack(upper, one, two, mixed, sums, up, wide, devices):
    rows = 2 * one.shape[0] * one.shape[1] // devices + 8
    shapes = small_shapes(devices // 2, rows)
    operands = (one, two, mixed, sums, up, wide)
    return pl.pallas_call(
        pack_kernel,
        out_shape=shapes,
        in_specs=[smem()] + vmem(len(operands)),
        out_specs=vmem(2),
        scratch_shapes=[pltpu.VMEM((devices // 2, 2, rows, LANES), F32)],
        compiler_params=params(),
        cost_estimate=cost(0, 0),
        name="pack",
    )(upper, *operands)


def merge_small(keep_ref, got_ref):
    rows = keep_ref.shape[1] - 8
    tail = got_ref[:, rows:].astype(F32)
    return (
        keep_ref[:, :rows] + got_ref[:, :rows].astype(F32),
        keep_ref[:, rows:] + tail[:, :8] + tail[:, 8:],
    )


def fold_small_kernel(upper_ref, keep_ref, got_ref, send_ref, out_ref, sum_ref):
    half, _, rows, _ = sum_ref.shape
    top, tail = merge_small(keep_ref, got_ref)
    sum_ref[:, :, : rows - 8] = top.reshape(half, 2, rows - 8, LANES)
    sum_ref[:, :, rows - 8 :] = tail.reshape(half, 2, 8, LANES)
    emit(upper_ref, sum_ref, send_ref, out_ref)


def fold_small(keep, got, upper, deps=()):
    half, rows = keep.shape[0] // 2, keep.shape[1]
    return launch(
        deps,
        fold_small_kernel,
        out_shape=small_shapes(half, rows),
        in_specs=[smem()] + vmem(2),
        out_specs=vmem(2),
        scratch_shapes=[pltpu.VMEM((half, 2, rows, LANES), F32)],
        compiler_params=params(),
        cost_estimate=cost(0, 0),
        name="fold_small",
    )(upper, keep, got)


def vmem(count):
    return [pl.BlockSpec(memory_space=pltpu.VMEM)] * count


def end_small_kernel(keep_ref, got_ref, one_ref, two_ref, *rows_refs):
    top, tail = merge_small(keep_ref, got_ref)
    share, block = one_ref.shape
    one_ref[...] = top[0, :share, :block]
    two_ref[...] = top[0, share:, :block]
    for row, ref in enumerate(rows_refs):
        ref[...] = tail[0, row : row + 1, : ref.shape[1]]


def end_small(keep, got, share, block, widths):
    shapes = [jax.ShapeDtypeStruct((share, block), F32)] * 2
    shapes += [jax.ShapeDtypeStruct((1, width), F32) for width in widths]
    return pl.pallas_call(
        end_small_kernel,
        out_shape=shapes,
        in_specs=vmem(2),
        out_specs=vmem(len(shapes)),
        compiler_params=params(),
        cost_estimate=cost(0, 0),
        name="end_small",
    )(keep, got)


def begin_small_kernel(one_ref, two_ref, *rest):
    out_ref, rows_ref = rest[-2:]
    share, block = one_ref.shape
    out_ref[...] = jnp.zeros_like(out_ref)
    rows_ref[...] = jnp.zeros_like(rows_ref)
    out_ref[0, :share, :block] = one_ref[...]
    out_ref[0, share : 2 * share, :block] = two_ref[...]
    for row, ref in enumerate(rest[:-2]):
        rows_ref[row : row + 1, : ref.shape[1]] = ref[...].astype(F32)
    out_ref[0, 2 * share :, :] = rows_ref[...].astype(BF)


def begin_small(one, two, vectors):
    share = one.shape[0]
    operands = (one, two) + tuple(v[None] for v in vectors)
    return pl.pallas_call(
        begin_small_kernel,
        out_shape=jax.ShapeDtypeStruct((1, 2 * share + 16, LANES), BF),
        in_specs=vmem(len(operands)),
        out_specs=vmem(1)[0],
        scratch_shapes=[pltpu.VMEM((16, LANES), F32)],
        compiler_params=params(),
        cost_estimate=cost(0, 0),
        name="begin_small",
    )(*operands)


AXES = ("dp", "fsdp")


def swap(value, devices, bits):
    return lax.ppermute(value, AXES, [(i, i ^ (1 << bits[i & 1])) for i in range(devices)])


def doubling_orders(count):
    first = list(range(count - 1, 0, -1))
    second = list(first)
    for k in range(0, len(second) - 1, 2):
        second[k], second[k + 1] = second[k + 1], second[k]
    return first, second


def places_of(order):
    return [
        sum(1 << k for k, bit in enumerate(order) if mask >> (bit - 1) & 1) for mask in range(1 << len(order))
    ]


def join_kernel(*refs):
    out_ref = refs[-1]
    count = refs[0].shape[0]
    for k, ref in enumerate(refs[:-1]):
        out_ref[k * count : (k + 1) * count] = ref[...]


def join_rows(*pieces, deps=()):
    shape = jax.ShapeDtypeStruct((len(pieces) * pieces[0].shape[0],) + pieces[0].shape[1:], pieces[0].dtype)
    return launch(
        deps,
        join_kernel,
        out_shape=shape,
        in_specs=[pl.BlockSpec(memory_space=pltpu.VMEM) for _ in pieces],
        out_specs=pl.BlockSpec(memory_space=pltpu.VMEM),
        compiler_params=params(),
        cost_estimate=cost(0, 0),
        name="join",
    )(*pieces)


def hold(value, deps):
    def body(*refs):
        pass

    return pl.pallas_call(
        body,
        out_shape=jax.ShapeDtypeStruct(value.shape, value.dtype),
        in_specs=[any_space() for _ in range(1 + len(deps))],
        out_specs=any_space(),
        input_output_aliases={0: 0},
        compiler_params=params(),
        cost_estimate=cost(0, 0),
        name="hold",
    )(value, *deps)


def gather_small(value, me, devices, count):
    held = value[None]
    for bit in list(range(3, count)) + [2, 1, 0]:
        other = swap(held, devices, (bit, bit))
        upper = (me >> bit) & 1
        axis = 0 if bit > 2 else 1
        join_two = lambda a, b: jnp.stack([a, b], axis=axis).reshape((-1,) + value.shape)
        held = jnp.where(upper == 0, join_two(held, other), join_two(other, held))
    return held


def scatter_small(value, me, devices, count, exact):
    shape = value.shape[1:]
    rows = shape[0]
    total = value
    for bit in [0, 1, 2] + list(range(count - 1, 2, -1)):
        upper = (me >> bit) & 1
        axis = 0 if bit > 2 else 1
        pair = total.reshape(((2, -1) if bit > 2 else (-1, 2)) + shape)
        away = lax.dynamic_index_in_dim(pair, 1 - upper, axis, keepdims=False)
        keep = lax.dynamic_index_in_dim(pair, upper, axis, keepdims=False)
        sums = away[:, rows - exact :]
        top = lax.reduce_precision(sums, 8, 7)
        packet = jnp.concatenate([away[:, : rows - exact], top, sums - top], axis=1).astype(BF)
        got = swap(packet, devices, (bit, bit)).astype(F32)
        low = got[:, rows - exact : rows] + got[:, rows:]
        total = keep + jnp.concatenate([got[:, : rows - exact], low], axis=1)
    return total[0]


def chip_unit(up, down, core, devices):
    parts, share, feature = up.shape
    flat = up.reshape(parts * share, feature)
    other = swap(jnp.where(core == 0, down, flat), devices, (0, 0))
    up_unit = jnp.concatenate([up, other.reshape(up.shape)], axis=1).reshape(2 * parts * share, feature)
    return jnp.where(core == 0, up_unit, jnp.concatenate([other, down]))[None]


def fold_kernel(upper_ref, keep_away_ref, got_away_ref, keep_own_ref, got_own_ref, send_ref, keep_ref):
    send_ref[...] = (keep_away_ref[...].astype(F32) + got_away_ref[...].astype(F32)).astype(BF)
    keep_ref[...] = (keep_own_ref[...].astype(F32) + got_own_ref[...].astype(F32)).astype(BF)


def fold(keep, got, upper, deps=()):
    half = keep.shape[0] // 2
    each = min(2, half)
    unit = (each,) + keep.shape[1:]
    count = len(deps)
    away = pl.BlockSpec(unit, lambda i, up: ((1 - up[0]) * (half // each) + i, 0, 0))
    own = pl.BlockSpec(unit, lambda i, up: (up[0] * (half // each) + i, 0, 0))
    out = pl.BlockSpec(unit, lambda i, up: (i, 0, 0))
    shape = jax.ShapeDtypeStruct((half,) + keep.shape[1:], BF)

    def body(*refs):
        fold_kernel(*refs[:5], *refs[5 + count :])

    return pl.pallas_call(
        body,
        grid_spec=pltpu.PrefetchScalarGridSpec(
            num_scalar_prefetch=1,
            grid=(half // each,),
            in_specs=[away, away, own, own] + [any_space() for _ in deps],
            out_specs=[out, out],
        ),
        out_shape=(shape, shape),
        compiler_params=params(),
        cost_estimate=cost(0, 6 * half * keep[0].size),
        name="fold",
    )(upper, keep, got, keep, got, *deps)


def on_device(
    tokens, grad_out, region_rows, region_cols, ln1_gain, ln1_bias, spec_w1, spec_b1, spec_w2, spec_b2,
    ln2_gain, ln2_bias, w_up, up_bias, w_down, down_bias,
):
    devices = lax.axis_size(AXES[0]) * lax.axis_size(AXES[1])
    count = devices.bit_length() - 1
    me = lax.axis_index(AXES).astype(jnp.int32)
    core = me & 1
    me_one = me.reshape(1)
    feature = tokens.shape[-1]
    block = feature // BLOCKS
    share = ln1_gain.shape[0]
    cells = tokens.shape[1] * tokens.shape[2]
    hidden = w_up.shape[1]
    parts = hidden // feature
    tables = {name: jnp.asarray(value) for name, value in wave_matrices().items()}
    orders = doubling_orders(count)
    places = tuple(places_of(order) for order in orders)
    flat_tokens = tokens.reshape(cells, feature)
    flat_grad = grad_out.reshape(cells, feature)
    fast = devices // 2 == UNITS
    step = lambda value, k: swap(value, devices, (orders[0][k], orders[1][k]))

    padded = lambda v: jnp.pad(v, ((0, 0), (0, LANES - v.shape[1])))
    vectors = (spec_b1, spec_b2, ln1_gain, ln1_bias, ln2_gain, ln2_bias, up_bias, down_bias)
    if fast:
        own_up = w_up.reshape(share, parts, feature).transpose(1, 0, 2)
        unit = chip_unit(own_up, w_down, core, devices)
        bits = (3, 4, 2, 1, 0)
        hop = lambda value, mask: lax.ppermute(value, AXES, [(i, i ^ mask) for i in range(devices)])
        meet = lambda value, bit: hop(value, 1 << bit)
        small = begin_small(spec_w1, spec_w2, vectors)
        half, normal = first(region_rows, region_cols, flat_tokens, tables, deps=(unit, small))
        small = join_rows(small, *(hop(small, mask) for mask in (8, 16, 24)), deps=(half,))
        near = join_rows(unit, step(unit, 0), deps=(small,))
        small = join_rows(small, *(hop(small, mask) for mask in (4, 2, 6)), deps=(near,))
        near = join_rows(near, step(near, 1), deps=(small,))
        small = join_rows(small, meet(small, 0), deps=(near,))
        beside, across = step(near, 2), step(near, 3)
        weights, weight_bits, vector_bits, me_small = small, bits, bits, me_one
        vectors = small[:, 4 * share : 4 * share + 8].transpose(1, 0, 2).astype(F32)
    else:
        up = lax.all_gather(w_up, AXES, axis=0, tiled=True)
        up = up.reshape(UNITS, feature // UNITS, parts, feature).transpose(0, 2, 1, 3).reshape(UNITS, -1, feature)
        down = lax.all_gather(w_down, AXES, axis=0, tiled=True).reshape(UNITS, -1, feature)
        pieces = tuple(
            jnp.where(core == 0, one, two)[begin : begin + UNITS // 2]
            for one, two in ((up, down), (down, up))
            for begin in (0, UNITS // 2)
        )
        me_one = core.reshape(1)
        me_small = jnp.zeros_like(me_one)
        places = (tuple(range(UNITS)),) * 2
        small = jnp.concatenate([padded(spec_w1), padded(spec_w2)] + [padded(v[None]) for v in vectors])
        small = gather_small(small, me, devices, count)
        weights = small[:, : 4 * share].reshape(devices, 2, 2 * share, LANES).transpose(1, 0, 2, 3)
        weights = weights.reshape(2, 2 * UNITS, -1, LANES).transpose(1, 0, 2, 3).reshape(2 * UNITS, -1, LANES)
        weight_bits, vector_bits = tuple(range(5)), tuple(range(count))
        half, normal = first(region_rows, region_cols, flat_tokens, tables)
        vectors = small[:, 4 * share :].transpose(1, 0, 2).astype(F32)

    steps = KEPT // GROUP // TAKE
    core_swap = lambda value: swap(value, devices, (0, 0))
    made = mix_first(
        me_small, half, weights, vectors, tables, hidden, steps // 2, weight_bits, vector_bits,
        deps=(near,) if fast else (),
    )
    half1, modes1, heads, (mix1, mix2, wide, long, up_shift) = made[0], made[1:6], made[6:11], made[11:]
    deps = ()
    if fast:
        other_near = core_swap(near)
        deps = (other_near,)
    made = mix_second(half, mix1, mix2, wide, long, tables, steps // 2, steps // 2, deps=deps)
    half2, modes2 = made[0], made[1:6]
    if fast:
        beside = hold(beside, (half2,))
        far = step(beside, 3)
        deps = (beside,)
    middle, normed = space(region_rows, region_cols, half1, half2, flat_tokens, wide, tables, deps=deps)
    if fast:
        across = hold(across, (normed,))
        far = hold(far, (across,))
        pieces = (near, beside, across, far, other_near) + tuple(core_swap(v) for v in (beside, across, far))
    active, pre, branch, bias_grad, up_all, down_all = feed_up(
        region_rows, region_cols, me_one, normed, flat_grad, up_shift, pieces, places
    )
    send, keep = weight_grads(me_one, active, pre, branch, normed, places)
    tiles = cells // CELLS
    mixed, grad_middle, half_back, sums_two = feed_down(
        region_rows, region_cols, active, pre, middle, flat_grad, normal, wide, tables["first"], up_all, down_all,
        deps=(send,),
    )
    deps = ()
    if fast:
        ranks = [((me >> jnp.where(core == 0, *bit)) & 1).reshape(1) for bit in zip(*orders)]
        send, keep = fold(keep, swap(send, devices, (0, 0)), ranks[3], deps=(sums_two,))
        deps = (send,)
    half_back, one, two, one_head, two_head, bias_sums = mix_back(
        half_back, modes1, modes2, heads, mix1, mix2, tables, deps=deps
    )
    grad_one = block_grads(modes1[0], modes2[0], heads[0], one, one_head, "grad_mix1")
    if fast:
        send, keep = fold(keep, step(send, 3), ranks[2], deps=(grad_one,))
        deps = (send,)
    grad_two = block_grads(modes1[1], modes2[1], heads[1], two, two_head, "grad_mix2", deps=deps)
    last_args = (region_rows, region_cols, half_back, flat_tokens, grad_middle, wide, tables)
    if fast:
        uppers = [((me >> bit) & 1).reshape(1) for bit in range(count)]
        away, own = pack(uppers[0], grad_one, grad_two, bias_sums, sums_two, bias_grad, wide, devices)
        grad_tokens = last(*last_args, 0, 2, deps=(away,))
        send, keep = fold(keep, step(send, 2), ranks[1], deps=(grad_tokens,))
        away, own = fold_small(own, meet(away, 0), uppers[1], deps=(send,))
        grad_tokens = last(*last_args, 2, 2, (grad_tokens,), deps=(away,))
        away, own = fold_small(own, meet(away, 1), uppers[2], deps=(grad_tokens,))
        grad_tokens = last(*last_args, 4, 2, (grad_tokens,), deps=(away,))
        send, keep = fold(keep, step(send, 1), ranks[0], deps=(grad_tokens,))
        away, own = fold_small(own, meet(away, 2), uppers[3], deps=(send,))
        grad_tokens = last(*last_args, 6, 2, (grad_tokens,), deps=(away,))
        keep = hold(keep, (grad_tokens,))
        total = keep[0].astype(F32) + step(send, 0)[0].astype(F32)
        up_sum = total.reshape(parts, 2 * share, feature)
        lower = up_sum[:, :share].reshape(parts * share, feature)
        upper = up_sum[:, share:].reshape(parts * share, feature)
        each = parts * share
        leaving = jnp.where(core == 0, upper, total[:each])
        other = swap(leaving, devices, (0, 0))
        away, own = fold_small(own, meet(away, 3), uppers[4], deps=(leaving,))
        grad_w_up = jnp.where(core == 0, lower, other).reshape(parts, share, feature).transpose(1, 0, 2)
        grad_w_down = jnp.where(core == 0, other, total[each:])
        widths = (share,) * 5 + (2 * share,) * 2 + (hidden // devices,)
        blocks = end_small(own, meet(away, 4), 2 * share, block, widths)
        rows = [v.reshape(-1) for v in blocks[2:]]
        blocks = blocks[:2]
    else:
        scatter = lambda v: lax.psum_scatter(v.astype(F32), AXES, scatter_dimension=0, tiled=True)
        up = jnp.where(core == 0, keep, send).reshape(UNITS, parts, feature // UNITS, feature)
        grad_w_up = scatter(up.transpose(0, 2, 1, 3).reshape(feature, hidden))
        grad_w_down = scatter(jnp.where(core == 0, send, keep).reshape(hidden, feature))
        grad_tokens = last(*last_args, 0, tiles)
        owned = lambda v: jnp.pad(
            v.reshape(v.shape[0], devices, -1).transpose(1, 0, 2), ((0, 0), (0, 0), (0, LANES - v.shape[1] // devices))
        )
        narrow = jnp.concatenate(list(scale_grads(bias_sums, sums_two, wide)) + [sums_two[:3]])
        biases = bias_sums[:2].reshape(2, feature // LANES, 2, LANES).transpose(0, 2, 1, 3).reshape(2, 2 * feature)
        blocks = [v.reshape(devices, 2 * share, LANES) for v in (grad_one, grad_two)]
        packet = jnp.concatenate(blocks + [owned(narrow), owned(biases), owned(bias_grad)], axis=1)
        result = scatter_small(packet, me, devices, count, 8)
        widths = (share,) * 5 + (2 * share,) * 2 + (hidden // devices,)
        rows = [result[4 * share + k, :width] for k, width in enumerate(widths)]
        blocks = [result[k * 2 * share : (k + 1) * 2 * share, :block] for k in range(2)]
    return (
        mixed.reshape(tokens.shape),
        grad_tokens.reshape(tokens.shape),
        rows[0],
        rows[1],
        blocks[0],
        rows[5],
        blocks[1],
        rows[6],
        rows[2],
        rows[3],
        grad_w_up.reshape(share, hidden),
        rows[7],
        grad_w_down,
        rows[4],
    )


def solution(mesh):
    placed = P(AXES)
    return jax.shard_map(
        on_device, mesh=mesh, in_specs=(placed,) * 16, out_specs=(placed,) * 14, check_vma=False
    )
```

```python
import functools
import math

import jax
import jax.numpy as jnp
import numpy as np
from jax import lax
from jax.experimental import pallas as pl
from jax.experimental.pallas import tpu as pltpu
from jax.sharding import PartitionSpec as P

BF = jnp.bfloat16
F32 = jnp.float32
BLOCKS = 8
EPS = 1e-05
SHRINK = 0.01
ROWS = 32
COLS = 64
KEPT = COLS // 2
GROUP = 4
STEPS = ROWS // GROUP
CELLS = GROUP * COLS
MODES = (KEPT + 1) * ROWS
HEAD = (GROUP + 1) * ROWS
BODY = GROUP * ROWS
TAKE = 2
TOOK = TAKE * BODY
LANES = 128
C1 = math.sqrt(2.0 / math.pi)
C3 = 0.044715
UNITS = 16
VMEM_LIMIT = 60 * 1024 * 1024


def table_parts(values):
    high = values.astype(np.float32).astype(jnp.bfloat16)
    low = (values - high.astype(np.float64)).astype(np.float32).astype(jnp.bfloat16)
    return np.stack([high, low])


def wave_matrices():
    scale = 1.0 / math.sqrt(ROWS * COLS)
    w = np.arange(COLS)
    first = np.zeros((KEPT, 2, GROUP, GROUP, COLS))
    for k in range(KEPT):
        for h in range(GROUP):
            if k == 0:
                first[k, 0, h, h] = scale
                first[k, 1, h, h] = scale * np.where(w % 2 == 0, 1.0, -1.0)
            else:
                first[k, 0, h, h] = scale * np.cos(2 * np.pi * (k * w % COLS) / COLS)
                first[k, 1, h, h] = -scale * np.sin(2 * np.pi * (k * w % COLS) / COLS)
    first = first.reshape(CELLS, CELLS)
    p = np.arange(ROWS)
    turn = 2 * np.pi * (np.outer(p, p) % ROWS) / ROWS
    cos = np.cos(turn).reshape(ROWS, STEPS, GROUP)
    sin = np.sin(turn).reshape(ROWS, STEPS, GROUP)
    body = np.zeros((2, GROUP, ROWS, GROUP, STEPS, 2, GROUP))
    head = np.zeros((2, GROUP + 1, ROWS, GROUP, STEPS, 2, GROUP))
    for k in range(GROUP):
        body[0, k, :, k, :, 0] = cos
        body[0, k, :, k, :, 1] = sin
        body[1, k, :, k, :, 1] = cos
        body[1, k, :, k, :, 0] = -sin
    head[:, 1:GROUP, :, 1:] = body[:, 1:, :, 1:]
    for place, part in ((0, 0), (GROUP, 1)):
        head[0, place, :, 0, :, part] = cos
        head[1, place, :, 0, :, part] = -sin
    weight = np.full((2, GROUP + 1, ROWS, 1), 2.0)
    weight[:, 0] = 1.0
    weight[:, GROUP] = 1.0
    head = head.reshape(2 * HEAD, 2 * BODY)
    body = body.reshape(2 * BODY, 2 * BODY)
    head_weighted = head * weight.reshape(2 * HEAD, 1)
    body_weighted = body * 2.0
    return {
        "first": table_parts(first),
        "first_t": table_parts(first.T),
        "head": table_parts(head),
        "body": table_parts(body),
        "head_t": table_parts(head.T),
        "body_t": table_parts(body.T),
        "head_w": table_parts(head_weighted),
        "body_w": table_parts(body_weighted),
        "head_wt": table_parts(head_weighted.T),
        "body_wt": table_parts(body_weighted.T),
    }


def mm(left, right, dims=(1, 0)):
    return lax.dot_general(
        left, right, (((dims[0],), (dims[1],)), ((), ())), preferred_element_type=F32
    )


def split(values):
    high = values.astype(BF)
    return high, (values - high.astype(F32)).astype(BF)


def turn(table, values):
    high, low = split(values)
    return mm(table[0], high) + mm(table[1], high) + mm(table[0], low)


def normalize(values):
    centred = values - jnp.mean(values, axis=-1, keepdims=True)
    inverse = lax.rsqrt(jnp.mean(centred * centred, axis=-1, keepdims=True) + EPS)
    return centred * inverse, inverse


def norm_back(grad, gain, normal, inverse):
    scaled = grad * gain
    return inverse * (
        scaled
        - jnp.mean(scaled, axis=-1, keepdims=True)
        - normal * jnp.mean(scaled * normal, axis=-1, keepdims=True)
    )


def gelu_parts(value):
    square = value * value
    half = 0.5 + 0.5 * jnp.tanh(value * (C1 + (C1 * C3) * square))
    active = value * half
    slope = half + active * (1.0 - half) * (2.0 * C1 + (6.0 * C1 * C3) * square)
    return active, slope


def gelu(value):
    square = value * value
    return value * (0.5 + 0.5 * jnp.tanh(value * (C1 + (C1 * C3) * square)))


def live_rows(start, count, rows_ref, cols_ref):
    cell = start + lax.broadcasted_iota(jnp.int32, (count, 1), 0)
    inside = (cell // COLS < rows_ref[0]) & (cell % COLS < cols_ref[0])
    return jnp.where(inside, 1.0, 0.0).astype(F32)


def spread(piece, per_device, me, bits):
    devices = piece.shape[0]
    total = devices * per_device
    lane = lax.broadcasted_iota(jnp.int32, (LANES, total), 0)
    place = lax.broadcasted_iota(jnp.int32, (LANES, total), 1)
    pick = jnp.where(place % per_device == lane, 1.0, 0.0).astype(BF)
    wide = mm(piece.astype(BF), pick)
    row = lax.broadcasted_iota(jnp.int32, (devices, 1), 0)
    owner = jnp.full((devices, 1), me, jnp.int32)
    for k, bit in enumerate(bits):
        owner = owner ^ (((row >> k) & 1) << bit)
    where = lax.broadcasted_iota(jnp.int32, (devices, total), 1) // per_device
    return jnp.sum(jnp.where(owner == where, wide, 0.0), axis=0, keepdims=True)


def place_of(mask, bits):
    return sum(((mask >> bit) & 1) << k for k, bit in enumerate(bits))


def any_space():
    return pl.BlockSpec(memory_space=pl.ANY)


def single(shape):
    return pl.BlockSpec(shape, lambda *_: (0,) * len(shape), pipeline_mode=pl.Buffered(1))


def smem():
    return pl.BlockSpec(memory_space=pltpu.SMEM)


def params(**more):
    return pltpu.CompilerParams(vmem_limit_bytes=VMEM_LIMIT, **more)


def cost(flops, moved):
    return pl.CostEstimate(flops=0, bytes_accessed=0, transcendentals=0)


def launch(deps, kernel, *, in_specs, **more):
    count = len(in_specs)

    def body(*refs):
        kernel(*refs[:count], *refs[count + len(deps) :])

    call = pl.pallas_call(body, in_specs=list(in_specs) + [any_space() for _ in deps], **more)
    return lambda *operands: call(*operands, *deps)


def to_mixed(real, imag):
    tiles = []
    for at in range(0, real.shape[1], LANES):
        tiles += [real[:, at : at + LANES], imag[:, at : at + LANES]]
    return jnp.concatenate(tiles, axis=1)


def from_mixed(values):
    cut = lambda at: values[:, at : at + LANES]
    real = [cut(at) for at in range(0, values.shape[1], 2 * LANES)]
    imag = [cut(at + LANES) for at in range(0, values.shape[1], 2 * LANES)]
    return jnp.concatenate(real, axis=1), jnp.concatenate(imag, axis=1)


def mix_product(values, matrix_ref, back=False):
    feature = values.shape[1] // 2
    wide = 2 * LANES
    groups = []
    for group in range(2):
        part = values[:, group * feature : (group + 1) * feature]
        count = feature // wide
        for t in range(count):
            begin, end = max(t - 1, 0) * wide, min(t + 2, count) * wide
            here = slice(t * wide, (t + 1) * wide)
            if back:
                groups.append(mm(part[:, begin:end], matrix_ref[group, here, begin:end], (1, 1)))
            else:
                groups.append(mm(part[:, begin:end], matrix_ref[group, begin:end, here]))
    return jnp.concatenate(groups, axis=1)


def first_kernel(rows_ref, cols_ref, tokens_ref, first_ref, half_ref, normal_ref):
    feature = tokens_ref.shape[1]
    normal, _ = normalize(tokens_ref[...].astype(F32))
    live = live_rows(pl.program_id(0) * CELLS, CELLS, rows_ref, cols_ref)
    normal = normal * live
    normal_ref[...] = normal.astype(BF)
    half_ref[:, :, :feature] = turn(first_ref, normal).reshape(KEPT, 2 * GROUP, feature)
    ones = jnp.broadcast_to(live, (CELLS, LANES)).astype(BF)
    half_ref[:, :, feature:] = (mm(first_ref[0], ones) + mm(first_ref[1], ones)).reshape(KEPT, 2 * GROUP, LANES)


def first(rows, cols, tokens, tables, deps=()):
    cells, feature = tokens.shape
    table = tables["first"]
    return launch(
        deps,
        first_kernel,
        grid=(STEPS,),
        out_shape=(
            jax.ShapeDtypeStruct((KEPT, 2 * ROWS, feature + LANES), F32),
            jax.ShapeDtypeStruct((cells, feature), BF),
        ),
        in_specs=[smem(), smem(), pl.BlockSpec((CELLS, feature), lambda i: (i, 0)), single(table.shape)],
        out_specs=(
            pl.BlockSpec((KEPT, 2 * GROUP, feature + LANES), lambda i: (0, i, 0)),
            pl.BlockSpec((CELLS, feature), lambda i: (i, 0)),
        ),
        compiler_params=params(),
        cost_estimate=cost(6e9, 11e6),
        name="first",
    )(rows, cols, tokens, table)


def build_mix(me, bits, weights_ref, layer, out_ref, feature):
    block = feature // BLOCKS
    half = feature // 2
    per_group = BLOCKS // 2
    share = 2 * feature // weights_ref.shape[0]
    each = block // share
    out_ref[...] = jnp.zeros_like(out_ref)
    row = lax.broadcasted_iota(jnp.int32, (LANES, half), 0)
    column = lax.broadcasted_iota(jnp.int32, (LANES, half), 1)
    for b in range(per_group):
        shift = jnp.where((column - b * block == row) & (row < block), 1.0, 0.0).astype(BF)
        low, high = b * block, (b + 1) * block
        for group in range(2):
            for part in range(2):
                at = (part * BLOCKS + group * per_group + b) * each
                pieces = [
                    weights_ref[place_of((at + k) ^ me, bits), layer * share : (layer + 1) * share, :]
                    for k in range(each)
                ]
                placed = mm(jnp.concatenate(pieces, axis=0), shift).astype(BF)
                for t in range(low // LANES, (high - 1) // LANES + 1):
                    begin, end = max(low, t * LANES), min(high, (t + 1) * LANES)
                    for c in range(low // LANES, (high - 1) // LANES + 1):
                        piece = placed[begin - low : end - low, c * LANES : (c + 1) * LANES]
                        for up in range(2):
                            top = 2 * t * LANES + up * LANES + begin - t * LANES
                            left = (2 * c + (up ^ part)) * LANES
                            value = -piece if part == 1 and up == 1 else piece
                            here = (group, slice(top, top + end - begin), slice(left, left + LANES))
                            out_ref[here] = out_ref[here] + value


def to_modes(half_ref, head_ref, body_ref, is_head):
    width = half_ref.shape[2]
    real, imag, ends = [], [], ()
    for k in range(TAKE):
        begin = is_head and k == 0
        rows = HEAD if begin else BODY
        spec = turn(head_ref if begin else body_ref, half_ref[k * GROUP : (k + 1) * GROUP].reshape(2 * BODY, width))
        real.append(spec[:BODY])
        imag.append(spec[rows : rows + BODY])
        if begin:
            ends = (spec[BODY:rows], spec[rows + BODY :])
    if is_head:
        real.append(ends[0])
        imag.append(ends[1])
    return jnp.concatenate(real, axis=0), jnp.concatenate(imag, axis=0)


def from_modes(pair_of, head_ref, body_ref, is_head, out_ref):
    for k in range(TAKE):
        begin = is_head and k == 0
        parts = []
        for part in pair_of:
            parts.append(part[k * BODY : (k + 1) * BODY])
            if begin:
                parts.append(part[TOOK:])
        result = turn(head_ref if begin else body_ref, jnp.concatenate(parts, axis=0))
        out_ref[k * GROUP : (k + 1) * GROUP] = result.reshape(GROUP, 2 * ROWS, result.shape[1])


def mix_step(half_ref, head_ref, body_ref, back_head_ref, back_body_ref, mix1_ref, mix2_ref, wide_ref, long_ref,
             outs, heads, out_ref, is_head):
    feature = out_ref.shape[2]
    specs = to_modes(half_ref, head_ref, body_ref, is_head)
    gain = wide_ref[0:1, :]
    shift = wide_ref[1:2, :]

    def scaled(part):
        flat = jnp.concatenate([part[:, feature:]] * (feature // LANES), axis=1)
        return (part[:, :feature] * gain + flat * shift).astype(BF)

    inside = to_mixed(*(scaled(part) for part in specs))
    active, slope = gelu_parts(mix_product(inside, mix1_ref) + long_ref[0:1, :])
    hidden = active.astype(BF)
    value = mix_product(hidden, mix2_ref) + long_ref[1:2, :]
    bend = jnp.tanh(value / SHRINK)
    flat = jnp.concatenate([part[:, feature:] for part in specs], axis=1)
    for ref, head, kept in zip(outs, heads, (inside, hidden, slope, bend * bend, flat)):
        ref[...] = kept[:TOOK]
        if is_head:
            head[...] = kept[TOOK:]
    from_modes(from_mixed(value - SHRINK * bend), back_head_ref, back_body_ref, is_head, out_ref)


def mix_first_kernel(
    weight_bits, vector_bits, me_ref, half_ref, weights_ref, vector_in_ref, head_ref, body_ref, back_head_ref, back_body_ref,
    out_ref, low_ref, hidden_ref, slope_ref, bend_ref, flat_ref,
    low_head_ref, hidden_head_ref, slope_head_ref, bend_head_ref, flat_head_ref, mix1_ref, mix2_ref, wide_ref, long_ref, up_ref,
    vector_ref,
):
    feature = out_ref.shape[2]
    devices = vector_ref.shape[1]
    share = feature // devices
    step = pl.program_id(0)
    outs = (low_ref, hidden_ref, slope_ref, bend_ref, flat_ref)
    heads = (low_head_ref, hidden_head_ref, slope_head_ref, bend_head_ref, flat_head_ref)
    work = functools.partial(
        mix_step, half_ref, head_ref, body_ref, back_head_ref, back_body_ref, mix1_ref, mix2_ref, wide_ref, long_ref,
        outs, heads, out_ref,
    )

    @pl.when(step == 0)
    def _():
        me = me_ref[0]
        if vector_in_ref.shape == vector_ref.shape:
            vector_ref[...] = vector_in_ref[...]
        else:
            rows = weights_ref[:, 4 * share :, :].astype(F32)
            for d in range(devices):
                for k in range(vector_ref.shape[0]):
                    vector_ref[k, d : d + 1, :] = rows[d, k : k + 1, :]
        build_mix(me, weight_bits, weights_ref, 0, mix1_ref, feature)
        build_mix(me, weight_bits, weights_ref, 1, mix2_ref, feature)
        wide_ref[...] = jnp.zeros_like(wide_ref)
        long_ref[...] = jnp.zeros_like(long_ref)
        for row, at in enumerate((2, 3, 4, 5, 7)):
            wide_ref[row : row + 1, :] = spread(vector_ref[at], share, me, vector_bits)
        for row in range(2):
            both = spread(vector_ref[row], 2 * share, me, vector_bits)
            long_ref[row : row + 1, :] = to_mixed(both[:, :feature], both[:, feature:])
        up_ref[...] = spread(vector_ref[6], up_ref.shape[1] // devices, me, vector_bits)
        work(True)

    @pl.when(step > 0)
    def _():
        work(False)


def mix_second_kernel(
    half_ref, mix1_ref, mix2_ref, wide_ref, long_ref, body_ref, back_body_ref,
    out_ref, *outs,
):
    mix_step(
        half_ref, None, body_ref, None, back_body_ref, mix1_ref, mix2_ref, wide_ref, long_ref,
        outs, (None,) * 5, out_ref, False,
    )


def mode_shapes(rows, feature):
    wide = [jax.ShapeDtypeStruct((rows, 2 * feature), kind) for kind in (BF, BF, F32, F32)]
    return wide + [jax.ShapeDtypeStruct((rows, 2 * LANES), F32)]


def mode_blocks(feature):
    return [pl.BlockSpec((TOOK, width), lambda i: (i, 0)) for width in (2 * feature,) * 4 + (2 * LANES,)]


def half_block(width, begin=0):
    return pl.BlockSpec((TAKE * GROUP, 2 * ROWS, width), lambda i: (i + begin, 0, 0))


def mix_first(me, half, weights, vectors, tables, hidden, steps, weight_bits, vector_bits, deps=()):
    feature = half.shape[2] - LANES
    fixed = (weights, vectors, tables["head"], tables["body"], tables["head_wt"], tables["body_wt"])
    more = (
        jax.ShapeDtypeStruct((2, feature, feature), BF),
        jax.ShapeDtypeStruct((2, feature, feature), BF),
        jax.ShapeDtypeStruct((8, feature), F32),
        jax.ShapeDtypeStruct((8, 2 * feature), F32),
        jax.ShapeDtypeStruct((1, hidden), F32),
    )
    heads = mode_shapes(ROWS, feature)
    devices = vectors.shape[1] if vectors.shape[1] > 1 else weights.shape[0]
    return launch(
        deps,
        functools.partial(mix_first_kernel, weight_bits, vector_bits),
        grid=(steps,),
        out_shape=[jax.ShapeDtypeStruct((TAKE * GROUP * steps, 2 * ROWS, feature), F32)]
        + mode_shapes(TOOK * steps, feature) + heads + list(more),
        in_specs=[smem(), half_block(feature + LANES)] + [single(v.shape) for v in fixed],
        out_specs=[half_block(feature)] + mode_blocks(feature) + [single(v.shape) for v in heads]
        + [single(v.shape) for v in more],
        scratch_shapes=[pltpu.VMEM((8, devices, LANES), F32)],
        compiler_params=params(),
        cost_estimate=cost(9e9, 20e6),
        name="mix_first",
    )(me, half, *fixed)


def mix_second(half, mix1, mix2, wide, long, tables, begin, steps, deps=()):
    feature = half.shape[2] - LANES
    fixed = (mix1, mix2, wide, long, tables["body"], tables["body_wt"])
    return launch(
        deps,
        mix_second_kernel,
        grid=(steps,),
        out_shape=[jax.ShapeDtypeStruct((TAKE * GROUP * steps, 2 * ROWS, feature), F32)] + mode_shapes(TOOK * steps, feature),
        in_specs=[half_block(feature + LANES, begin)] + [single(v.shape) for v in fixed],
        out_specs=[half_block(feature)] + mode_blocks(feature),
        compiler_params=params(),
        cost_estimate=cost(9e9, 20e6),
        name="mix_second",
    )(half, *fixed)


def space_kernel(rows_ref, cols_ref, half1_ref, half2_ref, tokens_ref, first_t_ref, wide_ref, middle_ref, normed_ref):
    feature = tokens_ref.shape[1]
    flat = lambda ref: ref[...].reshape(-1, feature)
    spatial = turn(first_t_ref, jnp.concatenate([flat(half1_ref), flat(half2_ref)], axis=0))
    inputs = tokens_ref[...].astype(F32)
    live = live_rows(pl.program_id(0) * CELLS, CELLS, rows_ref, cols_ref)
    normal, _ = normalize(inputs)
    middle = inputs + live * (spatial + (normal * wide_ref[0:1, :] + wide_ref[1:2, :]))
    middle_ref[...] = middle
    normal, _ = normalize(middle)
    normed_ref[...] = (normal * wide_ref[2:3, :] + wide_ref[3:4, :]).astype(BF)


def column_block(rows, width):
    return pl.BlockSpec((rows, 2 * GROUP, width), lambda i: (0, i, 0))


def space(rows, cols, half1, half2, tokens, wide, tables, deps=()):
    cells, feature = tokens.shape
    table = tables["first_t"]
    block = pl.BlockSpec((CELLS, feature), lambda i: (i, 0))
    return launch(
        deps,
        space_kernel,
        grid=(STEPS,),
        out_shape=(jax.ShapeDtypeStruct((cells, feature), F32), jax.ShapeDtypeStruct((cells, feature), BF)),
        in_specs=[smem(), smem(), column_block(half1.shape[0], feature), column_block(half2.shape[0], feature),
                  block, single(table.shape), single(wide.shape)],
        out_specs=(block, block),
        compiler_params=params(),
        cost_estimate=cost(6e9, 20e6),
        name="space",
    )(rows, cols, half1, half2, tokens, table, wide)


def fetch_weights(me_ref, pieces, places, up_ref, down_ref, sems):
    each = pieces[0].shape[0]
    held = len(pieces) // 2
    count = each * held
    chip = me_ref[0] // 2

    def copies(own, core):
        target = (up_ref, down_ref)[core]
        source = pieces[:held] if own else pieces[held:]
        for mask in range(count):
            at = places[core][mask]
            part = source[at // each].at[at % each]
            yield pltpu.make_async_copy(part, target.at[chip ^ mask], sems.at[core, mask])

    for core in range(2):
        @pl.when(me_ref[0] % 2 == core)
        def _():
            for copy in copies(True, core):
                copy.start()
            for copy in copies(False, 1 - core):
                copy.start()

    def arrived(core):
        for copy in copies(True, core):
            copy.wait()

    return arrived


def weight_scratch(pieces):
    chips, rows, feature = UNITS, pieces[0].shape[1], pieces[0].shape[2]
    return [
        pltpu.VMEM((chips, rows, feature), BF),
        pltpu.VMEM((chips, rows, feature), BF),
        pltpu.SemaphoreType.DMA((2, chips)),
    ]


def up_part(up_ref, j, feature):
    share = up_ref.shape[1] * feature // (up_ref.shape[0] * up_ref.shape[1])
    return up_ref[:, j * share : (j + 1) * share, :].reshape(feature, feature)


def down_part(down_ref, j, feature):
    share = down_ref.shape[1]
    each = feature // share
    return down_ref[j * each : (j + 1) * each].reshape(feature, feature)


def up_kernel(places, rows_ref, cols_ref, me_ref, normed_ref, grad_ref, bias_ref, *rest):
    pieces = rest[:-10]
    active_ref, pre_ref, live_ref, bias_grad_ref, up_all_ref, down_all_ref, up_ref, down_ref, sems, out_sems = rest[-10:]
    tile, feature = normed_ref.shape
    step = pl.program_id(0)
    copies = [
        pltpu.make_async_copy(source, target, out_sems.at[k])
        for k, (source, target) in enumerate(((up_ref, up_all_ref), (down_ref, down_all_ref)))
    ]

    def work(arrived):
        live = live_rows(step * tile, tile, rows_ref, cols_ref)
        branch = (grad_ref[...].astype(F32) * live).astype(BF)
        live_ref[...] = branch
        normed = normed_ref[...]
        if arrived:
            arrived(0)
            copies[0].start()
        for j in range(active_ref.shape[1] // feature):
            place = slice(j * feature, (j + 1) * feature)
            value = mm(normed, up_part(up_ref, j, feature)) + bias_ref[:, place]
            if arrived and j == 0:
                arrived(1)
                copies[1].start()
            grad = mm(branch, down_part(down_ref, j, feature), (1, 1))
            active, slope = gelu_parts(value)
            active_ref[:, place] = active.astype(BF)
            low = (grad * slope).astype(BF)
            pre_ref[:, place] = low
            bias_grad_ref[:, place] += jnp.sum(low.astype(F32), axis=0, keepdims=True)

    @pl.when(step == 0)
    def _():
        bias_grad_ref[...] = jnp.zeros_like(bias_grad_ref)
        work(fetch_weights(me_ref, pieces, places, up_ref, down_ref, sems))

    @pl.when(step > 0)
    def _():
        work(None)

    @pl.when(step == pl.num_programs(0) - 1)
    def _():
        for copy in copies:
            copy.wait()


def feed_up(rows, cols, me, normed, grad, bias, pieces, places, tile=256, deps=()):
    cells, feature = normed.shape
    hidden = bias.shape[1]
    block = lambda width: pl.BlockSpec((tile, width), lambda i: (i, 0))
    weights = jax.ShapeDtypeStruct((UNITS,) + pieces[0].shape[1:], BF)
    return launch(
        deps,
        functools.partial(up_kernel, places),
        grid=(cells // tile,),
        out_shape=(
            jax.ShapeDtypeStruct((cells, hidden), BF),
            jax.ShapeDtypeStruct((cells, hidden), BF),
            jax.ShapeDtypeStruct((cells, feature), BF),
            jax.ShapeDtypeStruct((1, hidden), F32),
            weights,
            weights,
        ),
        in_specs=[smem(), smem(), smem(), block(feature), block(feature), single(bias.shape)]
        + [any_space() for _ in pieces],
        out_specs=(block(hidden), block(hidden), block(feature), single((1, hidden)), any_space(), any_space()),
        scratch_shapes=weight_scratch(pieces) + [pltpu.SemaphoreType.DMA((2,))],
        compiler_params=params(),
        cost_estimate=cost(0, 0),
        name="feed_up",
    )(rows, cols, me, normed, grad, bias, *pieces)


def weight_grad_kernel(places, me_ref, active_ref, pre_ref, branch_ref, normed_ref, send_ref, keep_ref, stage_ref, sems):
    step = pl.program_id(0)
    steps = pl.num_programs(0) // 2
    feature = branch_ref.shape[1]
    chips, rows, _ = send_ref.shape
    each = feature // rows
    share = feature // chips

    def down_copies(j, target):
        for c in range(each):
            source = stage_ref.at[j, pl.ds(c * rows, rows)]
            yield pltpu.make_async_copy(source, target.at[places[1][j * each + c]], sems.at[j, c])

    def up_copies(j, target):
        for c in range(chips):
            source = stage_ref.at[steps + j, pl.ds(c * share, share)]
            there = target.at[places[0][c], pl.ds(j * share, share)]
            yield pltpu.make_async_copy(source, there, sems.at[steps + j, c])

    @pl.when(step < steps)
    def _():
        stage_ref[step] = mm(active_ref[...], branch_ref[...], (0, 0)).astype(BF)

    @pl.when(step >= steps)
    def _():
        stage_ref[step] = mm(normed_ref[...], pre_ref[...], (0, 0)).astype(BF)

    total = stage_ref.shape[0] // 2
    for j in range(total):
        for core in range(2):
            targets = (send_ref, keep_ref) if core == 0 else (keep_ref, send_ref)

            @pl.when((step == j) & (me_ref[0] % 2 == core))
            def _():
                for copy in down_copies(j, targets[0]):
                    copy.start()

            @pl.when((step == total + j) & (me_ref[0] % 2 == core))
            def _():
                for copy in up_copies(j, targets[1]):
                    copy.start()

    @pl.when(step == 2 * steps - 1)
    def _():
        for j in range(total):
            for copy in down_copies(j, send_ref):
                copy.wait()
            for copy in up_copies(j, send_ref):
                copy.wait()


def weight_grads(me, active, pre, branch, normed, places, deps=()):
    cells, hidden = active.shape
    feature = branch.shape[1]
    tiles = hidden // feature
    chips = UNITS
    shape = jax.ShapeDtypeStruct((chips, hidden // chips, feature), BF)
    return launch(
        deps,
        functools.partial(weight_grad_kernel, places),
        grid=(2 * tiles,),
        out_shape=(shape, shape),
        in_specs=[
            smem(),
            pl.BlockSpec((cells, feature), lambda i: (0, jnp.minimum(i, tiles - 1))),
            pl.BlockSpec((cells, feature), lambda i: (0, jnp.maximum(i - tiles, 0))),
            single(branch.shape), single(normed.shape),
        ],
        out_specs=(any_space(), any_space()),
        scratch_shapes=[
            pltpu.VMEM((2 * tiles, feature, feature), BF),
            pltpu.SemaphoreType.DMA((2 * tiles, chips)),
        ],
        compiler_params=params(),
        cost_estimate=cost(4 * cells * feature * hidden, 40e6),
        name="weight_grads",
    )(me, active, pre, branch, normed)


def down_kernel(rows_ref, cols_ref, active_ref, pre_ref, middle_ref, grad_ref, normal_ref, wide_ref, first_ref,
                up_ref, down_ref, mixed_ref, grad_middle_ref, half_ref, sums_ref):
    tile, feature = middle_ref.shape
    hidden = active_ref.shape[1]
    step = pl.program_id(0)

    @pl.when(step == 0)
    def _():
        sums_ref[...] = jnp.zeros_like(sums_ref)

    live = live_rows(step * tile, tile, rows_ref, cols_ref)
    branch = mm(active_ref[...], down_ref[...].reshape(hidden, feature))
    grad_normed = jnp.zeros((tile, feature), F32)
    for j in range(hidden // feature):
        pre = pre_ref[:, j * feature : (j + 1) * feature]
        grad_normed = grad_normed + mm(pre, up_part(up_ref, j, feature), (1, 1))
    middle = middle_ref[...]
    mixed_ref[...] = (middle + live * (branch + wide_ref[4:5, :])).astype(BF)
    normal, inverse = normalize(middle)
    cotangent = grad_ref[...].astype(F32)
    grad_middle = cotangent + norm_back(grad_normed, wide_ref[2:3, :], normal, inverse)
    grad_middle_ref[...] = grad_middle
    masked = grad_middle * live
    half_ref[...] = turn(first_ref, masked).reshape(half_ref.shape)
    rows = (grad_normed * normal, grad_normed, cotangent * live, masked * normal_ref[...].astype(F32), masked)
    for row, value in enumerate(rows):
        sums_ref[row : row + 1, :] += jnp.sum(value, axis=0, keepdims=True)


def feed_down(rows, cols, active, pre, middle, grad, normal, wide, table, up, down, deps=()):
    cells, feature = middle.shape
    hidden = active.shape[1]
    block = lambda width: pl.BlockSpec((CELLS, width), lambda i: (i, 0))
    operands = (rows, cols, active, pre, middle, grad, normal, wide, table, up, down)
    return launch(
        deps,
        down_kernel,
        grid=(cells // CELLS,),
        out_shape=(
            jax.ShapeDtypeStruct((cells, feature), BF),
            jax.ShapeDtypeStruct((cells, feature), F32),
            jax.ShapeDtypeStruct((KEPT, 2 * ROWS, feature), F32),
            jax.ShapeDtypeStruct((8, feature), F32),
        ),
        in_specs=[smem(), smem(), block(hidden), block(hidden), block(feature), block(feature), block(feature)]
        + [single(v.shape) for v in operands[7:]],
        out_specs=(block(feature), block(feature), column_block(KEPT, feature), single((8, feature))),
        compiler_params=params(),
        cost_estimate=cost(0, 0),
        name="feed_down",
    )(*operands)


def back_step(half_ref, head_ref, body_ref, back_head_ref, back_body_ref, mix1_ref, mix2_ref, ins, in_heads,
              outs, out_heads, out_ref, sums_ref, is_head):
    feature = out_ref.shape[2]

    def read(k):
        if is_head:
            return jnp.concatenate([ins[k][...], in_heads[k][...]], axis=0)
        return ins[k][...]

    grads = to_modes(half_ref, head_ref, body_ref, is_head)
    grad_two = (to_mixed(*grads) * read(1)).astype(BF)
    grad_one = (mix_product(grad_two, mix2_ref, True) * read(0)).astype(BF)
    grad_spec = mix_product(grad_one, mix1_ref, True)
    from_modes(from_mixed(grad_spec), back_head_ref, back_body_ref, is_head, out_ref)
    for row, value in enumerate((grad_one, grad_two)):
        outs[row][...] = value[:TOOK]
        if is_head:
            out_heads[row][...] = value[TOOK:]
    flat = jnp.concatenate([read(3)] * (feature // LANES), axis=1)
    for row, value in enumerate((grad_one.astype(F32), grad_two.astype(F32), grad_spec * read(2).astype(F32), grad_spec * flat)):
        total = jnp.sum(value, axis=0, keepdims=True)
        sums_ref[row : row + 1, :] = total if is_head else sums_ref[row : row + 1, :] + total


def mix_back_kernel(
    half_ref, slope1_ref, slope2_ref, bend1_ref, bend2_ref, low1_ref, low2_ref, flat1_ref, flat2_ref,
    slope_head_ref, bend_head_ref, low_head_ref, flat_head_ref, mix1_ref, mix2_ref,
    head_ref, body_ref, back_head_ref, back_body_ref,
    out_ref, one_ref, two_ref, one_head_ref, two_head_ref, sums_ref,
):
    step = pl.program_id(0)
    steps = pl.num_programs(0) // 2
    work = functools.partial(
        back_step, half_ref, head_ref, body_ref, back_head_ref, back_body_ref, mix1_ref, mix2_ref
    )
    heads = (slope_head_ref, bend_head_ref, low_head_ref, flat_head_ref)
    more = (heads, (one_ref, two_ref), (one_head_ref, two_head_ref), out_ref, sums_ref)
    near = (slope1_ref, bend1_ref, low1_ref, flat1_ref)
    far = (slope2_ref, bend2_ref, low2_ref, flat2_ref)

    @pl.when(step == 0)
    def _():
        sums_ref[...] = jnp.zeros_like(sums_ref)
        work(near, *more, True)

    @pl.when((step > 0) & (step < steps))
    def _():
        work(near, *more, False)

    @pl.when(step >= steps)
    def _():
        work(far, *more, False)


def mix_back(half, modes1, modes2, heads, mix1, mix2, tables, deps=()):
    feature = half.shape[2]
    steps = KEPT // GROUP // TAKE
    fixed = tuple(heads[k] for k in (2, 3, 0, 4)) + (
        mix1, mix2, tables["head_w"], tables["body_w"], tables["head_t"], tables["body_t"]
    )
    moving = []
    specs = []
    for k in (2, 3, 0, 4):
        width = modes1[k].shape[1]
        moving += [modes1[k], modes2[k]]
        specs += [
            pl.BlockSpec((TOOK, width), lambda i: (jnp.minimum(i, steps // 2 - 1), 0)),
            pl.BlockSpec((TOOK, width), lambda i: (jnp.maximum(i - steps // 2, 0), 0)),
        ]
    low = lambda rows: jax.ShapeDtypeStruct((rows, 2 * feature), BF)
    body = pl.BlockSpec((TOOK, 2 * feature), lambda i: (i, 0))
    shapes = (
        jax.ShapeDtypeStruct((KEPT, 2 * ROWS, feature), F32), low(TOOK * steps), low(TOOK * steps),
        low(ROWS), low(ROWS), jax.ShapeDtypeStruct((8, 2 * feature), F32),
    )
    return launch(
        deps,
        mix_back_kernel,
        grid=(steps,),
        out_shape=shapes,
        in_specs=[half_block(feature)] + specs + [single(v.shape) for v in fixed],
        out_specs=[half_block(feature), body, body] + [single(v.shape) for v in shapes[3:]],
        compiler_params=params(),
        cost_estimate=cost(18e9, 30e6),
        name="mix_back",
    )(half, *moving, *fixed)


def block_kernel(left1_ref, left2_ref, left_head_ref, right_ref, right_head_ref, out_ref, natural_ref):
    wide = 2 * LANES
    count = left1_ref.shape[1] // wide
    cut = left1_ref.shape[0]
    for t in range(count):
        for c in range(max(t - 1, 0), min(t + 2, count)):
            left, right = slice(t * wide, (t + 1) * wide), slice(c * wide, (c + 1) * wide)
            total = (
                mm(left1_ref[:, left], right_ref[:cut, right], (0, 0))
                + mm(left2_ref[:, left], right_ref[cut:, right], (0, 0))
                + mm(left_head_ref[:, left], right_head_ref[:, right], (0, 0))
            )
            rows, lanes = slice(t * LANES, (t + 1) * LANES), slice(c * LANES, (c + 1) * LANES)
            natural_ref[0, rows, lanes] = total[:LANES, :LANES] + total[LANES:, LANES:]
            natural_ref[1, rows, lanes] = total[:LANES, LANES:] - total[LANES:, :LANES]
    per_group = BLOCKS // 2
    block = count * LANES // per_group
    for b in range(per_group):
        begin = b * block
        base = begin // LANES * LANES
        reach = min(base + wide, count * LANES) - base
        for part in range(2):
            piece = natural_ref[part, begin : begin + block, base : base + reach]
            if begin > base:
                piece = pltpu.roll(piece, reach - (begin - base), axis=1)
            out_ref[part, b * block : (b + 1) * block, :] = piece[:, :LANES]


def block_grads(left1, left2, left_head, right, right_head, name, deps=()):
    feature = left1.shape[1] // 2
    half = feature // 2
    block = lambda v: pl.BlockSpec((v.shape[0], feature), lambda i: (0, i))
    return launch(
        deps,
        block_kernel,
        grid=(2,),
        out_shape=jax.ShapeDtypeStruct((2, feature, LANES), F32),
        in_specs=[block(v) for v in (left1, left2, left_head, right, right_head)],
        out_specs=pl.BlockSpec((2, half, LANES), lambda i: (0, i, 0)),
        scratch_shapes=[pltpu.VMEM((2, half, half), F32)],
        compiler_params=params(),
        cost_estimate=cost(5e9, 7e6),
        name=name,
    )(left1, left2, left_head, right, right_head)


def last_kernel(begin, rows_ref, cols_ref, half_ref, tokens_ref, grad_ref, first_t_ref, wide_ref, *rest):
    out_ref = rest[-1]
    tile, feature = tokens_ref.shape
    live = live_rows((pl.program_id(0) + begin) * tile, tile, rows_ref, cols_ref)
    grad_middle = grad_ref[...]
    grad_normed = live * (grad_middle + turn(first_t_ref, half_ref[...].reshape(CELLS, feature)))
    normal, inverse = normalize(tokens_ref[...].astype(F32))
    out_ref[...] = grad_middle + norm_back(grad_normed, wide_ref[0:1, :], normal, inverse)


def last(rows, cols, half, tokens, grad, wide, tables, begin, steps, before=(), deps=()):
    cells, feature = tokens.shape
    first_t = tables["first_t"]
    block = pl.BlockSpec((CELLS, feature), lambda i: (i + begin, 0))
    operands = (rows, cols, half, tokens, grad, first_t, wide)
    return launch(
        deps,
        functools.partial(last_kernel, begin),
        grid=(steps,),
        out_shape=jax.ShapeDtypeStruct((cells, feature), F32),
        in_specs=[smem(), smem(), pl.BlockSpec((KEPT, 2 * GROUP, feature), lambda i: (0, i + begin, 0)), block, block,
                  single(first_t.shape), single(wide.shape)] + [any_space() for _ in before],
        out_specs=block,
        input_output_aliases={len(operands): 0} if before else {},
        compiler_params=params(),
        cost_estimate=cost(6e9, 20e6),
        name="last",
    )(*operands, *before)


def collect(value, per_device, devices):
    total = value.shape[1]
    owner = lax.broadcasted_iota(jnp.int32, (devices, total), 1) // per_device
    row = lax.broadcasted_iota(jnp.int32, (devices, total), 0)
    high, low = split(jnp.where(owner == row, jnp.broadcast_to(value, (devices, total)), 0.0))
    place = lax.broadcasted_iota(jnp.int32, (total, LANES), 0)
    lane = lax.broadcasted_iota(jnp.int32, (total, LANES), 1)
    pick = jnp.where(place % per_device == lane, 1.0, 0.0).astype(BF)
    return mm(high, pick) + mm(low, pick)


def emit(place, sum_ref, send_refs, keep_ref):
    half, _, rows, _ = sum_ref.shape
    rows = rows - 8
    for k, send_ref in enumerate(send_refs):
        away = sum_ref[:, pl.ds(place ^ (k + 1), 1)].reshape(half, rows + 8, LANES)
        high, low = split(away[:, rows:])
        send_ref[:, :rows] = away[:, :rows].astype(BF)
        send_ref[:, rows:] = jnp.concatenate([high.astype(F32), low.astype(F32)], axis=1).astype(BF)
    keep_ref[...] = sum_ref[:, pl.ds(place, 1)].reshape(half, rows + 8, LANES)


def pack_kernel(place_ref, one_ref, two_ref, mixed_ref, sums_ref, up_ref, wide_ref, send_ref, keep_ref, sum_ref):
    half, _, rows, _ = sum_ref.shape
    devices = 2 * half
    share = (rows - 8) // 4
    feature = sums_ref.shape[1]
    sum_ref[:, :, : 2 * share] = one_ref[...].reshape(half, 2, 2 * share, LANES)
    sum_ref[:, :, 2 * share : 4 * share] = two_ref[...].reshape(half, 2, 2 * share, LANES)
    first_gain, first_bias = scale_grads(mixed_ref, sums_ref, wide_ref)
    natural = [jnp.concatenate(from_mixed(mixed_ref[k : k + 1, :]), axis=1) for k in range(2)]
    narrow = [first_gain, first_bias] + [sums_ref[k : k + 1, :] for k in range(3)]
    for k, value in enumerate(narrow + natural + [up_ref[...]]):
        placed = collect(value, value.shape[1] // devices, devices)
        for d in range(devices):
            sum_ref[d // 2, d % 2, 4 * share + k : 4 * share + k + 1, :] = placed[d : d + 1, :]
    emit(place_ref[0], sum_ref, (send_ref,), keep_ref)


def scale_grads(mixed_ref, sums_ref, wide_ref):
    real, imag = from_mixed(mixed_ref[2:3, :])
    scaled = real + imag
    real, imag = from_mixed(mixed_ref[3:4, :])
    flat = real + imag
    gain = sums_ref[3:4, :] + (scaled - wide_ref[1:2, :] * flat) / wide_ref[0:1, :]
    return gain, sums_ref[4:5, :] + flat


def small_shapes(half, rows, others):
    shapes = [jax.ShapeDtypeStruct((half, rows + 8, LANES), BF)] * others
    return shapes + [jax.ShapeDtypeStruct((half, rows, LANES), F32)]


def pack(upper, one, two, mixed, sums, up, wide, devices):
    rows = 2 * one.shape[0] * one.shape[1] // devices + 8
    shapes = small_shapes(devices // 2, rows, 1)
    operands = (one, two, mixed, sums, up, wide)
    return pl.pallas_call(
        pack_kernel,
        out_shape=shapes,
        in_specs=[smem()] + vmem(len(operands)),
        out_specs=vmem(2),
        scratch_shapes=[pltpu.VMEM((devices // 2, 2, rows, LANES), F32)],
        compiler_params=params(),
        cost_estimate=cost(0, 0),
        name="pack",
    )(upper, *operands)


def merge_small(keep_ref, got_refs):
    rows = keep_ref.shape[1] - 8
    top, tail = keep_ref[:, :rows], keep_ref[:, rows:]
    for got_ref in got_refs:
        both = got_ref[:, rows:].astype(F32)
        top = top + got_ref[:, :rows].astype(F32)
        tail = tail + (both[:, :8] + both[:, 8:])
    return top, tail


def fold_small_kernel(others, place_ref, keep_ref, *rest):
    sum_ref = rest[-1]
    send_refs, out_ref = rest[-2 - others : -2], rest[-2]
    half, count, rows, _ = sum_ref.shape
    top, tail = merge_small(keep_ref, rest[: len(rest) - 2 - others])
    sum_ref[:, :, : rows - 8] = top.reshape(half, count, rows - 8, LANES)
    sum_ref[:, :, rows - 8 :] = tail.reshape(half, count, 8, LANES)
    emit(place_ref[0], sum_ref, send_refs, out_ref)


def fold_small(keep, got, place, count, deps=()):
    half, rows = keep.shape[0] // count, keep.shape[1]
    shapes = small_shapes(half, rows, count - 1)
    return launch(
        deps,
        functools.partial(fold_small_kernel, count - 1),
        out_shape=shapes,
        in_specs=[smem()] + vmem(1 + len(got)),
        out_specs=vmem(len(shapes)),
        scratch_shapes=[pltpu.VMEM((half, count, rows, LANES), F32)],
        compiler_params=params(),
        cost_estimate=cost(0, 0),
        name="fold_small",
    )(place, keep, *got)


def vmem(count):
    return [pl.BlockSpec(memory_space=pltpu.VMEM)] * count


def end_small_kernel(others, keep_ref, *rest):
    got_refs, (one_ref, two_ref, *rows_refs) = rest[:others], rest[others:]
    top, tail = merge_small(keep_ref, got_refs)
    share, block = one_ref.shape
    one_ref[...] = top[0, :share, :block]
    two_ref[...] = top[0, share:, :block]
    for row, ref in enumerate(rows_refs):
        ref[...] = tail[0, row : row + 1, : ref.shape[1]]


def end_small(keep, got, share, block, widths):
    shapes = [jax.ShapeDtypeStruct((share, block), F32)] * 2
    shapes += [jax.ShapeDtypeStruct((1, width), F32) for width in widths]
    return pl.pallas_call(
        functools.partial(end_small_kernel, len(got)),
        out_shape=shapes,
        in_specs=vmem(1 + len(got)),
        out_specs=vmem(len(shapes)),
        compiler_params=params(),
        cost_estimate=cost(0, 0),
        name="end_small",
    )(keep, *got)


def begin_small_kernel(one_ref, two_ref, *rest):
    out_ref, rows_ref = rest[-2:]
    share, block = one_ref.shape
    out_ref[...] = jnp.zeros_like(out_ref)
    rows_ref[...] = jnp.zeros_like(rows_ref)
    out_ref[0, :share, :block] = one_ref[...]
    out_ref[0, share : 2 * share, :block] = two_ref[...]
    for row, ref in enumerate(rest[:-2]):
        rows_ref[row : row + 1, : ref.shape[1]] = ref[...].astype(F32)
    out_ref[0, 2 * share :, :] = rows_ref[...].astype(BF)


def begin_small(one, two, vectors):
    share = one.shape[0]
    operands = (one, two) + tuple(v[None] for v in vectors)
    return pl.pallas_call(
        begin_small_kernel,
        out_shape=jax.ShapeDtypeStruct((1, 2 * share + 16, LANES), BF),
        in_specs=vmem(len(operands)),
        out_specs=vmem(1)[0],
        scratch_shapes=[pltpu.VMEM((16, LANES), F32)],
        compiler_params=params(),
        cost_estimate=cost(0, 0),
        name="begin_small",
    )(*operands)


AXES = ("dp", "fsdp")


def swap(value, devices, bits):
    return lax.ppermute(value, AXES, [(i, i ^ (1 << bits[i & 1])) for i in range(devices)])


def doubling_orders(count):
    first = list(range(count - 1, 0, -1))
    second = list(first)
    for k in range(0, len(second) - 1, 2):
        second[k], second[k + 1] = second[k + 1], second[k]
    return first, second


def places_of(order):
    return [
        sum(1 << k for k, bit in enumerate(order) if mask >> (bit - 1) & 1) for mask in range(1 << len(order))
    ]


def join_kernel(*refs):
    out_ref = refs[-1]
    count = refs[0].shape[0]
    for k, ref in enumerate(refs[:-1]):
        out_ref[k * count : (k + 1) * count] = ref[...]


def join_rows(*pieces, deps=()):
    shape = jax.ShapeDtypeStruct((len(pieces) * pieces[0].shape[0],) + pieces[0].shape[1:], pieces[0].dtype)
    return launch(
        deps,
        join_kernel,
        out_shape=shape,
        in_specs=[pl.BlockSpec(memory_space=pltpu.VMEM) for _ in pieces],
        out_specs=pl.BlockSpec(memory_space=pltpu.VMEM),
        compiler_params=params(),
        cost_estimate=cost(0, 0),
        name="join",
    )(*pieces)


def hold(value, deps):
    def body(*refs):
        pass

    return pl.pallas_call(
        body,
        out_shape=jax.ShapeDtypeStruct(value.shape, value.dtype),
        in_specs=[any_space() for _ in range(1 + len(deps))],
        out_specs=any_space(),
        input_output_aliases={0: 0},
        compiler_params=params(),
        cost_estimate=cost(0, 0),
        name="hold",
    )(value, *deps)


def gather_small(value, me, devices, count):
    held = value[None]
    for bit in list(range(3, count)) + [2, 1, 0]:
        other = swap(held, devices, (bit, bit))
        upper = (me >> bit) & 1
        axis = 0 if bit > 2 else 1
        join_two = lambda a, b: jnp.stack([a, b], axis=axis).reshape((-1,) + value.shape)
        held = jnp.where(upper == 0, join_two(held, other), join_two(other, held))
    return held


def scatter_small(value, me, devices, count, exact):
    shape = value.shape[1:]
    rows = shape[0]
    total = value
    for bit in [0, 1, 2] + list(range(count - 1, 2, -1)):
        upper = (me >> bit) & 1
        axis = 0 if bit > 2 else 1
        pair = total.reshape(((2, -1) if bit > 2 else (-1, 2)) + shape)
        away = lax.dynamic_index_in_dim(pair, 1 - upper, axis, keepdims=False)
        keep = lax.dynamic_index_in_dim(pair, upper, axis, keepdims=False)
        sums = away[:, rows - exact :]
        top = lax.reduce_precision(sums, 8, 7)
        packet = jnp.concatenate([away[:, : rows - exact], top, sums - top], axis=1).astype(BF)
        got = swap(packet, devices, (bit, bit)).astype(F32)
        low = got[:, rows - exact : rows] + got[:, rows:]
        total = keep + jnp.concatenate([got[:, : rows - exact], low], axis=1)
    return total[0]


def chip_unit(up, down, core, devices):
    parts, share, feature = up.shape
    flat = up.reshape(parts * share, feature)
    other = swap(jnp.where(core == 0, down, flat), devices, (0, 0))
    up_unit = jnp.concatenate([up, other.reshape(up.shape)], axis=1).reshape(2 * parts * share, feature)
    return jnp.where(core == 0, up_unit, jnp.concatenate([other, down]))[None]


def fold_kernel(upper_ref, keep_away_ref, got_away_ref, keep_own_ref, got_own_ref, send_ref, keep_ref):
    send_ref[...] = (keep_away_ref[...].astype(F32) + got_away_ref[...].astype(F32)).astype(BF)
    keep_ref[...] = (keep_own_ref[...].astype(F32) + got_own_ref[...].astype(F32)).astype(BF)


def fold(keep, got, upper, deps=()):
    half = keep.shape[0] // 2
    each = min(2, half)
    unit = (each,) + keep.shape[1:]
    count = len(deps)
    away = pl.BlockSpec(unit, lambda i, up: ((1 - up[0]) * (half // each) + i, 0, 0))
    own = pl.BlockSpec(unit, lambda i, up: (up[0] * (half // each) + i, 0, 0))
    out = pl.BlockSpec(unit, lambda i, up: (i, 0, 0))
    shape = jax.ShapeDtypeStruct((half,) + keep.shape[1:], BF)

    def body(*refs):
        fold_kernel(*refs[:5], *refs[5 + count :])

    return pl.pallas_call(
        body,
        grid_spec=pltpu.PrefetchScalarGridSpec(
            num_scalar_prefetch=1,
            grid=(half // each,),
            in_specs=[away, away, own, own] + [any_space() for _ in deps],
            out_specs=[out, out],
        ),
        out_shape=(shape, shape),
        compiler_params=params(),
        cost_estimate=cost(0, 6 * half * keep[0].size),
        name="fold",
    )(upper, keep, got, keep, got, *deps)


def on_device(
    tokens, grad_out, region_rows, region_cols, ln1_gain, ln1_bias, spec_w1, spec_b1, spec_w2, spec_b2,
    ln2_gain, ln2_bias, w_up, up_bias, w_down, down_bias,
):
    devices = lax.axis_size(AXES[0]) * lax.axis_size(AXES[1])
    count = devices.bit_length() - 1
    me = lax.axis_index(AXES).astype(jnp.int32)
    core = me & 1
    me_one = me.reshape(1)
    feature = tokens.shape[-1]
    block = feature // BLOCKS
    share = ln1_gain.shape[0]
    cells = tokens.shape[1] * tokens.shape[2]
    hidden = w_up.shape[1]
    parts = hidden // feature
    tables = {name: jnp.asarray(value) for name, value in wave_matrices().items()}
    orders = doubling_orders(count)
    places = tuple(places_of(order) for order in orders)
    flat_tokens = tokens.reshape(cells, feature)
    flat_grad = grad_out.reshape(cells, feature)
    fast = devices // 2 == UNITS
    step = lambda value, k: swap(value, devices, (orders[0][k], orders[1][k]))

    padded = lambda v: jnp.pad(v, ((0, 0), (0, LANES - v.shape[1])))
    vectors = (spec_b1, spec_b2, ln1_gain, ln1_bias, ln2_gain, ln2_bias, up_bias, down_bias)
    if fast:
        own_up = w_up.reshape(share, parts, feature).transpose(1, 0, 2)
        unit = chip_unit(own_up, w_down, core, devices)
        bits = (3, 4, 2, 1, 0)
        hop = lambda value, mask: lax.ppermute(value, AXES, [(i, i ^ mask) for i in range(devices)])
        meet = lambda value, bit: hop(value, 1 << bit)
        small = begin_small(spec_w1, spec_w2, vectors)
        half, normal = first(region_rows, region_cols, flat_tokens, tables, deps=(unit, small))
        small = join_rows(small, *(hop(small, mask) for mask in (8, 16, 24)), deps=(half,))
        near = join_rows(unit, step(unit, 0), deps=(small,))
        small = join_rows(small, *(hop(small, mask) for mask in (4, 2, 6)), deps=(near,))
        small = join_rows(small, meet(small, 0))
        near = join_rows(near, step(near, 1), deps=(small,))
        beside, across = step(near, 2), step(near, 3)
        weights, weight_bits, vector_bits, me_small = small, bits, bits, me_one
        vectors = jnp.zeros((8, 1, LANES), F32)
    else:
        up = lax.all_gather(w_up, AXES, axis=0, tiled=True)
        up = up.reshape(UNITS, feature // UNITS, parts, feature).transpose(0, 2, 1, 3).reshape(UNITS, -1, feature)
        down = lax.all_gather(w_down, AXES, axis=0, tiled=True).reshape(UNITS, -1, feature)
        pieces = tuple(
            jnp.where(core == 0, one, two)[begin : begin + UNITS // 2]
            for one, two in ((up, down), (down, up))
            for begin in (0, UNITS // 2)
        )
        me_one = core.reshape(1)
        me_small = jnp.zeros_like(me_one)
        places = (tuple(range(UNITS)),) * 2
        small = jnp.concatenate([padded(spec_w1), padded(spec_w2)] + [padded(v[None]) for v in vectors])
        small = gather_small(small, me, devices, count)
        weights = small[:, : 4 * share].reshape(devices, 2, 2 * share, LANES).transpose(1, 0, 2, 3)
        weights = weights.reshape(2, 2 * UNITS, -1, LANES).transpose(1, 0, 2, 3).reshape(2 * UNITS, -1, LANES)
        weight_bits, vector_bits = tuple(range(5)), tuple(range(count))
        half, normal = first(region_rows, region_cols, flat_tokens, tables)
        vectors = small[:, 4 * share :].transpose(1, 0, 2).astype(F32)

    steps = KEPT // GROUP // TAKE
    core_swap = lambda value: swap(value, devices, (0, 0))
    made = mix_first(
        me_small, half, weights, vectors, tables, hidden, steps // 2, weight_bits, vector_bits,
        deps=(near,) if fast else (),
    )
    half1, modes1, heads, (mix1, mix2, wide, long, up_shift) = made[0], made[1:6], made[6:11], made[11:]
    deps = ()
    if fast:
        other_near = core_swap(near)
        deps = (other_near,)
    made = mix_second(half, mix1, mix2, wide, long, tables, steps // 2, steps // 2, deps=deps)
    half2, modes2 = made[0], made[1:6]
    if fast:
        beside = hold(beside, (half2,))
        far = step(beside, 3)
        deps = (beside,)
    middle, normed = space(region_rows, region_cols, half1, half2, flat_tokens, wide, tables, deps=deps)
    if fast:
        across = hold(across, (normed,))
        far = hold(far, (across,))
        pieces = (near, beside, across, far, other_near) + tuple(core_swap(v) for v in (beside, across, far))
    active, pre, branch, bias_grad, up_all, down_all = feed_up(
        region_rows, region_cols, me_one, normed, flat_grad, up_shift, pieces, places
    )
    send, keep = weight_grads(me_one, active, pre, branch, normed, places)
    tiles = cells // CELLS
    mixed, grad_middle, half_back, sums_two = feed_down(
        region_rows, region_cols, active, pre, middle, flat_grad, normal, wide, tables["first"], up_all, down_all,
        deps=(send,),
    )
    deps = ()
    if fast:
        ranks = [((me >> jnp.where(core == 0, *bit)) & 1).reshape(1) for bit in zip(*orders)]
        send, keep = fold(keep, swap(send, devices, (0, 0)), ranks[3], deps=(sums_two,))
        deps = (send,)
    half_back, one, two, one_head, two_head, bias_sums = mix_back(
        half_back, modes1, modes2, heads, mix1, mix2, tables, deps=deps
    )
    grad_one = block_grads(modes1[0], modes2[0], heads[0], one, one_head, "grad_mix1")
    if fast:
        send, keep = fold(keep, step(send, 3), ranks[2], deps=(grad_one,))
        deps = (send,)
    grad_two = block_grads(modes1[1], modes2[1], heads[1], two, two_head, "grad_mix2", deps=deps)
    last_args = (region_rows, region_cols, half_back, flat_tokens, grad_middle, wide, tables)
    if fast:
        places_small = [v.reshape(1) for v in (me & 1, (me >> 1) & 3, me >> 3)]
        away, own = pack(places_small[0], grad_one, grad_two, bias_sums, sums_two, bias_grad, wide, devices)
        grad_tokens = last(*last_args, 0, 2, deps=(away,))
        *aways, own = fold_small(own, (hop(away, 1),), places_small[1], 4, deps=(grad_tokens,))
        send, keep = fold(keep, step(send, 2), ranks[1], deps=tuple(aways))
        gots = tuple(hop(v, mask) for v, mask in zip(aways, (2, 4, 6)))
        grad_tokens = last(*last_args, 2, 2, (grad_tokens,), deps=(send,))
        *aways, own = fold_small(own, gots, places_small[2], 4, deps=(grad_tokens,))
        gots = tuple(hop(v, mask) for v, mask in zip(aways, (8, 16, 24)))
        grad_tokens = last(*last_args, 4, 2, (grad_tokens,), deps=tuple(aways))
        send, keep = fold(keep, step(send, 1), ranks[0], deps=(grad_tokens, gots[0]))
        grad_tokens = last(*last_args, 6, 2, (grad_tokens,), deps=(send,))
        widths = (share,) * 5 + (2 * share,) * 2 + (hidden // devices,)
        blocks = end_small(hold(own, (grad_tokens,)), gots, 2 * share, block, widths)
        keep = hold(keep, (blocks[0],))
        total = keep[0].astype(F32) + step(send, 0)[0].astype(F32)
        up_sum = total.reshape(parts, 2 * share, feature)
        lower = up_sum[:, :share].reshape(parts * share, feature)
        upper = up_sum[:, share:].reshape(parts * share, feature)
        each = parts * share
        leaving = jnp.where(core == 0, upper, total[:each])
        other = swap(leaving, devices, (0, 0))
        grad_w_up = jnp.where(core == 0, lower, other).reshape(parts, share, feature).transpose(1, 0, 2)
        grad_w_down = jnp.where(core == 0, other, total[each:])
        rows = [v.reshape(-1) for v in blocks[2:]]
        blocks = blocks[:2]
    else:
        scatter = lambda v: lax.psum_scatter(v.astype(F32), AXES, scatter_dimension=0, tiled=True)
        up = jnp.where(core == 0, keep, send).reshape(UNITS, parts, feature // UNITS, feature)
        grad_w_up = scatter(up.transpose(0, 2, 1, 3).reshape(feature, hidden))
        grad_w_down = scatter(jnp.where(core == 0, send, keep).reshape(hidden, feature))
        grad_tokens = last(*last_args, 0, tiles)
        owned = lambda v: jnp.pad(
            v.reshape(v.shape[0], devices, -1).transpose(1, 0, 2), ((0, 0), (0, 0), (0, LANES - v.shape[1] // devices))
        )
        narrow = jnp.concatenate(list(scale_grads(bias_sums, sums_two, wide)) + [sums_two[:3]])
        biases = bias_sums[:2].reshape(2, feature // LANES, 2, LANES).transpose(0, 2, 1, 3).reshape(2, 2 * feature)
        blocks = [v.reshape(devices, 2 * share, LANES) for v in (grad_one, grad_two)]
        packet = jnp.concatenate(blocks + [owned(narrow), owned(biases), owned(bias_grad)], axis=1)
        result = scatter_small(packet, me, devices, count, 8)
        widths = (share,) * 5 + (2 * share,) * 2 + (hidden // devices,)
        rows = [result[4 * share + k, :width] for k, width in enumerate(widths)]
        blocks = [result[k * 2 * share : (k + 1) * 2 * share, :block] for k in range(2)]
    return (
        mixed.reshape(tokens.shape),
        grad_tokens.reshape(tokens.shape),
        rows[0],
        rows[1],
        blocks[0],
        rows[5],
        blocks[1],
        rows[6],
        rows[2],
        rows[3],
        grad_w_up.reshape(share, hidden),
        rows[7],
        grad_w_down,
        rows[4],
    )


def solution(mesh):
    placed = P(AXES)
    return jax.shard_map(
        on_device, mesh=mesh, in_specs=(placed,) * 16, out_specs=(placed,) * 14, check_vma=False
    )
```

```python
import functools
import math

import jax
import jax.numpy as jnp
import numpy as np
from jax import lax
from jax.experimental import pallas as pl
from jax.experimental.pallas import tpu as pltpu
from jax.sharding import PartitionSpec as P

BF = jnp.bfloat16
F32 = jnp.float32
BLOCKS = 8
EPS = 1e-05
SHRINK = 0.01
ROWS = 32
COLS = 64
KEPT = COLS // 2
GROUP = 4
STEPS = ROWS // GROUP
CELLS = GROUP * COLS
MODES = (KEPT + 1) * ROWS
HEAD = (GROUP + 1) * ROWS
BODY = GROUP * ROWS
TAKE = 2
TOOK = TAKE * BODY
LANES = 128
C1 = math.sqrt(2.0 / math.pi)
C3 = 0.044715
SIGMOID = -2.0 * C1 / math.log(2.0)
UNITS = 16
VMEM_LIMIT = 60 * 1024 * 1024
SMALL_LIMIT = 36 * 1024 * 1024


def table_parts(values):
    high = values.astype(np.float32).astype(jnp.bfloat16)
    low = (values - high.astype(np.float64)).astype(np.float32).astype(jnp.bfloat16)
    return np.stack([high, low])


def wave_matrices():
    scale = 1.0 / math.sqrt(ROWS * COLS)
    w = np.arange(COLS)
    first = np.zeros((KEPT, 2, GROUP, GROUP, COLS))
    for k in range(KEPT):
        for h in range(GROUP):
            if k == 0:
                first[k, 0, h, h] = scale
                first[k, 1, h, h] = scale * np.where(w % 2 == 0, 1.0, -1.0)
            else:
                first[k, 0, h, h] = scale * np.cos(2 * np.pi * (k * w % COLS) / COLS)
                first[k, 1, h, h] = -scale * np.sin(2 * np.pi * (k * w % COLS) / COLS)
    first = first.reshape(CELLS, CELLS)
    p = np.arange(ROWS)
    turn = 2 * np.pi * (np.outer(p, p) % ROWS) / ROWS
    cos = np.cos(turn).reshape(ROWS, STEPS, GROUP)
    sin = np.sin(turn).reshape(ROWS, STEPS, GROUP)
    body = np.zeros((2, GROUP, ROWS, GROUP, STEPS, 2, GROUP))
    head = np.zeros((2, GROUP + 1, ROWS, GROUP, STEPS, 2, GROUP))
    for k in range(GROUP):
        body[0, k, :, k, :, 0] = cos
        body[0, k, :, k, :, 1] = sin
        body[1, k, :, k, :, 1] = cos
        body[1, k, :, k, :, 0] = -sin
    head[:, 1:GROUP, :, 1:] = body[:, 1:, :, 1:]
    for place, part in ((0, 0), (GROUP, 1)):
        head[0, place, :, 0, :, part] = cos
        head[1, place, :, 0, :, part] = -sin
    weight = np.full((2, GROUP + 1, ROWS, 1), 2.0)
    weight[:, 0] = 1.0
    weight[:, GROUP] = 1.0
    head = head.reshape(2 * HEAD, 2 * BODY)
    body = body.reshape(2 * BODY, 2 * BODY)
    head_weighted = head * weight.reshape(2 * HEAD, 1)
    body_weighted = body * 2.0
    return {
        "first": table_parts(first),
        "first_t": table_parts(first.T),
        "head": table_parts(head),
        "body": table_parts(body),
        "head_t": table_parts(head.T),
        "body_t": table_parts(body.T),
        "head_w": table_parts(head_weighted),
        "body_w": table_parts(body_weighted),
        "head_wt": table_parts(head_weighted.T),
        "body_wt": table_parts(body_weighted.T),
    }


def mm(left, right, dims=(1, 0)):
    return lax.dot_general(
        left, right, (((dims[0],), (dims[1],)), ((), ())), preferred_element_type=F32
    )


def split(values):
    high = values.astype(BF)
    return high, (values - high.astype(F32)).astype(BF)


def turn(table, values):
    high, low = split(values)
    return mm(table[0], high) + mm(table[1], high) + mm(table[0], low)


def normalize(values):
    centred = values - jnp.mean(values, axis=-1, keepdims=True)
    inverse = lax.rsqrt(jnp.mean(centred * centred, axis=-1, keepdims=True) + EPS)
    return centred * inverse, inverse


def norm_back(grad, gain, normal, inverse):
    scaled = grad * gain
    return inverse * (
        scaled
        - jnp.mean(scaled, axis=-1, keepdims=True)
        - normal * jnp.mean(scaled * normal, axis=-1, keepdims=True)
    )


def gelu_parts(value):
    square = value * value
    half = 1.0 / (1.0 + jnp.exp2(value * (SIGMOID + (SIGMOID * C3) * square)))
    active = value * half
    slope = half + active * (1.0 - half) * (2.0 * C1 + (6.0 * C1 * C3) * square)
    return active, slope


def live_rows(start, count, rows_ref, cols_ref):
    cell = start + lax.broadcasted_iota(jnp.int32, (count, 1), 0)
    inside = (cell // COLS < rows_ref[0]) & (cell % COLS < cols_ref[0])
    return jnp.where(inside, 1.0, 0.0).astype(F32)


def spread(piece, per_device, me, bits):
    devices = piece.shape[0]
    total = devices * per_device
    lane = lax.broadcasted_iota(jnp.int32, (LANES, total), 0)
    place = lax.broadcasted_iota(jnp.int32, (LANES, total), 1)
    pick = jnp.where(place % per_device == lane, 1.0, 0.0).astype(BF)
    wide = mm(piece.astype(BF), pick)
    row = lax.broadcasted_iota(jnp.int32, (devices, 1), 0)
    owner = jnp.full((devices, 1), me, jnp.int32)
    for k, bit in enumerate(bits):
        owner = owner ^ (((row >> k) & 1) << bit)
    where = lax.broadcasted_iota(jnp.int32, (devices, total), 1) // per_device
    return jnp.sum(jnp.where(owner == where, wide, 0.0), axis=0, keepdims=True)


def place_of(mask, bits):
    return sum(((mask >> bit) & 1) << k for k, bit in enumerate(bits))


def any_space():
    return pl.BlockSpec(memory_space=pl.ANY)


def single(shape):
    return pl.BlockSpec(shape, lambda *_: (0,) * len(shape), pipeline_mode=pl.Buffered(1))


def smem():
    return pl.BlockSpec(memory_space=pltpu.SMEM)


def params(limit=VMEM_LIMIT):
    return pltpu.CompilerParams(vmem_limit_bytes=limit)


def cost(flops, moved):
    return pl.CostEstimate(flops=0, bytes_accessed=0, transcendentals=0)


def launch(deps, kernel, *, in_specs, **more):
    count = len(in_specs)

    def body(*refs):
        kernel(*refs[:count], *refs[count + len(deps) :])

    call = pl.pallas_call(body, in_specs=list(in_specs) + [any_space() for _ in deps], **more)
    return lambda *operands: call(*operands, *deps)


MARK = jax.ShapeDtypeStruct((8, LANES), F32)


def to_mixed(real, imag):
    tiles = []
    for at in range(0, real.shape[1], LANES):
        tiles += [real[:, at : at + LANES], imag[:, at : at + LANES]]
    return jnp.concatenate(tiles, axis=1)


def from_mixed(values):
    cut = lambda at: values[:, at : at + LANES]
    real = [cut(at) for at in range(0, values.shape[1], 2 * LANES)]
    imag = [cut(at + LANES) for at in range(0, values.shape[1], 2 * LANES)]
    return jnp.concatenate(real, axis=1), jnp.concatenate(imag, axis=1)


def mix_product(values, matrix_ref, back=False):
    feature = values.shape[1] // 2
    wide = 2 * LANES
    groups = []
    for group in range(2):
        part = values[:, group * feature : (group + 1) * feature]
        count = feature // wide
        for t in range(count):
            begin, end = max(t - 1, 0) * wide, min(t + 2, count) * wide
            here = slice(t * wide, (t + 1) * wide)
            if back:
                groups.append(mm(part[:, begin:end], matrix_ref[group, here, begin:end], (1, 1)))
            else:
                groups.append(mm(part[:, begin:end], matrix_ref[group, begin:end, here]))
    return jnp.concatenate(groups, axis=1)


def first_kernel(begin, rows_ref, cols_ref, tokens_ref, first_ref, *rest):
    half_ref, normal_ref, mark_ref = rest[-3:]
    mark_ref[...] = jnp.zeros_like(mark_ref)
    feature = tokens_ref.shape[1]
    start = (pl.program_id(0) + begin) * tokens_ref.shape[0]
    for k in range(tokens_ref.shape[0] // CELLS):
        here = slice(k * CELLS, (k + 1) * CELLS)
        there = slice(k * 2 * GROUP, (k + 1) * 2 * GROUP)
        normal, _ = normalize(tokens_ref[here, :].astype(F32))
        live = live_rows(start + k * CELLS, CELLS, rows_ref, cols_ref)
        normal = normal * live
        normal_ref[here, :] = normal.astype(BF)
        half_ref[:, there, :feature] = turn(first_ref, normal).reshape(KEPT, 2 * GROUP, feature)
        ones = jnp.broadcast_to(live, (CELLS, LANES)).astype(BF)
        flat = mm(first_ref[0], ones) + mm(first_ref[1], ones)
        half_ref[:, there, feature:] = flat.reshape(KEPT, 2 * GROUP, LANES)


def first(rows, cols, tokens, tables, begin, steps, before=(), deps=(), tiles=1):
    cells, feature = tokens.shape
    table = tables["first"]
    block = pl.BlockSpec((tiles * CELLS, feature), lambda i: (i + begin, 0))
    operands = (rows, cols, tokens, table)
    return launch(
        deps,
        functools.partial(first_kernel, begin),
        grid=(steps,),
        out_shape=(
            jax.ShapeDtypeStruct((KEPT, 2 * ROWS, feature + LANES), F32),
            jax.ShapeDtypeStruct((cells, feature), BF),
            MARK,
        ),
        in_specs=[smem(), smem(), block, single(table.shape)] + [any_space() for _ in before],
        out_specs=(
            pl.BlockSpec((KEPT, 2 * GROUP * tiles, feature + LANES), lambda i: (0, i + begin, 0)),
            block,
            single(MARK.shape),
        ),
        input_output_aliases={len(operands) + k: k for k in range(len(before))},
        compiler_params=params(),
        cost_estimate=cost(6e9, 11e6),
        name="first",
    )(*operands, *before)


def build_mix(me, bits, weights_ref, layer, out_ref, feature):
    block = feature // BLOCKS
    half = feature // 2
    per_group = BLOCKS // 2
    share = 2 * feature // weights_ref.shape[0]
    each = block // share
    out_ref[...] = jnp.zeros_like(out_ref)
    row = lax.broadcasted_iota(jnp.int32, (LANES, half), 0)
    column = lax.broadcasted_iota(jnp.int32, (LANES, half), 1)
    for b in range(per_group):
        shift = jnp.where((column - b * block == row) & (row < block), 1.0, 0.0).astype(BF)
        low, high = b * block, (b + 1) * block
        for group in range(2):
            for part in range(2):
                at = (part * BLOCKS + group * per_group + b) * each
                pieces = [
                    weights_ref[place_of((at + k) ^ me, bits), layer * share : (layer + 1) * share, :]
                    for k in range(each)
                ]
                placed = mm(jnp.concatenate(pieces, axis=0), shift).astype(BF)
                for t in range(low // LANES, (high - 1) // LANES + 1):
                    begin, end = max(low, t * LANES), min(high, (t + 1) * LANES)
                    for c in range(low // LANES, (high - 1) // LANES + 1):
                        piece = placed[begin - low : end - low, c * LANES : (c + 1) * LANES]
                        for up in range(2):
                            top = 2 * t * LANES + up * LANES + begin - t * LANES
                            left = (2 * c + (up ^ part)) * LANES
                            value = -piece if part == 1 and up == 1 else piece
                            here = (group, slice(top, top + end - begin), slice(left, left + LANES))
                            out_ref[here] = out_ref[here] + value


def to_modes(half_ref, head_ref, body_ref, is_head):
    width = half_ref.shape[2]
    real, imag, ends = [], [], ()
    for k in range(TAKE):
        begin = is_head and k == 0
        rows = HEAD if begin else BODY
        spec = turn(head_ref if begin else body_ref, half_ref[k * GROUP : (k + 1) * GROUP].reshape(2 * BODY, width))
        real.append(spec[:BODY])
        imag.append(spec[rows : rows + BODY])
        if begin:
            ends = (spec[BODY:rows], spec[rows + BODY :])
    if is_head:
        real.append(ends[0])
        imag.append(ends[1])
    return jnp.concatenate(real, axis=0), jnp.concatenate(imag, axis=0)


def from_modes(pair_of, head_ref, body_ref, is_head, out_ref):
    for k in range(TAKE):
        begin = is_head and k == 0
        parts = []
        for part in pair_of:
            parts.append(part[k * BODY : (k + 1) * BODY])
            if begin:
                parts.append(part[TOOK:])
        result = turn(head_ref if begin else body_ref, jnp.concatenate(parts, axis=0))
        out_ref[k * GROUP : (k + 1) * GROUP] = result.reshape(GROUP, 2 * ROWS, result.shape[1])


def mix_step(half_ref, head_ref, body_ref, back_head_ref, back_body_ref, mix1_ref, mix2_ref, wide_ref, long_ref,
             outs, heads, out_ref, is_head):
    feature = out_ref.shape[2]
    specs = to_modes(half_ref, head_ref, body_ref, is_head)
    gain = wide_ref[0:1, :]
    shift = wide_ref[1:2, :]

    def scaled(part):
        flat = jnp.concatenate([part[:, feature:]] * (feature // LANES), axis=1)
        return (part[:, :feature] * gain + flat * shift).astype(BF)

    inside = to_mixed(*(scaled(part) for part in specs))
    active, slope = gelu_parts(mix_product(inside, mix1_ref) + long_ref[0:1, :])
    hidden = active.astype(BF)
    value = mix_product(hidden, mix2_ref) + long_ref[1:2, :]
    bend = jnp.tanh(value / SHRINK)
    flat = jnp.concatenate([part[:, feature:] for part in specs], axis=1)
    for ref, head, kept in zip(outs, heads, (inside, hidden, slope, bend * bend, flat)):
        ref[...] = kept[:TOOK]
        if is_head:
            head[...] = kept[TOOK:]
    from_modes(from_mixed(value - SHRINK * bend), back_head_ref, back_body_ref, is_head, out_ref)


def mix_first_kernel(
    weight_bits, vector_bits, me_ref, half_ref, weights_ref, vector_in_ref, head_ref, body_ref, back_head_ref, back_body_ref,
    out_ref, low_ref, hidden_ref, slope_ref, bend_ref, flat_ref,
    low_head_ref, hidden_head_ref, slope_head_ref, bend_head_ref, flat_head_ref, mix1_ref, mix2_ref, wide_ref, long_ref, up_ref,
    vector_ref,
):
    feature = out_ref.shape[2]
    devices = vector_ref.shape[1]
    share = feature // devices
    step = pl.program_id(0)
    outs = (low_ref, hidden_ref, slope_ref, bend_ref, flat_ref)
    heads = (low_head_ref, hidden_head_ref, slope_head_ref, bend_head_ref, flat_head_ref)
    work = functools.partial(
        mix_step, half_ref, head_ref, body_ref, back_head_ref, back_body_ref, mix1_ref, mix2_ref, wide_ref, long_ref,
        outs, heads, out_ref,
    )

    @pl.when(step == 0)
    def _():
        me = me_ref[0]
        if vector_in_ref.shape == vector_ref.shape:
            vector_ref[...] = vector_in_ref[...]
        else:
            rows = weights_ref[:, 4 * share :, :].astype(F32)
            for d in range(devices):
                for k in range(vector_ref.shape[0]):
                    vector_ref[k, d : d + 1, :] = rows[d, k : k + 1, :]
        build_mix(me, weight_bits, weights_ref, 0, mix1_ref, feature)
        build_mix(me, weight_bits, weights_ref, 1, mix2_ref, feature)
        wide_ref[...] = jnp.zeros_like(wide_ref)
        long_ref[...] = jnp.zeros_like(long_ref)
        for row, at in enumerate((2, 3, 4, 5, 7)):
            wide_ref[row : row + 1, :] = spread(vector_ref[at], share, me, vector_bits)
        for row in range(2):
            both = spread(vector_ref[row], 2 * share, me, vector_bits)
            long_ref[row : row + 1, :] = to_mixed(both[:, :feature], both[:, feature:])
        up_ref[...] = spread(vector_ref[6], up_ref.shape[1] // devices, me, vector_bits)
        work(True)

    @pl.when(step > 0)
    def _():
        work(False)


def mix_second_kernel(
    half_ref, mix1_ref, mix2_ref, wide_ref, long_ref, body_ref, back_body_ref,
    out_ref, *outs,
):
    mix_step(
        half_ref, None, body_ref, None, back_body_ref, mix1_ref, mix2_ref, wide_ref, long_ref,
        outs, (None,) * 5, out_ref, False,
    )


def mode_shapes(rows, feature):
    wide = [jax.ShapeDtypeStruct((rows, 2 * feature), kind) for kind in (BF, BF, F32, F32)]
    return wide + [jax.ShapeDtypeStruct((rows, 2 * LANES), F32)]


def mode_blocks(feature):
    return [pl.BlockSpec((TOOK, width), lambda i: (i, 0)) for width in (2 * feature,) * 4 + (2 * LANES,)]


def half_block(width, begin=0):
    return pl.BlockSpec((TAKE * GROUP, 2 * ROWS, width), lambda i: (i + begin, 0, 0))


def mix_first(me, half, weights, vectors, tables, hidden, steps, weight_bits, vector_bits, deps=()):
    feature = half.shape[2] - LANES
    fixed = (weights, vectors, tables["head"], tables["body"], tables["head_wt"], tables["body_wt"])
    more = (
        jax.ShapeDtypeStruct((2, feature, feature), BF),
        jax.ShapeDtypeStruct((2, feature, feature), BF),
        jax.ShapeDtypeStruct((8, feature), F32),
        jax.ShapeDtypeStruct((8, 2 * feature), F32),
        jax.ShapeDtypeStruct((1, hidden), F32),
    )
    heads = mode_shapes(ROWS, feature)
    devices = vectors.shape[1] if vectors.shape[1] > 1 else weights.shape[0]
    return launch(
        deps,
        functools.partial(mix_first_kernel, weight_bits, vector_bits),
        grid=(steps,),
        out_shape=[jax.ShapeDtypeStruct((TAKE * GROUP * steps, 2 * ROWS, feature), F32)]
        + mode_shapes(TOOK * steps, feature) + heads + list(more),
        in_specs=[smem(), half_block(feature + LANES)] + [single(v.shape) for v in fixed],
        out_specs=[half_block(feature)] + mode_blocks(feature) + [single(v.shape) for v in heads]
        + [single(v.shape) for v in more],
        scratch_shapes=[pltpu.VMEM((8, devices, LANES), F32)],
        compiler_params=params(),
        cost_estimate=cost(9e9, 20e6),
        name="mix_first",
    )(me, half, *fixed)


def mix_second(half, mix1, mix2, wide, long, tables, begin, steps, deps=()):
    feature = half.shape[2] - LANES
    fixed = (mix1, mix2, wide, long, tables["body"], tables["body_wt"])
    return launch(
        deps,
        mix_second_kernel,
        grid=(steps,),
        out_shape=[jax.ShapeDtypeStruct((TAKE * GROUP * steps, 2 * ROWS, feature), F32)] + mode_shapes(TOOK * steps, feature),
        in_specs=[half_block(feature + LANES, begin)] + [single(v.shape) for v in fixed],
        out_specs=[half_block(feature)] + mode_blocks(feature),
        compiler_params=params(),
        cost_estimate=cost(9e9, 20e6),
        name="mix_second",
    )(half, *fixed)


def space_kernel(rows_ref, cols_ref, half1_ref, half2_ref, tokens_ref, first_t_ref, wide_ref, middle_ref, normed_ref, mark_ref):
    mark_ref[...] = jnp.zeros_like(mark_ref)
    feature = tokens_ref.shape[1]
    start = pl.program_id(0) * tokens_ref.shape[0]
    for k in range(tokens_ref.shape[0] // CELLS):
        here = slice(k * CELLS, (k + 1) * CELLS)
        flat = lambda ref: ref[:, k * 2 * GROUP : (k + 1) * 2 * GROUP, :].reshape(-1, feature)
        spatial = turn(first_t_ref, jnp.concatenate([flat(half1_ref), flat(half2_ref)], axis=0))
        inputs = tokens_ref[here, :].astype(F32)
        live = live_rows(start + k * CELLS, CELLS, rows_ref, cols_ref)
        normal, _ = normalize(inputs)
        middle = inputs + live * (spatial + (normal * wide_ref[0:1, :] + wide_ref[1:2, :]))
        middle_ref[here, :] = middle
        normal, _ = normalize(middle)
        normed_ref[here, :] = (normal * wide_ref[2:3, :] + wide_ref[3:4, :]).astype(BF)


def column_block(rows, width, tiles=1):
    return pl.BlockSpec((rows, 2 * GROUP * tiles, width), lambda i: (0, i, 0))


def space(rows, cols, half1, half2, tokens, wide, tables, deps=(), tiles=1):
    cells, feature = tokens.shape
    table = tables["first_t"]
    block = pl.BlockSpec((tiles * CELLS, feature), lambda i: (i, 0))
    return launch(
        deps,
        space_kernel,
        grid=(STEPS // tiles,),
        out_shape=(jax.ShapeDtypeStruct((cells, feature), F32), jax.ShapeDtypeStruct((cells, feature), BF), MARK),
        in_specs=[smem(), smem(), column_block(half1.shape[0], feature, tiles), column_block(half2.shape[0], feature, tiles),
                  block, single(table.shape), single(wide.shape)],
        out_specs=(block, block, single(MARK.shape)),
        compiler_params=params(),
        cost_estimate=cost(6e9, 20e6),
        name="space",
    )(rows, cols, half1, half2, tokens, table, wide)


def fetch_weights(me_ref, pieces, places, up_ref, down_ref, sems):
    each = pieces[0].shape[0]
    held = len(pieces) // 2
    count = each * held
    chip = me_ref[0] // 2

    def copies(own, core):
        target = (up_ref, down_ref)[core]
        source = pieces[:held] if own else pieces[held:]
        for mask in range(count):
            at = places[core][mask]
            part = source[at // each].at[at % each]
            yield pltpu.make_async_copy(part, target.at[chip ^ mask], sems.at[core, mask])

    for core in range(2):
        @pl.when(me_ref[0] % 2 == core)
        def _():
            for copy in copies(True, core):
                copy.start()
            for copy in copies(False, 1 - core):
                copy.start()

    def arrived(core):
        for copy in copies(True, core):
            copy.wait()

    return arrived


def weight_scratch(pieces):
    chips, rows, feature = UNITS, pieces[0].shape[1], pieces[0].shape[2]
    return [
        pltpu.VMEM((chips, rows, feature), BF),
        pltpu.VMEM((chips, rows, feature), BF),
        pltpu.SemaphoreType.DMA((2, chips)),
    ]


def up_part(up_ref, j, feature):
    share = up_ref.shape[1] * feature // (up_ref.shape[0] * up_ref.shape[1])
    return up_ref[:, j * share : (j + 1) * share, :].reshape(feature, feature)


def down_part(down_ref, j, feature):
    share = down_ref.shape[1]
    each = feature // share
    return down_ref[j * each : (j + 1) * each].reshape(feature, feature)


def up_kernel(places, rows_ref, cols_ref, me_ref, normed_ref, grad_ref, bias_ref, *rest):
    pieces = rest[:-10]
    active_ref, pre_ref, live_ref, bias_grad_ref, up_all_ref, down_all_ref, up_ref, down_ref, sems, out_sems = rest[-10:]
    tile, feature = normed_ref.shape
    step = pl.program_id(0)
    copies = [
        pltpu.make_async_copy(source, target, out_sems.at[k])
        for k, (source, target) in enumerate(((up_ref, up_all_ref), (down_ref, down_all_ref)))
    ]

    def work(arrived):
        live = live_rows(step * tile, tile, rows_ref, cols_ref)
        branch = (grad_ref[...].astype(F32) * live).astype(BF)
        live_ref[...] = branch
        normed = normed_ref[...]
        if arrived:
            arrived(0)
            copies[0].start()
        for j in range(active_ref.shape[1] // feature):
            place = slice(j * feature, (j + 1) * feature)
            value = mm(normed, up_part(up_ref, j, feature)) + bias_ref[:, place]
            if arrived and j == 0:
                arrived(1)
                copies[1].start()
            grad = mm(branch, down_part(down_ref, j, feature), (1, 1))
            active, slope = gelu_parts(value)
            active_ref[:, place] = active.astype(BF)
            grad = grad * slope
            pre_ref[:, place] = grad.astype(BF)
            bias_grad_ref[:, place] += jnp.sum(grad, axis=0, keepdims=True)

    @pl.when(step == 0)
    def _():
        bias_grad_ref[...] = jnp.zeros_like(bias_grad_ref)
        work(fetch_weights(me_ref, pieces, places, up_ref, down_ref, sems))

    @pl.when(step > 0)
    def _():
        work(None)

    @pl.when(step == pl.num_programs(0) - 1)
    def _():
        for copy in copies:
            copy.wait()


def feed_up(rows, cols, me, normed, grad, bias, pieces, places, tile=256, deps=()):
    cells, feature = normed.shape
    hidden = bias.shape[1]
    block = lambda width: pl.BlockSpec((tile, width), lambda i: (i, 0))
    weights = jax.ShapeDtypeStruct((UNITS,) + pieces[0].shape[1:], BF)
    return launch(
        deps,
        functools.partial(up_kernel, places),
        grid=(cells // tile,),
        out_shape=(
            jax.ShapeDtypeStruct((cells, hidden), BF),
            jax.ShapeDtypeStruct((cells, hidden), BF),
            jax.ShapeDtypeStruct((cells, feature), BF),
            jax.ShapeDtypeStruct((1, hidden), F32),
            weights,
            weights,
        ),
        in_specs=[smem(), smem(), smem(), block(feature), block(feature), single(bias.shape)]
        + [any_space() for _ in pieces],
        out_specs=(block(hidden), block(hidden), block(feature), single((1, hidden)), any_space(), any_space()),
        scratch_shapes=weight_scratch(pieces) + [pltpu.SemaphoreType.DMA((2,))],
        compiler_params=params(),
        cost_estimate=cost(0, 0),
        name="feed_up",
    )(rows, cols, me, normed, grad, bias, *pieces)


def weight_grad_kernel(places, me_ref, active_ref, pre_ref, branch_ref, normed_ref, send_ref, keep_ref, stage_ref, sems):
    step = pl.program_id(0)
    steps = pl.num_programs(0) // 2
    feature = branch_ref.shape[1]
    chips, rows, _ = send_ref.shape
    each = feature // rows
    share = feature // chips

    def down_copies(j, target):
        for c in range(each):
            source = stage_ref.at[j, pl.ds(c * rows, rows)]
            yield pltpu.make_async_copy(source, target.at[places[1][j * each + c]], sems.at[j, c])

    def up_copies(j, target):
        for c in range(chips):
            source = stage_ref.at[steps + j, pl.ds(c * share, share)]
            there = target.at[places[0][c], pl.ds(j * share, share)]
            yield pltpu.make_async_copy(source, there, sems.at[steps + j, c])

    @pl.when(step < steps)
    def _():
        stage_ref[step] = mm(active_ref[...], branch_ref[...], (0, 0)).astype(BF)

    @pl.when(step >= steps)
    def _():
        stage_ref[step] = mm(normed_ref[...], pre_ref[...], (0, 0)).astype(BF)

    total = stage_ref.shape[0] // 2
    for j in range(total):
        for core in range(2):
            targets = (send_ref, keep_ref) if core == 0 else (keep_ref, send_ref)

            @pl.when((step == j) & (me_ref[0] % 2 == core))
            def _():
                for copy in down_copies(j, targets[0]):
                    copy.start()

            @pl.when((step == total + j) & (me_ref[0] % 2 == core))
            def _():
                for copy in up_copies(j, targets[1]):
                    copy.start()

    @pl.when(step == 2 * steps - 1)
    def _():
        for j in range(total):
            for copy in down_copies(j, send_ref):
                copy.wait()
            for copy in up_copies(j, send_ref):
                copy.wait()


def weight_grads(me, active, pre, branch, normed, places, deps=()):
    cells, hidden = active.shape
    feature = branch.shape[1]
    tiles = hidden // feature
    chips = UNITS
    shape = jax.ShapeDtypeStruct((chips, hidden // chips, feature), BF)
    return launch(
        deps,
        functools.partial(weight_grad_kernel, places),
        grid=(2 * tiles,),
        out_shape=(shape, shape),
        in_specs=[
            smem(),
            pl.BlockSpec((cells, feature), lambda i: (0, jnp.minimum(i, tiles - 1))),
            pl.BlockSpec((cells, feature), lambda i: (0, jnp.maximum(i - tiles, 0))),
            single(branch.shape), single(normed.shape),
        ],
        out_specs=(any_space(), any_space()),
        scratch_shapes=[
            pltpu.VMEM((2 * tiles, feature, feature), BF),
            pltpu.SemaphoreType.DMA((2 * tiles, chips)),
        ],
        compiler_params=params(),
        cost_estimate=cost(4 * cells * feature * hidden, 40e6),
        name="weight_grads",
    )(me, active, pre, branch, normed)


def down_kernel(rows_ref, cols_ref, active_ref, pre_ref, middle_ref, grad_ref, normal_ref, wide_ref, first_ref,
                up_ref, down_ref, mixed_ref, grad_middle_ref, half_ref, sums_ref):
    tile, feature = middle_ref.shape
    hidden = active_ref.shape[1]
    step = pl.program_id(0)

    @pl.when(step == 0)
    def _():
        sums_ref[...] = jnp.zeros_like(sums_ref)

    live = live_rows(step * tile, tile, rows_ref, cols_ref)
    branch = mm(active_ref[...], down_ref[...].reshape(hidden, feature))
    grad_normed = jnp.zeros((tile, feature), F32)
    for j in range(hidden // feature):
        pre = pre_ref[:, j * feature : (j + 1) * feature]
        grad_normed = grad_normed + mm(pre, up_part(up_ref, j, feature), (1, 1))
    middle = middle_ref[...]
    mixed_ref[...] = (middle + live * (branch + wide_ref[4:5, :])).astype(BF)
    normal, inverse = normalize(middle)
    cotangent = grad_ref[...].astype(F32)
    grad_middle = cotangent + norm_back(grad_normed, wide_ref[2:3, :], normal, inverse)
    grad_middle_ref[...] = grad_middle
    masked = grad_middle * live
    half_ref[...] = turn(first_ref, masked).reshape(half_ref.shape)
    rows = (grad_normed * normal, grad_normed, cotangent * live, masked * normal_ref[...].astype(F32), masked)
    for row, value in enumerate(rows):
        sums_ref[row : row + 1, :] += jnp.sum(value, axis=0, keepdims=True)


def feed_down(rows, cols, active, pre, middle, grad, normal, wide, table, up, down, deps=()):
    cells, feature = middle.shape
    hidden = active.shape[1]
    block = lambda width: pl.BlockSpec((CELLS, width), lambda i: (i, 0))
    operands = (rows, cols, active, pre, middle, grad, normal, wide, table, up, down)
    return launch(
        deps,
        down_kernel,
        grid=(cells // CELLS,),
        out_shape=(
            jax.ShapeDtypeStruct((cells, feature), BF),
            jax.ShapeDtypeStruct((cells, feature), F32),
            jax.ShapeDtypeStruct((KEPT, 2 * ROWS, feature), F32),
            jax.ShapeDtypeStruct((8, feature), F32),
        ),
        in_specs=[smem(), smem(), block(hidden), block(hidden), block(feature), block(feature), block(feature)]
        + [single(v.shape) for v in operands[7:]],
        out_specs=(block(feature), block(feature), column_block(KEPT, feature), single((8, feature))),
        compiler_params=params(),
        cost_estimate=cost(0, 0),
        name="feed_down",
    )(*operands)


def back_step(half_ref, head_ref, body_ref, back_head_ref, back_body_ref, mix1_ref, mix2_ref, ins, in_heads,
              outs, out_heads, out_ref, sums_ref, is_head):
    feature = out_ref.shape[2]

    def read(k):
        if is_head:
            return jnp.concatenate([ins[k][...], in_heads[k][...]], axis=0)
        return ins[k][...]

    grads = to_modes(half_ref, head_ref, body_ref, is_head)
    grad_two = (to_mixed(*grads) * read(1)).astype(BF)
    grad_one = (mix_product(grad_two, mix2_ref, True) * read(0)).astype(BF)
    grad_spec = mix_product(grad_one, mix1_ref, True)
    from_modes(from_mixed(grad_spec), back_head_ref, back_body_ref, is_head, out_ref)
    for row, value in enumerate((grad_one, grad_two)):
        outs[row][...] = value[:TOOK]
        if is_head:
            out_heads[row][...] = value[TOOK:]
    flat = jnp.concatenate([read(3)] * (feature // LANES), axis=1)
    for row, value in enumerate((grad_one.astype(F32), grad_two.astype(F32), grad_spec * read(2).astype(F32), grad_spec * flat)):
        total = jnp.sum(value, axis=0, keepdims=True)
        sums_ref[row : row + 1, :] = total if is_head else sums_ref[row : row + 1, :] + total


def mix_back_kernel(
    half_ref, slope1_ref, slope2_ref, bend1_ref, bend2_ref, low1_ref, low2_ref, flat1_ref, flat2_ref,
    slope_head_ref, bend_head_ref, low_head_ref, flat_head_ref, mix1_ref, mix2_ref,
    head_ref, body_ref, back_head_ref, back_body_ref,
    out_ref, one_ref, two_ref, one_head_ref, two_head_ref, sums_ref,
):
    step = pl.program_id(0)
    steps = pl.num_programs(0) // 2
    work = functools.partial(
        back_step, half_ref, head_ref, body_ref, back_head_ref, back_body_ref, mix1_ref, mix2_ref
    )
    heads = (slope_head_ref, bend_head_ref, low_head_ref, flat_head_ref)
    more = (heads, (one_ref, two_ref), (one_head_ref, two_head_ref), out_ref, sums_ref)
    near = (slope1_ref, bend1_ref, low1_ref, flat1_ref)
    far = (slope2_ref, bend2_ref, low2_ref, flat2_ref)

    @pl.when(step == 0)
    def _():
        sums_ref[...] = jnp.zeros_like(sums_ref)
        work(near, *more, True)

    @pl.when((step > 0) & (step < steps))
    def _():
        work(near, *more, False)

    @pl.when(step >= steps)
    def _():
        work(far, *more, False)


def mix_back(half, modes1, modes2, heads, mix1, mix2, tables, deps=()):
    feature = half.shape[2]
    steps = KEPT // GROUP // TAKE
    fixed = tuple(heads[k] for k in (2, 3, 0, 4)) + (
        mix1, mix2, tables["head_w"], tables["body_w"], tables["head_t"], tables["body_t"]
    )
    moving = []
    specs = []
    for k in (2, 3, 0, 4):
        width = modes1[k].shape[1]
        moving += [modes1[k], modes2[k]]
        specs += [
            pl.BlockSpec((TOOK, width), lambda i: (jnp.minimum(i, steps // 2 - 1), 0)),
            pl.BlockSpec((TOOK, width), lambda i: (jnp.maximum(i - steps // 2, 0), 0)),
        ]
    low = lambda rows: jax.ShapeDtypeStruct((rows, 2 * feature), BF)
    body = pl.BlockSpec((TOOK, 2 * feature), lambda i: (i, 0))
    shapes = (
        jax.ShapeDtypeStruct((KEPT, 2 * ROWS, feature), F32), low(TOOK * steps), low(TOOK * steps),
        low(ROWS), low(ROWS), jax.ShapeDtypeStruct((8, 2 * feature), F32),
    )
    return launch(
        deps,
        mix_back_kernel,
        grid=(steps,),
        out_shape=shapes,
        in_specs=[half_block(feature)] + specs + [single(v.shape) for v in fixed],
        out_specs=[half_block(feature), body, body] + [single(v.shape) for v in shapes[3:]],
        compiler_params=params(),
        cost_estimate=cost(18e9, 30e6),
        name="mix_back",
    )(half, *moving, *fixed)


def block_kernel(left1_ref, left2_ref, left_head_ref, right_ref, right_head_ref, out_ref, natural_ref):
    wide = 2 * LANES
    count = left1_ref.shape[1] // wide
    cut = left1_ref.shape[0]
    for t in range(count):
        for c in range(max(t - 1, 0), min(t + 2, count)):
            left, right = slice(t * wide, (t + 1) * wide), slice(c * wide, (c + 1) * wide)
            total = (
                mm(left1_ref[:, left], right_ref[:cut, right], (0, 0))
                + mm(left2_ref[:, left], right_ref[cut:, right], (0, 0))
                + mm(left_head_ref[:, left], right_head_ref[:, right], (0, 0))
            )
            rows, lanes = slice(t * LANES, (t + 1) * LANES), slice(c * LANES, (c + 1) * LANES)
            natural_ref[0, rows, lanes] = total[:LANES, :LANES] + total[LANES:, LANES:]
            natural_ref[1, rows, lanes] = total[:LANES, LANES:] - total[LANES:, :LANES]
    per_group = BLOCKS // 2
    block = count * LANES // per_group
    for b in range(per_group):
        begin = b * block
        base = begin // LANES * LANES
        reach = min(base + wide, count * LANES) - base
        for part in range(2):
            piece = natural_ref[part, begin : begin + block, base : base + reach]
            if begin > base:
                piece = pltpu.roll(piece, reach - (begin - base), axis=1)
            out_ref[part, b * block : (b + 1) * block, :] = piece[:, :LANES]


def block_grads(left1, left2, left_head, right, right_head, name, deps=()):
    feature = left1.shape[1] // 2
    half = feature // 2
    block = lambda v: pl.BlockSpec((v.shape[0], feature), lambda i: (0, i))
    return launch(
        deps,
        block_kernel,
        grid=(2,),
        out_shape=jax.ShapeDtypeStruct((2, feature, LANES), F32),
        in_specs=[block(v) for v in (left1, left2, left_head, right, right_head)],
        out_specs=pl.BlockSpec((2, half, LANES), lambda i: (0, i, 0)),
        scratch_shapes=[pltpu.VMEM((2, half, half), F32)],
        compiler_params=params(),
        cost_estimate=cost(5e9, 7e6),
        name=name,
    )(left1, left2, left_head, right, right_head)


def last_kernel(begin, rows_ref, cols_ref, half_ref, tokens_ref, grad_ref, first_t_ref, wide_ref, *rest):
    out_ref, mark_ref = rest[-2:]
    mark_ref[...] = jnp.zeros_like(mark_ref)
    tile, feature = tokens_ref.shape
    live = live_rows((pl.program_id(0) + begin) * tile, tile, rows_ref, cols_ref)
    grad_middle = grad_ref[...]
    grad_normed = live * (grad_middle + turn(first_t_ref, half_ref[...].reshape(CELLS, feature)))
    normal, inverse = normalize(tokens_ref[...].astype(F32))
    out_ref[...] = grad_middle + norm_back(grad_normed, wide_ref[0:1, :], normal, inverse)


def last(rows, cols, half, tokens, grad, wide, tables, begin, steps, before=(), deps=()):
    cells, feature = tokens.shape
    first_t = tables["first_t"]
    block = pl.BlockSpec((CELLS, feature), lambda i: (i + begin, 0))
    operands = (rows, cols, half, tokens, grad, first_t, wide)
    return launch(
        deps,
        functools.partial(last_kernel, begin),
        grid=(steps,),
        out_shape=(jax.ShapeDtypeStruct((cells, feature), F32), MARK),
        in_specs=[smem(), smem(), pl.BlockSpec((KEPT, 2 * GROUP, feature), lambda i: (0, i + begin, 0)), block, block,
                  single(first_t.shape), single(wide.shape)] + [any_space() for _ in before],
        out_specs=(block, single(MARK.shape)),
        input_output_aliases={len(operands): 0} if before else {},
        compiler_params=params(),
        cost_estimate=cost(6e9, 20e6),
        name="last",
    )(*operands, *before)


def collect(value, per_device, devices):
    total = value.shape[1]
    owner = lax.broadcasted_iota(jnp.int32, (devices, total), 1) // per_device
    row = lax.broadcasted_iota(jnp.int32, (devices, total), 0)
    high, low = split(jnp.where(owner == row, jnp.broadcast_to(value, (devices, total)), 0.0))
    place = lax.broadcasted_iota(jnp.int32, (total, LANES), 0)
    lane = lax.broadcasted_iota(jnp.int32, (total, LANES), 1)
    pick = jnp.where(place % per_device == lane, 1.0, 0.0).astype(BF)
    return mm(high, pick) + mm(low, pick)


def emit(place, sum_ref, send_refs, keep_ref):
    half, _, rows, _ = sum_ref.shape
    rows = rows - 8
    for k, send_ref in enumerate(send_refs):
        away = sum_ref[:, pl.ds(place ^ (k + 1), 1)].reshape(half, rows + 8, LANES)
        high, low = split(away[:, rows:])
        send_ref[:, :rows] = away[:, :rows].astype(BF)
        send_ref[:, rows:] = jnp.concatenate([high.astype(F32), low.astype(F32)], axis=1).astype(BF)
    keep_ref[...] = sum_ref[:, pl.ds(place, 1)].reshape(half, rows + 8, LANES)


def pack_kernel(place_ref, one_ref, two_ref, mixed_ref, sums_ref, up_ref, wide_ref, send_ref, keep_ref, sum_ref):
    half, _, rows, _ = sum_ref.shape
    devices = 2 * half
    share = (rows - 8) // 4
    feature = sums_ref.shape[1]
    sum_ref[:, :, : 2 * share] = one_ref[...].reshape(half, 2, 2 * share, LANES)
    sum_ref[:, :, 2 * share : 4 * share] = two_ref[...].reshape(half, 2, 2 * share, LANES)
    first_gain, first_bias = scale_grads(mixed_ref, sums_ref, wide_ref)
    natural = [jnp.concatenate(from_mixed(mixed_ref[k : k + 1, :]), axis=1) for k in range(2)]
    narrow = [first_gain, first_bias] + [sums_ref[k : k + 1, :] for k in range(3)]
    for k, value in enumerate(narrow + natural + [up_ref[...]]):
        placed = collect(value, value.shape[1] // devices, devices)
        for d in range(devices):
            sum_ref[d // 2, d % 2, 4 * share + k : 4 * share + k + 1, :] = placed[d : d + 1, :]
    emit(place_ref[0], sum_ref, (send_ref,), keep_ref)


def scale_grads(mixed_ref, sums_ref, wide_ref):
    real, imag = from_mixed(mixed_ref[2:3, :])
    scaled = real + imag
    real, imag = from_mixed(mixed_ref[3:4, :])
    flat = real + imag
    gain = sums_ref[3:4, :] + (scaled - wide_ref[1:2, :] * flat) / wide_ref[0:1, :]
    return gain, sums_ref[4:5, :] + flat


def small_shapes(half, rows, others):
    shapes = [jax.ShapeDtypeStruct((half, rows + 8, LANES), BF)] * others
    return shapes + [jax.ShapeDtypeStruct((half, rows, LANES), F32)]


def pack(upper, one, two, mixed, sums, up, wide, devices):
    rows = 2 * one.shape[0] * one.shape[1] // devices + 8
    shapes = small_shapes(devices // 2, rows, 1)
    operands = (one, two, mixed, sums, up, wide)
    return pl.pallas_call(
        pack_kernel,
        out_shape=shapes,
        in_specs=[smem()] + vmem(len(operands)),
        out_specs=vmem(2),
        scratch_shapes=[pltpu.VMEM((devices // 2, 2, rows, LANES), F32)],
        compiler_params=params(),
        cost_estimate=cost(0, 0),
        name="pack",
    )(upper, *operands)


def merge_small(keep_ref, got_refs):
    rows = keep_ref.shape[1] - 8
    top, tail = keep_ref[:, :rows], keep_ref[:, rows:]
    for got_ref in got_refs:
        both = got_ref[:, rows:].astype(F32)
        top = top + got_ref[:, :rows].astype(F32)
        tail = tail + (both[:, :8] + both[:, 8:])
    return top, tail


def fold_small_kernel(others, place_ref, keep_ref, *rest):
    sum_ref = rest[-1]
    send_refs, out_ref = rest[-2 - others : -2], rest[-2]
    half, count, rows, _ = sum_ref.shape
    top, tail = merge_small(keep_ref, rest[: len(rest) - 2 - others])
    sum_ref[:, :, : rows - 8] = top.reshape(half, count, rows - 8, LANES)
    sum_ref[:, :, rows - 8 :] = tail.reshape(half, count, 8, LANES)
    emit(place_ref[0], sum_ref, send_refs, out_ref)


def fold_small(keep, got, place, count, deps=()):
    half, rows = keep.shape[0] // count, keep.shape[1]
    shapes = small_shapes(half, rows, count - 1)
    return launch(
        deps,
        functools.partial(fold_small_kernel, count - 1),
        out_shape=shapes,
        in_specs=[smem()] + vmem(1 + len(got)),
        out_specs=vmem(len(shapes)),
        scratch_shapes=[pltpu.VMEM((half, count, rows, LANES), F32)],
        compiler_params=params(SMALL_LIMIT),
        cost_estimate=cost(0, 0),
        name="fold_small",
    )(place, keep, *got)


def vmem(count):
    return [pl.BlockSpec(memory_space=pltpu.VMEM)] * count


def end_small_kernel(others, keep_ref, *rest):
    got_refs, (one_ref, two_ref, *rows_refs) = rest[:others], rest[others:]
    top, tail = merge_small(keep_ref, got_refs)
    share, block = one_ref.shape
    one_ref[...] = top[0, :share, :block]
    two_ref[...] = top[0, share:, :block]
    for row, ref in enumerate(rows_refs):
        ref[...] = tail[0, row : row + 1, : ref.shape[1]]


def end_small(keep, got, share, block, widths):
    shapes = [jax.ShapeDtypeStruct((share, block), F32)] * 2
    shapes += [jax.ShapeDtypeStruct((1, width), F32) for width in widths]
    return pl.pallas_call(
        functools.partial(end_small_kernel, len(got)),
        out_shape=shapes,
        in_specs=vmem(1 + len(got)),
        out_specs=vmem(len(shapes)),
        compiler_params=params(SMALL_LIMIT),
        cost_estimate=cost(0, 0),
        name="end_small",
    )(keep, *got)


def begin_small_kernel(one_ref, two_ref, *rest):
    out_ref, rows_ref = rest[-2:]
    share, block = one_ref.shape
    out_ref[...] = jnp.zeros_like(out_ref)
    rows_ref[...] = jnp.zeros_like(rows_ref)
    out_ref[0, :share, :block] = one_ref[...]
    out_ref[0, share : 2 * share, :block] = two_ref[...]
    for row, ref in enumerate(rest[:-2]):
        rows_ref[row : row + 1, : ref.shape[1]] = ref[...].astype(F32)
    out_ref[0, 2 * share :, :] = rows_ref[...].astype(BF)


def begin_small(one, two, vectors):
    share = one.shape[0]
    operands = (one, two) + tuple(v[None] for v in vectors)
    return pl.pallas_call(
        begin_small_kernel,
        out_shape=jax.ShapeDtypeStruct((1, 2 * share + 16, LANES), BF),
        in_specs=vmem(len(operands)),
        out_specs=vmem(1)[0],
        scratch_shapes=[pltpu.VMEM((16, LANES), F32)],
        compiler_params=params(),
        cost_estimate=cost(0, 0),
        name="begin_small",
    )(*operands)


AXES = ("dp", "fsdp")


def swap(value, devices, bits):
    return lax.ppermute(value, AXES, [(i, i ^ (1 << bits[i & 1])) for i in range(devices)])


def doubling_orders(count):
    first = list(range(count - 1, 0, -1))
    second = list(first)
    for k in range(0, len(second) - 1, 2):
        second[k], second[k + 1] = second[k + 1], second[k]
    return first, second


def places_of(order):
    return [
        sum(1 << k for k, bit in enumerate(order) if mask >> (bit - 1) & 1) for mask in range(1 << len(order))
    ]


def join_kernel(*refs):
    out_ref = refs[-1]
    count = refs[0].shape[0]
    for k, ref in enumerate(refs[:-1]):
        out_ref[k * count : (k + 1) * count] = ref[...]


def join_rows(*pieces, deps=()):
    shape = jax.ShapeDtypeStruct((len(pieces) * pieces[0].shape[0],) + pieces[0].shape[1:], pieces[0].dtype)
    return launch(
        deps,
        join_kernel,
        out_shape=shape,
        in_specs=[pl.BlockSpec(memory_space=pltpu.VMEM) for _ in pieces],
        out_specs=pl.BlockSpec(memory_space=pltpu.VMEM),
        compiler_params=params(SMALL_LIMIT),
        cost_estimate=cost(0, 0),
        name="join",
    )(*pieces)


def hold(value, deps):
    def body(*refs):
        pass

    return pl.pallas_call(
        body,
        out_shape=jax.ShapeDtypeStruct(value.shape, value.dtype),
        in_specs=[any_space() for _ in range(1 + len(deps))],
        out_specs=any_space(),
        input_output_aliases={0: 0},
        compiler_params=params(SMALL_LIMIT),
        cost_estimate=cost(0, 0),
        name="hold",
    )(value, *deps)


def gather_small(value, me, devices, count):
    held = value[None]
    for bit in list(range(3, count)) + [2, 1, 0]:
        other = swap(held, devices, (bit, bit))
        upper = (me >> bit) & 1
        axis = 0 if bit > 2 else 1
        join_two = lambda a, b: jnp.stack([a, b], axis=axis).reshape((-1,) + value.shape)
        held = jnp.where(upper == 0, join_two(held, other), join_two(other, held))
    return held


def scatter_small(value, me, devices, count, exact):
    shape = value.shape[1:]
    rows = shape[0]
    total = value
    for bit in [0, 1, 2] + list(range(count - 1, 2, -1)):
        upper = (me >> bit) & 1
        axis = 0 if bit > 2 else 1
        pair = total.reshape(((2, -1) if bit > 2 else (-1, 2)) + shape)
        away = lax.dynamic_index_in_dim(pair, 1 - upper, axis, keepdims=False)
        keep = lax.dynamic_index_in_dim(pair, upper, axis, keepdims=False)
        sums = away[:, rows - exact :]
        top = lax.reduce_precision(sums, 8, 7)
        packet = jnp.concatenate([away[:, : rows - exact], top, sums - top], axis=1).astype(BF)
        got = swap(packet, devices, (bit, bit)).astype(F32)
        low = got[:, rows - exact : rows] + got[:, rows:]
        total = keep + jnp.concatenate([got[:, : rows - exact], low], axis=1)
    return total[0]


def chip_unit(up, down, core, devices):
    parts, share, feature = up.shape
    flat = up.reshape(parts * share, feature)
    other = swap(jnp.where(core == 0, down, flat), devices, (0, 0))
    up_unit = jnp.concatenate([up, other.reshape(up.shape)], axis=1).reshape(2 * parts * share, feature)
    return jnp.where(core == 0, up_unit, jnp.concatenate([other, down]))[None]


def fold_kernel(upper_ref, keep_away_ref, got_away_ref, keep_own_ref, got_own_ref, send_ref, keep_ref):
    send_ref[...] = (keep_away_ref[...].astype(F32) + got_away_ref[...].astype(F32)).astype(BF)
    keep_ref[...] = (keep_own_ref[...].astype(F32) + got_own_ref[...].astype(F32)).astype(BF)


def fold(keep, got, upper, deps=()):
    half = keep.shape[0] // 2
    each = min(2, half)
    unit = (each,) + keep.shape[1:]
    count = len(deps)
    away = pl.BlockSpec(unit, lambda i, up: ((1 - up[0]) * (half // each) + i, 0, 0))
    own = pl.BlockSpec(unit, lambda i, up: (up[0] * (half // each) + i, 0, 0))
    out = pl.BlockSpec(unit, lambda i, up: (i, 0, 0))
    shape = jax.ShapeDtypeStruct((half,) + keep.shape[1:], BF)

    def body(*refs):
        fold_kernel(*refs[:5], *refs[5 + count :])

    return pl.pallas_call(
        body,
        grid_spec=pltpu.PrefetchScalarGridSpec(
            num_scalar_prefetch=1,
            grid=(half // each,),
            in_specs=[away, away, own, own] + [any_space() for _ in deps],
            out_specs=[out, out],
        ),
        out_shape=(shape, shape),
        compiler_params=params(),
        cost_estimate=cost(0, 6 * half * keep[0].size),
        name="fold",
    )(upper, keep, got, keep, got, *deps)


def on_device(
    tokens, grad_out, region_rows, region_cols, ln1_gain, ln1_bias, spec_w1, spec_b1, spec_w2, spec_b2,
    ln2_gain, ln2_bias, w_up, up_bias, w_down, down_bias,
):
    devices = lax.axis_size(AXES[0]) * lax.axis_size(AXES[1])
    count = devices.bit_length() - 1
    me = lax.axis_index(AXES).astype(jnp.int32)
    core = me & 1
    me_one = me.reshape(1)
    feature = tokens.shape[-1]
    block = feature // BLOCKS
    share = ln1_gain.shape[0]
    cells = tokens.shape[1] * tokens.shape[2]
    hidden = w_up.shape[1]
    parts = hidden // feature
    tables = {name: jnp.asarray(value) for name, value in wave_matrices().items()}
    orders = doubling_orders(count)
    places = tuple(places_of(order) for order in orders)
    flat_tokens = tokens.reshape(cells, feature)
    flat_grad = grad_out.reshape(cells, feature)
    fast = devices // 2 == UNITS
    step = lambda value, k: swap(value, devices, (orders[0][k], orders[1][k]))

    padded = lambda v: jnp.pad(v, ((0, 0), (0, LANES - v.shape[1])))
    vectors = (spec_b1, spec_b2, ln1_gain, ln1_bias, ln2_gain, ln2_bias, up_bias, down_bias)
    if fast:
        own_up = w_up.reshape(share, parts, feature).transpose(1, 0, 2)
        unit = chip_unit(own_up, w_down, core, devices)
        bits = (3, 4, 2, 1, 0)
        hop = lambda value, mask: lax.ppermute(value, AXES, [(i, i ^ mask) for i in range(devices)])
        meet = lambda value, bit: hop(value, 1 << bit)
        small = begin_small(spec_w1, spec_w2, vectors)
        made = first(region_rows, region_cols, flat_tokens, tables, 0, 2, deps=(unit, small), tiles=2)
        small = join_rows(small, *(hop(small, mask) for mask in (8, 16, 24)), deps=(made[2],))
        near = join_rows(unit, step(unit, 0), deps=(small,))
        half, normal, mark = first(region_rows, region_cols, flat_tokens, tables, 2, 2, made[:2], deps=(near,), tiles=2)
        small = join_rows(small, *(hop(small, mask) for mask in (4, 2, 6)), deps=(mark,))
        small = join_rows(small, meet(small, 0))
        near = join_rows(near, step(near, 1), deps=(small,))
        beside, across = step(near, 2), step(near, 3)
        weights, weight_bits, vector_bits, me_small = small, bits, bits, me_one
        vectors = jnp.zeros((8, 1, LANES), F32)
    else:
        up = lax.all_gather(w_up, AXES, axis=0, tiled=True)
        up = up.reshape(UNITS, feature // UNITS, parts, feature).transpose(0, 2, 1, 3).reshape(UNITS, -1, feature)
        down = lax.all_gather(w_down, AXES, axis=0, tiled=True).reshape(UNITS, -1, feature)
        pieces = tuple(
            jnp.where(core == 0, one, two)[begin : begin + UNITS // 2]
            for one, two in ((up, down), (down, up))
            for begin in (0, UNITS // 2)
        )
        me_one = core.reshape(1)
        me_small = jnp.zeros_like(me_one)
        places = (tuple(range(UNITS)),) * 2
        small = jnp.concatenate([padded(spec_w1), padded(spec_w2)] + [padded(v[None]) for v in vectors])
        small = gather_small(small, me, devices, count)
        weights = small[:, : 4 * share].reshape(devices, 2, 2 * share, LANES).transpose(1, 0, 2, 3)
        weights = weights.reshape(2, 2 * UNITS, -1, LANES).transpose(1, 0, 2, 3).reshape(2 * UNITS, -1, LANES)
        weight_bits, vector_bits = tuple(range(5)), tuple(range(count))
        half, normal, _ = first(region_rows, region_cols, flat_tokens, tables, 0, STEPS)
        vectors = small[:, 4 * share :].transpose(1, 0, 2).astype(F32)

    steps = KEPT // GROUP // TAKE
    core_swap = lambda value: swap(value, devices, (0, 0))
    made = mix_first(
        me_small, half, weights, vectors, tables, hidden, steps // 2, weight_bits, vector_bits,
        deps=(near,) if fast else (),
    )
    half1, modes1, heads, (mix1, mix2, wide, long, up_shift) = made[0], made[1:6], made[6:11], made[11:]
    deps = ()
    if fast:
        other_near = core_swap(near)
        deps = (other_near,)
    made = mix_second(half, mix1, mix2, wide, long, tables, steps // 2, steps // 2, deps=deps)
    half2, modes2 = made[0], made[1:6]
    if fast:
        beside = hold(beside, (modes2[4],))
        far = step(beside, 3)
        deps = (beside,)
    middle, normed, mark = space(region_rows, region_cols, half1, half2, flat_tokens, wide, tables, deps=deps, tiles=2)
    if fast:
        far = hold(far, (mark,))
        pieces = (near, beside, across, far, other_near) + tuple(core_swap(v) for v in (beside, across, far))
    active, pre, branch, bias_grad, up_all, down_all = feed_up(
        region_rows, region_cols, me_one, normed, flat_grad, up_shift, pieces, places
    )
    send, keep = weight_grads(me_one, active, pre, branch, normed, places)
    tiles = cells // CELLS
    mixed, grad_middle, half_back, sums_two = feed_down(
        region_rows, region_cols, active, pre, middle, flat_grad, normal, wide, tables["first"], up_all, down_all,
        deps=(send,),
    )
    deps = ()
    if fast:
        ranks = [((me >> jnp.where(core == 0, *bit)) & 1).reshape(1) for bit in zip(*orders)]
        send, keep = fold(keep, swap(send, devices, (0, 0)), ranks[3], deps=(sums_two,))
        deps = (send,)
    half_back, one, two, one_head, two_head, bias_sums = mix_back(
        half_back, modes1, modes2, heads, mix1, mix2, tables, deps=deps
    )
    grad_one = block_grads(modes1[0], modes2[0], heads[0], one, one_head, "grad_mix1")
    if fast:
        send, keep = fold(keep, step(send, 3), ranks[2], deps=(grad_one,))
        deps = (send,)
    grad_two = block_grads(modes1[1], modes2[1], heads[1], two, two_head, "grad_mix2", deps=deps)
    last_args = (region_rows, region_cols, half_back, flat_tokens, grad_middle, wide, tables)
    if fast:
        places_small = [v.reshape(1) for v in (me & 1, (me >> 1) & 3, me >> 3)]
        away, own = pack(places_small[0], grad_one, grad_two, bias_sums, sums_two, bias_grad, wide, devices)
        grad_tokens, mark = last(*last_args, 0, 2, deps=(away,))
        *aways, own = fold_small(own, (hop(away, 1),), places_small[1], 4, deps=(mark,))
        send, keep = fold(keep, step(send, 2), ranks[1], deps=tuple(aways))
        gots = tuple(hop(v, mask) for v, mask in zip(aways, (2, 4, 6)))
        grad_tokens, mark = last(*last_args, 2, 2, (grad_tokens,), deps=(send,))
        *aways, own = fold_small(own, gots, places_small[2], 4, deps=(mark,))
        gots = tuple(hop(v, mask) for v, mask in zip(aways, (8, 16, 24)))
        grad_tokens, mark = last(*last_args, 4, 2, (grad_tokens,), deps=tuple(aways))
        send, keep = fold(keep, step(send, 1), ranks[0], deps=(mark, gots[0]))
        grad_tokens, mark = last(*last_args, 6, 2, (grad_tokens,), deps=(send,))
        widths = (share,) * 5 + (2 * share,) * 2 + (hidden // devices,)
        blocks = end_small(hold(own, (mark,)), gots, 2 * share, block, widths)
        keep = hold(keep, (blocks[0],))
        total = keep[0].astype(F32) + step(send, 0)[0].astype(F32)
        up_sum = total.reshape(parts, 2 * share, feature)
        lower = up_sum[:, :share].reshape(parts * share, feature)
        upper = up_sum[:, share:].reshape(parts * share, feature)
        each = parts * share
        leaving = jnp.where(core == 0, upper, total[:each])
        other = swap(leaving, devices, (0, 0))
        grad_w_up = jnp.where(core == 0, lower, other).reshape(parts, share, feature).transpose(1, 0, 2)
        grad_w_down = jnp.where(core == 0, other, total[each:])
        rows = [v.reshape(-1) for v in blocks[2:]]
        blocks = blocks[:2]
    else:
        scatter = lambda v: lax.psum_scatter(v.astype(F32), AXES, scatter_dimension=0, tiled=True)
        up = jnp.where(core == 0, keep, send).reshape(UNITS, parts, feature // UNITS, feature)
        grad_w_up = scatter(up.transpose(0, 2, 1, 3).reshape(feature, hidden))
        grad_w_down = scatter(jnp.where(core == 0, send, keep).reshape(hidden, feature))
        grad_tokens, _ = last(*last_args, 0, tiles)
        owned = lambda v: jnp.pad(
            v.reshape(v.shape[0], devices, -1).transpose(1, 0, 2), ((0, 0), (0, 0), (0, LANES - v.shape[1] // devices))
        )
        narrow = jnp.concatenate(list(scale_grads(bias_sums, sums_two, wide)) + [sums_two[:3]])
        biases = bias_sums[:2].reshape(2, feature // LANES, 2, LANES).transpose(0, 2, 1, 3).reshape(2, 2 * feature)
        blocks = [v.reshape(devices, 2 * share, LANES) for v in (grad_one, grad_two)]
        packet = jnp.concatenate(blocks + [owned(narrow), owned(biases), owned(bias_grad)], axis=1)
        result = scatter_small(packet, me, devices, count, 8)
        widths = (share,) * 5 + (2 * share,) * 2 + (hidden // devices,)
        rows = [result[4 * share + k, :width] for k, width in enumerate(widths)]
        blocks = [result[k * 2 * share : (k + 1) * 2 * share, :block] for k in range(2)]
    return (
        mixed.reshape(tokens.shape),
        grad_tokens.reshape(tokens.shape),
        rows[0],
        rows[1],
        blocks[0],
        rows[5],
        blocks[1],
        rows[6],
        rows[2],
        rows[3],
        grad_w_up.reshape(share, hidden),
        rows[7],
        grad_w_down,
        rows[4],
    )


def solution(mesh):
    placed = P(AXES)
    return jax.shard_map(
        on_device, mesh=mesh, in_specs=(placed,) * 16, out_specs=(placed,) * 14, check_vma=False
    )
```

```python
import functools
import math

import jax
import jax.numpy as jnp
import numpy as np
from jax import lax
from jax.experimental import pallas as pl
from jax.experimental.pallas import tpu as pltpu
from jax.sharding import PartitionSpec as P

BF = jnp.bfloat16
F32 = jnp.float32
BLOCKS = 8
EPS = 1e-05
SHRINK = 0.01
ROWS = 32
COLS = 64
KEPT = COLS // 2
GROUP = 4
STEPS = ROWS // GROUP
CELLS = GROUP * COLS
MODES = (KEPT + 1) * ROWS
HEAD = (GROUP + 1) * ROWS
BODY = GROUP * ROWS
TAKE = 2
TOOK = TAKE * BODY
LANES = 128
C1 = math.sqrt(2.0 / math.pi)
C3 = 0.044715
SIGMOID = -2.0 * C1 / math.log(2.0)
UNITS = 16
VMEM_LIMIT = 60 * 1024 * 1024
SMALL_LIMIT = 36 * 1024 * 1024


def table_parts(values):
    high = values.astype(np.float32).astype(jnp.bfloat16)
    low = (values - high.astype(np.float64)).astype(np.float32).astype(jnp.bfloat16)
    return np.stack([high, low])


def wave_matrices():
    scale = 1.0 / math.sqrt(ROWS * COLS)
    w = np.arange(COLS)
    first = np.zeros((KEPT, 2, GROUP, GROUP, COLS))
    for k in range(KEPT):
        for h in range(GROUP):
            if k == 0:
                first[k, 0, h, h] = scale
                first[k, 1, h, h] = scale * np.where(w % 2 == 0, 1.0, -1.0)
            else:
                first[k, 0, h, h] = scale * np.cos(2 * np.pi * (k * w % COLS) / COLS)
                first[k, 1, h, h] = -scale * np.sin(2 * np.pi * (k * w % COLS) / COLS)
    first = first.reshape(CELLS, CELLS)
    p = np.arange(ROWS)
    turn = 2 * np.pi * (np.outer(p, p) % ROWS) / ROWS
    cos = np.cos(turn).reshape(ROWS, STEPS, GROUP)
    sin = np.sin(turn).reshape(ROWS, STEPS, GROUP)
    body = np.zeros((2, GROUP, ROWS, GROUP, STEPS, 2, GROUP))
    head = np.zeros((2, GROUP + 1, ROWS, GROUP, STEPS, 2, GROUP))
    for k in range(GROUP):
        body[0, k, :, k, :, 0] = cos
        body[0, k, :, k, :, 1] = sin
        body[1, k, :, k, :, 1] = cos
        body[1, k, :, k, :, 0] = -sin
    head[:, 1:GROUP, :, 1:] = body[:, 1:, :, 1:]
    for place, part in ((0, 0), (GROUP, 1)):
        head[0, place, :, 0, :, part] = cos
        head[1, place, :, 0, :, part] = -sin
    weight = np.full((2, GROUP + 1, ROWS, 1), 2.0)
    weight[:, 0] = 1.0
    weight[:, GROUP] = 1.0
    head = head.reshape(2 * HEAD, 2 * BODY)
    body = body.reshape(2 * BODY, 2 * BODY)
    head_weighted = head * weight.reshape(2 * HEAD, 1)
    body_weighted = body * 2.0
    return {
        "first": table_parts(first),
        "first_t": table_parts(first.T),
        "head": table_parts(head),
        "body": table_parts(body),
        "head_t": table_parts(head.T),
        "body_t": table_parts(body.T),
        "head_w": table_parts(head_weighted),
        "body_w": table_parts(body_weighted),
        "head_wt": table_parts(head_weighted.T),
        "body_wt": table_parts(body_weighted.T),
    }


def mm(left, right, dims=(1, 0)):
    return lax.dot_general(
        left, right, (((dims[0],), (dims[1],)), ((), ())), preferred_element_type=F32
    )


def split(values):
    high = values.astype(BF)
    return high, (values - high.astype(F32)).astype(BF)


def turn(table, values):
    high, low = split(values)
    return mm(table[0], high) + mm(table[1], high) + mm(table[0], low)


def normalize(values):
    centred = values - jnp.mean(values, axis=-1, keepdims=True)
    inverse = lax.rsqrt(jnp.mean(centred * centred, axis=-1, keepdims=True) + EPS)
    return centred * inverse, inverse


def norm_back(grad, gain, normal, inverse):
    scaled = grad * gain
    return inverse * (
        scaled
        - jnp.mean(scaled, axis=-1, keepdims=True)
        - normal * jnp.mean(scaled * normal, axis=-1, keepdims=True)
    )


def gelu_parts(value):
    square = value * value
    half = 1.0 / (1.0 + jnp.exp2(value * (SIGMOID + (SIGMOID * C3) * square)))
    active = value * half
    slope = half + active * (1.0 - half) * (2.0 * C1 + (6.0 * C1 * C3) * square)
    return active, slope


def live_rows(start, count, rows_ref, cols_ref):
    cell = start + lax.broadcasted_iota(jnp.int32, (count, 1), 0)
    inside = (cell // COLS < rows_ref[0]) & (cell % COLS < cols_ref[0])
    return jnp.where(inside, 1.0, 0.0).astype(F32)


def spread(piece, per_device, me, bits):
    devices = piece.shape[0]
    total = devices * per_device
    lane = lax.broadcasted_iota(jnp.int32, (LANES, total), 0)
    place = lax.broadcasted_iota(jnp.int32, (LANES, total), 1)
    pick = jnp.where(place % per_device == lane, 1.0, 0.0).astype(BF)
    wide = mm(piece.astype(BF), pick)
    row = lax.broadcasted_iota(jnp.int32, (devices, 1), 0)
    owner = jnp.full((devices, 1), me, jnp.int32)
    for k, bit in enumerate(bits):
        owner = owner ^ (((row >> k) & 1) << bit)
    where = lax.broadcasted_iota(jnp.int32, (devices, total), 1) // per_device
    return jnp.sum(jnp.where(owner == where, wide, 0.0), axis=0, keepdims=True)


def place_of(mask, bits):
    return sum(((mask >> bit) & 1) << k for k, bit in enumerate(bits))


def any_space():
    return pl.BlockSpec(memory_space=pl.ANY)


def single(shape):
    return pl.BlockSpec(shape, lambda *_: (0,) * len(shape), pipeline_mode=pl.Buffered(1))


def smem():
    return pl.BlockSpec(memory_space=pltpu.SMEM)


def params(limit=VMEM_LIMIT):
    return pltpu.CompilerParams(vmem_limit_bytes=limit)


def cost(flops, moved):
    return pl.CostEstimate(flops=0, bytes_accessed=0, transcendentals=0)


def launch(deps, kernel, *, in_specs, **more):
    count = len(in_specs)

    def body(*refs):
        kernel(*refs[:count], *refs[count + len(deps) :])

    call = pl.pallas_call(body, in_specs=list(in_specs) + [any_space() for _ in deps], **more)
    return lambda *operands: call(*operands, *deps)


MARK = jax.ShapeDtypeStruct((8, LANES), F32)


def to_mixed(real, imag):
    tiles = []
    for at in range(0, real.shape[1], LANES):
        tiles += [real[:, at : at + LANES], imag[:, at : at + LANES]]
    return jnp.concatenate(tiles, axis=1)


def from_mixed(values):
    cut = lambda at: values[:, at : at + LANES]
    real = [cut(at) for at in range(0, values.shape[1], 2 * LANES)]
    imag = [cut(at + LANES) for at in range(0, values.shape[1], 2 * LANES)]
    return jnp.concatenate(real, axis=1), jnp.concatenate(imag, axis=1)


def mix_product(values, matrix_ref, back=False):
    feature = values.shape[1] // 2
    wide = 2 * LANES
    groups = []
    for group in range(2):
        part = values[:, group * feature : (group + 1) * feature]
        count = feature // wide
        for t in range(count):
            begin, end = max(t - 1, 0) * wide, min(t + 2, count) * wide
            here = slice(t * wide, (t + 1) * wide)
            if back:
                groups.append(mm(part[:, begin:end], matrix_ref[group, here, begin:end], (1, 1)))
            else:
                groups.append(mm(part[:, begin:end], matrix_ref[group, begin:end, here]))
    return jnp.concatenate(groups, axis=1)


def first_kernel(begin, rows_ref, cols_ref, tokens_ref, first_ref, *rest):
    half_ref, normal_ref, mark_ref = rest[-3:]
    mark_ref[...] = jnp.zeros_like(mark_ref)
    feature = tokens_ref.shape[1]
    start = (pl.program_id(0) + begin) * tokens_ref.shape[0]
    for k in range(tokens_ref.shape[0] // CELLS):
        here = slice(k * CELLS, (k + 1) * CELLS)
        there = slice(k * 2 * GROUP, (k + 1) * 2 * GROUP)
        normal, _ = normalize(tokens_ref[here, :].astype(F32))
        live = live_rows(start + k * CELLS, CELLS, rows_ref, cols_ref)
        normal = normal * live
        normal_ref[here, :] = normal.astype(BF)
        half_ref[:, there, :feature] = turn(first_ref, normal).reshape(KEPT, 2 * GROUP, feature)
        ones = jnp.broadcast_to(live, (CELLS, LANES)).astype(BF)
        flat = mm(first_ref[0], ones) + mm(first_ref[1], ones)
        half_ref[:, there, feature:] = flat.reshape(KEPT, 2 * GROUP, LANES)


def first(rows, cols, tokens, tables, begin, steps, before=(), deps=(), tiles=1):
    cells, feature = tokens.shape
    table = tables["first"]
    block = pl.BlockSpec((tiles * CELLS, feature), lambda i: (i + begin, 0))
    operands = (rows, cols, tokens, table)
    return launch(
        deps,
        functools.partial(first_kernel, begin),
        grid=(steps,),
        out_shape=(
            jax.ShapeDtypeStruct((KEPT, 2 * ROWS, feature + LANES), F32),
            jax.ShapeDtypeStruct((cells, feature), BF),
            MARK,
        ),
        in_specs=[smem(), smem(), block, single(table.shape)] + [any_space() for _ in before],
        out_specs=(
            pl.BlockSpec((KEPT, 2 * GROUP * tiles, feature + LANES), lambda i: (0, i + begin, 0)),
            block,
            single(MARK.shape),
        ),
        input_output_aliases={len(operands) + k: k for k in range(len(before))},
        compiler_params=params(),
        cost_estimate=cost(6e9, 11e6),
        name="first",
    )(*operands, *before)


def build_mix(me, bits, weights_ref, layer, out_ref, feature):
    block = feature // BLOCKS
    half = feature // 2
    per_group = BLOCKS // 2
    share = 2 * feature // weights_ref.shape[0]
    each = block // share
    out_ref[...] = jnp.zeros_like(out_ref)
    row = lax.broadcasted_iota(jnp.int32, (LANES, half), 0)
    column = lax.broadcasted_iota(jnp.int32, (LANES, half), 1)
    for b in range(per_group):
        shift = jnp.where((column - b * block == row) & (row < block), 1.0, 0.0).astype(BF)
        low, high = b * block, (b + 1) * block
        for group in range(2):
            for part in range(2):
                at = (part * BLOCKS + group * per_group + b) * each
                pieces = [
                    weights_ref[place_of((at + k) ^ me, bits), layer * share : (layer + 1) * share, :]
                    for k in range(each)
                ]
                placed = mm(jnp.concatenate(pieces, axis=0), shift).astype(BF)
                for t in range(low // LANES, (high - 1) // LANES + 1):
                    begin, end = max(low, t * LANES), min(high, (t + 1) * LANES)
                    for c in range(low // LANES, (high - 1) // LANES + 1):
                        piece = placed[begin - low : end - low, c * LANES : (c + 1) * LANES]
                        for up in range(2):
                            top = 2 * t * LANES + up * LANES + begin - t * LANES
                            left = (2 * c + (up ^ part)) * LANES
                            value = -piece if part == 1 and up == 1 else piece
                            here = (group, slice(top, top + end - begin), slice(left, left + LANES))
                            out_ref[here] = out_ref[here] + value


def to_modes(half_ref, head_ref, body_ref, is_head):
    width = half_ref.shape[2]
    real, imag, ends = [], [], ()
    for k in range(TAKE):
        begin = is_head and k == 0
        rows = HEAD if begin else BODY
        spec = turn(head_ref if begin else body_ref, half_ref[k * GROUP : (k + 1) * GROUP].reshape(2 * BODY, width))
        real.append(spec[:BODY])
        imag.append(spec[rows : rows + BODY])
        if begin:
            ends = (spec[BODY:rows], spec[rows + BODY :])
    if is_head:
        real.append(ends[0])
        imag.append(ends[1])
    return jnp.concatenate(real, axis=0), jnp.concatenate(imag, axis=0)


def from_modes(pair_of, head_ref, body_ref, is_head, out_ref):
    for k in range(TAKE):
        begin = is_head and k == 0
        parts = []
        for part in pair_of:
            parts.append(part[k * BODY : (k + 1) * BODY])
            if begin:
                parts.append(part[TOOK:])
        result = turn(head_ref if begin else body_ref, jnp.concatenate(parts, axis=0))
        out_ref[k * GROUP : (k + 1) * GROUP] = result.reshape(GROUP, 2 * ROWS, result.shape[1])


def mix_step(half_ref, head_ref, body_ref, back_head_ref, back_body_ref, mix1_ref, mix2_ref, wide_ref, long_ref,
             outs, heads, out_ref, is_head):
    feature = out_ref.shape[2]
    specs = to_modes(half_ref, head_ref, body_ref, is_head)
    gain = wide_ref[0:1, :]
    shift = wide_ref[1:2, :]

    def scaled(part):
        flat = jnp.concatenate([part[:, feature:]] * (feature // LANES), axis=1)
        return (part[:, :feature] * gain + flat * shift).astype(BF)

    inside = to_mixed(*(scaled(part) for part in specs))
    active, slope = gelu_parts(mix_product(inside, mix1_ref) + long_ref[0:1, :])
    hidden = active.astype(BF)
    value = mix_product(hidden, mix2_ref) + long_ref[1:2, :]
    bend = jnp.tanh(value / SHRINK)
    flat = jnp.concatenate([part[:, feature:] for part in specs], axis=1)
    for ref, head, kept in zip(outs, heads, (inside, hidden, slope, bend * bend, flat)):
        ref[...] = kept[:TOOK]
        if is_head:
            head[...] = kept[TOOK:]
    from_modes(from_mixed(value - SHRINK * bend), back_head_ref, back_body_ref, is_head, out_ref)


def prepare_kernel(
    weight_bits, vector_bits, me_ref, weights_ref, vector_in_ref,
    mix1_ref, mix2_ref, wide_ref, long_ref, up_ref, vector_ref,
):
    feature = wide_ref.shape[1]
    devices = vector_ref.shape[1]
    share = feature // devices
    me = me_ref[0]
    if vector_in_ref.shape == vector_ref.shape:
        vector_ref[...] = vector_in_ref[...]
    else:
        rows = weights_ref[:, 4 * share :, :].astype(F32)
        for d in range(devices):
            for k in range(vector_ref.shape[0]):
                vector_ref[k, d : d + 1, :] = rows[d, k : k + 1, :]
    build_mix(me, weight_bits, weights_ref, 0, mix1_ref, feature)
    build_mix(me, weight_bits, weights_ref, 1, mix2_ref, feature)
    wide_ref[...] = jnp.zeros_like(wide_ref)
    long_ref[...] = jnp.zeros_like(long_ref)
    for row, at in enumerate((2, 3, 4, 5, 7)):
        wide_ref[row : row + 1, :] = spread(vector_ref[at], share, me, vector_bits)
    for row in range(2):
        both = spread(vector_ref[row], 2 * share, me, vector_bits)
        long_ref[row : row + 1, :] = to_mixed(both[:, :feature], both[:, feature:])
    up_ref[...] = spread(vector_ref[6], up_ref.shape[1] // devices, me, vector_bits)


def prepare(me, weights, vectors, feature, hidden, weight_bits, vector_bits):
    shapes = (
        jax.ShapeDtypeStruct((2, feature, feature), BF),
        jax.ShapeDtypeStruct((2, feature, feature), BF),
        jax.ShapeDtypeStruct((8, feature), F32),
        jax.ShapeDtypeStruct((8, 2 * feature), F32),
        jax.ShapeDtypeStruct((1, hidden), F32),
    )
    devices = vectors.shape[1] if vectors.shape[1] > 1 else weights.shape[0]
    return pl.pallas_call(
        functools.partial(prepare_kernel, weight_bits, vector_bits),
        out_shape=shapes,
        in_specs=[smem()] + vmem(2),
        out_specs=vmem(len(shapes)),
        scratch_shapes=[pltpu.VMEM((8, devices, LANES), F32)],
        compiler_params=params(),
        cost_estimate=cost(0, 0),
        name="prepare",
    )(me, weights, vectors)


def mix_first_kernel(
    half_ref, mix1_ref, mix2_ref, wide_ref, long_ref, head_ref, body_ref, back_head_ref, back_body_ref,
    out_ref, *rest,
):
    work = functools.partial(
        mix_step, half_ref, head_ref, body_ref, back_head_ref, back_body_ref, mix1_ref, mix2_ref, wide_ref, long_ref,
        rest[:5], rest[5:], out_ref,
    )

    @pl.when(pl.program_id(0) == 0)
    def _():
        work(True)

    @pl.when(pl.program_id(0) > 0)
    def _():
        work(False)


def mix_second_kernel(
    half_ref, mix1_ref, mix2_ref, wide_ref, long_ref, body_ref, back_body_ref,
    out_ref, *outs,
):
    mix_step(
        half_ref, None, body_ref, None, back_body_ref, mix1_ref, mix2_ref, wide_ref, long_ref,
        outs, (None,) * 5, out_ref, False,
    )


def mode_shapes(rows, feature):
    wide = [jax.ShapeDtypeStruct((rows, 2 * feature), kind) for kind in (BF, BF, F32, F32)]
    return wide + [jax.ShapeDtypeStruct((rows, 2 * LANES), F32)]


def mode_blocks(feature):
    return [pl.BlockSpec((TOOK, width), lambda i: (i, 0)) for width in (2 * feature,) * 4 + (2 * LANES,)]


def half_block(width, begin=0):
    return pl.BlockSpec((TAKE * GROUP, 2 * ROWS, width), lambda i: (i + begin, 0, 0))


def mix_first(half, mix1, mix2, wide, long, tables, steps, deps=()):
    feature = half.shape[2] - LANES
    fixed = (mix1, mix2, wide, long, tables["head"], tables["body"], tables["head_wt"], tables["body_wt"])
    heads = mode_shapes(ROWS, feature)
    return launch(
        deps,
        mix_first_kernel,
        grid=(steps,),
        out_shape=[jax.ShapeDtypeStruct((TAKE * GROUP * steps, 2 * ROWS, feature), F32)]
        + mode_shapes(TOOK * steps, feature) + heads,
        in_specs=[half_block(feature + LANES)] + [single(v.shape) for v in fixed],
        out_specs=[half_block(feature)] + mode_blocks(feature) + [single(v.shape) for v in heads],
        compiler_params=params(),
        cost_estimate=cost(9e9, 20e6),
        name="mix_first",
    )(half, *fixed)


def mix_second(half, mix1, mix2, wide, long, tables, begin, steps, deps=()):
    feature = half.shape[2] - LANES
    fixed = (mix1, mix2, wide, long, tables["body"], tables["body_wt"])
    return launch(
        deps,
        mix_second_kernel,
        grid=(steps,),
        out_shape=[jax.ShapeDtypeStruct((TAKE * GROUP * steps, 2 * ROWS, feature), F32)] + mode_shapes(TOOK * steps, feature),
        in_specs=[half_block(feature + LANES, begin)] + [single(v.shape) for v in fixed],
        out_specs=[half_block(feature)] + mode_blocks(feature),
        compiler_params=params(),
        cost_estimate=cost(9e9, 20e6),
        name="mix_second",
    )(half, *fixed)


def space_kernel(rows_ref, cols_ref, half1_ref, half2_ref, tokens_ref, first_t_ref, wide_ref, middle_ref, normed_ref, mark_ref):
    mark_ref[...] = jnp.zeros_like(mark_ref)
    feature = tokens_ref.shape[1]
    start = pl.program_id(0) * tokens_ref.shape[0]
    for k in range(tokens_ref.shape[0] // CELLS):
        here = slice(k * CELLS, (k + 1) * CELLS)
        flat = lambda ref: ref[:, k * 2 * GROUP : (k + 1) * 2 * GROUP, :].reshape(-1, feature)
        spatial = turn(first_t_ref, jnp.concatenate([flat(half1_ref), flat(half2_ref)], axis=0))
        inputs = tokens_ref[here, :].astype(F32)
        live = live_rows(start + k * CELLS, CELLS, rows_ref, cols_ref)
        normal, _ = normalize(inputs)
        middle = inputs + live * (spatial + (normal * wide_ref[0:1, :] + wide_ref[1:2, :]))
        middle_ref[here, :] = middle
        normal, _ = normalize(middle)
        normed_ref[here, :] = (normal * wide_ref[2:3, :] + wide_ref[3:4, :]).astype(BF)


def column_block(rows, width, tiles=1):
    return pl.BlockSpec((rows, 2 * GROUP * tiles, width), lambda i: (0, i, 0))


def space(rows, cols, half1, half2, tokens, wide, tables, deps=(), tiles=1):
    cells, feature = tokens.shape
    table = tables["first_t"]
    block = pl.BlockSpec((tiles * CELLS, feature), lambda i: (i, 0))
    return launch(
        deps,
        space_kernel,
        grid=(STEPS // tiles,),
        out_shape=(jax.ShapeDtypeStruct((cells, feature), F32), jax.ShapeDtypeStruct((cells, feature), BF), MARK),
        in_specs=[smem(), smem(), column_block(half1.shape[0], feature, tiles), column_block(half2.shape[0], feature, tiles),
                  block, single(table.shape), single(wide.shape)],
        out_specs=(block, block, single(MARK.shape)),
        compiler_params=params(),
        cost_estimate=cost(6e9, 20e6),
        name="space",
    )(rows, cols, half1, half2, tokens, table, wide)


def fetch_weights(me_ref, pieces, places, up_ref, down_ref, sems):
    each = pieces[0].shape[0]
    held = len(pieces) // 2
    count = each * held
    chip = me_ref[0] // 2

    def copies(own, core):
        target = (up_ref, down_ref)[core]
        source = pieces[:held] if own else pieces[held:]
        for mask in range(count):
            at = places[core][mask]
            part = source[at // each].at[at % each]
            yield pltpu.make_async_copy(part, target.at[chip ^ mask], sems.at[core, mask])

    for core in range(2):
        @pl.when(me_ref[0] % 2 == core)
        def _():
            for copy in copies(True, core):
                copy.start()
            for copy in copies(False, 1 - core):
                copy.start()

    def arrived(core):
        for copy in copies(True, core):
            copy.wait()

    return arrived


def weight_scratch(pieces):
    chips, rows, feature = UNITS, pieces[0].shape[1], pieces[0].shape[2]
    return [
        pltpu.VMEM((chips, rows, feature), BF),
        pltpu.VMEM((chips, rows, feature), BF),
        pltpu.SemaphoreType.DMA((2, chips)),
    ]


def up_part(up_ref, j, feature):
    share = up_ref.shape[1] * feature // (up_ref.shape[0] * up_ref.shape[1])
    return up_ref[:, j * share : (j + 1) * share, :].reshape(feature, feature)


def down_part(down_ref, j, feature):
    share = down_ref.shape[1]
    each = feature // share
    return down_ref[j * each : (j + 1) * each].reshape(feature, feature)


def feed_kernel(places, rows_ref, cols_ref, me_ref, normed_in_ref, grad_ref, bias_ref, *rest):
    pieces = rest[:-17]
    (
        active_all_ref, pre_all_ref, bias_grad_ref, up_all_ref, down_all_ref, send_ref, keep_ref,
        active_ref, pre_ref, normed_ref, branch_ref, up_ref, down_ref, sems, weight_sems, row_sems, grad_sems,
    ) = rest[-17:]
    tile, feature = normed_in_ref.shape
    cells, hidden = active_ref.shape
    tiles = cells // tile
    parts = hidden // feature
    chips, share, _ = up_ref.shape
    each = chips // parts
    small = share // parts
    step = pl.program_id(0)
    mine = pl.ds(pl.multiple_of(jnp.minimum(step, tiles - 1) * tile, tile), tile)
    copies = [
        pltpu.make_async_copy(source, target, weight_sems.at[k])
        for k, (source, target) in enumerate(((up_ref, up_all_ref), (down_ref, down_all_ref)))
    ]

    def row_copies(k):
        here = pl.ds(k * tile, tile)
        return (
            pltpu.make_async_copy(active_ref.at[here], active_all_ref.at[here], row_sems.at[0, k]),
            pltpu.make_async_copy(pre_ref.at[here], pre_all_ref.at[here], row_sems.at[1, k]),
        )

    def work(arrived):
        live = live_rows(step * tile, tile, rows_ref, cols_ref)
        branch = (grad_ref[...].astype(F32) * live).astype(BF)
        branch_ref[mine, :] = branch
        normed = normed_in_ref[...]
        normed_ref[mine, :] = normed
        if arrived:
            arrived(0)
            copies[0].start()
        for j in range(parts):
            place = slice(j * feature, (j + 1) * feature)
            value = mm(normed, up_part(up_ref, j, feature)) + bias_ref[:, place]
            if arrived and j == 0:
                arrived(1)
                copies[1].start()
            grad = mm(branch, down_part(down_ref, j, feature), (1, 1))
            active, slope = gelu_parts(value)
            active_ref[mine, place] = active.astype(BF)
            grad = grad * slope
            pre_ref[mine, place] = grad.astype(BF)
            bias_grad_ref[:, place] += jnp.sum(grad, axis=0, keepdims=True)

    @pl.when(step == 0)
    def _():
        bias_grad_ref[...] = jnp.zeros_like(bias_grad_ref)
        work(fetch_weights(me_ref, pieces, places, up_ref, down_ref, sems))

    @pl.when((step > 0) & (step < tiles))
    def _():
        work(None)

    for k in range(tiles):
        @pl.when(step == k)
        def _():
            for copy in row_copies(k):
                copy.start()

    def down_copies(j, target):
        for k in range(each):
            yield pltpu.make_async_copy(up_ref.at[j * each + k], target.at[places[1][j * each + k]], grad_sems.at[j, k])

    def up_copies(j, target):
        for k in range(chips):
            source = down_ref.at[j * each + k // each, pl.ds(k % each * small, small)]
            there = target.at[places[0][k], pl.ds(j * small, small)]
            yield pltpu.make_async_copy(source, there, grad_sems.at[parts + j, k])

    @pl.when(step == tiles)
    def _():
        for copy in copies:
            copy.wait()

    @pl.when((step >= tiles) & (step < tiles + parts))
    def _():
        j = step - tiles
        lanes = pl.ds(pl.multiple_of(j * feature, LANES), feature)
        piece = mm(active_ref[:, lanes], branch_ref[...], (0, 0)).astype(BF)
        up_ref[pl.ds(j * each, each)] = piece.reshape(each, share, feature)

    @pl.when(step >= tiles + parts)
    def _():
        j = step - tiles - parts
        lanes = pl.ds(pl.multiple_of(j * feature, LANES), feature)
        piece = mm(normed_ref[...], pre_ref[:, lanes], (0, 0)).astype(BF)
        down_ref[pl.ds(j * each, each)] = piece.reshape(each, share, feature)

    for j in range(parts):
        for core in range(2):
            targets = (send_ref, keep_ref) if core == 0 else (keep_ref, send_ref)

            @pl.when((step == tiles + j) & (me_ref[0] % 2 == core))
            def _():
                for copy in down_copies(j, targets[0]):
                    copy.start()

            @pl.when((step == tiles + parts + j) & (me_ref[0] % 2 == core))
            def _():
                for copy in up_copies(j, targets[1]):
                    copy.start()

    @pl.when(step == tiles + 2 * parts - 1)
    def _():
        for k in range(tiles):
            for copy in row_copies(k):
                copy.wait()
        for j in range(parts):
            for copy in down_copies(j, send_ref):
                copy.wait()
            for copy in up_copies(j, send_ref):
                copy.wait()


def feed(rows, cols, me, normed, grad, bias, pieces, places, tile=256, deps=()):
    cells, feature = normed.shape
    hidden = bias.shape[1]
    tiles, parts = cells // tile, hidden // feature
    block = pl.BlockSpec((tile, feature), lambda i: (jnp.minimum(i, tiles - 1), 0))
    weights = jax.ShapeDtypeStruct((UNITS,) + pieces[0].shape[1:], BF)
    rows_shape = jax.ShapeDtypeStruct((cells, hidden), BF)
    return launch(
        deps,
        functools.partial(feed_kernel, places),
        grid=(tiles + 2 * parts,),
        out_shape=(rows_shape, rows_shape, jax.ShapeDtypeStruct((1, hidden), F32)) + (weights,) * 4,
        in_specs=[smem(), smem(), smem(), block, block, single(bias.shape)] + [any_space() for _ in pieces],
        out_specs=(any_space(), any_space(), single((1, hidden))) + (any_space(),) * 4,
        scratch_shapes=[
            pltpu.VMEM((cells, hidden), BF),
            pltpu.VMEM((cells, hidden), BF),
            pltpu.VMEM((cells, feature), BF),
            pltpu.VMEM((cells, feature), BF),
            *weight_scratch(pieces),
            pltpu.SemaphoreType.DMA((2,)),
            pltpu.SemaphoreType.DMA((2, tiles)),
            pltpu.SemaphoreType.DMA((2 * parts, UNITS)),
        ],
        compiler_params=params(),
        cost_estimate=cost(0, 0),
        name="feed",
    )(rows, cols, me, normed, grad, bias, *pieces)


def down_kernel(rows_ref, cols_ref, active_ref, pre_ref, middle_ref, grad_ref, normal_ref, wide_ref, first_ref,
                up_ref, down_ref, mixed_ref, grad_middle_ref, half_ref, sums_ref):
    tile, feature = middle_ref.shape
    hidden = active_ref.shape[1]
    step = pl.program_id(0)

    @pl.when(step == 0)
    def _():
        sums_ref[...] = jnp.zeros_like(sums_ref)

    live = live_rows(step * tile, tile, rows_ref, cols_ref)
    branch = mm(active_ref[...], down_ref[...].reshape(hidden, feature))
    grad_normed = jnp.zeros((tile, feature), F32)
    for j in range(hidden // feature):
        pre = pre_ref[:, j * feature : (j + 1) * feature]
        grad_normed = grad_normed + mm(pre, up_part(up_ref, j, feature), (1, 1))
    middle = middle_ref[...]
    mixed_ref[...] = (middle + live * (branch + wide_ref[4:5, :])).astype(BF)
    normal, inverse = normalize(middle)
    cotangent = grad_ref[...].astype(F32)
    grad_middle = cotangent + norm_back(grad_normed, wide_ref[2:3, :], normal, inverse)
    grad_middle_ref[...] = grad_middle
    masked = grad_middle * live
    half_ref[...] = turn(first_ref, masked).reshape(half_ref.shape)
    rows = (grad_normed * normal, grad_normed, cotangent * live, masked * normal_ref[...].astype(F32), masked)
    for row, value in enumerate(rows):
        sums_ref[row : row + 1, :] += jnp.sum(value, axis=0, keepdims=True)


def feed_down(rows, cols, active, pre, middle, grad, normal, wide, table, up, down, deps=()):
    cells, feature = middle.shape
    hidden = active.shape[1]
    block = lambda width: pl.BlockSpec((CELLS, width), lambda i: (i, 0))
    operands = (rows, cols, active, pre, middle, grad, normal, wide, table, up, down)
    return launch(
        deps,
        down_kernel,
        grid=(cells // CELLS,),
        out_shape=(
            jax.ShapeDtypeStruct((cells, feature), BF),
            jax.ShapeDtypeStruct((cells, feature), F32),
            jax.ShapeDtypeStruct((KEPT, 2 * ROWS, feature), F32),
            jax.ShapeDtypeStruct((8, feature), F32),
        ),
        in_specs=[smem(), smem(), block(hidden), block(hidden), block(feature), block(feature), block(feature)]
        + [single(v.shape) for v in operands[7:]],
        out_specs=(block(feature), block(feature), column_block(KEPT, feature), single((8, feature))),
        compiler_params=params(),
        cost_estimate=cost(0, 0),
        name="feed_down",
    )(*operands)


def back_step(half_ref, head_ref, body_ref, back_head_ref, back_body_ref, mix1_ref, mix2_ref, ins, in_heads,
              outs, out_heads, out_ref, sums_ref, is_head):
    feature = out_ref.shape[2]

    def read(k):
        if is_head:
            return jnp.concatenate([ins[k][...], in_heads[k][...]], axis=0)
        return ins[k][...]

    grads = to_modes(half_ref, head_ref, body_ref, is_head)
    grad_two = (to_mixed(*grads) * read(1)).astype(BF)
    grad_one = (mix_product(grad_two, mix2_ref, True) * read(0)).astype(BF)
    grad_spec = mix_product(grad_one, mix1_ref, True)
    from_modes(from_mixed(grad_spec), back_head_ref, back_body_ref, is_head, out_ref)
    for row, value in enumerate((grad_one, grad_two)):
        outs[row][...] = value[:TOOK]
        if is_head:
            out_heads[row][...] = value[TOOK:]
    flat = jnp.concatenate([read(3)] * (feature // LANES), axis=1)
    for row, value in enumerate((grad_one.astype(F32), grad_two.astype(F32), grad_spec * read(2).astype(F32), grad_spec * flat)):
        total = jnp.sum(value, axis=0, keepdims=True)
        sums_ref[row : row + 1, :] = total if is_head else sums_ref[row : row + 1, :] + total


def mix_back_kernel(
    half_ref, slope1_ref, slope2_ref, bend1_ref, bend2_ref, low1_ref, low2_ref, flat1_ref, flat2_ref,
    slope_head_ref, bend_head_ref, low_head_ref, flat_head_ref, mix1_ref, mix2_ref,
    head_ref, body_ref, back_head_ref, back_body_ref,
    out_ref, one_ref, two_ref, one_head_ref, two_head_ref, sums_ref,
):
    step = pl.program_id(0)
    steps = pl.num_programs(0) // 2
    work = functools.partial(
        back_step, half_ref, head_ref, body_ref, back_head_ref, back_body_ref, mix1_ref, mix2_ref
    )
    heads = (slope_head_ref, bend_head_ref, low_head_ref, flat_head_ref)
    more = (heads, (one_ref, two_ref), (one_head_ref, two_head_ref), out_ref, sums_ref)
    near = (slope1_ref, bend1_ref, low1_ref, flat1_ref)
    far = (slope2_ref, bend2_ref, low2_ref, flat2_ref)

    @pl.when(step == 0)
    def _():
        sums_ref[...] = jnp.zeros_like(sums_ref)
        work(near, *more, True)

    @pl.when((step > 0) & (step < steps))
    def _():
        work(near, *more, False)

    @pl.when(step >= steps)
    def _():
        work(far, *more, False)


def mix_back(half, modes1, modes2, heads, mix1, mix2, tables, deps=()):
    feature = half.shape[2]
    steps = KEPT // GROUP // TAKE
    fixed = tuple(heads[k] for k in (2, 3, 0, 4)) + (
        mix1, mix2, tables["head_w"], tables["body_w"], tables["head_t"], tables["body_t"]
    )
    moving = []
    specs = []
    for k in (2, 3, 0, 4):
        width = modes1[k].shape[1]
        moving += [modes1[k], modes2[k]]
        specs += [
            pl.BlockSpec((TOOK, width), lambda i: (jnp.minimum(i, steps // 2 - 1), 0)),
            pl.BlockSpec((TOOK, width), lambda i: (jnp.maximum(i - steps // 2, 0), 0)),
        ]
    low = lambda rows: jax.ShapeDtypeStruct((rows, 2 * feature), BF)
    body = pl.BlockSpec((TOOK, 2 * feature), lambda i: (i, 0))
    shapes = (
        jax.ShapeDtypeStruct((KEPT, 2 * ROWS, feature), F32), low(TOOK * steps), low(TOOK * steps),
        low(ROWS), low(ROWS), jax.ShapeDtypeStruct((8, 2 * feature), F32),
    )
    return launch(
        deps,
        mix_back_kernel,
        grid=(steps,),
        out_shape=shapes,
        in_specs=[half_block(feature)] + specs + [single(v.shape) for v in fixed],
        out_specs=[half_block(feature), body, body] + [single(v.shape) for v in shapes[3:]],
        compiler_params=params(),
        cost_estimate=cost(18e9, 30e6),
        name="mix_back",
    )(half, *moving, *fixed)


def block_kernel(left1_ref, left2_ref, left_head_ref, right_ref, right_head_ref, out_ref, natural_ref):
    wide = 2 * LANES
    count = left1_ref.shape[1] // wide
    cut = left1_ref.shape[0]
    for t in range(count):
        for c in range(max(t - 1, 0), min(t + 2, count)):
            left, right = slice(t * wide, (t + 1) * wide), slice(c * wide, (c + 1) * wide)
            total = (
                mm(left1_ref[:, left], right_ref[:cut, right], (0, 0))
                + mm(left2_ref[:, left], right_ref[cut:, right], (0, 0))
                + mm(left_head_ref[:, left], right_head_ref[:, right], (0, 0))
            )
            rows, lanes = slice(t * LANES, (t + 1) * LANES), slice(c * LANES, (c + 1) * LANES)
            natural_ref[0, rows, lanes] = total[:LANES, :LANES] + total[LANES:, LANES:]
            natural_ref[1, rows, lanes] = total[:LANES, LANES:] - total[LANES:, :LANES]
    per_group = BLOCKS // 2
    block = count * LANES // per_group
    for b in range(per_group):
        begin = b * block
        base = begin // LANES * LANES
        reach = min(base + wide, count * LANES) - base
        for part in range(2):
            piece = natural_ref[part, begin : begin + block, base : base + reach]
            if begin > base:
                piece = pltpu.roll(piece, reach - (begin - base), axis=1)
            out_ref[part, b * block : (b + 1) * block, :] = piece[:, :LANES]


def block_grads(left1, left2, left_head, right, right_head, name, deps=()):
    feature = left1.shape[1] // 2
    half = feature // 2
    block = lambda v: pl.BlockSpec((v.shape[0], feature), lambda i: (0, i))
    return launch(
        deps,
        block_kernel,
        grid=(2,),
        out_shape=jax.ShapeDtypeStruct((2, feature, LANES), F32),
        in_specs=[block(v) for v in (left1, left2, left_head, right, right_head)],
        out_specs=pl.BlockSpec((2, half, LANES), lambda i: (0, i, 0)),
        scratch_shapes=[pltpu.VMEM((2, half, half), F32)],
        compiler_params=params(),
        cost_estimate=cost(5e9, 7e6),
        name=name,
    )(left1, left2, left_head, right, right_head)


def last_kernel(begin, rows_ref, cols_ref, half_ref, tokens_ref, grad_ref, first_t_ref, wide_ref, *rest):
    out_ref, mark_ref = rest[-2:]
    mark_ref[...] = jnp.zeros_like(mark_ref)
    tile, feature = tokens_ref.shape
    live = live_rows((pl.program_id(0) + begin) * tile, tile, rows_ref, cols_ref)
    grad_middle = grad_ref[...]
    grad_normed = live * (grad_middle + turn(first_t_ref, half_ref[...].reshape(CELLS, feature)))
    normal, inverse = normalize(tokens_ref[...].astype(F32))
    out_ref[...] = grad_middle + norm_back(grad_normed, wide_ref[0:1, :], normal, inverse)


def last(rows, cols, half, tokens, grad, wide, tables, begin, steps, before=(), deps=()):
    cells, feature = tokens.shape
    first_t = tables["first_t"]
    block = pl.BlockSpec((CELLS, feature), lambda i: (i + begin, 0))
    operands = (rows, cols, half, tokens, grad, first_t, wide)
    return launch(
        deps,
        functools.partial(last_kernel, begin),
        grid=(steps,),
        out_shape=(jax.ShapeDtypeStruct((cells, feature), F32), MARK),
        in_specs=[smem(), smem(), pl.BlockSpec((KEPT, 2 * GROUP, feature), lambda i: (0, i + begin, 0)), block, block,
                  single(first_t.shape), single(wide.shape)] + [any_space() for _ in before],
        out_specs=(block, single(MARK.shape)),
        input_output_aliases={len(operands): 0} if before else {},
        compiler_params=params(),
        cost_estimate=cost(6e9, 20e6),
        name="last",
    )(*operands, *before)


def collect(value, per_device, devices):
    total = value.shape[1]
    owner = lax.broadcasted_iota(jnp.int32, (devices, total), 1) // per_device
    row = lax.broadcasted_iota(jnp.int32, (devices, total), 0)
    high, low = split(jnp.where(owner == row, jnp.broadcast_to(value, (devices, total)), 0.0))
    place = lax.broadcasted_iota(jnp.int32, (total, LANES), 0)
    lane = lax.broadcasted_iota(jnp.int32, (total, LANES), 1)
    pick = jnp.where(place % per_device == lane, 1.0, 0.0).astype(BF)
    return mm(high, pick) + mm(low, pick)


def emit(place, sum_ref, send_refs, keep_ref):
    half, _, rows, _ = sum_ref.shape
    rows = rows - 8
    for k, send_ref in enumerate(send_refs):
        away = sum_ref[:, pl.ds(place ^ (k + 1), 1)].reshape(half, rows + 8, LANES)
        high, low = split(away[:, rows:])
        send_ref[:, :rows] = away[:, :rows].astype(BF)
        send_ref[:, rows:] = jnp.concatenate([high.astype(F32), low.astype(F32)], axis=1).astype(BF)
    keep_ref[...] = sum_ref[:, pl.ds(place, 1)].reshape(half, rows + 8, LANES)


def pack_kernel(place_ref, one_ref, two_ref, mixed_ref, sums_ref, up_ref, wide_ref, send_ref, keep_ref, sum_ref):
    half, _, rows, _ = sum_ref.shape
    devices = 2 * half
    share = (rows - 8) // 4
    feature = sums_ref.shape[1]
    sum_ref[:, :, : 2 * share] = one_ref[...].reshape(half, 2, 2 * share, LANES)
    sum_ref[:, :, 2 * share : 4 * share] = two_ref[...].reshape(half, 2, 2 * share, LANES)
    first_gain, first_bias = scale_grads(mixed_ref, sums_ref, wide_ref)
    natural = [jnp.concatenate(from_mixed(mixed_ref[k : k + 1, :]), axis=1) for k in range(2)]
    narrow = [first_gain, first_bias] + [sums_ref[k : k + 1, :] for k in range(3)]
    for k, value in enumerate(narrow + natural + [up_ref[...]]):
        placed = collect(value, value.shape[1] // devices, devices)
        for d in range(devices):
            sum_ref[d // 2, d % 2, 4 * share + k : 4 * share + k + 1, :] = placed[d : d + 1, :]
    emit(place_ref[0], sum_ref, (send_ref,), keep_ref)


def scale_grads(mixed_ref, sums_ref, wide_ref):
    real, imag = from_mixed(mixed_ref[2:3, :])
    scaled = real + imag
    real, imag = from_mixed(mixed_ref[3:4, :])
    flat = real + imag
    gain = sums_ref[3:4, :] + (scaled - wide_ref[1:2, :] * flat) / wide_ref[0:1, :]
    return gain, sums_ref[4:5, :] + flat


def small_shapes(half, rows, others):
    shapes = [jax.ShapeDtypeStruct((half, rows + 8, LANES), BF)] * others
    return shapes + [jax.ShapeDtypeStruct((half, rows, LANES), F32)]


def pack(upper, one, two, mixed, sums, up, wide, devices):
    rows = 2 * one.shape[0] * one.shape[1] // devices + 8
    shapes = small_shapes(devices // 2, rows, 1)
    operands = (one, two, mixed, sums, up, wide)
    return pl.pallas_call(
        pack_kernel,
        out_shape=shapes,
        in_specs=[smem()] + vmem(len(operands)),
        out_specs=vmem(2),
        scratch_shapes=[pltpu.VMEM((devices // 2, 2, rows, LANES), F32)],
        compiler_params=params(),
        cost_estimate=cost(0, 0),
        name="pack",
    )(upper, *operands)


def merge_small(keep_ref, got_refs):
    rows = keep_ref.shape[1] - 8
    top, tail = keep_ref[:, :rows], keep_ref[:, rows:]
    for got_ref in got_refs:
        both = got_ref[:, rows:].astype(F32)
        top = top + got_ref[:, :rows].astype(F32)
        tail = tail + (both[:, :8] + both[:, 8:])
    return top, tail


def fold_small_kernel(others, place_ref, keep_ref, *rest):
    sum_ref = rest[-1]
    send_refs, out_ref = rest[-2 - others : -2], rest[-2]
    half, count, rows, _ = sum_ref.shape
    top, tail = merge_small(keep_ref, rest[: len(rest) - 2 - others])
    sum_ref[:, :, : rows - 8] = top.reshape(half, count, rows - 8, LANES)
    sum_ref[:, :, rows - 8 :] = tail.reshape(half, count, 8, LANES)
    emit(place_ref[0], sum_ref, send_refs, out_ref)


def fold_small(keep, got, place, count, deps=()):
    half, rows = keep.shape[0] // count, keep.shape[1]
    shapes = small_shapes(half, rows, count - 1)
    return launch(
        deps,
        functools.partial(fold_small_kernel, count - 1),
        out_shape=shapes,
        in_specs=[smem()] + vmem(1 + len(got)),
        out_specs=vmem(len(shapes)),
        scratch_shapes=[pltpu.VMEM((half, count, rows, LANES), F32)],
        compiler_params=params(SMALL_LIMIT),
        cost_estimate=cost(0, 0),
        name="fold_small",
    )(place, keep, *got)


def vmem(count):
    return [pl.BlockSpec(memory_space=pltpu.VMEM)] * count


def end_small_kernel(others, keep_ref, *rest):
    got_refs, (one_ref, two_ref, *rows_refs) = rest[:others], rest[others:]
    top, tail = merge_small(keep_ref, got_refs)
    share, block = one_ref.shape
    one_ref[...] = top[0, :share, :block]
    two_ref[...] = top[0, share:, :block]
    for row, ref in enumerate(rows_refs):
        ref[...] = tail[0, row : row + 1, : ref.shape[1]]


def end_small(keep, got, share, block, widths):
    shapes = [jax.ShapeDtypeStruct((share, block), F32)] * 2
    shapes += [jax.ShapeDtypeStruct((1, width), F32) for width in widths]
    return pl.pallas_call(
        functools.partial(end_small_kernel, len(got)),
        out_shape=shapes,
        in_specs=vmem(1 + len(got)),
        out_specs=vmem(len(shapes)),
        compiler_params=params(SMALL_LIMIT),
        cost_estimate=cost(0, 0),
        name="end_small",
    )(keep, *got)


def begin_small_kernel(one_ref, two_ref, *rest):
    out_ref, rows_ref = rest[-2:]
    share, block = one_ref.shape
    out_ref[...] = jnp.zeros_like(out_ref)
    rows_ref[...] = jnp.zeros_like(rows_ref)
    out_ref[0, :share, :block] = one_ref[...]
    out_ref[0, share : 2 * share, :block] = two_ref[...]
    for row, ref in enumerate(rest[:-2]):
        rows_ref[row : row + 1, : ref.shape[1]] = ref[...].astype(F32)
    out_ref[0, 2 * share :, :] = rows_ref[...].astype(BF)


def begin_small(one, two, vectors):
    share = one.shape[0]
    operands = (one, two) + tuple(v[None] for v in vectors)
    return pl.pallas_call(
        begin_small_kernel,
        out_shape=jax.ShapeDtypeStruct((1, 2 * share + 16, LANES), BF),
        in_specs=vmem(len(operands)),
        out_specs=vmem(1)[0],
        scratch_shapes=[pltpu.VMEM((16, LANES), F32)],
        compiler_params=params(),
        cost_estimate=cost(0, 0),
        name="begin_small",
    )(*operands)


AXES = ("dp", "fsdp")


def swap(value, devices, bits):
    return lax.ppermute(value, AXES, [(i, i ^ (1 << bits[i & 1])) for i in range(devices)])


def doubling_orders(count):
    first = list(range(count - 1, 0, -1))
    second = list(first)
    for k in range(0, len(second) - 1, 2):
        second[k], second[k + 1] = second[k + 1], second[k]
    return first, second


def places_of(order):
    return [
        sum(1 << k for k, bit in enumerate(order) if mask >> (bit - 1) & 1) for mask in range(1 << len(order))
    ]


def join_kernel(*refs):
    out_ref = refs[-1]
    count = refs[0].shape[0]
    for k, ref in enumerate(refs[:-1]):
        out_ref[k * count : (k + 1) * count] = ref[...]


def join_rows(*pieces, deps=()):
    shape = jax.ShapeDtypeStruct((len(pieces) * pieces[0].shape[0],) + pieces[0].shape[1:], pieces[0].dtype)
    return launch(
        deps,
        join_kernel,
        out_shape=shape,
        in_specs=[pl.BlockSpec(memory_space=pltpu.VMEM) for _ in pieces],
        out_specs=pl.BlockSpec(memory_space=pltpu.VMEM),
        compiler_params=params(SMALL_LIMIT),
        cost_estimate=cost(0, 0),
        name="join",
    )(*pieces)


def hold(value, deps):
    def body(*refs):
        pass

    return pl.pallas_call(
        body,
        out_shape=jax.ShapeDtypeStruct(value.shape, value.dtype),
        in_specs=[any_space() for _ in range(1 + len(deps))],
        out_specs=any_space(),
        input_output_aliases={0: 0},
        compiler_params=params(SMALL_LIMIT),
        cost_estimate=cost(0, 0),
        name="hold",
    )(value, *deps)


def gather_small(value, me, devices, count):
    held = value[None]
    for bit in list(range(3, count)) + [2, 1, 0]:
        other = swap(held, devices, (bit, bit))
        upper = (me >> bit) & 1
        axis = 0 if bit > 2 else 1
        join_two = lambda a, b: jnp.stack([a, b], axis=axis).reshape((-1,) + value.shape)
        held = jnp.where(upper == 0, join_two(held, other), join_two(other, held))
    return held


def scatter_small(value, me, devices, count, exact):
    shape = value.shape[1:]
    rows = shape[0]
    total = value
    for bit in [0, 1, 2] + list(range(count - 1, 2, -1)):
        upper = (me >> bit) & 1
        axis = 0 if bit > 2 else 1
        pair = total.reshape(((2, -1) if bit > 2 else (-1, 2)) + shape)
        away = lax.dynamic_index_in_dim(pair, 1 - upper, axis, keepdims=False)
        keep = lax.dynamic_index_in_dim(pair, upper, axis, keepdims=False)
        sums = away[:, rows - exact :]
        top = lax.reduce_precision(sums, 8, 7)
        packet = jnp.concatenate([away[:, : rows - exact], top, sums - top], axis=1).astype(BF)
        got = swap(packet, devices, (bit, bit)).astype(F32)
        low = got[:, rows - exact : rows] + got[:, rows:]
        total = keep + jnp.concatenate([got[:, : rows - exact], low], axis=1)
    return total[0]


def chip_unit(up, down, core, devices):
    parts, share, feature = up.shape
    flat = up.reshape(parts * share, feature)
    other = swap(jnp.where(core == 0, down, flat), devices, (0, 0))
    up_unit = jnp.concatenate([up, other.reshape(up.shape)], axis=1).reshape(2 * parts * share, feature)
    return jnp.where(core == 0, up_unit, jnp.concatenate([other, down]))[None]


def fold_kernel(upper_ref, keep_away_ref, got_away_ref, keep_own_ref, got_own_ref, send_ref, keep_ref):
    send_ref[...] = (keep_away_ref[...].astype(F32) + got_away_ref[...].astype(F32)).astype(BF)
    keep_ref[...] = (keep_own_ref[...].astype(F32) + got_own_ref[...].astype(F32)).astype(BF)


def fold(keep, got, upper, deps=()):
    half = keep.shape[0] // 2
    each = min(2, half)
    unit = (each,) + keep.shape[1:]
    count = len(deps)
    away = pl.BlockSpec(unit, lambda i, up: ((1 - up[0]) * (half // each) + i, 0, 0))
    own = pl.BlockSpec(unit, lambda i, up: (up[0] * (half // each) + i, 0, 0))
    out = pl.BlockSpec(unit, lambda i, up: (i, 0, 0))
    shape = jax.ShapeDtypeStruct((half,) + keep.shape[1:], BF)

    def body(*refs):
        fold_kernel(*refs[:5], *refs[5 + count :])

    return pl.pallas_call(
        body,
        grid_spec=pltpu.PrefetchScalarGridSpec(
            num_scalar_prefetch=1,
            grid=(half // each,),
            in_specs=[away, away, own, own] + [any_space() for _ in deps],
            out_specs=[out, out],
        ),
        out_shape=(shape, shape),
        compiler_params=params(VMEM_LIMIT if half >= 8 else SMALL_LIMIT),
        cost_estimate=cost(0, 6 * half * keep[0].size),
        name="fold",
    )(upper, keep, got, keep, got, *deps)


def on_device(
    tokens, grad_out, region_rows, region_cols, ln1_gain, ln1_bias, spec_w1, spec_b1, spec_w2, spec_b2,
    ln2_gain, ln2_bias, w_up, up_bias, w_down, down_bias,
):
    devices = lax.axis_size(AXES[0]) * lax.axis_size(AXES[1])
    count = devices.bit_length() - 1
    me = lax.axis_index(AXES).astype(jnp.int32)
    core = me & 1
    me_one = me.reshape(1)
    feature = tokens.shape[-1]
    block = feature // BLOCKS
    share = ln1_gain.shape[0]
    cells = tokens.shape[1] * tokens.shape[2]
    hidden = w_up.shape[1]
    parts = hidden // feature
    tables = {name: jnp.asarray(value) for name, value in wave_matrices().items()}
    orders = doubling_orders(count)
    places = tuple(places_of(order) for order in orders)
    flat_tokens = tokens.reshape(cells, feature)
    flat_grad = grad_out.reshape(cells, feature)
    fast = devices // 2 == UNITS
    step = lambda value, k: swap(value, devices, (orders[0][k], orders[1][k]))

    padded = lambda v: jnp.pad(v, ((0, 0), (0, LANES - v.shape[1])))
    vectors = (spec_b1, spec_b2, ln1_gain, ln1_bias, ln2_gain, ln2_bias, up_bias, down_bias)
    if fast:
        own_up = w_up.reshape(share, parts, feature).transpose(1, 0, 2)
        unit = chip_unit(own_up, w_down, core, devices)
        bits = (3, 4, 2, 1, 0)
        hop = lambda value, mask: lax.ppermute(value, AXES, [(i, i ^ mask) for i in range(devices)])
        meet = lambda value, bit: hop(value, 1 << bit)
        small = begin_small(spec_w1, spec_w2, vectors)
        made = first(region_rows, region_cols, flat_tokens, tables, 0, 2, deps=(unit, small), tiles=2)
        small = join_rows(small, *(hop(small, mask) for mask in (8, 16, 24)), deps=(made[2],))
        near = join_rows(unit, step(unit, 0), deps=(small,))
        half, normal, mark = first(region_rows, region_cols, flat_tokens, tables, 2, 2, made[:2], deps=(near,), tiles=2)
        small = join_rows(small, *(hop(small, mask) for mask in (4, 2, 6)), deps=(mark,))
        small = join_rows(small, meet(small, 0))
        weights, weight_bits, vector_bits, me_small = small, bits, bits, me_one
        vectors = jnp.zeros((8, 1, LANES), F32)
    else:
        up = lax.all_gather(w_up, AXES, axis=0, tiled=True)
        up = up.reshape(UNITS, feature // UNITS, parts, feature).transpose(0, 2, 1, 3).reshape(UNITS, -1, feature)
        down = lax.all_gather(w_down, AXES, axis=0, tiled=True).reshape(UNITS, -1, feature)
        pieces = tuple(
            jnp.where(core == 0, one, two)[begin : begin + UNITS // 2]
            for one, two in ((up, down), (down, up))
            for begin in (0, UNITS // 2)
        )
        me_one = core.reshape(1)
        me_small = jnp.zeros_like(me_one)
        places = (tuple(range(UNITS)),) * 2
        small = jnp.concatenate([padded(spec_w1), padded(spec_w2)] + [padded(v[None]) for v in vectors])
        small = gather_small(small, me, devices, count)
        weights = small[:, : 4 * share].reshape(devices, 2, 2 * share, LANES).transpose(1, 0, 2, 3)
        weights = weights.reshape(2, 2 * UNITS, -1, LANES).transpose(1, 0, 2, 3).reshape(2 * UNITS, -1, LANES)
        weight_bits, vector_bits = tuple(range(5)), tuple(range(count))
        half, normal, _ = first(region_rows, region_cols, flat_tokens, tables, 0, STEPS)
        vectors = small[:, 4 * share :].transpose(1, 0, 2).astype(F32)

    steps = KEPT // GROUP // TAKE
    core_swap = lambda value: swap(value, devices, (0, 0))
    mix1, mix2, wide, long, up_shift = prepare(
        me_small, weights, vectors, feature, hidden, weight_bits, vector_bits
    )
    deps = ()
    if fast:
        near = join_rows(near, step(near, 1), deps=(up_shift,))
        deps = (near,)
    made = mix_first(half, mix1, mix2, wide, long, tables, steps // 2, deps=deps)
    half1, modes1, heads = made[0], made[1:6], made[6:11]
    deps = ()
    if fast:
        beside, across = step(near, 2), step(near, 3)
        other_near = core_swap(near)
        deps = (other_near, heads[4])
    made = mix_second(half, mix1, mix2, wide, long, tables, steps // 2, steps // 2, deps=deps)
    half2, modes2 = made[0], made[1:6]
    if fast:
        beside = hold(beside, (modes2[4],))
        far = step(beside, 3)
        deps = (beside,)
    middle, normed, mark = space(
        region_rows, region_cols, half1, half2, flat_tokens, wide, tables, deps=deps, tiles=2
    )
    if fast:
        far = hold(far, (mark,))
        pieces = (near, beside, across, far, other_near) + tuple(core_swap(v) for v in (beside, across, far))
    active, pre, bias_grad, up_all, down_all, send, keep = feed(
        region_rows, region_cols, me_one, normed, flat_grad, up_shift, pieces, places
    )
    tiles = cells // CELLS
    mixed, grad_middle, half_back, sums_two = feed_down(
        region_rows, region_cols, active, pre, middle, flat_grad, normal, wide, tables["first"], up_all, down_all,
        deps=(send,),
    )
    deps = ()
    if fast:
        ranks = [((me >> jnp.where(core == 0, *bit)) & 1).reshape(1) for bit in zip(*orders)]
        send, keep = fold(keep, swap(send, devices, (0, 0)), ranks[3], deps=(sums_two,))
        deps = (send,)
    half_back, one, two, one_head, two_head, bias_sums = mix_back(
        half_back, modes1, modes2, heads, mix1, mix2, tables, deps=deps
    )
    grad_one = block_grads(modes1[0], modes2[0], heads[0], one, one_head, "grad_mix1")
    if fast:
        send, keep = fold(keep, step(send, 3), ranks[2], deps=(grad_one,))
        deps = (send,)
    grad_two = block_grads(modes1[1], modes2[1], heads[1], two, two_head, "grad_mix2", deps=deps)
    last_args = (region_rows, region_cols, half_back, flat_tokens, grad_middle, wide, tables)
    if fast:
        places_small = [v.reshape(1) for v in (me & 1, (me >> 1) & 3, me >> 3)]
        away, own = pack(places_small[0], grad_one, grad_two, bias_sums, sums_two, bias_grad, wide, devices)
        grad_tokens, mark = last(*last_args, 0, 2, deps=(away,))
        *aways, own = fold_small(own, (hop(away, 1),), places_small[1], 4, deps=(mark,))
        send, keep = fold(keep, step(send, 2), ranks[1], deps=tuple(aways))
        gots = tuple(hop(v, mask) for v, mask in zip(aways, (2, 4, 6)))
        grad_tokens, mark = last(*last_args, 2, 2, (grad_tokens,), deps=(send,))
        *aways, own = fold_small(own, gots, places_small[2], 4, deps=(mark,))
        gots = tuple(hop(v, mask) for v, mask in zip(aways, (8, 16, 24)))
        grad_tokens, mark = last(*last_args, 4, 2, (grad_tokens,), deps=tuple(aways))
        send, keep = fold(keep, step(send, 1), ranks[0], deps=(mark, gots[0]))
        grad_tokens, mark = last(*last_args, 6, 2, (grad_tokens,), deps=(send,))
        widths = (share,) * 5 + (2 * share,) * 2 + (hidden // devices,)
        blocks = end_small(hold(own, (mark,)), gots, 2 * share, block, widths)
        keep = hold(keep, (blocks[0],))
        total = keep[0].astype(F32) + step(send, 0)[0].astype(F32)
        up_sum = total.reshape(parts, 2 * share, feature)
        lower = up_sum[:, :share].reshape(parts * share, feature)
        upper = up_sum[:, share:].reshape(parts * share, feature)
        each = parts * share
        leaving = jnp.where(core == 0, upper, total[:each])
        other = swap(leaving, devices, (0, 0))
        grad_w_up = jnp.where(core == 0, lower, other).reshape(parts, share, feature).transpose(1, 0, 2)
        grad_w_down = jnp.where(core == 0, other, total[each:])
        rows = [v.reshape(-1) for v in blocks[2:]]
        blocks = blocks[:2]
    else:
        scatter = lambda v: lax.psum_scatter(v.astype(F32), AXES, scatter_dimension=0, tiled=True)
        up = jnp.where(core == 0, keep, send).reshape(UNITS, parts, feature // UNITS, feature)
        grad_w_up = scatter(up.transpose(0, 2, 1, 3).reshape(feature, hidden))
        grad_w_down = scatter(jnp.where(core == 0, send, keep).reshape(hidden, feature))
        grad_tokens, _ = last(*last_args, 0, tiles)
        owned = lambda v: jnp.pad(
            v.reshape(v.shape[0], devices, -1).transpose(1, 0, 2), ((0, 0), (0, 0), (0, LANES - v.shape[1] // devices))
        )
        narrow = jnp.concatenate(list(scale_grads(bias_sums, sums_two, wide)) + [sums_two[:3]])
        biases = bias_sums[:2].reshape(2, feature // LANES, 2, LANES).transpose(0, 2, 1, 3).reshape(2, 2 * feature)
        blocks = [v.reshape(devices, 2 * share, LANES) for v in (grad_one, grad_two)]
        packet = jnp.concatenate(blocks + [owned(narrow), owned(biases), owned(bias_grad)], axis=1)
        result = scatter_small(packet, me, devices, count, 8)
        widths = (share,) * 5 + (2 * share,) * 2 + (hidden // devices,)
        rows = [result[4 * share + k, :width] for k, width in enumerate(widths)]
        blocks = [result[k * 2 * share : (k + 1) * 2 * share, :block] for k in range(2)]
    return (
        mixed.reshape(tokens.shape),
        grad_tokens.reshape(tokens.shape),
        rows[0],
        rows[1],
        blocks[0],
        rows[5],
        blocks[1],
        rows[6],
        rows[2],
        rows[3],
        grad_w_up.reshape(share, hidden),
        rows[7],
        grad_w_down,
        rows[4],
    )


def solution(mesh):
    placed = P(AXES)
    return jax.shard_map(
        on_device, mesh=mesh, in_specs=(placed,) * 16, out_specs=(placed,) * 14, check_vma=False
    )
```

```python
import functools
import math

import jax
import jax.numpy as jnp
import numpy as np
from jax import lax
from jax.experimental import pallas as pl
from jax.experimental.pallas import tpu as pltpu
from jax.sharding import PartitionSpec as P

BF = jnp.bfloat16
F32 = jnp.float32
BLOCKS = 8
EPS = 1e-05
SHRINK = 0.01
ROWS = 32
COLS = 64
KEPT = COLS // 2
GROUP = 4
STEPS = ROWS // GROUP
CELLS = GROUP * COLS
MODES = (KEPT + 1) * ROWS
HEAD = (GROUP + 1) * ROWS
BODY = GROUP * ROWS
TAKE = 2
TOOK = TAKE * BODY
LANES = 128
C1 = math.sqrt(2.0 / math.pi)
C3 = 0.044715
SIGMOID = -2.0 * C1 / math.log(2.0)
UNITS = 16
WIDTH = 256
VMEM_LIMIT = 60 * 1024 * 1024
SMALL_LIMIT = 36 * 1024 * 1024


def table_parts(values):
    high = values.astype(np.float32).astype(jnp.bfloat16)
    low = (values - high.astype(np.float64)).astype(np.float32).astype(jnp.bfloat16)
    return np.stack([high, low])


def wave_matrices():
    scale = 1.0 / math.sqrt(ROWS * COLS)
    w = np.arange(COLS)
    first = np.zeros((KEPT, 2, GROUP, GROUP, COLS))
    for k in range(KEPT):
        for h in range(GROUP):
            if k == 0:
                first[k, 0, h, h] = scale
                first[k, 1, h, h] = scale * np.where(w % 2 == 0, 1.0, -1.0)
            else:
                first[k, 0, h, h] = scale * np.cos(2 * np.pi * (k * w % COLS) / COLS)
                first[k, 1, h, h] = -scale * np.sin(2 * np.pi * (k * w % COLS) / COLS)
    first = first.reshape(CELLS, CELLS)
    p = np.arange(ROWS)
    turn = 2 * np.pi * (np.outer(p, p) % ROWS) / ROWS
    cos = np.cos(turn).reshape(ROWS, STEPS, GROUP)
    sin = np.sin(turn).reshape(ROWS, STEPS, GROUP)
    body = np.zeros((2, GROUP, ROWS, GROUP, STEPS, 2, GROUP))
    head = np.zeros((2, GROUP + 1, ROWS, GROUP, STEPS, 2, GROUP))
    for k in range(GROUP):
        body[0, k, :, k, :, 0] = cos
        body[0, k, :, k, :, 1] = sin
        body[1, k, :, k, :, 1] = cos
        body[1, k, :, k, :, 0] = -sin
    head[:, 1:GROUP, :, 1:] = body[:, 1:, :, 1:]
    for place, part in ((0, 0), (GROUP, 1)):
        head[0, place, :, 0, :, part] = cos
        head[1, place, :, 0, :, part] = -sin
    weight = np.full((2, GROUP + 1, ROWS, 1), 2.0)
    weight[:, 0] = 1.0
    weight[:, GROUP] = 1.0
    head = head.reshape(2 * HEAD, 2 * BODY)
    body = body.reshape(2 * BODY, 2 * BODY)
    head_weighted = head * weight.reshape(2 * HEAD, 1)
    body_weighted = body * 2.0
    return {
        "first": table_parts(first),
        "first_t": table_parts(first.T),
        "head": table_parts(head),
        "body": table_parts(body),
        "head_t": table_parts(head.T),
        "body_t": table_parts(body.T),
        "head_w": table_parts(head_weighted),
        "body_w": table_parts(body_weighted),
        "head_wt": table_parts(head_weighted.T),
        "body_wt": table_parts(body_weighted.T),
    }


def mm(left, right, dims=(1, 0)):
    return lax.dot_general(
        left, right, (((dims[0],), (dims[1],)), ((), ())), preferred_element_type=F32
    )


def split(values):
    high = values.astype(BF)
    return high, (values - high.astype(F32)).astype(BF)


def turn(table, values):
    high, low = split(values)
    return mm(table[0], high) + mm(table[1], high) + mm(table[0], low)


def turn_once(table, values):
    return mm(table[0], values.astype(BF))


def normalize(values):
    centred = values - jnp.mean(values, axis=-1, keepdims=True)
    inverse = lax.rsqrt(jnp.mean(centred * centred, axis=-1, keepdims=True) + EPS)
    return centred * inverse, inverse


def norm_back(grad, gain, normal, inverse):
    scaled = grad * gain
    return inverse * (
        scaled
        - jnp.mean(scaled, axis=-1, keepdims=True)
        - normal * jnp.mean(scaled * normal, axis=-1, keepdims=True)
    )


def gelu_parts(value):
    square = value * value
    half = 1.0 / (1.0 + jnp.exp2(value * (SIGMOID + (SIGMOID * C3) * square)))
    active = value * half
    slope = half + active * (1.0 - half) * (2.0 * C1 + (6.0 * C1 * C3) * square)
    return active, slope


def live_rows(start, count, rows_ref, cols_ref):
    cell = start + lax.broadcasted_iota(jnp.int32, (count, 1), 0)
    inside = (cell // COLS < rows_ref[0]) & (cell % COLS < cols_ref[0])
    return jnp.where(inside, 1.0, 0.0).astype(F32)


def spread(piece, per_device, me, bits):
    devices = piece.shape[0]
    total = devices * per_device
    lane = lax.broadcasted_iota(jnp.int32, (LANES, total), 0)
    place = lax.broadcasted_iota(jnp.int32, (LANES, total), 1)
    pick = jnp.where(place % per_device == lane, 1.0, 0.0).astype(BF)
    wide = mm(piece.astype(BF), pick)
    row = lax.broadcasted_iota(jnp.int32, (devices, 1), 0)
    owner = jnp.full((devices, 1), me, jnp.int32)
    for k, bit in enumerate(bits):
        owner = owner ^ (((row >> k) & 1) << bit)
    where = lax.broadcasted_iota(jnp.int32, (devices, total), 1) // per_device
    return jnp.sum(jnp.where(owner == where, wide, 0.0), axis=0, keepdims=True)


def place_of(mask, bits):
    return sum(((mask >> bit) & 1) << k for k, bit in enumerate(bits))


MARK = jax.ShapeDtypeStruct((8, LANES), F32)


def any_space():
    return pl.BlockSpec(memory_space=pl.ANY)


def single(shape):
    return pl.BlockSpec(shape, lambda *_: (0,) * len(shape), pipeline_mode=pl.Buffered(1))


def smem():
    return pl.BlockSpec(memory_space=pltpu.SMEM)


def params(limit=VMEM_LIMIT):
    return pltpu.CompilerParams(vmem_limit_bytes=limit)


def cost(flops, moved):
    return pl.CostEstimate(flops=0, bytes_accessed=0, transcendentals=0)


def unread(deps):
    return [pl.BlockSpec(memory_space=pltpu.HBM) if v.shape == MARK.shape else any_space() for v in deps]


def launch(deps, kernel, *, in_specs, **more):
    count = len(in_specs)

    def body(*refs):
        kernel(*refs[:count], *refs[count + len(deps) :])

    call = pl.pallas_call(body, in_specs=list(in_specs) + unread(deps), **more)
    return lambda *operands: call(*operands, *deps)


def to_mixed(real, imag):
    tiles = []
    for at in range(0, real.shape[1], LANES):
        tiles += [real[:, at : at + LANES], imag[:, at : at + LANES]]
    return jnp.concatenate(tiles, axis=1)


def from_mixed(values):
    cut = lambda at: values[:, at : at + LANES]
    real = [cut(at) for at in range(0, values.shape[1], 2 * LANES)]
    imag = [cut(at + LANES) for at in range(0, values.shape[1], 2 * LANES)]
    return jnp.concatenate(real, axis=1), jnp.concatenate(imag, axis=1)


def mix_product(values, matrix_ref, back=False):
    feature = values.shape[1] // 2
    wide = 2 * LANES
    groups = []
    for group in range(2):
        part = values[:, group * feature : (group + 1) * feature]
        count = feature // wide
        for t in range(count):
            begin, end = max(t - 1, 0) * wide, min(t + 2, count) * wide
            here = slice(t * wide, (t + 1) * wide)
            if back:
                groups.append(mm(part[:, begin:end], matrix_ref[group, here, begin:end], (1, 1)))
            else:
                groups.append(mm(part[:, begin:end], matrix_ref[group, begin:end, here]))
    return jnp.concatenate(groups, axis=1)


def first_kernel(begin, rows_ref, cols_ref, tokens_ref, first_ref, *rest):
    half_ref, normal_ref, mark_ref = rest[-3:]
    mark_ref[...] = jnp.zeros_like(mark_ref)
    feature = tokens_ref.shape[1]
    start = (pl.program_id(0) + begin) * tokens_ref.shape[0]
    for k in range(tokens_ref.shape[0] // CELLS):
        here = slice(k * CELLS, (k + 1) * CELLS)
        there = slice(k * 2 * GROUP, (k + 1) * 2 * GROUP)
        normal, _ = normalize(tokens_ref[here, :].astype(F32))
        live = live_rows(start + k * CELLS, CELLS, rows_ref, cols_ref)
        normal = normal * live
        normal_ref[here, :] = normal.astype(BF)
        half_ref[:, there, :feature] = turn(first_ref, normal).reshape(KEPT, 2 * GROUP, feature)
        ones = jnp.broadcast_to(live, (CELLS, LANES)).astype(BF)
        flat = mm(first_ref[0], ones) + mm(first_ref[1], ones)
        half_ref[:, there, feature:] = flat.reshape(KEPT, 2 * GROUP, LANES)


def first(rows, cols, tokens, tables, begin, steps, before=(), deps=(), tiles=1):
    cells, feature = tokens.shape
    table = tables["first"]
    block = pl.BlockSpec((tiles * CELLS, feature), lambda i: (i + begin, 0))
    operands = (rows, cols, tokens, table)
    return launch(
        deps,
        functools.partial(first_kernel, begin),
        grid=(steps,),
        out_shape=(
            jax.ShapeDtypeStruct((KEPT, 2 * ROWS, feature + LANES), F32),
            jax.ShapeDtypeStruct((cells, feature), BF),
            MARK,
        ),
        in_specs=[smem(), smem(), block, single(table.shape)] + [any_space() for _ in before],
        out_specs=(
            pl.BlockSpec((KEPT, 2 * GROUP * tiles, feature + LANES), lambda i: (0, i + begin, 0)),
            block,
            single(MARK.shape),
        ),
        input_output_aliases={len(operands) + k: k for k in range(len(before))},
        compiler_params=params(),
        cost_estimate=cost(6e9, 11e6),
        name="first",
    )(*operands, *before)


def build_mix(me, bits, weights_ref, layer, out_ref, feature):
    block = feature // BLOCKS
    half = feature // 2
    per_group = BLOCKS // 2
    share = 2 * feature // weights_ref.shape[0]
    each = block // share
    out_ref[...] = jnp.zeros_like(out_ref)
    row = lax.broadcasted_iota(jnp.int32, (LANES, half), 0)
    column = lax.broadcasted_iota(jnp.int32, (LANES, half), 1)
    for b in range(per_group):
        shift = jnp.where((column - b * block == row) & (row < block), 1.0, 0.0).astype(BF)
        low, high = b * block, (b + 1) * block
        for group in range(2):
            for part in range(2):
                at = (part * BLOCKS + group * per_group + b) * each
                pieces = [
                    weights_ref[place_of((at + k) ^ me, bits), layer * share : (layer + 1) * share, :]
                    for k in range(each)
                ]
                placed = mm(jnp.concatenate(pieces, axis=0), shift).astype(BF)
                for t in range(low // LANES, (high - 1) // LANES + 1):
                    begin, end = max(low, t * LANES), min(high, (t + 1) * LANES)
                    for c in range(low // LANES, (high - 1) // LANES + 1):
                        piece = placed[begin - low : end - low, c * LANES : (c + 1) * LANES]
                        for up in range(2):
                            top = 2 * t * LANES + up * LANES + begin - t * LANES
                            left = (2 * c + (up ^ part)) * LANES
                            value = -piece if part == 1 and up == 1 else piece
                            here = (group, slice(top, top + end - begin), slice(left, left + LANES))
                            out_ref[here] = out_ref[here] + value


def to_modes(half_ref, head_ref, body_ref, is_head):
    width = half_ref.shape[2]
    real, imag, ends = [], [], ()
    for k in range(TAKE):
        begin = is_head and k == 0
        rows = HEAD if begin else BODY
        spec = turn(head_ref if begin else body_ref, half_ref[k * GROUP : (k + 1) * GROUP].reshape(2 * BODY, width))
        real.append(spec[:BODY])
        imag.append(spec[rows : rows + BODY])
        if begin:
            ends = (spec[BODY:rows], spec[rows + BODY :])
    if is_head:
        real.append(ends[0])
        imag.append(ends[1])
    return jnp.concatenate(real, axis=0), jnp.concatenate(imag, axis=0)


def from_modes(pair_of, head_ref, body_ref, is_head, out_ref, product):
    for k in range(TAKE):
        begin = is_head and k == 0
        parts = []
        for part in pair_of:
            parts.append(part[k * BODY : (k + 1) * BODY])
            if begin:
                parts.append(part[TOOK:])
        result = product(head_ref if begin else body_ref, jnp.concatenate(parts, axis=0))
        out_ref[k * GROUP : (k + 1) * GROUP] = result.reshape(GROUP, 2 * ROWS, result.shape[1])


def mix_step(half_ref, head_ref, body_ref, back_head_ref, back_body_ref, mix1_ref, mix2_ref, wide_ref, long_ref,
             outs, heads, out_ref, is_head):
    feature = out_ref.shape[2]
    specs = to_modes(half_ref, head_ref, body_ref, is_head)
    gain = wide_ref[0:1, :]
    shift = wide_ref[1:2, :]

    def scaled(part):
        flat = jnp.concatenate([part[:, feature:]] * (feature // LANES), axis=1)
        return (part[:, :feature] * gain + flat * shift).astype(BF)

    inside = to_mixed(*(scaled(part) for part in specs))
    active, slope = gelu_parts(mix_product(inside, mix1_ref) + long_ref[0:1, :])
    hidden = active.astype(BF)
    value = mix_product(hidden, mix2_ref) + long_ref[1:2, :]
    bend = jnp.tanh(value / SHRINK)
    flat = jnp.concatenate([part[:, feature:] for part in specs], axis=1)
    for ref, head, kept in zip(outs, heads, (inside, hidden, slope, bend * bend, flat)):
        ref[...] = kept[:TOOK]
        if is_head:
            head[...] = kept[TOOK:]
    from_modes(from_mixed(value - SHRINK * bend), back_head_ref, back_body_ref, is_head, out_ref, turn)


def prepare_kernel(
    weight_bits, vector_bits, me_ref, weights_ref, *rest,
):
    mix1_ref, mix2_ref, wide_ref, long_ref, up_ref, vector_ref = rest[-6:]
    feature = wide_ref.shape[1]
    devices = vector_ref.shape[1]
    share = feature // devices
    me = me_ref[0]
    if len(rest) > 6:
        vector_ref[...] = rest[0][...]
    else:
        rows = weights_ref[:, 4 * share :, :].astype(F32)
        for d in range(devices):
            for k in range(vector_ref.shape[0]):
                vector_ref[k, d : d + 1, :] = rows[d, k : k + 1, :]
    build_mix(me, weight_bits, weights_ref, 0, mix1_ref, feature)
    build_mix(me, weight_bits, weights_ref, 1, mix2_ref, feature)
    wide_ref[...] = jnp.zeros_like(wide_ref)
    long_ref[...] = jnp.zeros_like(long_ref)
    for row, at in enumerate((2, 3, 4, 5, 7)):
        wide_ref[row : row + 1, :] = spread(vector_ref[at], share, me, vector_bits)
    for row in range(2):
        both = spread(vector_ref[row], 2 * share, me, vector_bits)
        long_ref[row : row + 1, :] = to_mixed(both[:, :feature], both[:, feature:])
    up_ref[...] = spread(vector_ref[6], up_ref.shape[1] // devices, me, vector_bits)


def prepare(me, weights, vectors, feature, hidden, weight_bits, vector_bits):
    shapes = (
        jax.ShapeDtypeStruct((2, feature, feature), BF),
        jax.ShapeDtypeStruct((2, feature, feature), BF),
        jax.ShapeDtypeStruct((8, feature), F32),
        jax.ShapeDtypeStruct((8, 2 * feature), F32),
        jax.ShapeDtypeStruct((1, hidden), F32),
    )
    devices = vectors[0].shape[1] if vectors else weights.shape[0]
    return pl.pallas_call(
        functools.partial(prepare_kernel, weight_bits, vector_bits),
        out_shape=shapes,
        in_specs=[smem()] + vmem(1 + len(vectors)),
        out_specs=vmem(len(shapes)),
        scratch_shapes=[pltpu.VMEM((8, devices, LANES), F32)],
        compiler_params=params(),
        cost_estimate=cost(0, 0),
        name="prepare",
    )(me, weights, *vectors)


def mix_first_kernel(
    half_ref, mix1_ref, mix2_ref, wide_ref, long_ref, head_ref, body_ref, back_head_ref, back_body_ref,
    out_ref, *rest,
):
    work = functools.partial(
        mix_step, half_ref, head_ref, body_ref, back_head_ref, back_body_ref, mix1_ref, mix2_ref, wide_ref, long_ref,
        rest[:5], rest[5:], out_ref,
    )

    @pl.when(pl.program_id(0) == 0)
    def _():
        work(True)

    @pl.when(pl.program_id(0) > 0)
    def _():
        work(False)


def mix_second_kernel(
    half_ref, mix1_ref, mix2_ref, wide_ref, long_ref, body_ref, back_body_ref,
    out_ref, *outs,
):
    mix_step(
        half_ref, None, body_ref, None, back_body_ref, mix1_ref, mix2_ref, wide_ref, long_ref,
        outs, (None,) * 5, out_ref, False,
    )


def mode_shapes(rows, feature):
    wide = [jax.ShapeDtypeStruct((rows, 2 * feature), kind) for kind in (BF, BF, F32, F32)]
    return wide + [jax.ShapeDtypeStruct((rows, 2 * LANES), F32)]


def mode_blocks(feature):
    return [pl.BlockSpec((TOOK, width), lambda i: (i, 0)) for width in (2 * feature,) * 4 + (2 * LANES,)]


def half_block(width, begin=0):
    return pl.BlockSpec((TAKE * GROUP, 2 * ROWS, width), lambda i: (i + begin, 0, 0))


def mix_first(half, mix1, mix2, wide, long, tables, steps, deps=()):
    feature = half.shape[2] - LANES
    fixed = (mix1, mix2, wide, long, tables["head"], tables["body"], tables["head_wt"], tables["body_wt"])
    heads = mode_shapes(ROWS, feature)
    return launch(
        deps,
        mix_first_kernel,
        grid=(steps,),
        out_shape=[jax.ShapeDtypeStruct((TAKE * GROUP * steps, 2 * ROWS, feature), F32)]
        + mode_shapes(TOOK * steps, feature) + heads,
        in_specs=[half_block(feature + LANES)] + [single(v.shape) for v in fixed],
        out_specs=[half_block(feature)] + mode_blocks(feature) + [single(v.shape) for v in heads],
        compiler_params=params(),
        cost_estimate=cost(9e9, 20e6),
        name="mix_first",
    )(half, *fixed)


def mix_second(half, mix1, mix2, wide, long, tables, begin, steps, deps=()):
    feature = half.shape[2] - LANES
    fixed = (mix1, mix2, wide, long, tables["body"], tables["body_wt"])
    return launch(
        deps,
        mix_second_kernel,
        grid=(steps,),
        out_shape=[jax.ShapeDtypeStruct((TAKE * GROUP * steps, 2 * ROWS, feature), F32)] + mode_shapes(TOOK * steps, feature),
        in_specs=[half_block(feature + LANES, begin)] + [single(v.shape) for v in fixed],
        out_specs=[half_block(feature)] + mode_blocks(feature),
        compiler_params=params(),
        cost_estimate=cost(9e9, 20e6),
        name="mix_second",
    )(half, *fixed)


def space_kernel(rows_ref, cols_ref, half1_ref, half2_ref, tokens_ref, first_t_ref, wide_ref, middle_ref, normed_ref, mark_ref):
    mark_ref[...] = jnp.zeros_like(mark_ref)
    feature = tokens_ref.shape[1]
    start = pl.program_id(0) * tokens_ref.shape[0]
    for k in range(tokens_ref.shape[0] // CELLS):
        here = slice(k * CELLS, (k + 1) * CELLS)
        flat = lambda ref: ref[:, k * 2 * GROUP : (k + 1) * 2 * GROUP, :].reshape(-1, feature)
        spatial = turn(first_t_ref, jnp.concatenate([flat(half1_ref), flat(half2_ref)], axis=0))
        inputs = tokens_ref[here, :].astype(F32)
        live = live_rows(start + k * CELLS, CELLS, rows_ref, cols_ref)
        normal, _ = normalize(inputs)
        middle = inputs + live * (spatial + (normal * wide_ref[0:1, :] + wide_ref[1:2, :]))
        middle_ref[here, :] = middle
        normal, _ = normalize(middle)
        normed_ref[here, :] = (normal * wide_ref[2:3, :] + wide_ref[3:4, :]).astype(BF)


def column_block(rows, width, tiles=1):
    return pl.BlockSpec((rows, 2 * GROUP * tiles, width), lambda i: (0, i, 0))


def space(rows, cols, half1, half2, tokens, wide, tables, deps=(), tiles=1):
    cells, feature = tokens.shape
    table = tables["first_t"]
    block = pl.BlockSpec((tiles * CELLS, feature), lambda i: (i, 0))
    return launch(
        deps,
        space_kernel,
        grid=(STEPS // tiles,),
        out_shape=(jax.ShapeDtypeStruct((cells, feature), F32), jax.ShapeDtypeStruct((cells, feature), BF), MARK),
        in_specs=[smem(), smem(), column_block(half1.shape[0], feature, tiles), column_block(half2.shape[0], feature, tiles),
                  block, single(table.shape), single(wide.shape)],
        out_specs=(block, block, single(MARK.shape)),
        compiler_params=params(),
        cost_estimate=cost(6e9, 20e6),
        name="space",
    )(rows, cols, half1, half2, tokens, table, wide)


def fetch_weights(me_ref, pieces, places, up_ref, down_ref, sems):
    each = pieces[0].shape[0]
    held = len(pieces) // 2
    count = each * held
    chip = me_ref[0] // 2

    def copies(own, core):
        target = (up_ref, down_ref)[core]
        source = pieces[:held] if own else pieces[held:]
        for mask in range(count):
            at = places[core][mask]
            part = source[at // each].at[at % each]
            yield pltpu.make_async_copy(part, target.at[chip ^ mask], sems.at[core, mask])

    for core in range(2):
        @pl.when(me_ref[0] % 2 == core)
        def _():
            for copy in copies(True, core):
                copy.start()
            for copy in copies(False, 1 - core):
                copy.start()

    def arrived(core):
        for copy in copies(True, core):
            copy.wait()

    return arrived


def up_lanes(up_ref, j, begin, count, feature):
    share = up_ref.shape[1] * feature // (up_ref.shape[0] * up_ref.shape[1])
    return up_ref[:, j * share : (j + 1) * share, begin : begin + count].reshape(feature, count)


def down_rows(down_ref, begin, count):
    share = down_ref.shape[1]
    pieces = []
    at = begin
    while at < begin + count:
        unit, first_row = divmod(at, share)
        last_row = min(share, first_row + begin + count - at)
        pieces.append(down_ref[unit, first_row:last_row, :])
        at += last_row - first_row
    return jnp.concatenate(pieces, axis=0)


def weight_scratch(pieces):
    chips, rows, feature = UNITS, pieces[0].shape[1], pieces[0].shape[2]
    return [
        pltpu.VMEM((chips, rows, feature), BF),
        pltpu.VMEM((chips, rows, feature), BF),
        pltpu.SemaphoreType.DMA((2, chips)),
    ]


def up_part(up_ref, j, feature):
    share = up_ref.shape[1] * feature // (up_ref.shape[0] * up_ref.shape[1])
    return up_ref[:, j * share : (j + 1) * share, :].reshape(feature, feature)


def down_part(down_ref, j, feature):
    share = down_ref.shape[1]
    each = feature // share
    return down_ref[j * each : (j + 1) * each].reshape(feature, feature)


def feed_kernel(places, rows_ref, cols_ref, me_ref, normed_in_ref, grad_ref, bias_ref, *rest):
    pieces = rest[:-17]
    (
        active_all_ref, pre_all_ref, bias_grad_ref, up_all_ref, down_all_ref, send_ref, keep_ref,
        active_ref, pre_ref, normed_ref, branch_ref, up_ref, down_ref, sems, weight_sems, row_sems, grad_sems,
    ) = rest[-17:]
    tile, feature = normed_in_ref.shape
    cells, hidden = active_ref.shape
    tiles = cells // tile
    parts = hidden // feature
    chips, share, _ = up_ref.shape
    each = chips // parts
    small = share // parts
    step = pl.program_id(0)
    mine = pl.ds(pl.multiple_of(jnp.minimum(step, tiles - 1) * tile, tile), tile)
    copies = [
        pltpu.make_async_copy(source, target, weight_sems.at[k])
        for k, (source, target) in enumerate(((up_ref, up_all_ref), (down_ref, down_all_ref)))
    ]

    def row_copies(k):
        here = pl.ds(k * tile, tile)
        return (
            pltpu.make_async_copy(active_ref.at[here], active_all_ref.at[here], row_sems.at[0, k]),
            pltpu.make_async_copy(pre_ref.at[here], pre_all_ref.at[here], row_sems.at[1, k]),
        )

    def work(arrived):
        live = live_rows(step * tile, tile, rows_ref, cols_ref)
        branch = (grad_ref[...].astype(F32) * live).astype(BF)
        branch_ref[mine, :] = branch
        normed = normed_in_ref[...]
        normed_ref[mine, :] = normed
        if arrived:
            arrived(0)
            copies[0].start()
        for begin in range(0, hidden, WIDTH):
            place = slice(begin, begin + WIDTH)
            j, lane = divmod(begin, feature)
            value = mm(normed, up_lanes(up_ref, j, lane, WIDTH, feature)) + bias_ref[:, place]
            if arrived and begin == 0:
                arrived(1)
                copies[1].start()
            grad = mm(branch, down_rows(down_ref, begin, WIDTH), (1, 1))
            active, slope = gelu_parts(value)
            active_ref[mine, place] = active.astype(BF)
            grad = grad * slope
            pre_ref[mine, place] = grad.astype(BF)
            bias_grad_ref[:, place] += jnp.sum(grad, axis=0, keepdims=True)

    @pl.when(step == 0)
    def _():
        bias_grad_ref[...] = jnp.zeros_like(bias_grad_ref)
        work(fetch_weights(me_ref, pieces, places, up_ref, down_ref, sems))

    @pl.when((step > 0) & (step < tiles))
    def _():
        work(None)

    for k in range(tiles):
        @pl.when(step == k)
        def _():
            for copy in row_copies(k):
                copy.start()

    def down_copies(j, target):
        for k in range(each):
            yield pltpu.make_async_copy(up_ref.at[j * each + k], target.at[places[1][j * each + k]], grad_sems.at[j, k])

    def up_copies(j, target):
        for k in range(chips):
            source = down_ref.at[j * each + k // each, pl.ds(k % each * small, small)]
            there = target.at[places[0][k], pl.ds(j * small, small)]
            yield pltpu.make_async_copy(source, there, grad_sems.at[parts + j, k])

    @pl.when(step == tiles)
    def _():
        for copy in copies:
            copy.wait()

    @pl.when((step >= tiles) & (step < tiles + parts))
    def _():
        j = step - tiles
        for k in range(each // 2):
            lanes = pl.ds(pl.multiple_of(j * feature + k * 2 * share, LANES), 2 * share)
            piece = mm(active_ref[:, lanes], branch_ref[...], (0, 0)).astype(BF)
            up_ref[pl.ds(j * each + 2 * k, 2)] = piece.reshape(2, share, feature)

    @pl.when(step >= tiles + parts)
    def _():
        j = step - tiles - parts
        lanes = pl.ds(pl.multiple_of(j * feature, LANES), feature)
        for k in range(each // 2):
            piece = mm(normed_ref[:, k * 2 * share : (k + 1) * 2 * share], pre_ref[:, lanes], (0, 0)).astype(BF)
            down_ref[pl.ds(j * each + 2 * k, 2)] = piece.reshape(2, share, feature)

    for j in range(parts):
        for core in range(2):
            targets = (send_ref, keep_ref) if core == 0 else (keep_ref, send_ref)

            @pl.when((step == tiles + j) & (me_ref[0] % 2 == core))
            def _():
                for copy in down_copies(j, targets[0]):
                    copy.start()

            @pl.when((step == tiles + parts + j) & (me_ref[0] % 2 == core))
            def _():
                for copy in up_copies(j, targets[1]):
                    copy.start()

    @pl.when(step == tiles + 2 * parts - 1)
    def _():
        for k in range(tiles):
            for copy in row_copies(k):
                copy.wait()
        for j in range(parts):
            for copy in down_copies(j, send_ref):
                copy.wait()
            for copy in up_copies(j, send_ref):
                copy.wait()


def feed(rows, cols, me, normed, grad, bias, pieces, places, tile=256, deps=()):
    cells, feature = normed.shape
    hidden = bias.shape[1]
    tiles, parts = cells // tile, hidden // feature
    block = pl.BlockSpec((tile, feature), lambda i: (jnp.minimum(i, tiles - 1), 0))
    weights = jax.ShapeDtypeStruct((UNITS,) + pieces[0].shape[1:], BF)
    rows_shape = jax.ShapeDtypeStruct((cells, hidden), BF)
    return launch(
        deps,
        functools.partial(feed_kernel, places),
        grid=(tiles + 2 * parts,),
        out_shape=(rows_shape, rows_shape, jax.ShapeDtypeStruct((1, hidden), F32)) + (weights,) * 4,
        in_specs=[smem(), smem(), smem(), block, block, single(bias.shape)] + [any_space() for _ in pieces],
        out_specs=(any_space(), any_space(), single((1, hidden))) + (any_space(),) * 4,
        scratch_shapes=[
            pltpu.VMEM((cells, hidden), BF),
            pltpu.VMEM((cells, hidden), BF),
            pltpu.VMEM((cells, feature), BF),
            pltpu.VMEM((cells, feature), BF),
            *weight_scratch(pieces),
            pltpu.SemaphoreType.DMA((2,)),
            pltpu.SemaphoreType.DMA((2, tiles)),
            pltpu.SemaphoreType.DMA((2 * parts, UNITS)),
        ],
        compiler_params=params(),
        cost_estimate=cost(0, 0),
        name="feed",
    )(rows, cols, me, normed, grad, bias, *pieces)


def down_kernel(rows_ref, cols_ref, active_ref, pre_ref, middle_ref, grad_ref, normal_ref, wide_ref, first_ref,
                up_ref, down_ref, mixed_ref, grad_middle_ref, half_ref, sums_ref):
    tile, feature = middle_ref.shape
    hidden = active_ref.shape[1]
    step = pl.program_id(0)

    @pl.when(step == 0)
    def _():
        sums_ref[...] = jnp.zeros_like(sums_ref)

    live = live_rows(step * tile, tile, rows_ref, cols_ref)
    branch = mm(active_ref[...], down_ref[...].reshape(hidden, feature))
    up = jnp.concatenate([up_part(up_ref, j, feature) for j in range(hidden // feature)], axis=1)
    grad_normed = mm(pre_ref[...], up, (1, 1))
    middle = middle_ref[...]
    mixed_ref[...] = (middle + live * (branch + wide_ref[4:5, :])).astype(BF)
    normal, inverse = normalize(middle)
    cotangent = grad_ref[...].astype(F32)
    grad_middle = cotangent + norm_back(grad_normed, wide_ref[2:3, :], normal, inverse)
    grad_middle_ref[...] = grad_middle
    masked = grad_middle * live
    half_ref[...] = turn(first_ref, masked).reshape(half_ref.shape)
    rows = (grad_normed * normal, grad_normed, cotangent * live, masked * normal_ref[...].astype(F32), masked)
    for row, value in enumerate(rows):
        sums_ref[row : row + 1, :] += jnp.sum(value, axis=0, keepdims=True)


def feed_down(rows, cols, active, pre, middle, grad, normal, wide, table, up, down, deps=()):
    cells, feature = middle.shape
    hidden = active.shape[1]
    block = lambda width: pl.BlockSpec((CELLS, width), lambda i: (i, 0))
    operands = (rows, cols, active, pre, middle, grad, normal, wide, table, up, down)
    return launch(
        deps,
        down_kernel,
        grid=(cells // CELLS,),
        out_shape=(
            jax.ShapeDtypeStruct((cells, feature), BF),
            jax.ShapeDtypeStruct((cells, feature), F32),
            jax.ShapeDtypeStruct((KEPT, 2 * ROWS, feature), F32),
            jax.ShapeDtypeStruct((8, feature), F32),
        ),
        in_specs=[smem(), smem(), block(hidden), block(hidden), block(feature), block(feature), block(feature)]
        + [single(v.shape) for v in operands[7:]],
        out_specs=(block(feature), block(feature), column_block(KEPT, feature), single((8, feature))),
        compiler_params=params(),
        cost_estimate=cost(0, 0),
        name="feed_down",
    )(*operands)


def back_step(half_ref, head_ref, body_ref, back_head_ref, back_body_ref, mix1_ref, mix2_ref, ins, in_heads,
              outs, out_heads, out_ref, sums_ref, is_head):
    feature = out_ref.shape[2]

    def read(k):
        if is_head:
            return jnp.concatenate([ins[k][...], in_heads[k][...]], axis=0)
        return ins[k][...]

    grads = to_modes(half_ref, head_ref, body_ref, is_head)
    grad_two = (to_mixed(*grads) * read(1)).astype(BF)
    grad_one = (mix_product(grad_two, mix2_ref, True) * read(0)).astype(BF)
    grad_spec = mix_product(grad_one, mix1_ref, True)
    from_modes(from_mixed(grad_spec), back_head_ref, back_body_ref, is_head, out_ref, turn_once)
    for row, value in enumerate((grad_one, grad_two)):
        outs[row][...] = value[:TOOK]
        if is_head:
            out_heads[row][...] = value[TOOK:]
    flat = jnp.concatenate([read(3)] * (feature // LANES), axis=1)
    for row, value in enumerate((grad_one.astype(F32), grad_two.astype(F32), grad_spec * read(2).astype(F32), grad_spec * flat)):
        total = jnp.sum(value, axis=0, keepdims=True)
        sums_ref[row : row + 1, :] = total if is_head else sums_ref[row : row + 1, :] + total


def mix_back_kernel(
    half_ref, slope1_ref, slope2_ref, bend1_ref, bend2_ref, low1_ref, low2_ref, flat1_ref, flat2_ref,
    slope_head_ref, bend_head_ref, low_head_ref, flat_head_ref, mix1_ref, mix2_ref,
    head_ref, body_ref, back_head_ref, back_body_ref,
    out_ref, one_ref, two_ref, one_head_ref, two_head_ref, sums_ref,
):
    step = pl.program_id(0)
    steps = pl.num_programs(0) // 2
    work = functools.partial(
        back_step, half_ref, head_ref, body_ref, back_head_ref, back_body_ref, mix1_ref, mix2_ref
    )
    heads = (slope_head_ref, bend_head_ref, low_head_ref, flat_head_ref)
    more = (heads, (one_ref, two_ref), (one_head_ref, two_head_ref), out_ref, sums_ref)
    near = (slope1_ref, bend1_ref, low1_ref, flat1_ref)
    far = (slope2_ref, bend2_ref, low2_ref, flat2_ref)

    @pl.when(step == 0)
    def _():
        sums_ref[...] = jnp.zeros_like(sums_ref)
        work(near, *more, True)

    @pl.when((step > 0) & (step < steps))
    def _():
        work(near, *more, False)

    @pl.when(step >= steps)
    def _():
        work(far, *more, False)


def mix_back(half, modes1, modes2, heads, mix1, mix2, tables, deps=()):
    feature = half.shape[2]
    steps = KEPT // GROUP // TAKE
    fixed = tuple(heads[k] for k in (2, 3, 0, 4)) + (
        mix1, mix2, tables["head_w"], tables["body_w"], tables["head_t"], tables["body_t"]
    )
    moving = []
    specs = []
    for k in (2, 3, 0, 4):
        width = modes1[k].shape[1]
        moving += [modes1[k], modes2[k]]
        specs += [
            pl.BlockSpec((TOOK, width), lambda i: (jnp.minimum(i, steps // 2 - 1), 0)),
            pl.BlockSpec((TOOK, width), lambda i: (jnp.maximum(i - steps // 2, 0), 0)),
        ]
    low = lambda rows: jax.ShapeDtypeStruct((rows, 2 * feature), BF)
    body = pl.BlockSpec((TOOK, 2 * feature), lambda i: (i, 0))
    shapes = (
        jax.ShapeDtypeStruct((KEPT, 2 * ROWS, feature), F32), low(TOOK * steps), low(TOOK * steps),
        low(ROWS), low(ROWS), jax.ShapeDtypeStruct((8, 2 * feature), F32),
    )
    return launch(
        deps,
        mix_back_kernel,
        grid=(steps,),
        out_shape=shapes,
        in_specs=[half_block(feature)] + specs + [single(v.shape) for v in fixed],
        out_specs=[half_block(feature), body, body] + [single(v.shape) for v in shapes[3:]],
        compiler_params=params(),
        cost_estimate=cost(18e9, 30e6),
        name="mix_back",
    )(half, *moving, *fixed)


def block_kernel(left1_ref, left2_ref, left_head_ref, right_ref, right_head_ref, out_ref, natural_ref):
    wide = 2 * LANES
    count = left1_ref.shape[1] // wide
    cut = left1_ref.shape[0]
    for t in range(count):
        for c in range(max(t - 1, 0), min(t + 2, count)):
            left, right = slice(t * wide, (t + 1) * wide), slice(c * wide, (c + 1) * wide)
            total = (
                mm(left1_ref[:, left], right_ref[:cut, right], (0, 0))
                + mm(left2_ref[:, left], right_ref[cut:, right], (0, 0))
                + mm(left_head_ref[:, left], right_head_ref[:, right], (0, 0))
            )
            rows, lanes = slice(t * LANES, (t + 1) * LANES), slice(c * LANES, (c + 1) * LANES)
            natural_ref[0, rows, lanes] = total[:LANES, :LANES] + total[LANES:, LANES:]
            natural_ref[1, rows, lanes] = total[:LANES, LANES:] - total[LANES:, :LANES]
    per_group = BLOCKS // 2
    block = count * LANES // per_group
    for b in range(per_group):
        begin = b * block
        base = begin // LANES * LANES
        reach = min(base + wide, count * LANES) - base
        for part in range(2):
            piece = natural_ref[part, begin : begin + block, base : base + reach]
            if begin > base:
                piece = pltpu.roll(piece, reach - (begin - base), axis=1)
            out_ref[part, b * block : (b + 1) * block, :] = piece[:, :LANES]


def block_grads(left1, left2, left_head, right, right_head, name, deps=()):
    feature = left1.shape[1] // 2
    half = feature // 2
    block = lambda v: pl.BlockSpec((v.shape[0], feature), lambda i: (0, i))
    return launch(
        deps,
        block_kernel,
        grid=(2,),
        out_shape=jax.ShapeDtypeStruct((2, feature, LANES), F32),
        in_specs=[block(v) for v in (left1, left2, left_head, right, right_head)],
        out_specs=pl.BlockSpec((2, half, LANES), lambda i: (0, i, 0)),
        scratch_shapes=[pltpu.VMEM((2, half, half), F32)],
        compiler_params=params(),
        cost_estimate=cost(5e9, 7e6),
        name=name,
    )(left1, left2, left_head, right, right_head)


def last_kernel(begin, rows_ref, cols_ref, half_ref, tokens_ref, grad_ref, first_t_ref, wide_ref, *rest):
    out_ref, mark_ref = rest[-2:]
    mark_ref[...] = jnp.zeros_like(mark_ref)
    tile, feature = tokens_ref.shape
    live = live_rows((pl.program_id(0) + begin) * tile, tile, rows_ref, cols_ref)
    grad_middle = grad_ref[...]
    grad_normed = live * (grad_middle + turn_once(first_t_ref, half_ref[...].reshape(CELLS, feature)))
    normal, inverse = normalize(tokens_ref[...].astype(F32))
    out_ref[...] = grad_middle + norm_back(grad_normed, wide_ref[0:1, :], normal, inverse)


def last(rows, cols, half, tokens, grad, wide, tables, begin, steps, before=(), deps=()):
    cells, feature = tokens.shape
    first_t = tables["first_t"]
    block = pl.BlockSpec((CELLS, feature), lambda i: (i + begin, 0))
    operands = (rows, cols, half, tokens, grad, first_t, wide)
    return launch(
        deps,
        functools.partial(last_kernel, begin),
        grid=(steps,),
        out_shape=(jax.ShapeDtypeStruct((cells, feature), F32), MARK),
        in_specs=[smem(), smem(), pl.BlockSpec((KEPT, 2 * GROUP, feature), lambda i: (0, i + begin, 0)), block, block,
                  single(first_t.shape), single(wide.shape)] + [any_space() for _ in before],
        out_specs=(block, single(MARK.shape)),
        input_output_aliases={len(operands): 0} if before else {},
        compiler_params=params(),
        cost_estimate=cost(6e9, 20e6),
        name="last",
    )(*operands, *before)


def collect(value, per_device, devices):
    total = value.shape[1]
    owner = lax.broadcasted_iota(jnp.int32, (devices, total), 1) // per_device
    row = lax.broadcasted_iota(jnp.int32, (devices, total), 0)
    high, low = split(jnp.where(owner == row, jnp.broadcast_to(value, (devices, total)), 0.0))
    place = lax.broadcasted_iota(jnp.int32, (total, LANES), 0)
    lane = lax.broadcasted_iota(jnp.int32, (total, LANES), 1)
    pick = jnp.where(place % per_device == lane, 1.0, 0.0).astype(BF)
    return mm(high, pick) + mm(low, pick)


def emit(place, sum_ref, send_refs, keep_ref):
    half, _, rows, _ = sum_ref.shape
    rows = rows - 8
    for k, send_ref in enumerate(send_refs):
        away = sum_ref[:, pl.ds(place ^ (k + 1), 1)].reshape(half, rows + 8, LANES)
        high, low = split(away[:, rows:])
        send_ref[:, :rows] = away[:, :rows].astype(BF)
        send_ref[:, rows:] = jnp.concatenate([high.astype(F32), low.astype(F32)], axis=1).astype(BF)
    keep_ref[...] = sum_ref[:, pl.ds(place, 1)].reshape(half, rows + 8, LANES)


def pack_kernel(place_ref, one_ref, two_ref, mixed_ref, sums_ref, up_ref, wide_ref, send_ref, keep_ref, sum_ref):
    half, _, rows, _ = sum_ref.shape
    devices = 2 * half
    share = (rows - 8) // 4
    feature = sums_ref.shape[1]
    sum_ref[:, :, : 2 * share] = one_ref[...].reshape(half, 2, 2 * share, LANES)
    sum_ref[:, :, 2 * share : 4 * share] = two_ref[...].reshape(half, 2, 2 * share, LANES)
    first_gain, first_bias = scale_grads(mixed_ref, sums_ref, wide_ref)
    natural = [jnp.concatenate(from_mixed(mixed_ref[k : k + 1, :]), axis=1) for k in range(2)]
    narrow = [first_gain, first_bias] + [sums_ref[k : k + 1, :] for k in range(3)]
    for k, value in enumerate(narrow + natural + [up_ref[...]]):
        placed = collect(value, value.shape[1] // devices, devices)
        for d in range(devices):
            sum_ref[d // 2, d % 2, 4 * share + k : 4 * share + k + 1, :] = placed[d : d + 1, :]
    emit(place_ref[0], sum_ref, (send_ref,), keep_ref)


def scale_grads(mixed_ref, sums_ref, wide_ref):
    real, imag = from_mixed(mixed_ref[2:3, :])
    scaled = real + imag
    real, imag = from_mixed(mixed_ref[3:4, :])
    flat = real + imag
    gain = sums_ref[3:4, :] + (scaled - wide_ref[1:2, :] * flat) / wide_ref[0:1, :]
    return gain, sums_ref[4:5, :] + flat


def small_shapes(half, rows, others):
    shapes = [jax.ShapeDtypeStruct((half, rows + 8, LANES), BF)] * others
    return shapes + [jax.ShapeDtypeStruct((half, rows, LANES), F32)]


def pack(upper, one, two, mixed, sums, up, wide, devices):
    rows = 2 * one.shape[0] * one.shape[1] // devices + 8
    shapes = small_shapes(devices // 2, rows, 1)
    operands = (one, two, mixed, sums, up, wide)
    return pl.pallas_call(
        pack_kernel,
        out_shape=shapes,
        in_specs=[smem()] + vmem(len(operands)),
        out_specs=vmem(2),
        scratch_shapes=[pltpu.VMEM((devices // 2, 2, rows, LANES), F32)],
        compiler_params=params(),
        cost_estimate=cost(0, 0),
        name="pack",
    )(upper, *operands)


def merge_small(keep_ref, got_refs):
    rows = keep_ref.shape[1] - 8
    top, tail = keep_ref[:, :rows], keep_ref[:, rows:]
    for got_ref in got_refs:
        both = got_ref[:, rows:].astype(F32)
        top = top + got_ref[:, :rows].astype(F32)
        tail = tail + (both[:, :8] + both[:, 8:])
    return top, tail


def fold_small_kernel(others, place_ref, keep_ref, *rest):
    sum_ref = rest[-1]
    send_refs, out_ref = rest[-2 - others : -2], rest[-2]
    half, count, rows, _ = sum_ref.shape
    top, tail = merge_small(keep_ref, rest[: len(rest) - 2 - others])
    sum_ref[:, :, : rows - 8] = top.reshape(half, count, rows - 8, LANES)
    sum_ref[:, :, rows - 8 :] = tail.reshape(half, count, 8, LANES)
    emit(place_ref[0], sum_ref, send_refs, out_ref)


def fold_small(keep, got, place, count, deps=()):
    half, rows = keep.shape[0] // count, keep.shape[1]
    shapes = small_shapes(half, rows, count - 1)
    return launch(
        deps,
        functools.partial(fold_small_kernel, count - 1),
        out_shape=shapes,
        in_specs=[smem()] + vmem(1 + len(got)),
        out_specs=vmem(len(shapes)),
        scratch_shapes=[pltpu.VMEM((half, count, rows, LANES), F32)],
        compiler_params=params(SMALL_LIMIT),
        cost_estimate=cost(0, 0),
        name="fold_small",
    )(place, keep, *got)


def vmem(count):
    return [pl.BlockSpec(memory_space=pltpu.VMEM)] * count


def end_small_kernel(others, keep_ref, *rest):
    got_refs, (one_ref, two_ref, *rows_refs) = rest[:others], rest[others:]
    top, tail = merge_small(keep_ref, got_refs)
    share, block = one_ref.shape
    one_ref[...] = top[0, :share, :block]
    two_ref[...] = top[0, share:, :block]
    for row, ref in enumerate(rows_refs):
        ref[...] = tail[0, row : row + 1, : ref.shape[1]]


def end_small(keep, got, share, block, widths):
    shapes = [jax.ShapeDtypeStruct((share, block), F32)] * 2
    shapes += [jax.ShapeDtypeStruct((1, width), F32) for width in widths]
    return pl.pallas_call(
        functools.partial(end_small_kernel, len(got)),
        out_shape=shapes,
        in_specs=vmem(1 + len(got)),
        out_specs=vmem(len(shapes)),
        compiler_params=params(SMALL_LIMIT),
        cost_estimate=cost(0, 0),
        name="end_small",
    )(keep, *got)


def begin_small_kernel(one_ref, two_ref, *rest):
    out_ref, rows_ref = rest[-2:]
    share, block = one_ref.shape
    out_ref[...] = jnp.zeros_like(out_ref)
    rows_ref[...] = jnp.zeros_like(rows_ref)
    out_ref[0, :share, :block] = one_ref[...]
    out_ref[0, share : 2 * share, :block] = two_ref[...]
    for row, ref in enumerate(rest[:-2]):
        rows_ref[row : row + 1, : ref.shape[1]] = ref[...].astype(F32)
    out_ref[0, 2 * share :, :] = rows_ref[...].astype(BF)


def begin_small(one, two, vectors):
    share = one.shape[0]
    operands = (one, two) + tuple(v[None] for v in vectors)
    return pl.pallas_call(
        begin_small_kernel,
        out_shape=jax.ShapeDtypeStruct((1, 2 * share + 16, LANES), BF),
        in_specs=vmem(len(operands)),
        out_specs=vmem(1)[0],
        scratch_shapes=[pltpu.VMEM((16, LANES), F32)],
        compiler_params=params(),
        cost_estimate=cost(0, 0),
        name="begin_small",
    )(*operands)


AXES = ("dp", "fsdp")


def swap(value, devices, bits):
    return lax.ppermute(value, AXES, [(i, i ^ (1 << bits[i & 1])) for i in range(devices)])


def doubling_orders(count):
    first = list(range(count - 1, 0, -1))
    second = list(first)
    for k in range(0, len(second) - 1, 2):
        second[k], second[k + 1] = second[k + 1], second[k]
    return first, second


def places_of(order):
    return [
        sum(1 << k for k, bit in enumerate(order) if mask >> (bit - 1) & 1) for mask in range(1 << len(order))
    ]


def join_kernel(*refs):
    out_ref = refs[-1]
    count = refs[0].shape[0]
    for k, ref in enumerate(refs[:-1]):
        out_ref[k * count : (k + 1) * count] = ref[...]


def join_rows(*pieces, deps=()):
    shape = jax.ShapeDtypeStruct((len(pieces) * pieces[0].shape[0],) + pieces[0].shape[1:], pieces[0].dtype)
    return launch(
        deps,
        join_kernel,
        out_shape=shape,
        in_specs=[pl.BlockSpec(memory_space=pltpu.VMEM) for _ in pieces],
        out_specs=pl.BlockSpec(memory_space=pltpu.VMEM),
        compiler_params=params(SMALL_LIMIT),
        cost_estimate=cost(0, 0),
        name="join",
    )(*pieces)


def hold(value, deps):
    def body(*refs):
        pass

    return pl.pallas_call(
        body,
        out_shape=jax.ShapeDtypeStruct(value.shape, value.dtype),
        in_specs=[any_space()] + unread(deps),
        out_specs=any_space(),
        input_output_aliases={0: 0},
        compiler_params=params(SMALL_LIMIT),
        cost_estimate=cost(0, 0),
        name="hold",
    )(value, *deps)


def gather_small(value, me, devices, count):
    held = value[None]
    for bit in list(range(3, count)) + [2, 1, 0]:
        other = swap(held, devices, (bit, bit))
        upper = (me >> bit) & 1
        axis = 0 if bit > 2 else 1
        join_two = lambda a, b: jnp.stack([a, b], axis=axis).reshape((-1,) + value.shape)
        held = jnp.where(upper == 0, join_two(held, other), join_two(other, held))
    return held


def scatter_small(value, me, devices, count, exact):
    shape = value.shape[1:]
    rows = shape[0]
    total = value
    for bit in [0, 1, 2] + list(range(count - 1, 2, -1)):
        upper = (me >> bit) & 1
        axis = 0 if bit > 2 else 1
        pair = total.reshape(((2, -1) if bit > 2 else (-1, 2)) + shape)
        away = lax.dynamic_index_in_dim(pair, 1 - upper, axis, keepdims=False)
        keep = lax.dynamic_index_in_dim(pair, upper, axis, keepdims=False)
        sums = away[:, rows - exact :]
        top = lax.reduce_precision(sums, 8, 7)
        packet = jnp.concatenate([away[:, : rows - exact], top, sums - top], axis=1).astype(BF)
        got = swap(packet, devices, (bit, bit)).astype(F32)
        low = got[:, rows - exact : rows] + got[:, rows:]
        total = keep + jnp.concatenate([got[:, : rows - exact], low], axis=1)
    return total[0]


def chip_unit(up, down, core, devices):
    parts, share, feature = up.shape
    flat = up.reshape(parts * share, feature)
    other = swap(jnp.where(core == 0, down, flat), devices, (0, 0))
    up_unit = jnp.concatenate([up, other.reshape(up.shape)], axis=1).reshape(2 * parts * share, feature)
    return jnp.where(core == 0, up_unit, jnp.concatenate([other, down]))[None]


def fold_kernel(upper_ref, keep_away_ref, got_away_ref, keep_own_ref, got_own_ref, send_ref, keep_ref):
    send_ref[...] = (keep_away_ref[...].astype(F32) + got_away_ref[...].astype(F32)).astype(BF)
    keep_ref[...] = (keep_own_ref[...].astype(F32) + got_own_ref[...].astype(F32)).astype(BF)


def fold(keep, got, upper, deps=()):
    half = keep.shape[0] // 2
    each = min(4, half)
    unit = (each,) + keep.shape[1:]
    count = len(deps)
    away = pl.BlockSpec(unit, lambda i, up: ((1 - up[0]) * (half // each) + i, 0, 0))
    own = pl.BlockSpec(unit, lambda i, up: (up[0] * (half // each) + i, 0, 0))
    out = pl.BlockSpec(unit, lambda i, up: (i, 0, 0))
    shape = jax.ShapeDtypeStruct((half,) + keep.shape[1:], BF)

    def body(*refs):
        fold_kernel(*refs[:5], *refs[5 + count :])

    return pl.pallas_call(
        body,
        grid_spec=pltpu.PrefetchScalarGridSpec(
            num_scalar_prefetch=1,
            grid=(half // each,),
            in_specs=[away, away, own, own] + [any_space() for _ in deps],
            out_specs=[out, out],
        ),
        out_shape=(shape, shape),
        compiler_params=params(VMEM_LIMIT if half >= 8 else SMALL_LIMIT),
        cost_estimate=cost(0, 6 * half * keep[0].size),
        name="fold",
    )(upper, keep, got, keep, got, *deps)


def on_device(
    tokens, grad_out, region_rows, region_cols, ln1_gain, ln1_bias, spec_w1, spec_b1, spec_w2, spec_b2,
    ln2_gain, ln2_bias, w_up, up_bias, w_down, down_bias,
):
    devices = lax.axis_size(AXES[0]) * lax.axis_size(AXES[1])
    count = devices.bit_length() - 1
    me = lax.axis_index(AXES).astype(jnp.int32)
    core = me & 1
    me_one = me.reshape(1)
    feature = tokens.shape[-1]
    block = feature // BLOCKS
    share = ln1_gain.shape[0]
    cells = tokens.shape[1] * tokens.shape[2]
    hidden = w_up.shape[1]
    parts = hidden // feature
    tables = {name: jnp.asarray(value) for name, value in wave_matrices().items()}
    orders = doubling_orders(count)
    places = tuple(places_of(order) for order in orders)
    flat_tokens = tokens.reshape(cells, feature)
    flat_grad = grad_out.reshape(cells, feature)
    fast = devices // 2 == UNITS
    step = lambda value, k: swap(value, devices, (orders[0][k], orders[1][k]))

    padded = lambda v: jnp.pad(v, ((0, 0), (0, LANES - v.shape[1])))
    vectors = (spec_b1, spec_b2, ln1_gain, ln1_bias, ln2_gain, ln2_bias, up_bias, down_bias)
    if fast:
        own_up = w_up.reshape(share, parts, feature).transpose(1, 0, 2)
        unit = chip_unit(own_up, w_down, core, devices)
        bits = (3, 4, 2, 1, 0)
        hop = lambda value, mask: lax.ppermute(value, AXES, [(i, i ^ mask) for i in range(devices)])
        meet = lambda value, bit: hop(value, 1 << bit)
        small = begin_small(spec_w1, spec_w2, vectors)
        made = first(region_rows, region_cols, flat_tokens, tables, 0, 2, deps=(unit, small), tiles=2)
        small = join_rows(small, *(hop(small, mask) for mask in (8, 16, 24)), deps=(made[2],))
        near = join_rows(unit, step(unit, 0), deps=(small,))
        half, normal, mark = first(region_rows, region_cols, flat_tokens, tables, 2, 2, made[:2], deps=(near,), tiles=2)
        small = join_rows(small, *(hop(small, mask) for mask in (4, 2, 6)), deps=(mark,))
        small = join_rows(small, meet(small, 0))
        weights, weight_bits, vector_bits, me_small = small, bits, bits, me_one
        vectors = ()
    else:
        up = lax.all_gather(w_up, AXES, axis=0, tiled=True)
        up = up.reshape(UNITS, feature // UNITS, parts, feature).transpose(0, 2, 1, 3).reshape(UNITS, -1, feature)
        down = lax.all_gather(w_down, AXES, axis=0, tiled=True).reshape(UNITS, -1, feature)
        pieces = tuple(
            jnp.where(core == 0, one, two)[begin : begin + UNITS // 2]
            for one, two in ((up, down), (down, up))
            for begin in (0, UNITS // 2)
        )
        me_one = core.reshape(1)
        me_small = jnp.zeros_like(me_one)
        places = (tuple(range(UNITS)),) * 2
        small = jnp.concatenate([padded(spec_w1), padded(spec_w2)] + [padded(v[None]) for v in vectors])
        small = gather_small(small, me, devices, count)
        weights = small[:, : 4 * share].reshape(devices, 2, 2 * share, LANES).transpose(1, 0, 2, 3)
        weights = weights.reshape(2, 2 * UNITS, -1, LANES).transpose(1, 0, 2, 3).reshape(2 * UNITS, -1, LANES)
        weight_bits, vector_bits = tuple(range(5)), tuple(range(count))
        half, normal, _ = first(region_rows, region_cols, flat_tokens, tables, 0, STEPS)
        vectors = (small[:, 4 * share :].transpose(1, 0, 2).astype(F32),)

    steps = KEPT // GROUP // TAKE
    core_swap = lambda value: swap(value, devices, (0, 0))
    mix1, mix2, wide, long, up_shift = prepare(
        me_small, weights, vectors, feature, hidden, weight_bits, vector_bits
    )
    deps = ()
    if fast:
        near = join_rows(near, step(near, 1), deps=(up_shift,))
        deps = (near,)
    made = mix_first(half, mix1, mix2, wide, long, tables, steps // 2, deps=deps)
    half1, modes1, heads = made[0], made[1:6], made[6:11]
    deps = ()
    if fast:
        beside, across = step(near, 2), step(near, 3)
        other_near = core_swap(near)
        deps = (other_near, heads[4])
    made = mix_second(half, mix1, mix2, wide, long, tables, steps // 2, steps // 2, deps=deps)
    half2, modes2 = made[0], made[1:6]
    if fast:
        beside = hold(beside, (modes2[4],))
        far = step(beside, 3)
        deps = (beside,)
    middle, normed, mark = space(
        region_rows, region_cols, half1, half2, flat_tokens, wide, tables, deps=deps, tiles=2
    )
    if fast:
        far = hold(far, (mark,))
        pieces = (near, beside, across, far, other_near) + tuple(core_swap(v) for v in (beside, across, far))
    active, pre, bias_grad, up_all, down_all, send, keep = feed(
        region_rows, region_cols, me_one, normed, flat_grad, up_shift, pieces, places
    )
    tiles = cells // CELLS
    mixed, grad_middle, half_back, sums_two = feed_down(
        region_rows, region_cols, active, pre, middle, flat_grad, normal, wide, tables["first"], up_all, down_all,
        deps=(send,),
    )
    deps = ()
    if fast:
        ranks = [((me >> jnp.where(core == 0, *bit)) & 1).reshape(1) for bit in zip(*orders)]
        send, keep = fold(keep, swap(send, devices, (0, 0)), ranks[3], deps=(sums_two,))
        deps = (send,)
    half_back, one, two, one_head, two_head, bias_sums = mix_back(
        half_back, modes1, modes2, heads, mix1, mix2, tables, deps=deps
    )
    grad_one = block_grads(modes1[0], modes2[0], heads[0], one, one_head, "grad_mix1")
    if fast:
        send, keep = fold(keep, step(send, 3), ranks[2], deps=(grad_one,))
        deps = (send,)
    grad_two = block_grads(modes1[1], modes2[1], heads[1], two, two_head, "grad_mix2", deps=deps)
    last_args = (region_rows, region_cols, half_back, flat_tokens, grad_middle, wide, tables)
    if fast:
        places_small = [v.reshape(1) for v in (me & 1, (me >> 1) & 3, me >> 3)]
        away, own = pack(places_small[0], grad_one, grad_two, bias_sums, sums_two, bias_grad, wide, devices)
        grad_tokens, mark = last(*last_args, 0, 2, deps=(away,))
        *aways, own = fold_small(own, (hop(away, 1),), places_small[1], 4, deps=(mark,))
        send, keep = fold(keep, step(send, 2), ranks[1], deps=tuple(aways))
        gots = tuple(hop(v, mask) for v, mask in zip(aways, (2, 4, 6)))
        grad_tokens, mark = last(*last_args, 2, 2, (grad_tokens,), deps=(send,))
        *aways, own = fold_small(own, gots, places_small[2], 4, deps=(mark,))
        gots = tuple(hop(v, mask) for v, mask in zip(aways, (8, 16, 24)))
        grad_tokens, mark = last(*last_args, 4, 2, (grad_tokens,), deps=tuple(aways))
        send, keep = fold(keep, step(send, 1), ranks[0], deps=(mark, gots[0]))
        grad_tokens, mark = last(*last_args, 6, 2, (grad_tokens,), deps=(send,))
        widths = (share,) * 5 + (2 * share,) * 2 + (hidden // devices,)
        blocks = end_small(hold(own, (mark,)), gots, 2 * share, block, widths)
        keep = hold(keep, (blocks[0],))
        total = keep[0].astype(F32) + step(send, 0)[0].astype(F32)
        up_sum = total.reshape(parts, 2 * share, feature)
        lower = up_sum[:, :share].reshape(parts * share, feature)
        upper = up_sum[:, share:].reshape(parts * share, feature)
        each = parts * share
        leaving = jnp.where(core == 0, upper, total[:each])
        other = swap(leaving, devices, (0, 0))
        grad_w_up = jnp.where(core == 0, lower, other).reshape(parts, share, feature).transpose(1, 0, 2)
        grad_w_down = jnp.where(core == 0, other, total[each:])
        rows = [v.reshape(-1) for v in blocks[2:]]
        blocks = blocks[:2]
    else:
        scatter = lambda v: lax.psum_scatter(v.astype(F32), AXES, scatter_dimension=0, tiled=True)
        up = jnp.where(core == 0, keep, send).reshape(UNITS, parts, feature // UNITS, feature)
        grad_w_up = scatter(up.transpose(0, 2, 1, 3).reshape(feature, hidden))
        grad_w_down = scatter(jnp.where(core == 0, send, keep).reshape(hidden, feature))
        grad_tokens, _ = last(*last_args, 0, tiles)
        owned = lambda v: jnp.pad(
            v.reshape(v.shape[0], devices, -1).transpose(1, 0, 2), ((0, 0), (0, 0), (0, LANES - v.shape[1] // devices))
        )
        narrow = jnp.concatenate(list(scale_grads(bias_sums, sums_two, wide)) + [sums_two[:3]])
        biases = bias_sums[:2].reshape(2, feature // LANES, 2, LANES).transpose(0, 2, 1, 3).reshape(2, 2 * feature)
        blocks = [v.reshape(devices, 2 * share, LANES) for v in (grad_one, grad_two)]
        packet = jnp.concatenate(blocks + [owned(narrow), owned(biases), owned(bias_grad)], axis=1)
        result = scatter_small(packet, me, devices, count, 8)
        widths = (share,) * 5 + (2 * share,) * 2 + (hidden // devices,)
        rows = [result[4 * share + k, :width] for k, width in enumerate(widths)]
        blocks = [result[k * 2 * share : (k + 1) * 2 * share, :block] for k in range(2)]
    return (
        mixed.reshape(tokens.shape),
        grad_tokens.reshape(tokens.shape),
        rows[0],
        rows[1],
        blocks[0],
        rows[5],
        blocks[1],
        rows[6],
        rows[2],
        rows[3],
        grad_w_up.reshape(share, hidden),
        rows[7],
        grad_w_down,
        rows[4],
    )


def solution(mesh):
    placed = P(AXES)
    return jax.shard_map(
        on_device, mesh=mesh, in_specs=(placed,) * 16, out_specs=(placed,) * 14, check_vma=False
    )
```

```python
import functools
import math

import jax
import jax.numpy as jnp
import numpy as np
from jax import lax
from jax.experimental import pallas as pl
from jax.experimental.pallas import tpu as pltpu
from jax.sharding import PartitionSpec as P

BF = jnp.bfloat16
F32 = jnp.float32
BLOCKS = 8
EPS = 1e-05
SHRINK = 0.01
ROWS = 32
COLS = 64
KEPT = COLS // 2
GROUP = 4
STEPS = ROWS // GROUP
CELLS = GROUP * COLS
MODES = (KEPT + 1) * ROWS
HEAD = (GROUP + 1) * ROWS
BODY = GROUP * ROWS
TAKE = 2
TOOK = TAKE * BODY
LANES = 128
C1 = math.sqrt(2.0 / math.pi)
C3 = 0.044715
SIGMOID = -2.0 * C1 / math.log(2.0)
UNITS = 16
WIDTH = 256
VMEM_LIMIT = 60 * 1024 * 1024
SMALL_LIMIT = 36 * 1024 * 1024
MIDDLE_LIMIT = 50 * 1024 * 1024


def table_parts(values):
    high = values.astype(np.float32).astype(jnp.bfloat16)
    low = (values - high.astype(np.float64)).astype(np.float32).astype(jnp.bfloat16)
    return np.stack([high, low])


def wave_matrices():
    scale = 1.0 / math.sqrt(ROWS * COLS)
    w = np.arange(COLS)
    first = np.zeros((KEPT, 2, GROUP, GROUP, COLS))
    for k in range(KEPT):
        for h in range(GROUP):
            if k == 0:
                first[k, 0, h, h] = scale
                first[k, 1, h, h] = scale * np.where(w % 2 == 0, 1.0, -1.0)
            else:
                first[k, 0, h, h] = scale * np.cos(2 * np.pi * (k * w % COLS) / COLS)
                first[k, 1, h, h] = -scale * np.sin(2 * np.pi * (k * w % COLS) / COLS)
    first = first.reshape(CELLS, CELLS)
    p = np.arange(ROWS)
    turn = 2 * np.pi * (np.outer(p, p) % ROWS) / ROWS
    cos = np.cos(turn).reshape(ROWS, STEPS, GROUP)
    sin = np.sin(turn).reshape(ROWS, STEPS, GROUP)
    body = np.zeros((2, GROUP, ROWS, GROUP, STEPS, 2, GROUP))
    head = np.zeros((2, GROUP + 1, ROWS, GROUP, STEPS, 2, GROUP))
    for k in range(GROUP):
        body[0, k, :, k, :, 0] = cos
        body[0, k, :, k, :, 1] = sin
        body[1, k, :, k, :, 1] = cos
        body[1, k, :, k, :, 0] = -sin
    head[:, 1:GROUP, :, 1:] = body[:, 1:, :, 1:]
    for place, part in ((0, 0), (GROUP, 1)):
        head[0, place, :, 0, :, part] = cos
        head[1, place, :, 0, :, part] = -sin
    weight = np.full((2, GROUP + 1, ROWS, 1), 2.0)
    weight[:, 0] = 1.0
    weight[:, GROUP] = 1.0
    head = head.reshape(2 * HEAD, 2 * BODY)
    body = body.reshape(2 * BODY, 2 * BODY)
    head_weighted = head * weight.reshape(2 * HEAD, 1)
    body_weighted = body * 2.0
    return {
        "first": table_parts(first),
        "first_t": table_parts(first.T),
        "head": table_parts(head),
        "body": table_parts(body),
        "head_t": table_parts(head.T),
        "body_t": table_parts(body.T),
        "head_w": table_parts(head_weighted),
        "body_w": table_parts(body_weighted),
        "head_wt": table_parts(head_weighted.T),
        "body_wt": table_parts(body_weighted.T),
    }


def mm(left, right, dims=(1, 0)):
    return lax.dot_general(
        left, right, (((dims[0],), (dims[1],)), ((), ())), preferred_element_type=F32
    )


def split(values):
    high = values.astype(BF)
    return high, (values - high.astype(F32)).astype(BF)


def turn(table, values):
    high, low = split(values)
    return mm(table[0], high) + mm(table[1], high) + mm(table[0], low)


def turn_once(table, values):
    return mm(table[0], values.astype(BF))


def normalize(values):
    centred = values - jnp.mean(values, axis=-1, keepdims=True)
    inverse = lax.rsqrt(jnp.mean(centred * centred, axis=-1, keepdims=True) + EPS)
    return centred * inverse, inverse


def norm_back(grad, gain, normal, inverse):
    scaled = grad * gain
    return inverse * (
        scaled
        - jnp.mean(scaled, axis=-1, keepdims=True)
        - normal * jnp.mean(scaled * normal, axis=-1, keepdims=True)
    )


def gelu_parts(value):
    square = value * value
    half = 1.0 / (1.0 + jnp.exp2(value * (SIGMOID + (SIGMOID * C3) * square)))
    active = value * half
    slope = half + active * (1.0 - half) * (2.0 * C1 + (6.0 * C1 * C3) * square)
    return active, slope


def live_rows(start, count, rows_ref, cols_ref):
    cell = start + lax.broadcasted_iota(jnp.int32, (count, 1), 0)
    inside = (cell // COLS < rows_ref[0]) & (cell % COLS < cols_ref[0])
    return jnp.where(inside, 1.0, 0.0).astype(F32)


def spread(piece, per_device, me, bits):
    devices = piece.shape[0]
    total = devices * per_device
    lane = lax.broadcasted_iota(jnp.int32, (LANES, total), 0)
    place = lax.broadcasted_iota(jnp.int32, (LANES, total), 1)
    pick = jnp.where(place % per_device == lane, 1.0, 0.0).astype(BF)
    wide = mm(piece.astype(BF), pick)
    row = lax.broadcasted_iota(jnp.int32, (devices, 1), 0)
    owner = jnp.full((devices, 1), me, jnp.int32)
    for k, bit in enumerate(bits):
        owner = owner ^ (((row >> k) & 1) << bit)
    where = lax.broadcasted_iota(jnp.int32, (devices, total), 1) // per_device
    return jnp.sum(jnp.where(owner == where, wide, 0.0), axis=0, keepdims=True)


def place_of(mask, bits):
    return sum(((mask >> bit) & 1) << k for k, bit in enumerate(bits))


MARK = jax.ShapeDtypeStruct((8, LANES), F32)


def any_space():
    return pl.BlockSpec(memory_space=pl.ANY)


def single(shape):
    return pl.BlockSpec(shape, lambda *_: (0,) * len(shape), pipeline_mode=pl.Buffered(1))


def smem():
    return pl.BlockSpec(memory_space=pltpu.SMEM)


def params(limit=VMEM_LIMIT):
    return pltpu.CompilerParams(vmem_limit_bytes=limit)


def cost(flops, moved):
    return pl.CostEstimate(flops=0, bytes_accessed=0, transcendentals=0)


def unread(deps):
    return [pl.BlockSpec(memory_space=pltpu.HBM) if v.shape == MARK.shape else any_space() for v in deps]


def launch(deps, kernel, *, in_specs, **more):
    count = len(in_specs)

    def body(*refs):
        kernel(*refs[:count], *refs[count + len(deps) :])

    call = pl.pallas_call(body, in_specs=list(in_specs) + unread(deps), **more)
    return lambda *operands: call(*operands, *deps)


def to_mixed(real, imag):
    tiles = []
    for at in range(0, real.shape[1], LANES):
        tiles += [real[:, at : at + LANES], imag[:, at : at + LANES]]
    return jnp.concatenate(tiles, axis=1)


def from_mixed(values):
    cut = lambda at: values[:, at : at + LANES]
    real = [cut(at) for at in range(0, values.shape[1], 2 * LANES)]
    imag = [cut(at + LANES) for at in range(0, values.shape[1], 2 * LANES)]
    return jnp.concatenate(real, axis=1), jnp.concatenate(imag, axis=1)


def mix_product(values, matrix_ref, back=False):
    feature = values.shape[1] // 2
    wide = 2 * LANES
    groups = []
    for group in range(2):
        part = values[:, group * feature : (group + 1) * feature]
        count = feature // wide
        for t in range(count):
            begin, end = max(t - 1, 0) * wide, min(t + 2, count) * wide
            here = slice(t * wide, (t + 1) * wide)
            if back:
                groups.append(mm(part[:, begin:end], matrix_ref[group, here, begin:end], (1, 1)))
            else:
                groups.append(mm(part[:, begin:end], matrix_ref[group, begin:end, here]))
    return jnp.concatenate(groups, axis=1)


def first_kernel(begin, rows_ref, cols_ref, tokens_ref, first_ref, *rest):
    half_ref, normal_ref, mark_ref = rest[-3:]
    mark_ref[...] = jnp.zeros_like(mark_ref)
    feature = tokens_ref.shape[1]
    start = (pl.program_id(0) + begin) * tokens_ref.shape[0]
    for k in range(tokens_ref.shape[0] // CELLS):
        here = slice(k * CELLS, (k + 1) * CELLS)
        there = slice(k * 2 * GROUP, (k + 1) * 2 * GROUP)
        normal, _ = normalize(tokens_ref[here, :].astype(F32))
        live = live_rows(start + k * CELLS, CELLS, rows_ref, cols_ref)
        normal = normal * live
        normal_ref[here, :] = normal.astype(BF)
        half_ref[:, there, :feature] = turn(first_ref, normal).reshape(KEPT, 2 * GROUP, feature)
        ones = jnp.broadcast_to(live, (CELLS, LANES)).astype(BF)
        flat = mm(first_ref[0], ones) + mm(first_ref[1], ones)
        half_ref[:, there, feature:] = flat.reshape(KEPT, 2 * GROUP, LANES)


def first(rows, cols, tokens, tables, begin, steps, before=(), deps=(), tiles=1):
    cells, feature = tokens.shape
    table = tables["first"]
    block = pl.BlockSpec((tiles * CELLS, feature), lambda i: (i + begin, 0))
    operands = (rows, cols, tokens, table)
    return launch(
        deps,
        functools.partial(first_kernel, begin),
        grid=(steps,),
        out_shape=(
            jax.ShapeDtypeStruct((KEPT, 2 * ROWS, feature + LANES), F32),
            jax.ShapeDtypeStruct((cells, feature), BF),
            MARK,
        ),
        in_specs=[smem(), smem(), block, single(table.shape)] + [any_space() for _ in before],
        out_specs=(
            pl.BlockSpec((KEPT, 2 * GROUP * tiles, feature + LANES), lambda i: (0, i + begin, 0)),
            block,
            single(MARK.shape),
        ),
        input_output_aliases={len(operands) + k: k for k in range(len(before))},
        compiler_params=params(),
        cost_estimate=cost(6e9, 11e6),
        name="first",
    )(*operands, *before)


def build_mix(me, bits, weights_ref, layer, out_ref, feature):
    block = feature // BLOCKS
    half = feature // 2
    per_group = BLOCKS // 2
    share = 2 * feature // weights_ref.shape[0]
    each = block // share
    out_ref[...] = jnp.zeros_like(out_ref)
    row = lax.broadcasted_iota(jnp.int32, (LANES, half), 0)
    column = lax.broadcasted_iota(jnp.int32, (LANES, half), 1)
    for b in range(per_group):
        shift = jnp.where((column - b * block == row) & (row < block), 1.0, 0.0).astype(BF)
        low, high = b * block, (b + 1) * block
        for group in range(2):
            for part in range(2):
                at = (part * BLOCKS + group * per_group + b) * each
                pieces = [
                    weights_ref[place_of((at + k) ^ me, bits), layer * share : (layer + 1) * share, :]
                    for k in range(each)
                ]
                placed = mm(jnp.concatenate(pieces, axis=0), shift).astype(BF)
                for t in range(low // LANES, (high - 1) // LANES + 1):
                    begin, end = max(low, t * LANES), min(high, (t + 1) * LANES)
                    for c in range(low // LANES, (high - 1) // LANES + 1):
                        piece = placed[begin - low : end - low, c * LANES : (c + 1) * LANES]
                        for up in range(2):
                            top = 2 * t * LANES + up * LANES + begin - t * LANES
                            left = (2 * c + (up ^ part)) * LANES
                            value = -piece if part == 1 and up == 1 else piece
                            here = (group, slice(top, top + end - begin), slice(left, left + LANES))
                            out_ref[here] = out_ref[here] + value


def to_modes(half_ref, head_ref, body_ref, is_head):
    width = half_ref.shape[2]
    real, imag, ends = [], [], ()
    for k in range(TAKE):
        begin = is_head and k == 0
        rows = HEAD if begin else BODY
        spec = turn(head_ref if begin else body_ref, half_ref[k * GROUP : (k + 1) * GROUP].reshape(2 * BODY, width))
        real.append(spec[:BODY])
        imag.append(spec[rows : rows + BODY])
        if begin:
            ends = (spec[BODY:rows], spec[rows + BODY :])
    if is_head:
        real.append(ends[0])
        imag.append(ends[1])
    return jnp.concatenate(real, axis=0), jnp.concatenate(imag, axis=0)


def from_modes(pair_of, head_ref, body_ref, is_head, out_ref, product):
    for k in range(TAKE):
        begin = is_head and k == 0
        parts = []
        for part in pair_of:
            parts.append(part[k * BODY : (k + 1) * BODY])
            if begin:
                parts.append(part[TOOK:])
        result = product(head_ref if begin else body_ref, jnp.concatenate(parts, axis=0))
        out_ref[k * GROUP : (k + 1) * GROUP] = result.reshape(GROUP, 2 * ROWS, result.shape[1])


def mix_step(half_ref, head_ref, body_ref, back_head_ref, back_body_ref, mix1_ref, mix2_ref, wide_ref, long_ref,
             outs, heads, out_ref, is_head):
    feature = out_ref.shape[2]
    specs = to_modes(half_ref, head_ref, body_ref, is_head)
    gain = wide_ref[0:1, :]
    shift = wide_ref[1:2, :]

    def scaled(part):
        flat = jnp.concatenate([part[:, feature:]] * (feature // LANES), axis=1)
        return (part[:, :feature] * gain + flat * shift).astype(BF)

    inside = to_mixed(*(scaled(part) for part in specs))
    active, slope = gelu_parts(mix_product(inside, mix1_ref) + long_ref[0:1, :])
    hidden = active.astype(BF)
    value = mix_product(hidden, mix2_ref) + long_ref[1:2, :]
    bend = jnp.tanh(value / SHRINK)
    flat = jnp.concatenate([part[:, feature:] for part in specs], axis=1)
    for ref, head, kept in zip(outs, heads, (inside, hidden, slope, bend * bend, flat)):
        ref[...] = kept[:TOOK]
        if is_head:
            head[...] = kept[TOOK:]
    from_modes(from_mixed(value - SHRINK * bend), back_head_ref, back_body_ref, is_head, out_ref, turn)


def prepare_kernel(
    weight_bits, vector_bits, me_ref, weights_ref, *rest,
):
    mix1_ref, mix2_ref, wide_ref, long_ref, up_ref, vector_ref = rest[-6:]
    feature = wide_ref.shape[1]
    devices = vector_ref.shape[1]
    share = feature // devices
    me = me_ref[0]
    if len(rest) > 6:
        vector_ref[...] = rest[0][...]
    else:
        rows = weights_ref[:, 4 * share :, :].astype(F32)
        for d in range(devices):
            for k in range(vector_ref.shape[0]):
                vector_ref[k, d : d + 1, :] = rows[d, k : k + 1, :]
    build_mix(me, weight_bits, weights_ref, 0, mix1_ref, feature)
    build_mix(me, weight_bits, weights_ref, 1, mix2_ref, feature)
    wide_ref[...] = jnp.zeros_like(wide_ref)
    long_ref[...] = jnp.zeros_like(long_ref)
    for row, at in enumerate((2, 3, 4, 5, 7)):
        wide_ref[row : row + 1, :] = spread(vector_ref[at], share, me, vector_bits)
    for row in range(2):
        both = spread(vector_ref[row], 2 * share, me, vector_bits)
        long_ref[row : row + 1, :] = to_mixed(both[:, :feature], both[:, feature:])
    up_ref[...] = spread(vector_ref[6], up_ref.shape[1] // devices, me, vector_bits)


def prepare(me, weights, vectors, feature, hidden, weight_bits, vector_bits):
    shapes = (
        jax.ShapeDtypeStruct((2, feature, feature), BF),
        jax.ShapeDtypeStruct((2, feature, feature), BF),
        jax.ShapeDtypeStruct((8, feature), F32),
        jax.ShapeDtypeStruct((8, 2 * feature), F32),
        jax.ShapeDtypeStruct((1, hidden), F32),
    )
    devices = vectors[0].shape[1] if vectors else weights.shape[0]
    return pl.pallas_call(
        functools.partial(prepare_kernel, weight_bits, vector_bits),
        out_shape=shapes,
        in_specs=[smem()] + vmem(1 + len(vectors)),
        out_specs=vmem(len(shapes)),
        scratch_shapes=[pltpu.VMEM((8, devices, LANES), F32)],
        compiler_params=params(),
        cost_estimate=cost(0, 0),
        name="prepare",
    )(me, weights, *vectors)


def mix_first_kernel(
    half_ref, mix1_ref, mix2_ref, wide_ref, long_ref, head_ref, body_ref, back_head_ref, back_body_ref,
    out_ref, *rest,
):
    work = functools.partial(
        mix_step, half_ref, head_ref, body_ref, back_head_ref, back_body_ref, mix1_ref, mix2_ref, wide_ref, long_ref,
        rest[:5], rest[5:], out_ref,
    )

    @pl.when(pl.program_id(0) == 0)
    def _():
        work(True)

    @pl.when(pl.program_id(0) > 0)
    def _():
        work(False)


def mix_second_kernel(
    half_ref, mix1_ref, mix2_ref, wide_ref, long_ref, body_ref, back_body_ref,
    out_ref, *outs,
):
    mix_step(
        half_ref, None, body_ref, None, back_body_ref, mix1_ref, mix2_ref, wide_ref, long_ref,
        outs, (None,) * 5, out_ref, False,
    )


def mode_shapes(rows, feature):
    wide = [jax.ShapeDtypeStruct((rows, 2 * feature), kind) for kind in (BF, BF, F32, F32)]
    return wide + [jax.ShapeDtypeStruct((rows, 2 * LANES), F32)]


def mode_blocks(feature):
    return [pl.BlockSpec((TOOK, width), lambda i: (i, 0)) for width in (2 * feature,) * 4 + (2 * LANES,)]


def half_block(width, begin=0):
    return pl.BlockSpec((TAKE * GROUP, 2 * ROWS, width), lambda i: (i + begin, 0, 0))


def mix_first(half, mix1, mix2, wide, long, tables, steps, deps=()):
    feature = half.shape[2] - LANES
    fixed = (mix1, mix2, wide, long, tables["head"], tables["body"], tables["head_wt"], tables["body_wt"])
    heads = mode_shapes(ROWS, feature)
    return launch(
        deps,
        mix_first_kernel,
        grid=(steps,),
        out_shape=[jax.ShapeDtypeStruct((TAKE * GROUP * steps, 2 * ROWS, feature), F32)]
        + mode_shapes(TOOK * steps, feature) + heads,
        in_specs=[half_block(feature + LANES)] + [single(v.shape) for v in fixed],
        out_specs=[half_block(feature)] + mode_blocks(feature) + [single(v.shape) for v in heads],
        compiler_params=params(),
        cost_estimate=cost(9e9, 20e6),
        name="mix_first",
    )(half, *fixed)


def mix_second(half, mix1, mix2, wide, long, tables, begin, steps, deps=()):
    feature = half.shape[2] - LANES
    fixed = (mix1, mix2, wide, long, tables["body"], tables["body_wt"])
    return launch(
        deps,
        mix_second_kernel,
        grid=(steps,),
        out_shape=[jax.ShapeDtypeStruct((TAKE * GROUP * steps, 2 * ROWS, feature), F32)] + mode_shapes(TOOK * steps, feature),
        in_specs=[half_block(feature + LANES, begin)] + [single(v.shape) for v in fixed],
        out_specs=[half_block(feature)] + mode_blocks(feature),
        compiler_params=params(),
        cost_estimate=cost(9e9, 20e6),
        name="mix_second",
    )(half, *fixed)


def space_kernel(rows_ref, cols_ref, half1_ref, half2_ref, tokens_ref, first_t_ref, wide_ref, middle_ref, normed_ref, mark_ref):
    mark_ref[...] = jnp.zeros_like(mark_ref)
    feature = tokens_ref.shape[1]
    start = pl.program_id(0) * tokens_ref.shape[0]
    for k in range(tokens_ref.shape[0] // CELLS):
        here = slice(k * CELLS, (k + 1) * CELLS)
        flat = lambda ref: ref[:, k * 2 * GROUP : (k + 1) * 2 * GROUP, :].reshape(-1, feature)
        spatial = turn(first_t_ref, jnp.concatenate([flat(half1_ref), flat(half2_ref)], axis=0))
        inputs = tokens_ref[here, :].astype(F32)
        live = live_rows(start + k * CELLS, CELLS, rows_ref, cols_ref)
        normal, _ = normalize(inputs)
        middle = inputs + live * (spatial + (normal * wide_ref[0:1, :] + wide_ref[1:2, :]))
        middle_ref[here, :] = middle
        normal, _ = normalize(middle)
        normed_ref[here, :] = (normal * wide_ref[2:3, :] + wide_ref[3:4, :]).astype(BF)


def column_block(rows, width, tiles=1):
    return pl.BlockSpec((rows, 2 * GROUP * tiles, width), lambda i: (0, i, 0))


def space(rows, cols, half1, half2, tokens, wide, tables, deps=(), tiles=1):
    cells, feature = tokens.shape
    table = tables["first_t"]
    block = pl.BlockSpec((tiles * CELLS, feature), lambda i: (i, 0))
    return launch(
        deps,
        space_kernel,
        grid=(STEPS // tiles,),
        out_shape=(jax.ShapeDtypeStruct((cells, feature), F32), jax.ShapeDtypeStruct((cells, feature), BF), MARK),
        in_specs=[smem(), smem(), column_block(half1.shape[0], feature, tiles), column_block(half2.shape[0], feature, tiles),
                  block, single(table.shape), single(wide.shape)],
        out_specs=(block, block, single(MARK.shape)),
        compiler_params=params(),
        cost_estimate=cost(6e9, 20e6),
        name="space",
    )(rows, cols, half1, half2, tokens, table, wide)


def fetch_weights(me_ref, pieces, places, up_ref, down_ref, sems):
    each = pieces[0].shape[0]
    held = len(pieces) // 2
    count = each * held
    chip = me_ref[0] // 2

    def copies(own, core):
        target = (up_ref, down_ref)[core]
        source = pieces[:held] if own else pieces[held:]
        for mask in range(count):
            at = places[core][mask]
            part = source[at // each].at[at % each]
            yield pltpu.make_async_copy(part, target.at[chip ^ mask], sems.at[core, mask])

    for core in range(2):
        @pl.when(me_ref[0] % 2 == core)
        def _():
            for copy in copies(True, core):
                copy.start()
            for copy in copies(False, 1 - core):
                copy.start()

    def arrived(core):
        for copy in copies(True, core):
            copy.wait()

    return arrived


def up_lanes(up_ref, j, begin, count, feature):
    share = up_ref.shape[1] * feature // (up_ref.shape[0] * up_ref.shape[1])
    return up_ref[:, j * share : (j + 1) * share, begin : begin + count].reshape(feature, count)


def down_rows(down_ref, begin, count):
    share = down_ref.shape[1]
    pieces = []
    at = begin
    while at < begin + count:
        unit, first_row = divmod(at, share)
        last_row = min(share, first_row + begin + count - at)
        pieces.append(down_ref[unit, first_row:last_row, :])
        at += last_row - first_row
    return jnp.concatenate(pieces, axis=0)


def weight_scratch(pieces):
    chips, rows, feature = UNITS, pieces[0].shape[1], pieces[0].shape[2]
    return [
        pltpu.VMEM((chips, rows, feature), BF),
        pltpu.VMEM((chips, rows, feature), BF),
        pltpu.SemaphoreType.DMA((2, chips)),
    ]


def up_part(up_ref, j, feature):
    share = up_ref.shape[1] * feature // (up_ref.shape[0] * up_ref.shape[1])
    return up_ref[:, j * share : (j + 1) * share, :].reshape(feature, feature)


def down_part(down_ref, j, feature):
    share = down_ref.shape[1]
    each = feature // share
    return down_ref[j * each : (j + 1) * each].reshape(feature, feature)


def feed_kernel(places, rows_ref, cols_ref, me_ref, normed_in_ref, grad_ref, bias_ref, *rest):
    pieces = rest[:-17]
    (
        active_all_ref, pre_all_ref, bias_grad_ref, up_all_ref, down_all_ref, send_ref, keep_ref,
        active_ref, pre_ref, normed_ref, branch_ref, up_ref, down_ref, sems, weight_sems, row_sems, grad_sems,
    ) = rest[-17:]
    tile, feature = normed_in_ref.shape
    cells, hidden = active_ref.shape
    tiles = cells // tile
    parts = hidden // feature
    chips, share, _ = up_ref.shape
    each = chips // parts
    small = share // parts
    step = pl.program_id(0)
    mine = pl.ds(pl.multiple_of(jnp.minimum(step, tiles - 1) * tile, tile), tile)
    copies = [
        pltpu.make_async_copy(source, target, weight_sems.at[k])
        for k, (source, target) in enumerate(((up_ref, up_all_ref), (down_ref, down_all_ref)))
    ]

    def row_copies(k):
        here = pl.ds(k * tile, tile)
        return (
            pltpu.make_async_copy(active_ref.at[here], active_all_ref.at[here], row_sems.at[0, k]),
            pltpu.make_async_copy(pre_ref.at[here], pre_all_ref.at[here], row_sems.at[1, k]),
        )

    def work(arrived):
        live = live_rows(step * tile, tile, rows_ref, cols_ref)
        branch = (grad_ref[...].astype(F32) * live).astype(BF)
        branch_ref[mine, :] = branch
        normed = normed_in_ref[...]
        normed_ref[mine, :] = normed
        if arrived:
            arrived(0)
            copies[0].start()
        for begin in range(0, hidden, WIDTH):
            place = slice(begin, begin + WIDTH)
            j, lane = divmod(begin, feature)
            value = mm(normed, up_lanes(up_ref, j, lane, WIDTH, feature)) + bias_ref[:, place]
            if arrived and begin == 0:
                arrived(1)
                copies[1].start()
            grad = mm(branch, down_rows(down_ref, begin, WIDTH), (1, 1))
            active, slope = gelu_parts(value)
            active_ref[mine, place] = active.astype(BF)
            grad = grad * slope
            pre_ref[mine, place] = grad.astype(BF)
            bias_grad_ref[:, place] += jnp.sum(grad, axis=0, keepdims=True)

    @pl.when(step == 0)
    def _():
        bias_grad_ref[...] = jnp.zeros_like(bias_grad_ref)
        work(fetch_weights(me_ref, pieces, places, up_ref, down_ref, sems))

    @pl.when((step > 0) & (step < tiles))
    def _():
        work(None)

    for k in range(tiles):
        @pl.when(step == k)
        def _():
            for copy in row_copies(k):
                copy.start()

    def down_copies(j, target):
        for k in range(each):
            yield pltpu.make_async_copy(up_ref.at[j * each + k], target.at[places[1][j * each + k]], grad_sems.at[j, k])

    def up_copies(j, target):
        for k in range(chips):
            source = down_ref.at[j * each + k // each, pl.ds(k % each * small, small)]
            there = target.at[places[0][k], pl.ds(j * small, small)]
            yield pltpu.make_async_copy(source, there, grad_sems.at[parts + j, k])

    @pl.when(step == tiles)
    def _():
        for copy in copies:
            copy.wait()

    @pl.when((step >= tiles) & (step < tiles + parts))
    def _():
        j = step - tiles
        for k in range(each // 2):
            lanes = pl.ds(pl.multiple_of(j * feature + k * 2 * share, LANES), 2 * share)
            piece = mm(active_ref[:, lanes], branch_ref[...], (0, 0)).astype(BF)
            up_ref[pl.ds(j * each + 2 * k, 2)] = piece.reshape(2, share, feature)

    @pl.when(step >= tiles + parts)
    def _():
        j = step - tiles - parts
        lanes = pl.ds(pl.multiple_of(j * feature, LANES), feature)
        for k in range(each // 2):
            piece = mm(normed_ref[:, k * 2 * share : (k + 1) * 2 * share], pre_ref[:, lanes], (0, 0)).astype(BF)
            down_ref[pl.ds(j * each + 2 * k, 2)] = piece.reshape(2, share, feature)

    for j in range(parts):
        for core in range(2):
            targets = (send_ref, keep_ref) if core == 0 else (keep_ref, send_ref)

            @pl.when((step == tiles + j) & (me_ref[0] % 2 == core))
            def _():
                for copy in down_copies(j, targets[0]):
                    copy.start()

            @pl.when((step == tiles + parts + j) & (me_ref[0] % 2 == core))
            def _():
                for copy in up_copies(j, targets[1]):
                    copy.start()

    @pl.when(step == tiles + 2 * parts - 1)
    def _():
        for k in range(tiles):
            for copy in row_copies(k):
                copy.wait()
        for j in range(parts):
            for copy in down_copies(j, send_ref):
                copy.wait()
            for copy in up_copies(j, send_ref):
                copy.wait()


def feed(rows, cols, me, normed, grad, bias, pieces, places, tile=256, deps=()):
    cells, feature = normed.shape
    hidden = bias.shape[1]
    tiles, parts = cells // tile, hidden // feature
    block = pl.BlockSpec((tile, feature), lambda i: (jnp.minimum(i, tiles - 1), 0))
    weights = jax.ShapeDtypeStruct((UNITS,) + pieces[0].shape[1:], BF)
    rows_shape = jax.ShapeDtypeStruct((cells, hidden), BF)
    return launch(
        deps,
        functools.partial(feed_kernel, places),
        grid=(tiles + 2 * parts,),
        out_shape=(rows_shape, rows_shape, jax.ShapeDtypeStruct((1, hidden), F32)) + (weights,) * 4,
        in_specs=[smem(), smem(), smem(), block, block, single(bias.shape)] + [any_space() for _ in pieces],
        out_specs=(any_space(), any_space(), single((1, hidden))) + (any_space(),) * 4,
        scratch_shapes=[
            pltpu.VMEM((cells, hidden), BF),
            pltpu.VMEM((cells, hidden), BF),
            pltpu.VMEM((cells, feature), BF),
            pltpu.VMEM((cells, feature), BF),
            *weight_scratch(pieces),
            pltpu.SemaphoreType.DMA((2,)),
            pltpu.SemaphoreType.DMA((2, tiles)),
            pltpu.SemaphoreType.DMA((2 * parts, UNITS)),
        ],
        compiler_params=params(),
        cost_estimate=cost(0, 0),
        name="feed",
    )(rows, cols, me, normed, grad, bias, *pieces)


def down_kernel(rows_ref, cols_ref, active_ref, pre_ref, middle_ref, grad_ref, normal_ref, wide_ref, first_ref,
                up_ref, down_ref, mixed_ref, grad_middle_ref, half_ref, sums_ref):
    tile, feature = middle_ref.shape
    hidden = active_ref.shape[1]
    step = pl.program_id(0)

    @pl.when(step == 0)
    def _():
        sums_ref[...] = jnp.zeros_like(sums_ref)

    live = live_rows(step * tile, tile, rows_ref, cols_ref)
    branch = mm(active_ref[...], down_ref[...].reshape(hidden, feature))
    up = jnp.concatenate([up_part(up_ref, j, feature) for j in range(hidden // feature)], axis=1)
    grad_normed = mm(pre_ref[...], up, (1, 1))
    middle = middle_ref[...]
    mixed_ref[...] = (middle + live * (branch + wide_ref[4:5, :])).astype(BF)
    normal, inverse = normalize(middle)
    cotangent = grad_ref[...].astype(F32)
    grad_middle = cotangent + norm_back(grad_normed, wide_ref[2:3, :], normal, inverse)
    grad_middle_ref[...] = grad_middle
    masked = grad_middle * live
    half_ref[...] = turn(first_ref, masked).reshape(half_ref.shape)
    rows = (grad_normed * normal, grad_normed, cotangent * live, masked * normal_ref[...].astype(F32), masked)
    for row, value in enumerate(rows):
        sums_ref[row : row + 1, :] += jnp.sum(value, axis=0, keepdims=True)


def feed_down(rows, cols, active, pre, middle, grad, normal, wide, table, up, down, deps=()):
    cells, feature = middle.shape
    hidden = active.shape[1]
    block = lambda width: pl.BlockSpec((CELLS, width), lambda i: (i, 0))
    operands = (rows, cols, active, pre, middle, grad, normal, wide, table, up, down)
    return launch(
        deps,
        down_kernel,
        grid=(cells // CELLS,),
        out_shape=(
            jax.ShapeDtypeStruct((cells, feature), BF),
            jax.ShapeDtypeStruct((cells, feature), F32),
            jax.ShapeDtypeStruct((KEPT, 2 * ROWS, feature), F32),
            jax.ShapeDtypeStruct((8, feature), F32),
        ),
        in_specs=[smem(), smem(), block(hidden), block(hidden), block(feature), block(feature), block(feature)]
        + [single(v.shape) for v in operands[7:]],
        out_specs=(block(feature), block(feature), column_block(KEPT, feature), single((8, feature))),
        compiler_params=params(),
        cost_estimate=cost(0, 0),
        name="feed_down",
    )(*operands)


def back_step(half_ref, head_ref, body_ref, back_head_ref, back_body_ref, mix1_ref, mix2_ref, ins, in_heads,
              outs, out_heads, out_ref, sums_ref, is_head):
    feature = out_ref.shape[2]

    def read(k):
        if is_head:
            return jnp.concatenate([ins[k][...], in_heads[k][...]], axis=0)
        return ins[k][...]

    grads = to_modes(half_ref, head_ref, body_ref, is_head)
    grad_two = (to_mixed(*grads) * read(1)).astype(BF)
    grad_one = (mix_product(grad_two, mix2_ref, True) * read(0)).astype(BF)
    grad_spec = mix_product(grad_one, mix1_ref, True)
    from_modes(from_mixed(grad_spec), back_head_ref, back_body_ref, is_head, out_ref, turn_once)
    for row, value in enumerate((grad_one, grad_two)):
        outs[row][...] = value[:TOOK]
        if is_head:
            out_heads[row][...] = value[TOOK:]
    flat = jnp.concatenate([read(3)] * (feature // LANES), axis=1)
    for row, value in enumerate((grad_one.astype(F32), grad_two.astype(F32), grad_spec * read(2).astype(F32), grad_spec * flat)):
        total = jnp.sum(value, axis=0, keepdims=True)
        sums_ref[row : row + 1, :] = total if is_head else sums_ref[row : row + 1, :] + total


def mix_back_kernel(
    half_ref, slope1_ref, slope2_ref, bend1_ref, bend2_ref, low1_ref, low2_ref, flat1_ref, flat2_ref,
    slope_head_ref, bend_head_ref, low_head_ref, flat_head_ref, mix1_ref, mix2_ref,
    head_ref, body_ref, back_head_ref, back_body_ref,
    out_ref, one_ref, two_ref, one_head_ref, two_head_ref, sums_ref,
):
    step = pl.program_id(0)
    steps = pl.num_programs(0) // 2
    work = functools.partial(
        back_step, half_ref, head_ref, body_ref, back_head_ref, back_body_ref, mix1_ref, mix2_ref
    )
    heads = (slope_head_ref, bend_head_ref, low_head_ref, flat_head_ref)
    more = (heads, (one_ref, two_ref), (one_head_ref, two_head_ref), out_ref, sums_ref)
    near = (slope1_ref, bend1_ref, low1_ref, flat1_ref)
    far = (slope2_ref, bend2_ref, low2_ref, flat2_ref)

    @pl.when(step == 0)
    def _():
        sums_ref[...] = jnp.zeros_like(sums_ref)
        work(near, *more, True)

    @pl.when((step > 0) & (step < steps))
    def _():
        work(near, *more, False)

    @pl.when(step >= steps)
    def _():
        work(far, *more, False)


def mix_back(half, modes1, modes2, heads, mix1, mix2, tables, deps=()):
    feature = half.shape[2]
    steps = KEPT // GROUP // TAKE
    fixed = tuple(heads[k] for k in (2, 3, 0, 4)) + (
        mix1, mix2, tables["head_w"], tables["body_w"], tables["head_t"], tables["body_t"]
    )
    moving = []
    specs = []
    for k in (2, 3, 0, 4):
        width = modes1[k].shape[1]
        moving += [modes1[k], modes2[k]]
        specs += [
            pl.BlockSpec((TOOK, width), lambda i: (jnp.minimum(i, steps // 2 - 1), 0)),
            pl.BlockSpec((TOOK, width), lambda i: (jnp.maximum(i - steps // 2, 0), 0)),
        ]
    low = lambda rows: jax.ShapeDtypeStruct((rows, 2 * feature), BF)
    body = pl.BlockSpec((TOOK, 2 * feature), lambda i: (i, 0))
    shapes = (
        jax.ShapeDtypeStruct((KEPT, 2 * ROWS, feature), F32), low(TOOK * steps), low(TOOK * steps),
        low(ROWS), low(ROWS), jax.ShapeDtypeStruct((8, 2 * feature), F32),
    )
    return launch(
        deps,
        mix_back_kernel,
        grid=(steps,),
        out_shape=shapes,
        in_specs=[half_block(feature)] + specs + [single(v.shape) for v in fixed],
        out_specs=[half_block(feature), body, body] + [single(v.shape) for v in shapes[3:]],
        compiler_params=params(),
        cost_estimate=cost(18e9, 30e6),
        name="mix_back",
    )(half, *moving, *fixed)


def block_kernel(left1_ref, left2_ref, left_head_ref, right_ref, right_head_ref, out_ref, natural_ref):
    wide = 2 * LANES
    count = left1_ref.shape[1] // wide
    cut = left1_ref.shape[0]
    for t in range(count):
        for c in range(max(t - 1, 0), min(t + 2, count)):
            left, right = slice(t * wide, (t + 1) * wide), slice(c * wide, (c + 1) * wide)
            total = (
                mm(left1_ref[:, left], right_ref[:cut, right], (0, 0))
                + mm(left2_ref[:, left], right_ref[cut:, right], (0, 0))
                + mm(left_head_ref[:, left], right_head_ref[:, right], (0, 0))
            )
            rows, lanes = slice(t * LANES, (t + 1) * LANES), slice(c * LANES, (c + 1) * LANES)
            natural_ref[0, rows, lanes] = total[:LANES, :LANES] + total[LANES:, LANES:]
            natural_ref[1, rows, lanes] = total[:LANES, LANES:] - total[LANES:, :LANES]
    per_group = BLOCKS // 2
    block = count * LANES // per_group
    for b in range(per_group):
        begin = b * block
        base = begin // LANES * LANES
        reach = min(base + wide, count * LANES) - base
        for part in range(2):
            piece = natural_ref[part, begin : begin + block, base : base + reach]
            if begin > base:
                piece = pltpu.roll(piece, reach - (begin - base), axis=1)
            out_ref[part, b * block : (b + 1) * block, :] = piece[:, :LANES]


def block_grads(left1, left2, left_head, right, right_head, name, deps=()):
    feature = left1.shape[1] // 2
    half = feature // 2
    block = lambda v: pl.BlockSpec((v.shape[0], feature), lambda i: (0, i))
    return launch(
        deps,
        block_kernel,
        grid=(2,),
        out_shape=jax.ShapeDtypeStruct((2, feature, LANES), F32),
        in_specs=[block(v) for v in (left1, left2, left_head, right, right_head)],
        out_specs=pl.BlockSpec((2, half, LANES), lambda i: (0, i, 0)),
        scratch_shapes=[pltpu.VMEM((2, half, half), F32)],
        compiler_params=params(MIDDLE_LIMIT),
        cost_estimate=cost(5e9, 7e6),
        name=name,
    )(left1, left2, left_head, right, right_head)


def last_kernel(begin, rows_ref, cols_ref, half_ref, tokens_ref, grad_ref, first_t_ref, wide_ref, *rest):
    out_ref, mark_ref = rest[-2:]
    mark_ref[...] = jnp.zeros_like(mark_ref)
    tile, feature = tokens_ref.shape
    live = live_rows((pl.program_id(0) + begin) * tile, tile, rows_ref, cols_ref)
    grad_middle = grad_ref[...]
    grad_normed = live * (grad_middle + turn_once(first_t_ref, half_ref[...].reshape(CELLS, feature)))
    normal, inverse = normalize(tokens_ref[...].astype(F32))
    out_ref[...] = grad_middle + norm_back(grad_normed, wide_ref[0:1, :], normal, inverse)


def last(rows, cols, half, tokens, grad, wide, tables, begin, steps, before=(), deps=()):
    cells, feature = tokens.shape
    first_t = tables["first_t"]
    block = pl.BlockSpec((CELLS, feature), lambda i: (i + begin, 0))
    operands = (rows, cols, half, tokens, grad, first_t, wide)
    return launch(
        deps,
        functools.partial(last_kernel, begin),
        grid=(steps,),
        out_shape=(jax.ShapeDtypeStruct((cells, feature), F32), MARK),
        in_specs=[smem(), smem(), pl.BlockSpec((KEPT, 2 * GROUP, feature), lambda i: (0, i + begin, 0)), block, block,
                  single(first_t.shape), single(wide.shape)] + [any_space() for _ in before],
        out_specs=(block, single(MARK.shape)),
        input_output_aliases={len(operands): 0} if before else {},
        compiler_params=params(),
        cost_estimate=cost(6e9, 20e6),
        name="last",
    )(*operands, *before)


def collect(value, per_device, devices):
    total = value.shape[1]
    owner = lax.broadcasted_iota(jnp.int32, (devices, total), 1) // per_device
    row = lax.broadcasted_iota(jnp.int32, (devices, total), 0)
    high, low = split(jnp.where(owner == row, jnp.broadcast_to(value, (devices, total)), 0.0))
    place = lax.broadcasted_iota(jnp.int32, (total, LANES), 0)
    lane = lax.broadcasted_iota(jnp.int32, (total, LANES), 1)
    pick = jnp.where(place % per_device == lane, 1.0, 0.0).astype(BF)
    return mm(high, pick) + mm(low, pick)


def emit(place, sum_ref, send_refs, keep_ref):
    half, _, rows, _ = sum_ref.shape
    rows = rows - 8
    for k, send_ref in enumerate(send_refs):
        away = sum_ref[:, pl.ds(place ^ (k + 1), 1)].reshape(half, rows + 8, LANES)
        high, low = split(away[:, rows:])
        send_ref[:, :rows] = away[:, :rows].astype(BF)
        send_ref[:, rows:] = jnp.concatenate([high.astype(F32), low.astype(F32)], axis=1).astype(BF)
    keep_ref[...] = sum_ref[:, pl.ds(place, 1)].reshape(half, rows + 8, LANES)


def pack_kernel(place_ref, one_ref, two_ref, mixed_ref, sums_ref, up_ref, wide_ref, send_ref, keep_ref, sum_ref):
    half, _, rows, _ = sum_ref.shape
    devices = 2 * half
    share = (rows - 8) // 4
    feature = sums_ref.shape[1]
    sum_ref[:, :, : 2 * share] = one_ref[...].reshape(half, 2, 2 * share, LANES)
    sum_ref[:, :, 2 * share : 4 * share] = two_ref[...].reshape(half, 2, 2 * share, LANES)
    first_gain, first_bias = scale_grads(mixed_ref, sums_ref, wide_ref)
    natural = [jnp.concatenate(from_mixed(mixed_ref[k : k + 1, :]), axis=1) for k in range(2)]
    narrow = [first_gain, first_bias] + [sums_ref[k : k + 1, :] for k in range(3)]
    for k, value in enumerate(narrow + natural + [up_ref[...]]):
        placed = collect(value, value.shape[1] // devices, devices)
        for d in range(devices):
            sum_ref[d // 2, d % 2, 4 * share + k : 4 * share + k + 1, :] = placed[d : d + 1, :]
    emit(place_ref[0], sum_ref, (send_ref,), keep_ref)


def scale_grads(mixed_ref, sums_ref, wide_ref):
    real, imag = from_mixed(mixed_ref[2:3, :])
    scaled = real + imag
    real, imag = from_mixed(mixed_ref[3:4, :])
    flat = real + imag
    gain = sums_ref[3:4, :] + (scaled - wide_ref[1:2, :] * flat) / wide_ref[0:1, :]
    return gain, sums_ref[4:5, :] + flat


def small_shapes(half, rows, others):
    shapes = [jax.ShapeDtypeStruct((half, rows + 8, LANES), BF)] * others
    return shapes + [jax.ShapeDtypeStruct((half, rows, LANES), F32)]


def pack(upper, one, two, mixed, sums, up, wide, devices):
    rows = 2 * one.shape[0] * one.shape[1] // devices + 8
    shapes = small_shapes(devices // 2, rows, 1)
    operands = (one, two, mixed, sums, up, wide)
    return pl.pallas_call(
        pack_kernel,
        out_shape=shapes,
        in_specs=[smem()] + vmem(len(operands)),
        out_specs=vmem(2),
        scratch_shapes=[pltpu.VMEM((devices // 2, 2, rows, LANES), F32)],
        compiler_params=params(MIDDLE_LIMIT),
        cost_estimate=cost(0, 0),
        name="pack",
    )(upper, *operands)


def merge_small(keep_ref, got_refs):
    rows = keep_ref.shape[1] - 8
    top, tail = keep_ref[:, :rows], keep_ref[:, rows:]
    for got_ref in got_refs:
        both = got_ref[:, rows:].astype(F32)
        top = top + got_ref[:, :rows].astype(F32)
        tail = tail + (both[:, :8] + both[:, 8:])
    return top, tail


def fold_small_kernel(others, place_ref, keep_ref, *rest):
    sum_ref = rest[-1]
    send_refs, out_ref = rest[-2 - others : -2], rest[-2]
    half, count, rows, _ = sum_ref.shape
    top, tail = merge_small(keep_ref, rest[: len(rest) - 2 - others])
    sum_ref[:, :, : rows - 8] = top.reshape(half, count, rows - 8, LANES)
    sum_ref[:, :, rows - 8 :] = tail.reshape(half, count, 8, LANES)
    emit(place_ref[0], sum_ref, send_refs, out_ref)


def fold_small(keep, got, place, count, deps=()):
    half, rows = keep.shape[0] // count, keep.shape[1]
    shapes = small_shapes(half, rows, count - 1)
    return launch(
        deps,
        functools.partial(fold_small_kernel, count - 1),
        out_shape=shapes,
        in_specs=[smem()] + vmem(1 + len(got)),
        out_specs=vmem(len(shapes)),
        scratch_shapes=[pltpu.VMEM((half, count, rows, LANES), F32)],
        compiler_params=params(SMALL_LIMIT),
        cost_estimate=cost(0, 0),
        name="fold_small",
    )(place, keep, *got)


def vmem(count):
    return [pl.BlockSpec(memory_space=pltpu.VMEM)] * count


def end_small_kernel(others, keep_ref, *rest):
    got_refs, (one_ref, two_ref, *rows_refs) = rest[:others], rest[others:]
    top, tail = merge_small(keep_ref, got_refs)
    share, block = one_ref.shape
    one_ref[...] = top[0, :share, :block]
    two_ref[...] = top[0, share:, :block]
    for row, ref in enumerate(rows_refs):
        ref[...] = tail[0, row : row + 1, : ref.shape[1]]


def end_small(keep, got, share, block, widths):
    shapes = [jax.ShapeDtypeStruct((share, block), F32)] * 2
    shapes += [jax.ShapeDtypeStruct((1, width), F32) for width in widths]
    return pl.pallas_call(
        functools.partial(end_small_kernel, len(got)),
        out_shape=shapes,
        in_specs=vmem(1 + len(got)),
        out_specs=vmem(len(shapes)),
        compiler_params=params(SMALL_LIMIT),
        cost_estimate=cost(0, 0),
        name="end_small",
    )(keep, *got)


def begin_small_kernel(one_ref, two_ref, *rest):
    out_ref, rows_ref = rest[-2:]
    share, block = one_ref.shape
    out_ref[...] = jnp.zeros_like(out_ref)
    rows_ref[...] = jnp.zeros_like(rows_ref)
    out_ref[0, :share, :block] = one_ref[...]
    out_ref[0, share : 2 * share, :block] = two_ref[...]
    for row, ref in enumerate(rest[:-2]):
        rows_ref[row : row + 1, : ref.shape[1]] = ref[...].astype(F32)
    out_ref[0, 2 * share :, :] = rows_ref[...].astype(BF)


def begin_small(one, two, vectors):
    share = one.shape[0]
    operands = (one, two) + tuple(v[None] for v in vectors)
    return pl.pallas_call(
        begin_small_kernel,
        out_shape=jax.ShapeDtypeStruct((1, 2 * share + 16, LANES), BF),
        in_specs=vmem(len(operands)),
        out_specs=vmem(1)[0],
        scratch_shapes=[pltpu.VMEM((16, LANES), F32)],
        compiler_params=params(),
        cost_estimate=cost(0, 0),
        name="begin_small",
    )(*operands)


AXES = ("dp", "fsdp")


def swap(value, devices, bits):
    return lax.ppermute(value, AXES, [(i, i ^ (1 << bits[i & 1])) for i in range(devices)])


def doubling_orders(count):
    first = list(range(count - 1, 0, -1))
    second = list(first)
    for k in range(0, len(second) - 1, 2):
        second[k], second[k + 1] = second[k + 1], second[k]
    return first, second


def places_of(order):
    return [
        sum(1 << k for k, bit in enumerate(order) if mask >> (bit - 1) & 1) for mask in range(1 << len(order))
    ]


def join_kernel(*refs):
    out_ref = refs[-1]
    count = refs[0].shape[0]
    for k, ref in enumerate(refs[:-1]):
        out_ref[k * count : (k + 1) * count] = ref[...]


def join_rows(*pieces, deps=()):
    shape = jax.ShapeDtypeStruct((len(pieces) * pieces[0].shape[0],) + pieces[0].shape[1:], pieces[0].dtype)
    return launch(
        deps,
        join_kernel,
        out_shape=shape,
        in_specs=[pl.BlockSpec(memory_space=pltpu.VMEM) for _ in pieces],
        out_specs=pl.BlockSpec(memory_space=pltpu.VMEM),
        compiler_params=params(SMALL_LIMIT),
        cost_estimate=cost(0, 0),
        name="join",
    )(*pieces)


def hold(value, deps):
    def body(*refs):
        pass

    return pl.pallas_call(
        body,
        out_shape=jax.ShapeDtypeStruct(value.shape, value.dtype),
        in_specs=[any_space()] + unread(deps),
        out_specs=any_space(),
        input_output_aliases={0: 0},
        compiler_params=params(SMALL_LIMIT),
        cost_estimate=cost(0, 0),
        name="hold",
    )(value, *deps)


def gather_small(value, me, devices, count):
    held = value[None]
    for bit in list(range(3, count)) + [2, 1, 0]:
        other = swap(held, devices, (bit, bit))
        upper = (me >> bit) & 1
        axis = 0 if bit > 2 else 1
        join_two = lambda a, b: jnp.stack([a, b], axis=axis).reshape((-1,) + value.shape)
        held = jnp.where(upper == 0, join_two(held, other), join_two(other, held))
    return held


def scatter_small(value, me, devices, count, exact):
    shape = value.shape[1:]
    rows = shape[0]
    total = value
    for bit in [0, 1, 2] + list(range(count - 1, 2, -1)):
        upper = (me >> bit) & 1
        axis = 0 if bit > 2 else 1
        pair = total.reshape(((2, -1) if bit > 2 else (-1, 2)) + shape)
        away = lax.dynamic_index_in_dim(pair, 1 - upper, axis, keepdims=False)
        keep = lax.dynamic_index_in_dim(pair, upper, axis, keepdims=False)
        sums = away[:, rows - exact :]
        top = lax.reduce_precision(sums, 8, 7)
        packet = jnp.concatenate([away[:, : rows - exact], top, sums - top], axis=1).astype(BF)
        got = swap(packet, devices, (bit, bit)).astype(F32)
        low = got[:, rows - exact : rows] + got[:, rows:]
        total = keep + jnp.concatenate([got[:, : rows - exact], low], axis=1)
    return total[0]


def chip_unit(up, down, core, devices):
    parts, share, feature = up.shape
    flat = up.reshape(parts * share, feature)
    other = swap(jnp.where(core == 0, down, flat), devices, (0, 0))
    up_unit = jnp.concatenate([up, other.reshape(up.shape)], axis=1).reshape(2 * parts * share, feature)
    return jnp.where(core == 0, up_unit, jnp.concatenate([other, down]))[None]


def fold_kernel(upper_ref, keep_away_ref, got_away_ref, keep_own_ref, got_own_ref, send_ref, keep_ref):
    send_ref[...] = (keep_away_ref[...].astype(F32) + got_away_ref[...].astype(F32)).astype(BF)
    keep_ref[...] = (keep_own_ref[...].astype(F32) + got_own_ref[...].astype(F32)).astype(BF)


def fold(keep, got, upper, deps=()):
    half = keep.shape[0] // 2
    each = min(4, half)
    unit = (each,) + keep.shape[1:]
    count = len(deps)
    away = pl.BlockSpec(unit, lambda i, up: ((1 - up[0]) * (half // each) + i, 0, 0))
    own = pl.BlockSpec(unit, lambda i, up: (up[0] * (half // each) + i, 0, 0))
    out = pl.BlockSpec(unit, lambda i, up: (i, 0, 0))
    shape = jax.ShapeDtypeStruct((half,) + keep.shape[1:], BF)

    def body(*refs):
        fold_kernel(*refs[:5], *refs[5 + count :])

    return pl.pallas_call(
        body,
        grid_spec=pltpu.PrefetchScalarGridSpec(
            num_scalar_prefetch=1,
            grid=(half // each,),
            in_specs=[away, away, own, own] + [any_space() for _ in deps],
            out_specs=[out, out],
        ),
        out_shape=(shape, shape),
        compiler_params=params(VMEM_LIMIT if half >= 8 else SMALL_LIMIT),
        cost_estimate=cost(0, 6 * half * keep[0].size),
        name="fold",
    )(upper, keep, got, keep, got, *deps)


def on_device(
    tokens, grad_out, region_rows, region_cols, ln1_gain, ln1_bias, spec_w1, spec_b1, spec_w2, spec_b2,
    ln2_gain, ln2_bias, w_up, up_bias, w_down, down_bias,
):
    devices = lax.axis_size(AXES[0]) * lax.axis_size(AXES[1])
    count = devices.bit_length() - 1
    me = lax.axis_index(AXES).astype(jnp.int32)
    core = me & 1
    me_one = me.reshape(1)
    feature = tokens.shape[-1]
    block = feature // BLOCKS
    share = ln1_gain.shape[0]
    cells = tokens.shape[1] * tokens.shape[2]
    hidden = w_up.shape[1]
    parts = hidden // feature
    tables = {name: jnp.asarray(value) for name, value in wave_matrices().items()}
    orders = doubling_orders(count)
    places = tuple(places_of(order) for order in orders)
    flat_tokens = tokens.reshape(cells, feature)
    flat_grad = grad_out.reshape(cells, feature)
    fast = devices // 2 == UNITS
    step = lambda value, k: swap(value, devices, (orders[0][k], orders[1][k]))

    padded = lambda v: jnp.pad(v, ((0, 0), (0, LANES - v.shape[1])))
    vectors = (spec_b1, spec_b2, ln1_gain, ln1_bias, ln2_gain, ln2_bias, up_bias, down_bias)
    if fast:
        own_up = w_up.reshape(share, parts, feature).transpose(1, 0, 2)
        unit = chip_unit(own_up, w_down, core, devices)
        bits = (3, 4, 2, 1, 0)
        hop = lambda value, mask: lax.ppermute(value, AXES, [(i, i ^ mask) for i in range(devices)])
        meet = lambda value, bit: hop(value, 1 << bit)
        small = begin_small(spec_w1, spec_w2, vectors)
        made = first(region_rows, region_cols, flat_tokens, tables, 0, 2, deps=(unit, small), tiles=2)
        small = join_rows(small, *(hop(small, mask) for mask in (8, 16, 24)), deps=(made[2],))
        near = join_rows(unit, step(unit, 0), deps=(small,))
        half, normal, mark = first(region_rows, region_cols, flat_tokens, tables, 2, 2, made[:2], deps=(near,), tiles=2)
        small = join_rows(small, *(hop(small, mask) for mask in (4, 2, 6)), deps=(mark,))
        small = join_rows(small, meet(small, 0))
        weights, weight_bits, vector_bits, me_small = small, bits, bits, me_one
        vectors = ()
    else:
        up = lax.all_gather(w_up, AXES, axis=0, tiled=True)
        up = up.reshape(UNITS, feature // UNITS, parts, feature).transpose(0, 2, 1, 3).reshape(UNITS, -1, feature)
        down = lax.all_gather(w_down, AXES, axis=0, tiled=True).reshape(UNITS, -1, feature)
        pieces = tuple(
            jnp.where(core == 0, one, two)[begin : begin + UNITS // 2]
            for one, two in ((up, down), (down, up))
            for begin in (0, UNITS // 2)
        )
        me_one = core.reshape(1)
        me_small = jnp.zeros_like(me_one)
        places = (tuple(range(UNITS)),) * 2
        small = jnp.concatenate([padded(spec_w1), padded(spec_w2)] + [padded(v[None]) for v in vectors])
        small = gather_small(small, me, devices, count)
        weights = small[:, : 4 * share].reshape(devices, 2, 2 * share, LANES).transpose(1, 0, 2, 3)
        weights = weights.reshape(2, 2 * UNITS, -1, LANES).transpose(1, 0, 2, 3).reshape(2 * UNITS, -1, LANES)
        weight_bits, vector_bits = tuple(range(5)), tuple(range(count))
        half, normal, _ = first(region_rows, region_cols, flat_tokens, tables, 0, STEPS)
        vectors = (small[:, 4 * share :].transpose(1, 0, 2).astype(F32),)

    steps = KEPT // GROUP // TAKE
    core_swap = lambda value: swap(value, devices, (0, 0))
    mix1, mix2, wide, long, up_shift = prepare(
        me_small, weights, vectors, feature, hidden, weight_bits, vector_bits
    )
    deps = ()
    if fast:
        near = join_rows(near, step(near, 1), deps=(up_shift,))
        deps = (near,)
    made = mix_first(half, mix1, mix2, wide, long, tables, steps // 2, deps=deps)
    half1, modes1, heads = made[0], made[1:6], made[6:11]
    deps = ()
    if fast:
        beside, across = step(near, 2), step(near, 3)
        other_near = core_swap(near)
        deps = (other_near, heads[4])
    made = mix_second(half, mix1, mix2, wide, long, tables, steps // 2, steps // 2, deps=deps)
    half2, modes2 = made[0], made[1:6]
    if fast:
        beside = hold(beside, (modes2[4],))
        far = step(beside, 3)
        deps = (beside,)
    middle, normed, mark = space(
        region_rows, region_cols, half1, half2, flat_tokens, wide, tables, deps=deps, tiles=2
    )
    if fast:
        far = hold(far, (mark,))
        pieces = (near, beside, across, far, other_near) + tuple(core_swap(v) for v in (beside, across, far))
    active, pre, bias_grad, up_all, down_all, send, keep = feed(
        region_rows, region_cols, me_one, normed, flat_grad, up_shift, pieces, places
    )
    tiles = cells // CELLS
    mixed, grad_middle, half_back, sums_two = feed_down(
        region_rows, region_cols, active, pre, middle, flat_grad, normal, wide, tables["first"], up_all, down_all,
        deps=(send,),
    )
    deps = ()
    if fast:
        ranks = [((me >> jnp.where(core == 0, *bit)) & 1).reshape(1) for bit in zip(*orders)]
        send, keep = fold(keep, swap(send, devices, (0, 0)), ranks[3], deps=(sums_two,))
        deps = (send,)
    half_back, one, two, one_head, two_head, bias_sums = mix_back(
        half_back, modes1, modes2, heads, mix1, mix2, tables, deps=deps
    )
    grad_one = block_grads(modes1[0], modes2[0], heads[0], one, one_head, "grad_mix1")
    if fast:
        send, keep = fold(keep, step(send, 3), ranks[2], deps=(grad_one,))
        deps = (send,)
    grad_two = block_grads(modes1[1], modes2[1], heads[1], two, two_head, "grad_mix2", deps=deps)
    last_args = (region_rows, region_cols, half_back, flat_tokens, grad_middle, wide, tables)
    if fast:
        places_small = [v.reshape(1) for v in (me & 1, (me >> 1) & 3, me >> 3)]
        away, own = pack(places_small[0], grad_one, grad_two, bias_sums, sums_two, bias_grad, wide, devices)
        grad_tokens, mark = last(*last_args, 0, 2, deps=(away,))
        *aways, own = fold_small(own, (hop(away, 1),), places_small[1], 4, deps=(mark,))
        send, keep = fold(keep, step(send, 2), ranks[1], deps=tuple(aways))
        gots = tuple(hop(v, mask) for v, mask in zip(aways, (2, 4, 6)))
        grad_tokens, mark = last(*last_args, 2, 2, (grad_tokens,), deps=(send,))
        *aways, own = fold_small(own, gots, places_small[2], 4, deps=(mark,))
        gots = tuple(hop(v, mask) for v, mask in zip(aways, (8, 16, 24)))
        grad_tokens, mark = last(*last_args, 4, 2, (grad_tokens,), deps=tuple(aways))
        send, keep = fold(keep, step(send, 1), ranks[0], deps=(mark, gots[0]))
        grad_tokens, mark = last(*last_args, 6, 2, (grad_tokens,), deps=(send,))
        widths = (share,) * 5 + (2 * share,) * 2 + (hidden // devices,)
        blocks = end_small(hold(own, (mark,)), gots, 2 * share, block, widths)
        keep = hold(keep, (blocks[0],))
        total = keep[0].astype(F32) + step(send, 0)[0].astype(F32)
        up_sum = total.reshape(parts, 2 * share, feature)
        lower = up_sum[:, :share].reshape(parts * share, feature)
        upper = up_sum[:, share:].reshape(parts * share, feature)
        each = parts * share
        leaving = jnp.where(core == 0, upper, total[:each])
        other = swap(leaving, devices, (0, 0))
        grad_w_up = jnp.where(core == 0, lower, other).reshape(parts, share, feature).transpose(1, 0, 2)
        grad_w_down = jnp.where(core == 0, other, total[each:])
        rows = [v.reshape(-1) for v in blocks[2:]]
        blocks = blocks[:2]
    else:
        scatter = lambda v: lax.psum_scatter(v.astype(F32), AXES, scatter_dimension=0, tiled=True)
        up = jnp.where(core == 0, keep, send).reshape(UNITS, parts, feature // UNITS, feature)
        grad_w_up = scatter(up.transpose(0, 2, 1, 3).reshape(feature, hidden))
        grad_w_down = scatter(jnp.where(core == 0, send, keep).reshape(hidden, feature))
        grad_tokens, _ = last(*last_args, 0, tiles)
        owned = lambda v: jnp.pad(
            v.reshape(v.shape[0], devices, -1).transpose(1, 0, 2), ((0, 0), (0, 0), (0, LANES - v.shape[1] // devices))
        )
        narrow = jnp.concatenate(list(scale_grads(bias_sums, sums_two, wide)) + [sums_two[:3]])
        biases = bias_sums[:2].reshape(2, feature // LANES, 2, LANES).transpose(0, 2, 1, 3).reshape(2, 2 * feature)
        blocks = [v.reshape(devices, 2 * share, LANES) for v in (grad_one, grad_two)]
        packet = jnp.concatenate(blocks + [owned(narrow), owned(biases), owned(bias_grad)], axis=1)
        result = scatter_small(packet, me, devices, count, 8)
        widths = (share,) * 5 + (2 * share,) * 2 + (hidden // devices,)
        rows = [result[4 * share + k, :width] for k, width in enumerate(widths)]
        blocks = [result[k * 2 * share : (k + 1) * 2 * share, :block] for k in range(2)]
    return (
        mixed.reshape(tokens.shape),
        grad_tokens.reshape(tokens.shape),
        rows[0],
        rows[1],
        blocks[0],
        rows[5],
        blocks[1],
        rows[6],
        rows[2],
        rows[3],
        grad_w_up.reshape(share, hidden),
        rows[7],
        grad_w_down,
        rows[4],
    )


def solution(mesh):
    placed = P(AXES)
    return jax.shard_map(
        on_device, mesh=mesh, in_specs=(placed,) * 16, out_specs=(placed,) * 14, check_vma=False
    )
```

```python
import functools
import math

import jax
import jax.numpy as jnp
import numpy as np
from jax import lax
from jax.experimental import pallas as pl
from jax.experimental.pallas import tpu as pltpu
from jax.sharding import PartitionSpec as P

BF = jnp.bfloat16
F32 = jnp.float32
BLOCKS = 8
EPS = 1e-05
SHRINK = 0.01
ROWS = 32
COLS = 64
KEPT = COLS // 2
GROUP = 4
STEPS = ROWS // GROUP
CELLS = GROUP * COLS
MODES = (KEPT + 1) * ROWS
HEAD = (GROUP + 1) * ROWS
BODY = GROUP * ROWS
TAKE = 2
TOOK = TAKE * BODY
LANES = 128
C1 = math.sqrt(2.0 / math.pi)
C3 = 0.044715
SIGMOID = -2.0 * C1 / math.log(2.0)
UNITS = 16
WIDTH = 256
VMEM_LIMIT = 60 * 1024 * 1024
SMALL_LIMIT = 36 * 1024 * 1024
MIDDLE_LIMIT = 50 * 1024 * 1024


def table_parts(values):
    high = values.astype(np.float32).astype(jnp.bfloat16)
    low = (values - high.astype(np.float64)).astype(np.float32).astype(jnp.bfloat16)
    return np.stack([high, low])


def wave_matrices():
    scale = 1.0 / math.sqrt(ROWS * COLS)
    w = np.arange(COLS)
    first = np.zeros((KEPT, 2, GROUP, GROUP, COLS))
    for k in range(KEPT):
        for h in range(GROUP):
            if k == 0:
                first[k, 0, h, h] = scale
                first[k, 1, h, h] = scale * np.where(w % 2 == 0, 1.0, -1.0)
            else:
                first[k, 0, h, h] = scale * np.cos(2 * np.pi * (k * w % COLS) / COLS)
                first[k, 1, h, h] = -scale * np.sin(2 * np.pi * (k * w % COLS) / COLS)
    first = first.reshape(CELLS, CELLS)
    p = np.arange(ROWS)
    turn = 2 * np.pi * (np.outer(p, p) % ROWS) / ROWS
    cos = np.cos(turn).reshape(ROWS, STEPS, GROUP)
    sin = np.sin(turn).reshape(ROWS, STEPS, GROUP)
    body = np.zeros((2, GROUP, ROWS, GROUP, STEPS, 2, GROUP))
    head = np.zeros((2, GROUP + 1, ROWS, GROUP, STEPS, 2, GROUP))
    for k in range(GROUP):
        body[0, k, :, k, :, 0] = cos
        body[0, k, :, k, :, 1] = sin
        body[1, k, :, k, :, 1] = cos
        body[1, k, :, k, :, 0] = -sin
    head[:, 1:GROUP, :, 1:] = body[:, 1:, :, 1:]
    for place, part in ((0, 0), (GROUP, 1)):
        head[0, place, :, 0, :, part] = cos
        head[1, place, :, 0, :, part] = -sin
    weight = np.full((2, GROUP + 1, ROWS, 1), 2.0)
    weight[:, 0] = 1.0
    weight[:, GROUP] = 1.0
    head = head.reshape(2 * HEAD, 2 * BODY)
    body = body.reshape(2 * BODY, 2 * BODY)
    head_weighted = head * weight.reshape(2 * HEAD, 1)
    body_weighted = body * 2.0
    return {
        "first": table_parts(first),
        "first_t": table_parts(first.T),
        "head": table_parts(head),
        "body": table_parts(body),
        "head_t": table_parts(head.T),
        "body_t": table_parts(body.T),
        "head_w": table_parts(head_weighted),
        "body_w": table_parts(body_weighted),
        "head_wt": table_parts(head_weighted.T),
        "body_wt": table_parts(body_weighted.T),
    }


def mm(left, right, dims=(1, 0)):
    return lax.dot_general(
        left, right, (((dims[0],), (dims[1],)), ((), ())), preferred_element_type=F32
    )


def split(values):
    high = values.astype(BF)
    return high, (values - high.astype(F32)).astype(BF)


def turn(table, values):
    high, low = split(values)
    return mm(table[0], high) + mm(table[1], high) + mm(table[0], low)


def turn_once(table, values):
    return mm(table[0], values.astype(BF))


def normalize(values):
    centred = values - jnp.mean(values, axis=-1, keepdims=True)
    inverse = lax.rsqrt(jnp.mean(centred * centred, axis=-1, keepdims=True) + EPS)
    return centred * inverse, inverse


def norm_back(grad, gain, normal, inverse):
    scaled = grad * gain
    return inverse * (
        scaled
        - jnp.mean(scaled, axis=-1, keepdims=True)
        - normal * jnp.mean(scaled * normal, axis=-1, keepdims=True)
    )


def gelu_parts(value):
    square = value * value
    half = 1.0 / (1.0 + jnp.exp2(value * (SIGMOID + (SIGMOID * C3) * square)))
    active = value * half
    slope = half + active * (1.0 - half) * (2.0 * C1 + (6.0 * C1 * C3) * square)
    return active, slope


def live_rows(start, count, rows_ref, cols_ref):
    cell = start + lax.broadcasted_iota(jnp.int32, (count, 1), 0)
    inside = (cell // COLS < rows_ref[0]) & (cell % COLS < cols_ref[0])
    return jnp.where(inside, 1.0, 0.0).astype(F32)


def spread(piece, per_device, me, bits):
    devices = piece.shape[0]
    total = devices * per_device
    lane = lax.broadcasted_iota(jnp.int32, (LANES, total), 0)
    place = lax.broadcasted_iota(jnp.int32, (LANES, total), 1)
    pick = jnp.where(place % per_device == lane, 1.0, 0.0).astype(BF)
    wide = mm(piece.astype(BF), pick)
    row = lax.broadcasted_iota(jnp.int32, (devices, 1), 0)
    owner = jnp.full((devices, 1), me, jnp.int32)
    for k, bit in enumerate(bits):
        owner = owner ^ (((row >> k) & 1) << bit)
    where = lax.broadcasted_iota(jnp.int32, (devices, total), 1) // per_device
    return jnp.sum(jnp.where(owner == where, wide, 0.0), axis=0, keepdims=True)


def place_of(mask, bits):
    return sum(((mask >> bit) & 1) << k for k, bit in enumerate(bits))


MARK = jax.ShapeDtypeStruct((8, LANES), F32)


def any_space():
    return pl.BlockSpec(memory_space=pl.ANY)


def single(shape):
    return pl.BlockSpec(shape, lambda *_: (0,) * len(shape), pipeline_mode=pl.Buffered(1))


def smem():
    return pl.BlockSpec(memory_space=pltpu.SMEM)


def params(limit=VMEM_LIMIT):
    return pltpu.CompilerParams(vmem_limit_bytes=limit)


def cost(flops, moved):
    return pl.CostEstimate(flops=0, bytes_accessed=0, transcendentals=0)


def unread(deps):
    return [pl.BlockSpec(memory_space=pltpu.HBM) if v.shape == MARK.shape else any_space() for v in deps]


def launch(deps, kernel, *, in_specs, **more):
    count = len(in_specs)

    def body(*refs):
        kernel(*refs[:count], *refs[count + len(deps) :])

    call = pl.pallas_call(body, in_specs=list(in_specs) + unread(deps), **more)
    return lambda *operands: call(*operands, *deps)


def to_mixed(real, imag):
    tiles = []
    for at in range(0, real.shape[1], LANES):
        tiles += [real[:, at : at + LANES], imag[:, at : at + LANES]]
    return jnp.concatenate(tiles, axis=1)


def from_mixed(values):
    cut = lambda at: values[:, at : at + LANES]
    real = [cut(at) for at in range(0, values.shape[1], 2 * LANES)]
    imag = [cut(at + LANES) for at in range(0, values.shape[1], 2 * LANES)]
    return jnp.concatenate(real, axis=1), jnp.concatenate(imag, axis=1)


def mix_product(values, matrix_ref, back=False):
    feature = values.shape[1] // 2
    wide = 2 * LANES
    groups = []
    for group in range(2):
        part = values[:, group * feature : (group + 1) * feature]
        count = feature // wide
        for t in range(count):
            begin, end = max(t - 1, 0) * wide, min(t + 2, count) * wide
            here = slice(t * wide, (t + 1) * wide)
            if back:
                groups.append(mm(part[:, begin:end], matrix_ref[group, here, begin:end], (1, 1)))
            else:
                groups.append(mm(part[:, begin:end], matrix_ref[group, begin:end, here]))
    return jnp.concatenate(groups, axis=1)


def first_kernel(begin, rows_ref, cols_ref, tokens_ref, first_ref, *rest):
    half_ref, normal_ref, mark_ref = rest[-3:]
    mark_ref[...] = jnp.zeros_like(mark_ref)
    feature = tokens_ref.shape[1]
    start = (pl.program_id(0) + begin) * tokens_ref.shape[0]
    for k in range(tokens_ref.shape[0] // CELLS):
        here = slice(k * CELLS, (k + 1) * CELLS)
        there = slice(k * 2 * GROUP, (k + 1) * 2 * GROUP)
        normal, _ = normalize(tokens_ref[here, :].astype(F32))
        live = live_rows(start + k * CELLS, CELLS, rows_ref, cols_ref)
        normal = normal * live
        normal_ref[here, :] = normal.astype(BF)
        half_ref[:, there, :feature] = turn(first_ref, normal).reshape(KEPT, 2 * GROUP, feature)
        ones = jnp.broadcast_to(live, (CELLS, LANES)).astype(BF)
        flat = mm(first_ref[0], ones) + mm(first_ref[1], ones)
        half_ref[:, there, feature:] = flat.reshape(KEPT, 2 * GROUP, LANES)


def first(rows, cols, tokens, tables, begin, steps, before=(), deps=(), tiles=1):
    cells, feature = tokens.shape
    table = tables["first"]
    block = pl.BlockSpec((tiles * CELLS, feature), lambda i: (i + begin, 0))
    operands = (rows, cols, tokens, table)
    return launch(
        deps,
        functools.partial(first_kernel, begin),
        grid=(steps,),
        out_shape=(
            jax.ShapeDtypeStruct((KEPT, 2 * ROWS, feature + LANES), F32),
            jax.ShapeDtypeStruct((cells, feature), BF),
            MARK,
        ),
        in_specs=[smem(), smem(), block, single(table.shape)] + [any_space() for _ in before],
        out_specs=(
            pl.BlockSpec((KEPT, 2 * GROUP * tiles, feature + LANES), lambda i: (0, i + begin, 0)),
            block,
            single(MARK.shape),
        ),
        input_output_aliases={len(operands) + k: k for k in range(len(before))},
        compiler_params=params(),
        cost_estimate=cost(6e9, 11e6),
        name="first",
    )(*operands, *before)


def build_mix(me, bits, weights_ref, layer, out_ref, feature):
    block = feature // BLOCKS
    half = feature // 2
    per_group = BLOCKS // 2
    share = 2 * feature // weights_ref.shape[0]
    each = block // share
    out_ref[...] = jnp.zeros_like(out_ref)
    row = lax.broadcasted_iota(jnp.int32, (LANES, half), 0)
    column = lax.broadcasted_iota(jnp.int32, (LANES, half), 1)
    for b in range(per_group):
        shift = jnp.where((column - b * block == row) & (row < block), 1.0, 0.0).astype(BF)
        low, high = b * block, (b + 1) * block
        for group in range(2):
            for part in range(2):
                at = (part * BLOCKS + group * per_group + b) * each
                pieces = [
                    weights_ref[place_of((at + k) ^ me, bits), layer * share : (layer + 1) * share, :]
                    for k in range(each)
                ]
                placed = mm(jnp.concatenate(pieces, axis=0), shift).astype(BF)
                for t in range(low // LANES, (high - 1) // LANES + 1):
                    begin, end = max(low, t * LANES), min(high, (t + 1) * LANES)
                    for c in range(low // LANES, (high - 1) // LANES + 1):
                        piece = placed[begin - low : end - low, c * LANES : (c + 1) * LANES]
                        for up in range(2):
                            top = 2 * t * LANES + up * LANES + begin - t * LANES
                            left = (2 * c + (up ^ part)) * LANES
                            value = -piece if part == 1 and up == 1 else piece
                            here = (group, slice(top, top + end - begin), slice(left, left + LANES))
                            out_ref[here] = out_ref[here] + value


def to_modes(half_ref, head_ref, body_ref, is_head):
    width = half_ref.shape[2]
    real, imag, ends = [], [], ()
    for k in range(TAKE):
        begin = is_head and k == 0
        rows = HEAD if begin else BODY
        spec = turn(head_ref if begin else body_ref, half_ref[k * GROUP : (k + 1) * GROUP].reshape(2 * BODY, width))
        real.append(spec[:BODY])
        imag.append(spec[rows : rows + BODY])
        if begin:
            ends = (spec[BODY:rows], spec[rows + BODY :])
    if is_head:
        real.append(ends[0])
        imag.append(ends[1])
    return jnp.concatenate(real, axis=0), jnp.concatenate(imag, axis=0)


def from_modes(pair_of, head_ref, body_ref, is_head, out_ref, product):
    for k in range(TAKE):
        begin = is_head and k == 0
        parts = []
        for part in pair_of:
            parts.append(part[k * BODY : (k + 1) * BODY])
            if begin:
                parts.append(part[TOOK:])
        result = product(head_ref if begin else body_ref, jnp.concatenate(parts, axis=0))
        out_ref[k * GROUP : (k + 1) * GROUP] = result.reshape(GROUP, 2 * ROWS, result.shape[1])


def mix_step(half_ref, head_ref, body_ref, back_head_ref, back_body_ref, mix1_ref, mix2_ref, wide_ref, long_ref,
             outs, heads, out_ref, is_head):
    feature = out_ref.shape[2]
    specs = to_modes(half_ref, head_ref, body_ref, is_head)
    gain = wide_ref[0:1, :]
    shift = wide_ref[1:2, :]

    def scaled(part):
        flat = jnp.concatenate([part[:, feature:]] * (feature // LANES), axis=1)
        return (part[:, :feature] * gain + flat * shift).astype(BF)

    inside = to_mixed(*(scaled(part) for part in specs))
    active, slope = gelu_parts(mix_product(inside, mix1_ref) + long_ref[0:1, :])
    hidden = active.astype(BF)
    value = mix_product(hidden, mix2_ref) + long_ref[1:2, :]
    bend = jnp.tanh(value / SHRINK)
    flat = jnp.concatenate([part[:, feature:] for part in specs], axis=1)
    for ref, head, kept in zip(outs, heads, (inside, hidden, slope, bend * bend, flat)):
        ref[...] = kept[:TOOK]
        if is_head:
            head[...] = kept[TOOK:]
    from_modes(from_mixed(value - SHRINK * bend), back_head_ref, back_body_ref, is_head, out_ref, turn)


def prepare_kernel(
    weight_bits, vector_bits, me_ref, weights_ref, *rest,
):
    mix1_ref, mix2_ref, wide_ref, long_ref, up_ref, vector_ref = rest[-6:]
    feature = wide_ref.shape[1]
    devices = vector_ref.shape[1]
    share = feature // devices
    me = me_ref[0]
    if len(rest) > 6:
        vector_ref[...] = rest[0][...]
    else:
        rows = weights_ref[:, 4 * share :, :].astype(F32)
        for d in range(devices):
            for k in range(vector_ref.shape[0]):
                vector_ref[k, d : d + 1, :] = rows[d, k : k + 1, :]
    build_mix(me, weight_bits, weights_ref, 0, mix1_ref, feature)
    build_mix(me, weight_bits, weights_ref, 1, mix2_ref, feature)
    wide_ref[...] = jnp.zeros_like(wide_ref)
    long_ref[...] = jnp.zeros_like(long_ref)
    for row, at in enumerate((2, 3, 4, 5, 7)):
        wide_ref[row : row + 1, :] = spread(vector_ref[at], share, me, vector_bits)
    for row in range(2):
        both = spread(vector_ref[row], 2 * share, me, vector_bits)
        long_ref[row : row + 1, :] = to_mixed(both[:, :feature], both[:, feature:])
    up_ref[...] = spread(vector_ref[6], up_ref.shape[1] // devices, me, vector_bits)


def prepare(me, weights, vectors, feature, hidden, weight_bits, vector_bits):
    shapes = (
        jax.ShapeDtypeStruct((2, feature, feature), BF),
        jax.ShapeDtypeStruct((2, feature, feature), BF),
        jax.ShapeDtypeStruct((8, feature), F32),
        jax.ShapeDtypeStruct((8, 2 * feature), F32),
        jax.ShapeDtypeStruct((1, hidden), F32),
    )
    devices = vectors[0].shape[1] if vectors else weights.shape[0]
    return pl.pallas_call(
        functools.partial(prepare_kernel, weight_bits, vector_bits),
        out_shape=shapes,
        in_specs=[smem()] + vmem(1 + len(vectors)),
        out_specs=vmem(len(shapes)),
        scratch_shapes=[pltpu.VMEM((8, devices, LANES), F32)],
        compiler_params=params(),
        cost_estimate=cost(0, 0),
        name="prepare",
    )(me, weights, *vectors)


def mix_first_kernel(
    half_ref, mix1_ref, mix2_ref, wide_ref, long_ref, head_ref, body_ref, back_head_ref, back_body_ref,
    out_ref, *rest,
):
    work = functools.partial(
        mix_step, half_ref, head_ref, body_ref, back_head_ref, back_body_ref, mix1_ref, mix2_ref, wide_ref, long_ref,
        rest[:5], rest[5:], out_ref,
    )

    @pl.when(pl.program_id(0) == 0)
    def _():
        work(True)

    @pl.when(pl.program_id(0) > 0)
    def _():
        work(False)


def mix_second_kernel(
    half_ref, mix1_ref, mix2_ref, wide_ref, long_ref, body_ref, back_body_ref,
    out_ref, *outs,
):
    mix_step(
        half_ref, None, body_ref, None, back_body_ref, mix1_ref, mix2_ref, wide_ref, long_ref,
        outs, (None,) * 5, out_ref, False,
    )


def mode_shapes(rows, feature):
    wide = [jax.ShapeDtypeStruct((rows, 2 * feature), kind) for kind in (BF, BF, F32, F32)]
    return wide + [jax.ShapeDtypeStruct((rows, 2 * LANES), F32)]


def mode_blocks(feature):
    return [pl.BlockSpec((TOOK, width), lambda i: (i, 0)) for width in (2 * feature,) * 4 + (2 * LANES,)]


def half_block(width, begin=0):
    return pl.BlockSpec((TAKE * GROUP, 2 * ROWS, width), lambda i: (i + begin, 0, 0))


def mix_first(half, mix1, mix2, wide, long, tables, steps, deps=()):
    feature = half.shape[2] - LANES
    fixed = (mix1, mix2, wide, long, tables["head"], tables["body"], tables["head_wt"], tables["body_wt"])
    heads = mode_shapes(ROWS, feature)
    return launch(
        deps,
        mix_first_kernel,
        grid=(steps,),
        out_shape=[jax.ShapeDtypeStruct((TAKE * GROUP * steps, 2 * ROWS, feature), F32)]
        + mode_shapes(TOOK * steps, feature) + heads,
        in_specs=[half_block(feature + LANES)] + [single(v.shape) for v in fixed],
        out_specs=[half_block(feature)] + mode_blocks(feature) + [single(v.shape) for v in heads],
        compiler_params=params(),
        cost_estimate=cost(9e9, 20e6),
        name="mix_first",
    )(half, *fixed)


def mix_second(half, mix1, mix2, wide, long, tables, begin, steps, deps=()):
    feature = half.shape[2] - LANES
    fixed = (mix1, mix2, wide, long, tables["body"], tables["body_wt"])
    return launch(
        deps,
        mix_second_kernel,
        grid=(steps,),
        out_shape=[jax.ShapeDtypeStruct((TAKE * GROUP * steps, 2 * ROWS, feature), F32)] + mode_shapes(TOOK * steps, feature),
        in_specs=[half_block(feature + LANES, begin)] + [single(v.shape) for v in fixed],
        out_specs=[half_block(feature)] + mode_blocks(feature),
        compiler_params=params(),
        cost_estimate=cost(9e9, 20e6),
        name="mix_second",
    )(half, *fixed)


def space_kernel(rows_ref, cols_ref, half1_ref, half2_ref, tokens_ref, first_t_ref, wide_ref, middle_ref, normed_ref, mark_ref):
    mark_ref[...] = jnp.zeros_like(mark_ref)
    feature = tokens_ref.shape[1]
    start = pl.program_id(0) * tokens_ref.shape[0]
    for k in range(tokens_ref.shape[0] // CELLS):
        here = slice(k * CELLS, (k + 1) * CELLS)
        flat = lambda ref: ref[:, k * 2 * GROUP : (k + 1) * 2 * GROUP, :].reshape(-1, feature)
        spatial = turn(first_t_ref, jnp.concatenate([flat(half1_ref), flat(half2_ref)], axis=0))
        inputs = tokens_ref[here, :].astype(F32)
        live = live_rows(start + k * CELLS, CELLS, rows_ref, cols_ref)
        normal, _ = normalize(inputs)
        middle = inputs + live * (spatial + (normal * wide_ref[0:1, :] + wide_ref[1:2, :]))
        middle_ref[here, :] = middle
        normal, _ = normalize(middle)
        normed_ref[here, :] = (normal * wide_ref[2:3, :] + wide_ref[3:4, :]).astype(BF)


def column_block(rows, width, tiles=1):
    return pl.BlockSpec((rows, 2 * GROUP * tiles, width), lambda i: (0, i, 0))


def space(rows, cols, half1, half2, tokens, wide, tables, deps=(), tiles=1):
    cells, feature = tokens.shape
    table = tables["first_t"]
    block = pl.BlockSpec((tiles * CELLS, feature), lambda i: (i, 0))
    return launch(
        deps,
        space_kernel,
        grid=(STEPS // tiles,),
        out_shape=(jax.ShapeDtypeStruct((cells, feature), F32), jax.ShapeDtypeStruct((cells, feature), BF), MARK),
        in_specs=[smem(), smem(), column_block(half1.shape[0], feature, tiles), column_block(half2.shape[0], feature, tiles),
                  block, single(table.shape), single(wide.shape)],
        out_specs=(block, block, single(MARK.shape)),
        compiler_params=params(),
        cost_estimate=cost(6e9, 20e6),
        name="space",
    )(rows, cols, half1, half2, tokens, table, wide)


def fetch_weights(me_ref, pieces, places, up_ref, down_ref, sems):
    each = pieces[0].shape[0]
    held = len(pieces) // 2
    count = each * held
    chip = me_ref[0] // 2

    def copies(own, core):
        target = (up_ref, down_ref)[core]
        source = pieces[:held] if own else pieces[held:]
        for mask in range(count):
            at = places[core][mask]
            part = source[at // each].at[at % each]
            yield pltpu.make_async_copy(part, target.at[chip ^ mask], sems.at[core, mask])

    for core in range(2):
        @pl.when(me_ref[0] % 2 == core)
        def _():
            for copy in copies(True, core):
                copy.start()
            for copy in copies(False, 1 - core):
                copy.start()

    def arrived(core):
        for copy in copies(True, core):
            copy.wait()

    return arrived


def up_lanes(up_ref, j, begin, count, feature):
    share = up_ref.shape[1] * feature // (up_ref.shape[0] * up_ref.shape[1])
    return up_ref[:, j * share : (j + 1) * share, begin : begin + count].reshape(feature, count)


def down_rows(down_ref, begin, count):
    share = down_ref.shape[1]
    pieces = []
    at = begin
    while at < begin + count:
        unit, first_row = divmod(at, share)
        last_row = min(share, first_row + begin + count - at)
        pieces.append(down_ref[unit, first_row:last_row, :])
        at += last_row - first_row
    return jnp.concatenate(pieces, axis=0)


def weight_scratch(pieces):
    chips, rows, feature = UNITS, pieces[0].shape[1], pieces[0].shape[2]
    return [
        pltpu.VMEM((chips, rows, feature), BF),
        pltpu.VMEM((chips, rows, feature), BF),
        pltpu.SemaphoreType.DMA((2, chips)),
    ]


def up_part(up_ref, j, feature):
    share = up_ref.shape[1] * feature // (up_ref.shape[0] * up_ref.shape[1])
    return up_ref[:, j * share : (j + 1) * share, :].reshape(feature, feature)


def down_part(down_ref, j, feature):
    share = down_ref.shape[1]
    each = feature // share
    return down_ref[j * each : (j + 1) * each].reshape(feature, feature)


def feed_kernel(places, rows_ref, cols_ref, me_ref, normed_in_ref, grad_ref, bias_ref, *rest):
    pieces = rest[:-17]
    (
        active_all_ref, pre_all_ref, bias_grad_ref, up_all_ref, down_all_ref, send_ref, keep_ref,
        active_ref, pre_ref, normed_ref, branch_ref, up_ref, down_ref, sems, weight_sems, row_sems, grad_sems,
    ) = rest[-17:]
    tile, feature = normed_in_ref.shape
    cells, hidden = active_ref.shape
    tiles = cells // tile
    parts = hidden // feature
    chips, share, _ = up_ref.shape
    each = chips // parts
    small = share // parts
    step = pl.program_id(0)
    mine = pl.ds(pl.multiple_of(jnp.minimum(step, tiles - 1) * tile, tile), tile)
    copies = [
        pltpu.make_async_copy(source, target, weight_sems.at[k])
        for k, (source, target) in enumerate(((up_ref, up_all_ref), (down_ref, down_all_ref)))
    ]

    def row_copies(k):
        here = pl.ds(k * tile, tile)
        return (
            pltpu.make_async_copy(active_ref.at[here], active_all_ref.at[here], row_sems.at[0, k]),
            pltpu.make_async_copy(pre_ref.at[here], pre_all_ref.at[here], row_sems.at[1, k]),
        )

    def work(arrived):
        live = live_rows(step * tile, tile, rows_ref, cols_ref)
        branch = (grad_ref[...].astype(F32) * live).astype(BF)
        branch_ref[mine, :] = branch
        normed = normed_in_ref[...]
        normed_ref[mine, :] = normed
        if arrived:
            arrived(0)
            copies[0].start()
        for begin in range(0, hidden, WIDTH):
            place = slice(begin, begin + WIDTH)
            j, lane = divmod(begin, feature)
            value = mm(normed, up_lanes(up_ref, j, lane, WIDTH, feature)) + bias_ref[:, place]
            if arrived and begin == 0:
                arrived(1)
                copies[1].start()
            grad = mm(branch, down_rows(down_ref, begin, WIDTH), (1, 1))
            active, slope = gelu_parts(value)
            active_ref[mine, place] = active.astype(BF)
            grad = grad * slope
            pre_ref[mine, place] = grad.astype(BF)
            bias_grad_ref[:, place] += jnp.sum(grad, axis=0, keepdims=True)

    @pl.when(step == 0)
    def _():
        bias_grad_ref[...] = jnp.zeros_like(bias_grad_ref)
        work(fetch_weights(me_ref, pieces, places, up_ref, down_ref, sems))

    @pl.when((step > 0) & (step < tiles))
    def _():
        work(None)

    for k in range(tiles):
        @pl.when(step == k)
        def _():
            for copy in row_copies(k):
                copy.start()

    def down_copies(j, target):
        for k in range(each):
            yield pltpu.make_async_copy(up_ref.at[j * each + k], target.at[places[1][j * each + k]], grad_sems.at[j, k])

    def up_copies(j, target):
        for k in range(chips):
            source = down_ref.at[j * each + k // each, pl.ds(k % each * small, small)]
            there = target.at[places[0][k], pl.ds(j * small, small)]
            yield pltpu.make_async_copy(source, there, grad_sems.at[parts + j, k])

    @pl.when(step == tiles)
    def _():
        for copy in copies:
            copy.wait()

    @pl.when((step >= tiles) & (step < tiles + parts))
    def _():
        j = step - tiles
        for k in range(each // 2):
            lanes = pl.ds(pl.multiple_of(j * feature + k * 2 * share, LANES), 2 * share)
            piece = mm(active_ref[:, lanes], branch_ref[...], (0, 0)).astype(BF)
            up_ref[pl.ds(j * each + 2 * k, 2)] = piece.reshape(2, share, feature)

    @pl.when(step >= tiles + parts)
    def _():
        j = step - tiles - parts
        lanes = pl.ds(pl.multiple_of(j * feature, LANES), feature)
        for k in range(each // 2):
            piece = mm(normed_ref[:, k * 2 * share : (k + 1) * 2 * share], pre_ref[:, lanes], (0, 0)).astype(BF)
            down_ref[pl.ds(j * each + 2 * k, 2)] = piece.reshape(2, share, feature)

    for j in range(parts):
        for core in range(2):
            targets = (send_ref, keep_ref) if core == 0 else (keep_ref, send_ref)

            @pl.when((step == tiles + j) & (me_ref[0] % 2 == core))
            def _():
                for copy in down_copies(j, targets[0]):
                    copy.start()

            @pl.when((step == tiles + parts + j) & (me_ref[0] % 2 == core))
            def _():
                for copy in up_copies(j, targets[1]):
                    copy.start()

    @pl.when(step == tiles + 2 * parts - 1)
    def _():
        for k in range(tiles):
            for copy in row_copies(k):
                copy.wait()
        for j in range(parts):
            for copy in down_copies(j, send_ref):
                copy.wait()
            for copy in up_copies(j, send_ref):
                copy.wait()


def feed(rows, cols, me, normed, grad, bias, pieces, places, tile=256, deps=()):
    cells, feature = normed.shape
    hidden = bias.shape[1]
    tiles, parts = cells // tile, hidden // feature
    block = pl.BlockSpec((tile, feature), lambda i: (jnp.minimum(i, tiles - 1), 0))
    weights = jax.ShapeDtypeStruct((UNITS,) + pieces[0].shape[1:], BF)
    rows_shape = jax.ShapeDtypeStruct((cells, hidden), BF)
    return launch(
        deps,
        functools.partial(feed_kernel, places),
        grid=(tiles + 2 * parts,),
        out_shape=(rows_shape, rows_shape, jax.ShapeDtypeStruct((1, hidden), F32)) + (weights,) * 4,
        in_specs=[smem(), smem(), smem(), block, block, single(bias.shape)] + [any_space() for _ in pieces],
        out_specs=(any_space(), any_space(), single((1, hidden))) + (any_space(),) * 4,
        scratch_shapes=[
            pltpu.VMEM((cells, hidden), BF),
            pltpu.VMEM((cells, hidden), BF),
            pltpu.VMEM((cells, feature), BF),
            pltpu.VMEM((cells, feature), BF),
            *weight_scratch(pieces),
            pltpu.SemaphoreType.DMA((2,)),
            pltpu.SemaphoreType.DMA((2, tiles)),
            pltpu.SemaphoreType.DMA((2 * parts, UNITS)),
        ],
        compiler_params=params(),
        cost_estimate=cost(0, 0),
        name="feed",
    )(rows, cols, me, normed, grad, bias, *pieces)


def down_kernel(rows_ref, cols_ref, active_ref, pre_ref, middle_ref, grad_ref, normal_ref, wide_ref, first_ref,
                up_ref, down_ref, mixed_ref, grad_middle_ref, half_ref, sums_ref):
    tile, feature = middle_ref.shape
    hidden = active_ref.shape[1]
    step = pl.program_id(0)

    @pl.when(step == 0)
    def _():
        sums_ref[...] = jnp.zeros_like(sums_ref)

    live = live_rows(step * tile, tile, rows_ref, cols_ref)
    branch = mm(active_ref[...], down_ref[...].reshape(hidden, feature))
    up = jnp.concatenate([up_part(up_ref, j, feature) for j in range(hidden // feature)], axis=1)
    grad_normed = mm(pre_ref[...], up, (1, 1))
    middle = middle_ref[...]
    mixed_ref[...] = (middle + live * (branch + wide_ref[4:5, :])).astype(BF)
    normal, inverse = normalize(middle)
    cotangent = grad_ref[...].astype(F32)
    grad_middle = cotangent + norm_back(grad_normed, wide_ref[2:3, :], normal, inverse)
    grad_middle_ref[...] = grad_middle
    masked = grad_middle * live
    half_ref[...] = turn(first_ref, masked).reshape(half_ref.shape)
    rows = (grad_normed * normal, grad_normed, cotangent * live, masked * normal_ref[...].astype(F32), masked)
    for row, value in enumerate(rows):
        sums_ref[row : row + 1, :] += jnp.sum(value, axis=0, keepdims=True)


def feed_down(rows, cols, active, pre, middle, grad, normal, wide, table, up, down, deps=()):
    cells, feature = middle.shape
    hidden = active.shape[1]
    block = lambda width: pl.BlockSpec((CELLS, width), lambda i: (i, 0))
    operands = (rows, cols, active, pre, middle, grad, normal, wide, table, up, down)
    return launch(
        deps,
        down_kernel,
        grid=(cells // CELLS,),
        out_shape=(
            jax.ShapeDtypeStruct((cells, feature), BF),
            jax.ShapeDtypeStruct((cells, feature), F32),
            jax.ShapeDtypeStruct((KEPT, 2 * ROWS, feature), F32),
            jax.ShapeDtypeStruct((8, feature), F32),
        ),
        in_specs=[smem(), smem(), block(hidden), block(hidden), block(feature), block(feature), block(feature)]
        + [single(v.shape) for v in operands[7:]],
        out_specs=(block(feature), block(feature), column_block(KEPT, feature), single((8, feature))),
        compiler_params=params(),
        cost_estimate=cost(0, 0),
        name="feed_down",
    )(*operands)


def back_step(half_ref, head_ref, body_ref, back_head_ref, back_body_ref, mix1_ref, mix2_ref, ins, in_heads,
              outs, out_heads, out_ref, sums_ref, is_head):
    feature = out_ref.shape[2]

    def read(k):
        if is_head:
            return jnp.concatenate([ins[k][...], in_heads[k][...]], axis=0)
        return ins[k][...]

    grads = to_modes(half_ref, head_ref, body_ref, is_head)
    grad_two = (to_mixed(*grads) * read(1)).astype(BF)
    grad_one = (mix_product(grad_two, mix2_ref, True) * read(0)).astype(BF)
    grad_spec = mix_product(grad_one, mix1_ref, True)
    from_modes(from_mixed(grad_spec), back_head_ref, back_body_ref, is_head, out_ref, turn_once)
    for row, value in enumerate((grad_one, grad_two)):
        outs[row][...] = value[:TOOK]
        if is_head:
            out_heads[row][...] = value[TOOK:]
    flat = jnp.concatenate([read(3)] * (feature // LANES), axis=1)
    for row, value in enumerate((grad_one.astype(F32), grad_two.astype(F32), grad_spec * read(2).astype(F32), grad_spec * flat)):
        total = jnp.sum(value, axis=0, keepdims=True)
        sums_ref[row : row + 1, :] = total if is_head else sums_ref[row : row + 1, :] + total


def mix_back_kernel(
    half_ref, slope1_ref, slope2_ref, bend1_ref, bend2_ref, low1_ref, low2_ref, flat1_ref, flat2_ref,
    slope_head_ref, bend_head_ref, low_head_ref, flat_head_ref, mix1_ref, mix2_ref,
    head_ref, body_ref, back_head_ref, back_body_ref,
    out_ref, one_ref, two_ref, one_head_ref, two_head_ref, sums_ref,
):
    step = pl.program_id(0)
    steps = pl.num_programs(0) // 2
    work = functools.partial(
        back_step, half_ref, head_ref, body_ref, back_head_ref, back_body_ref, mix1_ref, mix2_ref
    )
    heads = (slope_head_ref, bend_head_ref, low_head_ref, flat_head_ref)
    more = (heads, (one_ref, two_ref), (one_head_ref, two_head_ref), out_ref, sums_ref)
    near = (slope1_ref, bend1_ref, low1_ref, flat1_ref)
    far = (slope2_ref, bend2_ref, low2_ref, flat2_ref)

    @pl.when(step == 0)
    def _():
        sums_ref[...] = jnp.zeros_like(sums_ref)
        work(near, *more, True)

    @pl.when((step > 0) & (step < steps))
    def _():
        work(near, *more, False)

    @pl.when(step >= steps)
    def _():
        work(far, *more, False)


def mix_back(half, modes1, modes2, heads, mix1, mix2, tables, deps=()):
    feature = half.shape[2]
    steps = KEPT // GROUP // TAKE
    fixed = tuple(heads[k] for k in (2, 3, 0, 4)) + (
        mix1, mix2, tables["head_w"], tables["body_w"], tables["head_t"], tables["body_t"]
    )
    moving = []
    specs = []
    for k in (2, 3, 0, 4):
        width = modes1[k].shape[1]
        moving += [modes1[k], modes2[k]]
        specs += [
            pl.BlockSpec((TOOK, width), lambda i: (jnp.minimum(i, steps // 2 - 1), 0)),
            pl.BlockSpec((TOOK, width), lambda i: (jnp.maximum(i - steps // 2, 0), 0)),
        ]
    low = lambda rows: jax.ShapeDtypeStruct((rows, 2 * feature), BF)
    body = pl.BlockSpec((TOOK, 2 * feature), lambda i: (i, 0))
    shapes = (
        jax.ShapeDtypeStruct((KEPT, 2 * ROWS, feature), F32), low(TOOK * steps), low(TOOK * steps),
        low(ROWS), low(ROWS), jax.ShapeDtypeStruct((8, 2 * feature), F32),
    )
    return launch(
        deps,
        mix_back_kernel,
        grid=(steps,),
        out_shape=shapes,
        in_specs=[half_block(feature)] + specs + [single(v.shape) for v in fixed],
        out_specs=[half_block(feature), body, body] + [single(v.shape) for v in shapes[3:]],
        compiler_params=params(),
        cost_estimate=cost(18e9, 30e6),
        name="mix_back",
    )(half, *moving, *fixed)


def block_kernel(left1_ref, left2_ref, left_head_ref, right_ref, right_head_ref, out_ref, natural_ref):
    wide = 2 * LANES
    count = left1_ref.shape[1] // wide
    cut = left1_ref.shape[0]
    for t in range(count):
        for c in range(max(t - 1, 0), min(t + 2, count)):
            left, right = slice(t * wide, (t + 1) * wide), slice(c * wide, (c + 1) * wide)
            total = (
                mm(left1_ref[:, left], right_ref[:cut, right], (0, 0))
                + mm(left2_ref[:, left], right_ref[cut:, right], (0, 0))
                + mm(left_head_ref[:, left], right_head_ref[:, right], (0, 0))
            )
            rows, lanes = slice(t * LANES, (t + 1) * LANES), slice(c * LANES, (c + 1) * LANES)
            natural_ref[0, rows, lanes] = total[:LANES, :LANES] + total[LANES:, LANES:]
            natural_ref[1, rows, lanes] = total[:LANES, LANES:] - total[LANES:, :LANES]
    per_group = BLOCKS // 2
    block = count * LANES // per_group
    for b in range(per_group):
        begin = b * block
        base = begin // LANES * LANES
        reach = min(base + wide, count * LANES) - base
        for part in range(2):
            piece = natural_ref[part, begin : begin + block, base : base + reach]
            if begin > base:
                piece = pltpu.roll(piece, reach - (begin - base), axis=1)
            out_ref[part, b * block : (b + 1) * block, :] = piece[:, :LANES]


def block_grads(left1, left2, left_head, right, right_head, name, deps=()):
    feature = left1.shape[1] // 2
    half = feature // 2
    block = lambda v: pl.BlockSpec((v.shape[0], feature), lambda i: (0, i))
    return launch(
        deps,
        block_kernel,
        grid=(2,),
        out_shape=jax.ShapeDtypeStruct((2, feature, LANES), F32),
        in_specs=[block(v) for v in (left1, left2, left_head, right, right_head)],
        out_specs=pl.BlockSpec((2, half, LANES), lambda i: (0, i, 0)),
        scratch_shapes=[pltpu.VMEM((2, half, half), F32)],
        compiler_params=params(MIDDLE_LIMIT),
        cost_estimate=cost(5e9, 7e6),
        name=name,
    )(left1, left2, left_head, right, right_head)


def last_kernel(begin, rows_ref, cols_ref, half_ref, tokens_ref, grad_ref, first_t_ref, wide_ref, *rest):
    out_ref, mark_ref = rest[-2:]
    mark_ref[...] = jnp.zeros_like(mark_ref)
    tile, feature = tokens_ref.shape
    live = live_rows((pl.program_id(0) + begin) * tile, tile, rows_ref, cols_ref)
    grad_middle = grad_ref[...]
    grad_normed = live * (grad_middle + turn_once(first_t_ref, half_ref[...].reshape(CELLS, feature)))
    normal, inverse = normalize(tokens_ref[...].astype(F32))
    out_ref[...] = grad_middle + norm_back(grad_normed, wide_ref[0:1, :], normal, inverse)


def last(rows, cols, half, tokens, grad, wide, tables, begin, steps, before=(), deps=()):
    cells, feature = tokens.shape
    first_t = tables["first_t"]
    block = pl.BlockSpec((CELLS, feature), lambda i: (i + begin, 0))
    operands = (rows, cols, half, tokens, grad, first_t, wide)
    return launch(
        deps,
        functools.partial(last_kernel, begin),
        grid=(steps,),
        out_shape=(jax.ShapeDtypeStruct((cells, feature), F32), MARK),
        in_specs=[smem(), smem(), pl.BlockSpec((KEPT, 2 * GROUP, feature), lambda i: (0, i + begin, 0)), block, block,
                  single(first_t.shape), single(wide.shape)] + [any_space() for _ in before],
        out_specs=(block, single(MARK.shape)),
        input_output_aliases={len(operands): 0} if before else {},
        compiler_params=params(),
        cost_estimate=cost(6e9, 20e6),
        name="last",
    )(*operands, *before)


def collect(value, per_device, devices):
    total = value.shape[1]
    owner = lax.broadcasted_iota(jnp.int32, (devices, total), 1) // per_device
    row = lax.broadcasted_iota(jnp.int32, (devices, total), 0)
    high, low = split(jnp.where(owner == row, jnp.broadcast_to(value, (devices, total)), 0.0))
    place = lax.broadcasted_iota(jnp.int32, (total, LANES), 0)
    lane = lax.broadcasted_iota(jnp.int32, (total, LANES), 1)
    pick = jnp.where(place % per_device == lane, 1.0, 0.0).astype(BF)
    return mm(high, pick) + mm(low, pick)


def emit(place, sum_ref, send_refs, keep_ref):
    half, _, rows, _ = sum_ref.shape
    rows = rows - 8
    for k, send_ref in enumerate(send_refs):
        away = sum_ref[:, pl.ds(place ^ (k + 1), 1)].reshape(half, rows + 8, LANES)
        high, low = split(away[:, rows:])
        send_ref[:, :rows] = away[:, :rows].astype(BF)
        send_ref[:, rows:] = jnp.concatenate([high.astype(F32), low.astype(F32)], axis=1).astype(BF)
    keep_ref[...] = sum_ref[:, pl.ds(place, 1)].reshape(half, rows + 8, LANES)


def pack_kernel(place_ref, one_ref, two_ref, mixed_ref, sums_ref, up_ref, wide_ref, send_ref, keep_ref, sum_ref):
    half, _, rows, _ = sum_ref.shape
    devices = 2 * half
    share = (rows - 8) // 4
    feature = sums_ref.shape[1]
    sum_ref[:, :, : 2 * share] = one_ref[...].reshape(half, 2, 2 * share, LANES)
    sum_ref[:, :, 2 * share : 4 * share] = two_ref[...].reshape(half, 2, 2 * share, LANES)
    first_gain, first_bias = scale_grads(mixed_ref, sums_ref, wide_ref)
    natural = [jnp.concatenate(from_mixed(mixed_ref[k : k + 1, :]), axis=1) for k in range(2)]
    narrow = [first_gain, first_bias] + [sums_ref[k : k + 1, :] for k in range(3)]
    for k, value in enumerate(narrow + natural + [up_ref[...]]):
        placed = collect(value, value.shape[1] // devices, devices)
        for d in range(devices):
            sum_ref[d // 2, d % 2, 4 * share + k : 4 * share + k + 1, :] = placed[d : d + 1, :]
    emit(place_ref[0], sum_ref, (send_ref,), keep_ref)


def scale_grads(mixed_ref, sums_ref, wide_ref):
    real, imag = from_mixed(mixed_ref[2:3, :])
    scaled = real + imag
    real, imag = from_mixed(mixed_ref[3:4, :])
    flat = real + imag
    gain = sums_ref[3:4, :] + (scaled - wide_ref[1:2, :] * flat) / wide_ref[0:1, :]
    return gain, sums_ref[4:5, :] + flat


def small_shapes(half, rows, others):
    shapes = [jax.ShapeDtypeStruct((half, rows + 8, LANES), BF)] * others
    return shapes + [jax.ShapeDtypeStruct((half, rows, LANES), F32)]


def pack(upper, one, two, mixed, sums, up, wide, devices):
    rows = 2 * one.shape[0] * one.shape[1] // devices + 8
    shapes = small_shapes(devices // 2, rows, 1)
    operands = (one, two, mixed, sums, up, wide)
    return pl.pallas_call(
        pack_kernel,
        out_shape=shapes,
        in_specs=[smem()] + vmem(len(operands)),
        out_specs=vmem(2),
        scratch_shapes=[pltpu.VMEM((devices // 2, 2, rows, LANES), F32)],
        compiler_params=params(MIDDLE_LIMIT),
        cost_estimate=cost(0, 0),
        name="pack",
    )(upper, *operands)


def merge_small(keep_ref, got_refs):
    rows = keep_ref.shape[1] - 8
    top, tail = keep_ref[:, :rows], keep_ref[:, rows:]
    for got_ref in got_refs:
        both = got_ref[:, rows:].astype(F32)
        top = top + got_ref[:, :rows].astype(F32)
        tail = tail + (both[:, :8] + both[:, 8:])
    return top, tail


def fold_small_kernel(others, place_ref, keep_ref, *rest):
    sum_ref = rest[-1]
    send_refs, out_ref = rest[-2 - others : -2], rest[-2]
    half, count, rows, _ = sum_ref.shape
    top, tail = merge_small(keep_ref, rest[: len(rest) - 2 - others])
    sum_ref[:, :, : rows - 8] = top.reshape(half, count, rows - 8, LANES)
    sum_ref[:, :, rows - 8 :] = tail.reshape(half, count, 8, LANES)
    emit(place_ref[0], sum_ref, send_refs, out_ref)


def fold_small(keep, got, place, count, deps=()):
    half, rows = keep.shape[0] // count, keep.shape[1]
    shapes = small_shapes(half, rows, count - 1)
    return launch(
        deps,
        functools.partial(fold_small_kernel, count - 1),
        out_shape=shapes,
        in_specs=[smem()] + vmem(1 + len(got)),
        out_specs=vmem(len(shapes)),
        scratch_shapes=[pltpu.VMEM((half, count, rows, LANES), F32)],
        compiler_params=params(SMALL_LIMIT),
        cost_estimate=cost(0, 0),
        name="fold_small",
    )(place, keep, *got)


def vmem(count):
    return [pl.BlockSpec(memory_space=pltpu.VMEM)] * count


def end_small_kernel(others, keep_ref, *rest):
    got_refs, (one_ref, two_ref, *rows_refs) = rest[:others], rest[others:]
    top, tail = merge_small(keep_ref, got_refs)
    share, block = one_ref.shape
    one_ref[...] = top[0, :share, :block]
    two_ref[...] = top[0, share:, :block]
    for row, ref in enumerate(rows_refs):
        ref[...] = tail[0, row : row + 1, : ref.shape[1]]


def end_small(keep, got, share, block, widths):
    shapes = [jax.ShapeDtypeStruct((share, block), F32)] * 2
    shapes += [jax.ShapeDtypeStruct((1, width), F32) for width in widths]
    return pl.pallas_call(
        functools.partial(end_small_kernel, len(got)),
        out_shape=shapes,
        in_specs=vmem(1 + len(got)),
        out_specs=vmem(len(shapes)),
        compiler_params=params(SMALL_LIMIT),
        cost_estimate=cost(0, 0),
        name="end_small",
    )(keep, *got)


def begin_small_kernel(one_ref, two_ref, *rest):
    out_ref, rows_ref = rest[-2:]
    share, block = one_ref.shape
    out_ref[...] = jnp.zeros_like(out_ref)
    rows_ref[...] = jnp.zeros_like(rows_ref)
    out_ref[0, :share, :block] = one_ref[...]
    out_ref[0, share : 2 * share, :block] = two_ref[...]
    for row, ref in enumerate(rest[:-2]):
        rows_ref[row : row + 1, : ref.shape[1]] = ref[...].astype(F32)
    out_ref[0, 2 * share :, :] = rows_ref[...].astype(BF)


def begin_small(one, two, vectors):
    share = one.shape[0]
    operands = (one, two) + tuple(v[None] for v in vectors)
    return pl.pallas_call(
        begin_small_kernel,
        out_shape=jax.ShapeDtypeStruct((1, 2 * share + 16, LANES), BF),
        in_specs=vmem(len(operands)),
        out_specs=vmem(1)[0],
        scratch_shapes=[pltpu.VMEM((16, LANES), F32)],
        compiler_params=params(),
        cost_estimate=cost(0, 0),
        name="begin_small",
    )(*operands)


AXES = ("dp", "fsdp")


def swap(value, devices, bits):
    return lax.ppermute(value, AXES, [(i, i ^ (1 << bits[i & 1])) for i in range(devices)])


def doubling_orders(count):
    first = list(range(count - 1, 0, -1))
    second = list(first)
    for k in range(0, len(second) - 1, 2):
        second[k], second[k + 1] = second[k + 1], second[k]
    return first, second


def places_of(order):
    return [
        sum(1 << k for k, bit in enumerate(order) if mask >> (bit - 1) & 1) for mask in range(1 << len(order))
    ]


def join_kernel(*refs):
    out_ref = refs[-1]
    count = refs[0].shape[0]
    for k, ref in enumerate(refs[:-1]):
        out_ref[k * count : (k + 1) * count] = ref[...]


def join_rows(*pieces, deps=()):
    shape = jax.ShapeDtypeStruct((len(pieces) * pieces[0].shape[0],) + pieces[0].shape[1:], pieces[0].dtype)
    return launch(
        deps,
        join_kernel,
        out_shape=shape,
        in_specs=[pl.BlockSpec(memory_space=pltpu.VMEM) for _ in pieces],
        out_specs=pl.BlockSpec(memory_space=pltpu.VMEM),
        compiler_params=params(SMALL_LIMIT),
        cost_estimate=cost(0, 0),
        name="join",
    )(*pieces)


def hold(value, deps):
    def body(*refs):
        pass

    return pl.pallas_call(
        body,
        out_shape=jax.ShapeDtypeStruct(value.shape, value.dtype),
        in_specs=[any_space()] + unread(deps),
        out_specs=any_space(),
        input_output_aliases={0: 0},
        compiler_params=params(SMALL_LIMIT),
        cost_estimate=cost(0, 0),
        name="hold",
    )(value, *deps)


def gather_small(value, me, devices, count):
    held = value[None]
    for bit in list(range(3, count)) + [2, 1, 0]:
        other = swap(held, devices, (bit, bit))
        upper = (me >> bit) & 1
        axis = 0 if bit > 2 else 1
        join_two = lambda a, b: jnp.stack([a, b], axis=axis).reshape((-1,) + value.shape)
        held = jnp.where(upper == 0, join_two(held, other), join_two(other, held))
    return held


def scatter_small(value, me, devices, count, exact):
    shape = value.shape[1:]
    rows = shape[0]
    total = value
    for bit in [0, 1, 2] + list(range(count - 1, 2, -1)):
        upper = (me >> bit) & 1
        axis = 0 if bit > 2 else 1
        pair = total.reshape(((2, -1) if bit > 2 else (-1, 2)) + shape)
        away = lax.dynamic_index_in_dim(pair, 1 - upper, axis, keepdims=False)
        keep = lax.dynamic_index_in_dim(pair, upper, axis, keepdims=False)
        sums = away[:, rows - exact :]
        top = lax.reduce_precision(sums, 8, 7)
        packet = jnp.concatenate([away[:, : rows - exact], top, sums - top], axis=1).astype(BF)
        got = swap(packet, devices, (bit, bit)).astype(F32)
        low = got[:, rows - exact : rows] + got[:, rows:]
        total = keep + jnp.concatenate([got[:, : rows - exact], low], axis=1)
    return total[0]


def chip_unit(up, down, core, devices):
    parts, share, feature = up.shape
    flat = up.reshape(parts * share, feature)
    other = swap(jnp.where(core == 0, down, flat), devices, (0, 0))
    up_unit = jnp.concatenate([up, other.reshape(up.shape)], axis=1).reshape(2 * parts * share, feature)
    return jnp.where(core == 0, up_unit, jnp.concatenate([other, down]))[None]


def fold_kernel(upper_ref, keep_away_ref, got_away_ref, keep_own_ref, got_own_ref, send_ref, keep_ref):
    send_ref[...] = (keep_away_ref[...].astype(F32) + got_away_ref[...].astype(F32)).astype(BF)
    keep_ref[...] = (keep_own_ref[...].astype(F32) + got_own_ref[...].astype(F32)).astype(BF)


def fold(keep, got, upper, deps=()):
    half = keep.shape[0] // 2
    each = min(4, half)
    unit = (each,) + keep.shape[1:]
    count = len(deps)
    away = pl.BlockSpec(unit, lambda i, up: ((1 - up[0]) * (half // each) + i, 0, 0))
    own = pl.BlockSpec(unit, lambda i, up: (up[0] * (half // each) + i, 0, 0))
    out = pl.BlockSpec(unit, lambda i, up: (i, 0, 0))
    shape = jax.ShapeDtypeStruct((half,) + keep.shape[1:], BF)

    def body(*refs):
        fold_kernel(*refs[:5], *refs[5 + count :])

    return pl.pallas_call(
        body,
        grid_spec=pltpu.PrefetchScalarGridSpec(
            num_scalar_prefetch=1,
            grid=(half // each,),
            in_specs=[away, away, own, own] + [any_space() for _ in deps],
            out_specs=[out, out],
        ),
        out_shape=(shape, shape),
        compiler_params=params(VMEM_LIMIT if half >= 8 else SMALL_LIMIT),
        cost_estimate=cost(0, 6 * half * keep[0].size),
        name="fold",
    )(upper, keep, got, keep, got, *deps)


def on_device(
    tokens, grad_out, region_rows, region_cols, ln1_gain, ln1_bias, spec_w1, spec_b1, spec_w2, spec_b2,
    ln2_gain, ln2_bias, w_up, up_bias, w_down, down_bias,
):
    devices = lax.axis_size(AXES[0]) * lax.axis_size(AXES[1])
    count = devices.bit_length() - 1
    me = lax.axis_index(AXES).astype(jnp.int32)
    core = me & 1
    me_one = me.reshape(1)
    feature = tokens.shape[-1]
    block = feature // BLOCKS
    share = ln1_gain.shape[0]
    cells = tokens.shape[1] * tokens.shape[2]
    hidden = w_up.shape[1]
    parts = hidden // feature
    tables = {name: jnp.asarray(value) for name, value in wave_matrices().items()}
    orders = doubling_orders(count)
    places = tuple(places_of(order) for order in orders)
    flat_tokens = tokens.reshape(cells, feature)
    flat_grad = grad_out.reshape(cells, feature)
    fast = devices // 2 == UNITS
    step = lambda value, k: swap(value, devices, (orders[0][k], orders[1][k]))

    padded = lambda v: jnp.pad(v, ((0, 0), (0, LANES - v.shape[1])))
    vectors = (spec_b1, spec_b2, ln1_gain, ln1_bias, ln2_gain, ln2_bias, up_bias, down_bias)
    if fast:
        own_up = w_up.reshape(share, parts, feature).transpose(1, 0, 2)
        unit = chip_unit(own_up, w_down, core, devices)
        bits = (3, 4, 2, 1, 0)
        hop = lambda value, mask: lax.ppermute(value, AXES, [(i, i ^ mask) for i in range(devices)])
        meet = lambda value, bit: hop(value, 1 << bit)
        small = begin_small(spec_w1, spec_w2, vectors)
        made = first(region_rows, region_cols, flat_tokens, tables, 0, 2, deps=(unit, small), tiles=2)
        small = join_rows(small, *(hop(small, mask) for mask in (8, 16, 24)), deps=(made[2],))
        near = join_rows(unit, step(unit, 0), deps=(small,))
        half, normal, mark = first(region_rows, region_cols, flat_tokens, tables, 2, 2, made[:2], deps=(near,), tiles=2)
        small = join_rows(small, *(hop(small, mask) for mask in (4, 2, 6)), deps=(mark,))
        small = join_rows(small, meet(small, 0))
        weights, weight_bits, vector_bits, me_small = small, bits, bits, me_one
        vectors = ()
    else:
        up = lax.all_gather(w_up, AXES, axis=0, tiled=True)
        up = up.reshape(UNITS, feature // UNITS, parts, feature).transpose(0, 2, 1, 3).reshape(UNITS, -1, feature)
        down = lax.all_gather(w_down, AXES, axis=0, tiled=True).reshape(UNITS, -1, feature)
        pieces = tuple(
            jnp.where(core == 0, one, two)[begin : begin + UNITS // 2]
            for one, two in ((up, down), (down, up))
            for begin in (0, UNITS // 2)
        )
        me_one = core.reshape(1)
        me_small = jnp.zeros_like(me_one)
        places = (tuple(range(UNITS)),) * 2
        small = jnp.concatenate([padded(spec_w1), padded(spec_w2)] + [padded(v[None]) for v in vectors])
        small = gather_small(small, me, devices, count)
        weights = small[:, : 4 * share].reshape(devices, 2, 2 * share, LANES).transpose(1, 0, 2, 3)
        weights = weights.reshape(2, 2 * UNITS, -1, LANES).transpose(1, 0, 2, 3).reshape(2 * UNITS, -1, LANES)
        weight_bits, vector_bits = tuple(range(5)), tuple(range(count))
        half, normal, _ = first(region_rows, region_cols, flat_tokens, tables, 0, STEPS)
        vectors = (small[:, 4 * share :].transpose(1, 0, 2).astype(F32),)

    steps = KEPT // GROUP // TAKE
    core_swap = lambda value: swap(value, devices, (0, 0))
    mix1, mix2, wide, long, up_shift = prepare(
        me_small, weights, vectors, feature, hidden, weight_bits, vector_bits
    )
    deps = ()
    if fast:
        near = join_rows(near, step(near, 1), deps=(up_shift,))
        deps = (near,)
    made = mix_first(half, mix1, mix2, wide, long, tables, steps // 2, deps=deps)
    half1, modes1, heads = made[0], made[1:6], made[6:11]
    deps = ()
    if fast:
        beside, across = step(near, 2), step(near, 3)
        other_near = core_swap(near)
        deps = (other_near, heads[4])
    made = mix_second(half, mix1, mix2, wide, long, tables, steps // 2, steps // 2, deps=deps)
    half2, modes2 = made[0], made[1:6]
    if fast:
        beside = hold(beside, (modes2[4],))
        far = step(beside, 3)
        deps = (beside,)
    middle, normed, mark = space(
        region_rows, region_cols, half1, half2, flat_tokens, wide, tables, deps=deps, tiles=2
    )
    if fast:
        far = hold(far, (mark,))
        pieces = (near, beside, across, far, other_near) + tuple(core_swap(v) for v in (beside, across, far))
    active, pre, bias_grad, up_all, down_all, send, keep = feed(
        region_rows, region_cols, me_one, normed, flat_grad, up_shift, pieces, places
    )
    tiles = cells // CELLS
    mixed, grad_middle, half_back, sums_two = feed_down(
        region_rows, region_cols, active, pre, middle, flat_grad, normal, wide, tables["first"], up_all, down_all,
        deps=(send,),
    )
    deps = ()
    if fast:
        ranks = [((me >> jnp.where(core == 0, *bit)) & 1).reshape(1) for bit in zip(*orders)]
        send, keep = fold(keep, swap(send, devices, (0, 0)), ranks[3], deps=(sums_two,))
        deps = (send,)
    half_back, one, two, one_head, two_head, bias_sums = mix_back(
        half_back, modes1, modes2, heads, mix1, mix2, tables, deps=deps
    )
    grad_one = block_grads(modes1[0], modes2[0], heads[0], one, one_head, "grad_mix1")
    if fast:
        send, keep = fold(keep, step(send, 3), ranks[2], deps=(grad_one,))
        deps = (send,)
    grad_two = block_grads(modes1[1], modes2[1], heads[1], two, two_head, "grad_mix2", deps=deps)
    last_args = (region_rows, region_cols, half_back, flat_tokens, grad_middle, wide, tables)
    if fast:
        places_small = [v.reshape(1) for v in (me & 1, (me >> 1) & 3, me >> 3)]
        away, own = pack(places_small[0], grad_one, grad_two, bias_sums, sums_two, bias_grad, wide, devices)
        grad_tokens, mark = last(*last_args, 0, 2, deps=(away,))
        *aways, own = fold_small(own, (hop(away, 1),), places_small[1], 4, deps=(mark,))
        send, keep = fold(keep, step(send, 2), ranks[1], deps=tuple(aways))
        gots = tuple(hop(v, mask) for v, mask in zip(aways, (2, 4, 6)))
        grad_tokens, mark = last(*last_args, 2, 2, (grad_tokens,), deps=(send,))
        *aways, own = fold_small(own, gots, places_small[2], 4, deps=(mark,))
        gots = tuple(hop(v, mask) for v, mask in zip(aways, (8, 16, 24)))
        grad_tokens, mark = last(*last_args, 4, 2, (grad_tokens,), deps=tuple(aways))
        send, keep = fold(keep, step(send, 1), ranks[0], deps=(mark,) + gots)
        grad_tokens, mark = last(*last_args, 6, 2, (grad_tokens,), deps=(send,))
        widths = (share,) * 5 + (2 * share,) * 2 + (hidden // devices,)
        blocks = end_small(hold(own, (mark,)), gots, 2 * share, block, widths)
        keep = hold(keep, (blocks[0],))
        total = keep[0].astype(F32) + step(send, 0)[0].astype(F32)
        up_sum = total.reshape(parts, 2 * share, feature)
        lower = up_sum[:, :share].reshape(parts * share, feature)
        upper = up_sum[:, share:].reshape(parts * share, feature)
        each = parts * share
        leaving = jnp.where(core == 0, upper, total[:each])
        other = swap(leaving, devices, (0, 0))
        grad_w_up = jnp.where(core == 0, lower, other).reshape(parts, share, feature).transpose(1, 0, 2)
        grad_w_down = jnp.where(core == 0, other, total[each:])
        rows = [v.reshape(-1) for v in blocks[2:]]
        blocks = blocks[:2]
    else:
        scatter = lambda v: lax.psum_scatter(v.astype(F32), AXES, scatter_dimension=0, tiled=True)
        up = jnp.where(core == 0, keep, send).reshape(UNITS, parts, feature // UNITS, feature)
        grad_w_up = scatter(up.transpose(0, 2, 1, 3).reshape(feature, hidden))
        grad_w_down = scatter(jnp.where(core == 0, send, keep).reshape(hidden, feature))
        grad_tokens, _ = last(*last_args, 0, tiles)
        owned = lambda v: jnp.pad(
            v.reshape(v.shape[0], devices, -1).transpose(1, 0, 2), ((0, 0), (0, 0), (0, LANES - v.shape[1] // devices))
        )
        narrow = jnp.concatenate(list(scale_grads(bias_sums, sums_two, wide)) + [sums_two[:3]])
        biases = bias_sums[:2].reshape(2, feature // LANES, 2, LANES).transpose(0, 2, 1, 3).reshape(2, 2 * feature)
        blocks = [v.reshape(devices, 2 * share, LANES) for v in (grad_one, grad_two)]
        packet = jnp.concatenate(blocks + [owned(narrow), owned(biases), owned(bias_grad)], axis=1)
        result = scatter_small(packet, me, devices, count, 8)
        widths = (share,) * 5 + (2 * share,) * 2 + (hidden // devices,)
        rows = [result[4 * share + k, :width] for k, width in enumerate(widths)]
        blocks = [result[k * 2 * share : (k + 1) * 2 * share, :block] for k in range(2)]
    return (
        mixed.reshape(tokens.shape),
        grad_tokens.reshape(tokens.shape),
        rows[0],
        rows[1],
        blocks[0],
        rows[5],
        blocks[1],
        rows[6],
        rows[2],
        rows[3],
        grad_w_up.reshape(share, hidden),
        rows[7],
        grad_w_down,
        rows[4],
    )


def solution(mesh):
    placed = P(AXES)
    return jax.shard_map(
        on_device, mesh=mesh, in_specs=(placed,) * 16, out_specs=(placed,) * 14, check_vma=False
    )
```
